32 devices in a mesh: bz: 2 (over x), by: 4 (over z), bx: 4 (over y, core).
Axes of the slice: x: 2, y: 2, z: 4, core: 2. Of those that a mesh axis runs over, the one named last changes fastest.
Arguments:
- density: float32 [16, 128, 1024], P('bz', 'by', 'bx'), may hold values from 0.2 to 1
- bin_index: int32 [16, 128, 1024], P('bz', 'by', 'bx'), may hold values from 0 to 255
- tf_colour: bfloat16 [3, 256], replicated, may hold values from 0 to 1
- tf_extinction: bfloat16 [256], replicated, may hold values from 0.049804688 to 8
- slab_rank: int32 [2], replicated, may hold values from 0 to 1, as said below
Outputs:
- frame: float32 [4, 256, 2048], P(None, ('by', 'bz'), 'bx')
The draws below stay inside these ranges and needn't reach their ends.
Inputs may be any that keep to these rules, and one draw needn't show every extreme that they name: slab_rank[i] is i XOR one fixed number: the front-to-back order of a binary tree of slabs in which either child may be the nearer one at each level.
All inputs are finite; a program needn't handle non-finite values.
Results may differ from the reference program's by a relative error of at most 0.0003.
The reference program's roundings to bfloat16 on the way count: a program that leaves them out, or rounds other values in their place, can miss the bound.
Values may be sent and summed in bfloat16 or wider, within the bound.
No kernel may reach another device: no remote copies, remote signals or barrier semaphores. Data moves between devices by JAX's collectives and lax.ppermute only.
A program may use at most 64 MiB of HBM per device.

```python
import math
import jax
import jax.numpy as jnp
import numpy as np
from jax import lax

VZ = 8
BINS = 256
SAMPLES = 16
SLABS = 2
NZ = 16
NY = 128
NX = 1024
HEIGHT = 256
WIDTH = 2048


def draw_slab_rank(key, part):
    key = jax.random.fold_in(key, 7)
    flip_mask = jax.random.randint(key, (), 0, SLABS, dtype=jnp.int32)
    return jnp.bitwise_xor(jnp.arange(SLABS, dtype=jnp.int32), flip_mask)


def plant(values, rng, smallest, top_value):
    dims = values.shape
    index_at = [jax.random.randint(jax.random.fold_in(rng, axis), (), 0, dims[axis]) for axis in range(len(dims))]
    values = values.at[tuple(index_at)].set(smallest)
    longest = dims.index(max(dims))
    index_at[longest] = (index_at[longest] + 1) % dims[longest]
    return values.at[tuple(index_at)].set(top_value)


def levels(rng, extent, shards, low, high):
    def one(axis_at, parts):
        heights = jax.random.uniform(jax.random.fold_in(jax.random.fold_in(rng, 6), axis_at), (parts,), jnp.float32, low / len(shards), high / len(shards))
        return jnp.repeat(jnp.exp(heights), extent[axis_at] // parts).reshape((-1,) + (1,) * (len(extent) - axis_at - 1))

    gain = one(*shards[0])
    for cut in shards[1:]:
        gain = gain * one(*cut)
    return gain


def rank_bounds(amount, slope):
    portions = [(1 << 20) // math.isqrt(grade ** slope) + 1 for grade in range(1, amount + 1)]
    scale = 1 + sum(portions) // (1 << 30)
    return np.cumsum(np.array([max(1, weight // scale) for weight in portions]))


def ranked(own_key, shape, amount, slope):
    table = rank_bounds(amount, slope)
    lot = jax.random.randint(jax.random.fold_in(own_key, 1), shape, 0, int(table[amount - 1]))
    grade = jnp.searchsorted(jnp.asarray(table, jnp.int32), lot, side="right")
    return jax.random.permutation(jax.random.fold_in(own_key, 2), amount)[grade].astype(jnp.int32)


def setup_inputs(seed: int = 0) -> dict:
    streams_of = jax.random.split(jax.random.key(seed), 6)
    return {
        "density": jnp.clip(0.2 + 0.8 * jax.random.uniform(streams_of[0], (NZ, NY, NX), jnp.float32) ** levels(streams_of[0], (NZ, NY, NX), ((0, 2), (1, 4), (2, 4)), -0.2, 0.2), 0.2, 1.0),
        "bin_index": plant(ranked(streams_of[1], (NZ, NY, NX), BINS, 2), jax.random.fold_in(streams_of[1], 3), 0, BINS - 1).astype(jnp.int32),
        "tf_colour": jnp.clip(jax.random.uniform(streams_of[2], (3, BINS), jnp.float32, 0.0, 1.0), 0.0, 1.0).astype(jnp.bfloat16),
        "tf_extinction": jnp.clip(jnp.exp(jax.random.uniform(streams_of[3], (BINS,), jnp.float32, math.log(0.049804688), math.log(8.0))), 0.049804688, 8.0).astype(jnp.bfloat16),
        "slab_rank": draw_slab_rank(jax.random.fold_in(streams_of[5], 71), 0),
    }


def resample_axis(field, axis):
    length = field.shape[axis] - 2
    lower_part = lax.slice_in_dim(field, 0, length, axis=axis)
    middle = lax.slice_in_dim(field, 1, length + 1, axis=axis)
    upper_part = lax.slice_in_dim(field, 2, length + 2, axis=axis)
    even_cells = 0.25 * lower_part + 0.75 * middle
    odd_cells = 0.75 * middle + 0.25 * upper_part
    joined = jnp.stack([even_cells, odd_cells], axis=axis + 1)
    shape_out = field.shape[:axis] + (2 * length,) + field.shape[axis + 1:]
    return joined.reshape(shape_out)


def blend_over(in_front, behind):
    return in_front + (1.0 - in_front[3])[None] * behind


def reference(density, bin_index, tf_colour, tf_extinction, slab_rank):
    padded_density = jnp.pad(density, 1)
    padded_bins = jnp.pad(bin_index, 1)
    colour_table = tf_colour.astype(jnp.float32)
    extinction = tf_extinction.astype(jnp.float32)
    places = jnp.arange(SLABS, dtype=jnp.int32)

    def slab_image(slab_number):
        start = (slab_number * VZ).astype(jnp.int32)
        dense_part = lax.dynamic_slice_in_dim(padded_density, start, VZ + 2, 0)
        bin_part = lax.dynamic_slice_in_dim(padded_bins, start, VZ + 2, 0)
        opacity = 1.0 - jnp.exp(-extinction[bin_part] * dense_part / NZ)
        colour_cells = jnp.concatenate([colour_table[:, bin_part] * opacity[None], opacity[None]], axis=0).astype(jnp.bfloat16)
        along_x = resample_axis(colour_cells.astype(jnp.float32), 3).astype(jnp.bfloat16)

        def add_sample(image_now, sample_index):
            centre = (sample_index // 2).astype(jnp.int32)
            parity = sample_index % 2
            layers = lax.dynamic_slice_in_dim(along_x, centre, 3, 1).astype(jnp.float32)
            lower_weight = jnp.where(parity == 0, 0.25, 0.0)
            upper_weight = jnp.where(parity == 1, 0.25, 0.0)
            mixed_layer = (lower_weight * layers[:, 0] + 0.75 * layers[:, 1] + upper_weight * layers[:, 2]).astype(jnp.bfloat16)
            sample = resample_axis(mixed_layer.astype(jnp.float32), 1)
            return blend_over(image_now, sample), None

        start_image = jnp.zeros((4, HEIGHT, WIDTH), jnp.float32)
        image_done, _ = lax.scan(add_sample, start_image, jnp.arange(SAMPLES, dtype=jnp.int32))
        return image_done

    def add_slab(composite, position):
        source = jnp.sum(jnp.where(slab_rank == position, places, 0)).astype(jnp.int32)
        return blend_over(composite, slab_image(source)), None

    start_frame = jnp.zeros((4, HEIGHT, WIDTH), jnp.float32)
    composite, _ = lax.scan(add_slab, start_frame, jnp.arange(SLABS, dtype=jnp.int32))
    return composite
```

```python
import jax
import jax.numpy as jnp
import numpy as np
from jax import lax
from jax.experimental import pallas as pl
from jax.experimental.pallas import tpu as pltpu
from jax.sharding import PartitionSpec as P


def with_halo(block, sides, width):
    for axis, dim in sides:
        count = lax.axis_size(axis)
        forward = [(i, i + 1) for i in range(count - 1)]
        backward = [(target, source) for source, target in forward]
        low = lax.ppermute(
            lax.slice_in_dim(block, block.shape[dim] - width, None, axis=dim), axis, forward
        )
        high = lax.ppermute(lax.slice_in_dim(block, 0, width, axis=dim), axis, backward)
        block = jnp.concatenate([low, block, high], axis=dim)
    return block


def partner_2(block, axis, stride):
    count = lax.axis_size(axis)
    route = []
    for low in range(count):
        high = low | 1 << stride
        if high != low and high < count:
            route += [(low, high), (high, low)]
    return lax.ppermute(block, axis, route)


def resample_table(length):
    row_index = lax.broadcasted_iota(jnp.int32, (2 * length, length + 2), 0)
    col_index = lax.broadcasted_iota(jnp.int32, (2 * length, length + 2), 1)
    centre = row_index // 2
    parity = row_index % 2
    weights_table = jnp.where(col_index == centre + 1, 0.75, 0.0)
    weights_table = weights_table + jnp.where((col_index == centre) & (parity == 0), 0.25, 0.0)
    weights_table = weights_table + jnp.where((col_index == centre + 2) & (parity == 1), 0.25, 0.0)
    return weights_table.astype(jnp.bfloat16)


def blend_over(in_front, behind):
    return in_front + (1.0 - in_front[3])[None] * behind


def classify(density, bin_index, tf_colour, tf_extinction, total_depth):
    depth_cells, height_cells, width_cells = density.shape
    lookup = jnp.concatenate([tf_colour, tf_extinction[None, :]], axis=0)
    table_size = lookup.shape[1]
    bin_rows = lax.broadcasted_iota(jnp.int32, (table_size, 1), 0)
    flat_bins = bin_index.reshape(depth_cells, height_cells * width_cells)
    flat_density = density.reshape(depth_cells, height_cells * width_cells)

    def one_layer(layer, result):
        layer_bins = lax.dynamic_index_in_dim(flat_bins, layer, 0, keepdims=True)
        layer_density = lax.dynamic_index_in_dim(flat_density, layer, 0, keepdims=False)
        one_hot = (layer_bins == bin_rows).astype(jnp.bfloat16)
        values = jnp.dot(lookup, one_hot, preferred_element_type=jnp.float32)
        opacity = 1.0 - jnp.exp(-values[3] * layer_density / total_depth)
        cells = jnp.concatenate([values[:3] * opacity[None], opacity[None]], axis=0).astype(
            jnp.bfloat16
        )
        return lax.dynamic_update_slice_in_dim(result, cells[:, None], layer, 1)

    start_cells = jnp.zeros((4, depth_cells, height_cells * width_cells), jnp.bfloat16)
    classified = lax.fori_loop(0, depth_cells, one_layer, start_cells)
    return classified.reshape(4, depth_cells, height_cells, width_cells)


def general_device(density, bin_index, tf_colour, tf_extinction, slab_rank):
    slab_count = lax.axis_size("bz")
    depth_cells, height_cells, width_cells = density.shape
    total_depth = float(depth_cells * slab_count)
    colour_cells = classify(density, bin_index, tf_colour, tf_extinction, total_depth)
    padded = with_halo(colour_cells, (("bz", 1), ("by", 2), ("bx", 3)), 1)
    along_x = jnp.einsum(
        "czyq,pq->czyp", padded, resample_table(width_cells), preferred_element_type=jnp.float32
    ).astype(jnp.bfloat16)
    y_table = resample_table(height_cells)

    def add_sample(sample_index, image_now):
        centre = sample_index // 2
        parity = sample_index % 2
        layers = lax.dynamic_slice_in_dim(along_x, centre, 3, 1).astype(jnp.float32)
        lower_weight = jnp.where(parity == 0, 0.25, 0.0)
        upper_weight = jnp.where(parity == 1, 0.25, 0.0)
        mixed_layer = (
            lower_weight * layers[:, 0] + 0.75 * layers[:, 1] + upper_weight * layers[:, 2]
        ).astype(jnp.bfloat16)
        sample = jnp.einsum("qy,cyp->cqp", y_table, mixed_layer, preferred_element_type=jnp.float32)
        return blend_over(image_now, sample)

    start_image = jnp.zeros((4, 2 * height_cells, 2 * width_cells), jnp.float32)
    slab_image = lax.fori_loop(0, 2 * depth_cells, add_sample, start_image)
    rows_piece = 2 * height_cells // slab_count
    my_index = lax.axis_index("bz")
    bit_levels = slab_count.bit_length() - 1
    composite = slab_image.reshape((4,) + (2,) * bit_levels + (rows_piece, 2 * width_cells))
    my_rank = lax.dynamic_index_in_dim(slab_rank, my_index, 0, keepdims=False)
    for level in range(bit_levels):
        position = bit_levels - level
        my_bit = my_index // 2**level % 2
        kept_half = lax.dynamic_index_in_dim(composite, my_bit, position, keepdims=False)
        outgoing = lax.dynamic_index_in_dim(composite, 1 - my_bit, position, keepdims=False)
        incoming = partner_2(outgoing, "bz", level)
        partner = my_index + (1 - 2 * my_bit) * 2**level
        partner_rank = lax.dynamic_index_in_dim(slab_rank, partner, 0, keepdims=False)
        mine_first = my_rank < partner_rank
        composite = blend_over(
            jnp.where(mine_first, kept_half, incoming), jnp.where(mine_first, incoming, kept_half)
        )
    return composite


LANES = 128
LEVELS = 65535.0


def pack_words(density, bins):
    level = (density * LEVELS + 0.5).astype(jnp.int32)
    return lax.shift_left(level, 16) | bins


def word_density(words):
    return lax.shift_right_logical(words, 16).astype(jnp.float32) * (1.0 / LEVELS)


def word_bins(words):
    return words & 0xFFFF


def cell_values(density, bins, tables, depth):
    low_bits = bins & (LANES - 1)
    upper = bins >= LANES

    def pick(channel):
        first, second = tables[channel]
        return jnp.where(
            upper,
            jnp.take_along_axis(second, low_bits, axis=1, mode="promise_in_bounds"),
            jnp.take_along_axis(first, low_bits, axis=1, mode="promise_in_bounds"),
        )

    opacity = 1.0 - jnp.exp(-pick(3) * density / depth)
    return [pick(0) * opacity, pick(1) * opacity, pick(2) * opacity, opacity]


def table_halves(colour_ref, extinction_ref, rows):
    colour = colour_ref[...].astype(jnp.float32)
    extinction = extinction_ref[...].astype(jnp.float32)
    result = []
    for channel in range(4):
        line = extinction if channel == 3 else colour[channel : channel + 1]
        result.append(
            [
                jnp.broadcast_to(line[:, half * LANES : (half + 1) * LANES], (rows, LANES))
                for half in range(2)
            ]
        )
    return result


def pack_kernel(
    density_ref, bins_ref, bulk_ref, first_ref, second_ref, columns_ref, own_ref, words_ref
):
    layers, rows, cols = density_ref.shape
    half = rows // 2
    me = lax.axis_index("bz")
    words_ref[...] = pack_words(density_ref[...], bins_ref[...])
    start = pl.multiple_of((1 - me) * half, half)
    row_at = lax.broadcasted_iota(jnp.int32, (rows, LANES), 0)
    lane_at = lax.broadcasted_iota(jnp.int32, (rows, LANES), 1)
    for z in range(layers):
        for part in range(half // 8):
            bulk_ref[z * (half // 8) + part] = words_ref[z, pl.ds(start + part * 8, 8), :]
        edge_rows = [words_ref[z, r : r + 1, :] for r in (0, half - 1, half, rows - 1)]
        front = me == 0
        bulk_ref[layers * (half // 8), z : z + 1, :] = jnp.where(front, edge_rows[1], edge_rows[2])
        own_ref[z : z + 1, :] = jnp.where(front, edge_rows[2], edge_rows[1])
        first_ref[z : z + 1, :] = jnp.where(front, edge_rows[3], edge_rows[0])
        second_ref[z : z + 1, :] = jnp.where(front, edge_rows[0], edge_rows[3])
        left = jnp.where(lane_at == row_at, words_ref[z, :, 0:1], 0)
        right = jnp.where(lane_at == row_at + rows, words_ref[z, :, cols - 1 : cols], 0)
        columns_ref[z : z + 1, :] = jnp.sum(left + right, axis=0, keepdims=True)


def pack(density, bin_index):
    layers, rows, cols = density.shape
    words = jnp.int32
    return pl.pallas_call(
        pack_kernel,
        out_shape=(
            jax.ShapeDtypeStruct((layers * (rows // 16) + 1, 8, cols), words),
            jax.ShapeDtypeStruct((layers, cols), words),
            jax.ShapeDtypeStruct((layers, cols), words),
            jax.ShapeDtypeStruct((layers, LANES), words),
            jax.ShapeDtypeStruct((layers, cols), words),
        ),
        scratch_shapes=[pltpu.VMEM((layers, rows, cols), words)],
        name="pack_cells",
    )(density, bin_index)


def render_kernel(
    rank_ref, density_ref, bins_ref, colour_ref, extinction_ref, weights_ref,
    bulk_ref, own_ref, first_ref, second_ref, columns_ref,
    out_ref, cells_ref, halo_ref, along_ref, edge_ref, lines_ref, mixed_ref,
):
    layers, rows, cols = density_ref.shape
    half = rows // 2
    parts = half // 8
    width = 2 * cols
    tiles = width // LANES
    slabs = 2
    depth = layers * slabs
    me, me_y, me_x = lax.axis_index("bz"), lax.axis_index("by"), lax.axis_index("bx")
    count_y, count_x = lax.axis_size("by"), lax.axis_size("bx")
    front = me == 0
    start = pl.multiple_of(me * half, half)
    total = float(depth)
    f32 = jnp.float32

    tables = table_halves(colour_ref, extinction_ref, 8)
    lane_at = lax.broadcasted_iota(jnp.int32, (8, LANES), 1)
    sub_at = lax.broadcasted_iota(jnp.int32, (8, LANES), 0)
    side_lane = lane_at & (rows - 1)
    has_side = lane_at < 2 * rows
    column_of_right = lane_at < rows

    near_y = jnp.where(front, me_y - 1, me_y + 1)
    for slab in range(slabs):
        for place in range(2):
            at_y = me_y if place == 0 else near_y
            in_y = (at_y >= 0) & (at_y < count_y)
            read_y = jnp.clip(at_y, 0, count_y - 1)
            row_base = (slab * count_y + read_y) * count_x
            right = columns_ref[row_base + jnp.minimum(me_x + 1, count_x - 1)]
            left = columns_ref[row_base + jnp.maximum(me_x - 1, 0)]
            right = jnp.where(in_y & (me_x + 1 < count_x), right, 0)
            left = jnp.where(in_y & (me_x > 0), left, 0)
            words = jnp.where(has_side, jnp.where(column_of_right, right, left), 0)
            values = cell_values(word_density(words), word_bins(words), tables, total)
            for channel in range(4):
                halo_ref[place, channel, pl.ds(slab * layers, layers), :] = values[channel]

    def store_cells(layer, part, tile, density, bins):
        values = cell_values(density, bins, tables, total)
        return values

    def classify_layer(z, carry, own):
        slab = me if own else 1 - me
        layer = slab * layers + z
        for tile in range(cols // LANES):
            lanes = pl.ds(tile * LANES, LANES)
            pieces = []
            for part in range(parts):
                if own:
                    density = density_ref[z, pl.ds(start + part * 8, 8), lanes]
                    bins = bins_ref[z, pl.ds(start + part * 8, 8), lanes]
                else:
                    words = bulk_ref[z * parts + part, :, lanes]
                    density, bins = word_density(words), word_bins(words)
                pieces.append(cell_values(density, bins, tables, total))
            for channel in range(4):
                block = jnp.concatenate([piece[channel] for piece in pieces], axis=0)
                base = pl.multiple_of((layer * 4 + channel) * half, half)
                cells_ref[pl.ds(base, half), lanes] = block.astype(jnp.bfloat16)
        for channel in range(4):
            line = halo_ref[0, channel, pl.ds(layer, 1), :]
            block = jnp.concatenate(
                [
                    jnp.where(
                        has_side & (side_lane == sub_at + start + part * 8),
                        jnp.broadcast_to(line, (8, LANES)),
                        0.0,
                    )
                    for part in range(parts)
                ],
                axis=0,
            )
            base = pl.multiple_of((layer * 4 + channel) * half, half)
            cells_ref[pl.ds(base, half), pl.ds(cols, LANES)] = block.astype(jnp.bfloat16)
        return carry

    lax.fori_loop(0, layers, lambda z, c: classify_layer(z, c, True), 0)
    lax.fori_loop(0, layers, lambda z, c: classify_layer(z, c, False), 0)

    edge_base = depth * 4 * half
    words_own_near = first_ref[...]
    words_other_near = second_ref[...]
    words_own_in = own_ref[...]
    words_other_in = bulk_ref[layers * parts]
    for slab in range(slabs):
        mine = me == slab
        near = jnp.where(mine, words_own_near, words_other_near)
        inside = jnp.where(mine, words_own_in, words_other_in)
        pair = [jnp.where(front, near, inside), jnp.where(front, inside, near)]
        for side in range(2):
            row = jnp.where(front, rows - 1, half - 1) if side == 0 else jnp.where(front, half, 0)
            from_near = front if side == 0 else jnp.logical_not(front)
            for tile in range(cols // LANES):
                words = pair[side][:, tile * LANES : (tile + 1) * LANES]
                values = cell_values(word_density(words), word_bins(words), tables, total)
                for channel in range(4):
                    edge_ref[side, channel, pl.ds(slab * layers, layers), pl.ds(tile * LANES, LANES)] = values[channel]
            for channel in range(4):
                line = jnp.where(
                    from_near,
                    halo_ref[1, channel, pl.ds(slab * layers, layers), :],
                    halo_ref[0, channel, pl.ds(slab * layers, layers), :],
                )
                edge_ref[side, channel, pl.ds(slab * layers, layers), pl.ds(cols, LANES)] = jnp.where(
                    has_side & (side_lane == row), line, 0.0
                )
    for side in range(2):
        for channel in range(4):
            base = edge_base + (side * 4 + channel) * depth
            cells_ref[pl.ds(base, depth), :] = edge_ref[side, channel].astype(jnp.bfloat16)

    chunk = 128
    pad = 4 * half

    def resample_x(index, carry):
        base = pl.multiple_of(index * chunk, chunk)
        result = jnp.dot(
            cells_ref[pl.ds(base, chunk), :], weights_ref[...], preferred_element_type=f32
        )
        result = result.astype(jnp.bfloat16).astype(f32)
        for tile in range(tiles):
            along_ref[tile, pl.ds(base + pad, chunk), :] = result[:, tile * LANES : (tile + 1) * LANES]
        return carry

    lax.fori_loop(0, (edge_base + 8 * depth) // chunk, resample_x, 0)

    layer_at = lax.broadcasted_iota(jnp.int32, (depth, LANES), 0)
    for tile in range(tiles):
        for side in range(2):
            for channel in range(4):
                base = pad + edge_base + (side * 4 + channel) * depth
                now = along_ref[tile, pl.ds(base, depth), :]
                before = jnp.where(layer_at == 0, 0.0, pltpu.roll(now, 1, 0))
                after = jnp.where(layer_at == depth - 1, 0.0, pltpu.roll(now, depth - 1, 0))
                for parity, other in enumerate((before, after)):
                    sample = (0.25 * other + 0.75 * now).astype(jnp.bfloat16).astype(f32)
                    lines_ref[tile, side, channel, parity] = 0.25 * sample

    for tile in range(tiles):
        along_ref[tile, pl.ds(0, pad), :] = jnp.zeros((pad, LANES), f32)
        along_ref[tile, pl.ds(pad + edge_base, pad), :] = jnp.zeros((pad, LANES), f32)

    top = sub_at == 0
    bottom = sub_at == 7

    def layer_rows(tile, layer, channel):
        base = pl.multiple_of(pad + (layer * 4 + channel) * half, half)
        return [along_ref[tile, pl.ds(base + part * 8, 8), :] for part in range(parts)]

    def over_layer(tile, layer, image):
        for parity in range(2):
            beside = layer - 1 + 2 * parity
            clear = [[1.0 - image[3][part][odd] for odd in range(2)] for part in range(parts)]
            updated = []
            for channel in range(4):
                here = layer_rows(tile, layer, channel)
                other = layer_rows(tile, beside, channel)
                mixed = [
                    (0.25 * other[part] + 0.75 * here[part]).astype(jnp.bfloat16).astype(f32)
                    for part in range(parts)
                ]
                quarter = [0.25 * value for value in mixed]
                centre = [0.75 * value for value in mixed]
                down = [pltpu.roll(value, 1, 0) for value in quarter]
                up = [pltpu.roll(value, 7, 0) for value in quarter]
                above = lines_ref[tile, 0, channel, parity, pl.ds(layer, 1), :]
                below = lines_ref[tile, 1, channel, parity, pl.ds(layer, 1), :]
                channel_image = []
                for part in range(parts):
                    upper = down[part - 1] if part > 0 else jnp.broadcast_to(above, (8, LANES))
                    lower = up[part + 1] if part + 1 < parts else jnp.broadcast_to(below, (8, LANES))
                    even = centre[part] + jnp.where(top, upper, down[part])
                    odd = centre[part] + jnp.where(bottom, lower, up[part])
                    channel_image.append(
                        [
                            image[channel][part][0] + clear[part][0] * even,
                            image[channel][part][1] + clear[part][1] * odd,
                        ]
                    )
                updated.append(channel_image)
            image = updated
        return image

    flip = rank_ref[0]

    def one_tile(tile, carry):
        def one_slab(position, image):
            slab = position ^ flip
            for z in range(layers):
                image = over_layer(tile, slab * layers + z, image)
            return image

        zero = jnp.zeros((8, LANES), f32)
        image = [[[zero, zero] for _ in range(parts)] for _ in range(4)]
        image = lax.fori_loop(0, slabs, one_slab, image)
        lanes = pl.ds(pl.multiple_of(tile * LANES, LANES), LANES)
        for channel in range(4):
            for part in range(parts):
                for odd in range(2):
                    mixed_ref[channel, pl.ds(part * 16 + odd, 8, stride=2), :] = image[channel][part][odd]
            out_ref[channel, :, lanes] = mixed_ref[channel]
        return carry

    lax.fori_loop(0, tiles, one_tile, 0)


def column_weights(cols, rows):
    table = np.zeros((cols + LANES, 2 * cols), np.float32)
    for c in range(cols):
        table[c, 2 * c : 2 * c + 2] = 0.75
        if c > 0:
            table[c - 1, 2 * c] = 0.25
        if c + 1 < cols:
            table[c + 1, 2 * c + 1] = 0.25
    table[cols : cols + rows, 2 * cols - 1] = 0.25
    table[cols + rows : cols + 2 * rows, 0] = 0.25
    return jnp.asarray(table, jnp.bfloat16)


def two_slab_device(density, bin_index, tf_colour, tf_extinction, slab_rank):
    layers, rows, cols = density.shape
    half = rows // 2
    depth = 2 * layers
    tiles = 2 * cols // LANES
    count_y, count_x = lax.axis_size("by"), lax.axis_size("bx")
    bulk, first, second, columns, own = pack(density, bin_index)

    def at(z, y):
        return z * count_y + y

    swap = [(0, 1), (1, 0)]
    same_slab = [(at(0, y), at(0, y + 1)) for y in range(count_y - 1)]
    same_slab += [(at(1, y + 1), at(1, y)) for y in range(count_y - 1)]
    other_slab = [(at(1, y), at(0, y + 1)) for y in range(count_y - 1)]
    other_slab += [(at(0, y + 1), at(1, y)) for y in range(count_y - 1)]
    columns = lax.all_gather(columns, ("bz", "by", "bx"))
    bulk = lax.ppermute(bulk, "bz", swap)
    first = lax.ppermute(first, ("bz", "by"), same_slab)
    second = lax.ppermute(second, ("bz", "by"), other_slab)
    f32 = jnp.float32
    vmem = pl.BlockSpec(memory_space=pltpu.VMEM)
    cell_rows = depth * 4 * half + 8 * depth
    return pl.pallas_call(
        render_kernel,
        out_shape=jax.ShapeDtypeStruct((4, rows, 2 * cols), f32),
        in_specs=[pl.BlockSpec(memory_space=pltpu.SMEM)] + [vmem] * 10,
        out_specs=vmem,
        scratch_shapes=[
            pltpu.VMEM((cell_rows, cols + LANES), jnp.bfloat16),
            pltpu.VMEM((2, 4, depth, LANES), f32),
            pltpu.VMEM((tiles, cell_rows + 8 * half, LANES), f32),
            pltpu.VMEM((2, 4, depth, cols + LANES), f32),
            pltpu.VMEM((tiles, 2, 4, 2, depth, LANES), f32),
            pltpu.VMEM((4, rows, LANES), f32),
        ],
        compiler_params=pltpu.CompilerParams(vmem_limit_bytes=32 * 1024 * 1024),
        name="render_block",
    )(
        slab_rank, density, bin_index, tf_colour, tf_extinction.reshape(1, -1),
        column_weights(cols, rows), bulk, own, first, second, columns,
    )


def on_device(density, bin_index, tf_colour, tf_extinction, slab_rank):
    if lax.axis_size("bz") == 2:
        return two_slab_device(density, bin_index, tf_colour, tf_extinction, slab_rank)
    return general_device(density, bin_index, tf_colour, tf_extinction, slab_rank)


def solution(mesh):
    return jax.shard_map(
        on_device,
        mesh=mesh,
        in_specs=(P("bz", "by", "bx"), P("bz", "by", "bx"), P(), P(), P()),
        out_specs=P(None, ("by", "bz"), "bx"),
        check_vma=False,
    )
```

```python
import jax
import jax.numpy as jnp
from jax import lax
from jax.experimental import pallas as pl
from jax.experimental.pallas import tpu as pltpu
from jax.sharding import PartitionSpec as P


def with_halo(block, sides, width):
    for axis, dim in sides:
        count = lax.axis_size(axis)
        forward = [(i, i + 1) for i in range(count - 1)]
        backward = [(target, source) for source, target in forward]
        low = lax.ppermute(
            lax.slice_in_dim(block, block.shape[dim] - width, None, axis=dim), axis, forward
        )
        high = lax.ppermute(lax.slice_in_dim(block, 0, width, axis=dim), axis, backward)
        block = jnp.concatenate([low, block, high], axis=dim)
    return block


def partner_2(block, axis, stride):
    count = lax.axis_size(axis)
    route = []
    for low in range(count):
        high = low | 1 << stride
        if high != low and high < count:
            route += [(low, high), (high, low)]
    return lax.ppermute(block, axis, route)


def resample_table(length):
    row_index = lax.broadcasted_iota(jnp.int32, (2 * length, length + 2), 0)
    col_index = lax.broadcasted_iota(jnp.int32, (2 * length, length + 2), 1)
    centre = row_index // 2
    parity = row_index % 2
    weights_table = jnp.where(col_index == centre + 1, 0.75, 0.0)
    weights_table = weights_table + jnp.where((col_index == centre) & (parity == 0), 0.25, 0.0)
    weights_table = weights_table + jnp.where((col_index == centre + 2) & (parity == 1), 0.25, 0.0)
    return weights_table.astype(jnp.bfloat16)


def blend_over(in_front, behind):
    return in_front + (1.0 - in_front[3])[None] * behind


def classify(density, bin_index, tf_colour, tf_extinction, total_depth):
    depth_cells, height_cells, width_cells = density.shape
    lookup = jnp.concatenate([tf_colour, tf_extinction[None, :]], axis=0)
    table_size = lookup.shape[1]
    bin_rows = lax.broadcasted_iota(jnp.int32, (table_size, 1), 0)
    flat_bins = bin_index.reshape(depth_cells, height_cells * width_cells)
    flat_density = density.reshape(depth_cells, height_cells * width_cells)

    def one_layer(layer, result):
        layer_bins = lax.dynamic_index_in_dim(flat_bins, layer, 0, keepdims=True)
        layer_density = lax.dynamic_index_in_dim(flat_density, layer, 0, keepdims=False)
        one_hot = (layer_bins == bin_rows).astype(jnp.bfloat16)
        values = jnp.dot(lookup, one_hot, preferred_element_type=jnp.float32)
        opacity = 1.0 - jnp.exp(-values[3] * layer_density / total_depth)
        cells = jnp.concatenate([values[:3] * opacity[None], opacity[None]], axis=0).astype(
            jnp.bfloat16
        )
        return lax.dynamic_update_slice_in_dim(result, cells[:, None], layer, 1)

    start_cells = jnp.zeros((4, depth_cells, height_cells * width_cells), jnp.bfloat16)
    classified = lax.fori_loop(0, depth_cells, one_layer, start_cells)
    return classified.reshape(4, depth_cells, height_cells, width_cells)


def general_device(density, bin_index, tf_colour, tf_extinction, slab_rank):
    slab_count = lax.axis_size("bz")
    depth_cells, height_cells, width_cells = density.shape
    total_depth = float(depth_cells * slab_count)
    colour_cells = classify(density, bin_index, tf_colour, tf_extinction, total_depth)
    padded = with_halo(colour_cells, (("bz", 1), ("by", 2), ("bx", 3)), 1)
    along_x = jnp.einsum(
        "czyq,pq->czyp", padded, resample_table(width_cells), preferred_element_type=jnp.float32
    ).astype(jnp.bfloat16)
    y_table = resample_table(height_cells)

    def add_sample(sample_index, image_now):
        centre = sample_index // 2
        parity = sample_index % 2
        layers = lax.dynamic_slice_in_dim(along_x, centre, 3, 1).astype(jnp.float32)
        lower_weight = jnp.where(parity == 0, 0.25, 0.0)
        upper_weight = jnp.where(parity == 1, 0.25, 0.0)
        mixed_layer = (
            lower_weight * layers[:, 0] + 0.75 * layers[:, 1] + upper_weight * layers[:, 2]
        ).astype(jnp.bfloat16)
        sample = jnp.einsum("qy,cyp->cqp", y_table, mixed_layer, preferred_element_type=jnp.float32)
        return blend_over(image_now, sample)

    start_image = jnp.zeros((4, 2 * height_cells, 2 * width_cells), jnp.float32)
    slab_image = lax.fori_loop(0, 2 * depth_cells, add_sample, start_image)
    rows_piece = 2 * height_cells // slab_count
    my_index = lax.axis_index("bz")
    bit_levels = slab_count.bit_length() - 1
    composite = slab_image.reshape((4,) + (2,) * bit_levels + (rows_piece, 2 * width_cells))
    my_rank = lax.dynamic_index_in_dim(slab_rank, my_index, 0, keepdims=False)
    for level in range(bit_levels):
        position = bit_levels - level
        my_bit = my_index // 2**level % 2
        kept_half = lax.dynamic_index_in_dim(composite, my_bit, position, keepdims=False)
        outgoing = lax.dynamic_index_in_dim(composite, 1 - my_bit, position, keepdims=False)
        incoming = partner_2(outgoing, "bz", level)
        partner = my_index + (1 - 2 * my_bit) * 2**level
        partner_rank = lax.dynamic_index_in_dim(slab_rank, partner, 0, keepdims=False)
        mine_first = my_rank < partner_rank
        composite = blend_over(
            jnp.where(mine_first, kept_half, incoming), jnp.where(mine_first, incoming, kept_half)
        )
    return composite


LANES = 128
LEVELS = 65535.0
VMEM = pl.BlockSpec(memory_space=pltpu.VMEM)


def pack_words(density, bins):
    level = (density * LEVELS + 0.5).astype(jnp.int32)
    return lax.shift_left(level, 16) | bins


def unpack_words(words):
    density = lax.shift_right_logical(words, 16).astype(jnp.float32) * (1.0 / LEVELS)
    return density, words & 0xFFFF


def cell_values(density, bins, tables, depth):
    low_bits = bins & (LANES - 1)
    upper = bins >= LANES

    def pick(channel):
        first, second = tables[channel]
        return jnp.where(
            upper,
            jnp.take_along_axis(second, low_bits, axis=1, mode="promise_in_bounds"),
            jnp.take_along_axis(first, low_bits, axis=1, mode="promise_in_bounds"),
        )

    opacity = (1.0 - jnp.exp(-pick(3) * density / depth)) * (1.0 / 64.0)
    return [pick(0) * opacity, pick(1) * opacity, pick(2) * opacity, opacity]


def table_halves(colour_ref, extinction_ref):
    colour = colour_ref[...].astype(jnp.float32)
    extinction = extinction_ref[...].astype(jnp.float32)
    result = []
    for channel in range(4):
        line = extinction if channel == 3 else colour[channel : channel + 1]
        result.append(
            [
                jnp.broadcast_to(line[:, half * LANES : (half + 1) * LANES], (8, LANES))
                for half in range(2)
            ]
        )
    return result


def cost(microseconds):
    return pl.CostEstimate(
        flops=0, bytes_accessed=int(3.6e6 * microseconds), transcendentals=0
    )


def columns_kernel(density_hbm, bins_hbm, columns_ref, density_ref, bins_ref, sems):
    layers, rows, cols = density_ref.shape
    copies = [
        pltpu.make_async_copy(density_hbm, density_ref, sems.at[0]),
        pltpu.make_async_copy(bins_hbm, bins_ref, sems.at[1]),
    ]
    for copy in copies:
        copy.start()
    for copy in copies:
        copy.wait()
    row_at = lax.broadcasted_iota(jnp.int32, (rows, LANES), 0)
    lane_at = lax.broadcasted_iota(jnp.int32, (rows, LANES), 1)
    for z in range(layers):
        first = pack_words(density_ref[z, :, 0:1], bins_ref[z, :, 0:1])
        last = pack_words(density_ref[z, :, cols - 1 : cols], bins_ref[z, :, cols - 1 : cols])
        line = jnp.where(lane_at == row_at, first, 0) + jnp.where(lane_at == row_at + rows, last, 0)
        columns_ref[z : z + 1, :] = jnp.sum(line, axis=0, keepdims=True)


def pack_kernel(density_ref, bins_ref, bulk_ref, edges_ref, words_ref):
    layers, rows, cols = density_ref.shape
    half = rows // 2
    front = lax.axis_index("bz") == 0
    start = pl.multiple_of(jnp.where(front, half, 0), half)
    for z in range(layers):
        words = pack_words(
            density_ref[z, pl.ds(start, half), :], bins_ref[z, pl.ds(start, half), :]
        )
        for tile in range(cols // LANES):
            lanes = slice(tile * LANES, (tile + 1) * LANES)
            words_ref[z, tile] = words[:, lanes]
            for part in range(2):
                bulk_ref[2 * z + part, :, lanes] = words_ref[z, tile, pl.ds(part, 8, stride=2), :]
        line = [
            pack_words(density_ref[z, r : r + 1, :], bins_ref[z, r : r + 1, :])
            for r in (0, half - 1, half, rows - 1)
        ]
        bulk_ref[2 * layers, z : z + 1, :] = jnp.where(front, line[1], line[2])
        edges_ref[0, z : z + 1, :] = jnp.where(front, line[2], line[1])
        edges_ref[1, z : z + 1, :] = jnp.where(front, line[0], line[3])


def diagonal_kernel(bulk_ref, edges_ref, halo_ref, weights_ref, line_ref):
    layers = edges_ref.shape[1]
    cols = edges_ref.shape[2]
    front = lax.axis_index("bz") == 0
    other = jnp.concatenate(
        [
            jnp.where(front, bulk_ref[2 * z, 0:1, :], bulk_ref[2 * z + 1, 7:8, :])
            for z in range(layers)
        ],
        axis=0,
    )
    mine = edges_ref[1]
    line_ref[0] = jnp.where(front, mine, other)
    line_ref[1] = jnp.where(front, other, mine)
    halo = halo_ref[...]
    halo_other = bulk_ref[2 * layers + 1, :, 0:LANES]
    line_ref[2, :, 0:LANES] = jnp.where(front, halo, halo_other)
    line_ref[2, :, LANES : 2 * LANES] = jnp.where(front, halo_other, halo)


def fill_weights(weights_ref, rows):
    cols = weights_ref.shape[0] - LANES
    row = lax.broadcasted_iota(jnp.int32, (cols, 2 * cols), 0)
    at = lax.broadcasted_iota(jnp.int32, (cols, 2 * cols), 1)
    centre = lax.shift_right_logical(at, 1)
    beside = centre - 1 + 2 * (at & 1)
    weights_ref[0:cols, :] = jnp.where(
        row == centre, 3.0, jnp.where(row == beside, 1.0, 0.0)
    ).astype(jnp.bfloat16)
    row = lax.broadcasted_iota(jnp.int32, (LANES, 2 * cols), 0)
    at = lax.broadcasted_iota(jnp.int32, (LANES, 2 * cols), 1)
    right = (row < rows) & (at == 2 * cols - 1)
    left = (row >= rows) & (row < 2 * rows) & (at == 0)
    weights_ref[cols : cols + LANES, :] = jnp.where(right | left, 1.0, 0.0).astype(jnp.bfloat16)


def lane_maps(rows):
    lane_at = lax.broadcasted_iota(jnp.int32, (8, LANES), 1)
    sub_at = lax.broadcasted_iota(jnp.int32, (8, LANES), 0)
    return lane_at & (rows - 1), lane_at < 2 * rows, sub_at


def along_columns(read_cells, halo_words, tables, weights_ref, cells_ref, values_ref, store, rows, layers, cols):
    total = float(2 * layers)
    start = lax.axis_index("bz") * (rows // 2)
    side_lane, has_side, sub_at = lane_maps(rows)
    halo = cell_values(*unpack_words(halo_words), tables, total)
    for channel in range(4):
        values_ref[channel] = halo[channel]
    for z in range(layers):
        for tile in range(cols // LANES):
            even = cell_values(*read_cells(z, 0, tile), tables, total)
            odd = cell_values(*read_cells(z, 1, tile), tables, total)
            for channel in range(4):
                base = (z * 4 + channel) * 16
                block = jnp.concatenate([even[channel], odd[channel]], axis=0)
                cells_ref[base : base + 16, tile * LANES : (tile + 1) * LANES] = block.astype(jnp.bfloat16)
        for channel in range(4):
            base = (z * 4 + channel) * 16
            line = jnp.broadcast_to(values_ref[channel, z : z + 1, :], (8, LANES))
            block = jnp.concatenate(
                [
                    jnp.where(has_side & (side_lane == start + 2 * sub_at + part), line, 0.0)
                    for part in range(2)
                ],
                axis=0,
            )
            cells_ref[base : base + 16, cols : cols + LANES] = block.astype(jnp.bfloat16)
    result = jnp.dot(cells_ref[...], weights_ref[...], preferred_element_type=jnp.float32)
    result = result.astype(jnp.bfloat16).astype(jnp.float32)
    for tile in range(2 * cols // LANES):
        store(tile, result[:, tile * LANES : (tile + 1) * LANES])


def own_kernel(
    density_ref, bins_ref, colour_ref, extinction_ref, halo_ref,
    along_ref, weights_ref, cells_ref, values_ref, rows_ref, binrows_ref,
):
    layers, rows, cols = density_ref.shape
    half = rows // 2
    start = pl.multiple_of(lax.axis_index("bz") * half, half)
    fill_weights(weights_ref, rows)
    tables = table_halves(colour_ref, extinction_ref)
    for z in range(layers):
        for tile in range(cols // LANES):
            lanes = slice(tile * LANES, (tile + 1) * LANES)
            rows_ref[z, tile] = density_ref[z, pl.ds(start, half), lanes]
            binrows_ref[z, tile] = bins_ref[z, pl.ds(start, half), lanes]

    def read_cells(z, part, tile):
        at = pl.ds(part, 8, stride=2)
        return rows_ref[z, tile, at, :], binrows_ref[z, tile, at, :]

    def store(tile, block):
        along_ref[tile] = block

    along_columns(
        read_cells, halo_ref[...], tables, weights_ref, cells_ref, values_ref, store, rows, layers, cols
    )


def other_kernel(
    bulk_ref, colour_ref, extinction_ref, weights_ref, own_ref,
    along_ref, cells_ref, values_ref,
):
    layers = (bulk_ref.shape[0] - 2) // 2
    cols = bulk_ref.shape[2]
    size = own_ref.shape[1]
    rows = 32
    me = lax.axis_index("bz")
    tables = table_halves(colour_ref, extinction_ref)
    pad = size // layers
    mine = pl.multiple_of(pad + me * size, pad)
    theirs = pl.multiple_of(pad + (1 - me) * size, pad)
    for tile in range(own_ref.shape[0]):
        along_ref[tile, 0:pad, :] = jnp.zeros((pad, LANES), jnp.float32)
        along_ref[tile, pad + 2 * size : 2 * pad + 2 * size, :] = jnp.zeros((pad, LANES), jnp.float32)
        along_ref[tile, pl.ds(mine, size), :] = own_ref[tile]

    def read_cells(z, part, tile):
        return unpack_words(bulk_ref[2 * z + part, :, tile * LANES : (tile + 1) * LANES])

    def store(tile, block):
        along_ref[tile, pl.ds(theirs, size), :] = block

    along_columns(
        read_cells, bulk_ref[2 * layers + 1, :, 0:LANES], tables, weights_ref, cells_ref, values_ref,
        store, rows, layers, cols,
    )


def render_kernel(
    rank_ref, colour_ref, extinction_ref, weights_ref, bulk_ref, edges_ref, halo_ref, near_ref, along_ref,
    out_ref, cells_ref, lines_ref, mixed_ref,
):
    layers, cols = edges_ref.shape[1:]
    depth = 2 * layers
    rows = out_ref.shape[1]
    half = rows // 2
    tiles = 2 * cols // LANES
    total = float(depth)
    f32 = jnp.float32
    me = lax.axis_index("bz")
    front = me == 0
    tables = table_halves(colour_ref, extinction_ref)
    side_lane, has_side, sub_at = lane_maps(rows)

    for slab in range(2):
        mine = me == slab
        inside = jnp.where(mine, edges_ref[0], bulk_ref[2 * layers])
        halo_inside = jnp.where(mine, halo_ref[...], bulk_ref[2 * layers + 1, :, 0:LANES])
        near = near_ref[slab]
        halo_near = near_ref[2, :, slab * LANES : (slab + 1) * LANES]
        for side in range(2):
            row = jnp.where(front, rows - 1, half - 1) if side == 0 else jnp.where(front, half, 0)
            use_near = front if side == 0 else jnp.logical_not(front)
            words = jnp.where(use_near, near, inside)
            halo = jnp.where(use_near, halo_near, halo_inside)
            base = side * 4 * depth + slab * layers
            blocks = [
                cell_values(*unpack_words(words[:, t * LANES : (t + 1) * LANES]), tables, total)
                for t in range(cols // LANES)
            ]
            values = cell_values(*unpack_words(halo), tables, total)
            blocks.append([jnp.where(has_side & (side_lane == row), value, 0.0) for value in values])
            for channel in range(4):
                for t, block in enumerate(blocks):
                    cells_ref[
                        base + channel * depth : base + channel * depth + layers,
                        t * LANES : (t + 1) * LANES,
                    ] = block[channel]
    edge = jnp.dot(
        cells_ref[...].astype(jnp.bfloat16), weights_ref[...], preferred_element_type=f32
    )
    edge = edge.astype(jnp.bfloat16).astype(f32)
    layer_at = lax.broadcasted_iota(jnp.int32, (depth, LANES), 0)
    for tile in range(tiles):
        for side in range(2):
            for channel in range(4):
                base = (side * 4 + channel) * depth
                now = edge[base : base + depth, tile * LANES : (tile + 1) * LANES]
                triple = 3.0 * now
                before = jnp.where(layer_at == 0, 0.0, pltpu.roll(now, 1, 0))
                after = jnp.where(layer_at == depth - 1, 0.0, pltpu.roll(now, depth - 1, 0))
                for parity, beside in enumerate((before, after)):
                    lines_ref[tile, side, channel, parity] = (
                        (beside + triple).astype(jnp.bfloat16).astype(f32)
                    )

    top = sub_at == 0
    bottom = sub_at == 7

    def layer_rows(tile, layer, channel):
        base = pl.multiple_of((layer * 4 + channel) * 16, 16)
        return [along_ref[tile, pl.ds(base + part * 8, 8), :] for part in range(2)]

    def over_layer(tile, layer, image):
        here = [layer_rows(tile, layer + 1, channel) for channel in range(4)]
        triple = [[3.0 * value for value in pair] for pair in here]
        for parity in range(2):
            clear = [1.0 - value for value in image[3]]
            updated = []
            for channel in range(4):
                beside = layer_rows(tile, layer + 2 * parity, channel)
                even, odd = [
                    (beside[part] + triple[channel][part]).astype(jnp.bfloat16).astype(f32)
                    for part in range(2)
                ]
                above = lines_ref[tile, 0, channel, parity, pl.ds(layer, 1), :]
                below = lines_ref[tile, 1, channel, parity, pl.ds(layer, 1), :]
                before_even = jnp.where(top, jnp.broadcast_to(above, (8, LANES)), pltpu.roll(odd, 1, 0))
                after_odd = jnp.where(bottom, jnp.broadcast_to(below, (8, LANES)), pltpu.roll(even, 7, 0))
                even_centre = 3.0 * even
                odd_centre = 3.0 * odd
                samples = [
                    before_even + even_centre, even_centre + odd, even + odd_centre, odd_centre + after_odd
                ]
                updated.append(
                    [image[channel][i] + clear[i] * samples[i] for i in range(4)]
                )
            image = updated
        return image

    flip = rank_ref[0]

    def one_tile(tile, carry):
        def one_slab(position, image):
            slab = position ^ flip
            for z in range(layers):
                image = over_layer(tile, slab * layers + z, image)
            return image

        zero = jnp.zeros((8, LANES), f32)
        image = [[zero] * 4 for _ in range(4)]
        image = lax.fori_loop(0, 2, one_slab, image)
        lanes = pl.ds(pl.multiple_of(tile * LANES, LANES), LANES)
        for channel in range(4):
            for i in range(4):
                mixed_ref[channel, pl.ds(i, 8, stride=4), :] = image[channel][i]
            out_ref[channel, :, lanes] = mixed_ref[channel]
        return carry

    lax.fori_loop(0, tiles, one_tile, 0)


def two_slab_device(density, bin_index, tf_colour, tf_extinction, slab_rank):
    layers, rows, cols = density.shape
    half = rows // 2
    tiles = 2 * cols // LANES
    size = layers * 4 * half
    count_y, count_x = lax.axis_size("by"), lax.axis_size("bx")
    f32, bf16, i32 = jnp.float32, jnp.bfloat16, jnp.int32
    extinction = tf_extinction.reshape(1, -1)
    params = pltpu.CompilerParams(vmem_limit_bytes=16 * 1024 * 1024)

    hbm = pl.BlockSpec(memory_space=pltpu.HBM)
    density = pltpu.with_memory_space_constraint(density, pltpu.HBM)
    bin_index = pltpu.with_memory_space_constraint(bin_index, pltpu.HBM)
    columns, density, bin_index = pl.pallas_call(
        columns_kernel,
        out_shape=(
            pltpu.VMEM((layers, LANES), i32),
            pltpu.VMEM(density.shape, f32),
            pltpu.VMEM(density.shape, i32),
        ),
        in_specs=[hbm] * 2,
        out_specs=(VMEM,) * 3,
        scratch_shapes=[pltpu.SemaphoreType.DMA((2,))],
        compiler_params=params,
        cost_estimate=cost(1.0),
        name="pack_columns",
    )(density, bin_index)

    pairs = [(x, x + 1) for x in range(0, count_x - 1, 2)]
    cross = [(x, x + 1) for x in range(1, count_x - 1, 2)]

    def both(route):
        return route + [(target, source) for source, target in route]

    across = lax.ppermute(columns, "bx", both(cross))
    beside = lax.ppermute(columns, "bx", both(pairs))
    bulk, edges = pl.pallas_call(
        pack_kernel,
        out_shape=(pltpu.VMEM((2 * layers + 1, 8, cols), i32), pltpu.VMEM((2, layers, cols), i32)),
        in_specs=[VMEM] * 2,
        out_specs=(VMEM, VMEM),
        scratch_shapes=[pltpu.VMEM((layers, cols // LANES, half, LANES), i32)],
        compiler_params=params,
        cost_estimate=cost(0.7),
        name="pack_block",
    )(density, bin_index)
    lane_at = lax.broadcasted_iota(i32, (layers, LANES), 1)
    right_is_beside = lax.axis_index("bx") % 2 == 0
    halo = jnp.where((lane_at < rows) == right_is_beside, beside, across)
    bulk = jnp.concatenate([bulk, jnp.concatenate([halo] * (cols // LANES), axis=1)[None]], axis=0)
    bulk = lax.ppermute(bulk, "bz", [(0, 1), (1, 0)])

    along, weights = pl.pallas_call(
        own_kernel,
        out_shape=(pltpu.VMEM((tiles, size, LANES), f32), pltpu.VMEM((cols + LANES, 2 * cols), bf16)),
        in_specs=[VMEM] * 5,
        out_specs=(VMEM, VMEM),
        scratch_shapes=[
            pltpu.VMEM((size, cols + LANES), bf16),
            pltpu.VMEM((4, layers, LANES), f32),
            pltpu.VMEM((layers, cols // LANES, half, LANES), f32),
            pltpu.VMEM((layers, cols // LANES, half, LANES), i32),
        ],
        compiler_params=params,
        cost_estimate=cost(2.0),
        name="own_slab",
    )(density, bin_index, tf_colour, extinction, halo)

    line = pl.pallas_call(
        diagonal_kernel,
        out_shape=pltpu.VMEM((3, layers, cols), i32),
        in_specs=[VMEM] * 4,
        out_specs=VMEM,
        compiler_params=params,
        cost_estimate=cost(0.2),
        name="diagonal_line",
    )(bulk, edges, halo, weights)
    route = [(count_y + y, y + 1) for y in range(count_y - 1)]
    near = lax.ppermute(line, ("bz", "by"), both(route))

    along = pl.pallas_call(
        other_kernel,
        out_shape=pltpu.VMEM((tiles, 2 * size + 2 * 4 * half, LANES), f32),
        in_specs=[VMEM] * 5,
        out_specs=VMEM,
        scratch_shapes=[
            pltpu.VMEM((size, cols + LANES), bf16),
            pltpu.VMEM((4, layers, LANES), f32),
        ],
        compiler_params=params,
        cost_estimate=cost(2.0),
        name="other_slab",
    )(bulk, tf_colour, extinction, weights, along)

    return pl.pallas_call(
        render_kernel,
        out_shape=jax.ShapeDtypeStruct((4, rows, 2 * cols), f32),
        in_specs=[pl.BlockSpec(memory_space=pltpu.SMEM)] + [VMEM] * 8,
        out_specs=VMEM,
        scratch_shapes=[
            pltpu.VMEM((8 * 2 * layers, cols + LANES), f32),
            pltpu.VMEM((tiles, 2, 4, 2, 2 * layers, LANES), f32),
            pltpu.VMEM((4, rows, LANES), f32),
        ],
        compiler_params=params,
        cost_estimate=cost(5.0),
        name="render_rows",
    )(slab_rank, tf_colour, extinction, weights, bulk, edges, halo, near, along)


def on_device(density, bin_index, tf_colour, tf_extinction, slab_rank):
    if lax.axis_size("bz") == 2:
        return two_slab_device(density, bin_index, tf_colour, tf_extinction, slab_rank)
    return general_device(density, bin_index, tf_colour, tf_extinction, slab_rank)


def solution(mesh):
    return jax.shard_map(
        on_device,
        mesh=mesh,
        in_specs=(P("bz", "by", "bx"), P("bz", "by", "bx"), P(), P(), P()),
        out_specs=P(None, ("by", "bz"), "bx"),
        check_vma=False,
    )
```

```python
import functools

import jax
import jax.numpy as jnp
from jax import lax
from jax.experimental import pallas as pl
from jax.experimental.pallas import tpu as pltpu
from jax.sharding import PartitionSpec as P


def with_halo(block, sides, width):
    for axis, dim in sides:
        count = lax.axis_size(axis)
        forward = [(i, i + 1) for i in range(count - 1)]
        backward = [(target, source) for source, target in forward]
        low = lax.ppermute(
            lax.slice_in_dim(block, block.shape[dim] - width, None, axis=dim), axis, forward
        )
        high = lax.ppermute(lax.slice_in_dim(block, 0, width, axis=dim), axis, backward)
        block = jnp.concatenate([low, block, high], axis=dim)
    return block


def partner_2(block, axis, stride):
    count = lax.axis_size(axis)
    route = []
    for low in range(count):
        high = low | 1 << stride
        if high != low and high < count:
            route += [(low, high), (high, low)]
    return lax.ppermute(block, axis, route)


def resample_table(length):
    row_index = lax.broadcasted_iota(jnp.int32, (2 * length, length + 2), 0)
    col_index = lax.broadcasted_iota(jnp.int32, (2 * length, length + 2), 1)
    centre = row_index // 2
    parity = row_index % 2
    weights_table = jnp.where(col_index == centre + 1, 0.75, 0.0)
    weights_table = weights_table + jnp.where((col_index == centre) & (parity == 0), 0.25, 0.0)
    weights_table = weights_table + jnp.where((col_index == centre + 2) & (parity == 1), 0.25, 0.0)
    return weights_table.astype(jnp.bfloat16)


def blend_over(in_front, behind):
    return in_front + (1.0 - in_front[3])[None] * behind


def classify(density, bin_index, tf_colour, tf_extinction, total_depth):
    depth_cells, height_cells, width_cells = density.shape
    lookup = jnp.concatenate([tf_colour, tf_extinction[None, :]], axis=0)
    table_size = lookup.shape[1]
    bin_rows = lax.broadcasted_iota(jnp.int32, (table_size, 1), 0)
    flat_bins = bin_index.reshape(depth_cells, height_cells * width_cells)
    flat_density = density.reshape(depth_cells, height_cells * width_cells)

    def one_layer(layer, result):
        layer_bins = lax.dynamic_index_in_dim(flat_bins, layer, 0, keepdims=True)
        layer_density = lax.dynamic_index_in_dim(flat_density, layer, 0, keepdims=False)
        one_hot = (layer_bins == bin_rows).astype(jnp.bfloat16)
        values = jnp.dot(lookup, one_hot, preferred_element_type=jnp.float32)
        opacity = 1.0 - jnp.exp(-values[3] * layer_density / total_depth)
        cells = jnp.concatenate([values[:3] * opacity[None], opacity[None]], axis=0).astype(
            jnp.bfloat16
        )
        return lax.dynamic_update_slice_in_dim(result, cells[:, None], layer, 1)

    start_cells = jnp.zeros((4, depth_cells, height_cells * width_cells), jnp.bfloat16)
    classified = lax.fori_loop(0, depth_cells, one_layer, start_cells)
    return classified.reshape(4, depth_cells, height_cells, width_cells)


def general_device(density, bin_index, tf_colour, tf_extinction, slab_rank):
    slab_count = lax.axis_size("bz")
    depth_cells, height_cells, width_cells = density.shape
    total_depth = float(depth_cells * slab_count)
    colour_cells = classify(density, bin_index, tf_colour, tf_extinction, total_depth)
    padded = with_halo(colour_cells, (("bz", 1), ("by", 2), ("bx", 3)), 1)
    along_x = jnp.einsum(
        "czyq,pq->czyp", padded, resample_table(width_cells), preferred_element_type=jnp.float32
    ).astype(jnp.bfloat16)
    y_table = resample_table(height_cells)

    def add_sample(sample_index, image_now):
        centre = sample_index // 2
        parity = sample_index % 2
        layers = lax.dynamic_slice_in_dim(along_x, centre, 3, 1).astype(jnp.float32)
        lower_weight = jnp.where(parity == 0, 0.25, 0.0)
        upper_weight = jnp.where(parity == 1, 0.25, 0.0)
        mixed_layer = (
            lower_weight * layers[:, 0] + 0.75 * layers[:, 1] + upper_weight * layers[:, 2]
        ).astype(jnp.bfloat16)
        sample = jnp.einsum("qy,cyp->cqp", y_table, mixed_layer, preferred_element_type=jnp.float32)
        return blend_over(image_now, sample)

    start_image = jnp.zeros((4, 2 * height_cells, 2 * width_cells), jnp.float32)
    slab_image = lax.fori_loop(0, 2 * depth_cells, add_sample, start_image)
    rows_piece = 2 * height_cells // slab_count
    my_index = lax.axis_index("bz")
    bit_levels = slab_count.bit_length() - 1
    composite = slab_image.reshape((4,) + (2,) * bit_levels + (rows_piece, 2 * width_cells))
    my_rank = lax.dynamic_index_in_dim(slab_rank, my_index, 0, keepdims=False)
    for level in range(bit_levels):
        position = bit_levels - level
        my_bit = my_index // 2**level % 2
        kept_half = lax.dynamic_index_in_dim(composite, my_bit, position, keepdims=False)
        outgoing = lax.dynamic_index_in_dim(composite, 1 - my_bit, position, keepdims=False)
        incoming = partner_2(outgoing, "bz", level)
        partner = my_index + (1 - 2 * my_bit) * 2**level
        partner_rank = lax.dynamic_index_in_dim(slab_rank, partner, 0, keepdims=False)
        mine_first = my_rank < partner_rank
        composite = blend_over(
            jnp.where(mine_first, kept_half, incoming), jnp.where(mine_first, incoming, kept_half)
        )
    return composite


LANES = 128
LEVELS = 65535.0
VMEM = pl.BlockSpec(memory_space=pltpu.VMEM)


def pack_words(density, bins):
    level = (density * LEVELS + 0.5).astype(jnp.int32)
    return lax.shift_left(level, 16) | bins


def unpack_words(words):
    density = lax.shift_right_logical(words, 16).astype(jnp.float32) * (1.0 / LEVELS)
    return density, words & 0xFFFF


def cell_values(density, bins, tables, depth):
    low_bits = bins & (LANES - 1)
    upper = bins >= LANES

    def pick(channel):
        first, second = tables[channel]
        return jnp.where(
            upper,
            jnp.take_along_axis(second, low_bits, axis=1, mode="promise_in_bounds"),
            jnp.take_along_axis(first, low_bits, axis=1, mode="promise_in_bounds"),
        )

    opacity = (1.0 - jnp.exp(-pick(3) * density / depth)) * (1.0 / 64.0)
    return [pick(0) * opacity, pick(1) * opacity, pick(2) * opacity, opacity]


def read_tables(tables_ref):
    return [[tables_ref[2 * channel + half] for half in range(2)] for channel in range(4)]


def cost(microseconds):
    return pl.CostEstimate(
        flops=0, bytes_accessed=int(3.6e6 * microseconds), transcendentals=0
    )


def columns_kernel(
    density_ref, bins_ref, colour_ref, extinction_ref, columns_ref, dense_ref, index_ref, tables_ref
):
    layers, rows, cols = density_ref.shape
    row_at = lax.broadcasted_iota(jnp.int32, (rows, LANES), 0)
    lane_at = lax.broadcasted_iota(jnp.int32, (rows, LANES), 1)
    for z in range(layers):
        first = pack_words(density_ref[z, :, 0:1], bins_ref[z, :, 0:1])
        last = pack_words(density_ref[z, :, cols - 1 : cols], bins_ref[z, :, cols - 1 : cols])
        line = jnp.where(lane_at == row_at, first, 0) + jnp.where(lane_at == row_at + rows, last, 0)
        columns_ref[z : z + 1, :] = jnp.sum(line, axis=0, keepdims=True)
        for tile in range(cols // LANES):
            lanes = slice(tile * LANES, (tile + 1) * LANES)
            dense_ref[z, tile] = density_ref[z, :, lanes]
            index_ref[z, tile] = bins_ref[z, :, lanes]
    colour = colour_ref[...].astype(jnp.float32)
    extinction = extinction_ref[...].astype(jnp.float32).reshape(1, 2 * LANES)
    for channel in range(4):
        line = extinction if channel == 3 else colour[channel : channel + 1]
        for half in range(2):
            tables_ref[2 * channel + half] = jnp.broadcast_to(
                line[:, half * LANES : (half + 1) * LANES], (8, LANES)
            )


def pack_kernel(
    dense_ref, index_ref, beside_ref, across_ref, cells_ref, bulk_ref, edges_ref, halo_ref
):
    layers, tiles, rows = dense_ref.shape[:3]
    half = rows // 2
    front = lax.axis_index("bz") == 0
    start = jnp.where(front, half, 0)
    me_x = lax.axis_index("bx")
    lane_at = lax.broadcasted_iota(jnp.int32, (layers, LANES), 1)
    even_x = lax.rem(me_x, 2) == 0
    right = jnp.where(even_x, beside_ref[...], across_ref[...])
    left = jnp.where(even_x, across_ref[...], beside_ref[...])
    right = jnp.where(me_x + 1 < lax.axis_size("bx"), right, 0)
    left = jnp.where(me_x > 0, left, 0)
    halo = jnp.where(lane_at < rows, right, jnp.where(lane_at < 2 * rows, left, 0))
    halo_ref[...] = halo
    for tile in range(tiles):
        lanes = slice(tile * LANES, (tile + 1) * LANES)
        bulk_ref[2 * layers + 1, :, lanes] = halo
        for z in range(layers):
            for part in range(2):
                at = pl.ds(start + part, half // 2, stride=2)
                bulk_ref[2 * z + part, :, lanes] = pack_words(
                    dense_ref[z, tile, at, :], index_ref[z, tile, at, :]
                )
            line = [
                pack_words(dense_ref[z, tile, r : r + 1, :], index_ref[z, tile, r : r + 1, :])
                for r in (0, half - 1, half, rows - 1)
            ]
            bulk_ref[2 * layers, z : z + 1, lanes] = jnp.where(front, line[1], line[2])
            edges_ref[0, z : z + 1, lanes] = jnp.where(front, line[2], line[1])
            edges_ref[1, z : z + 1, lanes] = jnp.where(front, line[0], line[3])


def diagonal_kernel(bulk_ref, edges_ref, halo_ref, along_ref, line_ref):
    layers = edges_ref.shape[1]
    front = lax.axis_index("bz") == 0
    other = jnp.concatenate(
        [
            jnp.where(front, bulk_ref[2 * z, 0:1, :], bulk_ref[2 * z + 1, 7:8, :])
            for z in range(layers)
        ],
        axis=0,
    )
    mine = edges_ref[1]
    line_ref[0] = jnp.where(front, mine, other)
    line_ref[1] = jnp.where(front, other, mine)
    halo = halo_ref[...]
    halo_other = bulk_ref[2 * layers + 1, :, 0:LANES]
    line_ref[2, :, 0:LANES] = jnp.where(front, halo, halo_other)
    line_ref[2, :, LANES : 2 * LANES] = jnp.where(front, halo_other, halo)


def fill_weights(weights_ref, rows):
    cols = weights_ref.shape[0] - LANES
    row = lax.broadcasted_iota(jnp.int32, (cols, 2 * cols), 0)
    at = lax.broadcasted_iota(jnp.int32, (cols, 2 * cols), 1)
    centre = lax.shift_right_logical(at, 1)
    beside = centre - 1 + 2 * (at & 1)
    weights_ref[0:cols, :] = jnp.where(
        row == centre, 3.0, jnp.where(row == beside, 1.0, 0.0)
    ).astype(jnp.bfloat16)
    row = lax.broadcasted_iota(jnp.int32, (LANES, 2 * cols), 0)
    at = lax.broadcasted_iota(jnp.int32, (LANES, 2 * cols), 1)
    right = (row < rows) & (at == 2 * cols - 1)
    left = (row >= rows) & (row < 2 * rows) & (at == 0)
    weights_ref[cols : cols + LANES, :] = jnp.where(right | left, 1.0, 0.0).astype(jnp.bfloat16)


def lane_maps(rows):
    lane_at = lax.broadcasted_iota(jnp.int32, (8, LANES), 1)
    sub_at = lax.broadcasted_iota(jnp.int32, (8, LANES), 0)
    return lane_at & (rows - 1), lane_at < 2 * rows, sub_at


def classify_rows(read_cells, tables, cells_ref, layers, tiles):
    total = float(2 * layers)
    for z in range(layers):
        for tile in range(tiles):
            even = cell_values(*read_cells(z, 0, tile), tables, total)
            odd = cell_values(*read_cells(z, 1, tile), tables, total)
            for channel in range(4):
                base = (z * 4 + channel) * 16
                block = jnp.concatenate([even[channel], odd[channel]], axis=0)
                cells_ref[base : base + 16, tile * LANES : (tile + 1) * LANES] = block.astype(jnp.bfloat16)


def classify_halo(words, tables, ends_ref, values_ref, rows):
    layers = words.shape[0]
    start = lax.axis_index("bz") * (rows // 2)
    side_lane, has_side, sub_at = lane_maps(rows)
    halo = cell_values(*unpack_words(words), tables, float(2 * layers))
    for channel in range(4):
        values_ref[channel] = halo[channel]
    for z in range(layers):
        for channel in range(4):
            base = (z * 4 + channel) * 16
            line = jnp.broadcast_to(values_ref[channel, z : z + 1, :], (8, LANES))
            block = jnp.concatenate(
                [
                    jnp.where(has_side & (side_lane == start + 2 * sub_at + part), line, 0.0)
                    for part in range(2)
                ],
                axis=0,
            )
            ends_ref[base : base + 16, :] = block.astype(jnp.bfloat16)


def along_columns(cells, ends, weights_ref):
    cols = cells.shape[1]
    result = jnp.dot(cells, weights_ref[0:cols, :], preferred_element_type=jnp.float32)
    result += jnp.dot(ends, weights_ref[cols : cols + LANES, :], preferred_element_type=jnp.float32)
    return result.astype(jnp.bfloat16).astype(jnp.float32)


def cells_kernel(dense_ref, index_ref, tables_ref, cells_ref, weights_ref):
    layers, tiles, rows = dense_ref.shape[:3]
    half = rows // 2
    start = lax.axis_index("bz") * half
    fill_weights(weights_ref, rows)

    def read_cells(z, part, tile):
        at = pl.ds(start + part, half // 2, stride=2)
        return dense_ref[z, tile, at, :], index_ref[z, tile, at, :]

    classify_rows(read_cells, read_tables(tables_ref), cells_ref, layers, tiles)


def own_kernel(rows, cells_ref, halo_ref, tables_ref, weights_ref, along_ref, ends_ref, values_ref):
    classify_halo(halo_ref[...], read_tables(tables_ref), ends_ref, values_ref, rows)
    result = along_columns(cells_ref[...], ends_ref[...], weights_ref)
    for tile in range(along_ref.shape[0]):
        along_ref[tile] = result[:, tile * LANES : (tile + 1) * LANES]


def other_kernel(
    rows, bulk_ref, tables_ref, weights_ref, own_ref, along_ref, cells_ref, ends_ref, values_ref
):
    layers = (bulk_ref.shape[0] - 2) // 2
    cols = bulk_ref.shape[2]
    size = own_ref.shape[1]
    me = lax.axis_index("bz")
    tables = read_tables(tables_ref)
    pad = size // layers
    mine = pl.multiple_of(pad + me * size, pad)
    theirs = pl.multiple_of(pad + (1 - me) * size, pad)
    for tile in range(own_ref.shape[0]):
        along_ref[tile, 0:pad, :] = jnp.zeros((pad, LANES), jnp.float32)
        along_ref[tile, pad + 2 * size : 2 * pad + 2 * size, :] = jnp.zeros((pad, LANES), jnp.float32)
        along_ref[tile, pl.ds(mine, size), :] = own_ref[tile]

    def read_cells(z, part, tile):
        return unpack_words(bulk_ref[2 * z + part, :, tile * LANES : (tile + 1) * LANES])

    classify_rows(read_cells, tables, cells_ref, layers, cols // LANES)
    classify_halo(bulk_ref[2 * layers + 1, :, 0:LANES], tables, ends_ref, values_ref, rows)
    result = along_columns(cells_ref[...], ends_ref[...], weights_ref)
    for tile in range(along_ref.shape[0]):
        along_ref[tile, pl.ds(theirs, size), :] = result[:, tile * LANES : (tile + 1) * LANES]


def render_kernel(
    rank_ref, tables_ref, weights_ref, bulk_ref, edges_ref, halo_ref, near_ref, along_ref,
    out_ref, cells_ref, lines_ref, mixed_ref,
):
    layers, cols = edges_ref.shape[1:]
    depth = 2 * layers
    rows = out_ref.shape[1]
    half = rows // 2
    tiles = 2 * cols // LANES
    total = float(depth)
    f32 = jnp.float32
    me = lax.axis_index("bz")
    front = me == 0
    tables = read_tables(tables_ref)
    side_lane, has_side, sub_at = lane_maps(rows)
    me_y = lax.axis_index("by")
    has_near = jnp.where(front, me_y > 0, me_y + 1 < lax.axis_size("by"))

    for slab in range(2):
        mine = me == slab
        inside = jnp.where(mine, edges_ref[0], bulk_ref[2 * layers])
        halo_inside = jnp.where(mine, halo_ref[...], bulk_ref[2 * layers + 1, :, 0:LANES])
        near = jnp.where(has_near, near_ref[slab], 0)
        halo_near = jnp.where(has_near, near_ref[2, :, slab * LANES : (slab + 1) * LANES], 0)
        for side in range(2):
            row = jnp.where(front, rows - 1, half - 1) if side == 0 else jnp.where(front, half, 0)
            use_near = front if side == 0 else jnp.logical_not(front)
            words = jnp.where(use_near, near, inside)
            halo = jnp.where(use_near, halo_near, halo_inside)
            base = side * 4 * depth + slab * layers
            blocks = [
                cell_values(*unpack_words(words[:, t * LANES : (t + 1) * LANES]), tables, total)
                for t in range(cols // LANES)
            ]
            values = cell_values(*unpack_words(halo), tables, total)
            blocks.append([jnp.where(has_side & (side_lane == row), value, 0.0) for value in values])
            for channel in range(4):
                for t, block in enumerate(blocks):
                    cells_ref[
                        base + channel * depth : base + channel * depth + layers,
                        t * LANES : (t + 1) * LANES,
                    ] = block[channel]
    edge = jnp.dot(
        cells_ref[...].astype(jnp.bfloat16), weights_ref[...], preferred_element_type=f32
    )
    edge = edge.astype(jnp.bfloat16).astype(f32)
    layer_at = lax.broadcasted_iota(jnp.int32, (depth, LANES), 0)
    for tile in range(tiles):
        for side in range(2):
            for channel in range(4):
                base = (side * 4 + channel) * depth
                now = edge[base : base + depth, tile * LANES : (tile + 1) * LANES]
                triple = 3.0 * now
                before = jnp.where(layer_at == 0, 0.0, pltpu.roll(now, 1, 0))
                after = jnp.where(layer_at == depth - 1, 0.0, pltpu.roll(now, depth - 1, 0))
                for parity, beside in enumerate((before, after)):
                    lines_ref[tile, side, channel, parity] = (
                        (beside + triple).astype(jnp.bfloat16).astype(f32)
                    )

    top = sub_at == 0
    bottom = sub_at == 7

    def layer_rows(tile, layer, channel):
        base = pl.multiple_of((layer * 4 + channel) * 16, 16)
        return [along_ref[tile, pl.ds(base + part * 8, 8), :] for part in range(2)]

    def over_layer(tile, layer, image):
        here = [layer_rows(tile, layer + 1, channel) for channel in range(4)]
        triple = [[3.0 * value for value in pair] for pair in here]
        for parity in range(2):
            clear = [1.0 - value for value in image[3]]
            updated = []
            for channel in range(4):
                beside = layer_rows(tile, layer + 2 * parity, channel)
                even, odd = [
                    (beside[part] + triple[channel][part]).astype(jnp.bfloat16).astype(f32)
                    for part in range(2)
                ]
                above = lines_ref[tile, 0, channel, parity, pl.ds(layer, 1), :]
                below = lines_ref[tile, 1, channel, parity, pl.ds(layer, 1), :]
                before_even = jnp.where(top, jnp.broadcast_to(above, (8, LANES)), pltpu.roll(odd, 1, 0))
                after_odd = jnp.where(bottom, jnp.broadcast_to(below, (8, LANES)), pltpu.roll(even, 7, 0))
                even_centre = 3.0 * even
                odd_centre = 3.0 * odd
                samples = [
                    before_even + even_centre, even_centre + odd, even + odd_centre, odd_centre + after_odd
                ]
                updated.append(
                    [image[channel][i] + clear[i] * samples[i] for i in range(4)]
                )
            image = updated
        return image

    flip = rank_ref[0]

    def one_tile(tile, carry):
        def one_slab(position, image):
            slab = position ^ flip
            for z in range(layers):
                image = over_layer(tile, slab * layers + z, image)
            return image

        zero = jnp.zeros((8, LANES), f32)
        image = [[zero] * 4 for _ in range(4)]
        image = lax.fori_loop(0, 2, one_slab, image)
        lanes = pl.ds(pl.multiple_of(tile * LANES, LANES), LANES)
        for channel in range(4):
            for i in range(4):
                mixed_ref[channel, pl.ds(i, 8, stride=4), :] = image[channel][i]
            out_ref[channel, :, lanes] = mixed_ref[channel]
        return carry

    lax.fori_loop(0, tiles, one_tile, 0)


def two_slab_device(density, bin_index, tf_colour, tf_extinction, slab_rank):
    layers, rows, cols = density.shape
    half = rows // 2
    tiles = 2 * cols // LANES
    size = layers * 4 * half
    count_y, count_x = lax.axis_size("by"), lax.axis_size("bx")
    f32, bf16, i32 = jnp.float32, jnp.bfloat16, jnp.int32

    def call(kernel, name, out_shape, time, scratch_shapes=(), in_specs=None):
        def run(*operands):
            return pl.pallas_call(
                kernel,
                out_shape=out_shape,
                in_specs=in_specs or [VMEM] * len(operands),
                out_specs=(VMEM,) * len(out_shape) if isinstance(out_shape, tuple) else VMEM,
                scratch_shapes=scratch_shapes,
                compiler_params=pltpu.CompilerParams(vmem_limit_bytes=16 * 1024 * 1024),
                cost_estimate=cost(time),
                name=name,
            )(*operands)

        return run

    def both(route):
        return route + [(target, source) for source, target in route]

    blocks = (layers, cols // LANES, rows, LANES)
    columns, dense, index, tables = call(
        columns_kernel,
        "pack_columns",
        (
            pltpu.VMEM((layers, LANES), i32),
            pltpu.VMEM(blocks, f32),
            pltpu.VMEM(blocks, i32),
            pltpu.VMEM((8, 8, LANES), f32),
        ),
        1.2,
    )(*[pltpu.with_memory_space_constraint(x, pltpu.HBM) for x in (density, bin_index, tf_colour, tf_extinction)])

    pairs = [(x, x + 1) for x in range(0, count_x, 2)]
    cross = [(x, (x + 1) % count_x) for x in range(1, count_x, 2)]
    beside = lax.ppermute(columns, "bx", both(pairs))
    across = lax.ppermute(columns, "bx", both(cross))

    cells, weights = call(
        cells_kernel,
        "own_cells",
        (pltpu.VMEM((size, cols), bf16), pltpu.VMEM((cols + LANES, 2 * cols), bf16)),
        0.5,
    )(dense, index, tables)
    bulk, edges, halo = call(
        pack_kernel,
        "pack_block",
        (
            pltpu.VMEM((2 * layers + 2, 8, cols), i32),
            pltpu.VMEM((2, layers, cols), i32),
            pltpu.VMEM((layers, LANES), i32),
        ),
        0.2,
    )(dense, index, beside, across, cells)
    bulk = lax.ppermute(bulk, "bz", [(0, 1), (1, 0)])

    ends = [pltpu.VMEM((size, LANES), bf16), pltpu.VMEM((4, layers, LANES), f32)]
    along = call(
        functools.partial(own_kernel, rows), "own_slab", pltpu.VMEM((tiles, size, LANES), f32), 0.7, ends
    )(cells, halo, tables, weights)
    line = call(diagonal_kernel, "diagonal_line", pltpu.VMEM((3, layers, cols), i32), 0.1)(
        bulk, edges, halo, along
    )
    route = [(count_y + y, (y + 1) % count_y) for y in range(count_y)]
    near = lax.ppermute(line, ("bz", "by"), both(route))
    along = call(
        functools.partial(other_kernel, rows),
        "other_slab",
        pltpu.VMEM((tiles, 2 * size + 2 * 4 * half, LANES), f32),
        1.0,
        [pltpu.VMEM((size, cols), bf16)] + ends,
    )(bulk, tables, weights, along)
    return call(
        render_kernel,
        "render_rows",
        jax.ShapeDtypeStruct((4, rows, 2 * cols), f32),
        3.6,
        [
            pltpu.VMEM((8 * 2 * layers, cols + LANES), f32),
            pltpu.VMEM((tiles, 2, 4, 2, 2 * layers, LANES), f32),
            pltpu.VMEM((4, rows, LANES), f32),
        ],
        [pl.BlockSpec(memory_space=pltpu.SMEM)] + [VMEM] * 7,
    )(slab_rank, tables, weights, bulk, edges, halo, near, along)


def on_device(density, bin_index, tf_colour, tf_extinction, slab_rank):
    if lax.axis_size("bz") == 2:
        return two_slab_device(density, bin_index, tf_colour, tf_extinction, slab_rank)
    return general_device(density, bin_index, tf_colour, tf_extinction, slab_rank)


def solution(mesh):
    return jax.shard_map(
        on_device,
        mesh=mesh,
        in_specs=(P("bz", "by", "bx"), P("bz", "by", "bx"), P(), P(), P()),
        out_specs=P(None, ("by", "bz"), "bx"),
        check_vma=False,
    )
```

```python
import jax
import jax.numpy as jnp
from jax import lax
from jax.experimental import pallas as pl
from jax.experimental.pallas import tpu as pltpu
from jax.sharding import PartitionSpec as P


def with_halo(block, sides, width):
    for axis, dim in sides:
        count = lax.axis_size(axis)
        forward = [(i, i + 1) for i in range(count - 1)]
        backward = [(target, source) for source, target in forward]
        low = lax.ppermute(
            lax.slice_in_dim(block, block.shape[dim] - width, None, axis=dim), axis, forward
        )
        high = lax.ppermute(lax.slice_in_dim(block, 0, width, axis=dim), axis, backward)
        block = jnp.concatenate([low, block, high], axis=dim)
    return block


def partner_2(block, axis, stride):
    count = lax.axis_size(axis)
    route = []
    for low in range(count):
        high = low | 1 << stride
        if high != low and high < count:
            route += [(low, high), (high, low)]
    return lax.ppermute(block, axis, route)


def resample_table(length):
    row_index = lax.broadcasted_iota(jnp.int32, (2 * length, length + 2), 0)
    col_index = lax.broadcasted_iota(jnp.int32, (2 * length, length + 2), 1)
    centre = row_index // 2
    parity = row_index % 2
    weights_table = jnp.where(col_index == centre + 1, 0.75, 0.0)
    weights_table = weights_table + jnp.where((col_index == centre) & (parity == 0), 0.25, 0.0)
    weights_table = weights_table + jnp.where((col_index == centre + 2) & (parity == 1), 0.25, 0.0)
    return weights_table.astype(jnp.bfloat16)


def blend_over(in_front, behind):
    return in_front + (1.0 - in_front[3])[None] * behind


def classify(density, bin_index, tf_colour, tf_extinction, total_depth):
    depth_cells, height_cells, width_cells = density.shape
    lookup = jnp.concatenate([tf_colour, tf_extinction[None, :]], axis=0)
    table_size = lookup.shape[1]
    bin_rows = lax.broadcasted_iota(jnp.int32, (table_size, 1), 0)
    flat_bins = bin_index.reshape(depth_cells, height_cells * width_cells)
    flat_density = density.reshape(depth_cells, height_cells * width_cells)

    def one_layer(layer, result):
        layer_bins = lax.dynamic_index_in_dim(flat_bins, layer, 0, keepdims=True)
        layer_density = lax.dynamic_index_in_dim(flat_density, layer, 0, keepdims=False)
        one_hot = (layer_bins == bin_rows).astype(jnp.bfloat16)
        values = jnp.dot(lookup, one_hot, preferred_element_type=jnp.float32)
        opacity = 1.0 - jnp.exp(-values[3] * layer_density / total_depth)
        cells = jnp.concatenate([values[:3] * opacity[None], opacity[None]], axis=0).astype(
            jnp.bfloat16
        )
        return lax.dynamic_update_slice_in_dim(result, cells[:, None], layer, 1)

    start_cells = jnp.zeros((4, depth_cells, height_cells * width_cells), jnp.bfloat16)
    classified = lax.fori_loop(0, depth_cells, one_layer, start_cells)
    return classified.reshape(4, depth_cells, height_cells, width_cells)


def general_device(density, bin_index, tf_colour, tf_extinction, slab_rank):
    slab_count = lax.axis_size("bz")
    depth_cells, height_cells, width_cells = density.shape
    total_depth = float(depth_cells * slab_count)
    colour_cells = classify(density, bin_index, tf_colour, tf_extinction, total_depth)
    padded = with_halo(colour_cells, (("bz", 1), ("by", 2), ("bx", 3)), 1)
    along_x = jnp.einsum(
        "czyq,pq->czyp", padded, resample_table(width_cells), preferred_element_type=jnp.float32
    ).astype(jnp.bfloat16)
    y_table = resample_table(height_cells)

    def add_sample(sample_index, image_now):
        centre = sample_index // 2
        parity = sample_index % 2
        layers = lax.dynamic_slice_in_dim(along_x, centre, 3, 1).astype(jnp.float32)
        lower_weight = jnp.where(parity == 0, 0.25, 0.0)
        upper_weight = jnp.where(parity == 1, 0.25, 0.0)
        mixed_layer = (
            lower_weight * layers[:, 0] + 0.75 * layers[:, 1] + upper_weight * layers[:, 2]
        ).astype(jnp.bfloat16)
        sample = jnp.einsum("qy,cyp->cqp", y_table, mixed_layer, preferred_element_type=jnp.float32)
        return blend_over(image_now, sample)

    start_image = jnp.zeros((4, 2 * height_cells, 2 * width_cells), jnp.float32)
    slab_image = lax.fori_loop(0, 2 * depth_cells, add_sample, start_image)
    rows_piece = 2 * height_cells // slab_count
    my_index = lax.axis_index("bz")
    bit_levels = slab_count.bit_length() - 1
    composite = slab_image.reshape((4,) + (2,) * bit_levels + (rows_piece, 2 * width_cells))
    my_rank = lax.dynamic_index_in_dim(slab_rank, my_index, 0, keepdims=False)
    for level in range(bit_levels):
        position = bit_levels - level
        my_bit = my_index // 2**level % 2
        kept_half = lax.dynamic_index_in_dim(composite, my_bit, position, keepdims=False)
        outgoing = lax.dynamic_index_in_dim(composite, 1 - my_bit, position, keepdims=False)
        incoming = partner_2(outgoing, "bz", level)
        partner = my_index + (1 - 2 * my_bit) * 2**level
        partner_rank = lax.dynamic_index_in_dim(slab_rank, partner, 0, keepdims=False)
        mine_first = my_rank < partner_rank
        composite = blend_over(
            jnp.where(mine_first, kept_half, incoming), jnp.where(mine_first, incoming, kept_half)
        )
    return composite


LANES = 128
LEVELS = 65535.0
VMEM = pl.BlockSpec(memory_space=pltpu.VMEM)


def pack_words(density, bins):
    level = (density * LEVELS + 0.5).astype(jnp.int32)
    return lax.shift_left(level, 16) | bins


def unpack_words(words):
    density = lax.shift_right_logical(words, 16).astype(jnp.float32) * (1.0 / LEVELS)
    return density, words & 0xFFFF


def cell_values(density, bins, tables, depth):
    low_bits = bins & (LANES - 1)
    upper = bins >= LANES

    def pick(channel):
        first, second = tables[channel]
        return jnp.where(
            upper,
            jnp.take_along_axis(second, low_bits, axis=1, mode="promise_in_bounds"),
            jnp.take_along_axis(first, low_bits, axis=1, mode="promise_in_bounds"),
        )

    opacity = (1.0 - jnp.exp(-pick(3) * density / depth)) * (1.0 / 64.0)
    return [pick(0) * opacity, pick(1) * opacity, pick(2) * opacity, opacity]


def read_tables(tables_ref):
    return [[tables_ref[2 * channel + half] for half in range(2)] for channel in range(4)]


def cost(microseconds):
    return pl.CostEstimate(
        flops=0, bytes_accessed=int(3.6e6 * microseconds), transcendentals=0
    )


def stage_kernel(
    density_ref, bins_ref, colour_ref, extinction_ref,
    small_ref, mine_ref, columns_ref, dense_ref, index_ref, tables_ref,
):
    layers, rows, cols = density_ref.shape
    front = lax.axis_index("bz") == 0
    row_at = lax.broadcasted_iota(jnp.int32, (rows, LANES), 0)
    lane_at = lax.broadcasted_iota(jnp.int32, (rows, LANES), 1)
    for z in range(layers):
        first = pack_words(density_ref[z, :, 0:1], bins_ref[z, :, 0:1])
        last = pack_words(density_ref[z, :, cols - 1 : cols], bins_ref[z, :, cols - 1 : cols])
        line = jnp.where(lane_at == row_at, first, 0) + jnp.where(lane_at == row_at + rows, last, 0)
        columns_ref[z : z + 1, :] = jnp.sum(line, axis=0, keepdims=True)
        top, bottom = [
            pack_words(density_ref[z, r : r + 1, :], bins_ref[z, r : r + 1, :]) for r in (0, rows - 1)
        ]
        small_ref[0, z : z + 1, :] = jnp.where(front, bottom, top)
        mine_ref[z : z + 1, :] = jnp.where(front, top, bottom)
        for tile in range(cols // LANES):
            lanes = slice(tile * LANES, (tile + 1) * LANES)
            dense_ref[z, tile] = density_ref[z, :, lanes]
            index_ref[z, tile] = bins_ref[z, :, lanes]
    for tile in range(cols // LANES):
        small_ref[1, :, tile * LANES : (tile + 1) * LANES] = columns_ref[...]
    colour = colour_ref[...].astype(jnp.float32)
    extinction = extinction_ref[...].astype(jnp.float32).reshape(1, 2 * LANES)
    for channel in range(4):
        line = extinction if channel == 3 else colour[channel : channel + 1]
        for half in range(2):
            tables_ref[2 * channel + half] = jnp.broadcast_to(
                line[:, half * LANES : (half + 1) * LANES], (8, LANES)
            )


def pack_kernel(dense_ref, index_ref, bulk_ref, inside_ref):
    layers, tiles, rows = dense_ref.shape[:3]
    half = rows // 2
    front = lax.axis_index("bz") == 0
    start = jnp.where(front, half, 0)
    for tile in range(tiles):
        lanes = slice(tile * LANES, (tile + 1) * LANES)
        for z in range(layers):
            for part in range(2):
                at = pl.ds(start + part, half // 2, stride=2)
                bulk_ref[2 * z + part, :, lanes] = pack_words(
                    dense_ref[z, tile, at, :], index_ref[z, tile, at, :]
                )
            line = [
                pack_words(dense_ref[z, tile, r : r + 1, :], index_ref[z, tile, r : r + 1, :])
                for r in (half - 1, half)
            ]
            bulk_ref[2 * layers, z : z + 1, lanes] = jnp.where(front, line[0], line[1])
            inside_ref[z : z + 1, lanes] = jnp.where(front, line[1], line[0])


def diagonal_kernel(mine_ref, other_ref, cells_ref, line_ref):
    front = lax.axis_index("bz") == 0
    line_ref[0] = jnp.where(front, mine_ref[...], other_ref[0])
    line_ref[1] = jnp.where(front, other_ref[0], mine_ref[...])


def side_kernel(columns_ref, other_ref, near_ref, along_ref, ends_ref):
    layers = columns_ref.shape[0]
    front = lax.axis_index("bz") == 0
    near_inside = has_near(front)
    lane_at = lax.broadcasted_iota(jnp.int32, (layers, LANES), 1)
    for slab in range(2):
        mine = front if slab == 0 else jnp.logical_not(front)
        columns = jnp.where(mine, columns_ref[...], other_ref[1, :, 0:LANES])
        near = jnp.where(near_inside, near_ref[slab], 0)
        cols = near.shape[1]
        columns = jnp.where(lane_at == 64, near[:, 0:1], columns)
        ends_ref[slab] = jnp.where(lane_at == 65, near[:, cols - 1 : cols], columns)


def has_near(front):
    me_y = lax.axis_index("by")
    return jnp.where(front, me_y > 0, me_y + 1 < lax.axis_size("by"))


def fill_weights(weights_ref, rows):
    cols = weights_ref.shape[0] - LANES
    row = lax.broadcasted_iota(jnp.int32, (cols, 2 * cols), 0)
    at = lax.broadcasted_iota(jnp.int32, (cols, 2 * cols), 1)
    centre = lax.shift_right_logical(at, 1)
    beside = centre - 1 + 2 * (at & 1)
    weights_ref[0:cols, :] = jnp.where(
        row == centre, 3.0, jnp.where(row == beside, 1.0, 0.0)
    ).astype(jnp.bfloat16)
    row = lax.broadcasted_iota(jnp.int32, (LANES, 2 * LANES), 0)
    at = lax.broadcasted_iota(jnp.int32, (LANES, 2 * LANES), 1)
    right = ((row < rows) | (row == 64)) & (at == 2 * LANES - 1)
    left = (((row >= rows) & (row < 2 * rows)) | (row == 65)) & (at == 0)
    weights_ref[cols : cols + LANES, 0 : 2 * LANES] = jnp.where(right | left, 1.0, 0.0).astype(
        jnp.bfloat16
    )


def lane_maps(rows):
    lane_at = lax.broadcasted_iota(jnp.int32, (8, LANES), 1)
    sub_at = lax.broadcasted_iota(jnp.int32, (8, LANES), 0)
    return lane_at & (rows - 1), lane_at < 2 * rows, sub_at


def classify_rows(read_cells, tables, cells_ref, layers, tiles):
    total = float(2 * layers)
    for z in range(layers):
        for tile in range(tiles):
            even = cell_values(*read_cells(z, 0, tile), tables, total)
            odd = cell_values(*read_cells(z, 1, tile), tables, total)
            for channel in range(4):
                base = (z * 4 + channel) * 16
                block = jnp.concatenate([even[channel], odd[channel]], axis=0)
                cells_ref[base : base + 16, tile * LANES : (tile + 1) * LANES] = block.astype(jnp.bfloat16)


def classify_halo(words, tables, ends_ref, values_ref, rows, base):
    layers = words.shape[0]
    start = lax.axis_index("bz") * (rows // 2)
    side_lane, has_side, sub_at = lane_maps(rows)
    halo = cell_values(*unpack_words(words), tables, float(2 * layers))
    for channel in range(4):
        values_ref[channel, 0:layers] = halo[channel]
    masks = [has_side & (side_lane == start + 2 * sub_at + part) for part in range(2)]
    for z in range(layers):
        for channel in range(4):
            line = jnp.broadcast_to(values_ref[channel, z : z + 1, :], (8, LANES))
            block = jnp.concatenate([jnp.where(mask, line, 0.0) for mask in masks], axis=0)
            at = base + (z * 4 + channel) * 16
            ends_ref[at : at + 16, :] = block.astype(jnp.bfloat16)
    return halo


def rounded(value):
    return value.astype(jnp.bfloat16).astype(jnp.float32)


def along_columns(cells, weights_ref, store):
    cols = cells.shape[1]
    tiles = 2 * cols // LANES
    result = jnp.dot(cells, weights_ref[0:cols, :], preferred_element_type=jnp.float32)
    for tile in range(tiles):
        block = result[:, tile * LANES : (tile + 1) * LANES]
        store(tile, block if tile in (0, tiles - 1) else rounded(block))


def cells_kernel(dense_ref, index_ref, tables_ref, cells_ref, weights_ref):
    layers, tiles, rows = dense_ref.shape[:3]
    half = rows // 2
    start = lax.axis_index("bz") * half
    fill_weights(weights_ref, rows)

    def read_cells(z, part, tile):
        at = pl.ds(start + part, half // 2, stride=2)
        return dense_ref[z, tile, at, :], index_ref[z, tile, at, :]

    classify_rows(read_cells, read_tables(tables_ref), cells_ref, layers, tiles)


def own_kernel(cells_ref, weights_ref, along_ref):
    def store(tile, block):
        along_ref[tile] = block

    along_columns(cells_ref[...], weights_ref, store)


def other_kernel(bulk_ref, tables_ref, weights_ref, own_ref, along_ref, cells_ref):
    layers = (bulk_ref.shape[0] - 1) // 2
    cols = bulk_ref.shape[2]
    size = own_ref.shape[1]
    me = lax.axis_index("bz")
    pad = size // layers
    mine = pl.multiple_of(pad + me * size, pad)
    theirs = pl.multiple_of(pad + (1 - me) * size, pad)
    for tile in range(own_ref.shape[0]):
        along_ref[tile, 0:pad, :] = jnp.zeros((pad, LANES), jnp.float32)
        along_ref[tile, pad + 2 * size : 2 * pad + 2 * size, :] = jnp.zeros((pad, LANES), jnp.float32)
        along_ref[tile, pl.ds(mine, size), :] = own_ref[tile]

    def read_cells(z, part, tile):
        return unpack_words(bulk_ref[2 * z + part, :, tile * LANES : (tile + 1) * LANES])

    def store(tile, block):
        along_ref[tile, pl.ds(theirs, size), :] = block

    classify_rows(read_cells, read_tables(tables_ref), cells_ref, layers, cols // LANES)
    along_columns(cells_ref[...], weights_ref, store)


def edge_lines(edge, tile, lines_ref, depth):
    layer_at = lax.broadcasted_iota(jnp.int32, (depth, LANES), 0)
    for side in range(2):
        for channel in range(4):
            base = (side * 4 + channel) * depth
            now = edge[base : base + depth]
            triple = 3.0 * now
            before = jnp.where(layer_at == 0, 0.0, pltpu.roll(now, 1, 0))
            after = jnp.where(layer_at == depth - 1, 0.0, pltpu.roll(now, depth - 1, 0))
            for parity, beside in enumerate((before, after)):
                lines_ref[tile, side, channel, parity] = rounded(beside + triple)


def render_tile(tile, along_ref, lines_ref, flip, layers):
    sub_at = lax.broadcasted_iota(jnp.int32, (8, LANES), 0)
    top = sub_at == 0
    bottom = sub_at == 7

    def layer_rows(layer, channel):
        base = pl.multiple_of((layer * 4 + channel) * 16, 16)
        return [along_ref[tile, pl.ds(base + part * 8, 8), :] for part in range(2)]

    def over_layer(layer, image):
        here = [layer_rows(layer + 1, channel) for channel in range(4)]
        triple = [[3.0 * value for value in pair] for pair in here]
        for parity in range(2):
            clear = [1.0 - value for value in image[3]]
            updated = []
            for channel in range(4):
                beside = layer_rows(layer + 2 * parity, channel)
                even, odd = [rounded(beside[part] + triple[channel][part]) for part in range(2)]
                above = lines_ref[tile, 0, channel, parity, pl.ds(layer, 1), :]
                below = lines_ref[tile, 1, channel, parity, pl.ds(layer, 1), :]
                before_even = jnp.where(top, jnp.broadcast_to(above, (8, LANES)), pltpu.roll(odd, 1, 0))
                after_odd = jnp.where(bottom, jnp.broadcast_to(below, (8, LANES)), pltpu.roll(even, 7, 0))
                even_centre = 3.0 * even
                odd_centre = 3.0 * odd
                samples = [
                    before_even + even_centre, even_centre + odd, even + odd_centre, odd_centre + after_odd
                ]
                updated.append([image[channel][i] + clear[i] * samples[i] for i in range(4)])
            image = updated
        return image

    def one_slab(position, image):
        slab = position ^ flip
        for z in range(layers):
            image = over_layer(slab * layers + z, image)
        return image

    zero = jnp.zeros((8, LANES), jnp.float32)
    return lax.fori_loop(0, 2, one_slab, [[zero] * 4 for _ in range(4)])


def inner_kernel(
    rank_ref, tables_ref, weights_ref, bulk_ref, inside_ref, near_ref, along_ref, ends_ref,
    image_ref, edge_ref, cells_ref, lines_ref, mixed_ref,
):
    layers, cols = inside_ref.shape
    depth = 2 * layers
    tiles = 2 * cols // LANES
    me = lax.axis_index("bz")
    front = me == 0
    tables = read_tables(tables_ref)
    near_inside = has_near(front)
    for slab in range(2):
        inside = jnp.where(me == slab, inside_ref[...], bulk_ref[2 * layers])
        near = jnp.where(near_inside, near_ref[slab], 0)
        for side in range(2):
            use_near = front if side == 0 else jnp.logical_not(front)
            words = jnp.where(use_near, near, inside)
            for t in range(cols // LANES):
                lanes = slice(t * LANES, (t + 1) * LANES)
                values = cell_values(*unpack_words(words[:, lanes]), tables, float(depth))
                for channel in range(4):
                    base = (side * 4 + channel) * depth + slab * layers
                    cells_ref[base : base + layers, lanes] = values[channel]
    edge = jnp.dot(
        cells_ref[...].astype(jnp.bfloat16), weights_ref[0:cols, :], preferred_element_type=jnp.float32
    )
    for tile in range(tiles):
        block = edge[:, tile * LANES : (tile + 1) * LANES]
        if tile in (0, tiles - 1):
            edge_ref[0 if tile == 0 else 1] = block
        else:
            edge_lines(rounded(block), tile - 1, lines_ref, depth)

    def one_tile(index, carry):
        image = render_tile(index, along_ref.at[1 : tiles - 1], lines_ref, rank_ref[0], layers)
        lanes = pl.ds(pl.multiple_of(index * LANES, LANES), LANES)
        for channel in range(4):
            for i in range(4):
                mixed_ref[channel, pl.ds(i, 8, stride=4), :] = image[channel][i]
            image_ref[channel, :, lanes] = mixed_ref[channel]
        return carry

    lax.fori_loop(0, tiles - 2, one_tile, 0)


def outer_kernel(
    rank_ref, tables_ref, weights_ref, beside_ref, across_ref, along_ref, edge_ref, image_ref,
    out_ref, ends_ref, values_ref, fixed_ref, lines_ref, mixed_ref,
):
    rows = out_ref.shape[1]
    cols = out_ref.shape[2] // 2
    layers = beside_ref.shape[1]
    depth = 2 * layers
    tiles = 2 * cols // LANES
    size = layers * 64
    pad = 64
    front = lax.axis_index("bz") == 0
    me_x = lax.axis_index("bx")
    even_x = lax.rem(me_x, 2) == 0
    tables = read_tables(tables_ref)
    lane_at = lax.broadcasted_iota(jnp.int32, (layers, LANES), 1)
    is_right = (lane_at < rows) | (lane_at == 64)
    for slab in range(2):
        right = jnp.where(even_x, beside_ref[slab], across_ref[slab])
        left = jnp.where(even_x, across_ref[slab], beside_ref[slab])
        right = jnp.where(me_x + 1 < lax.axis_size("bx"), right, 0)
        left = jnp.where(me_x > 0, left, 0)
        halo = jnp.where(is_right, right, left)
        values = classify_halo(halo, tables, ends_ref, values_ref, rows, slab * size)
        for side in range(2):
            row = jnp.where(front, 64, rows // 2 - 1) if side == 0 else jnp.where(front, rows // 2, 64)
            twin = jnp.where(row == 64, 65, row + rows)
            keep = (lane_at == row) | (lane_at == twin)
            for channel in range(4):
                values_ref[4 + side * 4 + channel, slab * layers : (slab + 1) * layers] = jnp.where(
                    keep, values[channel], 0.0
                )
    for line in range(8):
        base = 2 * size + line * depth
        ends_ref[base : base + depth, :] = values_ref[4 + line].astype(jnp.bfloat16)
    added = jnp.dot(
        ends_ref[...], weights_ref[cols : cols + LANES, 0 : 2 * LANES], preferred_element_type=jnp.float32
    )
    for index, tile in enumerate((0, tiles - 1)):
        block = added[:, index * LANES : (index + 1) * LANES]
        fixed_ref[index, 0:pad, :] = jnp.zeros((pad, LANES), jnp.float32)
        fixed_ref[index, pad + 2 * size :, :] = jnp.zeros((pad, LANES), jnp.float32)
        fixed_ref[index, pad : pad + 2 * size, :] = rounded(
            along_ref[tile, pad : pad + 2 * size, :] + block[0 : 2 * size]
        )
        edge_lines(rounded(edge_ref[index] + block[2 * size :]), index, lines_ref, depth)
    out_ref[:, :, LANES : 2 * cols - LANES] = image_ref[...]

    def one_tile(index, carry):
        image = render_tile(index, fixed_ref, lines_ref, rank_ref[0], layers)
        lanes = pl.ds(pl.multiple_of(index * (2 * cols - LANES), LANES), LANES)
        for channel in range(4):
            for i in range(4):
                mixed_ref[channel, pl.ds(i, 8, stride=4), :] = image[channel][i]
            out_ref[channel, :, lanes] = mixed_ref[channel]
        return carry

    lax.fori_loop(0, 2, one_tile, 0)


def two_slab_device(density, bin_index, tf_colour, tf_extinction, slab_rank):
    layers, rows, cols = density.shape
    half = rows // 2
    tiles = 2 * cols // LANES
    size = layers * 4 * half
    count_y, count_x = lax.axis_size("by"), lax.axis_size("bx")
    f32, bf16, i32 = jnp.float32, jnp.bfloat16, jnp.int32

    def call(kernel, name, out_shape, time, scratch_shapes=(), in_specs=None):
        def run(*operands):
            return pl.pallas_call(
                kernel,
                out_shape=out_shape,
                in_specs=in_specs or [VMEM] * len(operands),
                out_specs=(VMEM,) * len(out_shape) if isinstance(out_shape, tuple) else VMEM,
                scratch_shapes=scratch_shapes,
                compiler_params=pltpu.CompilerParams(vmem_limit_bytes=16 * 1024 * 1024),
                cost_estimate=cost(time),
                name=name,
            )(*operands)

        return run

    def both(route):
        return route + [(target, source) for source, target in route]

    blocks = (layers, cols // LANES, rows, LANES)
    small, mine, columns, dense, index, tables = call(
        stage_kernel,
        "stage_block",
        (
            pltpu.VMEM((2, layers, cols), i32),
            pltpu.VMEM((layers, cols), i32),
            pltpu.VMEM((layers, LANES), i32),
            pltpu.VMEM(blocks, f32),
            pltpu.VMEM(blocks, i32),
            pltpu.VMEM((8, 8, LANES), f32),
        ),
        1.2,
    )(*[pltpu.with_memory_space_constraint(x, pltpu.HBM) for x in (density, bin_index, tf_colour, tf_extinction)])
    swap = [(0, 1), (1, 0)]
    other_small = lax.ppermute(small, "bz", swap)
    bulk, inside = call(
        pack_kernel,
        "pack_block",
        (pltpu.VMEM((2 * layers + 1, 8, cols), i32), pltpu.VMEM((layers, cols), i32)),
        0.1,
    )(dense, index)
    bulk = lax.ppermute(bulk, "bz", swap)
    cells, weights = call(
        cells_kernel,
        "own_cells",
        (pltpu.VMEM((size, cols), bf16), pltpu.VMEM((cols + LANES, 2 * cols), bf16)),
        0.5,
    )(dense, index, tables)

    line = call(diagonal_kernel, "diagonal_line", pltpu.VMEM((2, layers, cols), i32), 0.1)(
        mine, other_small, cells
    )
    route = [(count_y + y, y + 1) for y in range(count_y - 1)]
    alone = [(0, 0), (2 * count_y - 1, 2 * count_y - 1)]
    near = lax.ppermute(line, ("bz", "by"), both(route) + alone)
    along = call(own_kernel, "own_slab", pltpu.VMEM((tiles, size, LANES), f32), 0.4)(cells, weights)
    along = call(
        other_kernel,
        "other_slab",
        pltpu.VMEM((tiles, 2 * size + 2 * 4 * half, LANES), f32),
        0.7,
        [pltpu.VMEM((size, cols), bf16)],
    )(bulk, tables, weights, along)
    ends = call(side_kernel, "side_columns", pltpu.VMEM((2, layers, LANES), i32), 0.1)(
        columns, other_small, near, along
    )
    pairs = [(x, x + 1) for x in range(0, count_x, 2)]
    cross = [(x, (x + 1) % count_x) for x in range(1, count_x, 2)]
    beside = lax.ppermute(ends, "bx", both(pairs))
    across = lax.ppermute(ends, "bx", both(cross))
    smem = pl.BlockSpec(memory_space=pltpu.SMEM)
    lines = pltpu.VMEM((2, 2, 4, 2, 2 * layers, LANES), f32)
    image, edge = call(
        inner_kernel,
        "inner_tiles",
        (pltpu.VMEM((4, rows, (tiles - 2) * LANES), f32), pltpu.VMEM((2, 16 * layers, LANES), f32)),
        2.0,
        [pltpu.VMEM((16 * layers, cols), f32), lines, pltpu.VMEM((4, rows, LANES), f32)],
        [smem] + [VMEM] * 7,
    )(slab_rank, tables, weights, bulk, inside, near, along, ends)
    return call(
        outer_kernel,
        "outer_tiles",
        jax.ShapeDtypeStruct((4, rows, 2 * cols), f32),
        2.0,
        [
            pltpu.VMEM((2 * size + 16 * layers, LANES), bf16),
            pltpu.VMEM((12, 2 * layers, LANES), f32),
            pltpu.VMEM((2, 2 * size + 2 * 4 * half, LANES), f32),
            lines,
            pltpu.VMEM((4, rows, LANES), f32),
        ],
        [smem] + [VMEM] * 7,
    )(slab_rank, tables, weights, beside, across, along, edge, image)


def on_device(density, bin_index, tf_colour, tf_extinction, slab_rank):
    if lax.axis_size("bz") == 2:
        return two_slab_device(density, bin_index, tf_colour, tf_extinction, slab_rank)
    return general_device(density, bin_index, tf_colour, tf_extinction, slab_rank)


def solution(mesh):
    return jax.shard_map(
        on_device,
        mesh=mesh,
        in_specs=(P("bz", "by", "bx"), P("bz", "by", "bx"), P(), P(), P()),
        out_specs=P(None, ("by", "bz"), "bx"),
        check_vma=False,
    )
```

```python
import jax
import jax.numpy as jnp
from jax import lax
from jax.experimental import pallas as pl
from jax.experimental.pallas import tpu as pltpu
from jax.sharding import PartitionSpec as P


def with_halo(block, sides, width):
    for axis, dim in sides:
        count = lax.axis_size(axis)
        forward = [(i, i + 1) for i in range(count - 1)]
        backward = [(target, source) for source, target in forward]
        low = lax.ppermute(
            lax.slice_in_dim(block, block.shape[dim] - width, None, axis=dim), axis, forward
        )
        high = lax.ppermute(lax.slice_in_dim(block, 0, width, axis=dim), axis, backward)
        block = jnp.concatenate([low, block, high], axis=dim)
    return block


def partner_2(block, axis, stride):
    count = lax.axis_size(axis)
    route = []
    for low in range(count):
        high = low | 1 << stride
        if high != low and high < count:
            route += [(low, high), (high, low)]
    return lax.ppermute(block, axis, route)


def resample_table(length):
    row_index = lax.broadcasted_iota(jnp.int32, (2 * length, length + 2), 0)
    col_index = lax.broadcasted_iota(jnp.int32, (2 * length, length + 2), 1)
    centre = row_index // 2
    parity = row_index % 2
    weights_table = jnp.where(col_index == centre + 1, 0.75, 0.0)
    weights_table = weights_table + jnp.where((col_index == centre) & (parity == 0), 0.25, 0.0)
    weights_table = weights_table + jnp.where((col_index == centre + 2) & (parity == 1), 0.25, 0.0)
    return weights_table.astype(jnp.bfloat16)


def blend_over(in_front, behind):
    return in_front + (1.0 - in_front[3])[None] * behind


def classify(density, bin_index, tf_colour, tf_extinction, total_depth):
    depth_cells, height_cells, width_cells = density.shape
    lookup = jnp.concatenate([tf_colour, tf_extinction[None, :]], axis=0)
    table_size = lookup.shape[1]
    bin_rows = lax.broadcasted_iota(jnp.int32, (table_size, 1), 0)
    flat_bins = bin_index.reshape(depth_cells, height_cells * width_cells)
    flat_density = density.reshape(depth_cells, height_cells * width_cells)

    def one_layer(layer, result):
        layer_bins = lax.dynamic_index_in_dim(flat_bins, layer, 0, keepdims=True)
        layer_density = lax.dynamic_index_in_dim(flat_density, layer, 0, keepdims=False)
        one_hot = (layer_bins == bin_rows).astype(jnp.bfloat16)
        values = jnp.dot(lookup, one_hot, preferred_element_type=jnp.float32)
        opacity = 1.0 - jnp.exp(-values[3] * layer_density / total_depth)
        cells = jnp.concatenate([values[:3] * opacity[None], opacity[None]], axis=0).astype(
            jnp.bfloat16
        )
        return lax.dynamic_update_slice_in_dim(result, cells[:, None], layer, 1)

    start_cells = jnp.zeros((4, depth_cells, height_cells * width_cells), jnp.bfloat16)
    classified = lax.fori_loop(0, depth_cells, one_layer, start_cells)
    return classified.reshape(4, depth_cells, height_cells, width_cells)


def general_device(density, bin_index, tf_colour, tf_extinction, slab_rank):
    slab_count = lax.axis_size("bz")
    depth_cells, height_cells, width_cells = density.shape
    total_depth = float(depth_cells * slab_count)
    colour_cells = classify(density, bin_index, tf_colour, tf_extinction, total_depth)
    padded = with_halo(colour_cells, (("bz", 1), ("by", 2), ("bx", 3)), 1)
    along_x = jnp.einsum(
        "czyq,pq->czyp", padded, resample_table(width_cells), preferred_element_type=jnp.float32
    ).astype(jnp.bfloat16)
    y_table = resample_table(height_cells)

    def add_sample(sample_index, image_now):
        centre = sample_index // 2
        parity = sample_index % 2
        layers = lax.dynamic_slice_in_dim(along_x, centre, 3, 1).astype(jnp.float32)
        lower_weight = jnp.where(parity == 0, 0.25, 0.0)
        upper_weight = jnp.where(parity == 1, 0.25, 0.0)
        mixed_layer = (
            lower_weight * layers[:, 0] + 0.75 * layers[:, 1] + upper_weight * layers[:, 2]
        ).astype(jnp.bfloat16)
        sample = jnp.einsum("qy,cyp->cqp", y_table, mixed_layer, preferred_element_type=jnp.float32)
        return blend_over(image_now, sample)

    start_image = jnp.zeros((4, 2 * height_cells, 2 * width_cells), jnp.float32)
    slab_image = lax.fori_loop(0, 2 * depth_cells, add_sample, start_image)
    rows_piece = 2 * height_cells // slab_count
    my_index = lax.axis_index("bz")
    bit_levels = slab_count.bit_length() - 1
    composite = slab_image.reshape((4,) + (2,) * bit_levels + (rows_piece, 2 * width_cells))
    my_rank = lax.dynamic_index_in_dim(slab_rank, my_index, 0, keepdims=False)
    for level in range(bit_levels):
        position = bit_levels - level
        my_bit = my_index // 2**level % 2
        kept_half = lax.dynamic_index_in_dim(composite, my_bit, position, keepdims=False)
        outgoing = lax.dynamic_index_in_dim(composite, 1 - my_bit, position, keepdims=False)
        incoming = partner_2(outgoing, "bz", level)
        partner = my_index + (1 - 2 * my_bit) * 2**level
        partner_rank = lax.dynamic_index_in_dim(slab_rank, partner, 0, keepdims=False)
        mine_first = my_rank < partner_rank
        composite = blend_over(
            jnp.where(mine_first, kept_half, incoming), jnp.where(mine_first, incoming, kept_half)
        )
    return composite


LANES = 128
LEVELS = 65535.0
VMEM = pl.BlockSpec(memory_space=pltpu.VMEM)


def pack_words(density, bins):
    level = (density * LEVELS + 0.5).astype(jnp.int32)
    return lax.shift_left(level, 16) | bins


def unpack_words(words):
    density = lax.shift_right_logical(words, 16).astype(jnp.float32) * (1.0 / LEVELS)
    return density, words & 0xFFFF


def cell_values(density, bins, tables, depth):
    low_bits = bins & (LANES - 1)
    upper = bins >= LANES

    def pick(channel):
        first, second = tables[channel]
        return jnp.where(
            upper,
            jnp.take_along_axis(second, low_bits, axis=1, mode="promise_in_bounds"),
            jnp.take_along_axis(first, low_bits, axis=1, mode="promise_in_bounds"),
        )

    opacity = (1.0 - jnp.exp(-pick(3) * density / depth)) * (1.0 / 64.0)
    return [pick(0) * opacity, pick(1) * opacity, pick(2) * opacity, opacity]


def read_tables(tables_ref):
    return [[tables_ref[2 * channel + half] for half in range(2)] for channel in range(4)]


def cost(microseconds):
    return pl.CostEstimate(
        flops=0, bytes_accessed=int(3.6e6 * microseconds), transcendentals=0
    )


def stage_kernel(
    density_ref, bins_ref, colour_ref, extinction_ref,
    small_ref, mine_ref, columns_ref, dense_ref, index_ref, tables_ref,
):
    layers, rows, cols = density_ref.shape
    front = lax.axis_index("bz") == 0
    row_at = lax.broadcasted_iota(jnp.int32, (rows, LANES), 0)
    lane_at = lax.broadcasted_iota(jnp.int32, (rows, LANES), 1)
    for z in range(layers):
        first = pack_words(density_ref[z, :, 0:1], bins_ref[z, :, 0:1])
        last = pack_words(density_ref[z, :, cols - 1 : cols], bins_ref[z, :, cols - 1 : cols])
        line = jnp.where(lane_at == row_at, first, 0) + jnp.where(lane_at == row_at + rows, last, 0)
        columns_ref[z : z + 1, :] = jnp.sum(line, axis=0, keepdims=True)
        top, bottom = [
            pack_words(density_ref[z, r : r + 1, :], bins_ref[z, r : r + 1, :]) for r in (0, rows - 1)
        ]
        small_ref[0, z : z + 1, :] = jnp.where(front, bottom, top)
        mine_ref[z : z + 1, :] = jnp.where(front, top, bottom)
        for tile in range(cols // LANES):
            lanes = slice(tile * LANES, (tile + 1) * LANES)
            dense_ref[z, tile] = density_ref[z, :, lanes]
            index_ref[z, tile] = bins_ref[z, :, lanes]
    for tile in range(cols // LANES):
        small_ref[1, :, tile * LANES : (tile + 1) * LANES] = columns_ref[...]
    colour = colour_ref[...].astype(jnp.float32)
    extinction = extinction_ref[...].astype(jnp.float32).reshape(1, 2 * LANES)
    for channel in range(4):
        line = extinction if channel == 3 else colour[channel : channel + 1]
        for half in range(2):
            tables_ref[2 * channel + half] = jnp.broadcast_to(
                line[:, half * LANES : (half + 1) * LANES], (8, LANES)
            )


def pack_kernel(dense_ref, index_ref, cells_ref, bulk_ref, inside_ref):
    layers, tiles, rows = dense_ref.shape[:3]
    half = rows // 2
    front = lax.axis_index("bz") == 0
    start = jnp.where(front, half, 0)
    for tile in range(tiles):
        lanes = slice(tile * LANES, (tile + 1) * LANES)
        for z in range(layers):
            for part in range(2):
                at = pl.ds(start + part, half // 2, stride=2)
                bulk_ref[2 * z + part, :, lanes] = pack_words(
                    dense_ref[z, tile, at, :], index_ref[z, tile, at, :]
                )
            line = [
                pack_words(dense_ref[z, tile, r : r + 1, :], index_ref[z, tile, r : r + 1, :])
                for r in (half - 1, half)
            ]
            bulk_ref[2 * layers, z : z + 1, lanes] = jnp.where(front, line[0], line[1])
            inside_ref[z : z + 1, lanes] = jnp.where(front, line[1], line[0])


def diagonal_kernel(mine_ref, other_ref, inside_ref, line_ref):
    front = lax.axis_index("bz") == 0
    line_ref[0] = jnp.where(front, mine_ref[...], other_ref[0])
    line_ref[1] = jnp.where(front, other_ref[0], mine_ref[...])


def side_kernel(columns_ref, other_ref, near_ref, along_ref, ends_ref):
    layers = columns_ref.shape[0]
    front = lax.axis_index("bz") == 0
    near_inside = has_near(front)
    lane_at = lax.broadcasted_iota(jnp.int32, (layers, LANES), 1)
    for slab in range(2):
        mine = front if slab == 0 else jnp.logical_not(front)
        columns = jnp.where(mine, columns_ref[...], other_ref[1, :, 0:LANES])
        near = jnp.where(near_inside, near_ref[slab], 0)
        cols = near.shape[1]
        columns = jnp.where(lane_at == 64, near[:, 0:1], columns)
        ends_ref[slab] = jnp.where(lane_at == 65, near[:, cols - 1 : cols], columns)


def has_near(front):
    me_y = lax.axis_index("by")
    return jnp.where(front, me_y > 0, me_y + 1 < lax.axis_size("by"))


def fill_weights(weights_ref, rows):
    cols = weights_ref.shape[0] - LANES
    row = lax.broadcasted_iota(jnp.int32, (cols, 2 * cols), 0)
    at = lax.broadcasted_iota(jnp.int32, (cols, 2 * cols), 1)
    centre = lax.shift_right_logical(at, 1)
    beside = centre - 1 + 2 * (at & 1)
    weights_ref[0:cols, :] = jnp.where(
        row == centre, 3.0, jnp.where(row == beside, 1.0, 0.0)
    ).astype(jnp.bfloat16)
    row = lax.broadcasted_iota(jnp.int32, (LANES, 2 * LANES), 0)
    at = lax.broadcasted_iota(jnp.int32, (LANES, 2 * LANES), 1)
    right = ((row < rows) | (row == 64)) & (at == 2 * LANES - 1)
    left = (((row >= rows) & (row < 2 * rows)) | (row == 65)) & (at == 0)
    weights_ref[cols : cols + LANES, 0 : 2 * LANES] = jnp.where(right | left, 1.0, 0.0).astype(
        jnp.bfloat16
    )


def lane_maps(rows):
    lane_at = lax.broadcasted_iota(jnp.int32, (8, LANES), 1)
    sub_at = lax.broadcasted_iota(jnp.int32, (8, LANES), 0)
    return lane_at & (rows - 1), lane_at < 2 * rows, sub_at


def classify_rows(read_cells, tables, cells_ref, layers, tiles):
    total = float(2 * layers)
    for z in range(layers):
        for tile in range(tiles):
            even = cell_values(*read_cells(z, 0, tile), tables, total)
            odd = cell_values(*read_cells(z, 1, tile), tables, total)
            for channel in range(4):
                base = (z * 4 + channel) * 16
                block = jnp.concatenate([even[channel], odd[channel]], axis=0)
                cells_ref[base : base + 16, tile * LANES : (tile + 1) * LANES] = block.astype(jnp.bfloat16)


def classify_halo(words, tables, ends_ref, values_ref, rows, base):
    layers = words.shape[0]
    start = lax.axis_index("bz") * (rows // 2)
    side_lane, has_side, sub_at = lane_maps(rows)
    halo = cell_values(*unpack_words(words), tables, float(2 * layers))
    for channel in range(4):
        values_ref[channel, 0:layers] = halo[channel]
    masks = [has_side & (side_lane == start + 2 * sub_at + part) for part in range(2)]
    for z in range(layers):
        for channel in range(4):
            line = jnp.broadcast_to(values_ref[channel, z : z + 1, :], (8, LANES))
            block = jnp.concatenate([jnp.where(mask, line, 0.0) for mask in masks], axis=0)
            at = base + (z * 4 + channel) * 16
            ends_ref[at : at + 16, :] = block.astype(jnp.bfloat16)
    return halo


def rounded(value):
    return value.astype(jnp.bfloat16).astype(jnp.float32)


def along_columns(cells, weights_ref, store):
    cols = cells.shape[1]
    tiles = 2 * cols // LANES
    result = jnp.dot(cells, weights_ref[0:cols, :], preferred_element_type=jnp.float32)
    for tile in range(tiles):
        block = result[:, tile * LANES : (tile + 1) * LANES]
        store(tile, block if tile in (0, tiles - 1) else rounded(block))


def cells_kernel(dense_ref, index_ref, tables_ref, cells_ref, weights_ref):
    layers, tiles, rows = dense_ref.shape[:3]
    half = rows // 2
    start = lax.axis_index("bz") * half
    fill_weights(weights_ref, rows)

    def read_cells(z, part, tile):
        at = pl.ds(start + part, half // 2, stride=2)
        return dense_ref[z, tile, at, :], index_ref[z, tile, at, :]

    classify_rows(read_cells, read_tables(tables_ref), cells_ref, layers, tiles)


def own_kernel(cells_ref, weights_ref, along_ref):
    def store(tile, block):
        along_ref[tile] = block

    along_columns(cells_ref[...], weights_ref, store)


def other_kernel(bulk_ref, tables_ref, weights_ref, own_ref, along_ref, cells_ref):
    layers = (bulk_ref.shape[0] - 1) // 2
    cols = bulk_ref.shape[2]
    size = own_ref.shape[1]
    me = lax.axis_index("bz")
    pad = size // layers
    mine = pl.multiple_of(pad + me * size, pad)
    theirs = pl.multiple_of(pad + (1 - me) * size, pad)
    for tile in range(own_ref.shape[0]):
        along_ref[tile, 0:pad, :] = jnp.zeros((pad, LANES), jnp.float32)
        along_ref[tile, pad + 2 * size : 2 * pad + 2 * size, :] = jnp.zeros((pad, LANES), jnp.float32)
        along_ref[tile, pl.ds(mine, size), :] = own_ref[tile]

    def read_cells(z, part, tile):
        return unpack_words(bulk_ref[2 * z + part, :, tile * LANES : (tile + 1) * LANES])

    def store(tile, block):
        along_ref[tile, pl.ds(theirs, size), :] = block

    classify_rows(read_cells, read_tables(tables_ref), cells_ref, layers, cols // LANES)
    along_columns(cells_ref[...], weights_ref, store)


def edge_lines(edge, tile, lines_ref, depth):
    layer_at = lax.broadcasted_iota(jnp.int32, (depth, LANES), 0)
    for side in range(2):
        for channel in range(4):
            base = (side * 4 + channel) * depth
            now = edge[base : base + depth]
            triple = 3.0 * now
            before = jnp.where(layer_at == 0, 0.0, pltpu.roll(now, 1, 0))
            after = jnp.where(layer_at == depth - 1, 0.0, pltpu.roll(now, depth - 1, 0))
            for parity, beside in enumerate((before, after)):
                lines_ref[tile, side, channel, parity] = rounded(beside + triple)


def render_tile(tile, along_ref, lines_ref, flip, layers):
    sub_at = lax.broadcasted_iota(jnp.int32, (8, LANES), 0)
    top = sub_at == 0
    bottom = sub_at == 7

    def layer_rows(layer, channel):
        base = pl.multiple_of((layer * 4 + channel) * 16, 16)
        return [along_ref[tile, pl.ds(base + part * 8, 8), :] for part in range(2)]

    def over_layer(layer, image):
        here = [layer_rows(layer + 1, channel) for channel in range(4)]
        triple = [[3.0 * value for value in pair] for pair in here]
        for parity in range(2):
            clear = [1.0 - value for value in image[3]]
            updated = []
            for channel in range(4):
                beside = layer_rows(layer + 2 * parity, channel)
                even, odd = [rounded(beside[part] + triple[channel][part]) for part in range(2)]
                above = lines_ref[tile, 0, channel, parity, pl.ds(layer, 1), :]
                below = lines_ref[tile, 1, channel, parity, pl.ds(layer, 1), :]
                before_even = jnp.where(top, jnp.broadcast_to(above, (8, LANES)), pltpu.roll(odd, 1, 0))
                after_odd = jnp.where(bottom, jnp.broadcast_to(below, (8, LANES)), pltpu.roll(even, 7, 0))
                even_centre = 3.0 * even
                odd_centre = 3.0 * odd
                samples = [
                    before_even + even_centre, even_centre + odd, even + odd_centre, odd_centre + after_odd
                ]
                updated.append([image[channel][i] + clear[i] * samples[i] for i in range(4)])
            image = updated
        return image

    def one_slab(position, image):
        slab = position ^ flip
        for z in range(layers):
            image = over_layer(slab * layers + z, image)
        return image

    zero = jnp.zeros((8, LANES), jnp.float32)
    return lax.fori_loop(0, 2, one_slab, [[zero] * 4 for _ in range(4)])


def inner_kernel(
    rank_ref, tables_ref, weights_ref, bulk_ref, inside_ref, near_ref, along_ref, ends_ref,
    image_ref, edge_ref, cells_ref, lines_ref, mixed_ref,
):
    layers, cols = inside_ref.shape
    depth = 2 * layers
    tiles = 2 * cols // LANES
    me = lax.axis_index("bz")
    front = me == 0
    tables = read_tables(tables_ref)
    near_inside = has_near(front)
    for slab in range(2):
        inside = jnp.where(me == slab, inside_ref[...], bulk_ref[2 * layers])
        near = jnp.where(near_inside, near_ref[slab], 0)
        for side in range(2):
            use_near = front if side == 0 else jnp.logical_not(front)
            words = jnp.where(use_near, near, inside)
            for t in range(cols // LANES):
                lanes = slice(t * LANES, (t + 1) * LANES)
                values = cell_values(*unpack_words(words[:, lanes]), tables, float(depth))
                for channel in range(4):
                    base = (side * 4 + channel) * depth + slab * layers
                    cells_ref[base : base + layers, lanes] = values[channel]
    edge = jnp.dot(
        cells_ref[...].astype(jnp.bfloat16), weights_ref[0:cols, :], preferred_element_type=jnp.float32
    )
    for tile in range(tiles):
        block = edge[:, tile * LANES : (tile + 1) * LANES]
        if tile in (0, tiles - 1):
            edge_ref[0 if tile == 0 else 1] = block
        else:
            edge_lines(rounded(block), tile - 1, lines_ref, depth)

    def one_tile(index, carry):
        image = render_tile(index, along_ref.at[1 : tiles - 1], lines_ref, rank_ref[0], layers)
        lanes = pl.ds(pl.multiple_of(index * LANES, LANES), LANES)
        for channel in range(4):
            for i in range(4):
                mixed_ref[channel, pl.ds(i, 8, stride=4), :] = image[channel][i]
            image_ref[channel, :, lanes] = mixed_ref[channel]
        return carry

    lax.fori_loop(0, tiles - 2, one_tile, 0)


def outer_kernel(
    rank_ref, tables_ref, weights_ref, beside_ref, across_ref, along_ref, edge_ref, image_ref,
    out_ref, ends_ref, values_ref, fixed_ref, lines_ref, mixed_ref,
):
    rows = out_ref.shape[1]
    cols = out_ref.shape[2] // 2
    layers = beside_ref.shape[1]
    depth = 2 * layers
    tiles = 2 * cols // LANES
    size = layers * 64
    pad = 64
    front = lax.axis_index("bz") == 0
    me_x = lax.axis_index("bx")
    even_x = lax.rem(me_x, 2) == 0
    tables = read_tables(tables_ref)
    lane_at = lax.broadcasted_iota(jnp.int32, (layers, LANES), 1)
    is_right = (lane_at < rows) | (lane_at == 64)
    for slab in range(2):
        right = jnp.where(even_x, beside_ref[slab], across_ref[slab])
        left = jnp.where(even_x, across_ref[slab], beside_ref[slab])
        right = jnp.where(me_x + 1 < lax.axis_size("bx"), right, 0)
        left = jnp.where(me_x > 0, left, 0)
        halo = jnp.where(is_right, right, left)
        values = classify_halo(halo, tables, ends_ref, values_ref, rows, slab * size)
        for side in range(2):
            row = jnp.where(front, 64, rows // 2 - 1) if side == 0 else jnp.where(front, rows // 2, 64)
            twin = jnp.where(row == 64, 65, row + rows)
            keep = (lane_at == row) | (lane_at == twin)
            for channel in range(4):
                values_ref[4 + side * 4 + channel, slab * layers : (slab + 1) * layers] = jnp.where(
                    keep, values[channel], 0.0
                )
    for line in range(8):
        base = 2 * size + line * depth
        ends_ref[base : base + depth, :] = values_ref[4 + line].astype(jnp.bfloat16)
    added = jnp.dot(
        ends_ref[...], weights_ref[cols : cols + LANES, 0 : 2 * LANES], preferred_element_type=jnp.float32
    )
    for index, tile in enumerate((0, tiles - 1)):
        block = added[:, index * LANES : (index + 1) * LANES]
        fixed_ref[index, 0:pad, :] = jnp.zeros((pad, LANES), jnp.float32)
        fixed_ref[index, pad + 2 * size :, :] = jnp.zeros((pad, LANES), jnp.float32)
        fixed_ref[index, pad : pad + 2 * size, :] = rounded(
            along_ref[tile, pad : pad + 2 * size, :] + block[0 : 2 * size]
        )
        edge_lines(rounded(edge_ref[index] + block[2 * size :]), index, lines_ref, depth)
    out_ref[:, :, LANES : 2 * cols - LANES] = image_ref[...]

    def one_tile(index, carry):
        image = render_tile(index, fixed_ref, lines_ref, rank_ref[0], layers)
        lanes = pl.ds(pl.multiple_of(index * (2 * cols - LANES), LANES), LANES)
        for channel in range(4):
            for i in range(4):
                mixed_ref[channel, pl.ds(i, 8, stride=4), :] = image[channel][i]
            out_ref[channel, :, lanes] = mixed_ref[channel]
        return carry

    lax.fori_loop(0, 2, one_tile, 0)


def two_slab_device(density, bin_index, tf_colour, tf_extinction, slab_rank):
    layers, rows, cols = density.shape
    half = rows // 2
    tiles = 2 * cols // LANES
    size = layers * 4 * half
    count_y, count_x = lax.axis_size("by"), lax.axis_size("bx")
    f32, bf16, i32 = jnp.float32, jnp.bfloat16, jnp.int32

    def call(kernel, name, out_shape, time, scratch_shapes=(), in_specs=None):
        def run(*operands):
            return pl.pallas_call(
                kernel,
                out_shape=out_shape,
                in_specs=in_specs or [VMEM] * len(operands),
                out_specs=(VMEM,) * len(out_shape) if isinstance(out_shape, tuple) else VMEM,
                scratch_shapes=scratch_shapes,
                compiler_params=pltpu.CompilerParams(vmem_limit_bytes=16 * 1024 * 1024),
                cost_estimate=cost(time),
                name=name,
            )(*operands)

        return run

    def both(route):
        return route + [(target, source) for source, target in route]

    blocks = (layers, cols // LANES, rows, LANES)
    small, mine, columns, dense, index, tables = call(
        stage_kernel,
        "stage_block",
        (
            pltpu.VMEM((2, layers, cols), i32),
            pltpu.VMEM((layers, cols), i32),
            pltpu.VMEM((layers, LANES), i32),
            pltpu.VMEM(blocks, f32),
            pltpu.VMEM(blocks, i32),
            pltpu.VMEM((8, 8, LANES), f32),
        ),
        1.2,
    )(*[pltpu.with_memory_space_constraint(x, pltpu.HBM) for x in (density, bin_index, tf_colour, tf_extinction)])
    swap = [(0, 1), (1, 0)]
    other_small = lax.ppermute(small, "bz", swap)
    cells, weights = call(
        cells_kernel,
        "own_cells",
        (pltpu.VMEM((size, cols), bf16), pltpu.VMEM((cols + LANES, 2 * cols), bf16)),
        0.5,
    )(dense, index, tables)
    bulk, inside = call(
        pack_kernel,
        "pack_block",
        (pltpu.VMEM((2 * layers + 1, 8, cols), i32), pltpu.VMEM((layers, cols), i32)),
        0.1,
    )(dense, index, cells)
    bulk = lax.ppermute(bulk, "bz", swap)

    line = call(diagonal_kernel, "diagonal_line", pltpu.VMEM((2, layers, cols), i32), 0.1)(
        mine, other_small, inside
    )
    def place(z, y, x):
        return (z * count_y + y) * count_x + x

    route = [
        (place(1, y, x), place(0, y + 1, x)) for y in range(count_y - 1) for x in range(count_x)
    ]
    for z, y in ((0, 0), (1, count_y - 1)):
        route += [(place(z, y, x), place(z, y, x + 1)) for x in range(0, count_x, 2)]
    near = lax.ppermute(line, ("bz", "by", "bx"), both(route))
    along = call(own_kernel, "own_slab", pltpu.VMEM((tiles, size, LANES), f32), 0.4)(cells, weights)
    along = call(
        other_kernel,
        "other_slab",
        pltpu.VMEM((tiles, 2 * size + 2 * 4 * half, LANES), f32),
        0.7,
        [pltpu.VMEM((size, cols), bf16)],
    )(bulk, tables, weights, along)
    ends = call(side_kernel, "side_columns", pltpu.VMEM((2, layers, LANES), i32), 0.1)(
        columns, other_small, near, along
    )
    pairs = [(x, x + 1) for x in range(0, count_x, 2)]
    cross = [(x, (x + 1) % count_x) for x in range(1, count_x, 2)]
    beside = lax.ppermute(ends, "bx", both(pairs))
    across = lax.ppermute(ends, "bx", both(cross))
    smem = pl.BlockSpec(memory_space=pltpu.SMEM)
    lines = pltpu.VMEM((2, 2, 4, 2, 2 * layers, LANES), f32)
    image, edge = call(
        inner_kernel,
        "inner_tiles",
        (pltpu.VMEM((4, rows, (tiles - 2) * LANES), f32), pltpu.VMEM((2, 16 * layers, LANES), f32)),
        2.0,
        [pltpu.VMEM((16 * layers, cols), f32), lines, pltpu.VMEM((4, rows, LANES), f32)],
        [smem] + [VMEM] * 7,
    )(slab_rank, tables, weights, bulk, inside, near, along, ends)
    return call(
        outer_kernel,
        "outer_tiles",
        jax.ShapeDtypeStruct((4, rows, 2 * cols), f32),
        2.0,
        [
            pltpu.VMEM((2 * size + 16 * layers, LANES), bf16),
            pltpu.VMEM((12, 2 * layers, LANES), f32),
            pltpu.VMEM((2, 2 * size + 2 * 4 * half, LANES), f32),
            lines,
            pltpu.VMEM((4, rows, LANES), f32),
        ],
        [smem] + [VMEM] * 7,
    )(slab_rank, tables, weights, beside, across, along, edge, image)


def on_device(density, bin_index, tf_colour, tf_extinction, slab_rank):
    if lax.axis_size("bz") == 2:
        return two_slab_device(density, bin_index, tf_colour, tf_extinction, slab_rank)
    return general_device(density, bin_index, tf_colour, tf_extinction, slab_rank)


def solution(mesh):
    return jax.shard_map(
        on_device,
        mesh=mesh,
        in_specs=(P("bz", "by", "bx"), P("bz", "by", "bx"), P(), P(), P()),
        out_specs=P(None, ("by", "bz"), "bx"),
        check_vma=False,
    )
```

```python
import jax
import jax.numpy as jnp
from jax import lax
from jax.experimental import pallas as pl
from jax.experimental.pallas import tpu as pltpu
from jax.sharding import PartitionSpec as P


def with_halo(block, sides, width):
    for axis, dim in sides:
        count = lax.axis_size(axis)
        forward = [(i, i + 1) for i in range(count - 1)]
        backward = [(target, source) for source, target in forward]
        low = lax.ppermute(
            lax.slice_in_dim(block, block.shape[dim] - width, None, axis=dim), axis, forward
        )
        high = lax.ppermute(lax.slice_in_dim(block, 0, width, axis=dim), axis, backward)
        block = jnp.concatenate([low, block, high], axis=dim)
    return block


def partner_2(block, axis, stride):
    count = lax.axis_size(axis)
    route = []
    for low in range(count):
        high = low | 1 << stride
        if high != low and high < count:
            route += [(low, high), (high, low)]
    return lax.ppermute(block, axis, route)


def resample_table(length):
    row_index = lax.broadcasted_iota(jnp.int32, (2 * length, length + 2), 0)
    col_index = lax.broadcasted_iota(jnp.int32, (2 * length, length + 2), 1)
    centre = row_index // 2
    parity = row_index % 2
    weights_table = jnp.where(col_index == centre + 1, 0.75, 0.0)
    weights_table = weights_table + jnp.where((col_index == centre) & (parity == 0), 0.25, 0.0)
    weights_table = weights_table + jnp.where((col_index == centre + 2) & (parity == 1), 0.25, 0.0)
    return weights_table.astype(jnp.bfloat16)


def blend_over(in_front, behind):
    return in_front + (1.0 - in_front[3])[None] * behind


def classify(density, bin_index, tf_colour, tf_extinction, total_depth):
    depth_cells, height_cells, width_cells = density.shape
    lookup = jnp.concatenate([tf_colour, tf_extinction[None, :]], axis=0)
    table_size = lookup.shape[1]
    bin_rows = lax.broadcasted_iota(jnp.int32, (table_size, 1), 0)
    flat_bins = bin_index.reshape(depth_cells, height_cells * width_cells)
    flat_density = density.reshape(depth_cells, height_cells * width_cells)

    def one_layer(layer, result):
        layer_bins = lax.dynamic_index_in_dim(flat_bins, layer, 0, keepdims=True)
        layer_density = lax.dynamic_index_in_dim(flat_density, layer, 0, keepdims=False)
        one_hot = (layer_bins == bin_rows).astype(jnp.bfloat16)
        values = jnp.dot(lookup, one_hot, preferred_element_type=jnp.float32)
        opacity = 1.0 - jnp.exp(-values[3] * layer_density / total_depth)
        cells = jnp.concatenate([values[:3] * opacity[None], opacity[None]], axis=0).astype(
            jnp.bfloat16
        )
        return lax.dynamic_update_slice_in_dim(result, cells[:, None], layer, 1)

    start_cells = jnp.zeros((4, depth_cells, height_cells * width_cells), jnp.bfloat16)
    classified = lax.fori_loop(0, depth_cells, one_layer, start_cells)
    return classified.reshape(4, depth_cells, height_cells, width_cells)


def general_device(density, bin_index, tf_colour, tf_extinction, slab_rank):
    slab_count = lax.axis_size("bz")
    depth_cells, height_cells, width_cells = density.shape
    total_depth = float(depth_cells * slab_count)
    colour_cells = classify(density, bin_index, tf_colour, tf_extinction, total_depth)
    padded = with_halo(colour_cells, (("bz", 1), ("by", 2), ("bx", 3)), 1)
    along_x = jnp.einsum(
        "czyq,pq->czyp", padded, resample_table(width_cells), preferred_element_type=jnp.float32
    ).astype(jnp.bfloat16)
    y_table = resample_table(height_cells)

    def add_sample(sample_index, image_now):
        centre = sample_index // 2
        parity = sample_index % 2
        layers = lax.dynamic_slice_in_dim(along_x, centre, 3, 1).astype(jnp.float32)
        lower_weight = jnp.where(parity == 0, 0.25, 0.0)
        upper_weight = jnp.where(parity == 1, 0.25, 0.0)
        mixed_layer = (
            lower_weight * layers[:, 0] + 0.75 * layers[:, 1] + upper_weight * layers[:, 2]
        ).astype(jnp.bfloat16)
        sample = jnp.einsum("qy,cyp->cqp", y_table, mixed_layer, preferred_element_type=jnp.float32)
        return blend_over(image_now, sample)

    start_image = jnp.zeros((4, 2 * height_cells, 2 * width_cells), jnp.float32)
    slab_image = lax.fori_loop(0, 2 * depth_cells, add_sample, start_image)
    rows_piece = 2 * height_cells // slab_count
    my_index = lax.axis_index("bz")
    bit_levels = slab_count.bit_length() - 1
    composite = slab_image.reshape((4,) + (2,) * bit_levels + (rows_piece, 2 * width_cells))
    my_rank = lax.dynamic_index_in_dim(slab_rank, my_index, 0, keepdims=False)
    for level in range(bit_levels):
        position = bit_levels - level
        my_bit = my_index // 2**level % 2
        kept_half = lax.dynamic_index_in_dim(composite, my_bit, position, keepdims=False)
        outgoing = lax.dynamic_index_in_dim(composite, 1 - my_bit, position, keepdims=False)
        incoming = partner_2(outgoing, "bz", level)
        partner = my_index + (1 - 2 * my_bit) * 2**level
        partner_rank = lax.dynamic_index_in_dim(slab_rank, partner, 0, keepdims=False)
        mine_first = my_rank < partner_rank
        composite = blend_over(
            jnp.where(mine_first, kept_half, incoming), jnp.where(mine_first, incoming, kept_half)
        )
    return composite


LANES = 128
LEVELS = 65535.0
VMEM = pl.BlockSpec(memory_space=pltpu.VMEM)


def pack_words(density, bins):
    level = (density * LEVELS + 0.5).astype(jnp.int32)
    return lax.shift_left(level, 16) | bins


def unpack_words(words):
    density = lax.shift_right_logical(words, 16).astype(jnp.float32) * (1.0 / LEVELS)
    return density, words & 0xFFFF


def cell_values(density, bins, tables, depth):
    low_bits = bins & (LANES - 1)
    upper = bins >= LANES

    def pick(channel):
        first, second = tables[channel]
        return jnp.where(
            upper,
            jnp.take_along_axis(second, low_bits, axis=1, mode="promise_in_bounds"),
            jnp.take_along_axis(first, low_bits, axis=1, mode="promise_in_bounds"),
        )

    opacity = (1.0 - jnp.exp(-pick(3) * density / depth)) * (1.0 / 64.0)
    return [pick(0) * opacity, pick(1) * opacity, pick(2) * opacity, opacity]


def read_tables(tables_ref):
    return [[tables_ref[2 * channel + half] for half in range(2)] for channel in range(4)]


def cost(microseconds):
    return pl.CostEstimate(
        flops=0, bytes_accessed=int(3.6e6 * microseconds), transcendentals=0
    )


def stage_kernel(
    density_ref, bins_ref, colour_ref, extinction_ref,
    first_ref, second_ref, columns_ref, dense_ref, index_ref, tables_ref,
):
    layers, rows, cols = density_ref.shape
    front = lax.axis_index("bz") == 0
    row_at = lax.broadcasted_iota(jnp.int32, (rows, LANES), 0)
    lane_at = lax.broadcasted_iota(jnp.int32, (rows, LANES), 1)
    for z in range(layers):
        first = pack_words(density_ref[z, :, 0:1], bins_ref[z, :, 0:1])
        last = pack_words(density_ref[z, :, cols - 1 : cols], bins_ref[z, :, cols - 1 : cols])
        line = jnp.where(lane_at == row_at, first, 0) + jnp.where(lane_at == row_at + rows, last, 0)
        columns_ref[z : z + 1, :] = jnp.sum(line, axis=0, keepdims=True)
        top, bottom = [
            pack_words(density_ref[z, r : r + 1, :], bins_ref[z, r : r + 1, :]) for r in (0, rows - 1)
        ]
        first_ref[z : z + 1, :] = jnp.where(front, bottom, top)
        second_ref[z : z + 1, :] = jnp.where(front, top, bottom)
        for tile in range(cols // LANES):
            lanes = slice(tile * LANES, (tile + 1) * LANES)
            dense_ref[z, tile] = density_ref[z, :, lanes]
            index_ref[z, tile] = bins_ref[z, :, lanes]
    colour = colour_ref[...].astype(jnp.float32)
    extinction = extinction_ref[...].astype(jnp.float32).reshape(1, 2 * LANES)
    for channel in range(4):
        line = extinction if channel == 3 else colour[channel : channel + 1]
        for half in range(2):
            tables_ref[2 * channel + half] = jnp.broadcast_to(
                line[:, half * LANES : (half + 1) * LANES], (8, LANES)
            )


def pack_kernel(dense_ref, index_ref, columns_ref, bulk_ref, inside_ref):
    layers, tiles, rows = dense_ref.shape[:3]
    half = rows // 2
    front = lax.axis_index("bz") == 0
    start = jnp.where(front, half, 0)
    for tile in range(tiles):
        lanes = slice(tile * LANES, (tile + 1) * LANES)
        bulk_ref[2 * layers + 1, :, lanes] = columns_ref[...]
        for z in range(layers):
            for part in range(2):
                at = pl.ds(start + part, half // 2, stride=2)
                bulk_ref[2 * z + part, :, lanes] = pack_words(
                    dense_ref[z, tile, at, :], index_ref[z, tile, at, :]
                )
            line = [
                pack_words(dense_ref[z, tile, r : r + 1, :], index_ref[z, tile, r : r + 1, :])
                for r in (half - 1, half)
            ]
            bulk_ref[2 * layers, z : z + 1, lanes] = jnp.where(front, line[0], line[1])
            inside_ref[z : z + 1, lanes] = jnp.where(front, line[1], line[0])


def near_words(slab, first_ref, second_ref):
    me = lax.axis_index("bz")
    words = jnp.where(me == slab, first_ref[...], second_ref[...])
    return jnp.where(has_near(me == 0), words, 0)


def side_kernel(columns_ref, bulk_ref, first_ref, second_ref, along_ref, ends_ref):
    layers = columns_ref.shape[0]
    front = lax.axis_index("bz") == 0
    lane_at = lax.broadcasted_iota(jnp.int32, (layers, LANES), 1)
    for slab in range(2):
        mine = front if slab == 0 else jnp.logical_not(front)
        columns = jnp.where(mine, columns_ref[...], bulk_ref[2 * layers + 1, :, 0:LANES])
        near = near_words(slab, first_ref, second_ref)
        cols = near.shape[1]
        columns = jnp.where(lane_at == 64, near[:, 0:1], columns)
        ends_ref[slab] = jnp.where(lane_at == 65, near[:, cols - 1 : cols], columns)


def has_near(front):
    me_y = lax.axis_index("by")
    return jnp.where(front, me_y > 0, me_y + 1 < lax.axis_size("by"))


def fill_weights(weights_ref, rows):
    cols = weights_ref.shape[0] - LANES
    row = lax.broadcasted_iota(jnp.int32, (cols, 2 * cols), 0)
    at = lax.broadcasted_iota(jnp.int32, (cols, 2 * cols), 1)
    centre = lax.shift_right_logical(at, 1)
    beside = centre - 1 + 2 * (at & 1)
    weights_ref[0:cols, :] = jnp.where(
        row == centre, 3.0, jnp.where(row == beside, 1.0, 0.0)
    ).astype(jnp.bfloat16)
    row = lax.broadcasted_iota(jnp.int32, (LANES, 2 * LANES), 0)
    at = lax.broadcasted_iota(jnp.int32, (LANES, 2 * LANES), 1)
    right = ((row < rows) | (row == 64)) & (at == 2 * LANES - 1)
    left = (((row >= rows) & (row < 2 * rows)) | (row == 65)) & (at == 0)
    weights_ref[cols : cols + LANES, 0 : 2 * LANES] = jnp.where(right | left, 1.0, 0.0).astype(
        jnp.bfloat16
    )


def lane_maps(rows):
    lane_at = lax.broadcasted_iota(jnp.int32, (8, LANES), 1)
    sub_at = lax.broadcasted_iota(jnp.int32, (8, LANES), 0)
    return lane_at & (rows - 1), lane_at < 2 * rows, sub_at


def classify_rows(read_cells, tables, cells_ref, layers, tiles):
    total = float(2 * layers)
    for z in range(layers):
        for tile in range(tiles):
            even = cell_values(*read_cells(z, 0, tile), tables, total)
            odd = cell_values(*read_cells(z, 1, tile), tables, total)
            for channel in range(4):
                base = (z * 4 + channel) * 16
                block = jnp.concatenate([even[channel], odd[channel]], axis=0)
                cells_ref[base : base + 16, tile * LANES : (tile + 1) * LANES] = block.astype(jnp.bfloat16)


def classify_halo(words, tables, ends_ref, values_ref, rows, base):
    layers = words.shape[0]
    start = lax.axis_index("bz") * (rows // 2)
    side_lane, has_side, sub_at = lane_maps(rows)
    halo = cell_values(*unpack_words(words), tables, float(2 * layers))
    for channel in range(4):
        values_ref[channel, 0:layers] = halo[channel]
    masks = [has_side & (side_lane == start + 2 * sub_at + part) for part in range(2)]
    for z in range(layers):
        for channel in range(4):
            line = jnp.broadcast_to(values_ref[channel, z : z + 1, :], (8, LANES))
            block = jnp.concatenate([jnp.where(mask, line, 0.0) for mask in masks], axis=0)
            at = base + (z * 4 + channel) * 16
            ends_ref[at : at + 16, :] = block.astype(jnp.bfloat16)
    return halo


def rounded(value):
    return value.astype(jnp.bfloat16).astype(jnp.float32)


def along_columns(cells, weights_ref, store):
    cols = cells.shape[1]
    tiles = 2 * cols // LANES
    result = jnp.dot(cells, weights_ref[0:cols, :], preferred_element_type=jnp.float32)
    for tile in range(tiles):
        block = result[:, tile * LANES : (tile + 1) * LANES]
        store(tile, block if tile in (0, tiles - 1) else rounded(block))


def cells_kernel(dense_ref, index_ref, tables_ref, cells_ref, weights_ref):
    layers, tiles, rows = dense_ref.shape[:3]
    half = rows // 2
    start = lax.axis_index("bz") * half
    fill_weights(weights_ref, rows)

    def read_cells(z, part, tile):
        at = pl.ds(start + part, half // 2, stride=2)
        return dense_ref[z, tile, at, :], index_ref[z, tile, at, :]

    classify_rows(read_cells, read_tables(tables_ref), cells_ref, layers, tiles)


def own_kernel(cells_ref, weights_ref, along_ref):
    def store(tile, block):
        along_ref[tile] = block

    along_columns(cells_ref[...], weights_ref, store)


def other_kernel(bulk_ref, tables_ref, weights_ref, own_ref, ends_ref, along_ref, cells_ref):
    layers = (bulk_ref.shape[0] - 2) // 2
    cols = bulk_ref.shape[2]
    size = own_ref.shape[1]
    me = lax.axis_index("bz")
    pad = size // layers
    mine = pl.multiple_of(pad + me * size, pad)
    theirs = pl.multiple_of(pad + (1 - me) * size, pad)
    for tile in range(own_ref.shape[0]):
        along_ref[tile, 0:pad, :] = jnp.zeros((pad, LANES), jnp.float32)
        along_ref[tile, pad + 2 * size : 2 * pad + 2 * size, :] = jnp.zeros((pad, LANES), jnp.float32)
        along_ref[tile, pl.ds(mine, size), :] = own_ref[tile]

    def read_cells(z, part, tile):
        return unpack_words(bulk_ref[2 * z + part, :, tile * LANES : (tile + 1) * LANES])

    def store(tile, block):
        along_ref[tile, pl.ds(theirs, size), :] = block

    classify_rows(read_cells, read_tables(tables_ref), cells_ref, layers, cols // LANES)
    along_columns(cells_ref[...], weights_ref, store)


def edge_lines(edge, tile, lines_ref, depth):
    layer_at = lax.broadcasted_iota(jnp.int32, (depth, LANES), 0)
    for side in range(2):
        for channel in range(4):
            base = (side * 4 + channel) * depth
            now = edge[base : base + depth]
            triple = 3.0 * now
            before = jnp.where(layer_at == 0, 0.0, pltpu.roll(now, 1, 0))
            after = jnp.where(layer_at == depth - 1, 0.0, pltpu.roll(now, depth - 1, 0))
            for parity, beside in enumerate((before, after)):
                lines_ref[tile, side, channel, parity] = rounded(beside + triple)


def render_tile(tile, along_ref, lines_ref, flip, layers):
    sub_at = lax.broadcasted_iota(jnp.int32, (8, LANES), 0)
    top = sub_at == 0
    bottom = sub_at == 7

    def layer_rows(layer, channel):
        base = pl.multiple_of((layer * 4 + channel) * 16, 16)
        return [along_ref[tile, pl.ds(base + part * 8, 8), :] for part in range(2)]

    def over_layer(layer, image):
        here = [layer_rows(layer + 1, channel) for channel in range(4)]
        triple = [[3.0 * value for value in pair] for pair in here]
        for parity in range(2):
            clear = [1.0 - value for value in image[3]]
            updated = []
            for channel in range(4):
                beside = layer_rows(layer + 2 * parity, channel)
                even, odd = [rounded(beside[part] + triple[channel][part]) for part in range(2)]
                above = lines_ref[tile, 0, channel, parity, pl.ds(layer, 1), :]
                below = lines_ref[tile, 1, channel, parity, pl.ds(layer, 1), :]
                before_even = jnp.where(top, jnp.broadcast_to(above, (8, LANES)), pltpu.roll(odd, 1, 0))
                after_odd = jnp.where(bottom, jnp.broadcast_to(below, (8, LANES)), pltpu.roll(even, 7, 0))
                even_centre = 3.0 * even
                odd_centre = 3.0 * odd
                samples = [
                    before_even + even_centre, even_centre + odd, even + odd_centre, odd_centre + after_odd
                ]
                updated.append([image[channel][i] + clear[i] * samples[i] for i in range(4)])
            image = updated
        return image

    def one_slab(position, image):
        slab = position ^ flip
        for z in range(layers):
            image = over_layer(slab * layers + z, image)
        return image

    zero = jnp.zeros((8, LANES), jnp.float32)
    return lax.fori_loop(0, 2, one_slab, [[zero] * 4 for _ in range(4)])


def inner_kernel(
    rank_ref, tables_ref, weights_ref, bulk_ref, inside_ref, first_ref, second_ref, along_ref,
    image_ref, edge_ref, cells_ref, lines_ref, mixed_ref,
):
    layers, cols = inside_ref.shape
    depth = 2 * layers
    tiles = 2 * cols // LANES
    me = lax.axis_index("bz")
    front = me == 0
    tables = read_tables(tables_ref)
    for slab in range(2):
        inside = jnp.where(me == slab, inside_ref[...], bulk_ref[2 * layers])
        near = near_words(slab, first_ref, second_ref)
        for side in range(2):
            use_near = front if side == 0 else jnp.logical_not(front)
            words = jnp.where(use_near, near, inside)
            for t in range(cols // LANES):
                lanes = slice(t * LANES, (t + 1) * LANES)
                values = cell_values(*unpack_words(words[:, lanes]), tables, float(depth))
                for channel in range(4):
                    base = (side * 4 + channel) * depth + slab * layers
                    cells_ref[base : base + layers, lanes] = values[channel]
    edge = jnp.dot(
        cells_ref[...].astype(jnp.bfloat16), weights_ref[0:cols, :], preferred_element_type=jnp.float32
    )
    for tile in range(tiles):
        block = edge[:, tile * LANES : (tile + 1) * LANES]
        if tile in (0, tiles - 1):
            edge_ref[0 if tile == 0 else 1] = block
        else:
            edge_lines(rounded(block), tile - 1, lines_ref, depth)

    def one_tile(index, carry):
        image = render_tile(index, along_ref.at[1 : tiles - 1], lines_ref, rank_ref[0], layers)
        lanes = pl.ds(pl.multiple_of(index * LANES, LANES), LANES)
        for channel in range(4):
            for i in range(4):
                mixed_ref[channel, pl.ds(i, 8, stride=4), :] = image[channel][i]
            image_ref[channel, :, lanes] = mixed_ref[channel]
        return carry

    lax.fori_loop(0, tiles - 2, one_tile, 0)


def outer_kernel(
    rank_ref, tables_ref, weights_ref, beside_ref, across_ref, along_ref, edge_ref, image_ref,
    out_ref, ends_ref, values_ref, fixed_ref, lines_ref, mixed_ref,
):
    rows = out_ref.shape[1]
    cols = out_ref.shape[2] // 2
    layers = beside_ref.shape[1]
    depth = 2 * layers
    tiles = 2 * cols // LANES
    size = layers * 64
    pad = 64
    front = lax.axis_index("bz") == 0
    me_x = lax.axis_index("bx")
    even_x = lax.rem(me_x, 2) == 0
    tables = read_tables(tables_ref)
    lane_at = lax.broadcasted_iota(jnp.int32, (layers, LANES), 1)
    is_right = (lane_at < rows) | (lane_at == 64)
    for slab in range(2):
        right = jnp.where(even_x, beside_ref[slab], across_ref[slab])
        left = jnp.where(even_x, across_ref[slab], beside_ref[slab])
        right = jnp.where(me_x + 1 < lax.axis_size("bx"), right, 0)
        left = jnp.where(me_x > 0, left, 0)
        halo = jnp.where(is_right, right, left)
        values = classify_halo(halo, tables, ends_ref, values_ref, rows, slab * size)
        for side in range(2):
            row = jnp.where(front, 64, rows // 2 - 1) if side == 0 else jnp.where(front, rows // 2, 64)
            twin = jnp.where(row == 64, 65, row + rows)
            keep = (lane_at == row) | (lane_at == twin)
            for channel in range(4):
                values_ref[4 + side * 4 + channel, slab * layers : (slab + 1) * layers] = jnp.where(
                    keep, values[channel], 0.0
                )
    for line in range(8):
        base = 2 * size + line * depth
        ends_ref[base : base + depth, :] = values_ref[4 + line].astype(jnp.bfloat16)
    added = jnp.dot(
        ends_ref[...], weights_ref[cols : cols + LANES, 0 : 2 * LANES], preferred_element_type=jnp.float32
    )
    for index, tile in enumerate((0, tiles - 1)):
        block = added[:, index * LANES : (index + 1) * LANES]
        fixed_ref[index, 0:pad, :] = jnp.zeros((pad, LANES), jnp.float32)
        fixed_ref[index, pad + 2 * size :, :] = jnp.zeros((pad, LANES), jnp.float32)
        fixed_ref[index, pad : pad + 2 * size, :] = rounded(
            along_ref[tile, pad : pad + 2 * size, :] + block[0 : 2 * size]
        )
        edge_lines(rounded(edge_ref[index] + block[2 * size :]), index, lines_ref, depth)
    out_ref[:, :, LANES : 2 * cols - LANES] = image_ref[...]

    def one_tile(index, carry):
        image = render_tile(index, fixed_ref, lines_ref, rank_ref[0], layers)
        lanes = pl.ds(pl.multiple_of(index * (2 * cols - LANES), LANES), LANES)
        for channel in range(4):
            for i in range(4):
                mixed_ref[channel, pl.ds(i, 8, stride=4), :] = image[channel][i]
            out_ref[channel, :, lanes] = mixed_ref[channel]
        return carry

    lax.fori_loop(0, 2, one_tile, 0)


def two_slab_device(density, bin_index, tf_colour, tf_extinction, slab_rank):
    layers, rows, cols = density.shape
    half = rows // 2
    tiles = 2 * cols // LANES
    size = layers * 4 * half
    count_y, count_x = lax.axis_size("by"), lax.axis_size("bx")
    f32, bf16, i32 = jnp.float32, jnp.bfloat16, jnp.int32

    def call(kernel, name, out_shape, time, scratch_shapes=(), in_specs=None):
        def run(*operands):
            return pl.pallas_call(
                kernel,
                out_shape=out_shape,
                in_specs=in_specs or [VMEM] * len(operands),
                out_specs=(VMEM,) * len(out_shape) if isinstance(out_shape, tuple) else VMEM,
                scratch_shapes=scratch_shapes,
                compiler_params=pltpu.CompilerParams(vmem_limit_bytes=16 * 1024 * 1024),
                cost_estimate=cost(time),
                name=name,
            )(*operands)

        return run

    def both(route):
        return route + [(target, source) for source, target in route]

    blocks = (layers, cols // LANES, rows, LANES)
    row = pltpu.VMEM((layers, cols), i32)
    first, second, columns, dense, index, tables = call(
        stage_kernel,
        "stage_block",
        (
            row,
            row,
            pltpu.VMEM((layers, LANES), i32),
            pltpu.VMEM(blocks, f32),
            pltpu.VMEM(blocks, i32),
            pltpu.VMEM((8, 8, LANES), f32),
        ),
        1.2,
    )(*[pltpu.with_memory_space_constraint(x, pltpu.HBM) for x in (density, bin_index, tf_colour, tf_extinction)])
    bulk, inside = call(
        pack_kernel, "pack_block", (pltpu.VMEM((2 * layers + 2, 8, cols), i32), row), 0.1
    )(dense, index, columns)

    def place(z, y, x):
        return (z * count_y + y) * count_x + x

    steps = range(count_y - 1)
    ring = [(place(0, y, 0), place(0, y + 1, 0)) for y in steps]
    ring += [(place(1, y + 1, 0), place(1, y, 0)) for y in steps]
    ring += [(place(0, count_y - 1, 0), place(1, count_y - 1, 0)), (place(1, 0, 0), place(0, 0, 0))]
    ring = [(source + x, target + x) for source, target in ring for x in range(count_x)]
    diagonal = [(place(1, y, x), place(0, y + 1, x)) for y in steps for x in range(count_x)]
    for z, y in ((0, 0), (1, count_y - 1)):
        diagonal += [(place(z, y, x), place(z, y, x + 1)) for x in range(0, count_x, 2)]
    axes = ("bz", "by", "bx")
    bulk = lax.ppermute(bulk, "bz", [(0, 1), (1, 0)])
    first = lax.ppermute(first, axes, ring)
    second = lax.ppermute(second, axes, both(diagonal))

    cells, weights = call(
        cells_kernel,
        "own_cells",
        (pltpu.VMEM((size, cols), bf16), pltpu.VMEM((cols + LANES, 2 * cols), bf16)),
        0.5,
    )(dense, index, tables)
    along = call(own_kernel, "own_slab", pltpu.VMEM((tiles, size, LANES), f32), 0.4)(cells, weights)
    ends = call(side_kernel, "side_columns", pltpu.VMEM((2, layers, LANES), i32), 0.1)(
        columns, bulk, first, second, along
    )
    pairs = [(x, x + 1) for x in range(0, count_x, 2)]
    cross = [(x, (x + 1) % count_x) for x in range(1, count_x, 2)]
    beside = lax.ppermute(ends, "bx", both(pairs))
    across = lax.ppermute(ends, "bx", both(cross))
    along = call(
        other_kernel,
        "other_slab",
        pltpu.VMEM((tiles, 2 * size + 2 * 4 * half, LANES), f32),
        0.8,
        [pltpu.VMEM((size, cols), bf16)],
    )(bulk, tables, weights, along, ends)
    smem = pl.BlockSpec(memory_space=pltpu.SMEM)
    lines = pltpu.VMEM((2, 2, 4, 2, 2 * layers, LANES), f32)
    image, edge = call(
        inner_kernel,
        "inner_tiles",
        (pltpu.VMEM((4, rows, (tiles - 2) * LANES), f32), pltpu.VMEM((2, 16 * layers, LANES), f32)),
        2.0,
        [pltpu.VMEM((16 * layers, cols), f32), lines, pltpu.VMEM((4, rows, LANES), f32)],
        [smem] + [VMEM] * 7,
    )(slab_rank, tables, weights, bulk, inside, first, second, along)
    return call(
        outer_kernel,
        "outer_tiles",
        jax.ShapeDtypeStruct((4, rows, 2 * cols), f32),
        2.0,
        [
            pltpu.VMEM((2 * size + 16 * layers, LANES), bf16),
            pltpu.VMEM((12, 2 * layers, LANES), f32),
            pltpu.VMEM((2, 2 * size + 2 * 4 * half, LANES), f32),
            lines,
            pltpu.VMEM((4, rows, LANES), f32),
        ],
        [smem] + [VMEM] * 7,
    )(slab_rank, tables, weights, beside, across, along, edge, image)


def on_device(density, bin_index, tf_colour, tf_extinction, slab_rank):
    if lax.axis_size("bz") == 2:
        return two_slab_device(density, bin_index, tf_colour, tf_extinction, slab_rank)
    return general_device(density, bin_index, tf_colour, tf_extinction, slab_rank)


def solution(mesh):
    return jax.shard_map(
        on_device,
        mesh=mesh,
        in_specs=(P("bz", "by", "bx"), P("bz", "by", "bx"), P(), P(), P()),
        out_specs=P(None, ("by", "bz"), "bx"),
        check_vma=False,
    )
```

```python
import functools

import jax
import jax.numpy as jnp
from jax import lax
from jax.experimental import pallas as pl
from jax.experimental.pallas import tpu as pltpu
from jax.sharding import PartitionSpec as P


def with_halo(block, sides, width):
    for axis, dim in sides:
        count = lax.axis_size(axis)
        forward = [(i, i + 1) for i in range(count - 1)]
        backward = [(target, source) for source, target in forward]
        low = lax.ppermute(
            lax.slice_in_dim(block, block.shape[dim] - width, None, axis=dim), axis, forward
        )
        high = lax.ppermute(lax.slice_in_dim(block, 0, width, axis=dim), axis, backward)
        block = jnp.concatenate([low, block, high], axis=dim)
    return block


def partner_2(block, axis, stride):
    count = lax.axis_size(axis)
    route = []
    for low in range(count):
        high = low | 1 << stride
        if high != low and high < count:
            route += [(low, high), (high, low)]
    return lax.ppermute(block, axis, route)


def resample_table(length):
    row_index = lax.broadcasted_iota(jnp.int32, (2 * length, length + 2), 0)
    col_index = lax.broadcasted_iota(jnp.int32, (2 * length, length + 2), 1)
    centre = row_index // 2
    parity = row_index % 2
    weights_table = jnp.where(col_index == centre + 1, 0.75, 0.0)
    weights_table = weights_table + jnp.where((col_index == centre) & (parity == 0), 0.25, 0.0)
    weights_table = weights_table + jnp.where((col_index == centre + 2) & (parity == 1), 0.25, 0.0)
    return weights_table.astype(jnp.bfloat16)


def blend_over(in_front, behind):
    return in_front + (1.0 - in_front[3])[None] * behind


def classify(density, bin_index, tf_colour, tf_extinction, total_depth):
    depth_cells, height_cells, width_cells = density.shape
    lookup = jnp.concatenate([tf_colour, tf_extinction[None, :]], axis=0)
    table_size = lookup.shape[1]
    bin_rows = lax.broadcasted_iota(jnp.int32, (table_size, 1), 0)
    flat_bins = bin_index.reshape(depth_cells, height_cells * width_cells)
    flat_density = density.reshape(depth_cells, height_cells * width_cells)

    def one_layer(layer, result):
        layer_bins = lax.dynamic_index_in_dim(flat_bins, layer, 0, keepdims=True)
        layer_density = lax.dynamic_index_in_dim(flat_density, layer, 0, keepdims=False)
        one_hot = (layer_bins == bin_rows).astype(jnp.bfloat16)
        values = jnp.dot(lookup, one_hot, preferred_element_type=jnp.float32)
        opacity = 1.0 - jnp.exp(-values[3] * layer_density / total_depth)
        cells = jnp.concatenate([values[:3] * opacity[None], opacity[None]], axis=0).astype(
            jnp.bfloat16
        )
        return lax.dynamic_update_slice_in_dim(result, cells[:, None], layer, 1)

    start_cells = jnp.zeros((4, depth_cells, height_cells * width_cells), jnp.bfloat16)
    classified = lax.fori_loop(0, depth_cells, one_layer, start_cells)
    return classified.reshape(4, depth_cells, height_cells, width_cells)


def general_device(density, bin_index, tf_colour, tf_extinction, slab_rank):
    slab_count = lax.axis_size("bz")
    depth_cells, height_cells, width_cells = density.shape
    total_depth = float(depth_cells * slab_count)
    colour_cells = classify(density, bin_index, tf_colour, tf_extinction, total_depth)
    padded = with_halo(colour_cells, (("bz", 1), ("by", 2), ("bx", 3)), 1)
    along_x = jnp.einsum(
        "czyq,pq->czyp", padded, resample_table(width_cells), preferred_element_type=jnp.float32
    ).astype(jnp.bfloat16)
    y_table = resample_table(height_cells)

    def add_sample(sample_index, image_now):
        centre = sample_index // 2
        parity = sample_index % 2
        layers = lax.dynamic_slice_in_dim(along_x, centre, 3, 1).astype(jnp.float32)
        lower_weight = jnp.where(parity == 0, 0.25, 0.0)
        upper_weight = jnp.where(parity == 1, 0.25, 0.0)
        mixed_layer = (
            lower_weight * layers[:, 0] + 0.75 * layers[:, 1] + upper_weight * layers[:, 2]
        ).astype(jnp.bfloat16)
        sample = jnp.einsum("qy,cyp->cqp", y_table, mixed_layer, preferred_element_type=jnp.float32)
        return blend_over(image_now, sample)

    start_image = jnp.zeros((4, 2 * height_cells, 2 * width_cells), jnp.float32)
    slab_image = lax.fori_loop(0, 2 * depth_cells, add_sample, start_image)
    rows_piece = 2 * height_cells // slab_count
    my_index = lax.axis_index("bz")
    bit_levels = slab_count.bit_length() - 1
    composite = slab_image.reshape((4,) + (2,) * bit_levels + (rows_piece, 2 * width_cells))
    my_rank = lax.dynamic_index_in_dim(slab_rank, my_index, 0, keepdims=False)
    for level in range(bit_levels):
        position = bit_levels - level
        my_bit = my_index // 2**level % 2
        kept_half = lax.dynamic_index_in_dim(composite, my_bit, position, keepdims=False)
        outgoing = lax.dynamic_index_in_dim(composite, 1 - my_bit, position, keepdims=False)
        incoming = partner_2(outgoing, "bz", level)
        partner = my_index + (1 - 2 * my_bit) * 2**level
        partner_rank = lax.dynamic_index_in_dim(slab_rank, partner, 0, keepdims=False)
        mine_first = my_rank < partner_rank
        composite = blend_over(
            jnp.where(mine_first, kept_half, incoming), jnp.where(mine_first, incoming, kept_half)
        )
    return composite


LANES = 128
LEVELS = 65535.0
VMEM = pl.BlockSpec(memory_space=pltpu.VMEM)


def pack_words(density, bins):
    level = (density * LEVELS + 0.5).astype(jnp.int32)
    return lax.shift_left(level, 16) | bins


def unpack_words(words):
    density = lax.shift_right_logical(words, 16).astype(jnp.float32) * (1.0 / LEVELS)
    return density, words & 0xFFFF


def cell_values(density, bins, tables, depth):
    low_bits = bins & (LANES - 1)
    upper = bins >= LANES

    def pick(channel):
        first, second = tables[channel]
        return jnp.where(
            upper,
            jnp.take_along_axis(second, low_bits, axis=1, mode="promise_in_bounds"),
            jnp.take_along_axis(first, low_bits, axis=1, mode="promise_in_bounds"),
        )

    opacity = (1.0 - jnp.exp(-pick(3) * density / depth)) * (1.0 / 64.0)
    return [pick(0) * opacity, pick(1) * opacity, pick(2) * opacity, opacity]


def read_tables(tables_ref):
    return [[tables_ref[2 * channel + half] for half in range(2)] for channel in range(4)]


def cost(microseconds):
    return pl.CostEstimate(
        flops=int(1e9 * microseconds), bytes_accessed=int(3.6e6 * microseconds), transcendentals=0
    )


def stage_kernel(
    density_ref, bins_ref, colour_ref, extinction_ref,
    first_ref, second_ref, columns_ref, dense_ref, index_ref, tables_ref,
):
    layers, rows, cols = density_ref.shape
    front = lax.axis_index("bz") == 0
    row_at = lax.broadcasted_iota(jnp.int32, (rows, LANES), 0)
    lane_at = lax.broadcasted_iota(jnp.int32, (rows, LANES), 1)
    for z in range(layers):
        first = pack_words(density_ref[z, :, 0:1], bins_ref[z, :, 0:1])
        last = pack_words(density_ref[z, :, cols - 1 : cols], bins_ref[z, :, cols - 1 : cols])
        line = jnp.where(lane_at == row_at, first, 0) + jnp.where(lane_at == row_at + rows, last, 0)
        columns_ref[z : z + 1, :] = jnp.sum(line, axis=0, keepdims=True)
        top, bottom = [
            pack_words(density_ref[z, r : r + 1, :], bins_ref[z, r : r + 1, :]) for r in (0, rows - 1)
        ]
        first_ref[z : z + 1, :] = jnp.where(front, bottom, top)
        second_ref[z : z + 1, :] = jnp.where(front, top, bottom)
        for tile in range(cols // LANES):
            lanes = slice(tile * LANES, (tile + 1) * LANES)
            dense_ref[z, tile] = density_ref[z, :, lanes]
            index_ref[z, tile] = bins_ref[z, :, lanes]
    colour = colour_ref[...].astype(jnp.float32)
    extinction = extinction_ref[...].astype(jnp.float32).reshape(1, 2 * LANES)
    for channel in range(4):
        line = extinction if channel == 3 else colour[channel : channel + 1]
        for half in range(2):
            tables_ref[2 * channel + half] = jnp.broadcast_to(
                line[:, half * LANES : (half + 1) * LANES], (8, LANES)
            )


def pack_kernel(dense_ref, index_ref, bulk_ref, inside_ref):
    layers, tiles, rows = dense_ref.shape[:3]
    half = rows // 2
    front = lax.axis_index("bz") == 0
    start = jnp.where(front, half, 0)
    for tile in range(tiles):
        lanes = slice(tile * LANES, (tile + 1) * LANES)
        for z in range(layers):
            for part in range(2):
                at = pl.ds(start + part, half // 2, stride=2)
                bulk_ref[2 * z + part, :, lanes] = pack_words(
                    dense_ref[z, tile, at, :], index_ref[z, tile, at, :]
                )
            line = [
                pack_words(dense_ref[z, tile, r : r + 1, :], index_ref[z, tile, r : r + 1, :])
                for r in (half - 1, half)
            ]
            bulk_ref[2 * layers, z : z + 1, lanes] = jnp.where(front, line[0], line[1])
            inside_ref[z : z + 1, lanes] = jnp.where(front, line[1], line[0])


def near_words(slab, first_ref, second_ref):
    me = lax.axis_index("bz")
    words = jnp.where(me == slab, first_ref[...], second_ref[...])
    return jnp.where(has_near(me == 0), words, 0)


def side_kernel(columns_ref, other_ref, first_ref, second_ref, ends_ref):
    layers = columns_ref.shape[0]
    front = lax.axis_index("bz") == 0
    lane_at = lax.broadcasted_iota(jnp.int32, (layers, LANES), 1)
    for slab in range(2):
        mine = front if slab == 0 else jnp.logical_not(front)
        columns = jnp.where(mine, columns_ref[...], other_ref[...])
        near = near_words(slab, first_ref, second_ref)
        cols = near.shape[1]
        columns = jnp.where(lane_at == 64, near[:, 0:1], columns)
        ends_ref[slab] = jnp.where(lane_at == 65, near[:, cols - 1 : cols], columns)


def has_near(front):
    me_y = lax.axis_index("by")
    return jnp.where(front, me_y > 0, me_y + 1 < lax.axis_size("by"))


def fill_weights(weights_ref, rows):
    cols = weights_ref.shape[0] - LANES
    row = lax.broadcasted_iota(jnp.int32, (cols, 2 * cols), 0)
    at = lax.broadcasted_iota(jnp.int32, (cols, 2 * cols), 1)
    centre = lax.shift_right_logical(at, 1)
    beside = centre - 1 + 2 * (at & 1)
    weights_ref[0:cols, :] = jnp.where(
        row == centre, 3.0, jnp.where(row == beside, 1.0, 0.0)
    ).astype(jnp.bfloat16)
    row = lax.broadcasted_iota(jnp.int32, (LANES, 2 * LANES), 0)
    at = lax.broadcasted_iota(jnp.int32, (LANES, 2 * LANES), 1)
    right = ((row < rows) | (row == 64)) & (at == 2 * LANES - 1)
    left = (((row >= rows) & (row < 2 * rows)) | (row == 65)) & (at == 0)
    weights_ref[cols : cols + LANES, 0 : 2 * LANES] = jnp.where(right | left, 1.0, 0.0).astype(
        jnp.bfloat16
    )


def lane_maps(rows):
    lane_at = lax.broadcasted_iota(jnp.int32, (8, LANES), 1)
    sub_at = lax.broadcasted_iota(jnp.int32, (8, LANES), 0)
    return lane_at & (rows - 1), lane_at < 2 * rows, sub_at


def classify_rows(read_cells, tables, cells_ref, layers, tiles):
    total = float(2 * layers)
    for z in range(layers):
        for tile in range(tiles):
            even = cell_values(*read_cells(z, 0, tile), tables, total)
            odd = cell_values(*read_cells(z, 1, tile), tables, total)
            for channel in range(4):
                base = (z * 4 + channel) * 16
                block = jnp.concatenate([even[channel], odd[channel]], axis=0)
                cells_ref[base : base + 16, tile * LANES : (tile + 1) * LANES] = block.astype(jnp.bfloat16)


def rounded(value):
    return value.astype(jnp.bfloat16).astype(jnp.float32)


def cells_kernel(dense_ref, index_ref, tables_ref, cells_ref, weights_ref):
    layers, tiles, rows = dense_ref.shape[:3]
    half = rows // 2
    start = lax.axis_index("bz") * half
    fill_weights(weights_ref, rows)

    def read_cells(z, part, tile):
        at = pl.ds(start + part, half // 2, stride=2)
        return dense_ref[z, tile, at, :], index_ref[z, tile, at, :]

    classify_rows(read_cells, read_tables(tables_ref), cells_ref, layers, tiles)


def halo_kernel(
    rows, beside_ref, across_ref, tables_ref, weights_ref, added_ref, ends_ref, values_ref, keep_ref
):
    layers = beside_ref.shape[1]
    cols = weights_ref.shape[0] - LANES
    size = layers * 64
    depth = 2 * layers
    front = lax.axis_index("bz") == 0
    start = lax.axis_index("bz") * (rows // 2)
    me_x = lax.axis_index("bx")
    even_x = lax.rem(me_x, 2) == 0
    tables = read_tables(tables_ref)
    side_lane, has_side, sub_at = lane_maps(rows)
    masks = [has_side & (side_lane == start + 2 * sub_at + part) for part in range(2)]
    lane_at = lax.broadcasted_iota(jnp.int32, (layers, LANES), 1)
    is_right = (lane_at < rows) | (lane_at == 64)
    for slab in range(2):
        right = jnp.where(even_x, beside_ref[slab], across_ref[slab])
        left = jnp.where(even_x, across_ref[slab], beside_ref[slab])
        right = jnp.where(me_x + 1 < lax.axis_size("bx"), right, 0)
        left = jnp.where(me_x > 0, left, 0)
        words = jnp.where(is_right, right, left)
        values = cell_values(*unpack_words(words), tables, float(depth))
        for channel in range(4):
            values_ref[channel] = values[channel]
        for z in range(layers):
            for channel in range(4):
                line = jnp.broadcast_to(values_ref[channel, z : z + 1, :], (8, LANES))
                block = jnp.concatenate([jnp.where(mask, line, 0.0) for mask in masks], axis=0)
                at = slab * size + (z * 4 + channel) * 16
                ends_ref[at : at + 16, :] = block.astype(jnp.bfloat16)
        for side in range(2):
            row = jnp.where(front, 64, rows // 2 - 1) if side == 0 else jnp.where(front, rows // 2, 64)
            twin = jnp.where(row == 64, 65, row + rows)
            keep = (lane_at == row) | (lane_at == twin)
            for channel in range(4):
                at = pl.ds(slab * layers * 8 + side * 4 + channel, layers, stride=8)
                keep_ref[at, :] = jnp.where(keep, values[channel], 0.0)
    ends_ref[2 * size :, :] = keep_ref[...].astype(jnp.bfloat16)
    added = jnp.dot(
        ends_ref[...], weights_ref[cols : cols + LANES, 0 : 2 * LANES], preferred_element_type=jnp.float32
    )
    for index in range(2):
        added_ref[index] = added[:, index * LANES : (index + 1) * LANES]


def along_columns(cells, weights_ref, added, store):
    cols = cells.shape[1]
    tiles = 2 * cols // LANES
    result = jnp.dot(cells, weights_ref[0:cols, :], preferred_element_type=jnp.float32)
    for tile in range(tiles):
        block = result[:, tile * LANES : (tile + 1) * LANES]
        if tile in (0, tiles - 1):
            block = block + added(0 if tile == 0 else 1)
        store(tile, rounded(block))


def own_kernel(cells_ref, weights_ref, added_ref, along_ref):
    size = cells_ref.shape[0]
    mine = pl.multiple_of(lax.axis_index("bz") * size, size)

    def store(tile, block):
        along_ref[tile] = block

    along_columns(cells_ref[...], weights_ref, lambda i: added_ref[i, pl.ds(mine, size), :], store)


def other_kernel(bulk_ref, tables_ref, weights_ref, added_ref, own_ref, along_ref, cells_ref):
    layers = (bulk_ref.shape[0] - 1) // 2
    cols = bulk_ref.shape[2]
    size = own_ref.shape[1]
    me = lax.axis_index("bz")
    pad = size // layers
    mine = pl.multiple_of(pad + me * size, pad)
    theirs = pl.multiple_of((1 - me) * size, pad)
    for tile in range(own_ref.shape[0]):
        along_ref[tile, 0:pad, :] = jnp.zeros((pad, LANES), jnp.float32)
        along_ref[tile, pad + 2 * size : 2 * pad + 2 * size, :] = jnp.zeros((pad, LANES), jnp.float32)
        along_ref[tile, pl.ds(mine, size), :] = own_ref[tile]

    def read_cells(z, part, tile):
        return unpack_words(bulk_ref[2 * z + part, :, tile * LANES : (tile + 1) * LANES])

    def store(tile, block):
        along_ref[tile, pl.ds(theirs + pad, size), :] = block

    classify_rows(read_cells, read_tables(tables_ref), cells_ref, layers, cols // LANES)
    along_columns(cells_ref[...], weights_ref, lambda i: added_ref[i, pl.ds(theirs, size), :], store)


def render_tile(tile, along_ref, lines_ref, flip, layers):
    sub_at = lax.broadcasted_iota(jnp.int32, (8, LANES), 0)
    top = sub_at == 0
    bottom = sub_at == 7

    def layer_rows(layer, channel):
        base = pl.multiple_of((layer * 4 + channel) * 16, 16)
        return [along_ref[tile, pl.ds(base + part * 8, 8), :] for part in range(2)]

    def over_layer(layer, image):
        here = [layer_rows(layer + 1, channel) for channel in range(4)]
        triple = [[3.0 * value for value in pair] for pair in here]
        for parity in range(2):
            clear = [1.0 - value for value in image[3]]
            updated = []
            line = (layer * 2 + parity) * 8
            for channel in range(4):
                beside = layer_rows(layer + 2 * parity, channel)
                even, odd = [rounded(beside[part] + triple[channel][part]) for part in range(2)]
                above = lines_ref[tile, pl.ds(line + channel, 8, stride=0), :]
                below = lines_ref[tile, pl.ds(line + 4 + channel, 8, stride=0), :]
                before_even = jnp.where(top, above, pltpu.roll(odd, 1, 0))
                after_odd = jnp.where(bottom, below, pltpu.roll(even, 7, 0))
                even_centre = 3.0 * even
                odd_centre = 3.0 * odd
                samples = [
                    before_even + even_centre, even_centre + odd, even + odd_centre, odd_centre + after_odd
                ]
                updated.append([image[channel][i] + clear[i] * samples[i] for i in range(4)])
            image = updated
        return image

    def one_slab(position, image):
        slab = position ^ flip
        for z in range(layers):
            image = over_layer(slab * layers + z, image)
        return image

    zero = jnp.zeros((8, LANES), jnp.float32)
    return lax.fori_loop(0, 2, one_slab, [[zero] * 4 for _ in range(4)])


def render_kernel(
    rank_ref, tables_ref, weights_ref, bulk_ref, inside_ref, first_ref, second_ref, added_ref, along_ref,
    out_ref, cells_ref, lines_ref, mixed_ref,
):
    layers, cols = inside_ref.shape
    depth = 2 * layers
    tiles = 2 * cols // LANES
    size = layers * 64
    me = lax.axis_index("bz")
    front = me == 0
    tables = read_tables(tables_ref)
    for slab in range(2):
        inside = jnp.where(me == slab, inside_ref[...], bulk_ref[2 * layers])
        near = near_words(slab, first_ref, second_ref)
        for side in range(2):
            use_near = front if side == 0 else jnp.logical_not(front)
            words = jnp.where(use_near, near, inside)
            for t in range(cols // LANES):
                values = cell_values(
                    *unpack_words(words[:, t * LANES : (t + 1) * LANES]), tables, float(depth)
                )
                for channel in range(4):
                    at = pl.ds(slab * layers * 8 + side * 4 + channel, layers, stride=8)
                    cells_ref[t, at, :] = values[channel]
    edge = sum(
        jnp.dot(
            cells_ref[t].astype(jnp.bfloat16),
            weights_ref[t * LANES : (t + 1) * LANES, :],
            preferred_element_type=jnp.float32,
        )
        for t in range(cols // LANES)
    )
    for tile in range(tiles):
        now = edge[:, tile * LANES : (tile + 1) * LANES]
        if tile in (0, tiles - 1):
            now = now + added_ref[0 if tile == 0 else 1, 2 * size : 2 * size + 8 * depth, :]
        now = rounded(now)
        triple = 3.0 * now
        empty = jnp.zeros((8, LANES), jnp.float32)
        for layer in range(depth):
            here = triple[layer * 8 : layer * 8 + 8]
            before = now[layer * 8 - 8 : layer * 8] if layer > 0 else empty
            after = now[layer * 8 + 8 : layer * 8 + 16] if layer + 1 < depth else empty
            lines_ref[tile, layer * 16 : layer * 16 + 8, :] = rounded(before + here)
            lines_ref[tile, layer * 16 + 8 : layer * 16 + 16, :] = rounded(after + here)

    def one_tile(tile, carry):
        image = render_tile(tile, along_ref, lines_ref, rank_ref[0], layers)
        lanes = pl.ds(pl.multiple_of(tile * LANES, LANES), LANES)
        for channel in range(4):
            for i in range(4):
                mixed_ref[channel, pl.ds(i, 8, stride=4), :] = image[channel][i]
            out_ref[channel, :, lanes] = mixed_ref[channel]
        return carry

    lax.fori_loop(0, tiles, one_tile, 0)


def two_slab_device(density, bin_index, tf_colour, tf_extinction, slab_rank):
    layers, rows, cols = density.shape
    half = rows // 2
    tiles = 2 * cols // LANES
    size = layers * 4 * half
    count_y, count_x = lax.axis_size("by"), lax.axis_size("bx")
    f32, bf16, i32 = jnp.float32, jnp.bfloat16, jnp.int32

    def call(kernel, name, out_shape, time, scratch_shapes=(), in_specs=None):
        def run(*operands):
            return pl.pallas_call(
                kernel,
                out_shape=out_shape,
                in_specs=in_specs or [VMEM] * len(operands),
                out_specs=(VMEM,) * len(out_shape) if isinstance(out_shape, tuple) else VMEM,
                scratch_shapes=scratch_shapes,
                compiler_params=pltpu.CompilerParams(vmem_limit_bytes=16 * 1024 * 1024),
                cost_estimate=cost(time),
                name=name,
            )(*operands)

        return run

    def both(route):
        return route + [(target, source) for source, target in route]

    blocks = (layers, cols // LANES, rows, LANES)
    row = pltpu.VMEM((layers, cols), i32)
    first, second, columns, dense, index, tables = call(
        stage_kernel,
        "stage_block",
        (
            row,
            row,
            pltpu.VMEM((layers, LANES), i32),
            pltpu.VMEM(blocks, f32),
            pltpu.VMEM(blocks, i32),
            pltpu.VMEM((8, 8, LANES), f32),
        ),
        1.2,
    )(*[pltpu.with_memory_space_constraint(x, pltpu.HBM) for x in (density, bin_index, tf_colour, tf_extinction)])
    def place(z, y, x):
        return (z * count_y + y) * count_x + x

    steps = range(count_y - 1)
    ring = [(place(0, y, 0), place(0, y + 1, 0)) for y in steps]
    ring += [(place(1, y + 1, 0), place(1, y, 0)) for y in steps]
    ring += [(place(0, count_y - 1, 0), place(1, count_y - 1, 0)), (place(1, 0, 0), place(0, 0, 0))]
    ring = [(source + x, target + x) for source, target in ring for x in range(count_x)]
    diagonal = [(place(1, y, x), place(0, y + 1, x)) for y in steps for x in range(count_x)]
    for z, y in ((0, 0), (1, count_y - 1)):
        diagonal += [(place(z, y, x), place(z, y, x + 1)) for x in range(0, count_x, 2)]
    axes = ("bz", "by", "bx")
    swap = [(0, 1), (1, 0)]
    second = lax.ppermute(second, axes, both(diagonal))
    other_columns = lax.ppermute(columns, "bz", swap)
    bulk, inside = call(pack_kernel, "pack_block", (pltpu.VMEM((2 * layers + 1, 8, cols), i32), row), 0.1)(
        dense, index
    )
    bulk = lax.ppermute(bulk, "bz", swap)
    first = lax.ppermute(first, axes, ring)

    cells, weights = call(
        cells_kernel,
        "own_cells",
        (pltpu.VMEM((size, cols), bf16), pltpu.VMEM((cols + LANES, 2 * cols), bf16)),
        0.5,
    )(dense, index, tables)
    ends = call(side_kernel, "side_columns", pltpu.VMEM((2, layers, LANES), i32), 0.1)(
        columns, other_columns, first, second
    )
    pairs = [(x, x + 1) for x in range(0, count_x, 2)]
    cross = [(x, (x + 1) % count_x) for x in range(1, count_x, 2)]
    beside = lax.ppermute(ends, "bx", both(pairs))
    across = lax.ppermute(ends, "bx", both(cross))
    added = call(
        functools.partial(halo_kernel, rows),
        "halo_columns",
        pltpu.VMEM((2, 2 * size + 16 * layers, LANES), f32),
        0.4,
        [
            pltpu.VMEM((2 * size + 16 * layers, LANES), bf16),
            pltpu.VMEM((4, layers, LANES), f32),
            pltpu.VMEM((16 * layers, LANES), f32),
        ],
    )(beside, across, tables, weights)
    along = call(own_kernel, "own_slab", pltpu.VMEM((tiles, size, LANES), f32), 2.0)(cells, weights, added)
    along = call(
        other_kernel,
        "other_slab",
        pltpu.VMEM((tiles, 2 * size + 2 * 4 * half, LANES), f32),
        0.8,
        [pltpu.VMEM((size, cols), bf16)],
    )(bulk, tables, weights, added, along)
    return call(
        render_kernel,
        "render_rows",
        jax.ShapeDtypeStruct((4, rows, 2 * cols), f32),
        3.0,
        [
            pltpu.VMEM((cols // LANES, 16 * layers, LANES), f32),
            pltpu.VMEM((tiles, 32 * layers, LANES), f32),
            pltpu.VMEM((4, rows, LANES), f32),
        ],
        [pl.BlockSpec(memory_space=pltpu.SMEM)] + [VMEM] * 8,
    )(slab_rank, tables, weights, bulk, inside, first, second, added, along)


def on_device(density, bin_index, tf_colour, tf_extinction, slab_rank):
    if lax.axis_size("bz") == 2:
        return two_slab_device(density, bin_index, tf_colour, tf_extinction, slab_rank)
    return general_device(density, bin_index, tf_colour, tf_extinction, slab_rank)


def solution(mesh):
    return jax.shard_map(
        on_device,
        mesh=mesh,
        in_specs=(P("bz", "by", "bx"), P("bz", "by", "bx"), P(), P(), P()),
        out_specs=P(None, ("by", "bz"), "bx"),
        check_vma=False,
    )
```

```python
import jax
import jax.numpy as jnp
from jax import lax
from jax.experimental import pallas as pl
from jax.experimental.pallas import tpu as pltpu
from jax.sharding import PartitionSpec as P


def with_halo(block, sides, width):
    for axis, dim in sides:
        count = lax.axis_size(axis)
        forward = [(i, i + 1) for i in range(count - 1)]
        backward = [(target, source) for source, target in forward]
        low = lax.ppermute(
            lax.slice_in_dim(block, block.shape[dim] - width, None, axis=dim), axis, forward
        )
        high = lax.ppermute(lax.slice_in_dim(block, 0, width, axis=dim), axis, backward)
        block = jnp.concatenate([low, block, high], axis=dim)
    return block


def partner_2(block, axis, stride):
    count = lax.axis_size(axis)
    route = []
    for low in range(count):
        high = low | 1 << stride
        if high != low and high < count:
            route += [(low, high), (high, low)]
    return lax.ppermute(block, axis, route)


def resample_table(length):
    row_index = lax.broadcasted_iota(jnp.int32, (2 * length, length + 2), 0)
    col_index = lax.broadcasted_iota(jnp.int32, (2 * length, length + 2), 1)
    centre = row_index // 2
    parity = row_index % 2
    weights_table = jnp.where(col_index == centre + 1, 0.75, 0.0)
    weights_table = weights_table + jnp.where((col_index == centre) & (parity == 0), 0.25, 0.0)
    weights_table = weights_table + jnp.where((col_index == centre + 2) & (parity == 1), 0.25, 0.0)
    return weights_table.astype(jnp.bfloat16)


def blend_over(in_front, behind):
    return in_front + (1.0 - in_front[3])[None] * behind


def classify(density, bin_index, tf_colour, tf_extinction, total_depth):
    depth_cells, height_cells, width_cells = density.shape
    lookup = jnp.concatenate([tf_colour, tf_extinction[None, :]], axis=0)
    table_size = lookup.shape[1]
    bin_rows = lax.broadcasted_iota(jnp.int32, (table_size, 1), 0)
    flat_bins = bin_index.reshape(depth_cells, height_cells * width_cells)
    flat_density = density.reshape(depth_cells, height_cells * width_cells)

    def one_layer(layer, result):
        layer_bins = lax.dynamic_index_in_dim(flat_bins, layer, 0, keepdims=True)
        layer_density = lax.dynamic_index_in_dim(flat_density, layer, 0, keepdims=False)
        one_hot = (layer_bins == bin_rows).astype(jnp.bfloat16)
        values = jnp.dot(lookup, one_hot, preferred_element_type=jnp.float32)
        opacity = 1.0 - jnp.exp(-values[3] * layer_density / total_depth)
        cells = jnp.concatenate([values[:3] * opacity[None], opacity[None]], axis=0).astype(
            jnp.bfloat16
        )
        return lax.dynamic_update_slice_in_dim(result, cells[:, None], layer, 1)

    start_cells = jnp.zeros((4, depth_cells, height_cells * width_cells), jnp.bfloat16)
    classified = lax.fori_loop(0, depth_cells, one_layer, start_cells)
    return classified.reshape(4, depth_cells, height_cells, width_cells)


def general_device(density, bin_index, tf_colour, tf_extinction, slab_rank):
    slab_count = lax.axis_size("bz")
    depth_cells, height_cells, width_cells = density.shape
    total_depth = float(depth_cells * slab_count)
    colour_cells = classify(density, bin_index, tf_colour, tf_extinction, total_depth)
    padded = with_halo(colour_cells, (("bz", 1), ("by", 2), ("bx", 3)), 1)
    along_x = jnp.einsum(
        "czyq,pq->czyp", padded, resample_table(width_cells), preferred_element_type=jnp.float32
    ).astype(jnp.bfloat16)
    y_table = resample_table(height_cells)

    def add_sample(sample_index, image_now):
        centre = sample_index // 2
        parity = sample_index % 2
        layers = lax.dynamic_slice_in_dim(along_x, centre, 3, 1).astype(jnp.float32)
        lower_weight = jnp.where(parity == 0, 0.25, 0.0)
        upper_weight = jnp.where(parity == 1, 0.25, 0.0)
        mixed_layer = (
            lower_weight * layers[:, 0] + 0.75 * layers[:, 1] + upper_weight * layers[:, 2]
        ).astype(jnp.bfloat16)
        sample = jnp.einsum("qy,cyp->cqp", y_table, mixed_layer, preferred_element_type=jnp.float32)
        return blend_over(image_now, sample)

    start_image = jnp.zeros((4, 2 * height_cells, 2 * width_cells), jnp.float32)
    slab_image = lax.fori_loop(0, 2 * depth_cells, add_sample, start_image)
    rows_piece = 2 * height_cells // slab_count
    my_index = lax.axis_index("bz")
    bit_levels = slab_count.bit_length() - 1
    composite = slab_image.reshape((4,) + (2,) * bit_levels + (rows_piece, 2 * width_cells))
    my_rank = lax.dynamic_index_in_dim(slab_rank, my_index, 0, keepdims=False)
    for level in range(bit_levels):
        position = bit_levels - level
        my_bit = my_index // 2**level % 2
        kept_half = lax.dynamic_index_in_dim(composite, my_bit, position, keepdims=False)
        outgoing = lax.dynamic_index_in_dim(composite, 1 - my_bit, position, keepdims=False)
        incoming = partner_2(outgoing, "bz", level)
        partner = my_index + (1 - 2 * my_bit) * 2**level
        partner_rank = lax.dynamic_index_in_dim(slab_rank, partner, 0, keepdims=False)
        mine_first = my_rank < partner_rank
        composite = blend_over(
            jnp.where(mine_first, kept_half, incoming), jnp.where(mine_first, incoming, kept_half)
        )
    return composite


LANES = 128
LEVELS = 65535.0
VMEM = pl.BlockSpec(memory_space=pltpu.VMEM)


def pack_words(density, bins):
    level = (density * LEVELS + 0.5).astype(jnp.int32)
    return lax.shift_left(level, 16) | bins


def unpack_words(words):
    density = lax.shift_right_logical(words, 16).astype(jnp.float32) * (1.0 / LEVELS)
    return density, words & 0xFFFF


def cell_values(density, bins, tables, depth):
    low_bits = bins & (LANES - 1)
    upper = bins >= LANES

    def pick(channel):
        first, second = tables[channel]
        return jnp.where(
            upper,
            jnp.take_along_axis(second, low_bits, axis=1, mode="promise_in_bounds"),
            jnp.take_along_axis(first, low_bits, axis=1, mode="promise_in_bounds"),
        )

    opacity = (1.0 - jnp.exp(-pick(3) * density / depth)) * (1.0 / 64.0)
    return [pick(0) * opacity, pick(1) * opacity, pick(2) * opacity, opacity]


def read_tables(tables_ref):
    return [[tables_ref[2 * channel + half] for half in range(2)] for channel in range(4)]


def cost(microseconds):
    return pl.CostEstimate(
        flops=int(1e9 * microseconds), bytes_accessed=int(3.6e6 * microseconds), transcendentals=0
    )


def stage_kernel(
    density_ref, bins_ref, colour_ref, extinction_ref,
    first_ref, second_ref, columns_ref, dense_ref, index_ref, tables_ref,
):
    layers, rows, cols = density_ref.shape
    front = lax.axis_index("bz") == 0
    row_at = lax.broadcasted_iota(jnp.int32, (rows, LANES), 0)
    lane_at = lax.broadcasted_iota(jnp.int32, (rows, LANES), 1)
    for z in range(layers):
        first = pack_words(density_ref[z, :, 0:1], bins_ref[z, :, 0:1])
        last = pack_words(density_ref[z, :, cols - 1 : cols], bins_ref[z, :, cols - 1 : cols])
        line = jnp.where(lane_at == row_at, first, 0) + jnp.where(lane_at == row_at + rows, last, 0)
        columns_ref[z : z + 1, :] = jnp.sum(line, axis=0, keepdims=True)
        top, bottom = [
            pack_words(density_ref[z, r : r + 1, :], bins_ref[z, r : r + 1, :]) for r in (0, rows - 1)
        ]
        first_ref[z : z + 1, :] = jnp.where(front, bottom, top)
        second_ref[z : z + 1, :] = jnp.where(front, top, bottom)
        for tile in range(cols // LANES):
            lanes = slice(tile * LANES, (tile + 1) * LANES)
            dense_ref[z, tile, 0:rows] = density_ref[z, :, lanes]
            index_ref[z, tile, 0:rows] = bins_ref[z, :, lanes]
    colour = colour_ref[...].astype(jnp.float32)
    extinction = extinction_ref[...].astype(jnp.float32).reshape(1, 2 * LANES)
    for channel in range(4):
        line = extinction if channel == 3 else colour[channel : channel + 1]
        for half in range(2):
            tables_ref[2 * channel + half] = jnp.broadcast_to(
                line[:, half * LANES : (half + 1) * LANES], (8, LANES)
            )


def pack_kernel(dense_ref, index_ref, columns_ref, bulk_ref, inside_ref):
    layers, tiles, rows = dense_ref.shape[0], dense_ref.shape[1], dense_ref.shape[2] - 8
    half = rows // 2
    front = lax.axis_index("bz") == 0
    start = jnp.where(front, half, 0)
    for tile in range(tiles):
        lanes = slice(tile * LANES, (tile + 1) * LANES)
        bulk_ref[2 * layers + 1, :, lanes] = columns_ref[...]
        for z in range(layers):
            for part in range(2):
                at = pl.ds(start + part, half // 2, stride=2)
                bulk_ref[2 * z + part, :, lanes] = pack_words(
                    dense_ref[z, tile, at, :], index_ref[z, tile, at, :]
                )
            line = [
                pack_words(dense_ref[z, tile, r : r + 1, :], index_ref[z, tile, r : r + 1, :])
                for r in (half - 1, half)
            ]
            bulk_ref[2 * layers, z : z + 1, lanes] = jnp.where(front, line[0], line[1])
            inside_ref[z : z + 1, lanes] = jnp.where(front, line[1], line[0])


def near_words(slab, first_ref, second_ref):
    me = lax.axis_index("bz")
    words = jnp.where(me == slab, first_ref[...], second_ref[...])
    return jnp.where(has_near(me == 0), words, 0)


def side_kernel(columns_ref, bulk_ref, first_ref, second_ref, along_ref, ends_ref):
    layers = columns_ref.shape[0]
    front = lax.axis_index("bz") == 0
    lane_at = lax.broadcasted_iota(jnp.int32, (layers, LANES), 1)
    for slab in range(2):
        mine = front if slab == 0 else jnp.logical_not(front)
        columns = jnp.where(mine, columns_ref[...], bulk_ref[2 * layers + 1, :, 0:LANES])
        near = near_words(slab, first_ref, second_ref)
        cols = near.shape[1]
        columns = jnp.where(lane_at == 64, near[:, 0:1], columns)
        ends_ref[slab] = jnp.where(lane_at == 65, near[:, cols - 1 : cols], columns)


def has_near(front):
    me_y = lax.axis_index("by")
    return jnp.where(front, me_y > 0, me_y + 1 < lax.axis_size("by"))


def fill_weights(weights_ref, rows):
    cols = weights_ref.shape[0] - LANES
    row = lax.broadcasted_iota(jnp.int32, (cols, 2 * cols), 0)
    at = lax.broadcasted_iota(jnp.int32, (cols, 2 * cols), 1)
    centre = lax.shift_right_logical(at, 1)
    beside = centre - 1 + 2 * (at & 1)
    weights_ref[0:cols, :] = jnp.where(
        row == centre, 3.0, jnp.where(row == beside, 1.0, 0.0)
    ).astype(jnp.bfloat16)
    row = lax.broadcasted_iota(jnp.int32, (LANES, 2 * LANES), 0)
    at = lax.broadcasted_iota(jnp.int32, (LANES, 2 * LANES), 1)
    right = ((row < rows) | (row == 64)) & (at == 2 * LANES - 1)
    left = (((row >= rows) & (row < 2 * rows)) | (row == 65)) & (at == 0)
    weights_ref[cols : cols + LANES, 0 : 2 * LANES] = jnp.where(right | left, 1.0, 0.0).astype(
        jnp.bfloat16
    )


def lane_maps(rows):
    lane_at = lax.broadcasted_iota(jnp.int32, (8, LANES), 1)
    sub_at = lax.broadcasted_iota(jnp.int32, (8, LANES), 0)
    return lane_at & (rows - 1), lane_at < 2 * rows, sub_at


def classify_rows(read_cells, tables, cells_ref, layers, tiles):
    total = float(2 * layers)
    for z in range(layers):
        for tile in range(tiles):
            even = cell_values(*read_cells(z, 0, tile), tables, total)
            odd = cell_values(*read_cells(z, 1, tile), tables, total)
            for channel in range(4):
                base = (z * 4 + channel) * 16
                block = jnp.concatenate([even[channel], odd[channel]], axis=0)
                cells_ref[base : base + 16, tile * LANES : (tile + 1) * LANES] = block.astype(jnp.bfloat16)


def rounded(value):
    return value.astype(jnp.bfloat16).astype(jnp.float32)


def cells_kernel(dense_ref, index_ref, tables_ref, cells_ref, weights_ref):
    layers, tiles, rows = dense_ref.shape[0], dense_ref.shape[1], dense_ref.shape[2] - 8
    half = rows // 2
    start = lax.axis_index("bz") * half
    fill_weights(weights_ref, rows)

    def read_cells(z, part, tile):
        at = pl.ds(start + part, half // 2, stride=2)
        return dense_ref[z, tile, at, :], index_ref[z, tile, at, :]

    classify_rows(read_cells, read_tables(tables_ref), cells_ref, layers, tiles)


def along_columns(cells, weights_ref, store):
    cols = cells.shape[1]
    tiles = 2 * cols // LANES
    result = jnp.dot(cells, weights_ref[0:cols, :], preferred_element_type=jnp.float32)
    for tile in range(tiles):
        block = result[:, tile * LANES : (tile + 1) * LANES]
        store(tile, block if tile in (0, tiles - 1) else rounded(block))


def own_kernel(cells_ref, weights_ref, along_ref):
    size = cells_ref.shape[0]
    pad = along_ref.shape[1] // 2 - size
    mine = pl.multiple_of(pad + lax.axis_index("bz") * size, pad)

    def store(tile, block):
        along_ref[tile, 0:pad, :] = jnp.zeros((pad, LANES), jnp.float32)
        along_ref[tile, pad + 2 * size :, :] = jnp.zeros((pad, LANES), jnp.float32)
        along_ref[tile, pl.ds(mine, size), :] = block

    along_columns(cells_ref[...], weights_ref, store)


def other_kernel(bulk_ref, tables_ref, weights_ref, ends_ref, own_ref, along_ref, cells_ref):
    layers = (bulk_ref.shape[0] - 2) // 2
    cols = bulk_ref.shape[2]
    size = cells_ref.shape[0]
    pad = along_ref.shape[1] // 2 - size
    theirs = pl.multiple_of(pad + (1 - lax.axis_index("bz")) * size, pad)

    def read_cells(z, part, tile):
        return unpack_words(bulk_ref[2 * z + part, :, tile * LANES : (tile + 1) * LANES])

    def store(tile, block):
        along_ref[tile, pl.ds(theirs, size), :] = block

    classify_rows(read_cells, read_tables(tables_ref), cells_ref, layers, cols // LANES)
    along_columns(cells_ref[...], weights_ref, store)


def edge_lines(now, lines_ref, depth):
    triple = 3.0 * now
    empty = jnp.zeros((8, LANES), jnp.float32)
    for layer in range(depth):
        here = triple[layer * 8 : layer * 8 + 8]
        before = now[layer * 8 - 8 : layer * 8] if layer > 0 else empty
        after = now[layer * 8 + 8 : layer * 8 + 16] if layer + 1 < depth else empty
        lines_ref[layer * 16 : layer * 16 + 8, :] = rounded(before + here)
        lines_ref[layer * 16 + 8 : layer * 16 + 16, :] = rounded(after + here)


def render_tile(along_ref, lines_ref, flip, layers):
    sub_at = lax.broadcasted_iota(jnp.int32, (8, LANES), 0)
    top = sub_at == 0
    bottom = sub_at == 7

    def one_slab(position, image):
        slab = position ^ flip
        view = along_ref.at[pl.ds(pl.multiple_of(slab * (layers * 64), 64), (layers + 2) * 64), :]
        lines = lines_ref.at[pl.ds(pl.multiple_of(slab * (layers * 16), 16), layers * 16 + 8), :]

        def layer_rows(layer, channel):
            base = (layer * 4 + channel) * 16
            return [view[base + part * 8 : base + part * 8 + 8, :] for part in range(2)]

        for z in range(layers):
            triple = [[3.0 * value for value in layer_rows(z + 1, channel)] for channel in range(4)]
            for parity in range(2):
                clear = [1.0 - value for value in image[3]]
                updated = []
                for channel in range(4):
                    beside = layer_rows(z + 2 * parity, channel)
                    even, odd = [rounded(beside[part] + triple[channel][part]) for part in range(2)]
                    line = (z * 2 + parity) * 8 + channel
                    above = lines[pl.ds(line, 8, stride=0), :]
                    below = lines[pl.ds(line + 4, 8, stride=0), :]
                    before_even = jnp.where(top, above, pltpu.roll(odd, 1, 0))
                    after_odd = jnp.where(bottom, below, pltpu.roll(even, 7, 0))
                    even_centre = 3.0 * even
                    odd_centre = 3.0 * odd
                    samples = [
                        before_even + even_centre,
                        even_centre + odd,
                        even + odd_centre,
                        odd_centre + after_odd,
                    ]
                    updated.append([image[channel][i] + clear[i] * samples[i] for i in range(4)])
                image = updated
        return image

    zero = jnp.zeros((8, LANES), jnp.float32)
    return lax.fori_loop(0, 2, one_slab, [[zero] * 4 for _ in range(4)])


def store_tile(image, mixed_ref, out_ref, lanes):
    for channel in range(4):
        for i in range(4):
            mixed_ref[channel, pl.ds(i, 8, stride=4), :] = image[channel][i]
        out_ref[channel, :, lanes] = mixed_ref[channel, 0:32]


def inner_kernel(
    rank_ref, tables_ref, weights_ref, bulk_ref, inside_ref, first_ref, second_ref, along_ref,
    image_ref, edge_ref, cells_ref, lines_ref, mixed_ref,
):
    layers, cols = inside_ref.shape
    depth = 2 * layers
    tiles = 2 * cols // LANES
    me = lax.axis_index("bz")
    front = me == 0
    tables = read_tables(tables_ref)
    for slab in range(2):
        inside = jnp.where(me == slab, inside_ref[...], bulk_ref[2 * layers])
        near = near_words(slab, first_ref, second_ref)
        for side in range(2):
            use_near = front if side == 0 else jnp.logical_not(front)
            words = jnp.where(use_near, near, inside)
            for t in range(cols // LANES):
                values = cell_values(
                    *unpack_words(words[:, t * LANES : (t + 1) * LANES]), tables, float(depth)
                )
                for channel in range(4):
                    at = pl.ds(slab * layers * 8 + side * 4 + channel, layers, stride=8)
                    cells_ref[t, at, :] = values[channel]
    edge = sum(
        jnp.dot(
            cells_ref[t, 0 : 8 * depth].astype(jnp.bfloat16),
            weights_ref[t * LANES : (t + 1) * LANES, :],
            preferred_element_type=jnp.float32,
        )
        for t in range(cols // LANES)
    )
    for tile in range(tiles):
        now = edge[:, tile * LANES : (tile + 1) * LANES]
        if tile in (0, tiles - 1):
            edge_ref[0 if tile == 0 else 1] = now
        else:
            edge_lines(rounded(now), lines_ref.at[tile - 1], depth)

    def one_tile(index, carry):
        image = render_tile(along_ref.at[index + 1], lines_ref.at[index], rank_ref[0], layers)
        store_tile(image, mixed_ref, image_ref, pl.ds(pl.multiple_of(index * LANES, LANES), LANES))
        return carry

    lax.fori_loop(0, tiles - 2, one_tile, 0)


def outer_kernel(
    rank_ref, tables_ref, weights_ref, beside_ref, across_ref, along_ref, edge_ref, image_ref,
    out_ref, ends_ref, values_ref, keep_ref, fixed_ref, lines_ref, mixed_ref,
):
    rows = out_ref.shape[1]
    cols = out_ref.shape[2] // 2
    layers = beside_ref.shape[1]
    depth = 2 * layers
    tiles = 2 * cols // LANES
    pad = 64
    size = layers * pad
    front = lax.axis_index("bz") == 0
    start = lax.axis_index("bz") * (rows // 2)
    me_x = lax.axis_index("bx")
    even_x = lax.rem(me_x, 2) == 0
    tables = read_tables(tables_ref)
    side_lane, has_side, sub_at = lane_maps(rows)
    masks = [has_side & (side_lane == start + 2 * sub_at + part) for part in range(2)]
    lane_at = lax.broadcasted_iota(jnp.int32, (layers, LANES), 1)
    is_right = (lane_at < rows) | (lane_at == 64)
    for slab in range(2):
        right = jnp.where(even_x, beside_ref[slab], across_ref[slab])
        left = jnp.where(even_x, across_ref[slab], beside_ref[slab])
        right = jnp.where(me_x + 1 < lax.axis_size("bx"), right, 0)
        left = jnp.where(me_x > 0, left, 0)
        words = jnp.where(is_right, right, left)
        values = cell_values(*unpack_words(words), tables, float(depth))
        for channel in range(4):
            values_ref[slab * 4 + channel, 0:layers] = values[channel]
        for z in range(layers):
            for channel in range(4):
                line = values_ref[slab * 4 + channel, pl.ds(z, 8, stride=0), :]
                block = jnp.concatenate([jnp.where(mask, line, 0.0) for mask in masks], axis=0)
                at = slab * size + (z * 4 + channel) * 16
                ends_ref[at : at + 16, :] = block.astype(jnp.bfloat16)
        for side in range(2):
            row = jnp.where(front, 64, rows // 2 - 1) if side == 0 else jnp.where(front, rows // 2, 64)
            twin = jnp.where(row == 64, 65, row + rows)
            keep = (lane_at == row) | (lane_at == twin)
            for channel in range(4):
                at = pl.ds(slab * layers * 8 + side * 4 + channel, layers, stride=8)
                keep_ref[at, :] = jnp.where(keep, values[channel], 0.0)
    ends_ref[2 * size :, :] = keep_ref[0 : 8 * depth].astype(jnp.bfloat16)
    added = jnp.dot(
        ends_ref[...], weights_ref[cols : cols + LANES, 0 : 2 * LANES], preferred_element_type=jnp.float32
    )
    for index, tile in enumerate((0, tiles - 1)):
        block = added[:, index * LANES : (index + 1) * LANES]
        fixed_ref[index, 0:pad, :] = jnp.zeros((pad, LANES), jnp.float32)
        fixed_ref[index, pad + 2 * size :, :] = jnp.zeros((pad, LANES), jnp.float32)
        fixed_ref[index, pad : pad + 2 * size, :] = rounded(
            along_ref[tile, pad : pad + 2 * size, :] + block[0 : 2 * size]
        )
        edge_lines(rounded(edge_ref[index] + block[2 * size :]), lines_ref.at[index], depth)
    out_ref[:, :, LANES : 2 * cols - LANES] = image_ref[...]

    def one_tile(index, carry):
        image = render_tile(fixed_ref.at[index], lines_ref.at[index], rank_ref[0], layers)
        lanes = pl.ds(pl.multiple_of(index * (2 * cols - LANES), LANES), LANES)
        store_tile(image, mixed_ref, out_ref, lanes)
        return carry

    lax.fori_loop(0, 2, one_tile, 0)


def two_slab_device(density, bin_index, tf_colour, tf_extinction, slab_rank):
    layers, rows, cols = density.shape
    half = rows // 2
    tiles = 2 * cols // LANES
    size = layers * 4 * half
    count_y, count_x = lax.axis_size("by"), lax.axis_size("bx")
    f32, bf16, i32 = jnp.float32, jnp.bfloat16, jnp.int32

    def call(kernel, name, out_shape, time, scratch_shapes=(), in_specs=None, aliases={}):
        def run(*operands):
            return pl.pallas_call(
                kernel,
                out_shape=out_shape,
                in_specs=in_specs or [VMEM] * len(operands),
                out_specs=(VMEM,) * len(out_shape) if isinstance(out_shape, tuple) else VMEM,
                scratch_shapes=scratch_shapes,
                input_output_aliases=aliases,
                compiler_params=pltpu.CompilerParams(vmem_limit_bytes=16 * 1024 * 1024),
                cost_estimate=cost(time),
                name=name,
            )(*operands)

        return run

    def both(route):
        return route + [(target, source) for source, target in route]

    blocks = (layers, cols // LANES, rows + 8, LANES)
    row = pltpu.VMEM((layers, cols), i32)
    first, second, columns, dense, index, tables = call(
        stage_kernel,
        "stage_block",
        (
            row,
            row,
            pltpu.VMEM((layers, LANES), i32),
            pltpu.VMEM(blocks, f32),
            pltpu.VMEM(blocks, i32),
            pltpu.VMEM((8, 8, LANES), f32),
        ),
        1.2,
    )(*[pltpu.with_memory_space_constraint(x, pltpu.HBM) for x in (density, bin_index, tf_colour, tf_extinction)])
    bulk, inside = call(
        pack_kernel, "pack_block", (pltpu.VMEM((2 * layers + 2, 8, cols), i32), row), 0.1
    )(dense, index, columns)

    def place(z, y, x):
        return (z * count_y + y) * count_x + x

    steps = range(count_y - 1)
    ring = [(place(0, y, 0), place(0, y + 1, 0)) for y in steps]
    ring += [(place(1, y + 1, 0), place(1, y, 0)) for y in steps]
    ring += [(place(0, count_y - 1, 0), place(1, count_y - 1, 0)), (place(1, 0, 0), place(0, 0, 0))]
    ring = [(source + x, target + x) for source, target in ring for x in range(count_x)]
    diagonal = [(place(1, y, x), place(0, y + 1, x)) for y in steps for x in range(count_x)]
    for z, y in ((0, 0), (1, count_y - 1)):
        diagonal += [(place(z, y, x), place(z, y, x + 1)) for x in range(0, count_x, 2)]
    axes = ("bz", "by", "bx")
    bulk = lax.ppermute(bulk, "bz", [(0, 1), (1, 0)])
    first = lax.ppermute(first, axes, ring)
    second = lax.ppermute(second, axes, both(diagonal))

    cells, weights = call(
        cells_kernel,
        "own_cells",
        (pltpu.VMEM((size, cols), bf16), pltpu.VMEM((cols + LANES, 2 * cols), bf16)),
        0.5,
    )(dense, index, tables)
    whole = pltpu.VMEM((tiles, 2 * size + 2 * 4 * half, LANES), f32)
    along = call(own_kernel, "own_slab", whole, 0.4)(cells, weights)
    ends = call(side_kernel, "side_columns", pltpu.VMEM((2, layers, LANES), i32), 0.1)(
        columns, bulk, first, second, along
    )
    pairs = [(x, x + 1) for x in range(0, count_x, 2)]
    cross = [(x, (x + 1) % count_x) for x in range(1, count_x, 2)]
    beside = lax.ppermute(ends, "bx", both(pairs))
    across = lax.ppermute(ends, "bx", both(cross))
    along = call(other_kernel, "other_slab", whole, 0.8, [pltpu.VMEM((size, cols), bf16)], aliases={4: 0})(
        bulk, tables, weights, ends, along
    )
    smem = pl.BlockSpec(memory_space=pltpu.SMEM)
    lines = pltpu.VMEM((2, 32 * layers + 8, LANES), f32)
    image, edge = call(
        inner_kernel,
        "inner_tiles",
        (pltpu.VMEM((4, rows, (tiles - 2) * LANES), f32), pltpu.VMEM((2, 16 * layers, LANES), f32)),
        2.0,
        [pltpu.VMEM((cols // LANES, 16 * layers + 8, LANES), f32), lines, pltpu.VMEM((4, rows + 8, LANES), f32)],
        [smem] + [VMEM] * 7,
    )(slab_rank, tables, weights, bulk, inside, first, second, along)
    return call(
        outer_kernel,
        "outer_tiles",
        jax.ShapeDtypeStruct((4, rows, 2 * cols), f32),
        2.0,
        [
            pltpu.VMEM((2 * size + 16 * layers, LANES), bf16),
            pltpu.VMEM((8, 2 * layers, LANES), f32),
            pltpu.VMEM((16 * layers + 8, LANES), f32),
            pltpu.VMEM((2, 2 * size + 2 * 4 * half, LANES), f32),
            lines,
            pltpu.VMEM((4, rows + 8, LANES), f32),
        ],
        [smem] + [VMEM] * 7,
    )(slab_rank, tables, weights, beside, across, along, edge, image)


def on_device(density, bin_index, tf_colour, tf_extinction, slab_rank):
    if lax.axis_size("bz") == 2:
        return two_slab_device(density, bin_index, tf_colour, tf_extinction, slab_rank)
    return general_device(density, bin_index, tf_colour, tf_extinction, slab_rank)


def solution(mesh):
    return jax.shard_map(
        on_device,
        mesh=mesh,
        in_specs=(P("bz", "by", "bx"), P("bz", "by", "bx"), P(), P(), P()),
        out_specs=P(None, ("by", "bz"), "bx"),
        check_vma=False,
    )
```

```python
import jax
import jax.numpy as jnp
from jax import lax
from jax.experimental import pallas as pl
from jax.experimental.pallas import tpu as pltpu
from jax.sharding import PartitionSpec as P


def with_halo(block, sides, width):
    for axis, dim in sides:
        count = lax.axis_size(axis)
        forward = [(i, i + 1) for i in range(count - 1)]
        backward = [(target, source) for source, target in forward]
        low = lax.ppermute(
            lax.slice_in_dim(block, block.shape[dim] - width, None, axis=dim), axis, forward
        )
        high = lax.ppermute(lax.slice_in_dim(block, 0, width, axis=dim), axis, backward)
        block = jnp.concatenate([low, block, high], axis=dim)
    return block


def partner_2(block, axis, stride):
    count = lax.axis_size(axis)
    route = []
    for low in range(count):
        high = low | 1 << stride
        if high != low and high < count:
            route += [(low, high), (high, low)]
    return lax.ppermute(block, axis, route)


def resample_table(length):
    row_index = lax.broadcasted_iota(jnp.int32, (2 * length, length + 2), 0)
    col_index = lax.broadcasted_iota(jnp.int32, (2 * length, length + 2), 1)
    centre = row_index // 2
    parity = row_index % 2
    weights_table = jnp.where(col_index == centre + 1, 0.75, 0.0)
    weights_table = weights_table + jnp.where((col_index == centre) & (parity == 0), 0.25, 0.0)
    weights_table = weights_table + jnp.where((col_index == centre + 2) & (parity == 1), 0.25, 0.0)
    return weights_table.astype(jnp.bfloat16)


def blend_over(in_front, behind):
    return in_front + (1.0 - in_front[3])[None] * behind


def classify(density, bin_index, tf_colour, tf_extinction, total_depth):
    depth_cells, height_cells, width_cells = density.shape
    lookup = jnp.concatenate([tf_colour, tf_extinction[None, :]], axis=0)
    table_size = lookup.shape[1]
    bin_rows = lax.broadcasted_iota(jnp.int32, (table_size, 1), 0)
    flat_bins = bin_index.reshape(depth_cells, height_cells * width_cells)
    flat_density = density.reshape(depth_cells, height_cells * width_cells)

    def one_layer(layer, result):
        layer_bins = lax.dynamic_index_in_dim(flat_bins, layer, 0, keepdims=True)
        layer_density = lax.dynamic_index_in_dim(flat_density, layer, 0, keepdims=False)
        one_hot = (layer_bins == bin_rows).astype(jnp.bfloat16)
        values = jnp.dot(lookup, one_hot, preferred_element_type=jnp.float32)
        opacity = 1.0 - jnp.exp(-values[3] * layer_density / total_depth)
        cells = jnp.concatenate([values[:3] * opacity[None], opacity[None]], axis=0).astype(
            jnp.bfloat16
        )
        return lax.dynamic_update_slice_in_dim(result, cells[:, None], layer, 1)

    start_cells = jnp.zeros((4, depth_cells, height_cells * width_cells), jnp.bfloat16)
    classified = lax.fori_loop(0, depth_cells, one_layer, start_cells)
    return classified.reshape(4, depth_cells, height_cells, width_cells)


def general_device(density, bin_index, tf_colour, tf_extinction, slab_rank):
    slab_count = lax.axis_size("bz")
    depth_cells, height_cells, width_cells = density.shape
    total_depth = float(depth_cells * slab_count)
    colour_cells = classify(density, bin_index, tf_colour, tf_extinction, total_depth)
    padded = with_halo(colour_cells, (("bz", 1), ("by", 2), ("bx", 3)), 1)
    along_x = jnp.einsum(
        "czyq,pq->czyp", padded, resample_table(width_cells), preferred_element_type=jnp.float32
    ).astype(jnp.bfloat16)
    y_table = resample_table(height_cells)

    def add_sample(sample_index, image_now):
        centre = sample_index // 2
        parity = sample_index % 2
        layers = lax.dynamic_slice_in_dim(along_x, centre, 3, 1).astype(jnp.float32)
        lower_weight = jnp.where(parity == 0, 0.25, 0.0)
        upper_weight = jnp.where(parity == 1, 0.25, 0.0)
        mixed_layer = (
            lower_weight * layers[:, 0] + 0.75 * layers[:, 1] + upper_weight * layers[:, 2]
        ).astype(jnp.bfloat16)
        sample = jnp.einsum("qy,cyp->cqp", y_table, mixed_layer, preferred_element_type=jnp.float32)
        return blend_over(image_now, sample)

    start_image = jnp.zeros((4, 2 * height_cells, 2 * width_cells), jnp.float32)
    slab_image = lax.fori_loop(0, 2 * depth_cells, add_sample, start_image)
    rows_piece = 2 * height_cells // slab_count
    my_index = lax.axis_index("bz")
    bit_levels = slab_count.bit_length() - 1
    composite = slab_image.reshape((4,) + (2,) * bit_levels + (rows_piece, 2 * width_cells))
    my_rank = lax.dynamic_index_in_dim(slab_rank, my_index, 0, keepdims=False)
    for level in range(bit_levels):
        position = bit_levels - level
        my_bit = my_index // 2**level % 2
        kept_half = lax.dynamic_index_in_dim(composite, my_bit, position, keepdims=False)
        outgoing = lax.dynamic_index_in_dim(composite, 1 - my_bit, position, keepdims=False)
        incoming = partner_2(outgoing, "bz", level)
        partner = my_index + (1 - 2 * my_bit) * 2**level
        partner_rank = lax.dynamic_index_in_dim(slab_rank, partner, 0, keepdims=False)
        mine_first = my_rank < partner_rank
        composite = blend_over(
            jnp.where(mine_first, kept_half, incoming), jnp.where(mine_first, incoming, kept_half)
        )
    return composite


LANES = 128
LEVELS = 65535.0
VMEM = pl.BlockSpec(memory_space=pltpu.VMEM)


def pack_words(density, bins):
    level = (density * LEVELS + 0.5).astype(jnp.int32)
    return lax.shift_left(level, 16) | bins


def unpack_words(words):
    density = lax.shift_right_logical(words, 16).astype(jnp.float32) * (1.0 / LEVELS)
    return density, words & 0xFFFF


def cell_values(density, bins, tables, depth):
    low_bits = bins & (LANES - 1)
    upper = bins >= LANES

    def pick(channel):
        first, second = tables[channel]
        return jnp.where(
            upper,
            jnp.take_along_axis(second, low_bits, axis=1, mode="promise_in_bounds"),
            jnp.take_along_axis(first, low_bits, axis=1, mode="promise_in_bounds"),
        )

    opacity = (1.0 - jnp.exp(-pick(3) * density / depth)) * (1.0 / 64.0)
    return [pick(0) * opacity, pick(1) * opacity, pick(2) * opacity, opacity]


def read_tables(tables_ref):
    return [[tables_ref[2 * channel + half] for half in range(2)] for channel in range(4)]


def cost(microseconds):
    return pl.CostEstimate(
        flops=int(1e9 * microseconds), bytes_accessed=int(3.6e6 * microseconds), transcendentals=0
    )


def stage_kernel(
    density_ref, bins_ref, colour_ref, extinction_ref,
    first_ref, second_ref, columns_ref, dense_ref, index_ref, tables_ref,
):
    layers, rows, cols = density_ref.shape
    front = lax.axis_index("bz") == 0
    row_at = lax.broadcasted_iota(jnp.int32, (rows, LANES), 0)
    lane_at = lax.broadcasted_iota(jnp.int32, (rows, LANES), 1)
    for z in range(layers):
        first = pack_words(density_ref[z, :, 0:1], bins_ref[z, :, 0:1])
        last = pack_words(density_ref[z, :, cols - 1 : cols], bins_ref[z, :, cols - 1 : cols])
        line = jnp.where(lane_at == row_at, first, 0) + jnp.where(lane_at == row_at + rows, last, 0)
        columns_ref[z : z + 1, :] = jnp.sum(line, axis=0, keepdims=True)
        top, bottom = [
            pack_words(density_ref[z, r : r + 1, :], bins_ref[z, r : r + 1, :]) for r in (0, rows - 1)
        ]
        first_ref[z : z + 1, :] = jnp.where(front, bottom, top)
        second_ref[z : z + 1, :] = jnp.where(front, top, bottom)
        for tile in range(cols // LANES):
            lanes = slice(tile * LANES, (tile + 1) * LANES)
            dense_ref[z, tile, 0:rows] = density_ref[z, :, lanes]
            index_ref[z, tile, 0:rows] = bins_ref[z, :, lanes]
    colour = colour_ref[...].astype(jnp.float32)
    extinction = extinction_ref[...].astype(jnp.float32).reshape(1, 2 * LANES)
    for channel in range(4):
        line = extinction if channel == 3 else colour[channel : channel + 1]
        for half in range(2):
            tables_ref[2 * channel + half] = jnp.broadcast_to(
                line[:, half * LANES : (half + 1) * LANES], (8, LANES)
            )


def pack_kernel(dense_ref, index_ref, columns_ref, bulk_ref, inside_ref):
    layers, tiles, rows = dense_ref.shape[0], dense_ref.shape[1], dense_ref.shape[2] - 8
    half = rows // 2
    front = lax.axis_index("bz") == 0
    start = jnp.where(front, half, 0)
    for tile in range(tiles):
        lanes = slice(tile * LANES, (tile + 1) * LANES)
        bulk_ref[2 * layers + 1, :, lanes] = columns_ref[...]
        for z in range(layers):
            for part in range(2):
                at = pl.ds(start + part, half // 2, stride=2)
                bulk_ref[2 * z + part, :, lanes] = pack_words(
                    dense_ref[z, tile, at, :], index_ref[z, tile, at, :]
                )
            line = [
                pack_words(dense_ref[z, tile, r : r + 1, :], index_ref[z, tile, r : r + 1, :])
                for r in (half - 1, half)
            ]
            bulk_ref[2 * layers, z : z + 1, lanes] = jnp.where(front, line[0], line[1])
            inside_ref[z : z + 1, lanes] = jnp.where(front, line[1], line[0])


def near_words(slab, first_ref, second_ref):
    me = lax.axis_index("bz")
    words = jnp.where(me == slab, first_ref[...], second_ref[...])
    return jnp.where(has_near(me == 0), words, 0)


def side_kernel(columns_ref, bulk_ref, first_ref, second_ref, along_ref, ends_ref):
    layers = columns_ref.shape[0]
    front = lax.axis_index("bz") == 0
    lane_at = lax.broadcasted_iota(jnp.int32, (layers, LANES), 1)
    for slab in range(2):
        mine = front if slab == 0 else jnp.logical_not(front)
        columns = jnp.where(mine, columns_ref[...], bulk_ref[2 * layers + 1, :, 0:LANES])
        near = near_words(slab, first_ref, second_ref)
        cols = near.shape[1]
        columns = jnp.where(lane_at == 64, near[:, 0:1], columns)
        ends_ref[slab] = jnp.where(lane_at == 65, near[:, cols - 1 : cols], columns)


def has_near(front):
    me_y = lax.axis_index("by")
    return jnp.where(front, me_y > 0, me_y + 1 < lax.axis_size("by"))


def fill_weights(weights_ref, rows):
    cols = weights_ref.shape[0] - LANES
    row = lax.broadcasted_iota(jnp.int32, (cols, 2 * cols), 0)
    at = lax.broadcasted_iota(jnp.int32, (cols, 2 * cols), 1)
    centre = lax.shift_right_logical(at, 1)
    beside = centre - 1 + 2 * (at & 1)
    weights_ref[0:cols, :] = jnp.where(
        row == centre, 3.0, jnp.where(row == beside, 1.0, 0.0)
    ).astype(jnp.bfloat16)
    row = lax.broadcasted_iota(jnp.int32, (LANES, 2 * LANES), 0)
    at = lax.broadcasted_iota(jnp.int32, (LANES, 2 * LANES), 1)
    right = ((row < rows) | (row == 64)) & (at == 2 * LANES - 1)
    left = (((row >= rows) & (row < 2 * rows)) | (row == 65)) & (at == 0)
    weights_ref[cols : cols + LANES, 0 : 2 * LANES] = jnp.where(right | left, 1.0, 0.0).astype(
        jnp.bfloat16
    )


def lane_maps(rows):
    lane_at = lax.broadcasted_iota(jnp.int32, (8, LANES), 1)
    sub_at = lax.broadcasted_iota(jnp.int32, (8, LANES), 0)
    return lane_at & (rows - 1), lane_at < 2 * rows, sub_at


def classify_rows(read_cells, tables, cells_ref, layers, tiles):
    total = float(2 * layers)
    for z in range(layers):
        for tile in range(tiles):
            even = cell_values(*read_cells(z, 0, tile), tables, total)
            odd = cell_values(*read_cells(z, 1, tile), tables, total)
            for channel in range(4):
                base = (z * 4 + channel) * 16
                block = jnp.concatenate([even[channel], odd[channel]], axis=0)
                cells_ref[base : base + 16, tile * LANES : (tile + 1) * LANES] = block.astype(jnp.bfloat16)


def rounded(value):
    return value.astype(jnp.bfloat16).astype(jnp.float32)


def cells_kernel(dense_ref, index_ref, tables_ref, cells_ref, weights_ref):
    layers, tiles, rows = dense_ref.shape[0], dense_ref.shape[1], dense_ref.shape[2] - 8
    half = rows // 2
    start = lax.axis_index("bz") * half
    fill_weights(weights_ref, rows)

    def read_cells(z, part, tile):
        at = pl.ds(start + part, half // 2, stride=2)
        return dense_ref[z, tile, at, :], index_ref[z, tile, at, :]

    classify_rows(read_cells, read_tables(tables_ref), cells_ref, layers, tiles)


def along_columns(cells, weights_ref, store):
    cols = cells.shape[1]
    tiles = 2 * cols // LANES
    result = jnp.dot(cells, weights_ref[0:cols, :], preferred_element_type=jnp.float32)
    for tile in range(tiles):
        block = result[:, tile * LANES : (tile + 1) * LANES]
        store(tile, block if tile in (0, tiles - 1) else rounded(block))


def own_kernel(cells_ref, weights_ref, along_ref):
    size = cells_ref.shape[0]
    pad = along_ref.shape[1] // 2 - size
    mine = pl.multiple_of(pad + lax.axis_index("bz") * size, pad)

    def store(tile, block):
        along_ref[tile, 0:pad, :] = jnp.zeros((pad, LANES), jnp.float32)
        along_ref[tile, pad + 2 * size :, :] = jnp.zeros((pad, LANES), jnp.float32)
        along_ref[tile, pl.ds(mine, size), :] = block

    along_columns(cells_ref[...], weights_ref, store)


def other_kernel(bulk_ref, tables_ref, weights_ref, ends_ref, own_ref, along_ref, cells_ref):
    layers = (bulk_ref.shape[0] - 2) // 2
    cols = bulk_ref.shape[2]
    size = cells_ref.shape[0]
    pad = along_ref.shape[1] // 2 - size
    theirs = pl.multiple_of(pad + (1 - lax.axis_index("bz")) * size, pad)

    def read_cells(z, part, tile):
        return unpack_words(bulk_ref[2 * z + part, :, tile * LANES : (tile + 1) * LANES])

    def store(tile, block):
        along_ref[tile, pl.ds(theirs, size), :] = block

    classify_rows(read_cells, read_tables(tables_ref), cells_ref, layers, cols // LANES)
    along_columns(cells_ref[...], weights_ref, store)


def edge_lines(now, lines_ref, depth):
    triple = 3.0 * now
    empty = jnp.zeros((8, LANES), jnp.float32)
    for layer in range(depth):
        here = triple[layer * 8 : layer * 8 + 8]
        before = now[layer * 8 - 8 : layer * 8] if layer > 0 else empty
        after = now[layer * 8 + 8 : layer * 8 + 16] if layer + 1 < depth else empty
        lines_ref[layer * 16 : layer * 16 + 8, :] = rounded(before + here)
        lines_ref[layer * 16 + 8 : layer * 16 + 16, :] = rounded(after + here)


def rounded_parts(value):
    scaled = value * 65537.0
    return scaled + (value - scaled)


def render_tile(along_ref, lines_ref, flip, layers):
    sub_at = lax.broadcasted_iota(jnp.int32, (8, LANES), 0)
    top = sub_at == 0
    bottom = sub_at == 7

    def one_slab(position, image):
        slab = position ^ flip
        view = along_ref.at[pl.ds(pl.multiple_of(slab * (layers * 64), 64), (layers + 2) * 64), :]
        lines = lines_ref.at[pl.ds(pl.multiple_of(slab * (layers * 16), 16), layers * 16 + 8), :]

        def layer_rows(layer, channel):
            base = (layer * 4 + channel) * 16
            return [view[base + part * 8 : base + part * 8 + 8, :] for part in range(2)]

        for z in range(layers):
            triple = [[3.0 * value for value in layer_rows(z + 1, channel)] for channel in range(4)]
            for parity in range(2):
                clear = [1.0 - value for value in image[3]]
                updated = []
                for channel in range(4):
                    beside = layer_rows(z + 2 * parity, channel)
                    even, odd = [rounded_parts(beside[part] + triple[channel][part]) for part in range(2)]
                    line = (z * 2 + parity) * 8 + channel
                    above = lines[pl.ds(line, 8, stride=0), :]
                    below = lines[pl.ds(line + 4, 8, stride=0), :]
                    before_even = jnp.where(top, above, pltpu.roll(odd, 1, 0))
                    after_odd = jnp.where(bottom, below, pltpu.roll(even, 7, 0))
                    even_centre = 3.0 * even
                    odd_centre = 3.0 * odd
                    samples = [
                        before_even + even_centre,
                        even_centre + odd,
                        even + odd_centre,
                        odd_centre + after_odd,
                    ]
                    updated.append([image[channel][i] + clear[i] * samples[i] for i in range(4)])
                image = updated
        return image

    zero = jnp.zeros((8, LANES), jnp.float32)
    return lax.fori_loop(0, 2, one_slab, [[zero] * 4 for _ in range(4)])


def store_tile(image, mixed_ref, out_ref, lanes):
    for channel in range(4):
        for i in range(4):
            mixed_ref[channel, pl.ds(i, 8, stride=4), :] = image[channel][i]
        out_ref[channel, :, lanes] = mixed_ref[channel, 0:32]


def inner_kernel(
    rank_ref, tables_ref, weights_ref, bulk_ref, inside_ref, first_ref, second_ref, along_ref,
    image_ref, edge_ref, cells_ref, lines_ref, mixed_ref,
):
    layers, cols = inside_ref.shape
    depth = 2 * layers
    tiles = 2 * cols // LANES
    me = lax.axis_index("bz")
    front = me == 0
    tables = read_tables(tables_ref)
    for slab in range(2):
        inside = jnp.where(me == slab, inside_ref[...], bulk_ref[2 * layers])
        near = near_words(slab, first_ref, second_ref)
        for side in range(2):
            use_near = front if side == 0 else jnp.logical_not(front)
            words = jnp.where(use_near, near, inside)
            for t in range(cols // LANES):
                values = cell_values(
                    *unpack_words(words[:, t * LANES : (t + 1) * LANES]), tables, float(depth)
                )
                for channel in range(4):
                    at = pl.ds(slab * layers * 8 + side * 4 + channel, layers, stride=8)
                    cells_ref[t, at, :] = values[channel]
    edge = sum(
        jnp.dot(
            cells_ref[t, 0 : 8 * depth].astype(jnp.bfloat16),
            weights_ref[t * LANES : (t + 1) * LANES, :],
            preferred_element_type=jnp.float32,
        )
        for t in range(cols // LANES)
    )
    for tile in range(tiles):
        now = edge[:, tile * LANES : (tile + 1) * LANES]
        if tile in (0, tiles - 1):
            edge_ref[0 if tile == 0 else 1] = now
        else:
            edge_lines(rounded(now), lines_ref.at[tile - 1], depth)

    def one_tile(index, carry):
        image = render_tile(along_ref.at[index + 1], lines_ref.at[index], rank_ref[0], layers)
        store_tile(image, mixed_ref, image_ref, pl.ds(pl.multiple_of(index * LANES, LANES), LANES))
        return carry

    lax.fori_loop(0, tiles - 2, one_tile, 0)


def outer_kernel(
    rank_ref, tables_ref, weights_ref, beside_ref, across_ref, along_ref, edge_ref, image_ref,
    out_ref, ends_ref, values_ref, keep_ref, fixed_ref, lines_ref, mixed_ref,
):
    rows = out_ref.shape[1]
    cols = out_ref.shape[2] // 2
    layers = beside_ref.shape[1]
    depth = 2 * layers
    tiles = 2 * cols // LANES
    pad = 64
    size = layers * pad
    front = lax.axis_index("bz") == 0
    start = lax.axis_index("bz") * (rows // 2)
    me_x = lax.axis_index("bx")
    even_x = lax.rem(me_x, 2) == 0
    tables = read_tables(tables_ref)
    side_lane, has_side, sub_at = lane_maps(rows)
    masks = [has_side & (side_lane == start + 2 * sub_at + part) for part in range(2)]
    lane_at = lax.broadcasted_iota(jnp.int32, (layers, LANES), 1)
    is_right = (lane_at < rows) | (lane_at == 64)
    for slab in range(2):
        right = jnp.where(even_x, beside_ref[slab], across_ref[slab])
        left = jnp.where(even_x, across_ref[slab], beside_ref[slab])
        right = jnp.where(me_x + 1 < lax.axis_size("bx"), right, 0)
        left = jnp.where(me_x > 0, left, 0)
        words = jnp.where(is_right, right, left)
        values = cell_values(*unpack_words(words), tables, float(depth))
        for channel in range(4):
            values_ref[slab * 4 + channel, 0:layers] = values[channel]
        for z in range(layers):
            for channel in range(4):
                line = values_ref[slab * 4 + channel, pl.ds(z, 8, stride=0), :]
                block = jnp.concatenate([jnp.where(mask, line, 0.0) for mask in masks], axis=0)
                at = slab * size + (z * 4 + channel) * 16
                ends_ref[at : at + 16, :] = block.astype(jnp.bfloat16)
        for side in range(2):
            row = jnp.where(front, 64, rows // 2 - 1) if side == 0 else jnp.where(front, rows // 2, 64)
            twin = jnp.where(row == 64, 65, row + rows)
            keep = (lane_at == row) | (lane_at == twin)
            for channel in range(4):
                at = pl.ds(slab * layers * 8 + side * 4 + channel, layers, stride=8)
                keep_ref[at, :] = jnp.where(keep, values[channel], 0.0)
    ends_ref[2 * size :, :] = keep_ref[0 : 8 * depth].astype(jnp.bfloat16)
    added = jnp.dot(
        ends_ref[...], weights_ref[cols : cols + LANES, 0 : 2 * LANES], preferred_element_type=jnp.float32
    )
    for index, tile in enumerate((0, tiles - 1)):
        block = added[:, index * LANES : (index + 1) * LANES]
        fixed_ref[index, 0:pad, :] = jnp.zeros((pad, LANES), jnp.float32)
        fixed_ref[index, pad + 2 * size :, :] = jnp.zeros((pad, LANES), jnp.float32)
        fixed_ref[index, pad : pad + 2 * size, :] = rounded(
            along_ref[tile, pad : pad + 2 * size, :] + block[0 : 2 * size]
        )
        edge_lines(rounded(edge_ref[index] + block[2 * size :]), lines_ref.at[index], depth)
    out_ref[:, :, LANES : 2 * cols - LANES] = image_ref[...]

    def one_tile(index, carry):
        image = render_tile(fixed_ref.at[index], lines_ref.at[index], rank_ref[0], layers)
        lanes = pl.ds(pl.multiple_of(index * (2 * cols - LANES), LANES), LANES)
        store_tile(image, mixed_ref, out_ref, lanes)
        return carry

    lax.fori_loop(0, 2, one_tile, 0)


def two_slab_device(density, bin_index, tf_colour, tf_extinction, slab_rank):
    layers, rows, cols = density.shape
    half = rows // 2
    tiles = 2 * cols // LANES
    size = layers * 4 * half
    count_y, count_x = lax.axis_size("by"), lax.axis_size("bx")
    f32, bf16, i32 = jnp.float32, jnp.bfloat16, jnp.int32

    def call(kernel, name, out_shape, time, scratch_shapes=(), in_specs=None, aliases={}):
        def run(*operands):
            return pl.pallas_call(
                kernel,
                out_shape=out_shape,
                in_specs=in_specs or [VMEM] * len(operands),
                out_specs=(VMEM,) * len(out_shape) if isinstance(out_shape, tuple) else VMEM,
                scratch_shapes=scratch_shapes,
                input_output_aliases=aliases,
                compiler_params=pltpu.CompilerParams(vmem_limit_bytes=16 * 1024 * 1024),
                cost_estimate=cost(time),
                name=name,
            )(*operands)

        return run

    def both(route):
        return route + [(target, source) for source, target in route]

    blocks = (layers, cols // LANES, rows + 8, LANES)
    row = pltpu.VMEM((layers, cols), i32)
    first, second, columns, dense, index, tables = call(
        stage_kernel,
        "stage_block",
        (
            row,
            row,
            pltpu.VMEM((layers, LANES), i32),
            pltpu.VMEM(blocks, f32),
            pltpu.VMEM(blocks, i32),
            pltpu.VMEM((8, 8, LANES), f32),
        ),
        1.2,
    )(*[pltpu.with_memory_space_constraint(x, pltpu.HBM) for x in (density, bin_index, tf_colour, tf_extinction)])
    bulk, inside = call(
        pack_kernel, "pack_block", (pltpu.VMEM((2 * layers + 2, 8, cols), i32), row), 0.1
    )(dense, index, columns)

    def place(z, y, x):
        return (z * count_y + y) * count_x + x

    steps = range(count_y - 1)
    ring = [(place(0, y, 0), place(0, y + 1, 0)) for y in steps]
    ring += [(place(1, y + 1, 0), place(1, y, 0)) for y in steps]
    ring += [(place(0, count_y - 1, 0), place(1, count_y - 1, 0)), (place(1, 0, 0), place(0, 0, 0))]
    ring = [(source + x, target + x) for source, target in ring for x in range(count_x)]
    diagonal = [(place(1, y, x), place(0, y + 1, x)) for y in steps for x in range(count_x)]
    for z, y in ((0, 0), (1, count_y - 1)):
        diagonal += [(place(z, y, x), place(z, y, x + 1)) for x in range(0, count_x, 2)]
    axes = ("bz", "by", "bx")
    bulk = lax.ppermute(bulk, "bz", [(0, 1), (1, 0)])
    first = lax.ppermute(first, axes, ring)
    second = lax.ppermute(second, axes, both(diagonal))

    cells, weights = call(
        cells_kernel,
        "own_cells",
        (pltpu.VMEM((size, cols), bf16), pltpu.VMEM((cols + LANES, 2 * cols), bf16)),
        0.5,
    )(dense, index, tables)
    whole = pltpu.VMEM((tiles, 2 * size + 2 * 4 * half, LANES), f32)
    along = call(own_kernel, "own_slab", whole, 2.0)(cells, weights)
    ends = call(side_kernel, "side_columns", pltpu.VMEM((2, layers, LANES), i32), 0.1)(
        columns, bulk, first, second, along
    )
    pairs = [(x, x + 1) for x in range(0, count_x, 2)]
    cross = [(x, (x + 1) % count_x) for x in range(1, count_x, 2)]
    beside = lax.ppermute(ends, "bx", both(pairs))
    across = lax.ppermute(ends, "bx", both(cross))
    along = call(other_kernel, "other_slab", whole, 0.8, [pltpu.VMEM((size, cols), bf16)], aliases={4: 0})(
        bulk, tables, weights, ends, along
    )
    smem = pl.BlockSpec(memory_space=pltpu.SMEM)
    lines = pltpu.VMEM((2, 32 * layers + 8, LANES), f32)
    image, edge = call(
        inner_kernel,
        "inner_tiles",
        (pltpu.VMEM((4, rows, (tiles - 2) * LANES), f32), pltpu.VMEM((2, 16 * layers, LANES), f32)),
        2.0,
        [pltpu.VMEM((cols // LANES, 16 * layers + 8, LANES), f32), lines, pltpu.VMEM((4, rows + 8, LANES), f32)],
        [smem] + [VMEM] * 7,
    )(slab_rank, tables, weights, bulk, inside, first, second, along)
    return call(
        outer_kernel,
        "outer_tiles",
        jax.ShapeDtypeStruct((4, rows, 2 * cols), f32),
        2.0,
        [
            pltpu.VMEM((2 * size + 16 * layers, LANES), bf16),
            pltpu.VMEM((8, 2 * layers, LANES), f32),
            pltpu.VMEM((16 * layers + 8, LANES), f32),
            pltpu.VMEM((2, 2 * size + 2 * 4 * half, LANES), f32),
            lines,
            pltpu.VMEM((4, rows + 8, LANES), f32),
        ],
        [smem] + [VMEM] * 7,
    )(slab_rank, tables, weights, beside, across, along, edge, image)


def on_device(density, bin_index, tf_colour, tf_extinction, slab_rank):
    if lax.axis_size("bz") == 2:
        return two_slab_device(density, bin_index, tf_colour, tf_extinction, slab_rank)
    return general_device(density, bin_index, tf_colour, tf_extinction, slab_rank)


def solution(mesh):
    return jax.shard_map(
        on_device,
        mesh=mesh,
        in_specs=(P("bz", "by", "bx"), P("bz", "by", "bx"), P(), P(), P()),
        out_specs=P(None, ("by", "bz"), "bx"),
        check_vma=False,
    )
```

```python
import functools

import jax
import jax.numpy as jnp
from jax import lax
from jax.experimental import pallas as pl
from jax.experimental.pallas import tpu as pltpu
from jax.sharding import PartitionSpec as P


def with_halo(block, sides, width):
    for axis, dim in sides:
        count = lax.axis_size(axis)
        forward = [(i, i + 1) for i in range(count - 1)]
        backward = [(target, source) for source, target in forward]
        low = lax.ppermute(
            lax.slice_in_dim(block, block.shape[dim] - width, None, axis=dim), axis, forward
        )
        high = lax.ppermute(lax.slice_in_dim(block, 0, width, axis=dim), axis, backward)
        block = jnp.concatenate([low, block, high], axis=dim)
    return block


def partner_2(block, axis, stride):
    count = lax.axis_size(axis)
    route = []
    for low in range(count):
        high = low | 1 << stride
        if high != low and high < count:
            route += [(low, high), (high, low)]
    return lax.ppermute(block, axis, route)


def resample_table(length):
    row_index = lax.broadcasted_iota(jnp.int32, (2 * length, length + 2), 0)
    col_index = lax.broadcasted_iota(jnp.int32, (2 * length, length + 2), 1)
    centre = row_index // 2
    parity = row_index % 2
    weights_table = jnp.where(col_index == centre + 1, 0.75, 0.0)
    weights_table = weights_table + jnp.where((col_index == centre) & (parity == 0), 0.25, 0.0)
    weights_table = weights_table + jnp.where((col_index == centre + 2) & (parity == 1), 0.25, 0.0)
    return weights_table.astype(jnp.bfloat16)


def blend_over(in_front, behind):
    return in_front + (1.0 - in_front[3])[None] * behind


def classify(density, bin_index, tf_colour, tf_extinction, total_depth):
    depth_cells, height_cells, width_cells = density.shape
    lookup = jnp.concatenate([tf_colour, tf_extinction[None, :]], axis=0)
    table_size = lookup.shape[1]
    bin_rows = lax.broadcasted_iota(jnp.int32, (table_size, 1), 0)
    flat_bins = bin_index.reshape(depth_cells, height_cells * width_cells)
    flat_density = density.reshape(depth_cells, height_cells * width_cells)

    def one_layer(layer, result):
        layer_bins = lax.dynamic_index_in_dim(flat_bins, layer, 0, keepdims=True)
        layer_density = lax.dynamic_index_in_dim(flat_density, layer, 0, keepdims=False)
        one_hot = (layer_bins == bin_rows).astype(jnp.bfloat16)
        values = jnp.dot(lookup, one_hot, preferred_element_type=jnp.float32)
        opacity = 1.0 - jnp.exp(-values[3] * layer_density / total_depth)
        cells = jnp.concatenate([values[:3] * opacity[None], opacity[None]], axis=0).astype(
            jnp.bfloat16
        )
        return lax.dynamic_update_slice_in_dim(result, cells[:, None], layer, 1)

    start_cells = jnp.zeros((4, depth_cells, height_cells * width_cells), jnp.bfloat16)
    classified = lax.fori_loop(0, depth_cells, one_layer, start_cells)
    return classified.reshape(4, depth_cells, height_cells, width_cells)


def general_device(density, bin_index, tf_colour, tf_extinction, slab_rank):
    slab_count = lax.axis_size("bz")
    depth_cells, height_cells, width_cells = density.shape
    total_depth = float(depth_cells * slab_count)
    colour_cells = classify(density, bin_index, tf_colour, tf_extinction, total_depth)
    padded = with_halo(colour_cells, (("bz", 1), ("by", 2), ("bx", 3)), 1)
    along_x = jnp.einsum(
        "czyq,pq->czyp", padded, resample_table(width_cells), preferred_element_type=jnp.float32
    ).astype(jnp.bfloat16)
    y_table = resample_table(height_cells)

    def add_sample(sample_index, image_now):
        centre = sample_index // 2
        parity = sample_index % 2
        layers = lax.dynamic_slice_in_dim(along_x, centre, 3, 1).astype(jnp.float32)
        lower_weight = jnp.where(parity == 0, 0.25, 0.0)
        upper_weight = jnp.where(parity == 1, 0.25, 0.0)
        mixed_layer = (
            lower_weight * layers[:, 0] + 0.75 * layers[:, 1] + upper_weight * layers[:, 2]
        ).astype(jnp.bfloat16)
        sample = jnp.einsum("qy,cyp->cqp", y_table, mixed_layer, preferred_element_type=jnp.float32)
        return blend_over(image_now, sample)

    start_image = jnp.zeros((4, 2 * height_cells, 2 * width_cells), jnp.float32)
    slab_image = lax.fori_loop(0, 2 * depth_cells, add_sample, start_image)
    rows_piece = 2 * height_cells // slab_count
    my_index = lax.axis_index("bz")
    bit_levels = slab_count.bit_length() - 1
    composite = slab_image.reshape((4,) + (2,) * bit_levels + (rows_piece, 2 * width_cells))
    my_rank = lax.dynamic_index_in_dim(slab_rank, my_index, 0, keepdims=False)
    for level in range(bit_levels):
        position = bit_levels - level
        my_bit = my_index // 2**level % 2
        kept_half = lax.dynamic_index_in_dim(composite, my_bit, position, keepdims=False)
        outgoing = lax.dynamic_index_in_dim(composite, 1 - my_bit, position, keepdims=False)
        incoming = partner_2(outgoing, "bz", level)
        partner = my_index + (1 - 2 * my_bit) * 2**level
        partner_rank = lax.dynamic_index_in_dim(slab_rank, partner, 0, keepdims=False)
        mine_first = my_rank < partner_rank
        composite = blend_over(
            jnp.where(mine_first, kept_half, incoming), jnp.where(mine_first, incoming, kept_half)
        )
    return composite


LANES = 128
LEVELS = 65535.0
VMEM = pl.BlockSpec(memory_space=pltpu.VMEM)


def pack_words(density, bins):
    level = (density * LEVELS + 0.5).astype(jnp.int32)
    return lax.shift_left(level, 16) | bins


def unpack_words(words):
    density = lax.shift_right_logical(words, 16).astype(jnp.float32) * (1.0 / LEVELS)
    return density, words & 0xFFFF


def cell_values(density, bins, tables, depth):
    low_bits = bins & (LANES - 1)
    upper = bins >= LANES

    def pick(channel):
        first, second = tables[channel]
        return jnp.where(
            upper,
            jnp.take_along_axis(second, low_bits, axis=1, mode="promise_in_bounds"),
            jnp.take_along_axis(first, low_bits, axis=1, mode="promise_in_bounds"),
        )

    opacity = (1.0 - jnp.exp(-pick(3) * density / depth)) * (1.0 / 64.0)
    return [pick(0) * opacity, pick(1) * opacity, pick(2) * opacity, opacity]


def read_tables(tables_ref):
    return [[tables_ref[2 * channel + half] for half in range(2)] for channel in range(4)]


def cost(microseconds):
    return pl.CostEstimate(
        flops=int(1e9 * microseconds), bytes_accessed=int(3.6e6 * microseconds), transcendentals=0
    )


def stage_kernel(
    density_ref, bins_ref, colour_ref, extinction_ref,
    first_ref, second_ref, columns_ref, dense_ref, index_ref, tables_ref,
):
    layers, rows, cols = density_ref.shape
    front = lax.axis_index("bz") == 0
    row_at = lax.broadcasted_iota(jnp.int32, (rows, LANES), 0)
    lane_at = lax.broadcasted_iota(jnp.int32, (rows, LANES), 1)
    for z in range(layers):
        first = pack_words(density_ref[z, :, 0:1], bins_ref[z, :, 0:1])
        last = pack_words(density_ref[z, :, cols - 1 : cols], bins_ref[z, :, cols - 1 : cols])
        line = jnp.where(lane_at == row_at, first, 0) + jnp.where(lane_at == row_at + LANES // 2, last, 0)
        columns_ref[z : z + 1, :] = jnp.sum(line, axis=0, keepdims=True)
        top, bottom = [
            pack_words(density_ref[z, r : r + 1, :], bins_ref[z, r : r + 1, :]) for r in (0, rows - 1)
        ]
        first_ref[z : z + 1, :] = jnp.where(front, bottom, top)
        second_ref[z : z + 1, :] = jnp.where(front, top, bottom)
        for tile in range(cols // LANES):
            lanes = slice(tile * LANES, (tile + 1) * LANES)
            dense_ref[z, tile, 0:rows] = density_ref[z, :, lanes]
            index_ref[z, tile, 0:rows] = bins_ref[z, :, lanes]
    colour = colour_ref[...].astype(jnp.float32)
    extinction = extinction_ref[...].astype(jnp.float32).reshape(1, 2 * LANES)
    for channel in range(4):
        line = extinction if channel == 3 else colour[channel : channel + 1]
        for half in range(2):
            tables_ref[2 * channel + half] = jnp.broadcast_to(
                line[:, half * LANES : (half + 1) * LANES], (8, LANES)
            )


def pack_kernel(dense_ref, index_ref, columns_ref, bulk_ref, inside_ref):
    layers, tiles, rows = dense_ref.shape[0], dense_ref.shape[1], dense_ref.shape[2] - 8
    half = rows // 2
    front = lax.axis_index("bz") == 0
    start = jnp.where(front, half, 0)
    for tile in range(tiles):
        lanes = slice(tile * LANES, (tile + 1) * LANES)
        bulk_ref[2 * layers + 1, :, lanes] = columns_ref[...]
        for z in range(layers):
            for part in range(2):
                at = pl.ds(start + part, half // 2, stride=2)
                bulk_ref[2 * z + part, :, lanes] = pack_words(
                    dense_ref[z, tile, at, :], index_ref[z, tile, at, :]
                )
            line = [
                pack_words(dense_ref[z, tile, r : r + 1, :], index_ref[z, tile, r : r + 1, :])
                for r in (half - 1, half)
            ]
            bulk_ref[2 * layers, z : z + 1, lanes] = jnp.where(front, line[0], line[1])
            inside_ref[z : z + 1, lanes] = jnp.where(front, line[1], line[0])


def near_words(slab, first_ref, second_ref):
    me = lax.axis_index("bz")
    words = jnp.where(me == slab, first_ref[...], second_ref[...])
    return jnp.where(has_near(me == 0), words, 0)


def side_kernel(rows, columns_ref, bulk_ref, first_ref, second_ref, along_ref, ends_ref):
    layers = columns_ref.shape[0]
    front = lax.axis_index("bz") == 0
    lane_at = lax.broadcasted_iota(jnp.int32, (layers, LANES), 1)
    for slab in range(2):
        mine = front if slab == 0 else jnp.logical_not(front)
        columns = jnp.where(mine, columns_ref[...], bulk_ref[2 * layers + 1, :, 0:LANES])
        near = near_words(slab, first_ref, second_ref)
        cols = near.shape[1]
        columns = jnp.where(lane_at == rows, near[:, 0:1], columns)
        ends_ref[slab] = jnp.where(
            lane_at == LANES // 2 + rows, near[:, cols - 1 : cols], columns
        )


def has_near(front):
    me_y = lax.axis_index("by")
    return jnp.where(front, me_y > 0, me_y + 1 < lax.axis_size("by"))


def fill_weights(weights_ref):
    cols = weights_ref.shape[0]
    row = lax.broadcasted_iota(jnp.int32, (cols, 2 * cols), 0)
    at = lax.broadcasted_iota(jnp.int32, (cols, 2 * cols), 1)
    centre = lax.shift_right_logical(at, 1)
    beside = centre - 1 + 2 * (at & 1)
    weights_ref[...] = jnp.where(row == centre, 3.0, jnp.where(row == beside, 1.0, 0.0)).astype(
        jnp.bfloat16
    )


def classify_rows(read_cells, tables, cells_ref, layers, tiles):
    total = float(2 * layers)
    for z in range(layers):
        for tile in range(tiles):
            even = cell_values(*read_cells(z, 0, tile), tables, total)
            odd = cell_values(*read_cells(z, 1, tile), tables, total)
            for channel in range(4):
                base = (z * 4 + channel) * 16
                block = jnp.concatenate([even[channel], odd[channel]], axis=0)
                cells_ref[base : base + 16, tile * LANES : (tile + 1) * LANES] = block.astype(jnp.bfloat16)


def rounded(value):
    return value.astype(jnp.bfloat16).astype(jnp.float32)


def cells_kernel(dense_ref, index_ref, tables_ref, cells_ref, weights_ref):
    layers, tiles, rows = dense_ref.shape[0], dense_ref.shape[1], dense_ref.shape[2] - 8
    half = rows // 2
    start = lax.axis_index("bz") * half
    fill_weights(weights_ref)

    def read_cells(z, part, tile):
        at = pl.ds(start + part, half // 2, stride=2)
        return dense_ref[z, tile, at, :], index_ref[z, tile, at, :]

    classify_rows(read_cells, read_tables(tables_ref), cells_ref, layers, tiles)


def along_columns(cells, weights_ref, store):
    result = rounded(jnp.dot(cells, weights_ref[...], preferred_element_type=jnp.float32))
    for tile in range(result.shape[1] // LANES):
        store(tile, result[:, tile * LANES : (tile + 1) * LANES])


def own_kernel(cells_ref, weights_ref, along_ref):
    size = cells_ref.shape[0]
    pad = along_ref.shape[1] // 2 - size
    mine = pl.multiple_of(pad + lax.axis_index("bz") * size, pad)

    def store(tile, block):
        along_ref[tile, 0:pad, :] = jnp.zeros((pad, LANES), jnp.float32)
        along_ref[tile, pad + 2 * size :, :] = jnp.zeros((pad, LANES), jnp.float32)
        along_ref[tile, pl.ds(mine, size), :] = block

    along_columns(cells_ref[...], weights_ref, store)


def other_kernel(bulk_ref, tables_ref, weights_ref, ends_ref, own_ref, along_ref, cells_ref):
    layers = (bulk_ref.shape[0] - 2) // 2
    cols = bulk_ref.shape[2]
    size = cells_ref.shape[0]
    pad = along_ref.shape[1] // 2 - size
    theirs = pl.multiple_of(pad + (1 - lax.axis_index("bz")) * size, pad)

    def read_cells(z, part, tile):
        return unpack_words(bulk_ref[2 * z + part, :, tile * LANES : (tile + 1) * LANES])

    def store(tile, block):
        along_ref[tile, pl.ds(theirs, size), :] = block

    classify_rows(read_cells, read_tables(tables_ref), cells_ref, layers, cols // LANES)
    along_columns(cells_ref[...], weights_ref, store)


def edge_lines(now, lines_ref, depth):
    triple = 3.0 * now
    empty = jnp.zeros((8, LANES), jnp.float32)
    for layer in range(depth):
        here = triple[layer * 8 : layer * 8 + 8]
        before = now[layer * 8 - 8 : layer * 8] if layer > 0 else empty
        after = now[layer * 8 + 8 : layer * 8 + 16] if layer + 1 < depth else empty
        lines_ref[layer * 16 : layer * 16 + 8, :] = rounded(before + here)
        lines_ref[layer * 16 + 8 : layer * 16 + 16, :] = rounded(after + here)


def render_tile(along_ref, lines_ref, flip, layers):
    sub_at = lax.broadcasted_iota(jnp.int32, (8, LANES), 0)
    top = sub_at == 0
    bottom = sub_at == 7

    def one_slab(position, image):
        slab = position ^ flip
        view = along_ref.at[pl.ds(pl.multiple_of(slab * (layers * 64), 64), (layers + 2) * 64), :]
        lines = lines_ref.at[pl.ds(pl.multiple_of(slab * (layers * 16), 16), layers * 16 + 8), :]

        def layer_rows(layer, channel):
            base = (layer * 4 + channel) * 16
            return [view[base + part * 8 : base + part * 8 + 8, :] for part in range(2)]

        for z in range(layers):
            triple = [[3.0 * value for value in layer_rows(z + 1, channel)] for channel in range(4)]
            for parity in range(2):
                clear = [1.0 - value for value in image[3]]
                updated = []
                for channel in range(4):
                    beside = layer_rows(z + 2 * parity, channel)
                    even, odd = [rounded(beside[part] + triple[channel][part]) for part in range(2)]
                    line = (z * 2 + parity) * 8 + channel
                    above = lines[pl.ds(line, 8, stride=0), :]
                    below = lines[pl.ds(line + 4, 8, stride=0), :]
                    before_even = jnp.where(top, above, pltpu.roll(odd, 1, 0))
                    after_odd = jnp.where(bottom, below, pltpu.roll(even, 7, 0))
                    even_centre = 3.0 * even
                    odd_centre = 3.0 * odd
                    samples = [
                        before_even + even_centre,
                        even_centre + odd,
                        even + odd_centre,
                        odd_centre + after_odd,
                    ]
                    updated.append([image[channel][i] + clear[i] * samples[i] for i in range(4)])
                image = updated
        return image

    zero = jnp.zeros((8, LANES), jnp.float32)
    return lax.fori_loop(0, 2, one_slab, [[zero] * 4 for _ in range(4)])


def store_tile(image, mixed_ref, out_ref, lanes):
    for channel in range(4):
        for i in range(4):
            mixed_ref[channel, pl.ds(i, 8, stride=4), :] = image[channel][i]
        out_ref[channel, :, lanes] = mixed_ref[channel, 0:32]


def inner_kernel(
    rank_ref, tables_ref, weights_ref, bulk_ref, inside_ref, first_ref, second_ref, along_ref,
    image_ref, edge_ref, cells_ref, lines_ref, mixed_ref,
):
    layers, cols = inside_ref.shape
    depth = 2 * layers
    tiles = 2 * cols // LANES
    me = lax.axis_index("bz")
    front = me == 0
    tables = read_tables(tables_ref)
    for slab in range(2):
        inside = jnp.where(me == slab, inside_ref[...], bulk_ref[2 * layers])
        near = near_words(slab, first_ref, second_ref)
        for side in range(2):
            use_near = front if side == 0 else jnp.logical_not(front)
            words = jnp.where(use_near, near, inside)
            for t in range(cols // LANES):
                values = cell_values(
                    *unpack_words(words[:, t * LANES : (t + 1) * LANES]), tables, float(depth)
                )
                for channel in range(4):
                    at = pl.ds(slab * layers * 8 + side * 4 + channel, layers, stride=8)
                    cells_ref[t, at, :] = values[channel]
    edge = sum(
        jnp.dot(
            cells_ref[t, 0 : 8 * depth].astype(jnp.bfloat16),
            weights_ref[t * LANES : (t + 1) * LANES, :],
            preferred_element_type=jnp.float32,
        )
        for t in range(cols // LANES)
    )
    edge = rounded(edge)
    for tile in range(tiles):
        now = edge[:, tile * LANES : (tile + 1) * LANES]
        if tile in (0, tiles - 1):
            edge_ref[0 if tile == 0 else 1] = now
        else:
            edge_lines(now, lines_ref.at[tile - 1], depth)

    def one_tile(index, carry):
        image = render_tile(along_ref.at[index + 1], lines_ref.at[index], rank_ref[0], layers)
        store_tile(image, mixed_ref, image_ref, pl.ds(pl.multiple_of(index * LANES, LANES), LANES))
        return carry

    lax.fori_loop(0, tiles - 2, one_tile, 0)


def outer_kernel(
    rank_ref, tables_ref, ends_ref, beside_ref, across_ref, along_ref, edge_ref, image_ref,
    out_ref, values_ref, turned_ref, keep_ref, fixed_ref, lines_ref, mixed_ref,
):
    rows = out_ref.shape[1]
    cols = out_ref.shape[2] // 2
    half = rows // 2
    layers = beside_ref.shape[1]
    depth = 2 * layers
    tiles = 2 * cols // LANES
    pad = 64
    size = layers * pad
    middle = LANES // 2
    front = lax.axis_index("bz") == 0
    start = lax.axis_index("bz") * half
    me_x = lax.axis_index("bx")
    even_x = lax.rem(me_x, 2) == 0
    tables = read_tables(tables_ref)
    lane_at = lax.broadcasted_iota(jnp.int32, (8, LANES), 1)
    places = [lane_at == 0, lane_at == LANES - 1]
    for slab in range(2):
        right = jnp.where(even_x, beside_ref[slab], across_ref[slab])
        left = jnp.where(even_x, across_ref[slab], beside_ref[slab])
        right = jnp.where(me_x + 1 < lax.axis_size("bx"), right, 0)
        left = jnp.where(me_x > 0, left, 0)
        words = jnp.where(lane_at < middle, right, left)
        mine = cell_values(*unpack_words(ends_ref[slab]), tables, float(depth))
        halo = cell_values(*unpack_words(words), tables, float(depth))
        for channel in range(4):
            value = rounded(
                3.0 * rounded(mine[channel]) + pltpu.roll(rounded(halo[channel]), middle, 1)
            )
            base = (slab * 4 + channel) * layers
            values_ref[base : base + layers, :] = value
            for side, (at_front, at_back) in enumerate(((rows, half - 1), (half, rows))):
                for index in range(2):
                    shift = index * middle
                    column = jnp.where(
                        front,
                        value[:, at_front + shift : at_front + shift + 1],
                        value[:, at_back + shift : at_back + shift + 1],
                    )
                    at = pl.ds(slab * layers * 8 + side * 4 + channel, layers, stride=8)
                    keep_ref[index, at, :] = jnp.broadcast_to(column, (layers, LANES))
    values_ref[8 * layers :, :] = jnp.zeros((LANES - 8 * layers, LANES), jnp.float32)
    turned_ref[0:LANES, :] = values_ref[...].T
    for index, tile in enumerate((0, tiles - 1)):
        place = places[index]
        fixed_ref[index, 0:pad, :] = jnp.zeros((pad, LANES), jnp.float32)
        fixed_ref[index, pad + 2 * size :, :] = jnp.zeros((pad, LANES), jnp.float32)
        for part in range(2):
            turned = turned_ref[pl.ds(index * middle + start + part, 8, stride=2), :]
            for slab in range(2):
                for z in range(layers):
                    for channel in range(4):
                        at = (slab * 4 + channel) * layers + z
                        base = pad + ((slab * layers + z) * 4 + channel) * 16 + part * 8
                        fixed_ref[index, base : base + 8, :] = jnp.where(
                            place, turned[:, at : at + 1], along_ref[tile, base : base + 8, :]
                        )
        wide = lax.broadcasted_iota(jnp.int32, (8 * depth, LANES), 1)
        now = jnp.where(wide == index * (LANES - 1), keep_ref[index, 0 : 8 * depth], edge_ref[index])
        edge_lines(now, lines_ref.at[index], depth)
    out_ref[:, :, LANES : 2 * cols - LANES] = image_ref[...]

    def one_tile(index, carry):
        image = render_tile(fixed_ref.at[index], lines_ref.at[index], rank_ref[0], layers)
        lanes = pl.ds(pl.multiple_of(index * (2 * cols - LANES), LANES), LANES)
        store_tile(image, mixed_ref, out_ref, lanes)
        return carry

    lax.fori_loop(0, 2, one_tile, 0)


def two_slab_device(density, bin_index, tf_colour, tf_extinction, slab_rank):
    layers, rows, cols = density.shape
    half = rows // 2
    tiles = 2 * cols // LANES
    size = layers * 4 * half
    count_y, count_x = lax.axis_size("by"), lax.axis_size("bx")
    f32, bf16, i32 = jnp.float32, jnp.bfloat16, jnp.int32

    def call(kernel, name, out_shape, time, scratch_shapes=(), in_specs=None, aliases={}):
        def run(*operands):
            return pl.pallas_call(
                kernel,
                out_shape=out_shape,
                in_specs=in_specs or [VMEM] * len(operands),
                out_specs=(VMEM,) * len(out_shape) if isinstance(out_shape, tuple) else VMEM,
                scratch_shapes=scratch_shapes,
                input_output_aliases=aliases,
                compiler_params=pltpu.CompilerParams(vmem_limit_bytes=16 * 1024 * 1024),
                cost_estimate=cost(time),
                name=name,
            )(*operands)

        return run

    def both(route):
        return route + [(target, source) for source, target in route]

    blocks = (layers, cols // LANES, rows + 8, LANES)
    row = pltpu.VMEM((layers, cols), i32)
    first, second, columns, dense, index, tables = call(
        stage_kernel,
        "stage_block",
        (
            row,
            row,
            pltpu.VMEM((layers, LANES), i32),
            pltpu.VMEM(blocks, f32),
            pltpu.VMEM(blocks, i32),
            pltpu.VMEM((8, 8, LANES), f32),
        ),
        1.2,
    )(*[pltpu.with_memory_space_constraint(x, pltpu.HBM) for x in (density, bin_index, tf_colour, tf_extinction)])
    bulk, inside = call(
        pack_kernel, "pack_block", (pltpu.VMEM((2 * layers + 2, 8, cols), i32), row), 0.1
    )(dense, index, columns)

    def place(z, y, x):
        return (z * count_y + y) * count_x + x

    steps = range(count_y - 1)
    ring = [(place(0, y, 0), place(0, y + 1, 0)) for y in steps]
    ring += [(place(1, y + 1, 0), place(1, y, 0)) for y in steps]
    ring += [(place(0, count_y - 1, 0), place(1, count_y - 1, 0)), (place(1, 0, 0), place(0, 0, 0))]
    ring = [(source + x, target + x) for source, target in ring for x in range(count_x)]
    diagonal = [(place(1, y, x), place(0, y + 1, x)) for y in steps for x in range(count_x)]
    for z, y in ((0, 0), (1, count_y - 1)):
        diagonal += [(place(z, y, x), place(z, y, x + 1)) for x in range(0, count_x, 2)]
    axes = ("bz", "by", "bx")
    bulk = lax.ppermute(bulk, "bz", [(0, 1), (1, 0)])
    first = lax.ppermute(first, axes, ring)
    second = lax.ppermute(second, axes, both(diagonal))

    cells, weights = call(
        cells_kernel,
        "own_cells",
        (pltpu.VMEM((size, cols), bf16), pltpu.VMEM((cols, 2 * cols), bf16)),
        0.5,
    )(dense, index, tables)
    whole = pltpu.VMEM((tiles, 2 * size + 2 * 4 * half, LANES), f32)
    along = call(own_kernel, "own_slab", whole, 0.4)(cells, weights)
    ends = call(functools.partial(side_kernel, rows), "side_columns", pltpu.VMEM((2, layers, LANES), i32), 0.1)(
        columns, bulk, first, second, along
    )
    pairs = [(x, x + 1) for x in range(0, count_x, 2)]
    cross = [(x, (x + 1) % count_x) for x in range(1, count_x, 2)]
    beside = lax.ppermute(ends, "bx", both(pairs))
    across = lax.ppermute(ends, "bx", both(cross))
    along = call(other_kernel, "other_slab", whole, 0.8, [pltpu.VMEM((size, cols), bf16)], aliases={4: 0})(
        bulk, tables, weights, ends, along
    )
    smem = pl.BlockSpec(memory_space=pltpu.SMEM)
    lines = pltpu.VMEM((2, 32 * layers + 8, LANES), f32)
    image, edge = call(
        inner_kernel,
        "inner_tiles",
        (pltpu.VMEM((4, rows, (tiles - 2) * LANES), f32), pltpu.VMEM((2, 16 * layers, LANES), f32)),
        2.0,
        [pltpu.VMEM((cols // LANES, 16 * layers + 8, LANES), f32), lines, pltpu.VMEM((4, rows + 8, LANES), f32)],
        [smem] + [VMEM] * 7,
    )(slab_rank, tables, weights, bulk, inside, first, second, along)
    return call(
        outer_kernel,
        "outer_tiles",
        jax.ShapeDtypeStruct((4, rows, 2 * cols), f32),
        2.0,
        [
            pltpu.VMEM((LANES, LANES), f32),
            pltpu.VMEM((LANES + 16, LANES), f32),
            pltpu.VMEM((2, 16 * layers + 8, LANES), f32),
            pltpu.VMEM((2, 2 * size + 2 * 4 * half, LANES), f32),
            lines,
            pltpu.VMEM((4, rows + 8, LANES), f32),
        ],
        [smem] + [VMEM] * 7,
    )(slab_rank, tables, ends, beside, across, along, edge, image)


def on_device(density, bin_index, tf_colour, tf_extinction, slab_rank):
    if lax.axis_size("bz") == 2:
        return two_slab_device(density, bin_index, tf_colour, tf_extinction, slab_rank)
    return general_device(density, bin_index, tf_colour, tf_extinction, slab_rank)


def solution(mesh):
    return jax.shard_map(
        on_device,
        mesh=mesh,
        in_specs=(P("bz", "by", "bx"), P("bz", "by", "bx"), P(), P(), P()),
        out_specs=P(None, ("by", "bz"), "bx"),
        check_vma=False,
    )
```

```python
import jax
import jax.numpy as jnp
from jax import lax
from jax.experimental import pallas as pl
from jax.experimental.pallas import tpu as pltpu
from jax.sharding import PartitionSpec as P


def with_halo(block, sides, width):
    for axis, dim in sides:
        count = lax.axis_size(axis)
        forward = [(i, i + 1) for i in range(count - 1)]
        backward = [(target, source) for source, target in forward]
        low = lax.ppermute(
            lax.slice_in_dim(block, block.shape[dim] - width, None, axis=dim), axis, forward
        )
        high = lax.ppermute(lax.slice_in_dim(block, 0, width, axis=dim), axis, backward)
        block = jnp.concatenate([low, block, high], axis=dim)
    return block


def partner_2(block, axis, stride):
    count = lax.axis_size(axis)
    route = []
    for low in range(count):
        high = low | 1 << stride
        if high != low and high < count:
            route += [(low, high), (high, low)]
    return lax.ppermute(block, axis, route)


def resample_table(length):
    row_index = lax.broadcasted_iota(jnp.int32, (2 * length, length + 2), 0)
    col_index = lax.broadcasted_iota(jnp.int32, (2 * length, length + 2), 1)
    centre = row_index // 2
    parity = row_index % 2
    weights_table = jnp.where(col_index == centre + 1, 0.75, 0.0)
    weights_table = weights_table + jnp.where((col_index == centre) & (parity == 0), 0.25, 0.0)
    weights_table = weights_table + jnp.where((col_index == centre + 2) & (parity == 1), 0.25, 0.0)
    return weights_table.astype(jnp.bfloat16)


def blend_over(in_front, behind):
    return in_front + (1.0 - in_front[3])[None] * behind


def classify(density, bin_index, tf_colour, tf_extinction, total_depth):
    depth_cells, height_cells, width_cells = density.shape
    lookup = jnp.concatenate([tf_colour, tf_extinction[None, :]], axis=0)
    table_size = lookup.shape[1]
    bin_rows = lax.broadcasted_iota(jnp.int32, (table_size, 1), 0)
    flat_bins = bin_index.reshape(depth_cells, height_cells * width_cells)
    flat_density = density.reshape(depth_cells, height_cells * width_cells)

    def one_layer(layer, result):
        layer_bins = lax.dynamic_index_in_dim(flat_bins, layer, 0, keepdims=True)
        layer_density = lax.dynamic_index_in_dim(flat_density, layer, 0, keepdims=False)
        one_hot = (layer_bins == bin_rows).astype(jnp.bfloat16)
        values = jnp.dot(lookup, one_hot, preferred_element_type=jnp.float32)
        opacity = 1.0 - jnp.exp(-values[3] * layer_density / total_depth)
        cells = jnp.concatenate([values[:3] * opacity[None], opacity[None]], axis=0).astype(
            jnp.bfloat16
        )
        return lax.dynamic_update_slice_in_dim(result, cells[:, None], layer, 1)

    start_cells = jnp.zeros((4, depth_cells, height_cells * width_cells), jnp.bfloat16)
    classified = lax.fori_loop(0, depth_cells, one_layer, start_cells)
    return classified.reshape(4, depth_cells, height_cells, width_cells)


def general_device(density, bin_index, tf_colour, tf_extinction, slab_rank):
    slab_count = lax.axis_size("bz")
    depth_cells, height_cells, width_cells = density.shape
    total_depth = float(depth_cells * slab_count)
    colour_cells = classify(density, bin_index, tf_colour, tf_extinction, total_depth)
    padded = with_halo(colour_cells, (("bz", 1), ("by", 2), ("bx", 3)), 1)
    along_x = jnp.einsum(
        "czyq,pq->czyp", padded, resample_table(width_cells), preferred_element_type=jnp.float32
    ).astype(jnp.bfloat16)
    y_table = resample_table(height_cells)

    def add_sample(sample_index, image_now):
        centre = sample_index // 2
        parity = sample_index % 2
        layers = lax.dynamic_slice_in_dim(along_x, centre, 3, 1).astype(jnp.float32)
        lower_weight = jnp.where(parity == 0, 0.25, 0.0)
        upper_weight = jnp.where(parity == 1, 0.25, 0.0)
        mixed_layer = (
            lower_weight * layers[:, 0] + 0.75 * layers[:, 1] + upper_weight * layers[:, 2]
        ).astype(jnp.bfloat16)
        sample = jnp.einsum("qy,cyp->cqp", y_table, mixed_layer, preferred_element_type=jnp.float32)
        return blend_over(image_now, sample)

    start_image = jnp.zeros((4, 2 * height_cells, 2 * width_cells), jnp.float32)
    slab_image = lax.fori_loop(0, 2 * depth_cells, add_sample, start_image)
    rows_piece = 2 * height_cells // slab_count
    my_index = lax.axis_index("bz")
    bit_levels = slab_count.bit_length() - 1
    composite = slab_image.reshape((4,) + (2,) * bit_levels + (rows_piece, 2 * width_cells))
    my_rank = lax.dynamic_index_in_dim(slab_rank, my_index, 0, keepdims=False)
    for level in range(bit_levels):
        position = bit_levels - level
        my_bit = my_index // 2**level % 2
        kept_half = lax.dynamic_index_in_dim(composite, my_bit, position, keepdims=False)
        outgoing = lax.dynamic_index_in_dim(composite, 1 - my_bit, position, keepdims=False)
        incoming = partner_2(outgoing, "bz", level)
        partner = my_index + (1 - 2 * my_bit) * 2**level
        partner_rank = lax.dynamic_index_in_dim(slab_rank, partner, 0, keepdims=False)
        mine_first = my_rank < partner_rank
        composite = blend_over(
            jnp.where(mine_first, kept_half, incoming), jnp.where(mine_first, incoming, kept_half)
        )
    return composite


LANES = 128
LEVELS = 65535.0
VMEM = pl.BlockSpec(memory_space=pltpu.VMEM)


def pack_words(density, bins):
    level = (density * LEVELS + 0.5).astype(jnp.int32)
    return lax.shift_left(level, 16) | bins


def unpack_words(words):
    density = lax.shift_right_logical(words, 16).astype(jnp.float32) * (1.0 / LEVELS)
    return density, words & 0xFFFF


def cell_values(density, bins, tables, depth):
    low_bits = bins & (LANES - 1)
    upper = bins >= LANES

    def pick(channel):
        first, second = tables[channel]
        return jnp.where(
            upper,
            jnp.take_along_axis(second, low_bits, axis=1, mode="promise_in_bounds"),
            jnp.take_along_axis(first, low_bits, axis=1, mode="promise_in_bounds"),
        )

    opacity = (1.0 - jnp.exp(-pick(3) * density / depth)) * (1.0 / 64.0)
    return [pick(0) * opacity, pick(1) * opacity, pick(2) * opacity, opacity]


def read_tables(tables_ref):
    return [[tables_ref[2 * channel + half] for half in range(2)] for channel in range(4)]


def cost(microseconds):
    return pl.CostEstimate(
        flops=int(1e9 * microseconds), bytes_accessed=int(3.6e6 * microseconds), transcendentals=0
    )


def stage_kernel(
    density_ref, bins_ref, colour_ref, extinction_ref,
    first_ref, second_ref, columns_ref, dense_ref, index_ref, tables_ref,
):
    layers, rows, cols = density_ref.shape
    front = lax.axis_index("bz") == 0
    row_at = lax.broadcasted_iota(jnp.int32, (rows, LANES), 0)
    lane_at = lax.broadcasted_iota(jnp.int32, (rows, LANES), 1)
    for z in range(layers):
        first = pack_words(density_ref[z, :, 0:1], bins_ref[z, :, 0:1])
        last = pack_words(density_ref[z, :, cols - 1 : cols], bins_ref[z, :, cols - 1 : cols])
        line = jnp.where(lane_at == row_at, first, 0) + jnp.where(lane_at == row_at + rows, last, 0)
        columns_ref[z : z + 1, :] = jnp.sum(line, axis=0, keepdims=True)
        top, bottom = [
            pack_words(density_ref[z, r : r + 1, :], bins_ref[z, r : r + 1, :]) for r in (0, rows - 1)
        ]
        first_ref[z : z + 1, :] = jnp.where(front, bottom, top)
        second_ref[z : z + 1, :] = jnp.where(front, top, bottom)
        for tile in range(cols // LANES):
            lanes = slice(tile * LANES, (tile + 1) * LANES)
            dense_ref[z, tile, 0:rows] = density_ref[z, :, lanes]
            index_ref[z, tile, 0:rows] = bins_ref[z, :, lanes]
    colour = colour_ref[...].astype(jnp.float32)
    extinction = extinction_ref[...].astype(jnp.float32).reshape(1, 2 * LANES)
    for channel in range(4):
        line = extinction if channel == 3 else colour[channel : channel + 1]
        for half in range(2):
            tables_ref[2 * channel + half] = jnp.broadcast_to(
                line[:, half * LANES : (half + 1) * LANES], (8, LANES)
            )


def pack_kernel(dense_ref, index_ref, columns_ref, bulk_ref, inside_ref):
    layers, tiles, rows = dense_ref.shape[0], dense_ref.shape[1], dense_ref.shape[2] - 8
    half = rows // 2
    front = lax.axis_index("bz") == 0
    start = jnp.where(front, half, 0)
    for tile in range(tiles):
        lanes = slice(tile * LANES, (tile + 1) * LANES)
        bulk_ref[2 * layers + 1, :, lanes] = columns_ref[...]
        for z in range(layers):
            for part in range(2):
                at = pl.ds(start + part, half // 2, stride=2)
                bulk_ref[2 * z + part, :, lanes] = pack_words(
                    dense_ref[z, tile, at, :], index_ref[z, tile, at, :]
                )
            line = [
                pack_words(dense_ref[z, tile, r : r + 1, :], index_ref[z, tile, r : r + 1, :])
                for r in (half - 1, half)
            ]
            bulk_ref[2 * layers, z : z + 1, lanes] = jnp.where(front, line[0], line[1])
            inside_ref[z : z + 1, lanes] = jnp.where(front, line[1], line[0])


def near_words(slab, first_ref, second_ref):
    me = lax.axis_index("bz")
    words = jnp.where(me == slab, first_ref[...], second_ref[...])
    return jnp.where(has_near(me == 0), words, 0)


def side_kernel(columns_ref, bulk_ref, first_ref, second_ref, along_ref, ends_ref):
    layers = columns_ref.shape[0]
    front = lax.axis_index("bz") == 0
    lane_at = lax.broadcasted_iota(jnp.int32, (layers, LANES), 1)
    for slab in range(2):
        mine = front if slab == 0 else jnp.logical_not(front)
        columns = jnp.where(mine, columns_ref[...], bulk_ref[2 * layers + 1, :, 0:LANES])
        near = near_words(slab, first_ref, second_ref)
        cols = near.shape[1]
        columns = jnp.where(lane_at == 64, near[:, 0:1], columns)
        ends_ref[slab] = jnp.where(lane_at == 65, near[:, cols - 1 : cols], columns)


def has_near(front):
    me_y = lax.axis_index("by")
    return jnp.where(front, me_y > 0, me_y + 1 < lax.axis_size("by"))


def fill_weights(weights_ref, rows):
    cols = weights_ref.shape[0] - LANES
    row = lax.broadcasted_iota(jnp.int32, (cols, 2 * cols), 0)
    at = lax.broadcasted_iota(jnp.int32, (cols, 2 * cols), 1)
    centre = lax.shift_right_logical(at, 1)
    beside = centre - 1 + 2 * (at & 1)
    weights_ref[0:cols, :] = jnp.where(
        row == centre, 3.0, jnp.where(row == beside, 1.0, 0.0)
    ).astype(jnp.bfloat16)
    row = lax.broadcasted_iota(jnp.int32, (LANES, 2 * LANES), 0)
    at = lax.broadcasted_iota(jnp.int32, (LANES, 2 * LANES), 1)
    right = ((row < rows) | (row == 64)) & (at == 2 * LANES - 1)
    left = (((row >= rows) & (row < 2 * rows)) | (row == 65)) & (at == 0)
    weights_ref[cols : cols + LANES, 0 : 2 * LANES] = jnp.where(right | left, 1.0, 0.0).astype(
        jnp.bfloat16
    )


def lane_maps(rows):
    lane_at = lax.broadcasted_iota(jnp.int32, (8, LANES), 1)
    sub_at = lax.broadcasted_iota(jnp.int32, (8, LANES), 0)
    return lane_at & (rows - 1), lane_at < 2 * rows, sub_at


def classify_rows(read_cells, tables, cells_ref, layers, tiles):
    total = float(2 * layers)
    for z in range(layers):
        for tile in range(tiles):
            even = cell_values(*read_cells(z, 0, tile), tables, total)
            odd = cell_values(*read_cells(z, 1, tile), tables, total)
            for channel in range(4):
                base = (z * 4 + channel) * 16
                block = jnp.concatenate([even[channel], odd[channel]], axis=0)
                cells_ref[base : base + 16, tile * LANES : (tile + 1) * LANES] = block.astype(jnp.bfloat16)


def rounded(value):
    return value.astype(jnp.bfloat16).astype(jnp.float32)


def cells_kernel(dense_ref, index_ref, tables_ref, cells_ref, weights_ref):
    layers, tiles, rows = dense_ref.shape[0], dense_ref.shape[1], dense_ref.shape[2] - 8
    half = rows // 2
    start = lax.axis_index("bz") * half
    fill_weights(weights_ref, rows)

    def read_cells(z, part, tile):
        at = pl.ds(start + part, half // 2, stride=2)
        return dense_ref[z, tile, at, :], index_ref[z, tile, at, :]

    classify_rows(read_cells, read_tables(tables_ref), cells_ref, layers, tiles)


def along_columns(cells, weights_ref, store):
    cols = cells.shape[1]
    tiles = 2 * cols // LANES
    result = jnp.dot(cells, weights_ref[0:cols, :], preferred_element_type=jnp.float32)
    for tile in range(tiles):
        block = result[:, tile * LANES : (tile + 1) * LANES]
        store(tile, block if tile in (0, tiles - 1) else rounded(block))


def own_kernel(cells_ref, weights_ref, along_ref):
    size = cells_ref.shape[0]
    pad = along_ref.shape[1] // 2 - size
    mine = pl.multiple_of(pad + lax.axis_index("bz") * size, pad)

    def store(tile, block):
        along_ref[tile, 0:pad, :] = jnp.zeros((pad, LANES), jnp.float32)
        along_ref[tile, pad + 2 * size :, :] = jnp.zeros((pad, LANES), jnp.float32)
        along_ref[tile, pl.ds(mine, size), :] = block

    along_columns(cells_ref[...], weights_ref, store)


def other_kernel(bulk_ref, tables_ref, weights_ref, ends_ref, own_ref, along_ref, cells_ref):
    layers = (bulk_ref.shape[0] - 2) // 2
    cols = bulk_ref.shape[2]
    size = cells_ref.shape[0]
    pad = along_ref.shape[1] // 2 - size
    theirs = pl.multiple_of(pad + (1 - lax.axis_index("bz")) * size, pad)

    def read_cells(z, part, tile):
        return unpack_words(bulk_ref[2 * z + part, :, tile * LANES : (tile + 1) * LANES])

    def store(tile, block):
        along_ref[tile, pl.ds(theirs, size), :] = block

    classify_rows(read_cells, read_tables(tables_ref), cells_ref, layers, cols // LANES)
    along_columns(cells_ref[...], weights_ref, store)


def edge_lines(now, shift_ref, depth):
    triple = 3.0 * now
    empty = jnp.zeros((8, LANES), jnp.float32)
    for layer in range(depth):
        here = triple[layer * 8 : layer * 8 + 8]
        before = now[layer * 8 - 8 : layer * 8] if layer > 0 else empty
        after = now[layer * 8 + 8 : layer * 8 + 16] if layer + 1 < depth else empty
        for parity, beside in enumerate((before, after)):
            line = rounded(beside + here)
            base = (layer * 2 + parity) * 128
            shift_ref[pl.ds(base + 23, 4, stride=32), :] = line[0:4]
            shift_ref[pl.ds(base + 8, 4, stride=32), :] = line[4:8]


def render_tile(along_ref, shift_ref, flip, layers):
    def one_slab(position, image):
        slab = position ^ flip
        view = along_ref.at[pl.ds(pl.multiple_of(slab * (layers * 64), 64), (layers + 2) * 64), :]
        shift = shift_ref.at[pl.ds(pl.multiple_of(slab * (layers * 256), 256), layers * 256), :]

        def layer_rows(layer, channel):
            base = (layer * 4 + channel) * 16
            return [view[base + part * 8 : base + part * 8 + 8, :] for part in range(2)]

        for z in range(layers):
            triple = [[3.0 * value for value in layer_rows(z + 1, channel)] for channel in range(4)]
            for parity in range(2):
                clear = [1.0 - value for value in image[3]]
                updated = []
                for channel in range(4):
                    beside = layer_rows(z + 2 * parity, channel)
                    even, odd = [rounded(beside[part] + triple[channel][part]) for part in range(2)]
                    base = ((z * 2 + parity) * 4 + channel) * 32
                    shift[base : base + 8, :] = even
                    shift[base + 24 : base + 32, :] = odd
                    before_even = shift[base + 23 : base + 31, :]
                    after_odd = shift[base + 1 : base + 9, :]
                    even_centre = 3.0 * even
                    odd_centre = 3.0 * odd
                    samples = [
                        before_even + even_centre,
                        even_centre + odd,
                        even + odd_centre,
                        odd_centre + after_odd,
                    ]
                    updated.append([image[channel][i] + clear[i] * samples[i] for i in range(4)])
                image = updated
        return image

    zero = jnp.zeros((8, LANES), jnp.float32)
    return lax.fori_loop(0, 2, one_slab, [[zero] * 4 for _ in range(4)])


def store_tile(image, mixed_ref, out_ref, lanes):
    for channel in range(4):
        for i in range(4):
            mixed_ref[channel, pl.ds(i, 8, stride=4), :] = image[channel][i]
        out_ref[channel, :, lanes] = mixed_ref[channel, 0:32]


def inner_kernel(
    rank_ref, tables_ref, weights_ref, bulk_ref, inside_ref, first_ref, second_ref, along_ref,
    image_ref, edge_ref, cells_ref, shift_ref, mixed_ref,
):
    layers, cols = inside_ref.shape
    depth = 2 * layers
    tiles = 2 * cols // LANES
    me = lax.axis_index("bz")
    front = me == 0
    tables = read_tables(tables_ref)
    for slab in range(2):
        inside = jnp.where(me == slab, inside_ref[...], bulk_ref[2 * layers])
        near = near_words(slab, first_ref, second_ref)
        for side in range(2):
            use_near = front if side == 0 else jnp.logical_not(front)
            words = jnp.where(use_near, near, inside)
            for t in range(cols // LANES):
                values = cell_values(
                    *unpack_words(words[:, t * LANES : (t + 1) * LANES]), tables, float(depth)
                )
                for channel in range(4):
                    at = pl.ds(slab * layers * 8 + side * 4 + channel, layers, stride=8)
                    cells_ref[t, at, :] = values[channel]
    edge = sum(
        jnp.dot(
            cells_ref[t, 0 : 8 * depth].astype(jnp.bfloat16),
            weights_ref[t * LANES : (t + 1) * LANES, :],
            preferred_element_type=jnp.float32,
        )
        for t in range(cols // LANES)
    )
    for tile in range(tiles):
        now = edge[:, tile * LANES : (tile + 1) * LANES]
        if tile in (0, tiles - 1):
            edge_ref[0 if tile == 0 else 1] = now
        else:
            edge_lines(rounded(now), shift_ref.at[tile - 1], depth)

    def one_tile(index, carry):
        image = render_tile(along_ref.at[index + 1], shift_ref.at[index], rank_ref[0], layers)
        store_tile(image, mixed_ref, image_ref, pl.ds(pl.multiple_of(index * LANES, LANES), LANES))
        return carry

    lax.fori_loop(0, tiles - 2, one_tile, 0)


def outer_kernel(
    rank_ref, tables_ref, weights_ref, beside_ref, across_ref, along_ref, edge_ref, image_ref,
    out_ref, ends_ref, values_ref, keep_ref, fixed_ref, shift_ref, mixed_ref,
):
    rows = out_ref.shape[1]
    cols = out_ref.shape[2] // 2
    layers = beside_ref.shape[1]
    depth = 2 * layers
    tiles = 2 * cols // LANES
    pad = 64
    size = layers * pad
    front = lax.axis_index("bz") == 0
    start = lax.axis_index("bz") * (rows // 2)
    me_x = lax.axis_index("bx")
    even_x = lax.rem(me_x, 2) == 0
    tables = read_tables(tables_ref)
    side_lane, has_side, sub_at = lane_maps(rows)
    masks = [has_side & (side_lane == start + 2 * sub_at + part) for part in range(2)]
    lane_at = lax.broadcasted_iota(jnp.int32, (layers, LANES), 1)
    is_right = (lane_at < rows) | (lane_at == 64)
    for slab in range(2):
        right = jnp.where(even_x, beside_ref[slab], across_ref[slab])
        left = jnp.where(even_x, across_ref[slab], beside_ref[slab])
        right = jnp.where(me_x + 1 < lax.axis_size("bx"), right, 0)
        left = jnp.where(me_x > 0, left, 0)
        words = jnp.where(is_right, right, left)
        values = cell_values(*unpack_words(words), tables, float(depth))
        for channel in range(4):
            values_ref[slab * 4 + channel, 0:layers] = values[channel]
        for z in range(layers):
            for channel in range(4):
                line = values_ref[slab * 4 + channel, pl.ds(z, 8, stride=0), :]
                block = jnp.concatenate([jnp.where(mask, line, 0.0) for mask in masks], axis=0)
                at = slab * size + (z * 4 + channel) * 16
                ends_ref[at : at + 16, :] = block.astype(jnp.bfloat16)
        for side in range(2):
            row = jnp.where(front, 64, rows // 2 - 1) if side == 0 else jnp.where(front, rows // 2, 64)
            twin = jnp.where(row == 64, 65, row + rows)
            keep = (lane_at == row) | (lane_at == twin)
            for channel in range(4):
                at = pl.ds(slab * layers * 8 + side * 4 + channel, layers, stride=8)
                keep_ref[at, :] = jnp.where(keep, values[channel], 0.0)
    ends_ref[2 * size :, :] = keep_ref[0 : 8 * depth].astype(jnp.bfloat16)
    added = jnp.dot(
        ends_ref[...], weights_ref[cols : cols + LANES, 0 : 2 * LANES], preferred_element_type=jnp.float32
    )
    for index, tile in enumerate((0, tiles - 1)):
        block = added[:, index * LANES : (index + 1) * LANES]
        fixed_ref[index, 0:pad, :] = jnp.zeros((pad, LANES), jnp.float32)
        fixed_ref[index, pad + 2 * size :, :] = jnp.zeros((pad, LANES), jnp.float32)
        fixed_ref[index, pad : pad + 2 * size, :] = rounded(
            along_ref[tile, pad : pad + 2 * size, :] + block[0 : 2 * size]
        )
        edge_lines(rounded(edge_ref[index] + block[2 * size :]), shift_ref.at[index], depth)
    out_ref[:, :, LANES : 2 * cols - LANES] = image_ref[...]

    def one_tile(index, carry):
        image = render_tile(fixed_ref.at[index], shift_ref.at[index], rank_ref[0], layers)
        lanes = pl.ds(pl.multiple_of(index * (2 * cols - LANES), LANES), LANES)
        store_tile(image, mixed_ref, out_ref, lanes)
        return carry

    lax.fori_loop(0, 2, one_tile, 0)


def two_slab_device(density, bin_index, tf_colour, tf_extinction, slab_rank):
    layers, rows, cols = density.shape
    half = rows // 2
    tiles = 2 * cols // LANES
    size = layers * 4 * half
    count_y, count_x = lax.axis_size("by"), lax.axis_size("bx")
    f32, bf16, i32 = jnp.float32, jnp.bfloat16, jnp.int32

    def call(kernel, name, out_shape, time, scratch_shapes=(), in_specs=None, aliases={}):
        def run(*operands):
            return pl.pallas_call(
                kernel,
                out_shape=out_shape,
                in_specs=in_specs or [VMEM] * len(operands),
                out_specs=(VMEM,) * len(out_shape) if isinstance(out_shape, tuple) else VMEM,
                scratch_shapes=scratch_shapes,
                input_output_aliases=aliases,
                compiler_params=pltpu.CompilerParams(vmem_limit_bytes=16 * 1024 * 1024),
                cost_estimate=cost(time),
                name=name,
            )(*operands)

        return run

    def both(route):
        return route + [(target, source) for source, target in route]

    blocks = (layers, cols // LANES, rows + 8, LANES)
    row = pltpu.VMEM((layers, cols), i32)
    first, second, columns, dense, index, tables = call(
        stage_kernel,
        "stage_block",
        (
            row,
            row,
            pltpu.VMEM((layers, LANES), i32),
            pltpu.VMEM(blocks, f32),
            pltpu.VMEM(blocks, i32),
            pltpu.VMEM((8, 8, LANES), f32),
        ),
        1.2,
    )(*[pltpu.with_memory_space_constraint(x, pltpu.HBM) for x in (density, bin_index, tf_colour, tf_extinction)])
    bulk, inside = call(
        pack_kernel, "pack_block", (pltpu.VMEM((2 * layers + 2, 8, cols), i32), row), 0.1
    )(dense, index, columns)

    def place(z, y, x):
        return (z * count_y + y) * count_x + x

    steps = range(count_y - 1)
    ring = [(place(0, y, 0), place(0, y + 1, 0)) for y in steps]
    ring += [(place(1, y + 1, 0), place(1, y, 0)) for y in steps]
    ring += [(place(0, count_y - 1, 0), place(1, count_y - 1, 0)), (place(1, 0, 0), place(0, 0, 0))]
    ring = [(source + x, target + x) for source, target in ring for x in range(count_x)]
    diagonal = [(place(1, y, x), place(0, y + 1, x)) for y in steps for x in range(count_x)]
    for z, y in ((0, 0), (1, count_y - 1)):
        diagonal += [(place(z, y, x), place(z, y, x + 1)) for x in range(0, count_x, 2)]
    axes = ("bz", "by", "bx")
    bulk = lax.ppermute(bulk, "bz", [(0, 1), (1, 0)])
    first = lax.ppermute(first, axes, ring)
    second = lax.ppermute(second, axes, both(diagonal))

    cells, weights = call(
        cells_kernel,
        "own_cells",
        (pltpu.VMEM((size, cols), bf16), pltpu.VMEM((cols + LANES, 2 * cols), bf16)),
        0.5,
    )(dense, index, tables)
    whole = pltpu.VMEM((tiles, 2 * size + 2 * 4 * half, LANES), f32)
    along = call(own_kernel, "own_slab", whole, 0.4)(cells, weights)
    ends = call(side_kernel, "side_columns", pltpu.VMEM((2, layers, LANES), i32), 0.1)(
        columns, bulk, first, second, along
    )
    pairs = [(x, x + 1) for x in range(0, count_x, 2)]
    cross = [(x, (x + 1) % count_x) for x in range(1, count_x, 2)]
    beside = lax.ppermute(ends, "bx", both(pairs))
    across = lax.ppermute(ends, "bx", both(cross))
    along = call(other_kernel, "other_slab", whole, 0.8, [pltpu.VMEM((size, cols), bf16)], aliases={4: 0})(
        bulk, tables, weights, ends, along
    )
    smem = pl.BlockSpec(memory_space=pltpu.SMEM)
    shift = pltpu.VMEM((2, 512 * layers + 128, LANES), f32)
    image, edge = call(
        inner_kernel,
        "inner_tiles",
        (pltpu.VMEM((4, rows, (tiles - 2) * LANES), f32), pltpu.VMEM((2, 16 * layers, LANES), f32)),
        2.0,
        [pltpu.VMEM((cols // LANES, 16 * layers + 8, LANES), f32), shift, pltpu.VMEM((4, rows + 8, LANES), f32)],
        [smem] + [VMEM] * 7,
    )(slab_rank, tables, weights, bulk, inside, first, second, along)
    return call(
        outer_kernel,
        "outer_tiles",
        jax.ShapeDtypeStruct((4, rows, 2 * cols), f32),
        2.0,
        [
            pltpu.VMEM((2 * size + 16 * layers, LANES), bf16),
            pltpu.VMEM((8, 2 * layers, LANES), f32),
            pltpu.VMEM((16 * layers + 8, LANES), f32),
            pltpu.VMEM((2, 2 * size + 2 * 4 * half, LANES), f32),
            shift,
            pltpu.VMEM((4, rows + 8, LANES), f32),
        ],
        [smem] + [VMEM] * 7,
    )(slab_rank, tables, weights, beside, across, along, edge, image)


def on_device(density, bin_index, tf_colour, tf_extinction, slab_rank):
    if lax.axis_size("bz") == 2:
        return two_slab_device(density, bin_index, tf_colour, tf_extinction, slab_rank)
    return general_device(density, bin_index, tf_colour, tf_extinction, slab_rank)


def solution(mesh):
    return jax.shard_map(
        on_device,
        mesh=mesh,
        in_specs=(P("bz", "by", "bx"), P("bz", "by", "bx"), P(), P(), P()),
        out_specs=P(None, ("by", "bz"), "bx"),
        check_vma=False,
    )
```

```python
import jax
import jax.numpy as jnp
from jax import lax
from jax.experimental import pallas as pl
from jax.experimental.pallas import tpu as pltpu
from jax.sharding import PartitionSpec as P


def with_halo(block, sides, width):
    for axis, dim in sides:
        count = lax.axis_size(axis)
        forward = [(i, i + 1) for i in range(count - 1)]
        backward = [(target, source) for source, target in forward]
        low = lax.ppermute(
            lax.slice_in_dim(block, block.shape[dim] - width, None, axis=dim), axis, forward
        )
        high = lax.ppermute(lax.slice_in_dim(block, 0, width, axis=dim), axis, backward)
        block = jnp.concatenate([low, block, high], axis=dim)
    return block


def partner_2(block, axis, stride):
    count = lax.axis_size(axis)
    route = []
    for low in range(count):
        high = low | 1 << stride
        if high != low and high < count:
            route += [(low, high), (high, low)]
    return lax.ppermute(block, axis, route)


def resample_table(length):
    row_index = lax.broadcasted_iota(jnp.int32, (2 * length, length + 2), 0)
    col_index = lax.broadcasted_iota(jnp.int32, (2 * length, length + 2), 1)
    centre = row_index // 2
    parity = row_index % 2
    weights_table = jnp.where(col_index == centre + 1, 0.75, 0.0)
    weights_table = weights_table + jnp.where((col_index == centre) & (parity == 0), 0.25, 0.0)
    weights_table = weights_table + jnp.where((col_index == centre + 2) & (parity == 1), 0.25, 0.0)
    return weights_table.astype(jnp.bfloat16)


def blend_over(in_front, behind):
    return in_front + (1.0 - in_front[3])[None] * behind


def classify(density, bin_index, tf_colour, tf_extinction, total_depth):
    depth_cells, height_cells, width_cells = density.shape
    lookup = jnp.concatenate([tf_colour, tf_extinction[None, :]], axis=0)
    table_size = lookup.shape[1]
    bin_rows = lax.broadcasted_iota(jnp.int32, (table_size, 1), 0)
    flat_bins = bin_index.reshape(depth_cells, height_cells * width_cells)
    flat_density = density.reshape(depth_cells, height_cells * width_cells)

    def one_layer(layer, result):
        layer_bins = lax.dynamic_index_in_dim(flat_bins, layer, 0, keepdims=True)
        layer_density = lax.dynamic_index_in_dim(flat_density, layer, 0, keepdims=False)
        one_hot = (layer_bins == bin_rows).astype(jnp.bfloat16)
        values = jnp.dot(lookup, one_hot, preferred_element_type=jnp.float32)
        opacity = 1.0 - jnp.exp(-values[3] * layer_density / total_depth)
        cells = jnp.concatenate([values[:3] * opacity[None], opacity[None]], axis=0).astype(
            jnp.bfloat16
        )
        return lax.dynamic_update_slice_in_dim(result, cells[:, None], layer, 1)

    start_cells = jnp.zeros((4, depth_cells, height_cells * width_cells), jnp.bfloat16)
    classified = lax.fori_loop(0, depth_cells, one_layer, start_cells)
    return classified.reshape(4, depth_cells, height_cells, width_cells)


def general_device(density, bin_index, tf_colour, tf_extinction, slab_rank):
    slab_count = lax.axis_size("bz")
    depth_cells, height_cells, width_cells = density.shape
    total_depth = float(depth_cells * slab_count)
    colour_cells = classify(density, bin_index, tf_colour, tf_extinction, total_depth)
    padded = with_halo(colour_cells, (("bz", 1), ("by", 2), ("bx", 3)), 1)
    along_x = jnp.einsum(
        "czyq,pq->czyp", padded, resample_table(width_cells), preferred_element_type=jnp.float32
    ).astype(jnp.bfloat16)
    y_table = resample_table(height_cells)

    def add_sample(sample_index, image_now):
        centre = sample_index // 2
        parity = sample_index % 2
        layers = lax.dynamic_slice_in_dim(along_x, centre, 3, 1).astype(jnp.float32)
        lower_weight = jnp.where(parity == 0, 0.25, 0.0)
        upper_weight = jnp.where(parity == 1, 0.25, 0.0)
        mixed_layer = (
            lower_weight * layers[:, 0] + 0.75 * layers[:, 1] + upper_weight * layers[:, 2]
        ).astype(jnp.bfloat16)
        sample = jnp.einsum("qy,cyp->cqp", y_table, mixed_layer, preferred_element_type=jnp.float32)
        return blend_over(image_now, sample)

    start_image = jnp.zeros((4, 2 * height_cells, 2 * width_cells), jnp.float32)
    slab_image = lax.fori_loop(0, 2 * depth_cells, add_sample, start_image)
    rows_piece = 2 * height_cells // slab_count
    my_index = lax.axis_index("bz")
    bit_levels = slab_count.bit_length() - 1
    composite = slab_image.reshape((4,) + (2,) * bit_levels + (rows_piece, 2 * width_cells))
    my_rank = lax.dynamic_index_in_dim(slab_rank, my_index, 0, keepdims=False)
    for level in range(bit_levels):
        position = bit_levels - level
        my_bit = my_index // 2**level % 2
        kept_half = lax.dynamic_index_in_dim(composite, my_bit, position, keepdims=False)
        outgoing = lax.dynamic_index_in_dim(composite, 1 - my_bit, position, keepdims=False)
        incoming = partner_2(outgoing, "bz", level)
        partner = my_index + (1 - 2 * my_bit) * 2**level
        partner_rank = lax.dynamic_index_in_dim(slab_rank, partner, 0, keepdims=False)
        mine_first = my_rank < partner_rank
        composite = blend_over(
            jnp.where(mine_first, kept_half, incoming), jnp.where(mine_first, incoming, kept_half)
        )
    return composite


LANES = 128
LEVELS = 65535.0
VMEM = pl.BlockSpec(memory_space=pltpu.VMEM)


def pack_words(density, bins):
    level = (density * LEVELS + 0.5).astype(jnp.int32)
    return lax.shift_left(level, 16) | bins


def unpack_words(words):
    density = lax.shift_right_logical(words, 16).astype(jnp.float32) * (1.0 / LEVELS)
    return density, words & 0xFFFF


def cell_values(density, bins, tables, depth):
    low_bits = bins & (LANES - 1)
    upper = bins >= LANES

    def pick(channel):
        first, second = tables[channel]
        return jnp.where(
            upper,
            jnp.take_along_axis(second, low_bits, axis=1, mode="promise_in_bounds"),
            jnp.take_along_axis(first, low_bits, axis=1, mode="promise_in_bounds"),
        )

    opacity = (1.0 - jnp.exp(-pick(3) * density / depth)) * (1.0 / 64.0)
    return [pick(0) * opacity, pick(1) * opacity, pick(2) * opacity, opacity]


def read_tables(tables_ref):
    return [[tables_ref[2 * channel + half] for half in range(2)] for channel in range(4)]


def cost(microseconds):
    return pl.CostEstimate(
        flops=int(1e9 * microseconds), bytes_accessed=int(3.6e6 * microseconds), transcendentals=0
    )


def stage_kernel(
    density_ref, bins_ref, colour_ref, extinction_ref,
    first_ref, second_ref, columns_ref, dense_ref, index_ref, tables_ref,
):
    layers, rows, cols = density_ref.shape
    front = lax.axis_index("bz") == 0
    row_at = lax.broadcasted_iota(jnp.int32, (rows, LANES), 0)
    lane_at = lax.broadcasted_iota(jnp.int32, (rows, LANES), 1)
    for z in range(layers):
        first = pack_words(density_ref[z, :, 0:1], bins_ref[z, :, 0:1])
        last = pack_words(density_ref[z, :, cols - 1 : cols], bins_ref[z, :, cols - 1 : cols])
        line = jnp.where(lane_at == row_at, first, 0) + jnp.where(lane_at == row_at + rows, last, 0)
        columns_ref[z : z + 1, :] = jnp.sum(line, axis=0, keepdims=True)
        top, bottom = [
            pack_words(density_ref[z, r : r + 1, :], bins_ref[z, r : r + 1, :]) for r in (0, rows - 1)
        ]
        first_ref[z : z + 1, :] = jnp.where(front, bottom, top)
        second_ref[z : z + 1, :] = jnp.where(front, top, bottom)
        for tile in range(cols // LANES):
            lanes = slice(tile * LANES, (tile + 1) * LANES)
            dense_ref[z, tile, 0:rows] = density_ref[z, :, lanes]
            index_ref[z, tile, 0:rows] = bins_ref[z, :, lanes]
    colour = colour_ref[...].astype(jnp.float32)
    extinction = extinction_ref[...].astype(jnp.float32).reshape(1, 2 * LANES)
    for channel in range(4):
        line = extinction if channel == 3 else colour[channel : channel + 1]
        for half in range(2):
            tables_ref[2 * channel + half] = jnp.broadcast_to(
                line[:, half * LANES : (half + 1) * LANES], (8, LANES)
            )


def pack_kernel(dense_ref, index_ref, columns_ref, bulk_ref, inside_ref):
    layers, tiles, rows = dense_ref.shape[0], dense_ref.shape[1], dense_ref.shape[2] - 8
    half = rows // 2
    front = lax.axis_index("bz") == 0
    start = jnp.where(front, half, 0)
    for tile in range(tiles):
        lanes = slice(tile * LANES, (tile + 1) * LANES)
        bulk_ref[2 * layers + 1, :, lanes] = columns_ref[...]
        for z in range(layers):
            for part in range(2):
                at = pl.ds(start + part, half // 2, stride=2)
                bulk_ref[2 * z + part, :, lanes] = pack_words(
                    dense_ref[z, tile, at, :], index_ref[z, tile, at, :]
                )
            line = [
                pack_words(dense_ref[z, tile, r : r + 1, :], index_ref[z, tile, r : r + 1, :])
                for r in (half - 1, half)
            ]
            bulk_ref[2 * layers, z : z + 1, lanes] = jnp.where(front, line[0], line[1])
            inside_ref[z : z + 1, lanes] = jnp.where(front, line[1], line[0])


def near_words(slab, first_ref, second_ref):
    me = lax.axis_index("bz")
    words = jnp.where(me == slab, first_ref[...], second_ref[...])
    return jnp.where(has_near(me == 0), words, 0)


def side_kernel(columns_ref, bulk_ref, first_ref, second_ref, along_ref, ends_ref):
    layers = columns_ref.shape[0]
    front = lax.axis_index("bz") == 0
    lane_at = lax.broadcasted_iota(jnp.int32, (layers, LANES), 1)
    for slab in range(2):
        mine = front if slab == 0 else jnp.logical_not(front)
        columns = jnp.where(mine, columns_ref[...], bulk_ref[2 * layers + 1, :, 0:LANES])
        near = near_words(slab, first_ref, second_ref)
        cols = near.shape[1]
        columns = jnp.where(lane_at == 64, near[:, 0:1], columns)
        ends_ref[slab] = jnp.where(lane_at == 65, near[:, cols - 1 : cols], columns)


def has_near(front):
    me_y = lax.axis_index("by")
    return jnp.where(front, me_y > 0, me_y + 1 < lax.axis_size("by"))


def fill_weights(weights_ref, rows):
    cols = weights_ref.shape[0] - LANES
    row = lax.broadcasted_iota(jnp.int32, (cols, 2 * cols), 0)
    at = lax.broadcasted_iota(jnp.int32, (cols, 2 * cols), 1)
    centre = lax.shift_right_logical(at, 1)
    beside = centre - 1 + 2 * (at & 1)
    weights_ref[0:cols, :] = jnp.where(
        row == centre, 3.0, jnp.where(row == beside, 1.0, 0.0)
    ).astype(jnp.bfloat16)
    row = lax.broadcasted_iota(jnp.int32, (LANES, 2 * LANES), 0)
    at = lax.broadcasted_iota(jnp.int32, (LANES, 2 * LANES), 1)
    right = ((row < rows) | (row == 64)) & (at == 2 * LANES - 1)
    left = (((row >= rows) & (row < 2 * rows)) | (row == 65)) & (at == 0)
    weights_ref[cols : cols + LANES, 0 : 2 * LANES] = jnp.where(right | left, 1.0, 0.0).astype(
        jnp.bfloat16
    )


def lane_maps(rows):
    lane_at = lax.broadcasted_iota(jnp.int32, (8, LANES), 1)
    sub_at = lax.broadcasted_iota(jnp.int32, (8, LANES), 0)
    return lane_at & (rows - 1), lane_at < 2 * rows, sub_at


def classify_rows(read_cells, tables, cells_ref, layers, tiles):
    total = float(2 * layers)

    def one_layer(z, carry):
        for tile in range(tiles):
            even = cell_values(*read_cells(z, 0, tile), tables, total)
            odd = cell_values(*read_cells(z, 1, tile), tables, total)
            for channel in range(4):
                base = pl.multiple_of((z * 4 + channel) * 16, 16)
                block = jnp.concatenate([even[channel], odd[channel]], axis=0)
                cells_ref[pl.ds(base, 16), tile * LANES : (tile + 1) * LANES] = block.astype(jnp.bfloat16)
        return carry

    lax.fori_loop(0, layers, one_layer, 0, unroll=2)


def rounded(value):
    return value.astype(jnp.bfloat16).astype(jnp.float32)


def cells_kernel(dense_ref, index_ref, tables_ref, cells_ref, weights_ref):
    layers, tiles, rows = dense_ref.shape[0], dense_ref.shape[1], dense_ref.shape[2] - 8
    half = rows // 2
    start = lax.axis_index("bz") * half
    fill_weights(weights_ref, rows)

    def read_cells(z, part, tile):
        at = pl.ds(start + part, half // 2, stride=2)
        return dense_ref[z, tile, at, :], index_ref[z, tile, at, :]

    classify_rows(read_cells, read_tables(tables_ref), cells_ref, layers, tiles)


def along_columns(cells, weights_ref, store):
    cols = cells.shape[1]
    tiles = 2 * cols // LANES
    result = jnp.dot(cells, weights_ref[0:cols, :], preferred_element_type=jnp.float32)
    for tile in range(tiles):
        block = result[:, tile * LANES : (tile + 1) * LANES]
        store(tile, block if tile in (0, tiles - 1) else rounded(block))


def own_kernel(cells_ref, weights_ref, along_ref):
    size = cells_ref.shape[0]
    pad = along_ref.shape[1] // 2 - size
    mine = pl.multiple_of(pad + lax.axis_index("bz") * size, pad)

    def store(tile, block):
        along_ref[tile, 0:pad, :] = jnp.zeros((pad, LANES), jnp.float32)
        along_ref[tile, pad + 2 * size :, :] = jnp.zeros((pad, LANES), jnp.float32)
        along_ref[tile, pl.ds(mine, size), :] = block

    along_columns(cells_ref[...], weights_ref, store)


def other_kernel(bulk_ref, tables_ref, weights_ref, ends_ref, own_ref, along_ref, cells_ref):
    layers = (bulk_ref.shape[0] - 2) // 2
    cols = bulk_ref.shape[2]
    size = cells_ref.shape[0]
    pad = along_ref.shape[1] // 2 - size
    theirs = pl.multiple_of(pad + (1 - lax.axis_index("bz")) * size, pad)

    def read_cells(z, part, tile):
        return unpack_words(bulk_ref[2 * z + part, :, tile * LANES : (tile + 1) * LANES])

    def store(tile, block):
        along_ref[tile, pl.ds(theirs, size), :] = block

    classify_rows(read_cells, read_tables(tables_ref), cells_ref, layers, cols // LANES)
    along_columns(cells_ref[...], weights_ref, store)


def edge_lines(now, lines_ref, depth):
    triple = 3.0 * now
    empty = jnp.zeros((8, LANES), jnp.float32)
    for layer in range(depth):
        here = triple[layer * 8 : layer * 8 + 8]
        before = now[layer * 8 - 8 : layer * 8] if layer > 0 else empty
        after = now[layer * 8 + 8 : layer * 8 + 16] if layer + 1 < depth else empty
        lines_ref[layer * 16 : layer * 16 + 8, :] = rounded(before + here)
        lines_ref[layer * 16 + 8 : layer * 16 + 16, :] = rounded(after + here)


def render_tile(along_ref, lines_ref, flip, layers):
    sub_at = lax.broadcasted_iota(jnp.int32, (8, LANES), 0)
    top = sub_at == 0
    bottom = sub_at == 7

    def one_layer(step, image):
        layer = ((step // layers) ^ flip) * layers + step % layers
        view = along_ref.at[pl.ds(pl.multiple_of(layer * 64, 64), 3 * 64), :]
        lines = lines_ref.at[pl.ds(pl.multiple_of(layer * 16, 16), 16 + 8), :]

        def layer_rows(offset, channel):
            base = (offset * 4 + channel) * 16
            return [view[base + part * 8 : base + part * 8 + 8, :] for part in range(2)]

        triple = [[3.0 * value for value in layer_rows(1, channel)] for channel in range(4)]
        for parity in range(2):
            clear = [1.0 - value for value in image[3]]
            updated = []
            for channel in range(4):
                beside = layer_rows(2 * parity, channel)
                even, odd = [rounded(beside[part] + triple[channel][part]) for part in range(2)]
                line = parity * 8 + channel
                above = lines[pl.ds(line, 8, stride=0), :]
                below = lines[pl.ds(line + 4, 8, stride=0), :]
                before_even = jnp.where(top, above, pltpu.roll(odd, 1, 0))
                after_odd = jnp.where(bottom, below, pltpu.roll(even, 7, 0))
                even_centre = 3.0 * even
                odd_centre = 3.0 * odd
                samples = [
                    before_even + even_centre,
                    even_centre + odd,
                    even + odd_centre,
                    odd_centre + after_odd,
                ]
                updated.append([image[channel][i] + clear[i] * samples[i] for i in range(4)])
            image = updated
        return image

    zero = jnp.zeros((8, LANES), jnp.float32)
    image = [[zero] * 4 for _ in range(4)]
    return lax.fori_loop(0, 2 * layers, one_layer, image, unroll=2)


def store_tile(image, mixed_ref, out_ref, lanes):
    for channel in range(4):
        for i in range(4):
            mixed_ref[channel, pl.ds(i, 8, stride=4), :] = image[channel][i]
        out_ref[channel, :, lanes] = mixed_ref[channel, 0:32]


def inner_kernel(
    rank_ref, tables_ref, weights_ref, bulk_ref, inside_ref, first_ref, second_ref, along_ref,
    image_ref, edge_ref, cells_ref, lines_ref, mixed_ref,
):
    layers, cols = inside_ref.shape
    depth = 2 * layers
    tiles = 2 * cols // LANES
    me = lax.axis_index("bz")
    front = me == 0
    tables = read_tables(tables_ref)
    for slab in range(2):
        inside = jnp.where(me == slab, inside_ref[...], bulk_ref[2 * layers])
        near = near_words(slab, first_ref, second_ref)
        for side in range(2):
            use_near = front if side == 0 else jnp.logical_not(front)
            words = jnp.where(use_near, near, inside)
            for t in range(cols // LANES):
                values = cell_values(
                    *unpack_words(words[:, t * LANES : (t + 1) * LANES]), tables, float(depth)
                )
                for channel in range(4):
                    at = pl.ds(slab * layers * 8 + side * 4 + channel, layers, stride=8)
                    cells_ref[t, at, :] = values[channel]
    edge = sum(
        jnp.dot(
            cells_ref[t, 0 : 8 * depth].astype(jnp.bfloat16),
            weights_ref[t * LANES : (t + 1) * LANES, :],
            preferred_element_type=jnp.float32,
        )
        for t in range(cols // LANES)
    )
    for tile in range(tiles):
        now = edge[:, tile * LANES : (tile + 1) * LANES]
        if tile in (0, tiles - 1):
            edge_ref[0 if tile == 0 else 1] = now
        else:
            edge_lines(rounded(now), lines_ref.at[tile - 1], depth)

    def one_tile(index, carry):
        image = render_tile(along_ref.at[index + 1], lines_ref.at[index], rank_ref[0], layers)
        store_tile(image, mixed_ref, image_ref, pl.ds(pl.multiple_of(index * LANES, LANES), LANES))
        return carry

    lax.fori_loop(0, tiles - 2, one_tile, 0)


def outer_kernel(
    rank_ref, tables_ref, weights_ref, beside_ref, across_ref, along_ref, edge_ref, image_ref,
    out_ref, ends_ref, values_ref, keep_ref, fixed_ref, lines_ref, mixed_ref,
):
    rows = out_ref.shape[1]
    cols = out_ref.shape[2] // 2
    layers = beside_ref.shape[1]
    depth = 2 * layers
    tiles = 2 * cols // LANES
    pad = 64
    size = layers * pad
    front = lax.axis_index("bz") == 0
    start = lax.axis_index("bz") * (rows // 2)
    me_x = lax.axis_index("bx")
    even_x = lax.rem(me_x, 2) == 0
    tables = read_tables(tables_ref)
    side_lane, has_side, sub_at = lane_maps(rows)
    masks = [has_side & (side_lane == start + 2 * sub_at + part) for part in range(2)]
    lane_at = lax.broadcasted_iota(jnp.int32, (layers, LANES), 1)
    is_right = (lane_at < rows) | (lane_at == 64)
    for slab in range(2):
        right = jnp.where(even_x, beside_ref[slab], across_ref[slab])
        left = jnp.where(even_x, across_ref[slab], beside_ref[slab])
        right = jnp.where(me_x + 1 < lax.axis_size("bx"), right, 0)
        left = jnp.where(me_x > 0, left, 0)
        words = jnp.where(is_right, right, left)
        values = cell_values(*unpack_words(words), tables, float(depth))
        for channel in range(4):
            values_ref[slab * 4 + channel, 0:layers] = values[channel]
        for z in range(layers):
            for channel in range(4):
                line = values_ref[slab * 4 + channel, pl.ds(z, 8, stride=0), :]
                block = jnp.concatenate([jnp.where(mask, line, 0.0) for mask in masks], axis=0)
                at = slab * size + (z * 4 + channel) * 16
                ends_ref[at : at + 16, :] = block.astype(jnp.bfloat16)
        for side in range(2):
            row = jnp.where(front, 64, rows // 2 - 1) if side == 0 else jnp.where(front, rows // 2, 64)
            twin = jnp.where(row == 64, 65, row + rows)
            keep = (lane_at == row) | (lane_at == twin)
            for channel in range(4):
                at = pl.ds(slab * layers * 8 + side * 4 + channel, layers, stride=8)
                keep_ref[at, :] = jnp.where(keep, values[channel], 0.0)
    ends_ref[2 * size :, :] = keep_ref[0 : 8 * depth].astype(jnp.bfloat16)
    added = jnp.dot(
        ends_ref[...], weights_ref[cols : cols + LANES, 0 : 2 * LANES], preferred_element_type=jnp.float32
    )
    for index, tile in enumerate((0, tiles - 1)):
        block = added[:, index * LANES : (index + 1) * LANES]
        fixed_ref[index, 0:pad, :] = jnp.zeros((pad, LANES), jnp.float32)
        fixed_ref[index, pad + 2 * size :, :] = jnp.zeros((pad, LANES), jnp.float32)
        fixed_ref[index, pad : pad + 2 * size, :] = rounded(
            along_ref[tile, pad : pad + 2 * size, :] + block[0 : 2 * size]
        )
        edge_lines(rounded(edge_ref[index] + block[2 * size :]), lines_ref.at[index], depth)
    out_ref[:, :, LANES : 2 * cols - LANES] = image_ref[...]

    def one_tile(index, carry):
        image = render_tile(fixed_ref.at[index], lines_ref.at[index], rank_ref[0], layers)
        lanes = pl.ds(pl.multiple_of(index * (2 * cols - LANES), LANES), LANES)
        store_tile(image, mixed_ref, out_ref, lanes)
        return carry

    lax.fori_loop(0, 2, one_tile, 0)


def two_slab_device(density, bin_index, tf_colour, tf_extinction, slab_rank):
    layers, rows, cols = density.shape
    half = rows // 2
    tiles = 2 * cols // LANES
    size = layers * 4 * half
    count_y, count_x = lax.axis_size("by"), lax.axis_size("bx")
    f32, bf16, i32 = jnp.float32, jnp.bfloat16, jnp.int32

    def call(kernel, name, out_shape, time, scratch_shapes=(), in_specs=None, aliases={}):
        def run(*operands):
            return pl.pallas_call(
                kernel,
                out_shape=out_shape,
                in_specs=in_specs or [VMEM] * len(operands),
                out_specs=(VMEM,) * len(out_shape) if isinstance(out_shape, tuple) else VMEM,
                scratch_shapes=scratch_shapes,
                input_output_aliases=aliases,
                compiler_params=pltpu.CompilerParams(vmem_limit_bytes=16 * 1024 * 1024),
                cost_estimate=cost(time),
                name=name,
            )(*operands)

        return run

    def both(route):
        return route + [(target, source) for source, target in route]

    blocks = (layers, cols // LANES, rows + 8, LANES)
    row = pltpu.VMEM((layers, cols), i32)
    first, second, columns, dense, index, tables = call(
        stage_kernel,
        "stage_block",
        (
            row,
            row,
            pltpu.VMEM((layers, LANES), i32),
            pltpu.VMEM(blocks, f32),
            pltpu.VMEM(blocks, i32),
            pltpu.VMEM((8, 8, LANES), f32),
        ),
        1.2,
    )(*[pltpu.with_memory_space_constraint(x, pltpu.HBM) for x in (density, bin_index, tf_colour, tf_extinction)])
    bulk, inside = call(
        pack_kernel, "pack_block", (pltpu.VMEM((2 * layers + 2, 8, cols), i32), row), 0.1
    )(dense, index, columns)

    def place(z, y, x):
        return (z * count_y + y) * count_x + x

    steps = range(count_y - 1)
    ring = [(place(0, y, 0), place(0, y + 1, 0)) for y in steps]
    ring += [(place(1, y + 1, 0), place(1, y, 0)) for y in steps]
    ring += [(place(0, count_y - 1, 0), place(1, count_y - 1, 0)), (place(1, 0, 0), place(0, 0, 0))]
    ring = [(source + x, target + x) for source, target in ring for x in range(count_x)]
    diagonal = [(place(1, y, x), place(0, y + 1, x)) for y in steps for x in range(count_x)]
    for z, y in ((0, 0), (1, count_y - 1)):
        diagonal += [(place(z, y, x), place(z, y, x + 1)) for x in range(0, count_x, 2)]
    axes = ("bz", "by", "bx")
    bulk = lax.ppermute(bulk, "bz", [(0, 1), (1, 0)])
    first = lax.ppermute(first, axes, ring)
    second = lax.ppermute(second, axes, both(diagonal))

    cells, weights = call(
        cells_kernel,
        "own_cells",
        (pltpu.VMEM((size, cols), bf16), pltpu.VMEM((cols + LANES, 2 * cols), bf16)),
        0.5,
    )(dense, index, tables)
    whole = pltpu.VMEM((tiles, 2 * size + 2 * 4 * half, LANES), f32)
    along = call(own_kernel, "own_slab", whole, 0.4)(cells, weights)
    ends = call(side_kernel, "side_columns", pltpu.VMEM((2, layers, LANES), i32), 0.1)(
        columns, bulk, first, second, along
    )
    pairs = [(x, x + 1) for x in range(0, count_x, 2)]
    cross = [(x, (x + 1) % count_x) for x in range(1, count_x, 2)]
    beside = lax.ppermute(ends, "bx", both(pairs))
    across = lax.ppermute(ends, "bx", both(cross))
    along = call(other_kernel, "other_slab", whole, 0.8, [pltpu.VMEM((size, cols), bf16)], aliases={4: 0})(
        bulk, tables, weights, ends, along
    )
    smem = pl.BlockSpec(memory_space=pltpu.SMEM)
    lines = pltpu.VMEM((2, 32 * layers + 8, LANES), f32)
    image, edge = call(
        inner_kernel,
        "inner_tiles",
        (pltpu.VMEM((4, rows, (tiles - 2) * LANES), f32), pltpu.VMEM((2, 16 * layers, LANES), f32)),
        2.0,
        [pltpu.VMEM((cols // LANES, 16 * layers + 8, LANES), f32), lines, pltpu.VMEM((4, rows + 8, LANES), f32)],
        [smem] + [VMEM] * 7,
    )(slab_rank, tables, weights, bulk, inside, first, second, along)
    return call(
        outer_kernel,
        "outer_tiles",
        jax.ShapeDtypeStruct((4, rows, 2 * cols), f32),
        2.0,
        [
            pltpu.VMEM((2 * size + 16 * layers, LANES), bf16),
            pltpu.VMEM((8, 2 * layers, LANES), f32),
            pltpu.VMEM((16 * layers + 8, LANES), f32),
            pltpu.VMEM((2, 2 * size + 2 * 4 * half, LANES), f32),
            lines,
            pltpu.VMEM((4, rows + 8, LANES), f32),
        ],
        [smem] + [VMEM] * 7,
    )(slab_rank, tables, weights, beside, across, along, edge, image)


def on_device(density, bin_index, tf_colour, tf_extinction, slab_rank):
    if lax.axis_size("bz") == 2:
        return two_slab_device(density, bin_index, tf_colour, tf_extinction, slab_rank)
    return general_device(density, bin_index, tf_colour, tf_extinction, slab_rank)


def solution(mesh):
    return jax.shard_map(
        on_device,
        mesh=mesh,
        in_specs=(P("bz", "by", "bx"), P("bz", "by", "bx"), P(), P(), P()),
        out_specs=P(None, ("by", "bz"), "bx"),
        check_vma=False,
    )
```

```python
import jax
import jax.numpy as jnp
from jax import lax
from jax.experimental import pallas as pl
from jax.experimental.pallas import tpu as pltpu
from jax.sharding import PartitionSpec as P


def with_halo(block, sides, width):
    for axis, dim in sides:
        count = lax.axis_size(axis)
        forward = [(i, i + 1) for i in range(count - 1)]
        backward = [(target, source) for source, target in forward]
        low = lax.ppermute(
            lax.slice_in_dim(block, block.shape[dim] - width, None, axis=dim), axis, forward
        )
        high = lax.ppermute(lax.slice_in_dim(block, 0, width, axis=dim), axis, backward)
        block = jnp.concatenate([low, block, high], axis=dim)
    return block


def partner_2(block, axis, stride):
    count = lax.axis_size(axis)
    route = []
    for low in range(count):
        high = low | 1 << stride
        if high != low and high < count:
            route += [(low, high), (high, low)]
    return lax.ppermute(block, axis, route)


def resample_table(length):
    row_index = lax.broadcasted_iota(jnp.int32, (2 * length, length + 2), 0)
    col_index = lax.broadcasted_iota(jnp.int32, (2 * length, length + 2), 1)
    centre = row_index // 2
    parity = row_index % 2
    weights_table = jnp.where(col_index == centre + 1, 0.75, 0.0)
    weights_table = weights_table + jnp.where((col_index == centre) & (parity == 0), 0.25, 0.0)
    weights_table = weights_table + jnp.where((col_index == centre + 2) & (parity == 1), 0.25, 0.0)
    return weights_table.astype(jnp.bfloat16)


def blend_over(in_front, behind):
    return in_front + (1.0 - in_front[3])[None] * behind


def classify(density, bin_index, tf_colour, tf_extinction, total_depth):
    depth_cells, height_cells, width_cells = density.shape
    lookup = jnp.concatenate([tf_colour, tf_extinction[None, :]], axis=0)
    table_size = lookup.shape[1]
    bin_rows = lax.broadcasted_iota(jnp.int32, (table_size, 1), 0)
    flat_bins = bin_index.reshape(depth_cells, height_cells * width_cells)
    flat_density = density.reshape(depth_cells, height_cells * width_cells)

    def one_layer(layer, result):
        layer_bins = lax.dynamic_index_in_dim(flat_bins, layer, 0, keepdims=True)
        layer_density = lax.dynamic_index_in_dim(flat_density, layer, 0, keepdims=False)
        one_hot = (layer_bins == bin_rows).astype(jnp.bfloat16)
        values = jnp.dot(lookup, one_hot, preferred_element_type=jnp.float32)
        opacity = 1.0 - jnp.exp(-values[3] * layer_density / total_depth)
        cells = jnp.concatenate([values[:3] * opacity[None], opacity[None]], axis=0).astype(
            jnp.bfloat16
        )
        return lax.dynamic_update_slice_in_dim(result, cells[:, None], layer, 1)

    start_cells = jnp.zeros((4, depth_cells, height_cells * width_cells), jnp.bfloat16)
    classified = lax.fori_loop(0, depth_cells, one_layer, start_cells)
    return classified.reshape(4, depth_cells, height_cells, width_cells)


def general_device(density, bin_index, tf_colour, tf_extinction, slab_rank):
    slab_count = lax.axis_size("bz")
    depth_cells, height_cells, width_cells = density.shape
    total_depth = float(depth_cells * slab_count)
    colour_cells = classify(density, bin_index, tf_colour, tf_extinction, total_depth)
    padded = with_halo(colour_cells, (("bz", 1), ("by", 2), ("bx", 3)), 1)
    along_x = jnp.einsum(
        "czyq,pq->czyp", padded, resample_table(width_cells), preferred_element_type=jnp.float32
    ).astype(jnp.bfloat16)
    y_table = resample_table(height_cells)

    def add_sample(sample_index, image_now):
        centre = sample_index // 2
        parity = sample_index % 2
        layers = lax.dynamic_slice_in_dim(along_x, centre, 3, 1).astype(jnp.float32)
        lower_weight = jnp.where(parity == 0, 0.25, 0.0)
        upper_weight = jnp.where(parity == 1, 0.25, 0.0)
        mixed_layer = (
            lower_weight * layers[:, 0] + 0.75 * layers[:, 1] + upper_weight * layers[:, 2]
        ).astype(jnp.bfloat16)
        sample = jnp.einsum("qy,cyp->cqp", y_table, mixed_layer, preferred_element_type=jnp.float32)
        return blend_over(image_now, sample)

    start_image = jnp.zeros((4, 2 * height_cells, 2 * width_cells), jnp.float32)
    slab_image = lax.fori_loop(0, 2 * depth_cells, add_sample, start_image)
    rows_piece = 2 * height_cells // slab_count
    my_index = lax.axis_index("bz")
    bit_levels = slab_count.bit_length() - 1
    composite = slab_image.reshape((4,) + (2,) * bit_levels + (rows_piece, 2 * width_cells))
    my_rank = lax.dynamic_index_in_dim(slab_rank, my_index, 0, keepdims=False)
    for level in range(bit_levels):
        position = bit_levels - level
        my_bit = my_index // 2**level % 2
        kept_half = lax.dynamic_index_in_dim(composite, my_bit, position, keepdims=False)
        outgoing = lax.dynamic_index_in_dim(composite, 1 - my_bit, position, keepdims=False)
        incoming = partner_2(outgoing, "bz", level)
        partner = my_index + (1 - 2 * my_bit) * 2**level
        partner_rank = lax.dynamic_index_in_dim(slab_rank, partner, 0, keepdims=False)
        mine_first = my_rank < partner_rank
        composite = blend_over(
            jnp.where(mine_first, kept_half, incoming), jnp.where(mine_first, incoming, kept_half)
        )
    return composite


LANES = 128
LEVELS = 65535.0
VMEM = pl.BlockSpec(memory_space=pltpu.VMEM)


def pack_words(density, bins):
    level = (density * LEVELS + 0.5).astype(jnp.int32)
    return lax.shift_left(level, 16) | bins


def unpack_words(words):
    density = lax.shift_right_logical(words, 16).astype(jnp.float32) * (1.0 / LEVELS)
    return density, words & 0xFFFF


def cell_values(density, bins, tables, depth):
    low_bits = bins & (LANES - 1)
    upper = bins >= LANES

    def pick(channel):
        first, second = tables[channel]
        return jnp.where(
            upper,
            jnp.take_along_axis(second, low_bits, axis=1, mode="promise_in_bounds"),
            jnp.take_along_axis(first, low_bits, axis=1, mode="promise_in_bounds"),
        )

    opacity = (1.0 - jnp.exp(-pick(3) * density / depth)) * (1.0 / 64.0)
    return [pick(0) * opacity, pick(1) * opacity, pick(2) * opacity, opacity]


def read_tables(tables_ref):
    return [[tables_ref[2 * channel + half] for half in range(2)] for channel in range(4)]


def cost(microseconds):
    return pl.CostEstimate(
        flops=int(1e9 * microseconds), bytes_accessed=int(3.6e6 * microseconds), transcendentals=0
    )


def stage_kernel(
    density_ref, bins_ref, colour_ref, extinction_ref,
    first_ref, second_ref, columns_ref, dense_ref, index_ref, tables_ref,
):
    layers, rows, cols = density_ref.shape
    front = lax.axis_index("bz") == 0
    row_at = lax.broadcasted_iota(jnp.int32, (rows, LANES), 0)
    lane_at = lax.broadcasted_iota(jnp.int32, (rows, LANES), 1)
    for z in range(layers):
        first = pack_words(density_ref[z, :, 0:1], bins_ref[z, :, 0:1])
        last = pack_words(density_ref[z, :, cols - 1 : cols], bins_ref[z, :, cols - 1 : cols])
        line = jnp.where(lane_at == row_at, first, 0) + jnp.where(lane_at == row_at + rows, last, 0)
        columns_ref[z : z + 1, :] = jnp.sum(line, axis=0, keepdims=True)
        top, bottom = [
            pack_words(density_ref[z, r : r + 1, :], bins_ref[z, r : r + 1, :]) for r in (0, rows - 1)
        ]
        first_ref[z : z + 1, :] = jnp.where(front, bottom, top)
        second_ref[z : z + 1, :] = jnp.where(front, top, bottom)
        for tile in range(cols // LANES):
            lanes = slice(tile * LANES, (tile + 1) * LANES)
            dense_ref[z, tile, 0:rows] = density_ref[z, :, lanes]
            index_ref[z, tile, 0:rows] = bins_ref[z, :, lanes]
    colour = colour_ref[...].astype(jnp.float32)
    extinction = extinction_ref[...].astype(jnp.float32).reshape(1, 2 * LANES)
    for channel in range(4):
        line = extinction if channel == 3 else colour[channel : channel + 1]
        for half in range(2):
            tables_ref[2 * channel + half] = jnp.broadcast_to(
                line[:, half * LANES : (half + 1) * LANES], (8, LANES)
            )


def pack_kernel(dense_ref, index_ref, columns_ref, bulk_ref, inside_ref):
    layers, tiles, rows = dense_ref.shape[0], dense_ref.shape[1], dense_ref.shape[2] - 8
    half = rows // 2
    front = lax.axis_index("bz") == 0
    start = jnp.where(front, half, 0)
    for tile in range(tiles):
        lanes = slice(tile * LANES, (tile + 1) * LANES)
        bulk_ref[2 * layers + 1, :, lanes] = columns_ref[...]
        for z in range(layers):
            for part in range(2):
                at = pl.ds(start + part, half // 2, stride=2)
                bulk_ref[2 * z + part, :, lanes] = pack_words(
                    dense_ref[z, tile, at, :], index_ref[z, tile, at, :]
                )
            line = [
                pack_words(dense_ref[z, tile, r : r + 1, :], index_ref[z, tile, r : r + 1, :])
                for r in (half - 1, half)
            ]
            bulk_ref[2 * layers, z : z + 1, lanes] = jnp.where(front, line[0], line[1])
            inside_ref[z : z + 1, lanes] = jnp.where(front, line[1], line[0])


def near_words(slab, first_ref, second_ref):
    me = lax.axis_index("bz")
    words = jnp.where(me == slab, first_ref[...], second_ref[...])
    return jnp.where(has_near(me == 0), words, 0)


def side_kernel(columns_ref, bulk_ref, second_ref, first_ref, along_ref, ends_ref):
    layers = columns_ref.shape[0]
    front = lax.axis_index("bz") == 0
    lane_at = lax.broadcasted_iota(jnp.int32, (layers, LANES), 1)
    for slab in range(2):
        mine = front if slab == 0 else jnp.logical_not(front)
        columns = jnp.where(mine, columns_ref[...], bulk_ref[2 * layers + 1, :, 0:LANES])
        near = near_words(slab, first_ref, second_ref)
        cols = near.shape[1]
        columns = jnp.where(lane_at == 64, near[:, 0:1], columns)
        ends_ref[slab] = jnp.where(lane_at == 65, near[:, cols - 1 : cols], columns)


def has_near(front):
    me_y = lax.axis_index("by")
    return jnp.where(front, me_y > 0, me_y + 1 < lax.axis_size("by"))


def fill_weights(weights_ref, rows):
    cols = weights_ref.shape[0] - LANES
    row = lax.broadcasted_iota(jnp.int32, (cols, 2 * cols), 0)
    at = lax.broadcasted_iota(jnp.int32, (cols, 2 * cols), 1)
    centre = lax.shift_right_logical(at, 1)
    beside = centre - 1 + 2 * (at & 1)
    weights_ref[0:cols, :] = jnp.where(
        row == centre, 3.0, jnp.where(row == beside, 1.0, 0.0)
    ).astype(jnp.bfloat16)
    row = lax.broadcasted_iota(jnp.int32, (LANES, 2 * LANES), 0)
    at = lax.broadcasted_iota(jnp.int32, (LANES, 2 * LANES), 1)
    right = ((row < rows) | (row == 64)) & (at == 2 * LANES - 1)
    left = (((row >= rows) & (row < 2 * rows)) | (row == 65)) & (at == 0)
    weights_ref[cols : cols + LANES, 0 : 2 * LANES] = jnp.where(right | left, 1.0, 0.0).astype(
        jnp.bfloat16
    )


def lane_maps(rows):
    lane_at = lax.broadcasted_iota(jnp.int32, (8, LANES), 1)
    sub_at = lax.broadcasted_iota(jnp.int32, (8, LANES), 0)
    return lane_at & (rows - 1), lane_at < 2 * rows, sub_at


def classify_rows(read_cells, tables, cells_ref, layers, tiles):
    total = float(2 * layers)
    for z in range(layers):
        for tile in range(tiles):
            even = cell_values(*read_cells(z, 0, tile), tables, total)
            odd = cell_values(*read_cells(z, 1, tile), tables, total)
            for channel in range(4):
                base = (z * 4 + channel) * 16
                block = jnp.concatenate([even[channel], odd[channel]], axis=0)
                cells_ref[base : base + 16, tile * LANES : (tile + 1) * LANES] = block.astype(jnp.bfloat16)


def rounded(value):
    return value.astype(jnp.bfloat16).astype(jnp.float32)


def cells_kernel(dense_ref, index_ref, tables_ref, cells_ref, weights_ref):
    layers, tiles, rows = dense_ref.shape[0], dense_ref.shape[1], dense_ref.shape[2] - 8
    half = rows // 2
    start = lax.axis_index("bz") * half
    fill_weights(weights_ref, rows)

    def read_cells(z, part, tile):
        at = pl.ds(start + part, half // 2, stride=2)
        return dense_ref[z, tile, at, :], index_ref[z, tile, at, :]

    classify_rows(read_cells, read_tables(tables_ref), cells_ref, layers, tiles)


def along_columns(cells, weights_ref, store):
    cols = cells.shape[1]
    tiles = 2 * cols // LANES
    result = jnp.dot(cells, weights_ref[0:cols, :], preferred_element_type=jnp.float32)
    for tile in range(tiles):
        block = result[:, tile * LANES : (tile + 1) * LANES]
        store(tile, block if tile in (0, tiles - 1) else rounded(block))


def own_kernel(cells_ref, weights_ref, along_ref):
    size = cells_ref.shape[0]
    pad = along_ref.shape[1] // 2 - size
    mine = pl.multiple_of(pad + lax.axis_index("bz") * size, pad)

    def store(tile, block):
        along_ref[tile, 0:pad, :] = jnp.zeros((pad, LANES), jnp.float32)
        along_ref[tile, pad + 2 * size :, :] = jnp.zeros((pad, LANES), jnp.float32)
        along_ref[tile, pl.ds(mine, size), :] = block

    along_columns(cells_ref[...], weights_ref, store)


def other_kernel(bulk_ref, tables_ref, weights_ref, ends_ref, own_ref, along_ref, cells_ref):
    layers = (bulk_ref.shape[0] - 2) // 2
    cols = bulk_ref.shape[2]
    size = cells_ref.shape[0]
    pad = along_ref.shape[1] // 2 - size
    theirs = pl.multiple_of(pad + (1 - lax.axis_index("bz")) * size, pad)

    def read_cells(z, part, tile):
        return unpack_words(bulk_ref[2 * z + part, :, tile * LANES : (tile + 1) * LANES])

    def store(tile, block):
        along_ref[tile, pl.ds(theirs, size), :] = block

    classify_rows(read_cells, read_tables(tables_ref), cells_ref, layers, cols // LANES)
    along_columns(cells_ref[...], weights_ref, store)


def edge_lines(now, lines_ref, depth):
    triple = 3.0 * now
    empty = jnp.zeros((8, LANES), jnp.float32)
    for layer in range(depth):
        here = triple[layer * 8 : layer * 8 + 8]
        before = now[layer * 8 - 8 : layer * 8] if layer > 0 else empty
        after = now[layer * 8 + 8 : layer * 8 + 16] if layer + 1 < depth else empty
        lines_ref[layer * 16 : layer * 16 + 8, :] = rounded(before + here)
        lines_ref[layer * 16 + 8 : layer * 16 + 16, :] = rounded(after + here)


def render_tile(along_ref, lines_ref, flip, layers):
    sub_at = lax.broadcasted_iota(jnp.int32, (8, LANES), 0)
    top = sub_at == 0
    bottom = sub_at == 7

    def one_slab(position, image):
        slab = position ^ flip
        view = along_ref.at[pl.ds(pl.multiple_of(slab * (layers * 64), 64), (layers + 2) * 64), :]
        lines = lines_ref.at[pl.ds(pl.multiple_of(slab * (layers * 16), 16), layers * 16 + 8), :]

        def layer_rows(layer, channel):
            base = (layer * 4 + channel) * 16
            return view[base : base + 16, :]

        for z in range(layers):
            triple = [3.0 * layer_rows(z + 1, channel) for channel in range(4)]
            for parity in range(2):
                clear = [1.0 - value for value in image[3]]
                updated = []
                for channel in range(4):
                    both = rounded(layer_rows(z + 2 * parity, channel) + triple[channel])
                    even, odd = both[0:8], both[8:16]
                    line = (z * 2 + parity) * 8 + channel
                    above = lines[pl.ds(line, 8, stride=0), :]
                    below = lines[pl.ds(line + 4, 8, stride=0), :]
                    before_even = jnp.where(top, above, pltpu.roll(odd, 1, 0))
                    after_odd = jnp.where(bottom, below, pltpu.roll(even, 7, 0))
                    even_centre = 3.0 * even
                    odd_centre = 3.0 * odd
                    samples = [
                        before_even + even_centre,
                        even_centre + odd,
                        even + odd_centre,
                        odd_centre + after_odd,
                    ]
                    updated.append([image[channel][i] + clear[i] * samples[i] for i in range(4)])
                image = updated
        return image

    zero = jnp.zeros((8, LANES), jnp.float32)
    return lax.fori_loop(0, 2, one_slab, [[zero] * 4 for _ in range(4)])


def store_tile(image, mixed_ref, out_ref, lanes):
    for channel in range(4):
        for i in range(4):
            mixed_ref[channel, pl.ds(i, 8, stride=4), :] = image[channel][i]
        out_ref[channel, :, lanes] = mixed_ref[channel, 0:32]


def inner_kernel(
    rank_ref, tables_ref, weights_ref, bulk_ref, inside_ref, second_ref, first_ref, along_ref,
    image_ref, edge_ref, cells_ref, lines_ref, mixed_ref,
):
    layers, cols = inside_ref.shape
    depth = 2 * layers
    tiles = 2 * cols // LANES
    me = lax.axis_index("bz")
    front = me == 0
    tables = read_tables(tables_ref)
    for slab in range(2):
        inside = jnp.where(me == slab, inside_ref[...], bulk_ref[2 * layers])
        near = near_words(slab, first_ref, second_ref)
        for side in range(2):
            use_near = front if side == 0 else jnp.logical_not(front)
            words = jnp.where(use_near, near, inside)
            for t in range(cols // LANES):
                values = cell_values(
                    *unpack_words(words[:, t * LANES : (t + 1) * LANES]), tables, float(depth)
                )
                for channel in range(4):
                    at = pl.ds(slab * layers * 8 + side * 4 + channel, layers, stride=8)
                    cells_ref[t, at, :] = values[channel]
    edge = sum(
        jnp.dot(
            cells_ref[t, 0 : 8 * depth].astype(jnp.bfloat16),
            weights_ref[t * LANES : (t + 1) * LANES, :],
            preferred_element_type=jnp.float32,
        )
        for t in range(cols // LANES)
    )
    for tile in range(tiles):
        now = edge[:, tile * LANES : (tile + 1) * LANES]
        if tile in (0, tiles - 1):
            edge_ref[0 if tile == 0 else 1] = now
        else:
            edge_lines(rounded(now), lines_ref.at[tile - 1], depth)

    def one_tile(index, carry):
        image = render_tile(along_ref.at[index + 1], lines_ref.at[index], rank_ref[0], layers)
        store_tile(image, mixed_ref, image_ref, pl.ds(pl.multiple_of(index * LANES, LANES), LANES))
        return carry

    lax.fori_loop(0, tiles - 2, one_tile, 0)


def outer_kernel(
    rank_ref, tables_ref, weights_ref, beside_ref, across_ref, along_ref, edge_ref, image_ref,
    out_ref, ends_ref, values_ref, keep_ref, fixed_ref, lines_ref, mixed_ref,
):
    rows = out_ref.shape[1]
    cols = out_ref.shape[2] // 2
    layers = beside_ref.shape[1]
    depth = 2 * layers
    tiles = 2 * cols // LANES
    pad = 64
    size = layers * pad
    front = lax.axis_index("bz") == 0
    start = lax.axis_index("bz") * (rows // 2)
    me_x = lax.axis_index("bx")
    even_x = lax.rem(me_x, 2) == 0
    tables = read_tables(tables_ref)
    side_lane, has_side, sub_at = lane_maps(rows)
    masks = [has_side & (side_lane == start + 2 * sub_at + part) for part in range(2)]
    lane_at = lax.broadcasted_iota(jnp.int32, (layers, LANES), 1)
    is_right = (lane_at < rows) | (lane_at == 64)
    for slab in range(2):
        right = jnp.where(even_x, beside_ref[slab], across_ref[slab])
        left = jnp.where(even_x, across_ref[slab], beside_ref[slab])
        right = jnp.where(me_x + 1 < lax.axis_size("bx"), right, 0)
        left = jnp.where(me_x > 0, left, 0)
        words = jnp.where(is_right, right, left)
        values = cell_values(*unpack_words(words), tables, float(depth))
        for channel in range(4):
            values_ref[slab * 4 + channel, 0:layers] = values[channel]
        for z in range(layers):
            for channel in range(4):
                line = values_ref[slab * 4 + channel, pl.ds(z, 8, stride=0), :]
                block = jnp.concatenate([jnp.where(mask, line, 0.0) for mask in masks], axis=0)
                at = slab * size + (z * 4 + channel) * 16
                ends_ref[at : at + 16, :] = block.astype(jnp.bfloat16)
        for side in range(2):
            row = jnp.where(front, 64, rows // 2 - 1) if side == 0 else jnp.where(front, rows // 2, 64)
            twin = jnp.where(row == 64, 65, row + rows)
            keep = (lane_at == row) | (lane_at == twin)
            for channel in range(4):
                at = pl.ds(slab * layers * 8 + side * 4 + channel, layers, stride=8)
                keep_ref[at, :] = jnp.where(keep, values[channel], 0.0)
    ends_ref[2 * size :, :] = keep_ref[0 : 8 * depth].astype(jnp.bfloat16)
    added = jnp.dot(
        ends_ref[...], weights_ref[cols : cols + LANES, 0 : 2 * LANES], preferred_element_type=jnp.float32
    )
    for index, tile in enumerate((0, tiles - 1)):
        block = added[:, index * LANES : (index + 1) * LANES]
        fixed_ref[index, 0:pad, :] = jnp.zeros((pad, LANES), jnp.float32)
        fixed_ref[index, pad + 2 * size :, :] = jnp.zeros((pad, LANES), jnp.float32)
        fixed_ref[index, pad : pad + 2 * size, :] = rounded(
            along_ref[tile, pad : pad + 2 * size, :] + block[0 : 2 * size]
        )
        edge_lines(rounded(edge_ref[index] + block[2 * size :]), lines_ref.at[index], depth)
    out_ref[:, :, LANES : 2 * cols - LANES] = image_ref[...]

    def one_tile(index, carry):
        image = render_tile(fixed_ref.at[index], lines_ref.at[index], rank_ref[0], layers)
        lanes = pl.ds(pl.multiple_of(index * (2 * cols - LANES), LANES), LANES)
        store_tile(image, mixed_ref, out_ref, lanes)
        return carry

    lax.fori_loop(0, 2, one_tile, 0)


def two_slab_device(density, bin_index, tf_colour, tf_extinction, slab_rank):
    layers, rows, cols = density.shape
    half = rows // 2
    tiles = 2 * cols // LANES
    size = layers * 4 * half
    count_y, count_x = lax.axis_size("by"), lax.axis_size("bx")
    f32, bf16, i32 = jnp.float32, jnp.bfloat16, jnp.int32

    def call(kernel, name, out_shape, time, scratch_shapes=(), in_specs=None, aliases={}):
        def run(*operands):
            return pl.pallas_call(
                kernel,
                out_shape=out_shape,
                in_specs=in_specs or [VMEM] * len(operands),
                out_specs=(VMEM,) * len(out_shape) if isinstance(out_shape, tuple) else VMEM,
                scratch_shapes=scratch_shapes,
                input_output_aliases=aliases,
                compiler_params=pltpu.CompilerParams(vmem_limit_bytes=16 * 1024 * 1024),
                cost_estimate=cost(time),
                name=name,
            )(*operands)

        return run

    def both(route):
        return route + [(target, source) for source, target in route]

    blocks = (layers, cols // LANES, rows + 8, LANES)
    row = pltpu.VMEM((layers, cols), i32)
    first, second, columns, dense, index, tables = call(
        stage_kernel,
        "stage_block",
        (
            row,
            row,
            pltpu.VMEM((layers, LANES), i32),
            pltpu.VMEM(blocks, f32),
            pltpu.VMEM(blocks, i32),
            pltpu.VMEM((8, 8, LANES), f32),
        ),
        1.2,
    )(*[pltpu.with_memory_space_constraint(x, pltpu.HBM) for x in (density, bin_index, tf_colour, tf_extinction)])
    bulk, inside = call(
        pack_kernel, "pack_block", (pltpu.VMEM((2 * layers + 2, 8, cols), i32), row), 0.1
    )(dense, index, columns)

    def place(z, y, x):
        return (z * count_y + y) * count_x + x

    steps = range(count_y - 1)
    ring = [(place(0, y, 0), place(0, y + 1, 0)) for y in steps]
    ring += [(place(1, y + 1, 0), place(1, y, 0)) for y in steps]
    ring += [(place(0, count_y - 1, 0), place(1, count_y - 1, 0)), (place(1, 0, 0), place(0, 0, 0))]
    ring = [(source + x, target + x) for source, target in ring for x in range(count_x)]
    diagonal = [(place(1, y, x), place(0, y + 1, x)) for y in steps for x in range(count_x)]
    for z, y in ((0, 0), (1, count_y - 1)):
        diagonal += [(place(z, y, x), place(z, y, x + 1)) for x in range(0, count_x, 2)]
    axes = ("bz", "by", "bx")
    bulk = lax.ppermute(bulk, "bz", [(0, 1), (1, 0)])
    first = lax.ppermute(first, axes, ring)
    second = lax.ppermute(second, axes, both(diagonal))

    cells, weights = call(
        cells_kernel,
        "own_cells",
        (pltpu.VMEM((size, cols), bf16), pltpu.VMEM((cols + LANES, 2 * cols), bf16)),
        0.5,
    )(dense, index, tables)
    whole = pltpu.VMEM((tiles, 2 * size + 2 * 4 * half, LANES), f32)
    along = call(own_kernel, "own_slab", whole, 0.4)(cells, weights)
    ends = call(side_kernel, "side_columns", pltpu.VMEM((2, layers, LANES), i32), 0.1)(
        columns, bulk, second, first, along
    )
    pairs = [(x, x + 1) for x in range(0, count_x, 2)]
    cross = [(x, (x + 1) % count_x) for x in range(1, count_x, 2)]
    beside = lax.ppermute(ends, "bx", both(pairs))
    across = lax.ppermute(ends, "bx", both(cross))
    along = call(other_kernel, "other_slab", whole, 0.8, [pltpu.VMEM((size, cols), bf16)], aliases={4: 0})(
        bulk, tables, weights, ends, along
    )
    smem = pl.BlockSpec(memory_space=pltpu.SMEM)
    lines = pltpu.VMEM((2, 32 * layers + 8, LANES), f32)
    image, edge = call(
        inner_kernel,
        "inner_tiles",
        (pltpu.VMEM((4, rows, (tiles - 2) * LANES), f32), pltpu.VMEM((2, 16 * layers, LANES), f32)),
        2.0,
        [pltpu.VMEM((cols // LANES, 16 * layers + 8, LANES), f32), lines, pltpu.VMEM((4, rows + 8, LANES), f32)],
        [smem] + [VMEM] * 7,
    )(slab_rank, tables, weights, bulk, inside, second, first, along)
    return call(
        outer_kernel,
        "outer_tiles",
        jax.ShapeDtypeStruct((4, rows, 2 * cols), f32),
        2.0,
        [
            pltpu.VMEM((2 * size + 16 * layers, LANES), bf16),
            pltpu.VMEM((8, 2 * layers, LANES), f32),
            pltpu.VMEM((16 * layers + 8, LANES), f32),
            pltpu.VMEM((2, 2 * size + 2 * 4 * half, LANES), f32),
            lines,
            pltpu.VMEM((4, rows + 8, LANES), f32),
        ],
        [smem] + [VMEM] * 7,
    )(slab_rank, tables, weights, beside, across, along, edge, image)


def on_device(density, bin_index, tf_colour, tf_extinction, slab_rank):
    if lax.axis_size("bz") == 2:
        return two_slab_device(density, bin_index, tf_colour, tf_extinction, slab_rank)
    return general_device(density, bin_index, tf_colour, tf_extinction, slab_rank)


def solution(mesh):
    return jax.shard_map(
        on_device,
        mesh=mesh,
        in_specs=(P("bz", "by", "bx"), P("bz", "by", "bx"), P(), P(), P()),
        out_specs=P(None, ("by", "bz"), "bx"),
        check_vma=False,
    )
```

```python
import jax
import jax.numpy as jnp
from jax import lax
from jax.experimental import pallas as pl
from jax.experimental.pallas import tpu as pltpu
from jax.sharding import PartitionSpec as P


def with_halo(block, sides, width):
    for axis, dim in sides:
        count = lax.axis_size(axis)
        forward = [(i, i + 1) for i in range(count - 1)]
        backward = [(target, source) for source, target in forward]
        low = lax.ppermute(
            lax.slice_in_dim(block, block.shape[dim] - width, None, axis=dim), axis, forward
        )
        high = lax.ppermute(lax.slice_in_dim(block, 0, width, axis=dim), axis, backward)
        block = jnp.concatenate([low, block, high], axis=dim)
    return block


def partner_2(block, axis, stride):
    count = lax.axis_size(axis)
    route = []
    for low in range(count):
        high = low | 1 << stride
        if high != low and high < count:
            route += [(low, high), (high, low)]
    return lax.ppermute(block, axis, route)


def resample_table(length):
    row_index = lax.broadcasted_iota(jnp.int32, (2 * length, length + 2), 0)
    col_index = lax.broadcasted_iota(jnp.int32, (2 * length, length + 2), 1)
    centre = row_index // 2
    parity = row_index % 2
    weights_table = jnp.where(col_index == centre + 1, 0.75, 0.0)
    weights_table = weights_table + jnp.where((col_index == centre) & (parity == 0), 0.25, 0.0)
    weights_table = weights_table + jnp.where((col_index == centre + 2) & (parity == 1), 0.25, 0.0)
    return weights_table.astype(jnp.bfloat16)


def blend_over(in_front, behind):
    return in_front + (1.0 - in_front[3])[None] * behind


def classify(density, bin_index, tf_colour, tf_extinction, total_depth):
    depth_cells, height_cells, width_cells = density.shape
    lookup = jnp.concatenate([tf_colour, tf_extinction[None, :]], axis=0)
    table_size = lookup.shape[1]
    bin_rows = lax.broadcasted_iota(jnp.int32, (table_size, 1), 0)
    flat_bins = bin_index.reshape(depth_cells, height_cells * width_cells)
    flat_density = density.reshape(depth_cells, height_cells * width_cells)

    def one_layer(layer, result):
        layer_bins = lax.dynamic_index_in_dim(flat_bins, layer, 0, keepdims=True)
        layer_density = lax.dynamic_index_in_dim(flat_density, layer, 0, keepdims=False)
        one_hot = (layer_bins == bin_rows).astype(jnp.bfloat16)
        values = jnp.dot(lookup, one_hot, preferred_element_type=jnp.float32)
        opacity = 1.0 - jnp.exp(-values[3] * layer_density / total_depth)
        cells = jnp.concatenate([values[:3] * opacity[None], opacity[None]], axis=0).astype(
            jnp.bfloat16
        )
        return lax.dynamic_update_slice_in_dim(result, cells[:, None], layer, 1)

    start_cells = jnp.zeros((4, depth_cells, height_cells * width_cells), jnp.bfloat16)
    classified = lax.fori_loop(0, depth_cells, one_layer, start_cells)
    return classified.reshape(4, depth_cells, height_cells, width_cells)


def general_device(density, bin_index, tf_colour, tf_extinction, slab_rank):
    slab_count = lax.axis_size("bz")
    depth_cells, height_cells, width_cells = density.shape
    total_depth = float(depth_cells * slab_count)
    colour_cells = classify(density, bin_index, tf_colour, tf_extinction, total_depth)
    padded = with_halo(colour_cells, (("bz", 1), ("by", 2), ("bx", 3)), 1)
    along_x = jnp.einsum(
        "czyq,pq->czyp", padded, resample_table(width_cells), preferred_element_type=jnp.float32
    ).astype(jnp.bfloat16)
    y_table = resample_table(height_cells)

    def add_sample(sample_index, image_now):
        centre = sample_index // 2
        parity = sample_index % 2
        layers = lax.dynamic_slice_in_dim(along_x, centre, 3, 1).astype(jnp.float32)
        lower_weight = jnp.where(parity == 0, 0.25, 0.0)
        upper_weight = jnp.where(parity == 1, 0.25, 0.0)
        mixed_layer = (
            lower_weight * layers[:, 0] + 0.75 * layers[:, 1] + upper_weight * layers[:, 2]
        ).astype(jnp.bfloat16)
        sample = jnp.einsum("qy,cyp->cqp", y_table, mixed_layer, preferred_element_type=jnp.float32)
        return blend_over(image_now, sample)

    start_image = jnp.zeros((4, 2 * height_cells, 2 * width_cells), jnp.float32)
    slab_image = lax.fori_loop(0, 2 * depth_cells, add_sample, start_image)
    rows_piece = 2 * height_cells // slab_count
    my_index = lax.axis_index("bz")
    bit_levels = slab_count.bit_length() - 1
    composite = slab_image.reshape((4,) + (2,) * bit_levels + (rows_piece, 2 * width_cells))
    my_rank = lax.dynamic_index_in_dim(slab_rank, my_index, 0, keepdims=False)
    for level in range(bit_levels):
        position = bit_levels - level
        my_bit = my_index // 2**level % 2
        kept_half = lax.dynamic_index_in_dim(composite, my_bit, position, keepdims=False)
        outgoing = lax.dynamic_index_in_dim(composite, 1 - my_bit, position, keepdims=False)
        incoming = partner_2(outgoing, "bz", level)
        partner = my_index + (1 - 2 * my_bit) * 2**level
        partner_rank = lax.dynamic_index_in_dim(slab_rank, partner, 0, keepdims=False)
        mine_first = my_rank < partner_rank
        composite = blend_over(
            jnp.where(mine_first, kept_half, incoming), jnp.where(mine_first, incoming, kept_half)
        )
    return composite


LANES = 128
LEVELS = 65535.0
VMEM = pl.BlockSpec(memory_space=pltpu.VMEM)


def pack_words(density, bins):
    level = (density * LEVELS + 0.5).astype(jnp.int32)
    return lax.shift_left(level, 16) | bins


def unpack_words(words):
    density = lax.shift_right_logical(words, 16).astype(jnp.float32) * (1.0 / LEVELS)
    return density, words & 0xFFFF


def cell_values(density, bins, tables, depth):
    low_bits = bins & (LANES - 1)
    upper = bins >= LANES

    def pick(channel):
        first, second = tables[channel]
        return jnp.where(
            upper,
            jnp.take_along_axis(second, low_bits, axis=1, mode="promise_in_bounds"),
            jnp.take_along_axis(first, low_bits, axis=1, mode="promise_in_bounds"),
        )

    opacity = (1.0 - jnp.exp(-pick(3) * density / depth)) * (1.0 / 64.0)
    return [pick(0) * opacity, pick(1) * opacity, pick(2) * opacity, opacity]


def read_tables(tables_ref):
    return [[tables_ref[2 * channel + half] for half in range(2)] for channel in range(4)]


def cost(microseconds):
    return pl.CostEstimate(
        flops=int(1e9 * microseconds), bytes_accessed=int(3.6e6 * microseconds), transcendentals=0
    )


def stage_kernel(
    density_ref, bins_ref, colour_ref, extinction_ref,
    first_ref, second_ref, columns_ref, dense_ref, index_ref, tables_ref,
):
    layers, rows, cols = density_ref.shape
    front = lax.axis_index("bz") == 0
    row_at = lax.broadcasted_iota(jnp.int32, (rows, LANES), 0)
    lane_at = lax.broadcasted_iota(jnp.int32, (rows, LANES), 1)
    for z in range(layers):
        first = pack_words(density_ref[z, :, 0:1], bins_ref[z, :, 0:1])
        last = pack_words(density_ref[z, :, cols - 1 : cols], bins_ref[z, :, cols - 1 : cols])
        line = jnp.where(lane_at == row_at, first, 0) + jnp.where(lane_at == row_at + rows, last, 0)
        columns_ref[z : z + 1, :] = jnp.sum(line, axis=0, keepdims=True)
        top, bottom = [
            pack_words(density_ref[z, r : r + 1, :], bins_ref[z, r : r + 1, :]) for r in (0, rows - 1)
        ]
        first_ref[z : z + 1, :] = jnp.where(front, bottom, top)
        second_ref[z : z + 1, :] = jnp.where(front, top, bottom)
        for tile in range(cols // LANES):
            lanes = slice(tile * LANES, (tile + 1) * LANES)
            dense_ref[z, tile, 0:rows] = density_ref[z, :, lanes]
            index_ref[z, tile, 0:rows] = bins_ref[z, :, lanes]
    colour = colour_ref[...].astype(jnp.float32)
    extinction = extinction_ref[...].astype(jnp.float32).reshape(1, 2 * LANES)
    for channel in range(4):
        line = extinction if channel == 3 else colour[channel : channel + 1]
        for half in range(2):
            tables_ref[2 * channel + half] = jnp.broadcast_to(
                line[:, half * LANES : (half + 1) * LANES], (8, LANES)
            )


def pack_kernel(dense_ref, index_ref, columns_ref, bulk_ref, inside_ref):
    layers, tiles, rows = dense_ref.shape[0], dense_ref.shape[1], dense_ref.shape[2] - 8
    half = rows // 2
    front = lax.axis_index("bz") == 0
    start = jnp.where(front, half, 0)
    for tile in range(tiles):
        lanes = slice(tile * LANES, (tile + 1) * LANES)
        bulk_ref[2 * layers + 1, :, lanes] = columns_ref[...]
        for z in range(layers):
            for part in range(2):
                at = pl.ds(start + part, half // 2, stride=2)
                bulk_ref[2 * z + part, :, lanes] = pack_words(
                    dense_ref[z, tile, at, :], index_ref[z, tile, at, :]
                )
            line = [
                pack_words(dense_ref[z, tile, r : r + 1, :], index_ref[z, tile, r : r + 1, :])
                for r in (half - 1, half)
            ]
            bulk_ref[2 * layers, z : z + 1, lanes] = jnp.where(front, line[0], line[1])
            inside_ref[z : z + 1, lanes] = jnp.where(front, line[1], line[0])


def near_words(slab, first_ref, second_ref):
    me = lax.axis_index("bz")
    words = jnp.where(me == slab, first_ref[...], second_ref[...])
    return jnp.where(has_near(me == 0), words, 0)


def side_kernel(columns_ref, bulk_ref, second_ref, first_ref, part_ref, ends_ref):
    layers = columns_ref.shape[0]
    front = lax.axis_index("bz") == 0
    lane_at = lax.broadcasted_iota(jnp.int32, (layers, LANES), 1)
    for slab in range(2):
        mine = front if slab == 0 else jnp.logical_not(front)
        columns = jnp.where(mine, columns_ref[...], bulk_ref[2 * layers + 1, :, 0:LANES])
        near = near_words(slab, first_ref, second_ref)
        cols = near.shape[1]
        columns = jnp.where(lane_at == 64, near[:, 0:1], columns)
        ends_ref[slab] = jnp.where(lane_at == 65, near[:, cols - 1 : cols], columns)


def has_near(front):
    me_y = lax.axis_index("by")
    return jnp.where(front, me_y > 0, me_y + 1 < lax.axis_size("by"))


def fill_weights(weights_ref, rows):
    cols = weights_ref.shape[0] - LANES
    row = lax.broadcasted_iota(jnp.int32, (cols, 2 * cols), 0)
    at = lax.broadcasted_iota(jnp.int32, (cols, 2 * cols), 1)
    centre = lax.shift_right_logical(at, 1)
    beside = centre - 1 + 2 * (at & 1)
    weights_ref[0:cols, :] = jnp.where(
        row == centre, 3.0, jnp.where(row == beside, 1.0, 0.0)
    ).astype(jnp.bfloat16)
    row = lax.broadcasted_iota(jnp.int32, (LANES, 2 * LANES), 0)
    at = lax.broadcasted_iota(jnp.int32, (LANES, 2 * LANES), 1)
    right = ((row < rows) | (row == 64)) & (at == 2 * LANES - 1)
    left = (((row >= rows) & (row < 2 * rows)) | (row == 65)) & (at == 0)
    weights_ref[cols : cols + LANES, 0 : 2 * LANES] = jnp.where(right | left, 1.0, 0.0).astype(
        jnp.bfloat16
    )


def lane_maps(rows):
    lane_at = lax.broadcasted_iota(jnp.int32, (8, LANES), 1)
    sub_at = lax.broadcasted_iota(jnp.int32, (8, LANES), 0)
    return lane_at & (rows - 1), lane_at < 2 * rows, sub_at


def classify_rows(read_cells, tables, cells_ref, layers, tiles):
    total = float(2 * layers)
    for z in range(layers):
        for tile in range(tiles):
            even = cell_values(*read_cells(z, 0, tile), tables, total)
            odd = cell_values(*read_cells(z, 1, tile), tables, total)
            for channel in range(4):
                base = (z * 4 + channel) * 16
                block = jnp.concatenate([even[channel], odd[channel]], axis=0)
                cells_ref[base : base + 16, tile * LANES : (tile + 1) * LANES] = block.astype(jnp.bfloat16)


def rounded(value):
    return value.astype(jnp.bfloat16).astype(jnp.float32)


def cells_kernel(dense_ref, index_ref, tables_ref, cells_ref, weights_ref):
    layers, tiles, rows = dense_ref.shape[0], dense_ref.shape[1], dense_ref.shape[2] - 8
    half = rows // 2
    start = lax.axis_index("bz") * half
    fill_weights(weights_ref, rows)

    def read_cells(z, part, tile):
        at = pl.ds(start + part, half // 2, stride=2)
        return dense_ref[z, tile, at, :], index_ref[z, tile, at, :]

    classify_rows(read_cells, read_tables(tables_ref), cells_ref, layers, tiles)


def along_columns(cells, weights_ref, store):
    cols = cells.shape[1]
    tiles = 2 * cols // LANES
    result = jnp.dot(cells, weights_ref[0:cols, :], preferred_element_type=jnp.float32)
    for tile in range(tiles):
        block = result[:, tile * LANES : (tile + 1) * LANES]
        store(tile, block if tile in (0, tiles - 1) else rounded(block))


def own_kernel(cells_ref, weights_ref, along_ref):
    size = cells_ref.shape[0]
    pad = along_ref.shape[1] // 2 - size
    mine = pl.multiple_of(pad + lax.axis_index("bz") * size, pad)

    def store(tile, block):
        along_ref[tile, 0:pad, :] = jnp.zeros((pad, LANES), jnp.float32)
        along_ref[tile, pad + 2 * size :, :] = jnp.zeros((pad, LANES), jnp.float32)
        along_ref[tile, pl.ds(mine, size), :] = block

    along_columns(cells_ref[...], weights_ref, store)


def other_kernel(bulk_ref, tables_ref, weights_ref, ends_ref, own_ref, along_ref, cells_ref):
    layers = (bulk_ref.shape[0] - 2) // 2
    cols = bulk_ref.shape[2]
    size = cells_ref.shape[0]
    pad = along_ref.shape[1] // 2 - size
    theirs = pl.multiple_of(pad + (1 - lax.axis_index("bz")) * size, pad)

    def read_cells(z, part, tile):
        return unpack_words(bulk_ref[2 * z + part, :, tile * LANES : (tile + 1) * LANES])

    def store(tile, block):
        along_ref[tile, pl.ds(theirs, size), :] = block

    classify_rows(read_cells, read_tables(tables_ref), cells_ref, layers, cols // LANES)
    along_columns(cells_ref[...], weights_ref, store)


def edge_cells(near, inside, tables, cells_ref, front, base, depth):
    layers, cols = near.shape
    for side in range(2):
        use_near = front if side == 0 else jnp.logical_not(front)
        words = jnp.where(use_near, near, inside)
        for t in range(cols // LANES):
            values = cell_values(
                *unpack_words(words[:, t * LANES : (t + 1) * LANES]), tables, float(depth)
            )
            for channel in range(4):
                at = pl.ds(base + side * 4 + channel, layers, stride=8)
                cells_ref[t, at, :] = values[channel]


def edge_columns(cells_ref, count, weights_ref):
    return sum(
        jnp.dot(
            cells_ref[t, 0:count].astype(jnp.bfloat16),
            weights_ref[t * LANES : (t + 1) * LANES, :],
            preferred_element_type=jnp.float32,
        )
        for t in range(cells_ref.shape[0])
    )


def edge_lines(now, lines_ref, before=None, after=None):
    depth = now.shape[0] // 8
    triple = 3.0 * now
    empty = jnp.zeros((8, LANES), jnp.float32)
    rows = [now[layer * 8 : layer * 8 + 8] for layer in range(depth)]
    rows = [empty if before is None else before] + rows + [empty if after is None else after]
    for layer in range(depth):
        here = triple[layer * 8 : layer * 8 + 8]
        for parity in range(2):
            at = layer * 16 + parity * 8
            lines_ref[at : at + 8, :] = rounded(rows[layer + 2 * parity] + here)


def row_samples(both, above, below):
    sub_at = lax.broadcasted_iota(jnp.int32, (8, LANES), 0)
    even, odd = both[0:8], both[8:16]
    before_even = jnp.where(sub_at == 0, above, pltpu.roll(odd, 1, 0))
    after_odd = jnp.where(sub_at == 7, below, pltpu.roll(even, 7, 0))
    even_centre = 3.0 * even
    odd_centre = 3.0 * odd
    return [before_even + even_centre, even_centre + odd, even + odd_centre, odd_centre + after_odd]


def over_layers(view, lines, layers, image, keep_first=None, keep_last=None):
    def layer_rows(layer, channel):
        base = (layer * 4 + channel) * 16
        return view[base : base + 16, :]

    for z in range(layers):
        triple = [3.0 * layer_rows(z + 1, channel) for channel in range(4)]
        for parity in range(2):
            keep = None
            if (z, parity) == (0, 0):
                keep = keep_first
            if (z, parity) == (layers - 1, 1):
                keep = keep_last
            clear = [1.0 - value for value in image[3]]
            updated = []
            for channel in range(4):
                both = rounded(layer_rows(z + 2 * parity, channel) + triple[channel])
                line = (z * 2 + parity) * 8 + channel
                above = lines[pl.ds(line, 8, stride=0), :]
                below = lines[pl.ds(line + 4, 8, stride=0), :]
                samples = row_samples(both, above, below)
                if keep is not None:
                    samples = [jnp.where(keep, sample, 0.0) for sample in samples]
                updated.append([image[channel][i] + clear[i] * samples[i] for i in range(4)])
            image = updated
    return image


def empty_image():
    zero = jnp.zeros((8, LANES), jnp.float32)
    return [[zero] * 4 for _ in range(4)]


def slab_views(along_ref, lines_ref, slab, layers):
    along_at = pl.multiple_of(slab * (layers * 64), 64)
    lines_at = pl.multiple_of(slab * (layers * 16), 16)
    return (
        along_ref.at[pl.ds(along_at, (layers + 2) * 64), :],
        lines_ref.at[pl.ds(lines_at, layers * 16 + 8), :],
    )


def render_tile(along_ref, lines_ref, flip, layers):
    def one_slab(position, image):
        view, lines = slab_views(along_ref, lines_ref, position ^ flip, layers)
        return over_layers(view, lines, layers, image)

    return lax.fori_loop(0, 2, one_slab, empty_image())


def own_tiles_kernel(
    tables_ref, weights_ref, inside_ref, first_ref, along_ref,
    part_ref, edge_ref, cells_ref, lines_ref,
):
    layers, cols = inside_ref.shape
    me = lax.axis_index("bz")
    front = me == 0
    near = jnp.where(has_near(front), first_ref[...], 0)
    edge_cells(near, inside_ref[...], read_tables(tables_ref), cells_ref, front, 0, 2 * layers)
    edge = edge_columns(cells_ref, 8 * layers, weights_ref)
    edge_ref[...] = edge
    edge = rounded(edge)
    tiles = edge.shape[1] // LANES
    for index in range(tiles - 2):
        edge_lines(edge[:, (index + 1) * LANES : (index + 2) * LANES], lines_ref.at[index])

    def one_tile(index, carry):
        view, _ = slab_views(along_ref.at[index + 1], lines_ref.at[index], me, layers)
        image = over_layers(
            view, lines_ref.at[index], layers, empty_image(), front, jnp.logical_not(front)
        )
        for channel in range(4):
            for i in range(4):
                part_ref[index, channel * 4 + i] = image[channel][i]
        return carry

    lax.fori_loop(0, tiles - 2, one_tile, 0)


def joined(first, in_front, behind):
    top = [[jnp.where(first, x, y) for x, y in zip(a, b)] for a, b in zip(in_front, behind)]
    low = [[jnp.where(first, y, x) for x, y in zip(a, b)] for a, b in zip(in_front, behind)]
    clear = [1.0 - value for value in top[3]]
    return [[top[c][i] + clear[i] * low[c][i] for i in range(4)] for c in range(4)]


def store_tile(image, mixed_ref, out_ref, lanes):
    for channel in range(4):
        for i in range(4):
            mixed_ref[channel, pl.ds(i, 8, stride=4), :] = image[channel][i]
        out_ref[channel, :, lanes] = mixed_ref[channel, 0:32]


def inner_kernel(
    rank_ref, tables_ref, weights_ref, bulk_ref, second_ref, own_edge_ref, part_ref, along_ref,
    image_ref, edge_ref, cells_ref, lines_ref, between_ref, mixed_ref,
):
    cols = bulk_ref.shape[2]
    layers = (bulk_ref.shape[0] - 2) // 2
    tiles = 2 * cols // LANES
    me = lax.axis_index("bz")
    front = me == 0
    near = jnp.where(has_near(front), second_ref[...], 0)
    edge_cells(near, bulk_ref[2 * layers], read_tables(tables_ref), cells_ref, front, 0, 2 * layers)
    edge = edge_columns(cells_ref, 8 * layers, weights_ref)
    for tile in range(tiles):
        lanes = slice(tile * LANES, (tile + 1) * LANES)
        mine, theirs = own_edge_ref[:, lanes], edge[:, lanes]
        if tile in (0, tiles - 1):
            index = 0 if tile == 0 else 1
            edge_ref[index, 0 : 8 * layers] = jnp.where(front, mine, theirs)
            edge_ref[index, 8 * layers : 16 * layers] = jnp.where(front, theirs, mine)
        else:
            mine, theirs = rounded(mine), rounded(theirs)
            index = tile - 1
            before = jnp.where(front, mine[8 * layers - 8 :], 0.0)
            after = jnp.where(front, 0.0, mine[0:8])
            edge_lines(theirs, lines_ref.at[index], before, after)
            here = jnp.where(front, mine[8 * layers - 8 :], mine[0:8])
            beside = jnp.where(front, theirs[0:8], theirs[8 * layers - 8 :])
            between_ref[index, 0:8] = rounded(beside + 3.0 * here)

    flip = rank_ref[0]

    def one_tile(index, carry):
        along = along_ref.at[index + 1]
        view, _ = slab_views(along, lines_ref.at[index], 1 - me, layers)
        other = over_layers(view, lines_ref.at[index], layers, empty_image())
        here_at = pl.multiple_of(jnp.where(front, layers, layers + 1) * 64, 64)
        beside_at = pl.multiple_of(jnp.where(front, layers + 1, layers) * 64, 64)
        between = []
        for channel in range(4):
            here = along[pl.ds(here_at + channel * 16, 16), :]
            beside = along[pl.ds(beside_at + channel * 16, 16), :]
            above = between_ref[index, pl.ds(channel, 8, stride=0), :]
            below = between_ref[index, pl.ds(channel + 4, 8, stride=0), :]
            between.append(row_samples(rounded(beside + 3.0 * here), above, below))
        part = [[part_ref[index, channel * 4 + i] for i in range(4)] for channel in range(4)]
        mine = joined(front, part, between)
        image = joined((me ^ flip) == 0, mine, other)
        store_tile(image, mixed_ref, image_ref, pl.ds(pl.multiple_of(index * LANES, LANES), LANES))
        return carry

    lax.fori_loop(0, tiles - 2, one_tile, 0)


def outer_kernel(
    rank_ref, tables_ref, weights_ref, beside_ref, across_ref, along_ref, edge_ref, image_ref,
    out_ref, ends_ref, values_ref, keep_ref, fixed_ref, lines_ref, mixed_ref,
):
    rows = out_ref.shape[1]
    cols = out_ref.shape[2] // 2
    layers = beside_ref.shape[1]
    depth = 2 * layers
    tiles = 2 * cols // LANES
    pad = 64
    size = layers * pad
    front = lax.axis_index("bz") == 0
    start = lax.axis_index("bz") * (rows // 2)
    me_x = lax.axis_index("bx")
    even_x = lax.rem(me_x, 2) == 0
    tables = read_tables(tables_ref)
    side_lane, has_side, sub_at = lane_maps(rows)
    masks = [has_side & (side_lane == start + 2 * sub_at + part) for part in range(2)]
    lane_at = lax.broadcasted_iota(jnp.int32, (layers, LANES), 1)
    is_right = (lane_at < rows) | (lane_at == 64)
    for slab in range(2):
        right = jnp.where(even_x, beside_ref[slab], across_ref[slab])
        left = jnp.where(even_x, across_ref[slab], beside_ref[slab])
        right = jnp.where(me_x + 1 < lax.axis_size("bx"), right, 0)
        left = jnp.where(me_x > 0, left, 0)
        words = jnp.where(is_right, right, left)
        values = cell_values(*unpack_words(words), tables, float(depth))
        for channel in range(4):
            values_ref[slab * 4 + channel, 0:layers] = values[channel]
        for z in range(layers):
            for channel in range(4):
                line = values_ref[slab * 4 + channel, pl.ds(z, 8, stride=0), :]
                block = jnp.concatenate([jnp.where(mask, line, 0.0) for mask in masks], axis=0)
                at = slab * size + (z * 4 + channel) * 16
                ends_ref[at : at + 16, :] = block.astype(jnp.bfloat16)
        for side in range(2):
            row = jnp.where(front, 64, rows // 2 - 1) if side == 0 else jnp.where(front, rows // 2, 64)
            twin = jnp.where(row == 64, 65, row + rows)
            keep = (lane_at == row) | (lane_at == twin)
            for channel in range(4):
                at = pl.ds(slab * layers * 8 + side * 4 + channel, layers, stride=8)
                keep_ref[at, :] = jnp.where(keep, values[channel], 0.0)
    ends_ref[2 * size :, :] = keep_ref[0 : 8 * depth].astype(jnp.bfloat16)
    added = jnp.dot(
        ends_ref[...], weights_ref[cols : cols + LANES, 0 : 2 * LANES], preferred_element_type=jnp.float32
    )
    for index, tile in enumerate((0, tiles - 1)):
        block = added[:, index * LANES : (index + 1) * LANES]
        fixed_ref[index, 0:pad, :] = jnp.zeros((pad, LANES), jnp.float32)
        fixed_ref[index, pad + 2 * size :, :] = jnp.zeros((pad, LANES), jnp.float32)
        fixed_ref[index, pad : pad + 2 * size, :] = rounded(
            along_ref[tile, pad : pad + 2 * size, :] + block[0 : 2 * size]
        )
        edge_lines(rounded(edge_ref[index] + block[2 * size :]), lines_ref.at[index])
    out_ref[:, :, LANES : 2 * cols - LANES] = image_ref[...]

    def one_tile(index, carry):
        image = render_tile(fixed_ref.at[index], lines_ref.at[index], rank_ref[0], layers)
        lanes = pl.ds(pl.multiple_of(index * (2 * cols - LANES), LANES), LANES)
        store_tile(image, mixed_ref, out_ref, lanes)
        return carry

    lax.fori_loop(0, 2, one_tile, 0)


def two_slab_device(density, bin_index, tf_colour, tf_extinction, slab_rank):
    layers, rows, cols = density.shape
    half = rows // 2
    tiles = 2 * cols // LANES
    size = layers * 4 * half
    count_y, count_x = lax.axis_size("by"), lax.axis_size("bx")
    f32, bf16, i32 = jnp.float32, jnp.bfloat16, jnp.int32

    def call(kernel, name, out_shape, time, scratch_shapes=(), in_specs=None, aliases={}):
        def run(*operands):
            return pl.pallas_call(
                kernel,
                out_shape=out_shape,
                in_specs=in_specs or [VMEM] * len(operands),
                out_specs=(VMEM,) * len(out_shape) if isinstance(out_shape, tuple) else VMEM,
                scratch_shapes=scratch_shapes,
                input_output_aliases=aliases,
                compiler_params=pltpu.CompilerParams(vmem_limit_bytes=16 * 1024 * 1024),
                cost_estimate=cost(time),
                name=name,
            )(*operands)

        return run

    def both(route):
        return route + [(target, source) for source, target in route]

    blocks = (layers, cols // LANES, rows + 8, LANES)
    row = pltpu.VMEM((layers, cols), i32)
    first, second, columns, dense, index, tables = call(
        stage_kernel,
        "stage_block",
        (
            row,
            row,
            pltpu.VMEM((layers, LANES), i32),
            pltpu.VMEM(blocks, f32),
            pltpu.VMEM(blocks, i32),
            pltpu.VMEM((8, 8, LANES), f32),
        ),
        1.2,
    )(*[pltpu.with_memory_space_constraint(x, pltpu.HBM) for x in (density, bin_index, tf_colour, tf_extinction)])
    bulk, inside = call(
        pack_kernel, "pack_block", (pltpu.VMEM((2 * layers + 2, 8, cols), i32), row), 0.1
    )(dense, index, columns)

    def place(z, y, x):
        return (z * count_y + y) * count_x + x

    steps = range(count_y - 1)
    ring = [(place(0, y, 0), place(0, y + 1, 0)) for y in steps]
    ring += [(place(1, y + 1, 0), place(1, y, 0)) for y in steps]
    ring += [(place(0, count_y - 1, 0), place(1, count_y - 1, 0)), (place(1, 0, 0), place(0, 0, 0))]
    ring = [(source + x, target + x) for source, target in ring for x in range(count_x)]
    diagonal = [(place(1, y, x), place(0, y + 1, x)) for y in steps for x in range(count_x)]
    for z, y in ((0, 0), (1, count_y - 1)):
        diagonal += [(place(z, y, x), place(z, y, x + 1)) for x in range(0, count_x, 2)]
    axes = ("bz", "by", "bx")
    bulk = lax.ppermute(bulk, "bz", [(0, 1), (1, 0)])
    first = lax.ppermute(first, axes, ring)
    second = lax.ppermute(second, axes, both(diagonal))

    cells, weights = call(
        cells_kernel,
        "own_cells",
        (pltpu.VMEM((size, cols), bf16), pltpu.VMEM((cols + LANES, 2 * cols), bf16)),
        0.5,
    )(dense, index, tables)
    whole = pltpu.VMEM((tiles, 2 * size + 2 * 4 * half, LANES), f32)
    along = call(own_kernel, "own_slab", whole, 0.4)(cells, weights)
    lines = pltpu.VMEM((2, 32 * layers + 8, LANES), f32)
    edge_rows = pltpu.VMEM((cols // LANES, 8 * layers + 8, LANES), f32)
    part, own_edge = call(
        own_tiles_kernel,
        "own_tiles",
        (pltpu.VMEM((tiles - 2, 16, 8, LANES), f32), pltpu.VMEM((8 * layers, 2 * cols), f32)),
        0.1,
        [edge_rows, lines],
    )(tables, weights, inside, first, along)
    ends = call(side_kernel, "side_columns", pltpu.VMEM((2, layers, LANES), i32), 0.1)(
        columns, bulk, second, first, part
    )
    pairs = [(x, x + 1) for x in range(0, count_x, 2)]
    cross = [(x, (x + 1) % count_x) for x in range(1, count_x, 2)]
    beside = lax.ppermute(ends, "bx", both(pairs))
    across = lax.ppermute(ends, "bx", both(cross))
    along = call(other_kernel, "other_slab", whole, 0.8, [pltpu.VMEM((size, cols), bf16)], aliases={4: 0})(
        bulk, tables, weights, ends, along
    )
    smem = pl.BlockSpec(memory_space=pltpu.SMEM)
    image, edge = call(
        inner_kernel,
        "inner_tiles",
        (pltpu.VMEM((4, rows, (tiles - 2) * LANES), f32), pltpu.VMEM((2, 16 * layers, LANES), f32)),
        2.0,
        [
            edge_rows,
            lines,
            pltpu.VMEM((tiles - 2, 16, LANES), f32),
            pltpu.VMEM((4, rows + 8, LANES), f32),
        ],
        [smem] + [VMEM] * 7,
    )(slab_rank, tables, weights, bulk, second, own_edge, part, along)
    return call(
        outer_kernel,
        "outer_tiles",
        jax.ShapeDtypeStruct((4, rows, 2 * cols), f32),
        2.0,
        [
            pltpu.VMEM((2 * size + 16 * layers, LANES), bf16),
            pltpu.VMEM((8, 2 * layers, LANES), f32),
            pltpu.VMEM((16 * layers + 8, LANES), f32),
            pltpu.VMEM((2, 2 * size + 2 * 4 * half, LANES), f32),
            lines,
            pltpu.VMEM((4, rows + 8, LANES), f32),
        ],
        [smem] + [VMEM] * 7,
    )(slab_rank, tables, weights, beside, across, along, edge, image)


def on_device(density, bin_index, tf_colour, tf_extinction, slab_rank):
    if lax.axis_size("bz") == 2:
        return two_slab_device(density, bin_index, tf_colour, tf_extinction, slab_rank)
    return general_device(density, bin_index, tf_colour, tf_extinction, slab_rank)


def solution(mesh):
    return jax.shard_map(
        on_device,
        mesh=mesh,
        in_specs=(P("bz", "by", "bx"), P("bz", "by", "bx"), P(), P(), P()),
        out_specs=P(None, ("by", "bz"), "bx"),
        check_vma=False,
    )
```

```python
import jax
import jax.numpy as jnp
from jax import lax
from jax.experimental import pallas as pl
from jax.experimental.pallas import tpu as pltpu
from jax.sharding import PartitionSpec as P


def with_halo(block, sides, width):
    for axis, dim in sides:
        count = lax.axis_size(axis)
        forward = [(i, i + 1) for i in range(count - 1)]
        backward = [(target, source) for source, target in forward]
        low = lax.ppermute(
            lax.slice_in_dim(block, block.shape[dim] - width, None, axis=dim), axis, forward
        )
        high = lax.ppermute(lax.slice_in_dim(block, 0, width, axis=dim), axis, backward)
        block = jnp.concatenate([low, block, high], axis=dim)
    return block


def partner_2(block, axis, stride):
    count = lax.axis_size(axis)
    route = []
    for low in range(count):
        high = low | 1 << stride
        if high != low and high < count:
            route += [(low, high), (high, low)]
    return lax.ppermute(block, axis, route)


def resample_table(length):
    row_index = lax.broadcasted_iota(jnp.int32, (2 * length, length + 2), 0)
    col_index = lax.broadcasted_iota(jnp.int32, (2 * length, length + 2), 1)
    centre = row_index // 2
    parity = row_index % 2
    weights_table = jnp.where(col_index == centre + 1, 0.75, 0.0)
    weights_table = weights_table + jnp.where((col_index == centre) & (parity == 0), 0.25, 0.0)
    weights_table = weights_table + jnp.where((col_index == centre + 2) & (parity == 1), 0.25, 0.0)
    return weights_table.astype(jnp.bfloat16)


def blend_over(in_front, behind):
    return in_front + (1.0 - in_front[3])[None] * behind


def classify(density, bin_index, tf_colour, tf_extinction, total_depth):
    depth_cells, height_cells, width_cells = density.shape
    lookup = jnp.concatenate([tf_colour, tf_extinction[None, :]], axis=0)
    table_size = lookup.shape[1]
    bin_rows = lax.broadcasted_iota(jnp.int32, (table_size, 1), 0)
    flat_bins = bin_index.reshape(depth_cells, height_cells * width_cells)
    flat_density = density.reshape(depth_cells, height_cells * width_cells)

    def one_layer(layer, result):
        layer_bins = lax.dynamic_index_in_dim(flat_bins, layer, 0, keepdims=True)
        layer_density = lax.dynamic_index_in_dim(flat_density, layer, 0, keepdims=False)
        one_hot = (layer_bins == bin_rows).astype(jnp.bfloat16)
        values = jnp.dot(lookup, one_hot, preferred_element_type=jnp.float32)
        opacity = 1.0 - jnp.exp(-values[3] * layer_density / total_depth)
        cells = jnp.concatenate([values[:3] * opacity[None], opacity[None]], axis=0).astype(
            jnp.bfloat16
        )
        return lax.dynamic_update_slice_in_dim(result, cells[:, None], layer, 1)

    start_cells = jnp.zeros((4, depth_cells, height_cells * width_cells), jnp.bfloat16)
    classified = lax.fori_loop(0, depth_cells, one_layer, start_cells)
    return classified.reshape(4, depth_cells, height_cells, width_cells)


def general_device(density, bin_index, tf_colour, tf_extinction, slab_rank):
    slab_count = lax.axis_size("bz")
    depth_cells, height_cells, width_cells = density.shape
    total_depth = float(depth_cells * slab_count)
    colour_cells = classify(density, bin_index, tf_colour, tf_extinction, total_depth)
    padded = with_halo(colour_cells, (("bz", 1), ("by", 2), ("bx", 3)), 1)
    along_x = jnp.einsum(
        "czyq,pq->czyp", padded, resample_table(width_cells), preferred_element_type=jnp.float32
    ).astype(jnp.bfloat16)
    y_table = resample_table(height_cells)

    def add_sample(sample_index, image_now):
        centre = sample_index // 2
        parity = sample_index % 2
        layers = lax.dynamic_slice_in_dim(along_x, centre, 3, 1).astype(jnp.float32)
        lower_weight = jnp.where(parity == 0, 0.25, 0.0)
        upper_weight = jnp.where(parity == 1, 0.25, 0.0)
        mixed_layer = (
            lower_weight * layers[:, 0] + 0.75 * layers[:, 1] + upper_weight * layers[:, 2]
        ).astype(jnp.bfloat16)
        sample = jnp.einsum("qy,cyp->cqp", y_table, mixed_layer, preferred_element_type=jnp.float32)
        return blend_over(image_now, sample)

    start_image = jnp.zeros((4, 2 * height_cells, 2 * width_cells), jnp.float32)
    slab_image = lax.fori_loop(0, 2 * depth_cells, add_sample, start_image)
    rows_piece = 2 * height_cells // slab_count
    my_index = lax.axis_index("bz")
    bit_levels = slab_count.bit_length() - 1
    composite = slab_image.reshape((4,) + (2,) * bit_levels + (rows_piece, 2 * width_cells))
    my_rank = lax.dynamic_index_in_dim(slab_rank, my_index, 0, keepdims=False)
    for level in range(bit_levels):
        position = bit_levels - level
        my_bit = my_index // 2**level % 2
        kept_half = lax.dynamic_index_in_dim(composite, my_bit, position, keepdims=False)
        outgoing = lax.dynamic_index_in_dim(composite, 1 - my_bit, position, keepdims=False)
        incoming = partner_2(outgoing, "bz", level)
        partner = my_index + (1 - 2 * my_bit) * 2**level
        partner_rank = lax.dynamic_index_in_dim(slab_rank, partner, 0, keepdims=False)
        mine_first = my_rank < partner_rank
        composite = blend_over(
            jnp.where(mine_first, kept_half, incoming), jnp.where(mine_first, incoming, kept_half)
        )
    return composite


LANES = 128
LEVELS = 65535.0
VMEM = pl.BlockSpec(memory_space=pltpu.VMEM)


def pack_words(density, bins):
    level = (density * LEVELS + 0.5).astype(jnp.int32)
    return lax.shift_left(level, 16) | bins


def unpack_words(words):
    density = lax.shift_right_logical(words, 16).astype(jnp.float32) * (1.0 / LEVELS)
    return density, words & 0xFFFF


def cell_values(density, bins, tables, depth):
    low_bits = bins & (LANES - 1)
    upper = bins >= LANES

    def pick(channel):
        first, second = tables[channel]
        return jnp.where(
            upper,
            jnp.take_along_axis(second, low_bits, axis=1, mode="promise_in_bounds"),
            jnp.take_along_axis(first, low_bits, axis=1, mode="promise_in_bounds"),
        )

    opacity = (1.0 - jnp.exp(-pick(3) * density / depth)) * (1.0 / 64.0)
    return [pick(0) * opacity, pick(1) * opacity, pick(2) * opacity, opacity]


def read_tables(tables_ref):
    return [[tables_ref[2 * channel + half] for half in range(2)] for channel in range(4)]


def cost(microseconds):
    return pl.CostEstimate(
        flops=int(1e9 * microseconds), bytes_accessed=int(3.6e6 * microseconds), transcendentals=0
    )


def stage_kernel(
    density_ref, bins_ref, colour_ref, extinction_ref,
    first_ref, second_ref, columns_ref, dense_ref, index_ref, tables_ref,
):
    layers, rows, cols = density_ref.shape
    front = lax.axis_index("bz") == 0
    row_at = lax.broadcasted_iota(jnp.int32, (rows, LANES), 0)
    lane_at = lax.broadcasted_iota(jnp.int32, (rows, LANES), 1)
    for z in range(layers):
        first = pack_words(density_ref[z, :, 0:1], bins_ref[z, :, 0:1])
        last = pack_words(density_ref[z, :, cols - 1 : cols], bins_ref[z, :, cols - 1 : cols])
        line = jnp.where(lane_at == row_at, first, 0) + jnp.where(lane_at == row_at + rows, last, 0)
        columns_ref[z : z + 1, :] = jnp.sum(line, axis=0, keepdims=True)
        top, bottom = [
            pack_words(density_ref[z, r : r + 1, :], bins_ref[z, r : r + 1, :]) for r in (0, rows - 1)
        ]
        first_ref[z : z + 1, :] = jnp.where(front, bottom, top)
        second_ref[z : z + 1, :] = jnp.where(front, top, bottom)
        for tile in range(cols // LANES):
            lanes = slice(tile * LANES, (tile + 1) * LANES)
            dense_ref[z, tile, 0:rows] = density_ref[z, :, lanes]
            index_ref[z, tile, 0:rows] = bins_ref[z, :, lanes]
    colour = colour_ref[...].astype(jnp.float32)
    extinction = extinction_ref[...].astype(jnp.float32).reshape(1, 2 * LANES)
    for channel in range(4):
        line = extinction if channel == 3 else colour[channel : channel + 1]
        for half in range(2):
            tables_ref[2 * channel + half] = jnp.broadcast_to(
                line[:, half * LANES : (half + 1) * LANES], (8, LANES)
            )


def pack_kernel(dense_ref, index_ref, columns_ref, bulk_ref, inside_ref):
    layers, tiles, rows = dense_ref.shape[0], dense_ref.shape[1], dense_ref.shape[2] - 8
    half = rows // 2
    front = lax.axis_index("bz") == 0
    start = jnp.where(front, half, 0)
    for tile in range(tiles):
        lanes = slice(tile * LANES, (tile + 1) * LANES)
        bulk_ref[2 * layers + 1, :, lanes] = columns_ref[...]
        for z in range(layers):
            for part in range(2):
                at = pl.ds(start + part, half // 2, stride=2)
                bulk_ref[2 * z + part, :, lanes] = pack_words(
                    dense_ref[z, tile, at, :], index_ref[z, tile, at, :]
                )
            line = [
                pack_words(dense_ref[z, tile, r : r + 1, :], index_ref[z, tile, r : r + 1, :])
                for r in (half - 1, half)
            ]
            bulk_ref[2 * layers, z : z + 1, lanes] = jnp.where(front, line[0], line[1])
            inside_ref[z : z + 1, lanes] = jnp.where(front, line[1], line[0])


def near_words(slab, first_ref, second_ref):
    me = lax.axis_index("bz")
    words = jnp.where(me == slab, first_ref[...], second_ref[...])
    return jnp.where(has_near(me == 0), words, 0)


def side_kernel(columns_ref, bulk_ref, second_ref, first_ref, along_ref, ends_ref):
    layers = columns_ref.shape[0]
    front = lax.axis_index("bz") == 0
    lane_at = lax.broadcasted_iota(jnp.int32, (layers, LANES), 1)
    for slab in range(2):
        mine = front if slab == 0 else jnp.logical_not(front)
        columns = jnp.where(mine, columns_ref[...], bulk_ref[2 * layers + 1, :, 0:LANES])
        near = near_words(slab, first_ref, second_ref)
        cols = near.shape[1]
        columns = jnp.where(lane_at == 64, near[:, 0:1], columns)
        ends_ref[slab] = jnp.where(lane_at == 65, near[:, cols - 1 : cols], columns)


def has_near(front):
    me_y = lax.axis_index("by")
    return jnp.where(front, me_y > 0, me_y + 1 < lax.axis_size("by"))


def fill_weights(weights_ref, rows):
    cols = weights_ref.shape[0] - LANES
    row = lax.broadcasted_iota(jnp.int32, (cols, 2 * cols), 0)
    at = lax.broadcasted_iota(jnp.int32, (cols, 2 * cols), 1)
    centre = lax.shift_right_logical(at, 1)
    beside = centre - 1 + 2 * (at & 1)
    weights_ref[0:cols, :] = jnp.where(
        row == centre, 3.0, jnp.where(row == beside, 1.0, 0.0)
    ).astype(jnp.bfloat16)
    row = lax.broadcasted_iota(jnp.int32, (LANES, 2 * LANES), 0)
    at = lax.broadcasted_iota(jnp.int32, (LANES, 2 * LANES), 1)
    right = ((row < rows) | (row == 64)) & (at == 2 * LANES - 1)
    left = (((row >= rows) & (row < 2 * rows)) | (row == 65)) & (at == 0)
    weights_ref[cols : cols + LANES, 0 : 2 * LANES] = jnp.where(right | left, 1.0, 0.0).astype(
        jnp.bfloat16
    )


def lane_maps(rows):
    lane_at = lax.broadcasted_iota(jnp.int32, (8, LANES), 1)
    sub_at = lax.broadcasted_iota(jnp.int32, (8, LANES), 0)
    return lane_at & (rows - 1), lane_at < 2 * rows, sub_at


def classify_rows(read_cells, tables, cells_ref, layers, tiles):
    total = float(2 * layers)
    for z in range(layers):
        for tile in range(tiles):
            even = cell_values(*read_cells(z, 0, tile), tables, total)
            odd = cell_values(*read_cells(z, 1, tile), tables, total)
            for channel in range(4):
                base = (z * 4 + channel) * 16
                block = jnp.concatenate([even[channel], odd[channel]], axis=0)
                cells_ref[base : base + 16, tile * LANES : (tile + 1) * LANES] = block.astype(jnp.bfloat16)


def rounded(value):
    return value.astype(jnp.bfloat16).astype(jnp.float32)


def cells_kernel(dense_ref, index_ref, tables_ref, cells_ref, weights_ref, mix_ref):
    layers, tiles, rows = dense_ref.shape[0], dense_ref.shape[1], dense_ref.shape[2] - 8
    half = rows // 2
    start = lax.axis_index("bz") * half
    fill_weights(weights_ref, rows)
    fill_rows(mix_ref)

    def read_cells(z, part, tile):
        at = pl.ds(start + part, half // 2, stride=2)
        return dense_ref[z, tile, at, :], index_ref[z, tile, at, :]

    classify_rows(read_cells, read_tables(tables_ref), cells_ref, layers, tiles)


def along_columns(cells, weights_ref, store):
    cols = cells.shape[1]
    tiles = 2 * cols // LANES
    result = jnp.dot(cells, weights_ref[0:cols, :], preferred_element_type=jnp.float32)
    for tile in range(tiles):
        block = result[:, tile * LANES : (tile + 1) * LANES]
        store(tile, block if tile in (0, tiles - 1) else rounded(block))


def own_kernel(cells_ref, weights_ref, along_ref):
    size = cells_ref.shape[0]
    pad = along_ref.shape[1] // 2 - size
    mine = pl.multiple_of(pad + lax.axis_index("bz") * size, pad)

    def store(tile, block):
        along_ref[tile, 0:pad, :] = jnp.zeros((pad, LANES), jnp.float32)
        along_ref[tile, pad + 2 * size :, :] = jnp.zeros((pad, LANES), jnp.float32)
        along_ref[tile, pl.ds(mine, size), :] = block

    along_columns(cells_ref[...], weights_ref, store)


def other_kernel(bulk_ref, tables_ref, weights_ref, ends_ref, own_ref, along_ref, cells_ref):
    layers = (bulk_ref.shape[0] - 2) // 2
    cols = bulk_ref.shape[2]
    size = cells_ref.shape[0]
    pad = along_ref.shape[1] // 2 - size
    theirs = pl.multiple_of(pad + (1 - lax.axis_index("bz")) * size, pad)

    def read_cells(z, part, tile):
        return unpack_words(bulk_ref[2 * z + part, :, tile * LANES : (tile + 1) * LANES])

    def store(tile, block):
        along_ref[tile, pl.ds(theirs, size), :] = block

    classify_rows(read_cells, read_tables(tables_ref), cells_ref, layers, cols // LANES)
    along_columns(cells_ref[...], weights_ref, store)


def edge_lines(now, lines_ref, depth):
    triple = 3.0 * now
    empty = jnp.zeros((8, LANES), jnp.float32)
    for layer in range(depth):
        here = triple[layer * 8 : layer * 8 + 8]
        before = now[layer * 8 - 8 : layer * 8] if layer > 0 else empty
        after = now[layer * 8 + 8 : layer * 8 + 16] if layer + 1 < depth else empty
        for parity, beside in enumerate((before, after)):
            line = jnp.concatenate([beside + here, empty], axis=0)
            at = (layer * 2 + parity) * 16
            lines_ref[at : at + 16, :] = line.astype(jnp.bfloat16)


def render_pair(along_refs, lines_refs, rows_ref, flip, layers):
    def one_slab(position, image):
        slab = position ^ flip
        along_at = pl.ds(pl.multiple_of(slab * (layers * 64), 64), (layers + 2) * 64)
        lines_at = pl.ds(pl.multiple_of(slab * (layers * 32), 32), layers * 32)
        views = [ref.at[along_at, :] for ref in along_refs]
        lines = [ref.at[lines_at, :] for ref in lines_refs]

        def layer_rows(view, layer, channel):
            base = (layer * 4 + channel) * 16
            return view[base : base + 16, :]

        def both(pieces):
            return jnp.concatenate(pieces, axis=1)

        for z in range(layers):
            triple = [[3.0 * layer_rows(v, z + 1, channel) for v in views] for channel in range(4)]
            mixed = []
            for parity in range(2):
                for channel in range(4):
                    mixed.append(
                        both(
                            [
                                (layer_rows(v, z + 2 * parity, channel) + t).astype(jnp.bfloat16)
                                for v, t in zip(views, triple[channel])
                            ]
                        )
                    )
                at = (z * 2 + parity) * 16
                mixed.append(both([line[at : at + 16, :] for line in lines]))
            samples = jnp.dot(
                rows_ref[...], jnp.concatenate(mixed, axis=0), preferred_element_type=jnp.float32
            )
            for parity in range(2):
                clear = 1.0 - image[3]
                base = parity * 128
                image = [
                    image[channel] + clear * samples[base + channel * 32 : base + channel * 32 + 32]
                    for channel in range(4)
                ]
        return image

    return lax.fori_loop(0, 2, one_slab, [jnp.zeros((32, 2 * LANES), jnp.float32)] * 4)


def fill_rows(rows_ref):
    m = lax.broadcasted_iota(jnp.int32, rows_ref.shape, 0)
    k = lax.broadcasted_iota(jnp.int32, rows_ref.shape, 1)
    second = k >= 80
    k = jnp.where(second, k - 80, k)
    centre = lax.shift_right_logical(m & 31, 1)
    beside = centre - 1 + 2 * (m & 1)
    channel = lax.shift_right_logical(m, 5) & 3
    own = k < 64
    k_channel = jnp.where(own, lax.shift_right_logical(k, 4), k & 3)
    k_row = 2 * (k & 7) + (lax.shift_right_logical(k, 3) & 1)
    k_row = jnp.where(own, k_row, jnp.where(k < 68, -1, jnp.where(k < 72, 16, 99)))
    same = (k_channel == channel) & (second == (m >= 128))
    value = jnp.where(k_row == centre, 3.0, jnp.where(k_row == beside, 1.0, 0.0))
    rows_ref[...] = jnp.where(same, value, 0.0).astype(jnp.bfloat16)


def inner_kernel(
    rank_ref, tables_ref, weights_ref, bulk_ref, inside_ref, second_ref, first_ref, mix_ref, along_ref,
    image_ref, edge_ref, cells_ref, lines_ref,
):
    layers, cols = inside_ref.shape
    depth = 2 * layers
    tiles = 2 * cols // LANES
    me = lax.axis_index("bz")
    front = me == 0
    tables = read_tables(tables_ref)
    for slab in range(2):
        inside = jnp.where(me == slab, inside_ref[...], bulk_ref[2 * layers])
        near = near_words(slab, first_ref, second_ref)
        for side in range(2):
            use_near = front if side == 0 else jnp.logical_not(front)
            words = jnp.where(use_near, near, inside)
            for t in range(cols // LANES):
                values = cell_values(
                    *unpack_words(words[:, t * LANES : (t + 1) * LANES]), tables, float(depth)
                )
                for channel in range(4):
                    at = pl.ds(slab * layers * 8 + side * 4 + channel, layers, stride=8)
                    cells_ref[t, at, :] = values[channel]
    edge = sum(
        jnp.dot(
            cells_ref[t, 0 : 8 * depth].astype(jnp.bfloat16),
            weights_ref[t * LANES : (t + 1) * LANES, :],
            preferred_element_type=jnp.float32,
        )
        for t in range(cols // LANES)
    )
    for tile in range(tiles):
        now = edge[:, tile * LANES : (tile + 1) * LANES]
        if tile in (0, tiles - 1):
            edge_ref[0 if tile == 0 else 1] = now
        else:
            edge_lines(rounded(now), lines_ref.at[tile - 1], depth)

    image = render_pair(
        [along_ref.at[1], along_ref.at[2]], [lines_ref.at[0], lines_ref.at[1]], mix_ref, rank_ref[0], layers
    )
    for channel in range(4):
        image_ref[channel] = image[channel]


def outer_kernel(
    rank_ref, tables_ref, weights_ref, beside_ref, across_ref, mix_ref, along_ref, edge_ref, image_ref,
    out_ref, ends_ref, values_ref, keep_ref, fixed_ref, lines_ref,
):
    rows = out_ref.shape[1]
    cols = out_ref.shape[2] // 2
    layers = beside_ref.shape[1]
    depth = 2 * layers
    tiles = 2 * cols // LANES
    pad = 64
    size = layers * pad
    front = lax.axis_index("bz") == 0
    start = lax.axis_index("bz") * (rows // 2)
    me_x = lax.axis_index("bx")
    even_x = lax.rem(me_x, 2) == 0
    tables = read_tables(tables_ref)
    side_lane, has_side, sub_at = lane_maps(rows)
    masks = [has_side & (side_lane == start + 2 * sub_at + part) for part in range(2)]
    lane_at = lax.broadcasted_iota(jnp.int32, (layers, LANES), 1)
    is_right = (lane_at < rows) | (lane_at == 64)
    for slab in range(2):
        right = jnp.where(even_x, beside_ref[slab], across_ref[slab])
        left = jnp.where(even_x, across_ref[slab], beside_ref[slab])
        right = jnp.where(me_x + 1 < lax.axis_size("bx"), right, 0)
        left = jnp.where(me_x > 0, left, 0)
        words = jnp.where(is_right, right, left)
        values = cell_values(*unpack_words(words), tables, float(depth))
        for channel in range(4):
            values_ref[slab * 4 + channel, 0:layers] = values[channel]
        for z in range(layers):
            for channel in range(4):
                line = values_ref[slab * 4 + channel, pl.ds(z, 8, stride=0), :]
                block = jnp.concatenate([jnp.where(mask, line, 0.0) for mask in masks], axis=0)
                at = slab * size + (z * 4 + channel) * 16
                ends_ref[at : at + 16, :] = block.astype(jnp.bfloat16)
        for side in range(2):
            row = jnp.where(front, 64, rows // 2 - 1) if side == 0 else jnp.where(front, rows // 2, 64)
            twin = jnp.where(row == 64, 65, row + rows)
            keep = (lane_at == row) | (lane_at == twin)
            for channel in range(4):
                at = pl.ds(slab * layers * 8 + side * 4 + channel, layers, stride=8)
                keep_ref[at, :] = jnp.where(keep, values[channel], 0.0)
    ends_ref[2 * size :, :] = keep_ref[0 : 8 * depth].astype(jnp.bfloat16)
    added = jnp.dot(
        ends_ref[...], weights_ref[cols : cols + LANES, 0 : 2 * LANES], preferred_element_type=jnp.float32
    )
    for index, tile in enumerate((0, tiles - 1)):
        block = added[:, index * LANES : (index + 1) * LANES]
        fixed_ref[index, 0:pad, :] = jnp.zeros((pad, LANES), jnp.float32)
        fixed_ref[index, pad + 2 * size :, :] = jnp.zeros((pad, LANES), jnp.float32)
        fixed_ref[index, pad : pad + 2 * size, :] = rounded(
            along_ref[tile, pad : pad + 2 * size, :] + block[0 : 2 * size]
        )
        edge_lines(rounded(edge_ref[index] + block[2 * size :]), lines_ref.at[index], depth)
    out_ref[:, :, LANES : 2 * cols - LANES] = image_ref[...]

    image = render_pair(
        [fixed_ref.at[0], fixed_ref.at[1]], [lines_ref.at[0], lines_ref.at[1]], mix_ref, rank_ref[0], layers
    )
    for channel in range(4):
        out_ref[channel, :, 0:LANES] = image[channel][:, 0:LANES]
        out_ref[channel, :, 2 * cols - LANES : 2 * cols] = image[channel][:, LANES : 2 * LANES]


def two_slab_device(density, bin_index, tf_colour, tf_extinction, slab_rank):
    layers, rows, cols = density.shape
    half = rows // 2
    tiles = 2 * cols // LANES
    size = layers * 4 * half
    count_y, count_x = lax.axis_size("by"), lax.axis_size("bx")
    f32, bf16, i32 = jnp.float32, jnp.bfloat16, jnp.int32

    def call(kernel, name, out_shape, time, scratch_shapes=(), in_specs=None, aliases={}):
        def run(*operands):
            return pl.pallas_call(
                kernel,
                out_shape=out_shape,
                in_specs=in_specs or [VMEM] * len(operands),
                out_specs=(VMEM,) * len(out_shape) if isinstance(out_shape, tuple) else VMEM,
                scratch_shapes=scratch_shapes,
                input_output_aliases=aliases,
                compiler_params=pltpu.CompilerParams(vmem_limit_bytes=16 * 1024 * 1024),
                cost_estimate=cost(time),
                name=name,
            )(*operands)

        return run

    def both(route):
        return route + [(target, source) for source, target in route]

    blocks = (layers, cols // LANES, rows + 8, LANES)
    row = pltpu.VMEM((layers, cols), i32)
    first, second, columns, dense, index, tables = call(
        stage_kernel,
        "stage_block",
        (
            row,
            row,
            pltpu.VMEM((layers, LANES), i32),
            pltpu.VMEM(blocks, f32),
            pltpu.VMEM(blocks, i32),
            pltpu.VMEM((8, 8, LANES), f32),
        ),
        1.2,
    )(*[pltpu.with_memory_space_constraint(x, pltpu.HBM) for x in (density, bin_index, tf_colour, tf_extinction)])
    bulk, inside = call(
        pack_kernel, "pack_block", (pltpu.VMEM((2 * layers + 2, 8, cols), i32), row), 0.1
    )(dense, index, columns)

    def place(z, y, x):
        return (z * count_y + y) * count_x + x

    steps = range(count_y - 1)
    ring = [(place(0, y, 0), place(0, y + 1, 0)) for y in steps]
    ring += [(place(1, y + 1, 0), place(1, y, 0)) for y in steps]
    ring += [(place(0, count_y - 1, 0), place(1, count_y - 1, 0)), (place(1, 0, 0), place(0, 0, 0))]
    ring = [(source + x, target + x) for source, target in ring for x in range(count_x)]
    diagonal = [(place(1, y, x), place(0, y + 1, x)) for y in steps for x in range(count_x)]
    for z, y in ((0, 0), (1, count_y - 1)):
        diagonal += [(place(z, y, x), place(z, y, x + 1)) for x in range(0, count_x, 2)]
    axes = ("bz", "by", "bx")
    bulk = lax.ppermute(bulk, "bz", [(0, 1), (1, 0)])
    first = lax.ppermute(first, axes, ring)
    second = lax.ppermute(second, axes, both(diagonal))

    cells, weights, mix = call(
        cells_kernel,
        "own_cells",
        (
            pltpu.VMEM((size, cols), bf16),
            pltpu.VMEM((cols + LANES, 2 * cols), bf16),
            pltpu.VMEM((256, 160), bf16),
        ),
        0.5,
    )(dense, index, tables)
    whole = pltpu.VMEM((tiles, 2 * size + 2 * 4 * half, LANES), f32)
    along = call(own_kernel, "own_slab", whole, 0.4)(cells, weights)
    ends = call(side_kernel, "side_columns", pltpu.VMEM((2, layers, LANES), i32), 0.1)(
        columns, bulk, second, first, along
    )
    pairs = [(x, x + 1) for x in range(0, count_x, 2)]
    cross = [(x, (x + 1) % count_x) for x in range(1, count_x, 2)]
    beside = lax.ppermute(ends, "bx", both(pairs))
    across = lax.ppermute(ends, "bx", both(cross))
    along = call(other_kernel, "other_slab", whole, 0.8, [pltpu.VMEM((size, cols), bf16)], aliases={4: 0})(
        bulk, tables, weights, ends, along
    )
    smem = pl.BlockSpec(memory_space=pltpu.SMEM)
    lines = pltpu.VMEM((2, 64 * layers, LANES), bf16)
    image, edge = call(
        inner_kernel,
        "inner_tiles",
        (pltpu.VMEM((4, rows, (tiles - 2) * LANES), f32), pltpu.VMEM((2, 16 * layers, LANES), f32)),
        2.0,
        [pltpu.VMEM((cols // LANES, 16 * layers + 8, LANES), f32), lines],
        [smem] + [VMEM] * 8,
    )(slab_rank, tables, weights, bulk, inside, second, first, mix, along)
    return call(
        outer_kernel,
        "outer_tiles",
        jax.ShapeDtypeStruct((4, rows, 2 * cols), f32),
        2.0,
        [
            pltpu.VMEM((2 * size + 16 * layers, LANES), bf16),
            pltpu.VMEM((8, 2 * layers, LANES), f32),
            pltpu.VMEM((16 * layers + 8, LANES), f32),
            pltpu.VMEM((2, 2 * size + 2 * 4 * half, LANES), f32),
            lines,
        ],
        [smem] + [VMEM] * 8,
    )(slab_rank, tables, weights, beside, across, mix, along, edge, image)


def on_device(density, bin_index, tf_colour, tf_extinction, slab_rank):
    if lax.axis_size("bz") == 2:
        return two_slab_device(density, bin_index, tf_colour, tf_extinction, slab_rank)
    return general_device(density, bin_index, tf_colour, tf_extinction, slab_rank)


def solution(mesh):
    return jax.shard_map(
        on_device,
        mesh=mesh,
        in_specs=(P("bz", "by", "bx"), P("bz", "by", "bx"), P(), P(), P()),
        out_specs=P(None, ("by", "bz"), "bx"),
        check_vma=False,
    )
```

```python
import jax
import jax.numpy as jnp
from jax import lax
from jax.experimental import pallas as pl
from jax.experimental.pallas import tpu as pltpu
from jax.sharding import PartitionSpec as P


def with_halo(block, sides, width):
    for axis, dim in sides:
        count = lax.axis_size(axis)
        forward = [(i, i + 1) for i in range(count - 1)]
        backward = [(target, source) for source, target in forward]
        low = lax.ppermute(
            lax.slice_in_dim(block, block.shape[dim] - width, None, axis=dim), axis, forward
        )
        high = lax.ppermute(lax.slice_in_dim(block, 0, width, axis=dim), axis, backward)
        block = jnp.concatenate([low, block, high], axis=dim)
    return block


def partner_2(block, axis, stride):
    count = lax.axis_size(axis)
    route = []
    for low in range(count):
        high = low | 1 << stride
        if high != low and high < count:
            route += [(low, high), (high, low)]
    return lax.ppermute(block, axis, route)


def resample_table(length):
    row_index = lax.broadcasted_iota(jnp.int32, (2 * length, length + 2), 0)
    col_index = lax.broadcasted_iota(jnp.int32, (2 * length, length + 2), 1)
    centre = row_index // 2
    parity = row_index % 2
    weights_table = jnp.where(col_index == centre + 1, 0.75, 0.0)
    weights_table = weights_table + jnp.where((col_index == centre) & (parity == 0), 0.25, 0.0)
    weights_table = weights_table + jnp.where((col_index == centre + 2) & (parity == 1), 0.25, 0.0)
    return weights_table.astype(jnp.bfloat16)


def blend_over(in_front, behind):
    return in_front + (1.0 - in_front[3])[None] * behind


def classify(density, bin_index, tf_colour, tf_extinction, total_depth):
    depth_cells, height_cells, width_cells = density.shape
    lookup = jnp.concatenate([tf_colour, tf_extinction[None, :]], axis=0)
    table_size = lookup.shape[1]
    bin_rows = lax.broadcasted_iota(jnp.int32, (table_size, 1), 0)
    flat_bins = bin_index.reshape(depth_cells, height_cells * width_cells)
    flat_density = density.reshape(depth_cells, height_cells * width_cells)

    def one_layer(layer, result):
        layer_bins = lax.dynamic_index_in_dim(flat_bins, layer, 0, keepdims=True)
        layer_density = lax.dynamic_index_in_dim(flat_density, layer, 0, keepdims=False)
        one_hot = (layer_bins == bin_rows).astype(jnp.bfloat16)
        values = jnp.dot(lookup, one_hot, preferred_element_type=jnp.float32)
        opacity = 1.0 - jnp.exp(-values[3] * layer_density / total_depth)
        cells = jnp.concatenate([values[:3] * opacity[None], opacity[None]], axis=0).astype(
            jnp.bfloat16
        )
        return lax.dynamic_update_slice_in_dim(result, cells[:, None], layer, 1)

    start_cells = jnp.zeros((4, depth_cells, height_cells * width_cells), jnp.bfloat16)
    classified = lax.fori_loop(0, depth_cells, one_layer, start_cells)
    return classified.reshape(4, depth_cells, height_cells, width_cells)


def general_device(density, bin_index, tf_colour, tf_extinction, slab_rank):
    slab_count = lax.axis_size("bz")
    depth_cells, height_cells, width_cells = density.shape
    total_depth = float(depth_cells * slab_count)
    colour_cells = classify(density, bin_index, tf_colour, tf_extinction, total_depth)
    padded = with_halo(colour_cells, (("bz", 1), ("by", 2), ("bx", 3)), 1)
    along_x = jnp.einsum(
        "czyq,pq->czyp", padded, resample_table(width_cells), preferred_element_type=jnp.float32
    ).astype(jnp.bfloat16)
    y_table = resample_table(height_cells)

    def add_sample(sample_index, image_now):
        centre = sample_index // 2
        parity = sample_index % 2
        layers = lax.dynamic_slice_in_dim(along_x, centre, 3, 1).astype(jnp.float32)
        lower_weight = jnp.where(parity == 0, 0.25, 0.0)
        upper_weight = jnp.where(parity == 1, 0.25, 0.0)
        mixed_layer = (
            lower_weight * layers[:, 0] + 0.75 * layers[:, 1] + upper_weight * layers[:, 2]
        ).astype(jnp.bfloat16)
        sample = jnp.einsum("qy,cyp->cqp", y_table, mixed_layer, preferred_element_type=jnp.float32)
        return blend_over(image_now, sample)

    start_image = jnp.zeros((4, 2 * height_cells, 2 * width_cells), jnp.float32)
    slab_image = lax.fori_loop(0, 2 * depth_cells, add_sample, start_image)
    rows_piece = 2 * height_cells // slab_count
    my_index = lax.axis_index("bz")
    bit_levels = slab_count.bit_length() - 1
    composite = slab_image.reshape((4,) + (2,) * bit_levels + (rows_piece, 2 * width_cells))
    my_rank = lax.dynamic_index_in_dim(slab_rank, my_index, 0, keepdims=False)
    for level in range(bit_levels):
        position = bit_levels - level
        my_bit = my_index // 2**level % 2
        kept_half = lax.dynamic_index_in_dim(composite, my_bit, position, keepdims=False)
        outgoing = lax.dynamic_index_in_dim(composite, 1 - my_bit, position, keepdims=False)
        incoming = partner_2(outgoing, "bz", level)
        partner = my_index + (1 - 2 * my_bit) * 2**level
        partner_rank = lax.dynamic_index_in_dim(slab_rank, partner, 0, keepdims=False)
        mine_first = my_rank < partner_rank
        composite = blend_over(
            jnp.where(mine_first, kept_half, incoming), jnp.where(mine_first, incoming, kept_half)
        )
    return composite


LANES = 128
LEVELS = 65535.0
VMEM = pl.BlockSpec(memory_space=pltpu.VMEM)


def pack_words(density, bins):
    level = (density * LEVELS + 0.5).astype(jnp.int32)
    return lax.shift_left(level, 16) | bins


def unpack_words(words):
    density = lax.shift_right_logical(words, 16).astype(jnp.float32) * (1.0 / LEVELS)
    return density, words & 0xFFFF


def cell_values(density, bins, tables, depth):
    low_bits = bins & (LANES - 1)
    upper = bins >= LANES

    def pick(channel):
        first, second = tables[channel]
        return jnp.where(
            upper,
            jnp.take_along_axis(second, low_bits, axis=1, mode="promise_in_bounds"),
            jnp.take_along_axis(first, low_bits, axis=1, mode="promise_in_bounds"),
        )

    opacity = (1.0 - jnp.exp(-pick(3) * density / depth)) * (1.0 / 64.0)
    return [pick(0) * opacity, pick(1) * opacity, pick(2) * opacity, opacity]


def read_tables(tables_ref):
    return [[tables_ref[2 * channel + half] for half in range(2)] for channel in range(4)]


def cost(microseconds):
    return pl.CostEstimate(
        flops=int(1e9 * microseconds), bytes_accessed=int(3.6e6 * microseconds), transcendentals=0
    )


def stage_kernel(
    density_ref, bins_ref, colour_ref, extinction_ref,
    first_ref, second_ref, columns_ref, dense_ref, index_ref, tables_ref,
):
    layers, rows, cols = density_ref.shape
    front = lax.axis_index("bz") == 0
    row_at = lax.broadcasted_iota(jnp.int32, (rows, LANES), 0)
    lane_at = lax.broadcasted_iota(jnp.int32, (rows, LANES), 1)
    for z in range(layers):
        first = pack_words(density_ref[z, :, 0:1], bins_ref[z, :, 0:1])
        last = pack_words(density_ref[z, :, cols - 1 : cols], bins_ref[z, :, cols - 1 : cols])
        line = jnp.where(lane_at == row_at, first, 0) + jnp.where(lane_at == row_at + rows, last, 0)
        columns_ref[z : z + 1, :] = jnp.sum(line, axis=0, keepdims=True)
        top, bottom = [
            pack_words(density_ref[z, r : r + 1, :], bins_ref[z, r : r + 1, :]) for r in (0, rows - 1)
        ]
        first_ref[z : z + 1, :] = jnp.where(front, bottom, top)
        second_ref[z : z + 1, :] = jnp.where(front, top, bottom)
        for tile in range(cols // LANES):
            lanes = slice(tile * LANES, (tile + 1) * LANES)
            dense_ref[z, tile, 0:rows] = density_ref[z, :, lanes]
            index_ref[z, tile, 0:rows] = bins_ref[z, :, lanes]
    colour = colour_ref[...].astype(jnp.float32)
    extinction = extinction_ref[...].astype(jnp.float32).reshape(1, 2 * LANES)
    for channel in range(4):
        line = extinction if channel == 3 else colour[channel : channel + 1]
        for half in range(2):
            tables_ref[2 * channel + half] = jnp.broadcast_to(
                line[:, half * LANES : (half + 1) * LANES], (8, LANES)
            )


def pack_kernel(dense_ref, index_ref, columns_ref, bulk_ref, inside_ref):
    layers, tiles, rows = dense_ref.shape[0], dense_ref.shape[1], dense_ref.shape[2] - 8
    half = rows // 2
    front = lax.axis_index("bz") == 0
    start = jnp.where(front, half, 0)
    for tile in range(tiles):
        lanes = slice(tile * LANES, (tile + 1) * LANES)
        bulk_ref[2 * layers + 1, :, lanes] = columns_ref[...]
        for z in range(layers):
            for part in range(2):
                at = pl.ds(start + part, half // 2, stride=2)
                bulk_ref[2 * z + part, :, lanes] = pack_words(
                    dense_ref[z, tile, at, :], index_ref[z, tile, at, :]
                )
            line = [
                pack_words(dense_ref[z, tile, r : r + 1, :], index_ref[z, tile, r : r + 1, :])
                for r in (half - 1, half)
            ]
            bulk_ref[2 * layers, z : z + 1, lanes] = jnp.where(front, line[0], line[1])
            inside_ref[z : z + 1, lanes] = jnp.where(front, line[1], line[0])


def near_words(slab, first_ref, second_ref):
    me = lax.axis_index("bz")
    words = jnp.where(me == slab, first_ref[...], second_ref[...])
    return jnp.where(has_near(me == 0), words, 0)


def side_kernel(columns_ref, bulk_ref, second_ref, first_ref, along_ref, ends_ref):
    layers = columns_ref.shape[0]
    front = lax.axis_index("bz") == 0
    lane_at = lax.broadcasted_iota(jnp.int32, (layers, LANES), 1)
    for slab in range(2):
        mine = front if slab == 0 else jnp.logical_not(front)
        columns = jnp.where(mine, columns_ref[...], bulk_ref[2 * layers + 1, :, 0:LANES])
        near = near_words(slab, first_ref, second_ref)
        cols = near.shape[1]
        columns = jnp.where(lane_at == 64, near[:, 0:1], columns)
        ends_ref[slab] = jnp.where(lane_at == 65, near[:, cols - 1 : cols], columns)


def has_near(front):
    me_y = lax.axis_index("by")
    return jnp.where(front, me_y > 0, me_y + 1 < lax.axis_size("by"))


def fill_weights(weights_ref, rows):
    cols = weights_ref.shape[0] - LANES
    row = lax.broadcasted_iota(jnp.int32, (cols, 2 * cols), 0)
    at = lax.broadcasted_iota(jnp.int32, (cols, 2 * cols), 1)
    centre = lax.shift_right_logical(at, 1)
    beside = centre - 1 + 2 * (at & 1)
    weights_ref[0:cols, :] = jnp.where(
        row == centre, 3.0, jnp.where(row == beside, 1.0, 0.0)
    ).astype(jnp.bfloat16)
    row = lax.broadcasted_iota(jnp.int32, (LANES, 2 * LANES), 0)
    at = lax.broadcasted_iota(jnp.int32, (LANES, 2 * LANES), 1)
    right = ((row < rows) | (row == 64)) & (at == 2 * LANES - 1)
    left = (((row >= rows) & (row < 2 * rows)) | (row == 65)) & (at == 0)
    weights_ref[cols : cols + LANES, 0 : 2 * LANES] = jnp.where(right | left, 1.0, 0.0).astype(
        jnp.bfloat16
    )


def lane_maps(rows):
    lane_at = lax.broadcasted_iota(jnp.int32, (8, LANES), 1)
    sub_at = lax.broadcasted_iota(jnp.int32, (8, LANES), 0)
    return lane_at & (rows - 1), lane_at < 2 * rows, sub_at


def classify_rows(read_cells, tables, cells_ref, layers, tiles):
    total = float(2 * layers)
    for z in range(layers):
        for tile in range(tiles):
            even = cell_values(*read_cells(z, 0, tile), tables, total)
            odd = cell_values(*read_cells(z, 1, tile), tables, total)
            for channel in range(4):
                base = (z * 4 + channel) * 16
                block = jnp.concatenate([even[channel], odd[channel]], axis=0)
                cells_ref[base : base + 16, tile * LANES : (tile + 1) * LANES] = block.astype(jnp.bfloat16)


def rounded(value):
    return value.astype(jnp.bfloat16).astype(jnp.float32)


def cells_kernel(dense_ref, index_ref, tables_ref, cells_ref, weights_ref, mix_ref):
    layers, tiles, rows = dense_ref.shape[0], dense_ref.shape[1], dense_ref.shape[2] - 8
    half = rows // 2
    start = lax.axis_index("bz") * half
    fill_weights(weights_ref, rows)
    fill_rows(mix_ref)

    def read_cells(z, part, tile):
        at = pl.ds(start + part, half // 2, stride=2)
        return dense_ref[z, tile, at, :], index_ref[z, tile, at, :]

    classify_rows(read_cells, read_tables(tables_ref), cells_ref, layers, tiles)


def along_columns(cells, weights_ref, store):
    cols = cells.shape[1]
    tiles = 2 * cols // LANES
    result = jnp.dot(cells, weights_ref[0:cols, :], preferred_element_type=jnp.float32)
    for tile in range(tiles):
        block = result[:, tile * LANES : (tile + 1) * LANES]
        store(tile, block if tile in (0, tiles - 1) else rounded(block))


def own_kernel(cells_ref, weights_ref, along_ref):
    size = cells_ref.shape[0]
    pad = along_ref.shape[1] // 2 - size
    mine = pl.multiple_of(pad + lax.axis_index("bz") * size, pad)

    def store(tile, block):
        along_ref[tile, 0:pad, :] = jnp.zeros((pad, LANES), jnp.float32)
        along_ref[tile, pad + 2 * size :, :] = jnp.zeros((pad, LANES), jnp.float32)
        along_ref[tile, pl.ds(mine, size), :] = block

    along_columns(cells_ref[...], weights_ref, store)


def other_kernel(bulk_ref, tables_ref, weights_ref, ends_ref, own_ref, along_ref, cells_ref):
    layers = (bulk_ref.shape[0] - 2) // 2
    cols = bulk_ref.shape[2]
    size = cells_ref.shape[0]
    pad = along_ref.shape[1] // 2 - size
    theirs = pl.multiple_of(pad + (1 - lax.axis_index("bz")) * size, pad)

    def read_cells(z, part, tile):
        return unpack_words(bulk_ref[2 * z + part, :, tile * LANES : (tile + 1) * LANES])

    def store(tile, block):
        along_ref[tile, pl.ds(theirs, size), :] = block

    classify_rows(read_cells, read_tables(tables_ref), cells_ref, layers, cols // LANES)
    along_columns(cells_ref[...], weights_ref, store)


def edge_lines(now, lines_ref, depth):
    triple = 3.0 * now
    empty = jnp.zeros((8, LANES), jnp.float32)
    for layer in range(depth):
        here = triple[layer * 8 : layer * 8 + 8]
        before = now[layer * 8 - 8 : layer * 8] if layer > 0 else empty
        after = now[layer * 8 + 8 : layer * 8 + 16] if layer + 1 < depth else empty
        for parity, beside in enumerate((before, after)):
            line = jnp.concatenate([beside + here, empty], axis=0)
            at = (layer * 2 + parity) * 16
            lines_ref[at : at + 16, :] = line.astype(jnp.bfloat16)


def render_pair(along_refs, lines_refs, rows_ref, flip, layers):
    def one_slab(position, image):
        slab = position ^ flip
        along_at = pl.ds(pl.multiple_of(slab * (layers * 64), 64), (layers + 2) * 64)
        lines_at = pl.ds(pl.multiple_of(slab * (layers * 32), 32), layers * 32)
        views = [ref.at[along_at, :] for ref in along_refs]
        lines = [ref.at[lines_at, :] for ref in lines_refs]

        def layer_rows(view, layer, channel):
            base = (layer * 4 + channel) * 16
            return view[base : base + 16, :]

        def both(pieces):
            return jnp.concatenate(pieces, axis=1)

        for z in range(layers):
            triple = [[3.0 * layer_rows(v, z + 1, channel) for v in views] for channel in range(4)]
            samples = []
            for parity in range(2):
                mixed = [
                    both(
                        [
                            (layer_rows(v, z + 2 * parity, channel) + t).astype(jnp.bfloat16)
                            for v, t in zip(views, triple[channel])
                        ]
                    )
                    for channel in range(4)
                ]
                at = (z * 2 + parity) * 16
                mixed.append(both([line[at : at + 16, :] for line in lines]))
                samples.append(
                    jnp.dot(
                        rows_ref[...],
                        jnp.concatenate(mixed, axis=0),
                        preferred_element_type=jnp.float32,
                    )
                )
            for sample in samples:
                clear = 1.0 - image[3]
                image = [
                    image[channel] + clear * sample[channel * 32 : channel * 32 + 32]
                    for channel in range(4)
                ]
        return image

    return lax.fori_loop(0, 2, one_slab, [jnp.zeros((32, 2 * LANES), jnp.float32)] * 4)


def fill_rows(rows_ref):
    m = lax.broadcasted_iota(jnp.int32, rows_ref.shape, 0)
    k = lax.broadcasted_iota(jnp.int32, rows_ref.shape, 1)
    centre = lax.shift_right_logical(m & 31, 1)
    beside = centre - 1 + 2 * (m & 1)
    own = k < 64
    k_channel = jnp.where(own, lax.shift_right_logical(k, 4), k & 3)
    k_row = 2 * (k & 7) + (lax.shift_right_logical(k, 3) & 1)
    k_row = jnp.where(own, k_row, jnp.where(k < 68, -1, jnp.where(k < 72, 16, 99)))
    same = k_channel == lax.shift_right_logical(m, 5)
    value = jnp.where(k_row == centre, 3.0, jnp.where(k_row == beside, 1.0, 0.0))
    rows_ref[...] = jnp.where(same, value, 0.0).astype(jnp.bfloat16)


def inner_kernel(
    rank_ref, tables_ref, weights_ref, bulk_ref, inside_ref, second_ref, first_ref, mix_ref, along_ref,
    image_ref, edge_ref, cells_ref, lines_ref,
):
    layers, cols = inside_ref.shape
    depth = 2 * layers
    tiles = 2 * cols // LANES
    me = lax.axis_index("bz")
    front = me == 0
    tables = read_tables(tables_ref)
    for slab in range(2):
        inside = jnp.where(me == slab, inside_ref[...], bulk_ref[2 * layers])
        near = near_words(slab, first_ref, second_ref)
        for side in range(2):
            use_near = front if side == 0 else jnp.logical_not(front)
            words = jnp.where(use_near, near, inside)
            for t in range(cols // LANES):
                values = cell_values(
                    *unpack_words(words[:, t * LANES : (t + 1) * LANES]), tables, float(depth)
                )
                for channel in range(4):
                    at = pl.ds(slab * layers * 8 + side * 4 + channel, layers, stride=8)
                    cells_ref[t, at, :] = values[channel]
    edge = sum(
        jnp.dot(
            cells_ref[t, 0 : 8 * depth].astype(jnp.bfloat16),
            weights_ref[t * LANES : (t + 1) * LANES, :],
            preferred_element_type=jnp.float32,
        )
        for t in range(cols // LANES)
    )
    for tile in range(tiles):
        now = edge[:, tile * LANES : (tile + 1) * LANES]
        if tile in (0, tiles - 1):
            edge_ref[0 if tile == 0 else 1] = now
        else:
            edge_lines(rounded(now), lines_ref.at[tile - 1], depth)

    image = render_pair(
        [along_ref.at[1], along_ref.at[2]], [lines_ref.at[0], lines_ref.at[1]], mix_ref, rank_ref[0], layers
    )
    for channel in range(4):
        image_ref[channel] = image[channel]


def outer_kernel(
    rank_ref, tables_ref, weights_ref, beside_ref, across_ref, mix_ref, along_ref, edge_ref, image_ref,
    out_ref, ends_ref, values_ref, keep_ref, fixed_ref, lines_ref,
):
    rows = out_ref.shape[1]
    cols = out_ref.shape[2] // 2
    layers = beside_ref.shape[1]
    depth = 2 * layers
    tiles = 2 * cols // LANES
    pad = 64
    size = layers * pad
    front = lax.axis_index("bz") == 0
    start = lax.axis_index("bz") * (rows // 2)
    me_x = lax.axis_index("bx")
    even_x = lax.rem(me_x, 2) == 0
    tables = read_tables(tables_ref)
    side_lane, has_side, sub_at = lane_maps(rows)
    masks = [has_side & (side_lane == start + 2 * sub_at + part) for part in range(2)]
    lane_at = lax.broadcasted_iota(jnp.int32, (layers, LANES), 1)
    is_right = (lane_at < rows) | (lane_at == 64)
    for slab in range(2):
        right = jnp.where(even_x, beside_ref[slab], across_ref[slab])
        left = jnp.where(even_x, across_ref[slab], beside_ref[slab])
        right = jnp.where(me_x + 1 < lax.axis_size("bx"), right, 0)
        left = jnp.where(me_x > 0, left, 0)
        words = jnp.where(is_right, right, left)
        values = cell_values(*unpack_words(words), tables, float(depth))
        for channel in range(4):
            values_ref[slab * 4 + channel, 0:layers] = values[channel]
        for z in range(layers):
            for channel in range(4):
                line = values_ref[slab * 4 + channel, pl.ds(z, 8, stride=0), :]
                block = jnp.concatenate([jnp.where(mask, line, 0.0) for mask in masks], axis=0)
                at = slab * size + (z * 4 + channel) * 16
                ends_ref[at : at + 16, :] = block.astype(jnp.bfloat16)
        for side in range(2):
            row = jnp.where(front, 64, rows // 2 - 1) if side == 0 else jnp.where(front, rows // 2, 64)
            twin = jnp.where(row == 64, 65, row + rows)
            keep = (lane_at == row) | (lane_at == twin)
            for channel in range(4):
                at = pl.ds(slab * layers * 8 + side * 4 + channel, layers, stride=8)
                keep_ref[at, :] = jnp.where(keep, values[channel], 0.0)
    ends_ref[2 * size :, :] = keep_ref[0 : 8 * depth].astype(jnp.bfloat16)
    added = jnp.dot(
        ends_ref[...], weights_ref[cols : cols + LANES, 0 : 2 * LANES], preferred_element_type=jnp.float32
    )
    for index, tile in enumerate((0, tiles - 1)):
        block = added[:, index * LANES : (index + 1) * LANES]
        fixed_ref[index, 0:pad, :] = jnp.zeros((pad, LANES), jnp.float32)
        fixed_ref[index, pad + 2 * size :, :] = jnp.zeros((pad, LANES), jnp.float32)
        fixed_ref[index, pad : pad + 2 * size, :] = rounded(
            along_ref[tile, pad : pad + 2 * size, :] + block[0 : 2 * size]
        )
        edge_lines(rounded(edge_ref[index] + block[2 * size :]), lines_ref.at[index], depth)
    out_ref[:, :, LANES : 2 * cols - LANES] = image_ref[...]

    image = render_pair(
        [fixed_ref.at[0], fixed_ref.at[1]], [lines_ref.at[0], lines_ref.at[1]], mix_ref, rank_ref[0], layers
    )
    for channel in range(4):
        out_ref[channel, :, 0:LANES] = image[channel][:, 0:LANES]
        out_ref[channel, :, 2 * cols - LANES : 2 * cols] = image[channel][:, LANES : 2 * LANES]


def two_slab_device(density, bin_index, tf_colour, tf_extinction, slab_rank):
    layers, rows, cols = density.shape
    half = rows // 2
    tiles = 2 * cols // LANES
    size = layers * 4 * half
    count_y, count_x = lax.axis_size("by"), lax.axis_size("bx")
    f32, bf16, i32 = jnp.float32, jnp.bfloat16, jnp.int32

    def call(kernel, name, out_shape, time, scratch_shapes=(), in_specs=None, aliases={}):
        def run(*operands):
            return pl.pallas_call(
                kernel,
                out_shape=out_shape,
                in_specs=in_specs or [VMEM] * len(operands),
                out_specs=(VMEM,) * len(out_shape) if isinstance(out_shape, tuple) else VMEM,
                scratch_shapes=scratch_shapes,
                input_output_aliases=aliases,
                compiler_params=pltpu.CompilerParams(vmem_limit_bytes=16 * 1024 * 1024),
                cost_estimate=cost(time),
                name=name,
            )(*operands)

        return run

    def both(route):
        return route + [(target, source) for source, target in route]

    blocks = (layers, cols // LANES, rows + 8, LANES)
    row = pltpu.VMEM((layers, cols), i32)
    first, second, columns, dense, index, tables = call(
        stage_kernel,
        "stage_block",
        (
            row,
            row,
            pltpu.VMEM((layers, LANES), i32),
            pltpu.VMEM(blocks, f32),
            pltpu.VMEM(blocks, i32),
            pltpu.VMEM((8, 8, LANES), f32),
        ),
        1.2,
    )(*[pltpu.with_memory_space_constraint(x, pltpu.HBM) for x in (density, bin_index, tf_colour, tf_extinction)])
    bulk, inside = call(
        pack_kernel, "pack_block", (pltpu.VMEM((2 * layers + 2, 8, cols), i32), row), 0.1
    )(dense, index, columns)

    def place(z, y, x):
        return (z * count_y + y) * count_x + x

    steps = range(count_y - 1)
    ring = [(place(0, y, 0), place(0, y + 1, 0)) for y in steps]
    ring += [(place(1, y + 1, 0), place(1, y, 0)) for y in steps]
    ring += [(place(0, count_y - 1, 0), place(1, count_y - 1, 0)), (place(1, 0, 0), place(0, 0, 0))]
    ring = [(source + x, target + x) for source, target in ring for x in range(count_x)]
    diagonal = [(place(1, y, x), place(0, y + 1, x)) for y in steps for x in range(count_x)]
    for z, y in ((0, 0), (1, count_y - 1)):
        diagonal += [(place(z, y, x), place(z, y, x + 1)) for x in range(0, count_x, 2)]
    axes = ("bz", "by", "bx")
    bulk = lax.ppermute(bulk, "bz", [(0, 1), (1, 0)])
    first = lax.ppermute(first, axes, ring)
    second = lax.ppermute(second, axes, both(diagonal))

    cells, weights, mix = call(
        cells_kernel,
        "own_cells",
        (
            pltpu.VMEM((size, cols), bf16),
            pltpu.VMEM((cols + LANES, 2 * cols), bf16),
            pltpu.VMEM((128, 80), bf16),
        ),
        0.5,
    )(dense, index, tables)
    whole = pltpu.VMEM((tiles, 2 * size + 2 * 4 * half, LANES), f32)
    along = call(own_kernel, "own_slab", whole, 0.4)(cells, weights)
    ends = call(side_kernel, "side_columns", pltpu.VMEM((2, layers, LANES), i32), 0.1)(
        columns, bulk, second, first, along
    )
    pairs = [(x, x + 1) for x in range(0, count_x, 2)]
    cross = [(x, (x + 1) % count_x) for x in range(1, count_x, 2)]
    beside = lax.ppermute(ends, "bx", both(pairs))
    across = lax.ppermute(ends, "bx", both(cross))
    along = call(other_kernel, "other_slab", whole, 0.8, [pltpu.VMEM((size, cols), bf16)], aliases={4: 0})(
        bulk, tables, weights, ends, along
    )
    smem = pl.BlockSpec(memory_space=pltpu.SMEM)
    lines = pltpu.VMEM((2, 64 * layers, LANES), bf16)
    image, edge = call(
        inner_kernel,
        "inner_tiles",
        (pltpu.VMEM((4, rows, (tiles - 2) * LANES), f32), pltpu.VMEM((2, 16 * layers, LANES), f32)),
        2.0,
        [pltpu.VMEM((cols // LANES, 16 * layers + 8, LANES), f32), lines],
        [smem] + [VMEM] * 8,
    )(slab_rank, tables, weights, bulk, inside, second, first, mix, along)
    return call(
        outer_kernel,
        "outer_tiles",
        jax.ShapeDtypeStruct((4, rows, 2 * cols), f32),
        2.0,
        [
            pltpu.VMEM((2 * size + 16 * layers, LANES), bf16),
            pltpu.VMEM((8, 2 * layers, LANES), f32),
            pltpu.VMEM((16 * layers + 8, LANES), f32),
            pltpu.VMEM((2, 2 * size + 2 * 4 * half, LANES), f32),
            lines,
        ],
        [smem] + [VMEM] * 8,
    )(slab_rank, tables, weights, beside, across, mix, along, edge, image)


def on_device(density, bin_index, tf_colour, tf_extinction, slab_rank):
    if lax.axis_size("bz") == 2:
        return two_slab_device(density, bin_index, tf_colour, tf_extinction, slab_rank)
    return general_device(density, bin_index, tf_colour, tf_extinction, slab_rank)


def solution(mesh):
    return jax.shard_map(
        on_device,
        mesh=mesh,
        in_specs=(P("bz", "by", "bx"), P("bz", "by", "bx"), P(), P(), P()),
        out_specs=P(None, ("by", "bz"), "bx"),
        check_vma=False,
    )
```

```python
import jax
import jax.numpy as jnp
from jax import lax
from jax.experimental import pallas as pl
from jax.experimental.pallas import tpu as pltpu
from jax.sharding import PartitionSpec as P


def with_halo(block, sides, width):
    for axis, dim in sides:
        count = lax.axis_size(axis)
        forward = [(i, i + 1) for i in range(count - 1)]
        backward = [(target, source) for source, target in forward]
        low = lax.ppermute(
            lax.slice_in_dim(block, block.shape[dim] - width, None, axis=dim), axis, forward
        )
        high = lax.ppermute(lax.slice_in_dim(block, 0, width, axis=dim), axis, backward)
        block = jnp.concatenate([low, block, high], axis=dim)
    return block


def partner_2(block, axis, stride):
    count = lax.axis_size(axis)
    route = []
    for low in range(count):
        high = low | 1 << stride
        if high != low and high < count:
            route += [(low, high), (high, low)]
    return lax.ppermute(block, axis, route)


def resample_table(length):
    row_index = lax.broadcasted_iota(jnp.int32, (2 * length, length + 2), 0)
    col_index = lax.broadcasted_iota(jnp.int32, (2 * length, length + 2), 1)
    centre = row_index // 2
    parity = row_index % 2
    weights_table = jnp.where(col_index == centre + 1, 0.75, 0.0)
    weights_table = weights_table + jnp.where((col_index == centre) & (parity == 0), 0.25, 0.0)
    weights_table = weights_table + jnp.where((col_index == centre + 2) & (parity == 1), 0.25, 0.0)
    return weights_table.astype(jnp.bfloat16)


def blend_over(in_front, behind):
    return in_front + (1.0 - in_front[3])[None] * behind


def classify(density, bin_index, tf_colour, tf_extinction, total_depth):
    depth_cells, height_cells, width_cells = density.shape
    lookup = jnp.concatenate([tf_colour, tf_extinction[None, :]], axis=0)
    table_size = lookup.shape[1]
    bin_rows = lax.broadcasted_iota(jnp.int32, (table_size, 1), 0)
    flat_bins = bin_index.reshape(depth_cells, height_cells * width_cells)
    flat_density = density.reshape(depth_cells, height_cells * width_cells)

    def one_layer(layer, result):
        layer_bins = lax.dynamic_index_in_dim(flat_bins, layer, 0, keepdims=True)
        layer_density = lax.dynamic_index_in_dim(flat_density, layer, 0, keepdims=False)
        one_hot = (layer_bins == bin_rows).astype(jnp.bfloat16)
        values = jnp.dot(lookup, one_hot, preferred_element_type=jnp.float32)
        opacity = 1.0 - jnp.exp(-values[3] * layer_density / total_depth)
        cells = jnp.concatenate([values[:3] * opacity[None], opacity[None]], axis=0).astype(
            jnp.bfloat16
        )
        return lax.dynamic_update_slice_in_dim(result, cells[:, None], layer, 1)

    start_cells = jnp.zeros((4, depth_cells, height_cells * width_cells), jnp.bfloat16)
    classified = lax.fori_loop(0, depth_cells, one_layer, start_cells)
    return classified.reshape(4, depth_cells, height_cells, width_cells)


def general_device(density, bin_index, tf_colour, tf_extinction, slab_rank):
    slab_count = lax.axis_size("bz")
    depth_cells, height_cells, width_cells = density.shape
    total_depth = float(depth_cells * slab_count)
    colour_cells = classify(density, bin_index, tf_colour, tf_extinction, total_depth)
    padded = with_halo(colour_cells, (("bz", 1), ("by", 2), ("bx", 3)), 1)
    along_x = jnp.einsum(
        "czyq,pq->czyp", padded, resample_table(width_cells), preferred_element_type=jnp.float32
    ).astype(jnp.bfloat16)
    y_table = resample_table(height_cells)

    def add_sample(sample_index, image_now):
        centre = sample_index // 2
        parity = sample_index % 2
        layers = lax.dynamic_slice_in_dim(along_x, centre, 3, 1).astype(jnp.float32)
        lower_weight = jnp.where(parity == 0, 0.25, 0.0)
        upper_weight = jnp.where(parity == 1, 0.25, 0.0)
        mixed_layer = (
            lower_weight * layers[:, 0] + 0.75 * layers[:, 1] + upper_weight * layers[:, 2]
        ).astype(jnp.bfloat16)
        sample = jnp.einsum("qy,cyp->cqp", y_table, mixed_layer, preferred_element_type=jnp.float32)
        return blend_over(image_now, sample)

    start_image = jnp.zeros((4, 2 * height_cells, 2 * width_cells), jnp.float32)
    slab_image = lax.fori_loop(0, 2 * depth_cells, add_sample, start_image)
    rows_piece = 2 * height_cells // slab_count
    my_index = lax.axis_index("bz")
    bit_levels = slab_count.bit_length() - 1
    composite = slab_image.reshape((4,) + (2,) * bit_levels + (rows_piece, 2 * width_cells))
    my_rank = lax.dynamic_index_in_dim(slab_rank, my_index, 0, keepdims=False)
    for level in range(bit_levels):
        position = bit_levels - level
        my_bit = my_index // 2**level % 2
        kept_half = lax.dynamic_index_in_dim(composite, my_bit, position, keepdims=False)
        outgoing = lax.dynamic_index_in_dim(composite, 1 - my_bit, position, keepdims=False)
        incoming = partner_2(outgoing, "bz", level)
        partner = my_index + (1 - 2 * my_bit) * 2**level
        partner_rank = lax.dynamic_index_in_dim(slab_rank, partner, 0, keepdims=False)
        mine_first = my_rank < partner_rank
        composite = blend_over(
            jnp.where(mine_first, kept_half, incoming), jnp.where(mine_first, incoming, kept_half)
        )
    return composite


LANES = 128
LEVELS = 65535.0
VMEM = pl.BlockSpec(memory_space=pltpu.VMEM)


def pack_words(density, bins):
    level = (density * LEVELS + 0.5).astype(jnp.int32)
    return lax.shift_left(level, 16) | bins


def unpack_words(words):
    density = lax.shift_right_logical(words, 16).astype(jnp.float32) * (1.0 / LEVELS)
    return density, words & 0xFFFF


def cell_values(density, bins, tables, depth):
    low_bits = bins & (LANES - 1)
    upper = bins >= LANES

    def pick(channel):
        first, second = tables[channel]
        return jnp.where(
            upper,
            jnp.take_along_axis(second, low_bits, axis=1, mode="promise_in_bounds"),
            jnp.take_along_axis(first, low_bits, axis=1, mode="promise_in_bounds"),
        )

    opacity = (1.0 - jnp.exp(-pick(3) * density / depth)) * (1.0 / 64.0)
    return [pick(0) * opacity, pick(1) * opacity, pick(2) * opacity, opacity]


def read_tables(tables_ref):
    return [[tables_ref[2 * channel + half] for half in range(2)] for channel in range(4)]


def cost(microseconds):
    return pl.CostEstimate(
        flops=int(1e9 * microseconds), bytes_accessed=int(3.6e6 * microseconds), transcendentals=0
    )


def stage_kernel(
    density_ref, bins_ref, colour_ref, extinction_ref,
    first_ref, second_ref, columns_ref, dense_ref, index_ref, tables_ref,
):
    layers, rows, cols = density_ref.shape
    front = lax.axis_index("bz") == 0
    row_at = lax.broadcasted_iota(jnp.int32, (rows, LANES), 0)
    lane_at = lax.broadcasted_iota(jnp.int32, (rows, LANES), 1)
    for z in range(layers):
        first = pack_words(density_ref[z, :, 0:1], bins_ref[z, :, 0:1])
        last = pack_words(density_ref[z, :, cols - 1 : cols], bins_ref[z, :, cols - 1 : cols])
        line = jnp.where(lane_at == row_at, first, 0) + jnp.where(lane_at == row_at + rows, last, 0)
        columns_ref[z : z + 1, :] = jnp.sum(line, axis=0, keepdims=True)
        top, bottom = [
            pack_words(density_ref[z, r : r + 1, :], bins_ref[z, r : r + 1, :]) for r in (0, rows - 1)
        ]
        first_ref[z : z + 1, :] = jnp.where(front, bottom, top)
        second_ref[z : z + 1, :] = jnp.where(front, top, bottom)
        for tile in range(cols // LANES):
            lanes = slice(tile * LANES, (tile + 1) * LANES)
            dense_ref[z, tile, 0:rows] = density_ref[z, :, lanes]
            index_ref[z, tile, 0:rows] = bins_ref[z, :, lanes]
    colour = colour_ref[...].astype(jnp.float32)
    extinction = extinction_ref[...].astype(jnp.float32).reshape(1, 2 * LANES)
    for channel in range(4):
        line = extinction if channel == 3 else colour[channel : channel + 1]
        for half in range(2):
            tables_ref[2 * channel + half] = jnp.broadcast_to(
                line[:, half * LANES : (half + 1) * LANES], (8, LANES)
            )


def pack_kernel(dense_ref, index_ref, columns_ref, bulk_ref, inside_ref):
    layers, tiles, rows = dense_ref.shape[0], dense_ref.shape[1], dense_ref.shape[2] - 8
    half = rows // 2
    front = lax.axis_index("bz") == 0
    start = jnp.where(front, half, 0)
    for tile in range(tiles):
        lanes = slice(tile * LANES, (tile + 1) * LANES)
        bulk_ref[2 * layers + 1, :, lanes] = columns_ref[...]
        for z in range(layers):
            for part in range(2):
                at = pl.ds(start + part, half // 2, stride=2)
                bulk_ref[2 * z + part, :, lanes] = pack_words(
                    dense_ref[z, tile, at, :], index_ref[z, tile, at, :]
                )
            line = [
                pack_words(dense_ref[z, tile, r : r + 1, :], index_ref[z, tile, r : r + 1, :])
                for r in (half - 1, half)
            ]
            bulk_ref[2 * layers, z : z + 1, lanes] = jnp.where(front, line[0], line[1])
            inside_ref[z : z + 1, lanes] = jnp.where(front, line[1], line[0])


def near_words(slab, first_ref, second_ref):
    me = lax.axis_index("bz")
    words = jnp.where(me == slab, first_ref[...], second_ref[...])
    return jnp.where(has_near(me == 0), words, 0)


def side_kernel(columns_ref, bulk_ref, second_ref, first_ref, along_ref, ends_ref):
    layers = columns_ref.shape[0]
    front = lax.axis_index("bz") == 0
    lane_at = lax.broadcasted_iota(jnp.int32, (layers, LANES), 1)
    for slab in range(2):
        mine = front if slab == 0 else jnp.logical_not(front)
        columns = jnp.where(mine, columns_ref[...], bulk_ref[2 * layers + 1, :, 0:LANES])
        near = near_words(slab, first_ref, second_ref)
        cols = near.shape[1]
        columns = jnp.where(lane_at == 64, near[:, 0:1], columns)
        ends_ref[slab] = jnp.where(lane_at == 65, near[:, cols - 1 : cols], columns)


def has_near(front):
    me_y = lax.axis_index("by")
    return jnp.where(front, me_y > 0, me_y + 1 < lax.axis_size("by"))


def fill_weights(weights_ref, rows):
    cols = weights_ref.shape[0] - LANES
    row = lax.broadcasted_iota(jnp.int32, (cols, 2 * cols), 0)
    at = lax.broadcasted_iota(jnp.int32, (cols, 2 * cols), 1)
    centre = lax.shift_right_logical(at, 1)
    beside = centre - 1 + 2 * (at & 1)
    weights_ref[0:cols, :] = jnp.where(
        row == centre, 3.0, jnp.where(row == beside, 1.0, 0.0)
    ).astype(jnp.bfloat16)
    row = lax.broadcasted_iota(jnp.int32, (LANES, 2 * LANES), 0)
    at = lax.broadcasted_iota(jnp.int32, (LANES, 2 * LANES), 1)
    right = ((row < rows) | (row == 64)) & (at == 2 * LANES - 1)
    left = (((row >= rows) & (row < 2 * rows)) | (row == 65)) & (at == 0)
    weights_ref[cols : cols + LANES, 0 : 2 * LANES] = jnp.where(right | left, 1.0, 0.0).astype(
        jnp.bfloat16
    )


def lane_maps(rows):
    lane_at = lax.broadcasted_iota(jnp.int32, (8, LANES), 1)
    sub_at = lax.broadcasted_iota(jnp.int32, (8, LANES), 0)
    return lane_at & (rows - 1), lane_at < 2 * rows, sub_at


def classify_rows(read_cells, tables, cells_ref, layers, tiles):
    total = float(2 * layers)
    for z in range(layers):
        for tile in range(tiles):
            even = cell_values(*read_cells(z, 0, tile), tables, total)
            odd = cell_values(*read_cells(z, 1, tile), tables, total)
            for channel in range(4):
                base = (z * 4 + channel) * 16
                block = jnp.concatenate([even[channel], odd[channel]], axis=0)
                cells_ref[base : base + 16, tile * LANES : (tile + 1) * LANES] = block.astype(jnp.bfloat16)


def rounded(value):
    return value.astype(jnp.bfloat16).astype(jnp.float32)


def cells_kernel(dense_ref, index_ref, tables_ref, cells_ref, weights_ref, mix_ref):
    layers, tiles, rows = dense_ref.shape[0], dense_ref.shape[1], dense_ref.shape[2] - 8
    half = rows // 2
    start = lax.axis_index("bz") * half
    fill_weights(weights_ref, rows)
    fill_rows(mix_ref)

    def read_cells(z, part, tile):
        at = pl.ds(start + part, half // 2, stride=2)
        return dense_ref[z, tile, at, :], index_ref[z, tile, at, :]

    classify_rows(read_cells, read_tables(tables_ref), cells_ref, layers, tiles)


def along_columns(cells, weights_ref, store):
    cols = cells.shape[1]
    tiles = 2 * cols // LANES
    result = jnp.dot(cells, weights_ref[0:cols, :], preferred_element_type=jnp.float32)
    for tile in range(tiles):
        block = result[:, tile * LANES : (tile + 1) * LANES]
        store(tile, block if tile in (0, tiles - 1) else rounded(block))


def own_kernel(cells_ref, weights_ref, along_ref):
    size = cells_ref.shape[0]
    pad = along_ref.shape[1] // 2 - size
    mine = pl.multiple_of(pad + lax.axis_index("bz") * size, pad)

    def store(tile, block):
        along_ref[tile, 0:pad, :] = jnp.zeros((pad, LANES), jnp.float32)
        along_ref[tile, pad + 2 * size :, :] = jnp.zeros((pad, LANES), jnp.float32)
        along_ref[tile, pl.ds(mine, size), :] = block

    along_columns(cells_ref[...], weights_ref, store)


def other_kernel(bulk_ref, tables_ref, weights_ref, ends_ref, own_ref, along_ref, cells_ref):
    layers = (bulk_ref.shape[0] - 2) // 2
    cols = bulk_ref.shape[2]
    size = cells_ref.shape[0]
    pad = along_ref.shape[1] // 2 - size
    theirs = pl.multiple_of(pad + (1 - lax.axis_index("bz")) * size, pad)

    def read_cells(z, part, tile):
        return unpack_words(bulk_ref[2 * z + part, :, tile * LANES : (tile + 1) * LANES])

    def store(tile, block):
        along_ref[tile, pl.ds(theirs, size), :] = block

    classify_rows(read_cells, read_tables(tables_ref), cells_ref, layers, cols // LANES)
    along_columns(cells_ref[...], weights_ref, store)


def edge_lines(now, packed_ref, lines_ref, depth):
    triple = 3.0 * now
    empty = jnp.zeros((8, LANES), jnp.float32)
    for layer in range(depth):
        at = layer * 8
        here = triple[at : at + 8]
        before = now[at - 8 : at] if layer > 0 else empty
        after = now[at + 8 : at + 16] if layer + 1 < depth else empty
        line = jnp.concatenate([before + here, empty], axis=0)
        packed_ref[2 * at : 2 * at + 16, :] = line.astype(jnp.bfloat16)
        lines_ref[at : at + 8, :] = rounded(after + here)


def render_pair(along_refs, packed_refs, lines_refs, rows_ref, flip, layers):
    sub_at = lax.broadcasted_iota(jnp.int32, (8, LANES), 0)
    top = sub_at == 0
    bottom = sub_at == 7

    def one_slab(position, image):
        slab = position ^ flip
        along_at = pl.ds(pl.multiple_of(slab * (layers * 64), 64), (layers + 2) * 64)
        packed_at = pl.ds(pl.multiple_of(slab * (layers * 16), 16), layers * 16)
        lines_at = pl.ds(pl.multiple_of(slab * (layers * 8), 8), layers * 8 + 8)
        views = [ref.at[along_at, :] for ref in along_refs]
        packed = [ref.at[packed_at, :] for ref in packed_refs]
        lines = [ref.at[lines_at, :] for ref in lines_refs]

        def layer_rows(view, layer, channel):
            base = (layer * 4 + channel) * 16
            return view[base : base + 16, :]

        def both(pieces):
            return jnp.concatenate(pieces, axis=1)

        def blend(image, samples):
            updated = []
            for tile in range(2):
                clear = [1.0 - value for value in image[tile][3]]
                updated.append(
                    [
                        [image[tile][c][i] + clear[i] * samples[tile][c][i] for i in range(4)]
                        for c in range(4)
                    ]
                )
            return updated

        for z in range(layers):
            triple = [[3.0 * layer_rows(v, z + 1, c) for c in range(4)] for v in views]
            mixed = [
                both(
                    [
                        (layer_rows(v, z, c) + t[c]).astype(jnp.bfloat16)
                        for v, t in zip(views, triple)
                    ]
                )
                for c in range(4)
            ]
            mixed.append(both([line[z * 16 : z * 16 + 16, :] for line in packed]))
            even = jnp.dot(
                rows_ref[...], jnp.concatenate(mixed, axis=0), preferred_element_type=jnp.float32
            )
            even = [
                [
                    [
                        even[c * 32 + i * 8 : c * 32 + i * 8 + 8, tile * LANES : (tile + 1) * LANES]
                        for i in range(4)
                    ]
                    for c in range(4)
                ]
                for tile in range(2)
            ]
            odd = []
            for tile in range(2):
                odd.append([])
                for c in range(4):
                    value = rounded(layer_rows(views[tile], z + 2, c) + triple[tile][c])
                    low, high = value[0:8], value[8:16]
                    above = lines[tile][pl.ds(z * 8 + c, 8, stride=0), :]
                    below = lines[tile][pl.ds(z * 8 + 4 + c, 8, stride=0), :]
                    before = jnp.where(top, above, pltpu.roll(high, 1, 0))
                    after = jnp.where(bottom, below, pltpu.roll(low, 7, 0))
                    low_centre = 3.0 * low
                    high_centre = 3.0 * high
                    odd[tile].append(
                        [before + low_centre, low_centre + high, low + high_centre, high_centre + after]
                    )
            image = blend(blend(image, even), odd)
        return image

    zero = jnp.zeros((8, LANES), jnp.float32)
    image = [[[zero] * 4 for _ in range(4)] for _ in range(2)]
    return lax.fori_loop(0, 2, one_slab, image)


def store_tile(image, mixed_ref, out_ref, lanes):
    for channel in range(4):
        for i in range(4):
            mixed_ref[channel, pl.ds(i, 8, stride=4), :] = image[channel][i]
        out_ref[channel, :, lanes] = mixed_ref[channel, 0:32]


def fill_rows(rows_ref):
    m = lax.broadcasted_iota(jnp.int32, rows_ref.shape, 0)
    k = lax.broadcasted_iota(jnp.int32, rows_ref.shape, 1)
    row = 4 * (m & 7) + (lax.shift_right_logical(m, 3) & 3)
    centre = lax.shift_right_logical(row, 1)
    beside = centre - 1 + 2 * (row & 1)
    own = k < 64
    k_channel = jnp.where(own, lax.shift_right_logical(k, 4), k & 3)
    k_row = 2 * (k & 7) + (lax.shift_right_logical(k, 3) & 1)
    k_row = jnp.where(own, k_row, jnp.where(k < 68, -1, jnp.where(k < 72, 16, 99)))
    same = k_channel == lax.shift_right_logical(m, 5)
    value = jnp.where(k_row == centre, 3.0, jnp.where(k_row == beside, 1.0, 0.0))
    rows_ref[...] = jnp.where(same, value, 0.0).astype(jnp.bfloat16)


def inner_kernel(
    rank_ref, tables_ref, weights_ref, bulk_ref, inside_ref, second_ref, first_ref, mix_ref, along_ref,
    image_ref, edge_ref, cells_ref, packed_ref, lines_ref, mixed_ref,
):
    layers, cols = inside_ref.shape
    depth = 2 * layers
    tiles = 2 * cols // LANES
    me = lax.axis_index("bz")
    front = me == 0
    tables = read_tables(tables_ref)
    for slab in range(2):
        inside = jnp.where(me == slab, inside_ref[...], bulk_ref[2 * layers])
        near = near_words(slab, first_ref, second_ref)
        for side in range(2):
            use_near = front if side == 0 else jnp.logical_not(front)
            words = jnp.where(use_near, near, inside)
            for t in range(cols // LANES):
                values = cell_values(
                    *unpack_words(words[:, t * LANES : (t + 1) * LANES]), tables, float(depth)
                )
                for channel in range(4):
                    at = pl.ds(slab * layers * 8 + side * 4 + channel, layers, stride=8)
                    cells_ref[t, at, :] = values[channel]
    edge = sum(
        jnp.dot(
            cells_ref[t, 0 : 8 * depth].astype(jnp.bfloat16),
            weights_ref[t * LANES : (t + 1) * LANES, :],
            preferred_element_type=jnp.float32,
        )
        for t in range(cols // LANES)
    )
    for tile in range(tiles):
        now = edge[:, tile * LANES : (tile + 1) * LANES]
        if tile in (0, tiles - 1):
            edge_ref[0 if tile == 0 else 1] = now
        else:
            edge_lines(rounded(now), packed_ref.at[tile - 1], lines_ref.at[tile - 1], depth)

    image = render_pair(
        [along_ref.at[1], along_ref.at[2]],
        [packed_ref.at[0], packed_ref.at[1]],
        [lines_ref.at[0], lines_ref.at[1]],
        mix_ref,
        rank_ref[0],
        layers,
    )
    for index in range(2):
        store_tile(image[index], mixed_ref, image_ref, slice(index * LANES, (index + 1) * LANES))


def outer_kernel(
    rank_ref, tables_ref, weights_ref, beside_ref, across_ref, mix_ref, along_ref, edge_ref, image_ref,
    out_ref, ends_ref, values_ref, keep_ref, fixed_ref, packed_ref, lines_ref, mixed_ref,
):
    rows = out_ref.shape[1]
    cols = out_ref.shape[2] // 2
    layers = beside_ref.shape[1]
    depth = 2 * layers
    tiles = 2 * cols // LANES
    pad = 64
    size = layers * pad
    front = lax.axis_index("bz") == 0
    start = lax.axis_index("bz") * (rows // 2)
    me_x = lax.axis_index("bx")
    even_x = lax.rem(me_x, 2) == 0
    tables = read_tables(tables_ref)
    side_lane, has_side, sub_at = lane_maps(rows)
    masks = [has_side & (side_lane == start + 2 * sub_at + part) for part in range(2)]
    lane_at = lax.broadcasted_iota(jnp.int32, (layers, LANES), 1)
    is_right = (lane_at < rows) | (lane_at == 64)
    for slab in range(2):
        right = jnp.where(even_x, beside_ref[slab], across_ref[slab])
        left = jnp.where(even_x, across_ref[slab], beside_ref[slab])
        right = jnp.where(me_x + 1 < lax.axis_size("bx"), right, 0)
        left = jnp.where(me_x > 0, left, 0)
        words = jnp.where(is_right, right, left)
        values = cell_values(*unpack_words(words), tables, float(depth))
        for channel in range(4):
            values_ref[slab * 4 + channel, 0:layers] = values[channel]
        for z in range(layers):
            for channel in range(4):
                line = values_ref[slab * 4 + channel, pl.ds(z, 8, stride=0), :]
                block = jnp.concatenate([jnp.where(mask, line, 0.0) for mask in masks], axis=0)
                at = slab * size + (z * 4 + channel) * 16
                ends_ref[at : at + 16, :] = block.astype(jnp.bfloat16)
        for side in range(2):
            row = jnp.where(front, 64, rows // 2 - 1) if side == 0 else jnp.where(front, rows // 2, 64)
            twin = jnp.where(row == 64, 65, row + rows)
            keep = (lane_at == row) | (lane_at == twin)
            for channel in range(4):
                at = pl.ds(slab * layers * 8 + side * 4 + channel, layers, stride=8)
                keep_ref[at, :] = jnp.where(keep, values[channel], 0.0)
    ends_ref[2 * size :, :] = keep_ref[0 : 8 * depth].astype(jnp.bfloat16)
    added = jnp.dot(
        ends_ref[...], weights_ref[cols : cols + LANES, 0 : 2 * LANES], preferred_element_type=jnp.float32
    )
    for index, tile in enumerate((0, tiles - 1)):
        block = added[:, index * LANES : (index + 1) * LANES]
        fixed_ref[index, 0:pad, :] = jnp.zeros((pad, LANES), jnp.float32)
        fixed_ref[index, pad + 2 * size :, :] = jnp.zeros((pad, LANES), jnp.float32)
        fixed_ref[index, pad : pad + 2 * size, :] = rounded(
            along_ref[tile, pad : pad + 2 * size, :] + block[0 : 2 * size]
        )
        edge_lines(rounded(edge_ref[index] + block[2 * size :]), packed_ref.at[index], lines_ref.at[index], depth)
    out_ref[:, :, LANES : 2 * cols - LANES] = image_ref[...]

    image = render_pair(
        [fixed_ref.at[0], fixed_ref.at[1]],
        [packed_ref.at[0], packed_ref.at[1]],
        [lines_ref.at[0], lines_ref.at[1]],
        mix_ref,
        rank_ref[0],
        layers,
    )
    for index, start in enumerate((0, 2 * cols - LANES)):
        store_tile(image[index], mixed_ref, out_ref, slice(start, start + LANES))


def two_slab_device(density, bin_index, tf_colour, tf_extinction, slab_rank):
    layers, rows, cols = density.shape
    half = rows // 2
    tiles = 2 * cols // LANES
    size = layers * 4 * half
    count_y, count_x = lax.axis_size("by"), lax.axis_size("bx")
    f32, bf16, i32 = jnp.float32, jnp.bfloat16, jnp.int32

    def call(kernel, name, out_shape, time, scratch_shapes=(), in_specs=None, aliases={}):
        def run(*operands):
            return pl.pallas_call(
                kernel,
                out_shape=out_shape,
                in_specs=in_specs or [VMEM] * len(operands),
                out_specs=(VMEM,) * len(out_shape) if isinstance(out_shape, tuple) else VMEM,
                scratch_shapes=scratch_shapes,
                input_output_aliases=aliases,
                compiler_params=pltpu.CompilerParams(vmem_limit_bytes=16 * 1024 * 1024),
                cost_estimate=cost(time),
                name=name,
            )(*operands)

        return run

    def both(route):
        return route + [(target, source) for source, target in route]

    blocks = (layers, cols // LANES, rows + 8, LANES)
    row = pltpu.VMEM((layers, cols), i32)
    first, second, columns, dense, index, tables = call(
        stage_kernel,
        "stage_block",
        (
            row,
            row,
            pltpu.VMEM((layers, LANES), i32),
            pltpu.VMEM(blocks, f32),
            pltpu.VMEM(blocks, i32),
            pltpu.VMEM((8, 8, LANES), f32),
        ),
        1.2,
    )(*[pltpu.with_memory_space_constraint(x, pltpu.HBM) for x in (density, bin_index, tf_colour, tf_extinction)])
    bulk, inside = call(
        pack_kernel, "pack_block", (pltpu.VMEM((2 * layers + 2, 8, cols), i32), row), 0.1
    )(dense, index, columns)

    def place(z, y, x):
        return (z * count_y + y) * count_x + x

    steps = range(count_y - 1)
    ring = [(place(0, y, 0), place(0, y + 1, 0)) for y in steps]
    ring += [(place(1, y + 1, 0), place(1, y, 0)) for y in steps]
    ring += [(place(0, count_y - 1, 0), place(1, count_y - 1, 0)), (place(1, 0, 0), place(0, 0, 0))]
    ring = [(source + x, target + x) for source, target in ring for x in range(count_x)]
    diagonal = [(place(1, y, x), place(0, y + 1, x)) for y in steps for x in range(count_x)]
    for z, y in ((0, 0), (1, count_y - 1)):
        diagonal += [(place(z, y, x), place(z, y, x + 1)) for x in range(0, count_x, 2)]
    axes = ("bz", "by", "bx")
    bulk = lax.ppermute(bulk, "bz", [(0, 1), (1, 0)])
    first = lax.ppermute(first, axes, ring)
    second = lax.ppermute(second, axes, both(diagonal))

    cells, weights, mix = call(
        cells_kernel,
        "own_cells",
        (
            pltpu.VMEM((size, cols), bf16),
            pltpu.VMEM((cols + LANES, 2 * cols), bf16),
            pltpu.VMEM((128, 80), bf16),
        ),
        0.5,
    )(dense, index, tables)
    whole = pltpu.VMEM((tiles, 2 * size + 2 * 4 * half, LANES), f32)
    along = call(own_kernel, "own_slab", whole, 0.4)(cells, weights)
    ends = call(side_kernel, "side_columns", pltpu.VMEM((2, layers, LANES), i32), 0.1)(
        columns, bulk, second, first, along
    )
    pairs = [(x, x + 1) for x in range(0, count_x, 2)]
    cross = [(x, (x + 1) % count_x) for x in range(1, count_x, 2)]
    beside = lax.ppermute(ends, "bx", both(pairs))
    across = lax.ppermute(ends, "bx", both(cross))
    along = call(other_kernel, "other_slab", whole, 0.8, [pltpu.VMEM((size, cols), bf16)], aliases={4: 0})(
        bulk, tables, weights, ends, along
    )
    smem = pl.BlockSpec(memory_space=pltpu.SMEM)
    lines = [
        pltpu.VMEM((2, 32 * layers, LANES), bf16),
        pltpu.VMEM((2, 16 * layers + 8, LANES), f32),
        pltpu.VMEM((4, rows + 8, LANES), f32),
    ]
    image, edge = call(
        inner_kernel,
        "inner_tiles",
        (pltpu.VMEM((4, rows, (tiles - 2) * LANES), f32), pltpu.VMEM((2, 16 * layers, LANES), f32)),
        2.0,
        [pltpu.VMEM((cols // LANES, 16 * layers + 8, LANES), f32)] + lines,
        [smem] + [VMEM] * 8,
    )(slab_rank, tables, weights, bulk, inside, second, first, mix, along)
    return call(
        outer_kernel,
        "outer_tiles",
        jax.ShapeDtypeStruct((4, rows, 2 * cols), f32),
        2.0,
        [
            pltpu.VMEM((2 * size + 16 * layers, LANES), bf16),
            pltpu.VMEM((8, 2 * layers, LANES), f32),
            pltpu.VMEM((16 * layers + 8, LANES), f32),
            pltpu.VMEM((2, 2 * size + 2 * 4 * half, LANES), f32),
        ]
        + lines,
        [smem] + [VMEM] * 8,
    )(slab_rank, tables, weights, beside, across, mix, along, edge, image)


def on_device(density, bin_index, tf_colour, tf_extinction, slab_rank):
    if lax.axis_size("bz") == 2:
        return two_slab_device(density, bin_index, tf_colour, tf_extinction, slab_rank)
    return general_device(density, bin_index, tf_colour, tf_extinction, slab_rank)


def solution(mesh):
    return jax.shard_map(
        on_device,
        mesh=mesh,
        in_specs=(P("bz", "by", "bx"), P("bz", "by", "bx"), P(), P(), P()),
        out_specs=P(None, ("by", "bz"), "bx"),
        check_vma=False,
    )
```

```python
import jax
import jax.numpy as jnp
from jax import lax
from jax.experimental import pallas as pl
from jax.experimental.pallas import tpu as pltpu
from jax.sharding import PartitionSpec as P


def with_halo(block, sides, width):
    for axis, dim in sides:
        count = lax.axis_size(axis)
        forward = [(i, i + 1) for i in range(count - 1)]
        backward = [(target, source) for source, target in forward]
        low = lax.ppermute(
            lax.slice_in_dim(block, block.shape[dim] - width, None, axis=dim), axis, forward
        )
        high = lax.ppermute(lax.slice_in_dim(block, 0, width, axis=dim), axis, backward)
        block = jnp.concatenate([low, block, high], axis=dim)
    return block


def partner_2(block, axis, stride):
    count = lax.axis_size(axis)
    route = []
    for low in range(count):
        high = low | 1 << stride
        if high != low and high < count:
            route += [(low, high), (high, low)]
    return lax.ppermute(block, axis, route)


def resample_table(length):
    row_index = lax.broadcasted_iota(jnp.int32, (2 * length, length + 2), 0)
    col_index = lax.broadcasted_iota(jnp.int32, (2 * length, length + 2), 1)
    centre = row_index // 2
    parity = row_index % 2
    weights_table = jnp.where(col_index == centre + 1, 0.75, 0.0)
    weights_table = weights_table + jnp.where((col_index == centre) & (parity == 0), 0.25, 0.0)
    weights_table = weights_table + jnp.where((col_index == centre + 2) & (parity == 1), 0.25, 0.0)
    return weights_table.astype(jnp.bfloat16)


def blend_over(in_front, behind):
    return in_front + (1.0 - in_front[3])[None] * behind


def classify(density, bin_index, tf_colour, tf_extinction, total_depth):
    depth_cells, height_cells, width_cells = density.shape
    lookup = jnp.concatenate([tf_colour, tf_extinction[None, :]], axis=0)
    table_size = lookup.shape[1]
    bin_rows = lax.broadcasted_iota(jnp.int32, (table_size, 1), 0)
    flat_bins = bin_index.reshape(depth_cells, height_cells * width_cells)
    flat_density = density.reshape(depth_cells, height_cells * width_cells)

    def one_layer(layer, result):
        layer_bins = lax.dynamic_index_in_dim(flat_bins, layer, 0, keepdims=True)
        layer_density = lax.dynamic_index_in_dim(flat_density, layer, 0, keepdims=False)
        one_hot = (layer_bins == bin_rows).astype(jnp.bfloat16)
        values = jnp.dot(lookup, one_hot, preferred_element_type=jnp.float32)
        opacity = 1.0 - jnp.exp(-values[3] * layer_density / total_depth)
        cells = jnp.concatenate([values[:3] * opacity[None], opacity[None]], axis=0).astype(
            jnp.bfloat16
        )
        return lax.dynamic_update_slice_in_dim(result, cells[:, None], layer, 1)

    start_cells = jnp.zeros((4, depth_cells, height_cells * width_cells), jnp.bfloat16)
    classified = lax.fori_loop(0, depth_cells, one_layer, start_cells)
    return classified.reshape(4, depth_cells, height_cells, width_cells)


def general_device(density, bin_index, tf_colour, tf_extinction, slab_rank):
    slab_count = lax.axis_size("bz")
    depth_cells, height_cells, width_cells = density.shape
    total_depth = float(depth_cells * slab_count)
    colour_cells = classify(density, bin_index, tf_colour, tf_extinction, total_depth)
    padded = with_halo(colour_cells, (("bz", 1), ("by", 2), ("bx", 3)), 1)
    along_x = jnp.einsum(
        "czyq,pq->czyp", padded, resample_table(width_cells), preferred_element_type=jnp.float32
    ).astype(jnp.bfloat16)
    y_table = resample_table(height_cells)

    def add_sample(sample_index, image_now):
        centre = sample_index // 2
        parity = sample_index % 2
        layers = lax.dynamic_slice_in_dim(along_x, centre, 3, 1).astype(jnp.float32)
        lower_weight = jnp.where(parity == 0, 0.25, 0.0)
        upper_weight = jnp.where(parity == 1, 0.25, 0.0)
        mixed_layer = (
            lower_weight * layers[:, 0] + 0.75 * layers[:, 1] + upper_weight * layers[:, 2]
        ).astype(jnp.bfloat16)
        sample = jnp.einsum("qy,cyp->cqp", y_table, mixed_layer, preferred_element_type=jnp.float32)
        return blend_over(image_now, sample)

    start_image = jnp.zeros((4, 2 * height_cells, 2 * width_cells), jnp.float32)
    slab_image = lax.fori_loop(0, 2 * depth_cells, add_sample, start_image)
    rows_piece = 2 * height_cells // slab_count
    my_index = lax.axis_index("bz")
    bit_levels = slab_count.bit_length() - 1
    composite = slab_image.reshape((4,) + (2,) * bit_levels + (rows_piece, 2 * width_cells))
    my_rank = lax.dynamic_index_in_dim(slab_rank, my_index, 0, keepdims=False)
    for level in range(bit_levels):
        position = bit_levels - level
        my_bit = my_index // 2**level % 2
        kept_half = lax.dynamic_index_in_dim(composite, my_bit, position, keepdims=False)
        outgoing = lax.dynamic_index_in_dim(composite, 1 - my_bit, position, keepdims=False)
        incoming = partner_2(outgoing, "bz", level)
        partner = my_index + (1 - 2 * my_bit) * 2**level
        partner_rank = lax.dynamic_index_in_dim(slab_rank, partner, 0, keepdims=False)
        mine_first = my_rank < partner_rank
        composite = blend_over(
            jnp.where(mine_first, kept_half, incoming), jnp.where(mine_first, incoming, kept_half)
        )
    return composite


LANES = 128
LEVELS = 65535.0
VMEM = pl.BlockSpec(memory_space=pltpu.VMEM)


def pack_words(density, bins):
    level = (density * LEVELS + 0.5).astype(jnp.int32)
    return lax.shift_left(level, 16) | bins


def unpack_words(words):
    density = lax.shift_right_logical(words, 16).astype(jnp.float32) * (1.0 / LEVELS)
    return density, words & 0xFFFF


def cell_values(density, bins, tables, depth):
    low_bits = bins & (LANES - 1)
    upper = bins >= LANES

    def pick(channel):
        first, second = tables[channel]
        return jnp.where(
            upper,
            jnp.take_along_axis(second, low_bits, axis=1, mode="promise_in_bounds"),
            jnp.take_along_axis(first, low_bits, axis=1, mode="promise_in_bounds"),
        )

    opacity = (1.0 - jnp.exp(-pick(3) * density / depth)) * (1.0 / 64.0)
    return [pick(0) * opacity, pick(1) * opacity, pick(2) * opacity, opacity]


def read_tables(tables_ref):
    return [[tables_ref[2 * channel + half] for half in range(2)] for channel in range(4)]


def cost(microseconds):
    return pl.CostEstimate(
        flops=int(1e9 * microseconds), bytes_accessed=int(3.6e6 * microseconds), transcendentals=0
    )


def stage_kernel(
    rank_ref, density_ref, bins_ref, colour_ref, extinction_ref,
    flip_ref, first_ref, second_ref, columns_ref, dense_ref, index_ref, tables_ref,
):
    flip_ref[0] = rank_ref[0]
    layers, rows, cols = density_ref.shape
    front = lax.axis_index("bz") == 0
    row_at = lax.broadcasted_iota(jnp.int32, (rows, LANES), 0)
    lane_at = lax.broadcasted_iota(jnp.int32, (rows, LANES), 1)
    for z in range(layers):
        first = pack_words(density_ref[z, :, 0:1], bins_ref[z, :, 0:1])
        last = pack_words(density_ref[z, :, cols - 1 : cols], bins_ref[z, :, cols - 1 : cols])
        line = jnp.where(lane_at == row_at, first, 0) + jnp.where(lane_at == row_at + rows, last, 0)
        columns_ref[z : z + 1, :] = jnp.sum(line, axis=0, keepdims=True)
        top, bottom = [
            pack_words(density_ref[z, r : r + 1, :], bins_ref[z, r : r + 1, :]) for r in (0, rows - 1)
        ]
        first_ref[z : z + 1, :] = jnp.where(front, bottom, top)
        second_ref[z : z + 1, :] = jnp.where(front, top, bottom)
        for tile in range(cols // LANES):
            lanes = slice(tile * LANES, (tile + 1) * LANES)
            dense_ref[z, tile, 0:rows] = density_ref[z, :, lanes]
            index_ref[z, tile, 0:rows] = bins_ref[z, :, lanes]
    colour = colour_ref[...].astype(jnp.float32)
    extinction = extinction_ref[...].astype(jnp.float32).reshape(1, 2 * LANES)
    for channel in range(4):
        line = extinction if channel == 3 else colour[channel : channel + 1]
        for half in range(2):
            tables_ref[2 * channel + half] = jnp.broadcast_to(
                line[:, half * LANES : (half + 1) * LANES], (8, LANES)
            )


def pack_kernel(dense_ref, index_ref, columns_ref, bulk_ref, inside_ref):
    layers, tiles, rows = dense_ref.shape[0], dense_ref.shape[1], dense_ref.shape[2] - 8
    half = rows // 2
    front = lax.axis_index("bz") == 0
    start = jnp.where(front, half, 0)
    for tile in range(tiles):
        lanes = slice(tile * LANES, (tile + 1) * LANES)
        bulk_ref[2 * layers + 1, :, lanes] = columns_ref[...]
        for z in range(layers):
            for part in range(2):
                at = pl.ds(start + part, half // 2, stride=2)
                bulk_ref[2 * z + part, :, lanes] = pack_words(
                    dense_ref[z, tile, at, :], index_ref[z, tile, at, :]
                )
            line = [
                pack_words(dense_ref[z, tile, r : r + 1, :], index_ref[z, tile, r : r + 1, :])
                for r in (half - 1, half)
            ]
            bulk_ref[2 * layers, z : z + 1, lanes] = jnp.where(front, line[0], line[1])
            inside_ref[z : z + 1, lanes] = jnp.where(front, line[1], line[0])


def near_words(slab, first_ref, second_ref):
    me = lax.axis_index("bz")
    words = jnp.where(me == slab, first_ref[...], second_ref[...])
    return jnp.where(has_near(me == 0), words, 0)


def side_kernel(columns_ref, bulk_ref, second_ref, first_ref, along_ref, ends_ref):
    layers = columns_ref.shape[0]
    front = lax.axis_index("bz") == 0
    lane_at = lax.broadcasted_iota(jnp.int32, (layers, LANES), 1)
    for slab in range(2):
        mine = front if slab == 0 else jnp.logical_not(front)
        columns = jnp.where(mine, columns_ref[...], bulk_ref[2 * layers + 1, :, 0:LANES])
        near = near_words(slab, first_ref, second_ref)
        cols = near.shape[1]
        columns = jnp.where(lane_at == 64, near[:, 0:1], columns)
        ends_ref[slab] = jnp.where(lane_at == 65, near[:, cols - 1 : cols], columns)


def has_near(front):
    me_y = lax.axis_index("by")
    return jnp.where(front, me_y > 0, me_y + 1 < lax.axis_size("by"))


def fill_weights(weights_ref, rows):
    cols = weights_ref.shape[0] - LANES
    row = lax.broadcasted_iota(jnp.int32, (cols, 2 * cols), 0)
    at = lax.broadcasted_iota(jnp.int32, (cols, 2 * cols), 1)
    centre = lax.shift_right_logical(at, 1)
    beside = centre - 1 + 2 * (at & 1)
    weights_ref[0:cols, :] = jnp.where(
        row == centre, 3.0, jnp.where(row == beside, 1.0, 0.0)
    ).astype(jnp.bfloat16)
    row = lax.broadcasted_iota(jnp.int32, (LANES, 2 * LANES), 0)
    at = lax.broadcasted_iota(jnp.int32, (LANES, 2 * LANES), 1)
    right = ((row < rows) | (row == 64)) & (at == 2 * LANES - 1)
    left = (((row >= rows) & (row < 2 * rows)) | (row == 65)) & (at == 0)
    weights_ref[cols : cols + LANES, 0 : 2 * LANES] = jnp.where(right | left, 1.0, 0.0).astype(
        jnp.bfloat16
    )


def lane_maps(rows):
    lane_at = lax.broadcasted_iota(jnp.int32, (8, LANES), 1)
    sub_at = lax.broadcasted_iota(jnp.int32, (8, LANES), 0)
    return lane_at & (rows - 1), lane_at < 2 * rows, sub_at


def classify_rows(read_cells, tables, cells_ref, layers, tiles):
    total = float(2 * layers)
    for z in range(layers):
        for tile in range(tiles):
            even = cell_values(*read_cells(z, 0, tile), tables, total)
            odd = cell_values(*read_cells(z, 1, tile), tables, total)
            for channel in range(4):
                base = (z * 4 + channel) * 16
                block = jnp.concatenate([even[channel], odd[channel]], axis=0)
                cells_ref[base : base + 16, tile * LANES : (tile + 1) * LANES] = block.astype(jnp.bfloat16)


def rounded(value):
    return value.astype(jnp.bfloat16).astype(jnp.float32)


def cells_kernel(dense_ref, index_ref, tables_ref, cells_ref, weights_ref, mix_ref):
    layers, tiles, rows = dense_ref.shape[0], dense_ref.shape[1], dense_ref.shape[2] - 8
    half = rows // 2
    start = lax.axis_index("bz") * half
    fill_weights(weights_ref, rows)
    fill_rows(mix_ref)

    def read_cells(z, part, tile):
        at = pl.ds(start + part, half // 2, stride=2)
        return dense_ref[z, tile, at, :], index_ref[z, tile, at, :]

    classify_rows(read_cells, read_tables(tables_ref), cells_ref, layers, tiles)


def along_columns(cells, weights_ref, store):
    cols = cells.shape[1]
    tiles = 2 * cols // LANES
    result = jnp.dot(cells, weights_ref[0:cols, :], preferred_element_type=jnp.float32)
    for tile in range(tiles):
        block = result[:, tile * LANES : (tile + 1) * LANES]
        store(tile, block if tile in (0, tiles - 1) else rounded(block))


def own_kernel(cells_ref, weights_ref, along_ref):
    size = cells_ref.shape[0]
    pad = along_ref.shape[1] // 2 - size
    mine = pl.multiple_of(pad + lax.axis_index("bz") * size, pad)

    def store(tile, block):
        along_ref[tile, 0:pad, :] = jnp.zeros((pad, LANES), jnp.float32)
        along_ref[tile, pad + 2 * size :, :] = jnp.zeros((pad, LANES), jnp.float32)
        along_ref[tile, pl.ds(mine, size), :] = block

    along_columns(cells_ref[...], weights_ref, store)


def other_kernel(bulk_ref, tables_ref, weights_ref, ends_ref, own_ref, along_ref, cells_ref):
    layers = (bulk_ref.shape[0] - 2) // 2
    cols = bulk_ref.shape[2]
    size = cells_ref.shape[0]
    pad = along_ref.shape[1] // 2 - size
    theirs = pl.multiple_of(pad + (1 - lax.axis_index("bz")) * size, pad)

    def read_cells(z, part, tile):
        return unpack_words(bulk_ref[2 * z + part, :, tile * LANES : (tile + 1) * LANES])

    def store(tile, block):
        along_ref[tile, pl.ds(theirs, size), :] = block

    classify_rows(read_cells, read_tables(tables_ref), cells_ref, layers, cols // LANES)
    along_columns(cells_ref[...], weights_ref, store)


def edge_lines(now, packed_ref, lines_ref, depth):
    triple = 3.0 * now
    empty = jnp.zeros((8, LANES), jnp.float32)
    for layer in range(depth):
        at = layer * 8
        here = triple[at : at + 8]
        before = now[at - 8 : at] if layer > 0 else empty
        after = now[at + 8 : at + 16] if layer + 1 < depth else empty
        line = jnp.concatenate([before + here, empty], axis=0)
        packed_ref[2 * at : 2 * at + 16, :] = line.astype(jnp.bfloat16)
        lines_ref[at : at + 8, :] = rounded(after + here)


def render_pair(along_refs, packed_refs, lines_refs, rows_ref, flip, layers):
    sub_at = lax.broadcasted_iota(jnp.int32, (8, LANES), 0)
    top = sub_at == 0
    bottom = sub_at == 7

    def one_slab(position, image):
        slab = position ^ flip
        along_at = pl.ds(pl.multiple_of(slab * (layers * 64), 64), (layers + 2) * 64)
        packed_at = pl.ds(pl.multiple_of(slab * (layers * 16), 16), layers * 16)
        lines_at = pl.ds(pl.multiple_of(slab * (layers * 8), 8), layers * 8 + 8)
        views = [ref.at[along_at, :] for ref in along_refs]
        packed = [ref.at[packed_at, :] for ref in packed_refs]
        lines = [ref.at[lines_at, :] for ref in lines_refs]

        def layer_rows(view, layer, channel):
            base = (layer * 4 + channel) * 16
            return view[base : base + 16, :]

        def both(pieces):
            return jnp.concatenate(pieces, axis=1)

        def blend(image, samples):
            updated = []
            for tile in range(2):
                clear = [1.0 - value for value in image[tile][3]]
                updated.append(
                    [
                        [image[tile][c][i] + clear[i] * samples[tile][c][i] for i in range(4)]
                        for c in range(4)
                    ]
                )
            return updated

        for z in range(layers):
            triple = [[3.0 * layer_rows(v, z + 1, c) for c in range(4)] for v in views]
            mixed = [
                both(
                    [
                        (layer_rows(v, z, c) + t[c]).astype(jnp.bfloat16)
                        for v, t in zip(views, triple)
                    ]
                )
                for c in range(4)
            ]
            mixed.append(both([line[z * 16 : z * 16 + 16, :] for line in packed]))
            even = jnp.dot(
                rows_ref[...], jnp.concatenate(mixed, axis=0), preferred_element_type=jnp.float32
            )
            even = [
                [
                    [
                        even[c * 32 + i * 8 : c * 32 + i * 8 + 8, tile * LANES : (tile + 1) * LANES]
                        for i in range(4)
                    ]
                    for c in range(4)
                ]
                for tile in range(2)
            ]
            odd = []
            for tile in range(2):
                odd.append([])
                for c in range(4):
                    value = rounded(layer_rows(views[tile], z + 2, c) + triple[tile][c])
                    low, high = value[0:8], value[8:16]
                    above = lines[tile][pl.ds(z * 8 + c, 8, stride=0), :]
                    below = lines[tile][pl.ds(z * 8 + 4 + c, 8, stride=0), :]
                    before = jnp.where(top, above, pltpu.roll(high, 1, 0))
                    after = jnp.where(bottom, below, pltpu.roll(low, 7, 0))
                    low_centre = 3.0 * low
                    high_centre = 3.0 * high
                    odd[tile].append(
                        [before + low_centre, low_centre + high, low + high_centre, high_centre + after]
                    )
            image = blend(blend(image, even), odd)
        return image

    zero = jnp.zeros((8, LANES), jnp.float32)
    image = [[[zero] * 4 for _ in range(4)] for _ in range(2)]
    return lax.fori_loop(0, 2, one_slab, image)


def store_tile(image, mixed_ref, out_ref, lanes):
    for channel in range(4):
        for i in range(4):
            mixed_ref[channel, pl.ds(i, 8, stride=4), :] = image[channel][i]
        out_ref[channel, :, lanes] = mixed_ref[channel, 0:32]


def fill_rows(rows_ref):
    m = lax.broadcasted_iota(jnp.int32, rows_ref.shape, 0)
    k = lax.broadcasted_iota(jnp.int32, rows_ref.shape, 1)
    row = 4 * (m & 7) + (lax.shift_right_logical(m, 3) & 3)
    centre = lax.shift_right_logical(row, 1)
    beside = centre - 1 + 2 * (row & 1)
    own = k < 64
    k_channel = jnp.where(own, lax.shift_right_logical(k, 4), k & 3)
    k_row = 2 * (k & 7) + (lax.shift_right_logical(k, 3) & 1)
    k_row = jnp.where(own, k_row, jnp.where(k < 68, -1, jnp.where(k < 72, 16, 99)))
    same = k_channel == lax.shift_right_logical(m, 5)
    value = jnp.where(k_row == centre, 3.0, jnp.where(k_row == beside, 1.0, 0.0))
    rows_ref[...] = jnp.where(same, value, 0.0).astype(jnp.bfloat16)


def inner_kernel(
    flip_ref, tables_ref, weights_ref, bulk_ref, inside_ref, second_ref, first_ref, mix_ref, along_ref,
    image_ref, edge_ref, cells_ref, packed_ref, lines_ref, mixed_ref,
):
    layers, cols = inside_ref.shape
    depth = 2 * layers
    tiles = 2 * cols // LANES
    me = lax.axis_index("bz")
    front = me == 0
    tables = read_tables(tables_ref)
    for slab in range(2):
        inside = jnp.where(me == slab, inside_ref[...], bulk_ref[2 * layers])
        near = near_words(slab, first_ref, second_ref)
        for side in range(2):
            use_near = front if side == 0 else jnp.logical_not(front)
            words = jnp.where(use_near, near, inside)
            for t in range(cols // LANES):
                values = cell_values(
                    *unpack_words(words[:, t * LANES : (t + 1) * LANES]), tables, float(depth)
                )
                for channel in range(4):
                    at = pl.ds(slab * layers * 8 + side * 4 + channel, layers, stride=8)
                    cells_ref[t, at, :] = values[channel]
    edge = sum(
        jnp.dot(
            cells_ref[t, 0 : 8 * depth].astype(jnp.bfloat16),
            weights_ref[t * LANES : (t + 1) * LANES, :],
            preferred_element_type=jnp.float32,
        )
        for t in range(cols // LANES)
    )
    for tile in range(tiles):
        now = edge[:, tile * LANES : (tile + 1) * LANES]
        if tile in (0, tiles - 1):
            edge_ref[0 if tile == 0 else 1] = now
        else:
            edge_lines(rounded(now), packed_ref.at[tile - 1], lines_ref.at[tile - 1], depth)

    image = render_pair(
        [along_ref.at[1], along_ref.at[2]],
        [packed_ref.at[0], packed_ref.at[1]],
        [lines_ref.at[0], lines_ref.at[1]],
        mix_ref,
        flip_ref[0],
        layers,
    )
    for index in range(2):
        store_tile(image[index], mixed_ref, image_ref, slice(index * LANES, (index + 1) * LANES))


def outer_kernel(
    flip_ref, tables_ref, weights_ref, beside_ref, across_ref, mix_ref, along_ref, edge_ref, image_ref,
    out_ref, ends_ref, values_ref, keep_ref, fixed_ref, packed_ref, lines_ref, mixed_ref,
):
    rows = out_ref.shape[1]
    cols = out_ref.shape[2] // 2
    layers = beside_ref.shape[1]
    depth = 2 * layers
    tiles = 2 * cols // LANES
    pad = 64
    size = layers * pad
    front = lax.axis_index("bz") == 0
    start = lax.axis_index("bz") * (rows // 2)
    me_x = lax.axis_index("bx")
    even_x = lax.rem(me_x, 2) == 0
    tables = read_tables(tables_ref)
    side_lane, has_side, sub_at = lane_maps(rows)
    masks = [has_side & (side_lane == start + 2 * sub_at + part) for part in range(2)]
    lane_at = lax.broadcasted_iota(jnp.int32, (layers, LANES), 1)
    is_right = (lane_at < rows) | (lane_at == 64)
    for slab in range(2):
        right = jnp.where(even_x, beside_ref[slab], across_ref[slab])
        left = jnp.where(even_x, across_ref[slab], beside_ref[slab])
        right = jnp.where(me_x + 1 < lax.axis_size("bx"), right, 0)
        left = jnp.where(me_x > 0, left, 0)
        words = jnp.where(is_right, right, left)
        values = cell_values(*unpack_words(words), tables, float(depth))
        for channel in range(4):
            values_ref[slab * 4 + channel, 0:layers] = values[channel]
        for z in range(layers):
            for channel in range(4):
                line = values_ref[slab * 4 + channel, pl.ds(z, 8, stride=0), :]
                block = jnp.concatenate([jnp.where(mask, line, 0.0) for mask in masks], axis=0)
                at = slab * size + (z * 4 + channel) * 16
                ends_ref[at : at + 16, :] = block.astype(jnp.bfloat16)
        for side in range(2):
            row = jnp.where(front, 64, rows // 2 - 1) if side == 0 else jnp.where(front, rows // 2, 64)
            twin = jnp.where(row == 64, 65, row + rows)
            keep = (lane_at == row) | (lane_at == twin)
            for channel in range(4):
                at = pl.ds(slab * layers * 8 + side * 4 + channel, layers, stride=8)
                keep_ref[at, :] = jnp.where(keep, values[channel], 0.0)
    ends_ref[2 * size :, :] = keep_ref[0 : 8 * depth].astype(jnp.bfloat16)
    added = jnp.dot(
        ends_ref[...], weights_ref[cols : cols + LANES, 0 : 2 * LANES], preferred_element_type=jnp.float32
    )
    for index, tile in enumerate((0, tiles - 1)):
        block = added[:, index * LANES : (index + 1) * LANES]
        fixed_ref[index, 0:pad, :] = jnp.zeros((pad, LANES), jnp.float32)
        fixed_ref[index, pad + 2 * size :, :] = jnp.zeros((pad, LANES), jnp.float32)
        fixed_ref[index, pad : pad + 2 * size, :] = rounded(
            along_ref[tile, pad : pad + 2 * size, :] + block[0 : 2 * size]
        )
        edge_lines(rounded(edge_ref[index] + block[2 * size :]), packed_ref.at[index], lines_ref.at[index], depth)
    out_ref[:, :, LANES : 2 * cols - LANES] = image_ref[...]

    image = render_pair(
        [fixed_ref.at[0], fixed_ref.at[1]],
        [packed_ref.at[0], packed_ref.at[1]],
        [lines_ref.at[0], lines_ref.at[1]],
        mix_ref,
        flip_ref[0],
        layers,
    )
    for index, start in enumerate((0, 2 * cols - LANES)):
        store_tile(image[index], mixed_ref, out_ref, slice(start, start + LANES))


def two_slab_device(density, bin_index, tf_colour, tf_extinction, slab_rank):
    layers, rows, cols = density.shape
    half = rows // 2
    tiles = 2 * cols // LANES
    size = layers * 4 * half
    count_y, count_x = lax.axis_size("by"), lax.axis_size("bx")
    f32, bf16, i32 = jnp.float32, jnp.bfloat16, jnp.int32

    def call(kernel, name, out_shape, time, scratch_shapes=(), in_specs=None, out_specs=None, aliases={}):
        def run(*operands):
            return pl.pallas_call(
                kernel,
                out_shape=out_shape,
                in_specs=in_specs or [VMEM] * len(operands),
                out_specs=out_specs
                or ((VMEM,) * len(out_shape) if isinstance(out_shape, tuple) else VMEM),
                scratch_shapes=scratch_shapes,
                input_output_aliases=aliases,
                compiler_params=pltpu.CompilerParams(vmem_limit_bytes=16 * 1024 * 1024),
                cost_estimate=cost(time),
                name=name,
            )(*operands)

        return run

    def both(route):
        return route + [(target, source) for source, target in route]

    blocks = (layers, cols // LANES, rows + 8, LANES)
    row = pltpu.VMEM((layers, cols), i32)
    smem = pl.BlockSpec(memory_space=pltpu.SMEM)
    inputs = [
        pltpu.with_memory_space_constraint(x, pltpu.HBM)
        for x in (slab_rank, density, bin_index, tf_colour, tf_extinction)
    ]
    flip, first, second, columns, dense, index, tables = call(
        stage_kernel,
        "stage_block",
        (
            pltpu.SMEM((1,), i32),
            row,
            row,
            pltpu.VMEM((layers, LANES), i32),
            pltpu.VMEM(blocks, f32),
            pltpu.VMEM(blocks, i32),
            pltpu.VMEM((8, 8, LANES), f32),
        ),
        1.2,
        in_specs=[smem] + [VMEM] * 4,
        out_specs=(smem,) + (VMEM,) * 6,
    )(*inputs)
    bulk, inside = call(
        pack_kernel, "pack_block", (pltpu.VMEM((2 * layers + 2, 8, cols), i32), row), 0.1
    )(dense, index, columns)

    def place(z, y, x):
        return (z * count_y + y) * count_x + x

    steps = range(count_y - 1)
    ring = [(place(0, y, 0), place(0, y + 1, 0)) for y in steps]
    ring += [(place(1, y + 1, 0), place(1, y, 0)) for y in steps]
    ring += [(place(0, count_y - 1, 0), place(1, count_y - 1, 0)), (place(1, 0, 0), place(0, 0, 0))]
    ring = [(source + x, target + x) for source, target in ring for x in range(count_x)]
    diagonal = [(place(1, y, x), place(0, y + 1, x)) for y in steps for x in range(count_x)]
    for z, y in ((0, 0), (1, count_y - 1)):
        diagonal += [(place(z, y, x), place(z, y, x + 1)) for x in range(0, count_x, 2)]
    axes = ("bz", "by", "bx")
    bulk = lax.ppermute(bulk, "bz", [(0, 1), (1, 0)])
    first = lax.ppermute(first, axes, ring)
    second = lax.ppermute(second, axes, both(diagonal))

    cells, weights, mix = call(
        cells_kernel,
        "own_cells",
        (
            pltpu.VMEM((size, cols), bf16),
            pltpu.VMEM((cols + LANES, 2 * cols), bf16),
            pltpu.VMEM((128, 80), bf16),
        ),
        0.5,
    )(dense, index, tables)
    whole = pltpu.VMEM((tiles, 2 * size + 2 * 4 * half, LANES), f32)
    along = call(own_kernel, "own_slab", whole, 0.4)(cells, weights)
    ends = call(side_kernel, "side_columns", pltpu.VMEM((2, layers, LANES), i32), 0.1)(
        columns, bulk, second, first, along
    )
    pairs = [(x, x + 1) for x in range(0, count_x, 2)]
    cross = [(x, (x + 1) % count_x) for x in range(1, count_x, 2)]
    beside = lax.ppermute(ends, "bx", both(pairs))
    across = lax.ppermute(ends, "bx", both(cross))
    along = call(other_kernel, "other_slab", whole, 0.8, [pltpu.VMEM((size, cols), bf16)], aliases={4: 0})(
        bulk, tables, weights, ends, along
    )
    lines = [
        pltpu.VMEM((2, 32 * layers, LANES), bf16),
        pltpu.VMEM((2, 16 * layers + 8, LANES), f32),
        pltpu.VMEM((4, rows + 8, LANES), f32),
    ]
    image, edge = call(
        inner_kernel,
        "inner_tiles",
        (pltpu.VMEM((4, rows, (tiles - 2) * LANES), f32), pltpu.VMEM((2, 16 * layers, LANES), f32)),
        2.0,
        [pltpu.VMEM((cols // LANES, 16 * layers + 8, LANES), f32)] + lines,
        [smem] + [VMEM] * 8,
    )(flip, tables, weights, bulk, inside, second, first, mix, along)
    return call(
        outer_kernel,
        "outer_tiles",
        jax.ShapeDtypeStruct((4, rows, 2 * cols), f32),
        2.0,
        [
            pltpu.VMEM((2 * size + 16 * layers, LANES), bf16),
            pltpu.VMEM((8, 2 * layers, LANES), f32),
            pltpu.VMEM((16 * layers + 8, LANES), f32),
            pltpu.VMEM((2, 2 * size + 2 * 4 * half, LANES), f32),
        ]
        + lines,
        [smem] + [VMEM] * 8,
    )(flip, tables, weights, beside, across, mix, along, edge, image)


def on_device(density, bin_index, tf_colour, tf_extinction, slab_rank):
    if lax.axis_size("bz") == 2:
        return two_slab_device(density, bin_index, tf_colour, tf_extinction, slab_rank)
    return general_device(density, bin_index, tf_colour, tf_extinction, slab_rank)


def solution(mesh):
    return jax.shard_map(
        on_device,
        mesh=mesh,
        in_specs=(P("bz", "by", "bx"), P("bz", "by", "bx"), P(), P(), P()),
        out_specs=P(None, ("by", "bz"), "bx"),
        check_vma=False,
    )
```

```python
import functools

import jax
import jax.numpy as jnp
from jax import lax
from jax.experimental import pallas as pl
from jax.experimental.pallas import tpu as pltpu
from jax.sharding import PartitionSpec as P


def with_halo(block, sides, width):
    for axis, dim in sides:
        count = lax.axis_size(axis)
        forward = [(i, i + 1) for i in range(count - 1)]
        backward = [(target, source) for source, target in forward]
        low = lax.ppermute(
            lax.slice_in_dim(block, block.shape[dim] - width, None, axis=dim), axis, forward
        )
        high = lax.ppermute(lax.slice_in_dim(block, 0, width, axis=dim), axis, backward)
        block = jnp.concatenate([low, block, high], axis=dim)
    return block


def partner_2(block, axis, stride):
    count = lax.axis_size(axis)
    route = []
    for low in range(count):
        high = low | 1 << stride
        if high != low and high < count:
            route += [(low, high), (high, low)]
    return lax.ppermute(block, axis, route)


def resample_table(length):
    row_index = lax.broadcasted_iota(jnp.int32, (2 * length, length + 2), 0)
    col_index = lax.broadcasted_iota(jnp.int32, (2 * length, length + 2), 1)
    centre = row_index // 2
    parity = row_index % 2
    weights_table = jnp.where(col_index == centre + 1, 0.75, 0.0)
    weights_table = weights_table + jnp.where((col_index == centre) & (parity == 0), 0.25, 0.0)
    weights_table = weights_table + jnp.where((col_index == centre + 2) & (parity == 1), 0.25, 0.0)
    return weights_table.astype(jnp.bfloat16)


def blend_over(in_front, behind):
    return in_front + (1.0 - in_front[3])[None] * behind


def classify(density, bin_index, tf_colour, tf_extinction, total_depth):
    depth_cells, height_cells, width_cells = density.shape
    lookup = jnp.concatenate([tf_colour, tf_extinction[None, :]], axis=0)
    table_size = lookup.shape[1]
    bin_rows = lax.broadcasted_iota(jnp.int32, (table_size, 1), 0)
    flat_bins = bin_index.reshape(depth_cells, height_cells * width_cells)
    flat_density = density.reshape(depth_cells, height_cells * width_cells)

    def one_layer(layer, result):
        layer_bins = lax.dynamic_index_in_dim(flat_bins, layer, 0, keepdims=True)
        layer_density = lax.dynamic_index_in_dim(flat_density, layer, 0, keepdims=False)
        one_hot = (layer_bins == bin_rows).astype(jnp.bfloat16)
        values = jnp.dot(lookup, one_hot, preferred_element_type=jnp.float32)
        opacity = 1.0 - jnp.exp(-values[3] * layer_density / total_depth)
        cells = jnp.concatenate([values[:3] * opacity[None], opacity[None]], axis=0).astype(
            jnp.bfloat16
        )
        return lax.dynamic_update_slice_in_dim(result, cells[:, None], layer, 1)

    start_cells = jnp.zeros((4, depth_cells, height_cells * width_cells), jnp.bfloat16)
    classified = lax.fori_loop(0, depth_cells, one_layer, start_cells)
    return classified.reshape(4, depth_cells, height_cells, width_cells)


def general_device(density, bin_index, tf_colour, tf_extinction, slab_rank):
    slab_count = lax.axis_size("bz")
    depth_cells, height_cells, width_cells = density.shape
    total_depth = float(depth_cells * slab_count)
    colour_cells = classify(density, bin_index, tf_colour, tf_extinction, total_depth)
    padded = with_halo(colour_cells, (("bz", 1), ("by", 2), ("bx", 3)), 1)
    along_x = jnp.einsum(
        "czyq,pq->czyp", padded, resample_table(width_cells), preferred_element_type=jnp.float32
    ).astype(jnp.bfloat16)
    y_table = resample_table(height_cells)

    def add_sample(sample_index, image_now):
        centre = sample_index // 2
        parity = sample_index % 2
        layers = lax.dynamic_slice_in_dim(along_x, centre, 3, 1).astype(jnp.float32)
        lower_weight = jnp.where(parity == 0, 0.25, 0.0)
        upper_weight = jnp.where(parity == 1, 0.25, 0.0)
        mixed_layer = (
            lower_weight * layers[:, 0] + 0.75 * layers[:, 1] + upper_weight * layers[:, 2]
        ).astype(jnp.bfloat16)
        sample = jnp.einsum("qy,cyp->cqp", y_table, mixed_layer, preferred_element_type=jnp.float32)
        return blend_over(image_now, sample)

    start_image = jnp.zeros((4, 2 * height_cells, 2 * width_cells), jnp.float32)
    slab_image = lax.fori_loop(0, 2 * depth_cells, add_sample, start_image)
    rows_piece = 2 * height_cells // slab_count
    my_index = lax.axis_index("bz")
    bit_levels = slab_count.bit_length() - 1
    composite = slab_image.reshape((4,) + (2,) * bit_levels + (rows_piece, 2 * width_cells))
    my_rank = lax.dynamic_index_in_dim(slab_rank, my_index, 0, keepdims=False)
    for level in range(bit_levels):
        position = bit_levels - level
        my_bit = my_index // 2**level % 2
        kept_half = lax.dynamic_index_in_dim(composite, my_bit, position, keepdims=False)
        outgoing = lax.dynamic_index_in_dim(composite, 1 - my_bit, position, keepdims=False)
        incoming = partner_2(outgoing, "bz", level)
        partner = my_index + (1 - 2 * my_bit) * 2**level
        partner_rank = lax.dynamic_index_in_dim(slab_rank, partner, 0, keepdims=False)
        mine_first = my_rank < partner_rank
        composite = blend_over(
            jnp.where(mine_first, kept_half, incoming), jnp.where(mine_first, incoming, kept_half)
        )
    return composite


LANES = 128
LEVELS = 65535.0
VMEM = pl.BlockSpec(memory_space=pltpu.VMEM)


def pack_words(density, bins):
    level = (density * LEVELS + 0.5).astype(jnp.int32)
    return lax.shift_left(level, 16) | bins


def unpack_words(words):
    density = lax.shift_right_logical(words, 16).astype(jnp.float32) * (1.0 / LEVELS)
    return density, words & 0xFFFF


def cell_values(density, bins, tables, depth):
    low_bits = bins & (LANES - 1)
    upper = bins >= LANES

    def pick(channel):
        first, second = tables[channel]
        return jnp.where(
            upper,
            jnp.take_along_axis(second, low_bits, axis=1, mode="promise_in_bounds"),
            jnp.take_along_axis(first, low_bits, axis=1, mode="promise_in_bounds"),
        )

    opacity = (1.0 - jnp.exp(-pick(3) * density / depth)) * (1.0 / 64.0)
    return [pick(0) * opacity, pick(1) * opacity, pick(2) * opacity, opacity]


def read_tables(tables_ref):
    return [[tables_ref[2 * channel + half] for half in range(2)] for channel in range(4)]


def cost(microseconds):
    return pl.CostEstimate(
        flops=int(1e9 * microseconds), bytes_accessed=int(3.6e6 * microseconds), transcendentals=0
    )


def stage_kernel(
    rank_ref, density_ref, bins_ref, colour_ref, extinction_ref,
    flip_ref, first_ref, second_ref, columns_ref, dense_ref, index_ref, tables_ref,
):
    flip_ref[0] = rank_ref[0]
    layers, rows, cols = density_ref.shape
    front = lax.axis_index("bz") == 0
    row_at = lax.broadcasted_iota(jnp.int32, (rows, LANES), 0)
    lane_at = lax.broadcasted_iota(jnp.int32, (rows, LANES), 1)
    for z in range(layers):
        first = pack_words(density_ref[z, :, 0:1], bins_ref[z, :, 0:1])
        last = pack_words(density_ref[z, :, cols - 1 : cols], bins_ref[z, :, cols - 1 : cols])
        line = jnp.where(lane_at == row_at, first, 0) + jnp.where(lane_at == row_at + LANES // 2, last, 0)
        columns_ref[z : z + 1, :] = jnp.sum(line, axis=0, keepdims=True)
        top, bottom = [
            pack_words(density_ref[z, r : r + 1, :], bins_ref[z, r : r + 1, :]) for r in (0, rows - 1)
        ]
        first_ref[z : z + 1, :] = jnp.where(front, bottom, top)
        second_ref[z : z + 1, :] = jnp.where(front, top, bottom)
        for tile in range(cols // LANES):
            lanes = slice(tile * LANES, (tile + 1) * LANES)
            dense_ref[z, tile, 0:rows] = density_ref[z, :, lanes]
            index_ref[z, tile, 0:rows] = bins_ref[z, :, lanes]
    colour = colour_ref[...].astype(jnp.float32)
    extinction = extinction_ref[...].astype(jnp.float32).reshape(1, 2 * LANES)
    for channel in range(4):
        line = extinction if channel == 3 else colour[channel : channel + 1]
        for half in range(2):
            tables_ref[2 * channel + half] = jnp.broadcast_to(
                line[:, half * LANES : (half + 1) * LANES], (8, LANES)
            )


def pack_kernel(dense_ref, index_ref, columns_ref, bulk_ref, inside_ref):
    layers, tiles, rows = dense_ref.shape[0], dense_ref.shape[1], dense_ref.shape[2] - 8
    half = rows // 2
    front = lax.axis_index("bz") == 0
    start = jnp.where(front, half, 0)
    for tile in range(tiles):
        lanes = slice(tile * LANES, (tile + 1) * LANES)
        bulk_ref[2 * layers + 1, :, lanes] = columns_ref[...]
        for z in range(layers):
            for part in range(2):
                at = pl.ds(start + part, half // 2, stride=2)
                bulk_ref[2 * z + part, :, lanes] = pack_words(
                    dense_ref[z, tile, at, :], index_ref[z, tile, at, :]
                )
            line = [
                pack_words(dense_ref[z, tile, r : r + 1, :], index_ref[z, tile, r : r + 1, :])
                for r in (half - 1, half)
            ]
            bulk_ref[2 * layers, z : z + 1, lanes] = jnp.where(front, line[0], line[1])
            inside_ref[z : z + 1, lanes] = jnp.where(front, line[1], line[0])


def near_words(slab, first_ref, second_ref):
    me = lax.axis_index("bz")
    words = jnp.where(me == slab, first_ref[...], second_ref[...])
    return jnp.where(has_near(me == 0), words, 0)


def side_kernel(rows, columns_ref, bulk_ref, second_ref, first_ref, along_ref, ends_ref):
    layers = columns_ref.shape[0]
    front = lax.axis_index("bz") == 0
    lane_at = lax.broadcasted_iota(jnp.int32, (layers, LANES), 1)
    for slab in range(2):
        mine = front if slab == 0 else jnp.logical_not(front)
        columns = jnp.where(mine, columns_ref[...], bulk_ref[2 * layers + 1, :, 0:LANES])
        near = near_words(slab, first_ref, second_ref)
        cols = near.shape[1]
        columns = jnp.where(lane_at == rows, near[:, 0:1], columns)
        ends_ref[slab] = jnp.where(
            lane_at == LANES // 2 + rows, near[:, cols - 1 : cols], columns
        )


def has_near(front):
    me_y = lax.axis_index("by")
    return jnp.where(front, me_y > 0, me_y + 1 < lax.axis_size("by"))


def fill_weights(weights_ref):
    cols = weights_ref.shape[0]
    row = lax.broadcasted_iota(jnp.int32, (cols, 2 * cols), 0)
    at = lax.broadcasted_iota(jnp.int32, (cols, 2 * cols), 1)
    centre = lax.shift_right_logical(at, 1)
    beside = centre - 1 + 2 * (at & 1)
    weights_ref[...] = jnp.where(row == centre, 3.0, jnp.where(row == beside, 1.0, 0.0)).astype(
        jnp.bfloat16
    )


def classify_rows(read_cells, tables, cells_ref, layers, tiles):
    total = float(2 * layers)
    for z in range(layers):
        for tile in range(tiles):
            even = cell_values(*read_cells(z, 0, tile), tables, total)
            odd = cell_values(*read_cells(z, 1, tile), tables, total)
            for channel in range(4):
                base = (z * 4 + channel) * 16
                block = jnp.concatenate([even[channel], odd[channel]], axis=0)
                cells_ref[base : base + 16, tile * LANES : (tile + 1) * LANES] = block.astype(jnp.bfloat16)


def rounded(value):
    return value.astype(jnp.bfloat16).astype(jnp.float32)


def cells_kernel(dense_ref, index_ref, tables_ref, cells_ref, weights_ref, mix_ref):
    layers, tiles, rows = dense_ref.shape[0], dense_ref.shape[1], dense_ref.shape[2] - 8
    half = rows // 2
    start = lax.axis_index("bz") * half
    fill_weights(weights_ref)
    fill_rows(mix_ref)

    def read_cells(z, part, tile):
        at = pl.ds(start + part, half // 2, stride=2)
        return dense_ref[z, tile, at, :], index_ref[z, tile, at, :]

    classify_rows(read_cells, read_tables(tables_ref), cells_ref, layers, tiles)


def along_columns(cells, weights_ref, store):
    result = rounded(jnp.dot(cells, weights_ref[...], preferred_element_type=jnp.float32))
    for tile in range(result.shape[1] // LANES):
        store(tile, result[:, tile * LANES : (tile + 1) * LANES])


def own_kernel(cells_ref, weights_ref, along_ref):
    size = cells_ref.shape[0]
    pad = along_ref.shape[1] // 2 - size
    mine = pl.multiple_of(pad + lax.axis_index("bz") * size, pad)

    def store(tile, block):
        along_ref[tile, 0:pad, :] = jnp.zeros((pad, LANES), jnp.float32)
        along_ref[tile, pad + 2 * size :, :] = jnp.zeros((pad, LANES), jnp.float32)
        along_ref[tile, pl.ds(mine, size), :] = block

    along_columns(cells_ref[...], weights_ref, store)


def other_kernel(bulk_ref, tables_ref, weights_ref, ends_ref, own_ref, along_ref, cells_ref):
    layers = (bulk_ref.shape[0] - 2) // 2
    cols = bulk_ref.shape[2]
    size = cells_ref.shape[0]
    pad = along_ref.shape[1] // 2 - size
    theirs = pl.multiple_of(pad + (1 - lax.axis_index("bz")) * size, pad)

    def read_cells(z, part, tile):
        return unpack_words(bulk_ref[2 * z + part, :, tile * LANES : (tile + 1) * LANES])

    def store(tile, block):
        along_ref[tile, pl.ds(theirs, size), :] = block

    classify_rows(read_cells, read_tables(tables_ref), cells_ref, layers, cols // LANES)
    along_columns(cells_ref[...], weights_ref, store)


def edge_lines(now, packed_ref, lines_ref, depth):
    triple = 3.0 * now
    empty = jnp.zeros((8, LANES), jnp.float32)
    for layer in range(depth):
        at = layer * 8
        here = triple[at : at + 8]
        before = now[at - 8 : at] if layer > 0 else empty
        after = now[at + 8 : at + 16] if layer + 1 < depth else empty
        line = jnp.concatenate([before + here, empty], axis=0)
        packed_ref[2 * at : 2 * at + 16, :] = line.astype(jnp.bfloat16)
        lines_ref[at : at + 8, :] = rounded(after + here)


def render_pair(along_refs, packed_refs, lines_refs, rows_ref, flip, layers):
    sub_at = lax.broadcasted_iota(jnp.int32, (8, LANES), 0)
    top = sub_at == 0
    bottom = sub_at == 7

    def one_slab(position, image):
        slab = position ^ flip
        along_at = pl.ds(pl.multiple_of(slab * (layers * 64), 64), (layers + 2) * 64)
        packed_at = pl.ds(pl.multiple_of(slab * (layers * 16), 16), layers * 16)
        lines_at = pl.ds(pl.multiple_of(slab * (layers * 8), 8), layers * 8 + 8)
        views = [ref.at[along_at, :] for ref in along_refs]
        packed = [ref.at[packed_at, :] for ref in packed_refs]
        lines = [ref.at[lines_at, :] for ref in lines_refs]

        def layer_rows(view, layer, channel):
            base = (layer * 4 + channel) * 16
            return view[base : base + 16, :]

        def both(pieces):
            return jnp.concatenate(pieces, axis=1)

        def blend(image, samples):
            updated = []
            for tile in range(2):
                clear = [1.0 - value for value in image[tile][3]]
                updated.append(
                    [
                        [image[tile][c][i] + clear[i] * samples[tile][c][i] for i in range(4)]
                        for c in range(4)
                    ]
                )
            return updated

        for z in range(layers):
            triple = [[3.0 * layer_rows(v, z + 1, c) for c in range(4)] for v in views]
            mixed = [
                both(
                    [
                        (layer_rows(v, z, c) + t[c]).astype(jnp.bfloat16)
                        for v, t in zip(views, triple)
                    ]
                )
                for c in range(4)
            ]
            mixed.append(both([line[z * 16 : z * 16 + 16, :] for line in packed]))
            even = jnp.dot(
                rows_ref[...], jnp.concatenate(mixed, axis=0), preferred_element_type=jnp.float32
            )
            even = [
                [
                    [
                        even[c * 32 + i * 8 : c * 32 + i * 8 + 8, tile * LANES : (tile + 1) * LANES]
                        for i in range(4)
                    ]
                    for c in range(4)
                ]
                for tile in range(2)
            ]
            odd = []
            for tile in range(2):
                odd.append([])
                for c in range(4):
                    value = rounded(layer_rows(views[tile], z + 2, c) + triple[tile][c])
                    low, high = value[0:8], value[8:16]
                    above = lines[tile][pl.ds(z * 8 + c, 8, stride=0), :]
                    below = lines[tile][pl.ds(z * 8 + 4 + c, 8, stride=0), :]
                    before = jnp.where(top, above, pltpu.roll(high, 1, 0))
                    after = jnp.where(bottom, below, pltpu.roll(low, 7, 0))
                    low_centre = 3.0 * low
                    high_centre = 3.0 * high
                    odd[tile].append(
                        [before + low_centre, low_centre + high, low + high_centre, high_centre + after]
                    )
            image = blend(blend(image, even), odd)
        return image

    zero = jnp.zeros((8, LANES), jnp.float32)
    image = [[[zero] * 4 for _ in range(4)] for _ in range(2)]
    return lax.fori_loop(0, 2, one_slab, image)


def fill_rows(rows_ref):
    m = lax.broadcasted_iota(jnp.int32, rows_ref.shape, 0)
    k = lax.broadcasted_iota(jnp.int32, rows_ref.shape, 1)
    row = 4 * (m & 7) + (lax.shift_right_logical(m, 3) & 3)
    centre = lax.shift_right_logical(row, 1)
    beside = centre - 1 + 2 * (row & 1)
    own = k < 64
    k_channel = jnp.where(own, lax.shift_right_logical(k, 4), k & 3)
    k_row = 2 * (k & 7) + (lax.shift_right_logical(k, 3) & 1)
    k_row = jnp.where(own, k_row, jnp.where(k < 68, -1, jnp.where(k < 72, 16, 99)))
    same = k_channel == lax.shift_right_logical(m, 5)
    value = jnp.where(k_row == centre, 3.0, jnp.where(k_row == beside, 1.0, 0.0))
    rows_ref[...] = jnp.where(same, value, 0.0).astype(jnp.bfloat16)


def tiles_kernel(
    flip_ref, tables_ref, weights_ref, bulk_ref, inside_ref, second_ref, first_ref, ends_ref, mix_ref,
    along_ref, image_ref, mine_ref, cells_ref, packed_ref, lines_ref,
):
    layers, cols = inside_ref.shape
    depth = 2 * layers
    tiles = 2 * cols // LANES
    me = lax.axis_index("bz")
    front = me == 0
    tables = read_tables(tables_ref)
    for slab in range(2):
        inside = jnp.where(me == slab, inside_ref[...], bulk_ref[2 * layers])
        near = near_words(slab, first_ref, second_ref)
        for side in range(2):
            use_near = front if side == 0 else jnp.logical_not(front)
            words = jnp.where(use_near, near, inside)
            for t in range(cols // LANES):
                values = cell_values(
                    *unpack_words(words[:, t * LANES : (t + 1) * LANES]), tables, float(depth)
                )
                for channel in range(4):
                    at = pl.ds(slab * layers * 8 + side * 4 + channel, layers, stride=8)
                    cells_ref[t, at, :] = values[channel]
        values = cell_values(*unpack_words(ends_ref[slab]), tables, float(depth))
        for channel in range(4):
            mine_ref[slab * 4 + channel] = 3.0 * rounded(values[channel])
    edge = rounded(
        sum(
            jnp.dot(
                cells_ref[t, 0 : 8 * depth].astype(jnp.bfloat16),
                weights_ref[t * LANES : (t + 1) * LANES, :],
                preferred_element_type=jnp.float32,
            )
            for t in range(cols // LANES)
        )
    )
    for tile in range(tiles):
        now = edge[:, tile * LANES : (tile + 1) * LANES]
        edge_lines(now, packed_ref.at[tile], lines_ref.at[tile], depth)

    def one_pair(pair, carry):
        at = [2 * pair, 2 * pair + 1]
        image = render_pair(
            [along_ref.at[tile] for tile in at],
            [packed_ref.at[tile] for tile in at],
            [lines_ref.at[tile] for tile in at],
            mix_ref,
            flip_ref[0],
            layers,
        )
        for index, tile in enumerate(at):
            for channel in range(4):
                for i in range(4):
                    image_ref[tile, channel, pl.ds(i, 8, stride=4), :] = image[index][channel][i]
        return carry

    lax.fori_loop(0, tiles // 2, one_pair, 0)


def edge_kernel(
    flip_ref, tables_ref, beside_ref, across_ref, mine_ref, image_ref,
    out_ref, samples_ref, final_ref, turned_ref, fixed_ref,
):
    rows = out_ref.shape[1]
    cols = out_ref.shape[2] // 2
    half = rows // 2
    layers = beside_ref.shape[1]
    tiles = 2 * cols // LANES
    middle = LANES // 2
    front = lax.axis_index("bz") == 0
    start = pl.multiple_of(lax.axis_index("bz") * half, half)
    me_x = lax.axis_index("bx")
    even_x = lax.rem(me_x, 2) == 0
    tables = read_tables(tables_ref)
    lane_at = lax.broadcasted_iota(jnp.int32, (layers, LANES), 1)
    layer_at = lax.broadcasted_iota(jnp.int32, (layers, LANES), 0)
    first_lane = (lane_at & (middle - 1)) == 0
    along = [[], []]
    for slab in range(2):
        right = jnp.where(even_x, beside_ref[slab], across_ref[slab])
        left = jnp.where(even_x, across_ref[slab], beside_ref[slab])
        right = jnp.where(me_x + 1 < lax.axis_size("bx"), right, 0)
        left = jnp.where(me_x > 0, left, 0)
        words = pltpu.roll(jnp.where(lane_at < middle, right, left), middle, 1)
        halo = cell_values(*unpack_words(words), tables, float(2 * layers))
        for channel in range(4):
            along[slab].append(rounded(mine_ref[slab * 4 + channel] + rounded(halo[channel])))
    for channel in range(4):
        front_part, back_part = along[0][channel], along[1][channel]
        down = [pltpu.roll(front_part, 1, 0), pltpu.roll(back_part, 1, 0)]
        up = [pltpu.roll(front_part, layers - 1, 0), pltpu.roll(back_part, layers - 1, 0)]
        is_first, is_last = layer_at == 0, layer_at == layers - 1
        before = [jnp.where(is_first, 0.0, down[0]), jnp.where(is_first, down[0], down[1])]
        after = [jnp.where(is_last, up[1], up[0]), jnp.where(is_last, 0.0, up[1])]
        for slab in range(2):
            triple = 3.0 * along[slab][channel]
            for parity, other in enumerate((before[slab], after[slab])):
                mixed = rounded(other + triple)
                centre = 3.0 * mixed
                above = pltpu.roll(mixed, 1, 1)
                near = pltpu.roll(mixed, LANES - rows, 1)
                above = jnp.where(first_lane, jnp.where(front, near, above), above)
                below = pltpu.roll(mixed, LANES - 1, 1)
                for odd, value in enumerate((above + centre, centre + below)):
                    at = (parity * 2 + odd) * 4 + channel
                    samples_ref[slab, at, 0:layers, :] = value

    def one_slab(position, image):
        slab = position ^ flip_ref[0]
        for z in range(layers):
            for parity in range(2):
                clear = [1.0 - image[odd][3] for odd in range(2)]
                image = [
                    [
                        image[odd][channel]
                        + clear[odd]
                        * samples_ref[slab, (parity * 2 + odd) * 4 + channel, pl.ds(z, 8, stride=0), :]
                        for channel in range(4)
                    ]
                    for odd in range(2)
                ]
        return image

    zero = jnp.zeros((8, LANES), jnp.float32)
    image = lax.fori_loop(0, 2, one_slab, [[zero] * 4 for _ in range(2)])
    final_ref[8:, :] = jnp.zeros((LANES - 8, LANES), jnp.float32)
    for odd in range(2):
        for channel in range(4):
            at = odd * 4 + channel
            final_ref[at : at + 1, :] = image[odd][channel][0:1]
    turned_ref[...] = final_ref[...].T
    wide = lax.broadcasted_iota(jnp.int32, (half, LANES), 1)
    for index, tile in enumerate((0, tiles - 1)):
        place = wide == index * (LANES - 1)
        turned = turned_ref[pl.ds(start + index * middle, half), :]
        for channel in range(4):
            for odd in range(2):
                at = pl.ds(odd, half, stride=2)
                column = odd * 4 + channel
                fixed_ref[index, channel, at, :] = jnp.where(
                    place, turned[:, column : column + 1], image_ref[tile, channel, at, :]
                )
            out_ref[channel, :, tile * LANES : (tile + 1) * LANES] = fixed_ref[index, channel, 0:rows]
    for tile in range(1, tiles - 1):
        for channel in range(4):
            out_ref[channel, :, tile * LANES : (tile + 1) * LANES] = image_ref[tile, channel, 0:rows]


def two_slab_device(density, bin_index, tf_colour, tf_extinction, slab_rank):
    layers, rows, cols = density.shape
    half = rows // 2
    tiles = 2 * cols // LANES
    size = layers * 4 * half
    count_y, count_x = lax.axis_size("by"), lax.axis_size("bx")
    f32, bf16, i32 = jnp.float32, jnp.bfloat16, jnp.int32

    def call(kernel, name, out_shape, time, scratch_shapes=(), in_specs=None, out_specs=None, aliases={}):
        def run(*operands):
            return pl.pallas_call(
                kernel,
                out_shape=out_shape,
                in_specs=in_specs or [VMEM] * len(operands),
                out_specs=out_specs
                or ((VMEM,) * len(out_shape) if isinstance(out_shape, tuple) else VMEM),
                scratch_shapes=scratch_shapes,
                input_output_aliases=aliases,
                compiler_params=pltpu.CompilerParams(vmem_limit_bytes=16 * 1024 * 1024),
                cost_estimate=cost(time),
                name=name,
            )(*operands)

        return run

    def both(route):
        return route + [(target, source) for source, target in route]

    blocks = (layers, cols // LANES, rows + 8, LANES)
    row = pltpu.VMEM((layers, cols), i32)
    smem = pl.BlockSpec(memory_space=pltpu.SMEM)
    inputs = [
        pltpu.with_memory_space_constraint(x, pltpu.HBM)
        for x in (slab_rank, density, bin_index, tf_colour, tf_extinction)
    ]
    flip, first, second, columns, dense, index, tables = call(
        stage_kernel,
        "stage_block",
        (
            pltpu.SMEM((1,), i32),
            row,
            row,
            pltpu.VMEM((layers, LANES), i32),
            pltpu.VMEM(blocks, f32),
            pltpu.VMEM(blocks, i32),
            pltpu.VMEM((8, 8, LANES), f32),
        ),
        1.2,
        in_specs=[smem] + [VMEM] * 4,
        out_specs=(smem,) + (VMEM,) * 6,
    )(*inputs)
    bulk, inside = call(
        pack_kernel, "pack_block", (pltpu.VMEM((2 * layers + 2, 8, cols), i32), row), 0.1
    )(dense, index, columns)

    def place(z, y, x):
        return (z * count_y + y) * count_x + x

    steps = range(count_y - 1)
    ring = [(place(0, y, 0), place(0, y + 1, 0)) for y in steps]
    ring += [(place(1, y + 1, 0), place(1, y, 0)) for y in steps]
    ring += [(place(0, count_y - 1, 0), place(1, count_y - 1, 0)), (place(1, 0, 0), place(0, 0, 0))]
    ring = [(source + x, target + x) for source, target in ring for x in range(count_x)]
    diagonal = [(place(1, y, x), place(0, y + 1, x)) for y in steps for x in range(count_x)]
    for z, y in ((0, 0), (1, count_y - 1)):
        diagonal += [(place(z, y, x), place(z, y, x + 1)) for x in range(0, count_x, 2)]
    axes = ("bz", "by", "bx")
    bulk = lax.ppermute(bulk, "bz", [(0, 1), (1, 0)])
    first = lax.ppermute(first, axes, ring)
    second = lax.ppermute(second, axes, both(diagonal))

    cells, weights, mix = call(
        cells_kernel,
        "own_cells",
        (
            pltpu.VMEM((size, cols), bf16),
            pltpu.VMEM((cols, 2 * cols), bf16),
            pltpu.VMEM((128, 80), bf16),
        ),
        0.5,
    )(dense, index, tables)
    whole = pltpu.VMEM((tiles, 2 * size + 2 * 4 * half, LANES), f32)
    along = call(own_kernel, "own_slab", whole, 0.4)(cells, weights)
    ends = call(functools.partial(side_kernel, rows), "side_columns", pltpu.VMEM((2, layers, LANES), i32), 0.1)(
        columns, bulk, second, first, along
    )
    pairs = [(x, x + 1) for x in range(0, count_x, 2)]
    cross = [(x, (x + 1) % count_x) for x in range(1, count_x, 2)]
    beside = lax.ppermute(ends, "bx", both(pairs))
    across = lax.ppermute(ends, "bx", both(cross))
    along = call(other_kernel, "other_slab", whole, 0.8, [pltpu.VMEM((size, cols), bf16)], aliases={4: 0})(
        bulk, tables, weights, ends, along
    )
    image, mine = call(
        tiles_kernel,
        "render_tiles",
        (pltpu.VMEM((tiles, 4, rows + 8, LANES), f32), pltpu.VMEM((8, layers, LANES), f32)),
        2.0,
        [
            pltpu.VMEM((cols // LANES, 16 * layers + 8, LANES), f32),
            pltpu.VMEM((tiles, 32 * layers, LANES), bf16),
            pltpu.VMEM((tiles, 16 * layers + 8, LANES), f32),
        ],
        [smem] + [VMEM] * 9,
    )(flip, tables, weights, bulk, inside, second, first, ends, mix, along)
    return call(
        edge_kernel,
        "edge_columns",
        jax.ShapeDtypeStruct((4, rows, 2 * cols), f32),
        1.0,
        [
            pltpu.VMEM((2, 16, 2 * layers, LANES), f32),
            pltpu.VMEM((LANES, LANES), f32),
            pltpu.VMEM((LANES, LANES), f32),
            pltpu.VMEM((2, 4, rows + 8, LANES), f32),
        ],
        [smem] + [VMEM] * 5,
    )(flip, tables, beside, across, mine, image)


def on_device(density, bin_index, tf_colour, tf_extinction, slab_rank):
    if lax.axis_size("bz") == 2:
        return two_slab_device(density, bin_index, tf_colour, tf_extinction, slab_rank)
    return general_device(density, bin_index, tf_colour, tf_extinction, slab_rank)


def solution(mesh):
    return jax.shard_map(
        on_device,
        mesh=mesh,
        in_specs=(P("bz", "by", "bx"), P("bz", "by", "bx"), P(), P(), P()),
        out_specs=P(None, ("by", "bz"), "bx"),
        check_vma=False,
    )
```

```python
import functools

import jax
import jax.numpy as jnp
from jax import lax
from jax.experimental import pallas as pl
from jax.experimental.pallas import tpu as pltpu
from jax.sharding import PartitionSpec as P


def with_halo(block, sides, width):
    for axis, dim in sides:
        count = lax.axis_size(axis)
        forward = [(i, i + 1) for i in range(count - 1)]
        backward = [(target, source) for source, target in forward]
        low = lax.ppermute(
            lax.slice_in_dim(block, block.shape[dim] - width, None, axis=dim), axis, forward
        )
        high = lax.ppermute(lax.slice_in_dim(block, 0, width, axis=dim), axis, backward)
        block = jnp.concatenate([low, block, high], axis=dim)
    return block


def partner_2(block, axis, stride):
    count = lax.axis_size(axis)
    route = []
    for low in range(count):
        high = low | 1 << stride
        if high != low and high < count:
            route += [(low, high), (high, low)]
    return lax.ppermute(block, axis, route)


def resample_table(length):
    row_index = lax.broadcasted_iota(jnp.int32, (2 * length, length + 2), 0)
    col_index = lax.broadcasted_iota(jnp.int32, (2 * length, length + 2), 1)
    centre = row_index // 2
    parity = row_index % 2
    weights_table = jnp.where(col_index == centre + 1, 0.75, 0.0)
    weights_table = weights_table + jnp.where((col_index == centre) & (parity == 0), 0.25, 0.0)
    weights_table = weights_table + jnp.where((col_index == centre + 2) & (parity == 1), 0.25, 0.0)
    return weights_table.astype(jnp.bfloat16)


def blend_over(in_front, behind):
    return in_front + (1.0 - in_front[3])[None] * behind


def classify(density, bin_index, tf_colour, tf_extinction, total_depth):
    depth_cells, height_cells, width_cells = density.shape
    lookup = jnp.concatenate([tf_colour, tf_extinction[None, :]], axis=0)
    table_size = lookup.shape[1]
    bin_rows = lax.broadcasted_iota(jnp.int32, (table_size, 1), 0)
    flat_bins = bin_index.reshape(depth_cells, height_cells * width_cells)
    flat_density = density.reshape(depth_cells, height_cells * width_cells)

    def one_layer(layer, result):
        layer_bins = lax.dynamic_index_in_dim(flat_bins, layer, 0, keepdims=True)
        layer_density = lax.dynamic_index_in_dim(flat_density, layer, 0, keepdims=False)
        one_hot = (layer_bins == bin_rows).astype(jnp.bfloat16)
        values = jnp.dot(lookup, one_hot, preferred_element_type=jnp.float32)
        opacity = 1.0 - jnp.exp(-values[3] * layer_density / total_depth)
        cells = jnp.concatenate([values[:3] * opacity[None], opacity[None]], axis=0).astype(
            jnp.bfloat16
        )
        return lax.dynamic_update_slice_in_dim(result, cells[:, None], layer, 1)

    start_cells = jnp.zeros((4, depth_cells, height_cells * width_cells), jnp.bfloat16)
    classified = lax.fori_loop(0, depth_cells, one_layer, start_cells)
    return classified.reshape(4, depth_cells, height_cells, width_cells)


def general_device(density, bin_index, tf_colour, tf_extinction, slab_rank):
    slab_count = lax.axis_size("bz")
    depth_cells, height_cells, width_cells = density.shape
    total_depth = float(depth_cells * slab_count)
    colour_cells = classify(density, bin_index, tf_colour, tf_extinction, total_depth)
    padded = with_halo(colour_cells, (("bz", 1), ("by", 2), ("bx", 3)), 1)
    along_x = jnp.einsum(
        "czyq,pq->czyp", padded, resample_table(width_cells), preferred_element_type=jnp.float32
    ).astype(jnp.bfloat16)
    y_table = resample_table(height_cells)

    def add_sample(sample_index, image_now):
        centre = sample_index // 2
        parity = sample_index % 2
        layers = lax.dynamic_slice_in_dim(along_x, centre, 3, 1).astype(jnp.float32)
        lower_weight = jnp.where(parity == 0, 0.25, 0.0)
        upper_weight = jnp.where(parity == 1, 0.25, 0.0)
        mixed_layer = (
            lower_weight * layers[:, 0] + 0.75 * layers[:, 1] + upper_weight * layers[:, 2]
        ).astype(jnp.bfloat16)
        sample = jnp.einsum("qy,cyp->cqp", y_table, mixed_layer, preferred_element_type=jnp.float32)
        return blend_over(image_now, sample)

    start_image = jnp.zeros((4, 2 * height_cells, 2 * width_cells), jnp.float32)
    slab_image = lax.fori_loop(0, 2 * depth_cells, add_sample, start_image)
    rows_piece = 2 * height_cells // slab_count
    my_index = lax.axis_index("bz")
    bit_levels = slab_count.bit_length() - 1
    composite = slab_image.reshape((4,) + (2,) * bit_levels + (rows_piece, 2 * width_cells))
    my_rank = lax.dynamic_index_in_dim(slab_rank, my_index, 0, keepdims=False)
    for level in range(bit_levels):
        position = bit_levels - level
        my_bit = my_index // 2**level % 2
        kept_half = lax.dynamic_index_in_dim(composite, my_bit, position, keepdims=False)
        outgoing = lax.dynamic_index_in_dim(composite, 1 - my_bit, position, keepdims=False)
        incoming = partner_2(outgoing, "bz", level)
        partner = my_index + (1 - 2 * my_bit) * 2**level
        partner_rank = lax.dynamic_index_in_dim(slab_rank, partner, 0, keepdims=False)
        mine_first = my_rank < partner_rank
        composite = blend_over(
            jnp.where(mine_first, kept_half, incoming), jnp.where(mine_first, incoming, kept_half)
        )
    return composite


LANES = 128
LEVELS = 65535.0
VMEM = pl.BlockSpec(memory_space=pltpu.VMEM)


def pack_words(density, bins):
    level = (density * LEVELS + 0.5).astype(jnp.int32)
    return lax.shift_left(level, 16) | bins


def unpack_words(words):
    density = lax.shift_right_logical(words, 16).astype(jnp.float32) * (1.0 / LEVELS)
    return density, words & 0xFFFF


def cell_values(density, bins, tables, depth):
    low_bits = bins & (LANES - 1)
    upper = bins >= LANES

    def pick(channel):
        first, second = tables[channel]
        return jnp.where(
            upper,
            jnp.take_along_axis(second, low_bits, axis=1, mode="promise_in_bounds"),
            jnp.take_along_axis(first, low_bits, axis=1, mode="promise_in_bounds"),
        )

    opacity = (1.0 - jnp.exp(-pick(3) * density / depth)) * (1.0 / 64.0)
    return [pick(0) * opacity, pick(1) * opacity, pick(2) * opacity, opacity]


def read_tables(tables_ref):
    return [[tables_ref[2 * channel + half] for half in range(2)] for channel in range(4)]


def cost(microseconds):
    return pl.CostEstimate(
        flops=int(1e9 * microseconds), bytes_accessed=int(3.6e6 * microseconds), transcendentals=0
    )


def stage_kernel(
    rank_ref, density_ref, bins_ref, colour_ref, extinction_ref,
    flip_ref, first_ref, second_ref, dense_ref, index_ref, tables_ref,
):
    flip_ref[0] = rank_ref[0]
    layers, rows, cols = density_ref.shape
    front = lax.axis_index("bz") == 0
    for z in range(layers):
        top, bottom = [
            pack_words(density_ref[z, r : r + 1, :], bins_ref[z, r : r + 1, :]) for r in (0, rows - 1)
        ]
        first_ref[z : z + 1, :] = jnp.where(front, bottom, top)
        second_ref[z : z + 1, :] = jnp.where(front, top, bottom)
        for tile in range(cols // LANES):
            lanes = slice(tile * LANES, (tile + 1) * LANES)
            dense_ref[z, tile, 0:rows] = density_ref[z, :, lanes]
            index_ref[z, tile, 0:rows] = bins_ref[z, :, lanes]
    colour = colour_ref[...].astype(jnp.float32)
    extinction = extinction_ref[...].astype(jnp.float32).reshape(1, 2 * LANES)
    for channel in range(4):
        line = extinction if channel == 3 else colour[channel : channel + 1]
        for half in range(2):
            tables_ref[2 * channel + half] = jnp.broadcast_to(
                line[:, half * LANES : (half + 1) * LANES], (8, LANES)
            )


def pack_kernel(dense_ref, index_ref, bulk_ref, inside_ref):
    layers, tiles, rows = dense_ref.shape[0], dense_ref.shape[1], dense_ref.shape[2] - 8
    half = rows // 2
    front = lax.axis_index("bz") == 0
    start = jnp.where(front, half, 0)
    for tile in range(tiles):
        lanes = slice(tile * LANES, (tile + 1) * LANES)
        for z in range(layers):
            for part in range(2):
                at = pl.ds(start + part, half // 2, stride=2)
                bulk_ref[2 * z + part, :, lanes] = pack_words(
                    dense_ref[z, tile, at, :], index_ref[z, tile, at, :]
                )
            line = [
                pack_words(dense_ref[z, tile, r : r + 1, :], index_ref[z, tile, r : r + 1, :])
                for r in (half - 1, half)
            ]
            bulk_ref[2 * layers, z : z + 1, lanes] = jnp.where(front, line[0], line[1])
            inside_ref[z : z + 1, lanes] = jnp.where(front, line[1], line[0])


def near_words(slab, first_ref, second_ref):
    me = lax.axis_index("bz")
    words = jnp.where(me == slab, first_ref[...], second_ref[...])
    return jnp.where(has_near(me == 0), words, 0)


def column_lines(read_words, inside, lines_ref, rows):
    layers, cols = inside.shape
    front = lax.axis_index("bz") == 0
    start = lax.axis_index("bz") * (rows // 2)
    middle = LANES // 2
    lane_at = lax.broadcasted_iota(jnp.int32, (8, LANES), 1)
    row_at = start + 2 * lax.broadcasted_iota(jnp.int32, (8, LANES), 0)
    for z in range(layers):
        line = jnp.zeros((8, LANES), jnp.int32)
        for part in range(2):
            first = read_words(z, part, 0)[:, 0:1]
            last = read_words(z, part, cols // LANES - 1)[:, LANES - 1 : LANES]
            line += jnp.where(lane_at == row_at + part, first, 0)
            line += jnp.where(lane_at == row_at + part + middle, last, 0)
        lines_ref[z : z + 1, :] = jnp.sum(line, axis=0, keepdims=True)
    beside = jnp.where(front, rows // 2, rows // 2 - 1)
    lines = jnp.where(lane_at == beside, inside[:, 0:1], lines_ref[...])
    lines_ref[...] = jnp.where(lane_at == beside + middle, inside[:, cols - 1 : cols], lines)


def side_kernel(rows, columns_ref, other_ref, second_ref, first_ref, ends_ref):
    layers = columns_ref.shape[0]
    front = lax.axis_index("bz") == 0
    lane_at = lax.broadcasted_iota(jnp.int32, (layers, LANES), 1)
    for slab in range(2):
        mine = front if slab == 0 else jnp.logical_not(front)
        columns = jnp.where(mine, columns_ref[...], other_ref[...])
        near = near_words(slab, first_ref, second_ref)
        cols = near.shape[1]
        columns = jnp.where(lane_at == rows, near[:, 0:1], columns)
        ends_ref[slab] = jnp.where(
            lane_at == LANES // 2 + rows, near[:, cols - 1 : cols], columns
        )


def has_near(front):
    me_y = lax.axis_index("by")
    return jnp.where(front, me_y > 0, me_y + 1 < lax.axis_size("by"))


def fill_weights(weights_ref):
    cols = weights_ref.shape[0]
    row = lax.broadcasted_iota(jnp.int32, (cols, 2 * cols), 0)
    at = lax.broadcasted_iota(jnp.int32, (cols, 2 * cols), 1)
    centre = lax.shift_right_logical(at, 1)
    beside = centre - 1 + 2 * (at & 1)
    weights_ref[...] = jnp.where(row == centre, 3.0, jnp.where(row == beside, 1.0, 0.0)).astype(
        jnp.bfloat16
    )


def classify_rows(read_cells, tables, cells_ref, layers, tiles):
    total = float(2 * layers)
    for z in range(layers):
        for tile in range(tiles):
            even = cell_values(*read_cells(z, 0, tile), tables, total)
            odd = cell_values(*read_cells(z, 1, tile), tables, total)
            for channel in range(4):
                base = (z * 4 + channel) * 16
                block = jnp.concatenate([even[channel], odd[channel]], axis=0)
                cells_ref[base : base + 16, tile * LANES : (tile + 1) * LANES] = block.astype(jnp.bfloat16)


def rounded(value):
    return value.astype(jnp.bfloat16).astype(jnp.float32)


def cells_kernel(dense_ref, index_ref, inside_ref, tables_ref, cells_ref, weights_ref, mix_ref, lines_ref):
    layers, tiles, rows = dense_ref.shape[0], dense_ref.shape[1], dense_ref.shape[2] - 8
    half = rows // 2
    start = lax.axis_index("bz") * half
    fill_weights(weights_ref)
    fill_rows(mix_ref)

    def read_cells(z, part, tile):
        at = pl.ds(start + part, half // 2, stride=2)
        return dense_ref[z, tile, at, :], index_ref[z, tile, at, :]

    classify_rows(read_cells, read_tables(tables_ref), cells_ref, layers, tiles)
    column_lines(lambda *at: pack_words(*read_cells(*at)), inside_ref[...], lines_ref, rows)


def along_columns(cells, weights_ref, store):
    result = rounded(jnp.dot(cells, weights_ref[...], preferred_element_type=jnp.float32))
    for tile in range(result.shape[1] // LANES):
        store(tile, result[:, tile * LANES : (tile + 1) * LANES])


def own_kernel(cells_ref, weights_ref, along_ref):
    size = cells_ref.shape[0]
    pad = along_ref.shape[1] // 2 - size
    mine = pl.multiple_of(pad + lax.axis_index("bz") * size, pad)

    def store(tile, block):
        along_ref[tile, 0:pad, :] = jnp.zeros((pad, LANES), jnp.float32)
        along_ref[tile, pad + 2 * size :, :] = jnp.zeros((pad, LANES), jnp.float32)
        along_ref[tile, pl.ds(mine, size), :] = block

    along_columns(cells_ref[...], weights_ref, store)


def other_kernel(
    rows, bulk_ref, tables_ref, weights_ref, own_ref, along_ref, columns_ref, cells_ref
):
    layers = (bulk_ref.shape[0] - 1) // 2
    cols = bulk_ref.shape[2]
    size = cells_ref.shape[0]
    pad = along_ref.shape[1] // 2 - size
    theirs = pl.multiple_of(pad + (1 - lax.axis_index("bz")) * size, pad)

    def read_words(z, part, tile):
        return bulk_ref[2 * z + part, :, tile * LANES : (tile + 1) * LANES]

    def read_cells(z, part, tile):
        return unpack_words(read_words(z, part, tile))

    def store(tile, block):
        along_ref[tile, pl.ds(theirs, size), :] = block

    column_lines(read_words, bulk_ref[2 * layers], columns_ref, rows)
    classify_rows(read_cells, read_tables(tables_ref), cells_ref, layers, cols // LANES)
    along_columns(cells_ref[...], weights_ref, store)


def edge_lines(now, packed_ref, lines_ref, depth):
    triple = 3.0 * now
    empty = jnp.zeros((8, LANES), jnp.float32)
    for layer in range(depth):
        at = layer * 8
        here = triple[at : at + 8]
        before = now[at - 8 : at] if layer > 0 else empty
        after = now[at + 8 : at + 16] if layer + 1 < depth else empty
        line = jnp.concatenate([before + here, empty], axis=0)
        packed_ref[2 * at : 2 * at + 16, :] = line.astype(jnp.bfloat16)
        lines_ref[at : at + 8, :] = rounded(after + here)


def render_pair(along_refs, packed_refs, lines_refs, rows_ref, flip, layers):
    sub_at = lax.broadcasted_iota(jnp.int32, (8, LANES), 0)
    top = sub_at == 0
    bottom = sub_at == 7

    def one_slab(position, image):
        slab = position ^ flip
        along_at = pl.ds(pl.multiple_of(slab * (layers * 64), 64), (layers + 2) * 64)
        packed_at = pl.ds(pl.multiple_of(slab * (layers * 16), 16), layers * 16)
        lines_at = pl.ds(pl.multiple_of(slab * (layers * 8), 8), layers * 8 + 8)
        views = [ref.at[along_at, :] for ref in along_refs]
        packed = [ref.at[packed_at, :] for ref in packed_refs]
        lines = [ref.at[lines_at, :] for ref in lines_refs]

        def layer_rows(view, layer, channel):
            base = (layer * 4 + channel) * 16
            return view[base : base + 16, :]

        def both(pieces):
            return jnp.concatenate(pieces, axis=1)

        def blend(image, samples):
            updated = []
            for tile in range(2):
                clear = [1.0 - value for value in image[tile][3]]
                updated.append(
                    [
                        [image[tile][c][i] + clear[i] * samples[tile][c][i] for i in range(4)]
                        for c in range(4)
                    ]
                )
            return updated

        for z in range(layers):
            triple = [[3.0 * layer_rows(v, z + 1, c) for c in range(4)] for v in views]
            mixed = [
                both(
                    [
                        (layer_rows(v, z, c) + t[c]).astype(jnp.bfloat16)
                        for v, t in zip(views, triple)
                    ]
                )
                for c in range(4)
            ]
            mixed.append(both([line[z * 16 : z * 16 + 16, :] for line in packed]))
            even = jnp.dot(
                rows_ref[...], jnp.concatenate(mixed, axis=0), preferred_element_type=jnp.float32
            )
            even = [
                [
                    [
                        even[c * 32 + i * 8 : c * 32 + i * 8 + 8, tile * LANES : (tile + 1) * LANES]
                        for i in range(4)
                    ]
                    for c in range(4)
                ]
                for tile in range(2)
            ]
            odd = []
            for tile in range(2):
                odd.append([])
                for c in range(4):
                    value = rounded(layer_rows(views[tile], z + 2, c) + triple[tile][c])
                    low, high = value[0:8], value[8:16]
                    above = lines[tile][pl.ds(z * 8 + c, 8, stride=0), :]
                    below = lines[tile][pl.ds(z * 8 + 4 + c, 8, stride=0), :]
                    before = jnp.where(top, above, pltpu.roll(high, 1, 0))
                    after = jnp.where(bottom, below, pltpu.roll(low, 7, 0))
                    low_centre = 3.0 * low
                    high_centre = 3.0 * high
                    odd[tile].append(
                        [before + low_centre, low_centre + high, low + high_centre, high_centre + after]
                    )
            image = blend(blend(image, even), odd)
        return image

    zero = jnp.zeros((8, LANES), jnp.float32)
    image = [[[zero] * 4 for _ in range(4)] for _ in range(2)]
    return lax.fori_loop(0, 2, one_slab, image)


def fill_rows(rows_ref):
    m = lax.broadcasted_iota(jnp.int32, rows_ref.shape, 0)
    k = lax.broadcasted_iota(jnp.int32, rows_ref.shape, 1)
    row = 4 * (m & 7) + (lax.shift_right_logical(m, 3) & 3)
    centre = lax.shift_right_logical(row, 1)
    beside = centre - 1 + 2 * (row & 1)
    own = k < 64
    k_channel = jnp.where(own, lax.shift_right_logical(k, 4), k & 3)
    k_row = 2 * (k & 7) + (lax.shift_right_logical(k, 3) & 1)
    k_row = jnp.where(own, k_row, jnp.where(k < 68, -1, jnp.where(k < 72, 16, 99)))
    same = k_channel == lax.shift_right_logical(m, 5)
    value = jnp.where(k_row == centre, 3.0, jnp.where(k_row == beside, 1.0, 0.0))
    rows_ref[...] = jnp.where(same, value, 0.0).astype(jnp.bfloat16)


def tiles_kernel(
    flip_ref, tables_ref, weights_ref, bulk_ref, inside_ref, second_ref, first_ref, ends_ref, mix_ref,
    along_ref, image_ref, mine_ref, cells_ref, packed_ref, lines_ref,
):
    layers, cols = inside_ref.shape
    depth = 2 * layers
    tiles = 2 * cols // LANES
    me = lax.axis_index("bz")
    front = me == 0
    tables = read_tables(tables_ref)
    for slab in range(2):
        inside = jnp.where(me == slab, inside_ref[...], bulk_ref[2 * layers])
        near = near_words(slab, first_ref, second_ref)
        for side in range(2):
            use_near = front if side == 0 else jnp.logical_not(front)
            words = jnp.where(use_near, near, inside)
            for t in range(cols // LANES):
                values = cell_values(
                    *unpack_words(words[:, t * LANES : (t + 1) * LANES]), tables, float(depth)
                )
                for channel in range(4):
                    at = pl.ds(slab * layers * 8 + side * 4 + channel, layers, stride=8)
                    cells_ref[t, at, :] = values[channel]
        values = cell_values(*unpack_words(ends_ref[slab]), tables, float(depth))
        for channel in range(4):
            mine_ref[slab * 4 + channel] = 3.0 * rounded(values[channel])
    edge = rounded(
        sum(
            jnp.dot(
                cells_ref[t, 0 : 8 * depth].astype(jnp.bfloat16),
                weights_ref[t * LANES : (t + 1) * LANES, :],
                preferred_element_type=jnp.float32,
            )
            for t in range(cols // LANES)
        )
    )
    for tile in range(tiles):
        now = edge[:, tile * LANES : (tile + 1) * LANES]
        edge_lines(now, packed_ref.at[tile], lines_ref.at[tile], depth)

    def one_pair(pair, carry):
        at = [2 * pair, 2 * pair + 1]
        image = render_pair(
            [along_ref.at[tile] for tile in at],
            [packed_ref.at[tile] for tile in at],
            [lines_ref.at[tile] for tile in at],
            mix_ref,
            flip_ref[0],
            layers,
        )
        for index, tile in enumerate(at):
            for channel in range(4):
                for i in range(4):
                    image_ref[tile, channel, pl.ds(i, 8, stride=4), :] = image[index][channel][i]
        return carry

    lax.fori_loop(0, tiles // 2, one_pair, 0)


def edge_kernel(
    flip_ref, tables_ref, beside_ref, across_ref, mine_ref, image_ref,
    out_ref, samples_ref, final_ref, turned_ref, fixed_ref,
):
    rows = out_ref.shape[1]
    cols = out_ref.shape[2] // 2
    half = rows // 2
    layers = beside_ref.shape[1]
    tiles = 2 * cols // LANES
    middle = LANES // 2
    front = lax.axis_index("bz") == 0
    start = pl.multiple_of(lax.axis_index("bz") * half, half)
    me_x = lax.axis_index("bx")
    even_x = lax.rem(me_x, 2) == 0
    tables = read_tables(tables_ref)
    lane_at = lax.broadcasted_iota(jnp.int32, (layers, LANES), 1)
    layer_at = lax.broadcasted_iota(jnp.int32, (layers, LANES), 0)
    first_lane = (lane_at & (middle - 1)) == 0
    along = [[], []]
    for slab in range(2):
        right = jnp.where(even_x, beside_ref[slab], across_ref[slab])
        left = jnp.where(even_x, across_ref[slab], beside_ref[slab])
        right = jnp.where(me_x + 1 < lax.axis_size("bx"), right, 0)
        left = jnp.where(me_x > 0, left, 0)
        words = pltpu.roll(jnp.where(lane_at < middle, right, left), middle, 1)
        halo = cell_values(*unpack_words(words), tables, float(2 * layers))
        for channel in range(4):
            along[slab].append(rounded(mine_ref[slab * 4 + channel] + rounded(halo[channel])))
    for channel in range(4):
        front_part, back_part = along[0][channel], along[1][channel]
        down = [pltpu.roll(front_part, 1, 0), pltpu.roll(back_part, 1, 0)]
        up = [pltpu.roll(front_part, layers - 1, 0), pltpu.roll(back_part, layers - 1, 0)]
        is_first, is_last = layer_at == 0, layer_at == layers - 1
        before = [jnp.where(is_first, 0.0, down[0]), jnp.where(is_first, down[0], down[1])]
        after = [jnp.where(is_last, up[1], up[0]), jnp.where(is_last, 0.0, up[1])]
        for slab in range(2):
            triple = 3.0 * along[slab][channel]
            for parity, other in enumerate((before[slab], after[slab])):
                mixed = rounded(other + triple)
                centre = 3.0 * mixed
                above = pltpu.roll(mixed, 1, 1)
                near = pltpu.roll(mixed, LANES - rows, 1)
                above = jnp.where(first_lane, jnp.where(front, near, above), above)
                below = pltpu.roll(mixed, LANES - 1, 1)
                for odd, value in enumerate((above + centre, centre + below)):
                    at = (parity * 2 + odd) * 4 + channel
                    samples_ref[slab, at, 0:layers, :] = value

    def over_some(slab, layers_at):
        zero = jnp.zeros((8, LANES), jnp.float32)
        image = [[zero] * 4 for _ in range(2)]
        for z in layers_at:
            for parity in range(2):
                clear = [1.0 - image[odd][3] for odd in range(2)]
                image = [
                    [
                        image[odd][channel]
                        + clear[odd]
                        * samples_ref[slab, (parity * 2 + odd) * 4 + channel, pl.ds(z, 8, stride=0), :]
                        for channel in range(4)
                    ]
                    for odd in range(2)
                ]
        return image

    def over(in_front, behind):
        return [
            [top + (1.0 - tops[3]) * low for top, low in zip(tops, lows)]
            for tops, lows in zip(in_front, behind)
        ]

    slabs = [
        over(
            over_some(slab, range(layers // 2)), over_some(slab, range(layers // 2, layers))
        )
        for slab in range(2)
    ]
    in_order = flip_ref[0] == 0
    image = over(
        *[
            [
                [jnp.where(in_order, x, y) for x, y in zip(xs, ys)]
                for xs, ys in zip(slabs[at], slabs[1 - at])
            ]
            for at in range(2)
        ]
    )
    final_ref[8:, :] = jnp.zeros((LANES - 8, LANES), jnp.float32)
    for odd in range(2):
        for channel in range(4):
            at = odd * 4 + channel
            final_ref[at : at + 1, :] = image[odd][channel][0:1]
    turned_ref[...] = final_ref[...].T
    wide = lax.broadcasted_iota(jnp.int32, (half, LANES), 1)
    for index, tile in enumerate((0, tiles - 1)):
        place = wide == index * (LANES - 1)
        turned = turned_ref[pl.ds(start + index * middle, half), :]
        for channel in range(4):
            for odd in range(2):
                at = pl.ds(odd, half, stride=2)
                column = odd * 4 + channel
                fixed_ref[index, channel, at, :] = jnp.where(
                    place, turned[:, column : column + 1], image_ref[tile, channel, at, :]
                )
            out_ref[channel, :, tile * LANES : (tile + 1) * LANES] = fixed_ref[index, channel, 0:rows]
    for tile in range(1, tiles - 1):
        for channel in range(4):
            out_ref[channel, :, tile * LANES : (tile + 1) * LANES] = image_ref[tile, channel, 0:rows]


def two_slab_device(density, bin_index, tf_colour, tf_extinction, slab_rank):
    layers, rows, cols = density.shape
    half = rows // 2
    tiles = 2 * cols // LANES
    size = layers * 4 * half
    count_y, count_x = lax.axis_size("by"), lax.axis_size("bx")
    f32, bf16, i32 = jnp.float32, jnp.bfloat16, jnp.int32

    def call(kernel, name, out_shape, time, scratch_shapes=(), in_specs=None, out_specs=None, aliases={}):
        def run(*operands):
            return pl.pallas_call(
                kernel,
                out_shape=out_shape,
                in_specs=in_specs or [VMEM] * len(operands),
                out_specs=out_specs
                or ((VMEM,) * len(out_shape) if isinstance(out_shape, tuple) else VMEM),
                scratch_shapes=scratch_shapes,
                input_output_aliases=aliases,
                compiler_params=pltpu.CompilerParams(vmem_limit_bytes=16 * 1024 * 1024),
                cost_estimate=cost(time),
                name=name,
            )(*operands)

        return run

    def both(route):
        return route + [(target, source) for source, target in route]

    blocks = (layers, cols // LANES, rows + 8, LANES)
    row = pltpu.VMEM((layers, cols), i32)
    smem = pl.BlockSpec(memory_space=pltpu.SMEM)
    inputs = [
        pltpu.with_memory_space_constraint(x, pltpu.HBM)
        for x in (slab_rank, density, bin_index, tf_colour, tf_extinction)
    ]
    flip, first, second, dense, index, tables = call(
        stage_kernel,
        "stage_block",
        (
            pltpu.SMEM((1,), i32),
            row,
            row,
            pltpu.VMEM(blocks, f32),
            pltpu.VMEM(blocks, i32),
            pltpu.VMEM((8, 8, LANES), f32),
        ),
        1.2,
        in_specs=[smem] + [VMEM] * 4,
        out_specs=(smem,) + (VMEM,) * 5,
    )(*inputs)
    bulk, inside = call(
        pack_kernel, "pack_block", (pltpu.VMEM((2 * layers + 1, 8, cols), i32), row), 0.1
    )(dense, index)

    def place(z, y, x):
        return (z * count_y + y) * count_x + x

    steps = range(count_y - 1)
    ring = [(place(0, y, 0), place(0, y + 1, 0)) for y in steps]
    ring += [(place(1, y + 1, 0), place(1, y, 0)) for y in steps]
    ring += [(place(0, count_y - 1, 0), place(1, count_y - 1, 0)), (place(1, 0, 0), place(0, 0, 0))]
    ring = [(source + x, target + x) for source, target in ring for x in range(count_x)]
    diagonal = [(place(1, y, x), place(0, y + 1, x)) for y in steps for x in range(count_x)]
    for z, y in ((0, 0), (1, count_y - 1)):
        diagonal += [(place(z, y, x), place(z, y, x + 1)) for x in range(0, count_x, 2)]
    axes = ("bz", "by", "bx")
    bulk = lax.ppermute(bulk, "bz", [(0, 1), (1, 0)])
    first = lax.ppermute(first, axes, ring)
    second = lax.ppermute(second, axes, both(diagonal))

    cells, weights, mix, columns = call(
        cells_kernel,
        "own_cells",
        (
            pltpu.VMEM((size, cols), bf16),
            pltpu.VMEM((cols, 2 * cols), bf16),
            pltpu.VMEM((128, 80), bf16),
            pltpu.VMEM((layers, LANES), i32),
        ),
        0.5,
    )(dense, index, inside, tables)
    whole = pltpu.VMEM((tiles, 2 * size + 2 * 4 * half, LANES), f32)
    along = call(own_kernel, "own_slab", whole, 0.4)(cells, weights)
    along, other_columns = call(
        functools.partial(other_kernel, rows),
        "other_slab",
        (whole, pltpu.VMEM((layers, LANES), i32)),
        0.8,
        [pltpu.VMEM((size, cols), bf16)],
        aliases={3: 0},
    )(bulk, tables, weights, along)
    ends = call(
        functools.partial(side_kernel, rows), "side_columns", pltpu.VMEM((2, layers, LANES), i32), 0.1
    )(columns, other_columns, second, first)
    pairs = [(x, x + 1) for x in range(0, count_x, 2)]
    cross = [(x, (x + 1) % count_x) for x in range(1, count_x, 2)]
    beside = lax.ppermute(ends, "bx", both(pairs))
    across = lax.ppermute(ends, "bx", both(cross))
    image, mine = call(
        tiles_kernel,
        "render_tiles",
        (pltpu.VMEM((tiles, 4, rows + 8, LANES), f32), pltpu.VMEM((8, layers, LANES), f32)),
        2.0,
        [
            pltpu.VMEM((cols // LANES, 16 * layers + 8, LANES), f32),
            pltpu.VMEM((tiles, 32 * layers, LANES), bf16),
            pltpu.VMEM((tiles, 16 * layers + 8, LANES), f32),
        ],
        [smem] + [VMEM] * 9,
    )(flip, tables, weights, bulk, inside, second, first, ends, mix, along)
    return call(
        edge_kernel,
        "edge_columns",
        jax.ShapeDtypeStruct((4, rows, 2 * cols), f32),
        1.0,
        [
            pltpu.VMEM((2, 16, 2 * layers, LANES), f32),
            pltpu.VMEM((LANES, LANES), f32),
            pltpu.VMEM((LANES, LANES), f32),
            pltpu.VMEM((2, 4, rows + 8, LANES), f32),
        ],
        [smem] + [VMEM] * 5,
    )(flip, tables, beside, across, mine, image)


def on_device(density, bin_index, tf_colour, tf_extinction, slab_rank):
    if lax.axis_size("bz") == 2:
        return two_slab_device(density, bin_index, tf_colour, tf_extinction, slab_rank)
    return general_device(density, bin_index, tf_colour, tf_extinction, slab_rank)


def solution(mesh):
    return jax.shard_map(
        on_device,
        mesh=mesh,
        in_specs=(P("bz", "by", "bx"), P("bz", "by", "bx"), P(), P(), P()),
        out_specs=P(None, ("by", "bz"), "bx"),
        check_vma=False,
    )
```

```python
import functools

import jax
import jax.numpy as jnp
from jax import lax
from jax.experimental import pallas as pl
from jax.experimental.pallas import tpu as pltpu
from jax.sharding import PartitionSpec as P


def with_halo(block, sides, width):
    for axis, dim in sides:
        count = lax.axis_size(axis)
        forward = [(i, i + 1) for i in range(count - 1)]
        backward = [(target, source) for source, target in forward]
        low = lax.ppermute(
            lax.slice_in_dim(block, block.shape[dim] - width, None, axis=dim), axis, forward
        )
        high = lax.ppermute(lax.slice_in_dim(block, 0, width, axis=dim), axis, backward)
        block = jnp.concatenate([low, block, high], axis=dim)
    return block


def partner_2(block, axis, stride):
    count = lax.axis_size(axis)
    route = []
    for low in range(count):
        high = low | 1 << stride
        if high != low and high < count:
            route += [(low, high), (high, low)]
    return lax.ppermute(block, axis, route)


def resample_table(length):
    row_index = lax.broadcasted_iota(jnp.int32, (2 * length, length + 2), 0)
    col_index = lax.broadcasted_iota(jnp.int32, (2 * length, length + 2), 1)
    centre = row_index // 2
    parity = row_index % 2
    weights_table = jnp.where(col_index == centre + 1, 0.75, 0.0)
    weights_table = weights_table + jnp.where((col_index == centre) & (parity == 0), 0.25, 0.0)
    weights_table = weights_table + jnp.where((col_index == centre + 2) & (parity == 1), 0.25, 0.0)
    return weights_table.astype(jnp.bfloat16)


def blend_over(in_front, behind):
    return in_front + (1.0 - in_front[3])[None] * behind


def classify(density, bin_index, tf_colour, tf_extinction, total_depth):
    depth_cells, height_cells, width_cells = density.shape
    lookup = jnp.concatenate([tf_colour, tf_extinction[None, :]], axis=0)
    table_size = lookup.shape[1]
    bin_rows = lax.broadcasted_iota(jnp.int32, (table_size, 1), 0)
    flat_bins = bin_index.reshape(depth_cells, height_cells * width_cells)
    flat_density = density.reshape(depth_cells, height_cells * width_cells)

    def one_layer(layer, result):
        layer_bins = lax.dynamic_index_in_dim(flat_bins, layer, 0, keepdims=True)
        layer_density = lax.dynamic_index_in_dim(flat_density, layer, 0, keepdims=False)
        one_hot = (layer_bins == bin_rows).astype(jnp.bfloat16)
        values = jnp.dot(lookup, one_hot, preferred_element_type=jnp.float32)
        opacity = 1.0 - jnp.exp(-values[3] * layer_density / total_depth)
        cells = jnp.concatenate([values[:3] * opacity[None], opacity[None]], axis=0).astype(
            jnp.bfloat16
        )
        return lax.dynamic_update_slice_in_dim(result, cells[:, None], layer, 1)

    start_cells = jnp.zeros((4, depth_cells, height_cells * width_cells), jnp.bfloat16)
    classified = lax.fori_loop(0, depth_cells, one_layer, start_cells)
    return classified.reshape(4, depth_cells, height_cells, width_cells)


def general_device(density, bin_index, tf_colour, tf_extinction, slab_rank):
    slab_count = lax.axis_size("bz")
    depth_cells, height_cells, width_cells = density.shape
    total_depth = float(depth_cells * slab_count)
    colour_cells = classify(density, bin_index, tf_colour, tf_extinction, total_depth)
    padded = with_halo(colour_cells, (("bz", 1), ("by", 2), ("bx", 3)), 1)
    along_x = jnp.einsum(
        "czyq,pq->czyp", padded, resample_table(width_cells), preferred_element_type=jnp.float32
    ).astype(jnp.bfloat16)
    y_table = resample_table(height_cells)

    def add_sample(sample_index, image_now):
        centre = sample_index // 2
        parity = sample_index % 2
        layers = lax.dynamic_slice_in_dim(along_x, centre, 3, 1).astype(jnp.float32)
        lower_weight = jnp.where(parity == 0, 0.25, 0.0)
        upper_weight = jnp.where(parity == 1, 0.25, 0.0)
        mixed_layer = (
            lower_weight * layers[:, 0] + 0.75 * layers[:, 1] + upper_weight * layers[:, 2]
        ).astype(jnp.bfloat16)
        sample = jnp.einsum("qy,cyp->cqp", y_table, mixed_layer, preferred_element_type=jnp.float32)
        return blend_over(image_now, sample)

    start_image = jnp.zeros((4, 2 * height_cells, 2 * width_cells), jnp.float32)
    slab_image = lax.fori_loop(0, 2 * depth_cells, add_sample, start_image)
    rows_piece = 2 * height_cells // slab_count
    my_index = lax.axis_index("bz")
    bit_levels = slab_count.bit_length() - 1
    composite = slab_image.reshape((4,) + (2,) * bit_levels + (rows_piece, 2 * width_cells))
    my_rank = lax.dynamic_index_in_dim(slab_rank, my_index, 0, keepdims=False)
    for level in range(bit_levels):
        position = bit_levels - level
        my_bit = my_index // 2**level % 2
        kept_half = lax.dynamic_index_in_dim(composite, my_bit, position, keepdims=False)
        outgoing = lax.dynamic_index_in_dim(composite, 1 - my_bit, position, keepdims=False)
        incoming = partner_2(outgoing, "bz", level)
        partner = my_index + (1 - 2 * my_bit) * 2**level
        partner_rank = lax.dynamic_index_in_dim(slab_rank, partner, 0, keepdims=False)
        mine_first = my_rank < partner_rank
        composite = blend_over(
            jnp.where(mine_first, kept_half, incoming), jnp.where(mine_first, incoming, kept_half)
        )
    return composite


LANES = 128
LEVELS = 65535.0
VMEM = pl.BlockSpec(memory_space=pltpu.VMEM)


def pack_words(density, bins):
    level = (density * LEVELS + 0.5).astype(jnp.int32)
    return lax.shift_left(level, 16) | bins


def unpack_words(words):
    density = lax.shift_right_logical(words, 16).astype(jnp.float32) * (1.0 / LEVELS)
    return density, words & 0xFFFF


def cell_values(density, bins, tables, depth):
    low_bits = bins & (LANES - 1)
    upper = bins >= LANES

    def pick(channel):
        first, second = tables[channel]
        return jnp.where(
            upper,
            jnp.take_along_axis(second, low_bits, axis=1, mode="promise_in_bounds"),
            jnp.take_along_axis(first, low_bits, axis=1, mode="promise_in_bounds"),
        )

    opacity = (1.0 - jnp.exp(-pick(3) * density / depth)) * (1.0 / 64.0)
    return [pick(0) * opacity, pick(1) * opacity, pick(2) * opacity, opacity]


def read_tables(tables_ref):
    return [[tables_ref[2 * channel + half] for half in range(2)] for channel in range(4)]


def cost(microseconds):
    return pl.CostEstimate(
        flops=int(1e9 * microseconds), bytes_accessed=int(3.6e6 * microseconds), transcendentals=0
    )


def stage_kernel(
    rank_ref, density_ref, bins_ref, colour_ref, extinction_ref,
    flip_ref, first_ref, second_ref, bulk_ref, inside_ref, dense_ref, index_ref, tables_ref,
):
    flip_ref[0] = rank_ref[0]
    layers, rows, cols = density_ref.shape
    front = lax.axis_index("bz") == 0
    for z in range(layers):
        top, bottom = [
            pack_words(density_ref[z, r : r + 1, :], bins_ref[z, r : r + 1, :]) for r in (0, rows - 1)
        ]
        first_ref[z : z + 1, :] = jnp.where(front, bottom, top)
        second_ref[z : z + 1, :] = jnp.where(front, top, bottom)
        for tile in range(cols // LANES):
            lanes = slice(tile * LANES, (tile + 1) * LANES)
            dense_ref[z, tile, 0:rows] = density_ref[z, :, lanes]
            index_ref[z, tile, 0:rows] = bins_ref[z, :, lanes]
    pack_block(dense_ref, index_ref, bulk_ref, inside_ref)
    colour = colour_ref[...].astype(jnp.float32)
    extinction = extinction_ref[...].astype(jnp.float32).reshape(1, 2 * LANES)
    for channel in range(4):
        line = extinction if channel == 3 else colour[channel : channel + 1]
        for half in range(2):
            tables_ref[2 * channel + half] = jnp.broadcast_to(
                line[:, half * LANES : (half + 1) * LANES], (8, LANES)
            )


def pack_block(dense_ref, index_ref, bulk_ref, inside_ref):
    layers, tiles, rows = dense_ref.shape[0], dense_ref.shape[1], dense_ref.shape[2] - 8
    half = rows // 2
    front = lax.axis_index("bz") == 0
    start = jnp.where(front, half, 0)
    for tile in range(tiles):
        lanes = slice(tile * LANES, (tile + 1) * LANES)
        for z in range(layers):
            for part in range(2):
                at = pl.ds(start + part, half // 2, stride=2)
                bulk_ref[2 * z + part, :, lanes] = pack_words(
                    dense_ref[z, tile, at, :], index_ref[z, tile, at, :]
                )
            line = [
                pack_words(dense_ref[z, tile, r : r + 1, :], index_ref[z, tile, r : r + 1, :])
                for r in (half - 1, half)
            ]
            bulk_ref[2 * layers, z : z + 1, lanes] = jnp.where(front, line[0], line[1])
            inside_ref[z : z + 1, lanes] = jnp.where(front, line[1], line[0])


def near_words(slab, first_ref, second_ref):
    me = lax.axis_index("bz")
    words = jnp.where(me == slab, first_ref[...], second_ref[...])
    return jnp.where(has_near(me == 0), words, 0)


def column_lines(read_words, inside, lines_ref, rows):
    layers, cols = inside.shape
    front = lax.axis_index("bz") == 0
    start = lax.axis_index("bz") * (rows // 2)
    middle = LANES // 2
    lane_at = lax.broadcasted_iota(jnp.int32, (8, LANES), 1)
    row_at = start + 2 * lax.broadcasted_iota(jnp.int32, (8, LANES), 0)
    for z in range(layers):
        line = jnp.zeros((8, LANES), jnp.int32)
        for part in range(2):
            first = read_words(z, part, 0)[:, 0:1]
            last = read_words(z, part, cols // LANES - 1)[:, LANES - 1 : LANES]
            line += jnp.where(lane_at == row_at + part, first, 0)
            line += jnp.where(lane_at == row_at + part + middle, last, 0)
        lines_ref[z : z + 1, :] = jnp.sum(line, axis=0, keepdims=True)
    beside = jnp.where(front, rows // 2, rows // 2 - 1)
    lines = jnp.where(lane_at == beside, inside[:, 0:1], lines_ref[...])
    lines_ref[...] = jnp.where(lane_at == beside + middle, inside[:, cols - 1 : cols], lines)


def side_kernel(rows, columns_ref, other_ref, second_ref, first_ref, ends_ref):
    layers = columns_ref.shape[0]
    front = lax.axis_index("bz") == 0
    lane_at = lax.broadcasted_iota(jnp.int32, (layers, LANES), 1)
    for slab in range(2):
        mine = front if slab == 0 else jnp.logical_not(front)
        columns = jnp.where(mine, columns_ref[...], other_ref[...])
        near = near_words(slab, first_ref, second_ref)
        cols = near.shape[1]
        columns = jnp.where(lane_at == rows, near[:, 0:1], columns)
        ends_ref[slab] = jnp.where(
            lane_at == LANES // 2 + rows, near[:, cols - 1 : cols], columns
        )


def has_near(front):
    me_y = lax.axis_index("by")
    return jnp.where(front, me_y > 0, me_y + 1 < lax.axis_size("by"))


def fill_weights(weights_ref):
    cols = weights_ref.shape[0]
    row = lax.broadcasted_iota(jnp.int32, (cols, 2 * cols), 0)
    at = lax.broadcasted_iota(jnp.int32, (cols, 2 * cols), 1)
    centre = lax.shift_right_logical(at, 1)
    beside = centre - 1 + 2 * (at & 1)
    weights_ref[...] = jnp.where(row == centre, 3.0, jnp.where(row == beside, 1.0, 0.0)).astype(
        jnp.bfloat16
    )


def classify_rows(read_cells, tables, cells_ref, layers, tiles):
    total = float(2 * layers)
    for z in range(layers):
        for tile in range(tiles):
            even = cell_values(*read_cells(z, 0, tile), tables, total)
            odd = cell_values(*read_cells(z, 1, tile), tables, total)
            for channel in range(4):
                base = (z * 4 + channel) * 16
                block = jnp.concatenate([even[channel], odd[channel]], axis=0)
                cells_ref[base : base + 16, tile * LANES : (tile + 1) * LANES] = block.astype(jnp.bfloat16)


def rounded(value):
    return value.astype(jnp.bfloat16).astype(jnp.float32)


def cells_kernel(dense_ref, index_ref, inside_ref, tables_ref, cells_ref, weights_ref, mix_ref, lines_ref):
    layers, tiles, rows = dense_ref.shape[0], dense_ref.shape[1], dense_ref.shape[2] - 8
    half = rows // 2
    start = lax.axis_index("bz") * half
    fill_weights(weights_ref)
    fill_rows(mix_ref)

    def read_cells(z, part, tile):
        at = pl.ds(start + part, half // 2, stride=2)
        return dense_ref[z, tile, at, :], index_ref[z, tile, at, :]

    classify_rows(read_cells, read_tables(tables_ref), cells_ref, layers, tiles)
    column_lines(lambda *at: pack_words(*read_cells(*at)), inside_ref[...], lines_ref, rows)


def along_columns(cells, weights_ref, store):
    result = rounded(jnp.dot(cells, weights_ref[...], preferred_element_type=jnp.float32))
    for tile in range(result.shape[1] // LANES):
        store(tile, result[:, tile * LANES : (tile + 1) * LANES])


def own_kernel(cells_ref, weights_ref, along_ref):
    size = cells_ref.shape[0]
    pad = along_ref.shape[1] // 2 - size
    mine = pl.multiple_of(pad + lax.axis_index("bz") * size, pad)

    def store(tile, block):
        along_ref[tile, 0:pad, :] = jnp.zeros((pad, LANES), jnp.float32)
        along_ref[tile, pad + 2 * size :, :] = jnp.zeros((pad, LANES), jnp.float32)
        along_ref[tile, pl.ds(mine, size), :] = block

    along_columns(cells_ref[...], weights_ref, store)


def other_kernel(
    rows, bulk_ref, tables_ref, weights_ref, own_ref, along_ref, columns_ref, cells_ref
):
    layers = (bulk_ref.shape[0] - 1) // 2
    cols = bulk_ref.shape[2]
    size = cells_ref.shape[0]
    pad = along_ref.shape[1] // 2 - size
    theirs = pl.multiple_of(pad + (1 - lax.axis_index("bz")) * size, pad)

    def read_words(z, part, tile):
        return bulk_ref[2 * z + part, :, tile * LANES : (tile + 1) * LANES]

    def read_cells(z, part, tile):
        return unpack_words(read_words(z, part, tile))

    def store(tile, block):
        along_ref[tile, pl.ds(theirs, size), :] = block

    column_lines(read_words, bulk_ref[2 * layers], columns_ref, rows)
    classify_rows(read_cells, read_tables(tables_ref), cells_ref, layers, cols // LANES)
    along_columns(cells_ref[...], weights_ref, store)


def edge_lines(now, packed_ref, lines_ref, depth):
    triple = 3.0 * now
    empty = jnp.zeros((8, LANES), jnp.float32)
    for layer in range(depth):
        at = layer * 8
        here = triple[at : at + 8]
        before = now[at - 8 : at] if layer > 0 else empty
        after = now[at + 8 : at + 16] if layer + 1 < depth else empty
        line = jnp.concatenate([before + here, empty], axis=0)
        packed_ref[2 * at : 2 * at + 16, :] = line.astype(jnp.bfloat16)
        lines_ref[at : at + 8, :] = rounded(after + here)


def render_pair(along_refs, packed_refs, lines_refs, rows_ref, flip, layers):
    sub_at = lax.broadcasted_iota(jnp.int32, (8, LANES), 0)
    top = sub_at == 0
    bottom = sub_at == 7

    def one_slab(position, image):
        slab = position ^ flip
        along_at = pl.ds(pl.multiple_of(slab * (layers * 64), 64), (layers + 2) * 64)
        packed_at = pl.ds(pl.multiple_of(slab * (layers * 16), 16), layers * 16)
        lines_at = pl.ds(pl.multiple_of(slab * (layers * 8), 8), layers * 8 + 8)
        views = [ref.at[along_at, :] for ref in along_refs]
        packed = [ref.at[packed_at, :] for ref in packed_refs]
        lines = [ref.at[lines_at, :] for ref in lines_refs]

        def layer_rows(view, layer, channel):
            base = (layer * 4 + channel) * 16
            return view[base : base + 16, :]

        def both(pieces):
            return jnp.concatenate(pieces, axis=1)

        def blend(image, samples):
            updated = []
            for tile in range(2):
                clear = [1.0 - value for value in image[tile][3]]
                updated.append(
                    [
                        [image[tile][c][i] + clear[i] * samples[tile][c][i] for i in range(4)]
                        for c in range(4)
                    ]
                )
            return updated

        for z in range(layers):
            triple = [[3.0 * layer_rows(v, z + 1, c) for c in range(4)] for v in views]
            mixed = [
                both(
                    [
                        (layer_rows(v, z, c) + t[c]).astype(jnp.bfloat16)
                        for v, t in zip(views, triple)
                    ]
                )
                for c in range(4)
            ]
            mixed.append(both([line[z * 16 : z * 16 + 16, :] for line in packed]))
            even = jnp.dot(
                rows_ref[...], jnp.concatenate(mixed, axis=0), preferred_element_type=jnp.float32
            )
            even = [
                [
                    [
                        even[c * 32 + i * 8 : c * 32 + i * 8 + 8, tile * LANES : (tile + 1) * LANES]
                        for i in range(4)
                    ]
                    for c in range(4)
                ]
                for tile in range(2)
            ]
            odd = []
            for tile in range(2):
                odd.append([])
                for c in range(4):
                    value = rounded(layer_rows(views[tile], z + 2, c) + triple[tile][c])
                    low, high = value[0:8], value[8:16]
                    above = lines[tile][pl.ds(z * 8 + c, 8, stride=0), :]
                    below = lines[tile][pl.ds(z * 8 + 4 + c, 8, stride=0), :]
                    before = jnp.where(top, above, pltpu.roll(high, 1, 0))
                    after = jnp.where(bottom, below, pltpu.roll(low, 7, 0))
                    low_centre = 3.0 * low
                    high_centre = 3.0 * high
                    odd[tile].append(
                        [before + low_centre, low_centre + high, low + high_centre, high_centre + after]
                    )
            image = blend(blend(image, even), odd)
        return image

    zero = jnp.zeros((8, LANES), jnp.float32)
    image = [[[zero] * 4 for _ in range(4)] for _ in range(2)]
    return lax.fori_loop(0, 2, one_slab, image)


def fill_rows(rows_ref):
    m = lax.broadcasted_iota(jnp.int32, rows_ref.shape, 0)
    k = lax.broadcasted_iota(jnp.int32, rows_ref.shape, 1)
    row = 4 * (m & 7) + (lax.shift_right_logical(m, 3) & 3)
    centre = lax.shift_right_logical(row, 1)
    beside = centre - 1 + 2 * (row & 1)
    own = k < 64
    k_channel = jnp.where(own, lax.shift_right_logical(k, 4), k & 3)
    k_row = 2 * (k & 7) + (lax.shift_right_logical(k, 3) & 1)
    k_row = jnp.where(own, k_row, jnp.where(k < 68, -1, jnp.where(k < 72, 16, 99)))
    same = k_channel == lax.shift_right_logical(m, 5)
    value = jnp.where(k_row == centre, 3.0, jnp.where(k_row == beside, 1.0, 0.0))
    rows_ref[...] = jnp.where(same, value, 0.0).astype(jnp.bfloat16)


def tiles_kernel(
    flip_ref, tables_ref, weights_ref, bulk_ref, inside_ref, second_ref, first_ref, ends_ref, mix_ref,
    along_ref, image_ref, mine_ref, cells_ref, packed_ref, lines_ref,
):
    layers, cols = inside_ref.shape
    depth = 2 * layers
    tiles = 2 * cols // LANES
    me = lax.axis_index("bz")
    front = me == 0
    tables = read_tables(tables_ref)
    for slab in range(2):
        inside = jnp.where(me == slab, inside_ref[...], bulk_ref[2 * layers])
        near = near_words(slab, first_ref, second_ref)
        for side in range(2):
            use_near = front if side == 0 else jnp.logical_not(front)
            words = jnp.where(use_near, near, inside)
            for t in range(cols // LANES):
                values = cell_values(
                    *unpack_words(words[:, t * LANES : (t + 1) * LANES]), tables, float(depth)
                )
                for channel in range(4):
                    at = pl.ds(slab * layers * 8 + side * 4 + channel, layers, stride=8)
                    cells_ref[t, at, :] = values[channel]
        values = cell_values(*unpack_words(ends_ref[slab]), tables, float(depth))
        for channel in range(4):
            mine_ref[slab * 4 + channel] = 3.0 * rounded(values[channel])
    edge = rounded(
        sum(
            jnp.dot(
                cells_ref[t, 0 : 8 * depth].astype(jnp.bfloat16),
                weights_ref[t * LANES : (t + 1) * LANES, :],
                preferred_element_type=jnp.float32,
            )
            for t in range(cols // LANES)
        )
    )
    for tile in range(tiles):
        now = edge[:, tile * LANES : (tile + 1) * LANES]
        edge_lines(now, packed_ref.at[tile], lines_ref.at[tile], depth)

    def one_pair(pair, carry):
        at = [2 * pair, 2 * pair + 1]
        image = render_pair(
            [along_ref.at[tile] for tile in at],
            [packed_ref.at[tile] for tile in at],
            [lines_ref.at[tile] for tile in at],
            mix_ref,
            flip_ref[0],
            layers,
        )
        for index, tile in enumerate(at):
            for channel in range(4):
                for i in range(4):
                    image_ref[tile, channel, pl.ds(i, 8, stride=4), :] = image[index][channel][i]
        return carry

    lax.fori_loop(0, tiles // 2, one_pair, 0)


def edge_kernel(
    flip_ref, tables_ref, beside_ref, across_ref, mine_ref, image_ref,
    out_ref, samples_ref, final_ref, turned_ref, fixed_ref, sems,
):
    rows = out_ref.shape[1]
    cols = out_ref.shape[2] // 2
    half = rows // 2
    layers = beside_ref.shape[1]
    tiles = 2 * cols // LANES
    middle = LANES // 2
    front = lax.axis_index("bz") == 0
    start = pl.multiple_of(lax.axis_index("bz") * half, half)
    me_x = lax.axis_index("bx")
    even_x = lax.rem(me_x, 2) == 0
    tables = read_tables(tables_ref)

    def to_out(tile, source):
        lanes = pl.ds(tile * LANES, LANES)
        return pltpu.make_async_copy(
            source.at[:, pl.ds(0, rows), :], out_ref.at[:, :, lanes], sems.at[tile]
        )

    copies = [to_out(tile, image_ref.at[tile]) for tile in range(1, tiles - 1)]
    for copy in copies:
        copy.start()
    lane_at = lax.broadcasted_iota(jnp.int32, (layers, LANES), 1)
    layer_at = lax.broadcasted_iota(jnp.int32, (layers, LANES), 0)
    first_lane = (lane_at & (middle - 1)) == 0
    along = [[], []]
    for slab in range(2):
        right = jnp.where(even_x, beside_ref[slab], across_ref[slab])
        left = jnp.where(even_x, across_ref[slab], beside_ref[slab])
        right = jnp.where(me_x + 1 < lax.axis_size("bx"), right, 0)
        left = jnp.where(me_x > 0, left, 0)
        words = pltpu.roll(jnp.where(lane_at < middle, right, left), middle, 1)
        halo = cell_values(*unpack_words(words), tables, float(2 * layers))
        for channel in range(4):
            along[slab].append(rounded(mine_ref[slab * 4 + channel] + rounded(halo[channel])))
    for channel in range(4):
        front_part, back_part = along[0][channel], along[1][channel]
        down = [pltpu.roll(front_part, 1, 0), pltpu.roll(back_part, 1, 0)]
        up = [pltpu.roll(front_part, layers - 1, 0), pltpu.roll(back_part, layers - 1, 0)]
        is_first, is_last = layer_at == 0, layer_at == layers - 1
        before = [jnp.where(is_first, 0.0, down[0]), jnp.where(is_first, down[0], down[1])]
        after = [jnp.where(is_last, up[1], up[0]), jnp.where(is_last, 0.0, up[1])]
        for slab in range(2):
            triple = 3.0 * along[slab][channel]
            for parity, other in enumerate((before[slab], after[slab])):
                mixed = rounded(other + triple)
                centre = 3.0 * mixed
                above = pltpu.roll(mixed, 1, 1)
                near = pltpu.roll(mixed, LANES - rows, 1)
                above = jnp.where(first_lane, jnp.where(front, near, above), above)
                below = pltpu.roll(mixed, LANES - 1, 1)
                for odd, value in enumerate((above + centre, centre + below)):
                    at = (parity * 2 + odd) * 4 + channel
                    samples_ref[slab, at, 0:layers, :] = value

    def over_some(slab, layers_at):
        zero = jnp.zeros((8, LANES), jnp.float32)
        image = [[zero] * 4 for _ in range(2)]
        for z in layers_at:
            for parity in range(2):
                clear = [1.0 - image[odd][3] for odd in range(2)]
                image = [
                    [
                        image[odd][channel]
                        + clear[odd]
                        * samples_ref[slab, (parity * 2 + odd) * 4 + channel, pl.ds(z, 8, stride=0), :]
                        for channel in range(4)
                    ]
                    for odd in range(2)
                ]
        return image

    def over(in_front, behind):
        return [
            [top + (1.0 - tops[3]) * low for top, low in zip(tops, lows)]
            for tops, lows in zip(in_front, behind)
        ]

    slabs = [
        over(
            over_some(slab, range(layers // 2)), over_some(slab, range(layers // 2, layers))
        )
        for slab in range(2)
    ]
    in_order = flip_ref[0] == 0
    image = over(
        *[
            [
                [jnp.where(in_order, x, y) for x, y in zip(xs, ys)]
                for xs, ys in zip(slabs[at], slabs[1 - at])
            ]
            for at in range(2)
        ]
    )
    for odd in range(2):
        for channel in range(4):
            at = odd * 4 + channel
            final_ref[at : at + 1, :] = image[odd][channel][0:1]
    turned_ref[:, 0:8] = final_ref[...].T
    wide = lax.broadcasted_iota(jnp.int32, (half, LANES), 1)
    for index, tile in enumerate((0, tiles - 1)):
        place = wide == index * (LANES - 1)
        turned = turned_ref[pl.ds(start + index * middle, half), :]
        for channel in range(4):
            for odd in range(2):
                at = pl.ds(odd, half, stride=2)
                column = odd * 4 + channel
                fixed_ref[index, channel, at, :] = jnp.where(
                    place, turned[:, column : column + 1], image_ref[tile, channel, at, :]
                )
        copies.append(to_out(tile, fixed_ref.at[index]))
        copies[-1].start()
    for copy in copies:
        copy.wait()


def two_slab_device(density, bin_index, tf_colour, tf_extinction, slab_rank):
    layers, rows, cols = density.shape
    half = rows // 2
    tiles = 2 * cols // LANES
    size = layers * 4 * half
    count_y, count_x = lax.axis_size("by"), lax.axis_size("bx")
    f32, bf16, i32 = jnp.float32, jnp.bfloat16, jnp.int32

    def call(kernel, name, out_shape, time, scratch_shapes=(), in_specs=None, out_specs=None, aliases={}):
        def run(*operands):
            return pl.pallas_call(
                kernel,
                out_shape=out_shape,
                in_specs=in_specs or [VMEM] * len(operands),
                out_specs=out_specs
                or ((VMEM,) * len(out_shape) if isinstance(out_shape, tuple) else VMEM),
                scratch_shapes=scratch_shapes,
                input_output_aliases=aliases,
                compiler_params=pltpu.CompilerParams(vmem_limit_bytes=16 * 1024 * 1024),
                cost_estimate=cost(time),
                name=name,
            )(*operands)

        return run

    def both(route):
        return route + [(target, source) for source, target in route]

    blocks = (layers, cols // LANES, rows + 8, LANES)
    row = pltpu.VMEM((layers, cols), i32)
    smem = pl.BlockSpec(memory_space=pltpu.SMEM)
    inputs = [
        pltpu.with_memory_space_constraint(x, pltpu.HBM)
        for x in (slab_rank, density, bin_index, tf_colour, tf_extinction)
    ]
    flip, first, second, bulk, inside, dense, index, tables = call(
        stage_kernel,
        "stage_block",
        (
            pltpu.SMEM((1,), i32),
            row,
            row,
            pltpu.VMEM((2 * layers + 1, 8, cols), i32),
            row,
            pltpu.VMEM(blocks, f32),
            pltpu.VMEM(blocks, i32),
            pltpu.VMEM((8, 8, LANES), f32),
        ),
        1.2,
        in_specs=[smem] + [VMEM] * 4,
        out_specs=(smem,) + (VMEM,) * 7,
    )(*inputs)
    def place(z, y, x):
        return (z * count_y + y) * count_x + x

    steps = range(count_y - 1)
    ring = [(place(0, y, 0), place(0, y + 1, 0)) for y in steps]
    ring += [(place(1, y + 1, 0), place(1, y, 0)) for y in steps]
    ring += [(place(0, count_y - 1, 0), place(1, count_y - 1, 0)), (place(1, 0, 0), place(0, 0, 0))]
    ring = [(source + x, target + x) for source, target in ring for x in range(count_x)]
    diagonal = [(place(1, y, x), place(0, y + 1, x)) for y in steps for x in range(count_x)]
    for z, y in ((0, 0), (1, count_y - 1)):
        diagonal += [(place(z, y, x), place(z, y, x + 1)) for x in range(0, count_x, 2)]
    axes = ("bz", "by", "bx")
    bulk = lax.ppermute(bulk, "bz", [(0, 1), (1, 0)])
    first = lax.ppermute(first, axes, ring)
    second = lax.ppermute(second, axes, both(diagonal))

    cells, weights, mix, columns = call(
        cells_kernel,
        "own_cells",
        (
            pltpu.VMEM((size, cols), bf16),
            pltpu.VMEM((cols, 2 * cols), bf16),
            pltpu.VMEM((128, 80), bf16),
            pltpu.VMEM((layers, LANES), i32),
        ),
        0.5,
    )(dense, index, inside, tables)
    whole = pltpu.VMEM((tiles, 2 * size + 2 * 4 * half, LANES), f32)
    along = call(own_kernel, "own_slab", whole, 0.4)(cells, weights)
    along, other_columns = call(
        functools.partial(other_kernel, rows),
        "other_slab",
        (whole, pltpu.VMEM((layers, LANES), i32)),
        0.8,
        [pltpu.VMEM((size, cols), bf16)],
        aliases={3: 0},
    )(bulk, tables, weights, along)
    ends = call(
        functools.partial(side_kernel, rows), "side_columns", pltpu.VMEM((2, layers, LANES), i32), 0.1
    )(columns, other_columns, second, first)
    pairs = [(x, x + 1) for x in range(0, count_x, 2)]
    cross = [(x, (x + 1) % count_x) for x in range(1, count_x, 2)]
    beside = lax.ppermute(ends, "bx", both(pairs))
    across = lax.ppermute(ends, "bx", both(cross))
    image, mine = call(
        tiles_kernel,
        "render_tiles",
        (pltpu.VMEM((tiles, 4, rows + 8, LANES), f32), pltpu.VMEM((8, layers, LANES), f32)),
        2.0,
        [
            pltpu.VMEM((cols // LANES, 16 * layers + 8, LANES), f32),
            pltpu.VMEM((tiles, 32 * layers, LANES), bf16),
            pltpu.VMEM((tiles, 16 * layers + 8, LANES), f32),
        ],
        [smem] + [VMEM] * 9,
    )(flip, tables, weights, bulk, inside, second, first, ends, mix, along)
    return call(
        edge_kernel,
        "edge_columns",
        jax.ShapeDtypeStruct((4, rows, 2 * cols), f32),
        1.0,
        [
            pltpu.VMEM((2, 16, 2 * layers, LANES), f32),
            pltpu.VMEM((8, LANES), f32),
            pltpu.VMEM((LANES, LANES), f32),
            pltpu.VMEM((2, 4, rows + 8, LANES), f32),
            pltpu.SemaphoreType.DMA((tiles,)),
        ],
        [smem] + [VMEM] * 5,
        pl.BlockSpec(memory_space=pltpu.HBM),
    )(flip, tables, beside, across, mine, image)


def on_device(density, bin_index, tf_colour, tf_extinction, slab_rank):
    if lax.axis_size("bz") == 2:
        return two_slab_device(density, bin_index, tf_colour, tf_extinction, slab_rank)
    return general_device(density, bin_index, tf_colour, tf_extinction, slab_rank)


def solution(mesh):
    return jax.shard_map(
        on_device,
        mesh=mesh,
        in_specs=(P("bz", "by", "bx"), P("bz", "by", "bx"), P(), P(), P()),
        out_specs=P(None, ("by", "bz"), "bx"),
        check_vma=False,
    )
```

```python
import functools

import jax
import jax.numpy as jnp
from jax import lax
from jax.experimental import pallas as pl
from jax.experimental.pallas import tpu as pltpu
from jax.sharding import PartitionSpec as P


def with_halo(block, sides, width):
    for axis, dim in sides:
        count = lax.axis_size(axis)
        forward = [(i, i + 1) for i in range(count - 1)]
        backward = [(target, source) for source, target in forward]
        low = lax.ppermute(
            lax.slice_in_dim(block, block.shape[dim] - width, None, axis=dim), axis, forward
        )
        high = lax.ppermute(lax.slice_in_dim(block, 0, width, axis=dim), axis, backward)
        block = jnp.concatenate([low, block, high], axis=dim)
    return block


def partner_2(block, axis, stride):
    count = lax.axis_size(axis)
    route = []
    for low in range(count):
        high = low | 1 << stride
        if high != low and high < count:
            route += [(low, high), (high, low)]
    return lax.ppermute(block, axis, route)


def resample_table(length):
    row_index = lax.broadcasted_iota(jnp.int32, (2 * length, length + 2), 0)
    col_index = lax.broadcasted_iota(jnp.int32, (2 * length, length + 2), 1)
    centre = row_index // 2
    parity = row_index % 2
    weights_table = jnp.where(col_index == centre + 1, 0.75, 0.0)
    weights_table = weights_table + jnp.where((col_index == centre) & (parity == 0), 0.25, 0.0)
    weights_table = weights_table + jnp.where((col_index == centre + 2) & (parity == 1), 0.25, 0.0)
    return weights_table.astype(jnp.bfloat16)


def blend_over(in_front, behind):
    return in_front + (1.0 - in_front[3])[None] * behind


def classify(density, bin_index, tf_colour, tf_extinction, total_depth):
    depth_cells, height_cells, width_cells = density.shape
    lookup = jnp.concatenate([tf_colour, tf_extinction[None, :]], axis=0)
    table_size = lookup.shape[1]
    bin_rows = lax.broadcasted_iota(jnp.int32, (table_size, 1), 0)
    flat_bins = bin_index.reshape(depth_cells, height_cells * width_cells)
    flat_density = density.reshape(depth_cells, height_cells * width_cells)

    def one_layer(layer, result):
        layer_bins = lax.dynamic_index_in_dim(flat_bins, layer, 0, keepdims=True)
        layer_density = lax.dynamic_index_in_dim(flat_density, layer, 0, keepdims=False)
        one_hot = (layer_bins == bin_rows).astype(jnp.bfloat16)
        values = jnp.dot(lookup, one_hot, preferred_element_type=jnp.float32)
        opacity = 1.0 - jnp.exp(-values[3] * layer_density / total_depth)
        cells = jnp.concatenate([values[:3] * opacity[None], opacity[None]], axis=0).astype(
            jnp.bfloat16
        )
        return lax.dynamic_update_slice_in_dim(result, cells[:, None], layer, 1)

    start_cells = jnp.zeros((4, depth_cells, height_cells * width_cells), jnp.bfloat16)
    classified = lax.fori_loop(0, depth_cells, one_layer, start_cells)
    return classified.reshape(4, depth_cells, height_cells, width_cells)


def general_device(density, bin_index, tf_colour, tf_extinction, slab_rank):
    slab_count = lax.axis_size("bz")
    depth_cells, height_cells, width_cells = density.shape
    total_depth = float(depth_cells * slab_count)
    colour_cells = classify(density, bin_index, tf_colour, tf_extinction, total_depth)
    padded = with_halo(colour_cells, (("bz", 1), ("by", 2), ("bx", 3)), 1)
    along_x = jnp.einsum(
        "czyq,pq->czyp", padded, resample_table(width_cells), preferred_element_type=jnp.float32
    ).astype(jnp.bfloat16)
    y_table = resample_table(height_cells)

    def add_sample(sample_index, image_now):
        centre = sample_index // 2
        parity = sample_index % 2
        layers = lax.dynamic_slice_in_dim(along_x, centre, 3, 1).astype(jnp.float32)
        lower_weight = jnp.where(parity == 0, 0.25, 0.0)
        upper_weight = jnp.where(parity == 1, 0.25, 0.0)
        mixed_layer = (
            lower_weight * layers[:, 0] + 0.75 * layers[:, 1] + upper_weight * layers[:, 2]
        ).astype(jnp.bfloat16)
        sample = jnp.einsum("qy,cyp->cqp", y_table, mixed_layer, preferred_element_type=jnp.float32)
        return blend_over(image_now, sample)

    start_image = jnp.zeros((4, 2 * height_cells, 2 * width_cells), jnp.float32)
    slab_image = lax.fori_loop(0, 2 * depth_cells, add_sample, start_image)
    rows_piece = 2 * height_cells // slab_count
    my_index = lax.axis_index("bz")
    bit_levels = slab_count.bit_length() - 1
    composite = slab_image.reshape((4,) + (2,) * bit_levels + (rows_piece, 2 * width_cells))
    my_rank = lax.dynamic_index_in_dim(slab_rank, my_index, 0, keepdims=False)
    for level in range(bit_levels):
        position = bit_levels - level
        my_bit = my_index // 2**level % 2
        kept_half = lax.dynamic_index_in_dim(composite, my_bit, position, keepdims=False)
        outgoing = lax.dynamic_index_in_dim(composite, 1 - my_bit, position, keepdims=False)
        incoming = partner_2(outgoing, "bz", level)
        partner = my_index + (1 - 2 * my_bit) * 2**level
        partner_rank = lax.dynamic_index_in_dim(slab_rank, partner, 0, keepdims=False)
        mine_first = my_rank < partner_rank
        composite = blend_over(
            jnp.where(mine_first, kept_half, incoming), jnp.where(mine_first, incoming, kept_half)
        )
    return composite


LANES = 128
LEVELS = 65535.0
VMEM = pl.BlockSpec(memory_space=pltpu.VMEM)


def pack_words(density, bins):
    level = (density * LEVELS + 0.5).astype(jnp.int32)
    return lax.shift_left(level, 16) | bins


def unpack_words(words):
    density = lax.shift_right_logical(words, 16).astype(jnp.float32) * (1.0 / LEVELS)
    return density, words & 0xFFFF


def cell_values(density, bins, tables, depth):
    low_bits = bins & (LANES - 1)
    upper = bins >= LANES

    def pick(channel):
        first, second = tables[channel]
        return jnp.where(
            upper,
            jnp.take_along_axis(second, low_bits, axis=1, mode="promise_in_bounds"),
            jnp.take_along_axis(first, low_bits, axis=1, mode="promise_in_bounds"),
        )

    opacity = (1.0 - jnp.exp(-pick(3) * density / depth)) * (1.0 / 64.0)
    return [pick(0) * opacity, pick(1) * opacity, pick(2) * opacity, opacity]


def read_tables(tables_ref):
    return [[tables_ref[2 * channel + half] for half in range(2)] for channel in range(4)]


def cost(microseconds):
    return pl.CostEstimate(
        flops=int(1e9 * microseconds), bytes_accessed=int(3.6e6 * microseconds), transcendentals=0
    )


def stage_kernel(
    rank_ref, density_ref, bins_ref, colour_ref, extinction_ref,
    flip_ref, first_ref, second_ref, bulk_ref, inside_ref, dense_ref, index_ref, tables_ref,
):
    flip_ref[0] = rank_ref[0]
    layers, rows, cols = density_ref.shape
    front = lax.axis_index("bz") == 0
    for z in range(layers):
        top, bottom = [
            pack_words(density_ref[z, r : r + 1, :], bins_ref[z, r : r + 1, :]) for r in (0, rows - 1)
        ]
        first_ref[z : z + 1, :] = jnp.where(front, bottom, top)
        second_ref[z : z + 1, :] = jnp.where(front, top, bottom)
        for tile in range(cols // LANES):
            lanes = slice(tile * LANES, (tile + 1) * LANES)
            dense_ref[z, tile, 0:rows] = density_ref[z, :, lanes]
            index_ref[z, tile, 0:rows] = bins_ref[z, :, lanes]
    pack_block(dense_ref, index_ref, bulk_ref, inside_ref)
    colour = colour_ref[...].astype(jnp.float32)
    extinction = extinction_ref[...].astype(jnp.float32).reshape(1, 2 * LANES)
    for channel in range(4):
        line = extinction if channel == 3 else colour[channel : channel + 1]
        for half in range(2):
            tables_ref[2 * channel + half] = jnp.broadcast_to(
                line[:, half * LANES : (half + 1) * LANES], (8, LANES)
            )


def pack_block(dense_ref, index_ref, bulk_ref, inside_ref):
    layers, tiles, rows = dense_ref.shape[0], dense_ref.shape[1], dense_ref.shape[2] - 8
    half = rows // 2
    front = lax.axis_index("bz") == 0
    start = jnp.where(front, half, 0)
    for tile in range(tiles):
        lanes = slice(tile * LANES, (tile + 1) * LANES)
        for z in range(layers):
            for part in range(2):
                at = pl.ds(start + part, half // 2, stride=2)
                bulk_ref[2 * z + part, :, lanes] = pack_words(
                    dense_ref[z, tile, at, :], index_ref[z, tile, at, :]
                )
            line = [
                pack_words(dense_ref[z, tile, r : r + 1, :], index_ref[z, tile, r : r + 1, :])
                for r in (half - 1, half)
            ]
            bulk_ref[2 * layers, z : z + 1, lanes] = jnp.where(front, line[0], line[1])
            inside_ref[z : z + 1, lanes] = jnp.where(front, line[1], line[0])


def near_words(slab, first_ref, second_ref):
    me = lax.axis_index("bz")
    words = jnp.where(me == slab, first_ref[...], second_ref[...])
    return jnp.where(has_near(me == 0), words, 0)


def column_lines(read_words, inside, lines_ref, rows):
    layers, cols = inside.shape
    front = lax.axis_index("bz") == 0
    start = lax.axis_index("bz") * (rows // 2)
    middle = LANES // 2
    lane_at = lax.broadcasted_iota(jnp.int32, (8, LANES), 1)
    row_at = start + 2 * lax.broadcasted_iota(jnp.int32, (8, LANES), 0)
    for z in range(layers):
        line = jnp.zeros((8, LANES), jnp.int32)
        for part in range(2):
            first = read_words(z, part, 0)[:, 0:1]
            last = read_words(z, part, cols // LANES - 1)[:, LANES - 1 : LANES]
            line += jnp.where(lane_at == row_at + part, first, 0)
            line += jnp.where(lane_at == row_at + part + middle, last, 0)
        lines_ref[z : z + 1, :] = jnp.sum(line, axis=0, keepdims=True)
    beside = jnp.where(front, rows // 2, rows // 2 - 1)
    lines = jnp.where(lane_at == beside, inside[:, 0:1], lines_ref[...])
    lines_ref[...] = jnp.where(lane_at == beside + middle, inside[:, cols - 1 : cols], lines)


def side_kernel(
    rows, columns_ref, bulk_ref, second_ref, first_ref, part_ref, ends_ref, other_ref
):
    layers, _ = columns_ref.shape
    front = lax.axis_index("bz") == 0
    lane_at = lax.broadcasted_iota(jnp.int32, (layers, LANES), 1)

    def read_words(z, part, tile):
        return bulk_ref[2 * z + part, :, tile * LANES : (tile + 1) * LANES]

    column_lines(read_words, bulk_ref[2 * layers], other_ref, rows)
    for slab in range(2):
        mine = front if slab == 0 else jnp.logical_not(front)
        columns = jnp.where(mine, columns_ref[...], other_ref[...])
        near = near_words(slab, first_ref, second_ref)
        cols = near.shape[1]
        columns = jnp.where(lane_at == rows, near[:, 0:1], columns)
        ends_ref[slab] = jnp.where(
            lane_at == LANES // 2 + rows, near[:, cols - 1 : cols], columns
        )


def has_near(front):
    me_y = lax.axis_index("by")
    return jnp.where(front, me_y > 0, me_y + 1 < lax.axis_size("by"))


def fill_weights(weights_ref):
    cols = weights_ref.shape[0]
    row = lax.broadcasted_iota(jnp.int32, (cols, 2 * cols), 0)
    at = lax.broadcasted_iota(jnp.int32, (cols, 2 * cols), 1)
    centre = lax.shift_right_logical(at, 1)
    beside = centre - 1 + 2 * (at & 1)
    weights_ref[...] = jnp.where(row == centre, 3.0, jnp.where(row == beside, 1.0, 0.0)).astype(
        jnp.bfloat16
    )


def classify_rows(read_cells, tables, cells_ref, layers, tiles):
    total = float(2 * layers)
    for z in range(layers):
        for tile in range(tiles):
            even = cell_values(*read_cells(z, 0, tile), tables, total)
            odd = cell_values(*read_cells(z, 1, tile), tables, total)
            for channel in range(4):
                base = (z * 4 + channel) * 16
                block = jnp.concatenate([even[channel], odd[channel]], axis=0)
                cells_ref[base : base + 16, tile * LANES : (tile + 1) * LANES] = block.astype(jnp.bfloat16)


def rounded(value):
    return value.astype(jnp.bfloat16).astype(jnp.float32)


def cells_kernel(dense_ref, index_ref, inside_ref, tables_ref, cells_ref, weights_ref, mix_ref, lines_ref):
    layers, tiles, rows = dense_ref.shape[0], dense_ref.shape[1], dense_ref.shape[2] - 8
    half = rows // 2
    start = lax.axis_index("bz") * half
    fill_weights(weights_ref)
    fill_rows(mix_ref)

    def read_cells(z, part, tile):
        at = pl.ds(start + part, half // 2, stride=2)
        return dense_ref[z, tile, at, :], index_ref[z, tile, at, :]

    classify_rows(read_cells, read_tables(tables_ref), cells_ref, layers, tiles)
    column_lines(lambda *at: pack_words(*read_cells(*at)), inside_ref[...], lines_ref, rows)


def along_columns(cells, weights_ref, store):
    result = rounded(jnp.dot(cells, weights_ref[...], preferred_element_type=jnp.float32))
    for tile in range(result.shape[1] // LANES):
        store(tile, result[:, tile * LANES : (tile + 1) * LANES])


def own_kernel(cells_ref, weights_ref, along_ref):
    size = cells_ref.shape[0]
    pad = 64
    mine = pl.multiple_of(pad + lax.axis_index("bz") * size, pad)

    def store(tile, block):
        along_ref[tile, 0:pad, :] = jnp.zeros((pad, LANES), jnp.float32)
        along_ref[tile, pad + 2 * size : 2 * pad + 2 * size, :] = jnp.zeros((pad, LANES), jnp.float32)
        along_ref[tile, pl.ds(mine, size), :] = block

    along_columns(cells_ref[...], weights_ref, store)


def other_kernel(bulk_ref, tables_ref, weights_ref, ends_ref, own_ref, along_ref, cells_ref):
    layers = (bulk_ref.shape[0] - 1) // 2
    cols = bulk_ref.shape[2]
    size = cells_ref.shape[0]
    pad = 64
    theirs = pl.multiple_of(pad + (1 - lax.axis_index("bz")) * size, pad)

    def read_cells(z, part, tile):
        return unpack_words(bulk_ref[2 * z + part, :, tile * LANES : (tile + 1) * LANES])

    def store(tile, block):
        along_ref[tile, pl.ds(theirs, size), :] = block

    classify_rows(read_cells, read_tables(tables_ref), cells_ref, layers, cols // LANES)
    along_columns(cells_ref[...], weights_ref, store)


def edge_cells(near, inside, tables, cells_ref, front, base):
    layers, cols = near.shape
    for side in range(2):
        use_near = front if side == 0 else jnp.logical_not(front)
        words = jnp.where(use_near, near, inside)
        for t in range(cols // LANES):
            values = cell_values(
                *unpack_words(words[:, t * LANES : (t + 1) * LANES]), tables, float(2 * layers)
            )
            for channel in range(4):
                at = pl.ds(base + side * 4 + channel, layers, stride=8)
                cells_ref[t, at, :] = values[channel]


def edge_along(cells_ref, count, weights_ref):
    return rounded(
        sum(
            jnp.dot(
                cells_ref[t, 0:count].astype(jnp.bfloat16),
                weights_ref[t * LANES : (t + 1) * LANES, :],
                preferred_element_type=jnp.float32,
            )
            for t in range(cells_ref.shape[0])
        )
    )


def edge_lines(now, packed_ref, lines_ref, depth):
    triple = 3.0 * now
    empty = jnp.zeros((8, LANES), jnp.float32)
    for layer in range(depth):
        at = layer * 8
        here = triple[at : at + 8]
        before = now[at - 8 : at] if layer > 0 else empty
        after = now[at + 8 : at + 16] if layer + 1 < depth else empty
        line = jnp.concatenate([before + here, empty], axis=0)
        packed_ref[2 * at : 2 * at + 16, :] = line.astype(jnp.bfloat16)
        lines_ref[at : at + 8, :] = rounded(after + here)


def row_samples(value, above, below):
    sub_at = lax.broadcasted_iota(jnp.int32, (8, LANES), 0)
    low, high = value[0:8], value[8:16]
    before = jnp.where(sub_at == 0, above, pltpu.roll(high, 1, 0))
    after = jnp.where(sub_at == 7, below, pltpu.roll(low, 7, 0))
    low_centre = 3.0 * low
    high_centre = 3.0 * high
    return [before + low_centre, low_centre + high, low + high_centre, high_centre + after]


def slab_pair(
    along_refs, packed_refs, lines_refs, rows_ref, slab, lines_slab, layers, keep_first=None, keep_last=None
):
    along_at = pl.ds(pl.multiple_of(slab * (layers * 64), 64), (layers + 2) * 64)
    packed_at = pl.ds(pl.multiple_of(lines_slab * (layers * 16), 16), layers * 16)
    lines_at = pl.ds(pl.multiple_of(lines_slab * (layers * 8), 8), layers * 8 + 8)
    views = [ref.at[along_at, :] for ref in along_refs]
    packed = [ref.at[packed_at, :] for ref in packed_refs]
    lines = [ref.at[lines_at, :] for ref in lines_refs]

    def layer_rows(view, layer, channel):
        base = (layer * 4 + channel) * 16
        return view[base : base + 16, :]

    def both(pieces):
        return jnp.concatenate(pieces, axis=1)

    def blend(image, samples, keep):
        updated = []
        for tile in range(2):
            clear = [1.0 - value for value in image[tile][3]]
            updated.append([])
            for c in range(4):
                values = samples[tile][c]
                if keep is not None:
                    values = [jnp.where(keep, value, 0.0) for value in values]
                updated[tile].append([image[tile][c][i] + clear[i] * values[i] for i in range(4)])
        return updated

    zero = jnp.zeros((8, LANES), jnp.float32)
    image = [[[zero] * 4 for _ in range(4)] for _ in range(2)]
    for z in range(layers):
        triple = [[3.0 * layer_rows(v, z + 1, c) for c in range(4)] for v in views]
        mixed = [
            both([(layer_rows(v, z, c) + t[c]).astype(jnp.bfloat16) for v, t in zip(views, triple)])
            for c in range(4)
        ]
        mixed.append(both([line[z * 16 : z * 16 + 16, :] for line in packed]))
        product = jnp.dot(
            rows_ref[...], jnp.concatenate(mixed, axis=0), preferred_element_type=jnp.float32
        )
        even, odd = [], []
        for tile in range(2):
            lanes = slice(tile * LANES, (tile + 1) * LANES)
            even.append(
                [
                    [product[c * 32 + i * 8 : c * 32 + i * 8 + 8, lanes] for i in range(4)]
                    for c in range(4)
                ]
            )
            odd.append([])
            for c in range(4):
                value = rounded(layer_rows(views[tile], z + 2, c) + triple[tile][c])
                above = lines[tile][pl.ds(z * 8 + c, 8, stride=0), :]
                below = lines[tile][pl.ds(z * 8 + 4 + c, 8, stride=0), :]
                odd[tile].append(row_samples(value, above, below))
        image = blend(image, even, keep_first if z == 0 else None)
        image = blend(image, odd, keep_last if z == layers - 1 else None)
    return image


def joined(first, in_front, behind):
    top = [[jnp.where(first, x, y) for x, y in zip(a, b)] for a, b in zip(in_front, behind)]
    low = [[jnp.where(first, y, x) for x, y in zip(a, b)] for a, b in zip(in_front, behind)]
    clear = [1.0 - value for value in top[3]]
    return [[top[c][i] + clear[i] * low[c][i] for i in range(4)] for c in range(4)]


def own_tiles_kernel(
    tables_ref, weights_ref, inside_ref, mix_ref, along_ref, part_ref, cells_ref, packed_ref, lines_ref
):
    layers, cols = inside_ref.shape
    me = lax.axis_index("bz")
    front = me == 0
    inside = inside_ref[...]
    edge_cells(jnp.zeros_like(inside), inside, read_tables(tables_ref), cells_ref, front, 0)
    edge = edge_along(cells_ref, 8 * layers, weights_ref)
    tiles = 2 * cols // LANES
    for tile in range(tiles):
        now = edge[:, tile * LANES : (tile + 1) * LANES]
        edge_lines(now, packed_ref.at[tile], lines_ref.at[tile], layers)
    for pair in range(tiles // 2):
        at = [2 * pair, 2 * pair + 1]
        image = slab_pair(
            [along_ref.at[tile] for tile in at],
            [packed_ref.at[tile] for tile in at],
            [lines_ref.at[tile] for tile in at],
            mix_ref,
            me,
            0,
            layers,
            front,
            jnp.logical_not(front),
        )
        for index, tile in enumerate(at):
            for channel in range(4):
                for i in range(4):
                    part_ref[tile, channel * 4 + i] = image[index][channel][i]


def fill_rows(rows_ref):
    m = lax.broadcasted_iota(jnp.int32, rows_ref.shape, 0)
    k = lax.broadcasted_iota(jnp.int32, rows_ref.shape, 1)
    row = 4 * (m & 7) + (lax.shift_right_logical(m, 3) & 3)
    centre = lax.shift_right_logical(row, 1)
    beside = centre - 1 + 2 * (row & 1)
    own = k < 64
    k_channel = jnp.where(own, lax.shift_right_logical(k, 4), k & 3)
    k_row = 2 * (k & 7) + (lax.shift_right_logical(k, 3) & 1)
    k_row = jnp.where(own, k_row, jnp.where(k < 68, -1, jnp.where(k < 72, 16, 99)))
    same = k_channel == lax.shift_right_logical(m, 5)
    value = jnp.where(k_row == centre, 3.0, jnp.where(k_row == beside, 1.0, 0.0))
    rows_ref[...] = jnp.where(same, value, 0.0).astype(jnp.bfloat16)


def tiles_kernel(
    flip_ref, tables_ref, weights_ref, bulk_ref, inside_ref, second_ref, first_ref, ends_ref, mix_ref,
    part_ref, along_ref, image_ref, mine_ref, cells_ref, packed_ref, lines_ref, edge_ref, between_ref,
):
    layers, cols = inside_ref.shape
    depth = 2 * layers
    tiles = 2 * cols // LANES
    me = lax.axis_index("bz")
    front = me == 0
    tables = read_tables(tables_ref)
    for slab in range(2):
        inside = jnp.where(me == slab, inside_ref[...], bulk_ref[2 * layers])
        near = near_words(slab, first_ref, second_ref)
        edge_cells(near, inside, tables, cells_ref, front, slab * layers * 8)
        values = cell_values(*unpack_words(ends_ref[slab]), tables, float(depth))
        for channel in range(4):
            mine_ref[slab * 4 + channel] = 3.0 * rounded(values[channel])
    edge = edge_along(cells_ref, 8 * depth, weights_ref)
    here_at, beside_at = layers * 8 - 8, layers * 8
    empty = jnp.zeros((8, LANES), jnp.float32)
    for tile in range(tiles):
        now = edge[:, tile * LANES : (tile + 1) * LANES]
        edge_lines(now, packed_ref.at[tile], lines_ref.at[tile], depth)
        upper, lower = now[here_at : here_at + 8], now[beside_at : beside_at + 8]
        between_ref[tile, 0:8] = rounded(
            jnp.where(front, lower, upper) + 3.0 * jnp.where(front, upper, lower)
        )
        edge_ref[tile, 0:8] = empty
        edge_ref[tile, 8 : 8 * depth + 8] = now
        edge_ref[tile, 8 * depth + 8 :] = empty

    row = jnp.where(front, 0, 15)
    first_layer = me * layers
    replaced = []
    for tile in range(tiles):
        inner, outer = [], []
        for z in range(layers + 2):
            at = (first_layer + z) * 64 + row
            inner.append(along_ref[tile, pl.ds(at, 4, stride=16), :])
            both = edge_ref[tile, pl.ds(pl.multiple_of((first_layer + z) * 8, 8), 8), :]
            outer.append(jnp.where(front, both[0:4], both[4:8]))
        image = jnp.zeros((4, LANES), jnp.float32)
        for z in range(layers):
            for parity in range(2):
                beside = z + 2 * parity
                sample = rounded(outer[beside] + 3.0 * outer[z + 1]) + 3.0 * rounded(
                    inner[beside] + 3.0 * inner[z + 1]
                )
                if (z, parity) == (0, 0):
                    sample = jnp.where(front, sample, 0.0)
                if (z, parity) == (layers - 1, 1):
                    sample = jnp.where(front, 0.0, sample)
                image = image + (1.0 - image[3:4]) * sample
        replaced.append(image)

    sub_at = lax.broadcasted_iota(jnp.int32, (8, LANES), 0)
    for pair in range(tiles // 2):
        at = [2 * pair, 2 * pair + 1]
        other = slab_pair(
            [along_ref.at[tile] for tile in at],
            [packed_ref.at[tile] for tile in at],
            [lines_ref.at[tile] for tile in at],
            mix_ref,
            1 - me,
            1 - me,
            layers,
        )
        for index, tile in enumerate(at):
            here = pl.multiple_of(jnp.where(front, layers, layers + 1) * 64, 64)
            beside = pl.multiple_of(jnp.where(front, layers + 1, layers) * 64, 64)
            between, part = [], []
            for c in range(4):
                value = rounded(
                    along_ref[tile, pl.ds(beside + c * 16, 16), :]
                    + 3.0 * along_ref[tile, pl.ds(here + c * 16, 16), :]
                )
                above = between_ref[tile, pl.ds(c, 8, stride=0), :]
                below = between_ref[tile, pl.ds(c + 4, 8, stride=0), :]
                between.append(row_samples(value, above, below))
                values = [part_ref[tile, c * 4 + i] for i in range(4)]
                line = replaced[tile][c : c + 1]
                values[0] = jnp.where(sub_at == 0, jnp.where(front, line, values[0]), values[0])
                values[3] = jnp.where(sub_at == 7, jnp.where(front, values[3], line), values[3])
                part.append(values)
            mine = joined(front, part, between)
            image = joined((me ^ flip_ref[0]) == 0, mine, other[index])
            for c in range(4):
                for i in range(4):
                    image_ref[tile, c, pl.ds(i, 8, stride=4), :] = image[c][i]


def edge_kernel(
    flip_ref, tables_ref, beside_ref, across_ref, mine_ref, image_ref,
    out_ref, samples_ref, final_ref, turned_ref, fixed_ref, sems,
):
    rows = out_ref.shape[1]
    cols = out_ref.shape[2] // 2
    half = rows // 2
    layers = beside_ref.shape[1]
    tiles = 2 * cols // LANES
    middle = LANES // 2
    front = lax.axis_index("bz") == 0
    start = pl.multiple_of(lax.axis_index("bz") * half, half)
    me_x = lax.axis_index("bx")
    even_x = lax.rem(me_x, 2) == 0
    tables = read_tables(tables_ref)

    def to_out(tile, source):
        lanes = pl.ds(tile * LANES, LANES)
        return pltpu.make_async_copy(
            source.at[:, pl.ds(0, rows), :], out_ref.at[:, :, lanes], sems.at[tile]
        )

    copies = [to_out(tile, image_ref.at[tile]) for tile in range(1, tiles - 1)]
    for copy in copies:
        copy.start()
    lane_at = lax.broadcasted_iota(jnp.int32, (layers, LANES), 1)
    layer_at = lax.broadcasted_iota(jnp.int32, (layers, LANES), 0)
    first_lane = (lane_at & (middle - 1)) == 0
    along = [[], []]
    for slab in range(2):
        right = jnp.where(even_x, beside_ref[slab], across_ref[slab])
        left = jnp.where(even_x, across_ref[slab], beside_ref[slab])
        right = jnp.where(me_x + 1 < lax.axis_size("bx"), right, 0)
        left = jnp.where(me_x > 0, left, 0)
        words = pltpu.roll(jnp.where(lane_at < middle, right, left), middle, 1)
        halo = cell_values(*unpack_words(words), tables, float(2 * layers))
        for channel in range(4):
            along[slab].append(rounded(mine_ref[slab * 4 + channel] + rounded(halo[channel])))
    for channel in range(4):
        front_part, back_part = along[0][channel], along[1][channel]
        down = [pltpu.roll(front_part, 1, 0), pltpu.roll(back_part, 1, 0)]
        up = [pltpu.roll(front_part, layers - 1, 0), pltpu.roll(back_part, layers - 1, 0)]
        is_first, is_last = layer_at == 0, layer_at == layers - 1
        before = [jnp.where(is_first, 0.0, down[0]), jnp.where(is_first, down[0], down[1])]
        after = [jnp.where(is_last, up[1], up[0]), jnp.where(is_last, 0.0, up[1])]
        for slab in range(2):
            triple = 3.0 * along[slab][channel]
            for parity, other in enumerate((before[slab], after[slab])):
                mixed = rounded(other + triple)
                centre = 3.0 * mixed
                above = pltpu.roll(mixed, 1, 1)
                near = pltpu.roll(mixed, LANES - rows, 1)
                above = jnp.where(first_lane, jnp.where(front, near, above), above)
                below = pltpu.roll(mixed, LANES - 1, 1)
                for odd, value in enumerate((above + centre, centre + below)):
                    at = (parity * 2 + odd) * 4 + channel
                    samples_ref[slab, at, 0:layers, :] = value

    def over_some(slab, layers_at):
        zero = jnp.zeros((8, LANES), jnp.float32)
        image = [[zero] * 4 for _ in range(2)]
        for z in layers_at:
            for parity in range(2):
                clear = [1.0 - image[odd][3] for odd in range(2)]
                image = [
                    [
                        image[odd][channel]
                        + clear[odd]
                        * samples_ref[slab, (parity * 2 + odd) * 4 + channel, pl.ds(z, 8, stride=0), :]
                        for channel in range(4)
                    ]
                    for odd in range(2)
                ]
        return image

    def over(in_front, behind):
        return [
            [top + (1.0 - tops[3]) * low for top, low in zip(tops, lows)]
            for tops, lows in zip(in_front, behind)
        ]

    slabs = [
        over(
            over_some(slab, range(layers // 2)), over_some(slab, range(layers // 2, layers))
        )
        for slab in range(2)
    ]
    in_order = flip_ref[0] == 0
    image = over(
        *[
            [
                [jnp.where(in_order, x, y) for x, y in zip(xs, ys)]
                for xs, ys in zip(slabs[at], slabs[1 - at])
            ]
            for at in range(2)
        ]
    )
    for odd in range(2):
        for channel in range(4):
            at = odd * 4 + channel
            final_ref[at : at + 1, :] = image[odd][channel][0:1]
    turned_ref[:, 0:8] = final_ref[...].T
    wide = lax.broadcasted_iota(jnp.int32, (half, LANES), 1)
    for index, tile in enumerate((0, tiles - 1)):
        place = wide == index * (LANES - 1)
        turned = turned_ref[pl.ds(start + index * middle, half), :]
        for channel in range(4):
            for odd in range(2):
                at = pl.ds(odd, half, stride=2)
                column = odd * 4 + channel
                fixed_ref[index, channel, at, :] = jnp.where(
                    place, turned[:, column : column + 1], image_ref[tile, channel, at, :]
                )
        copies.append(to_out(tile, fixed_ref.at[index]))
        copies[-1].start()
    for copy in copies:
        copy.wait()


def two_slab_device(density, bin_index, tf_colour, tf_extinction, slab_rank):
    layers, rows, cols = density.shape
    half = rows // 2
    tiles = 2 * cols // LANES
    size = layers * 4 * half
    count_y, count_x = lax.axis_size("by"), lax.axis_size("bx")
    f32, bf16, i32 = jnp.float32, jnp.bfloat16, jnp.int32

    def call(kernel, name, out_shape, time, scratch_shapes=(), in_specs=None, out_specs=None, aliases={}):
        def run(*operands):
            return pl.pallas_call(
                kernel,
                out_shape=out_shape,
                in_specs=in_specs or [VMEM] * len(operands),
                out_specs=out_specs
                or ((VMEM,) * len(out_shape) if isinstance(out_shape, tuple) else VMEM),
                scratch_shapes=scratch_shapes,
                input_output_aliases=aliases,
                compiler_params=pltpu.CompilerParams(vmem_limit_bytes=16 * 1024 * 1024),
                cost_estimate=cost(time),
                name=name,
            )(*operands)

        return run

    def both(route):
        return route + [(target, source) for source, target in route]

    blocks = (layers, cols // LANES, rows + 8, LANES)
    row = pltpu.VMEM((layers, cols), i32)
    smem = pl.BlockSpec(memory_space=pltpu.SMEM)
    inputs = [
        pltpu.with_memory_space_constraint(x, pltpu.HBM)
        for x in (slab_rank, density, bin_index, tf_colour, tf_extinction)
    ]
    flip, first, second, bulk, inside, dense, index, tables = call(
        stage_kernel,
        "stage_block",
        (
            pltpu.SMEM((1,), i32),
            row,
            row,
            pltpu.VMEM((2 * layers + 1, 8, cols), i32),
            row,
            pltpu.VMEM(blocks, f32),
            pltpu.VMEM(blocks, i32),
            pltpu.VMEM((8, 8, LANES), f32),
        ),
        1.2,
        in_specs=[smem] + [VMEM] * 4,
        out_specs=(smem,) + (VMEM,) * 7,
    )(*inputs)
    def place(z, y, x):
        return (z * count_y + y) * count_x + x

    steps = range(count_y - 1)
    ring = [(place(0, y, 0), place(0, y + 1, 0)) for y in steps]
    ring += [(place(1, y + 1, 0), place(1, y, 0)) for y in steps]
    ring += [(place(0, count_y - 1, 0), place(1, count_y - 1, 0)), (place(1, 0, 0), place(0, 0, 0))]
    ring = [(source + x, target + x) for source, target in ring for x in range(count_x)]
    diagonal = [(place(1, y, x), place(0, y + 1, x)) for y in steps for x in range(count_x)]
    for z, y in ((0, 0), (1, count_y - 1)):
        diagonal += [(place(z, y, x), place(z, y, x + 1)) for x in range(0, count_x, 2)]
    axes = ("bz", "by", "bx")
    bulk = lax.ppermute(bulk, "bz", [(0, 1), (1, 0)])
    first = lax.ppermute(first, axes, ring)
    second = lax.ppermute(second, axes, both(diagonal))

    cells, weights, mix, columns = call(
        cells_kernel,
        "own_cells",
        (
            pltpu.VMEM((size, cols), bf16),
            pltpu.VMEM((cols, 2 * cols), bf16),
            pltpu.VMEM((128, 80), bf16),
            pltpu.VMEM((layers, LANES), i32),
        ),
        0.5,
    )(dense, index, inside, tables)
    whole = pltpu.VMEM((tiles, 2 * size + 3 * 4 * half, LANES), f32)
    along = call(own_kernel, "own_slab", whole, 0.4)(cells, weights)
    edges = pltpu.VMEM((cols // LANES, 16 * layers + 8, LANES), f32)
    packed = pltpu.VMEM((tiles, 32 * layers, LANES), bf16)
    lines = pltpu.VMEM((tiles, 16 * layers + 8, LANES), f32)
    part = call(
        own_tiles_kernel,
        "own_tiles",
        pltpu.VMEM((tiles, 16, 8, LANES), f32),
        0.1,
        [edges, packed, lines],
    )(tables, weights, inside, mix, along)
    ends = call(
        functools.partial(side_kernel, rows),
        "side_columns",
        pltpu.VMEM((2, layers, LANES), i32),
        0.1,
        [pltpu.VMEM((layers, LANES), i32)],
    )(columns, bulk, second, first, part)
    pairs = [(x, x + 1) for x in range(0, count_x, 2)]
    cross = [(x, (x + 1) % count_x) for x in range(1, count_x, 2)]
    beside = lax.ppermute(ends, "bx", both(pairs))
    across = lax.ppermute(ends, "bx", both(cross))
    along = call(other_kernel, "other_slab", whole, 0.8, [pltpu.VMEM((size, cols), bf16)], aliases={4: 0})(
        bulk, tables, weights, ends, along
    )
    image, mine = call(
        tiles_kernel,
        "render_tiles",
        (pltpu.VMEM((tiles, 4, rows + 8, LANES), f32), pltpu.VMEM((8, layers, LANES), f32)),
        2.0,
        [
            edges,
            packed,
            lines,
            pltpu.VMEM((tiles, 16 * layers + 16, LANES), f32),
            pltpu.VMEM((tiles, 16, LANES), f32),
        ],
        [smem] + [VMEM] * 10,
    )(flip, tables, weights, bulk, inside, second, first, ends, mix, part, along)
    return call(
        edge_kernel,
        "edge_columns",
        jax.ShapeDtypeStruct((4, rows, 2 * cols), f32),
        1.0,
        [
            pltpu.VMEM((2, 16, 2 * layers, LANES), f32),
            pltpu.VMEM((8, LANES), f32),
            pltpu.VMEM((LANES, LANES), f32),
            pltpu.VMEM((2, 4, rows + 8, LANES), f32),
            pltpu.SemaphoreType.DMA((tiles,)),
        ],
        [smem] + [VMEM] * 5,
        pl.BlockSpec(memory_space=pltpu.HBM),
    )(flip, tables, beside, across, mine, image)


def on_device(density, bin_index, tf_colour, tf_extinction, slab_rank):
    if lax.axis_size("bz") == 2:
        return two_slab_device(density, bin_index, tf_colour, tf_extinction, slab_rank)
    return general_device(density, bin_index, tf_colour, tf_extinction, slab_rank)


def solution(mesh):
    return jax.shard_map(
        on_device,
        mesh=mesh,
        in_specs=(P("bz", "by", "bx"), P("bz", "by", "bx"), P(), P(), P()),
        out_specs=P(None, ("by", "bz"), "bx"),
        check_vma=False,
    )
```

```python
import functools

import jax
import jax.numpy as jnp
from jax import lax
from jax.experimental import pallas as pl
from jax.experimental.pallas import tpu as pltpu
from jax.sharding import PartitionSpec as P


def with_halo(block, sides, width):
    for axis, dim in sides:
        count = lax.axis_size(axis)
        forward = [(i, i + 1) for i in range(count - 1)]
        backward = [(target, source) for source, target in forward]
        low = lax.ppermute(
            lax.slice_in_dim(block, block.shape[dim] - width, None, axis=dim), axis, forward
        )
        high = lax.ppermute(lax.slice_in_dim(block, 0, width, axis=dim), axis, backward)
        block = jnp.concatenate([low, block, high], axis=dim)
    return block


def partner_2(block, axis, stride):
    count = lax.axis_size(axis)
    route = []
    for low in range(count):
        high = low | 1 << stride
        if high != low and high < count:
            route += [(low, high), (high, low)]
    return lax.ppermute(block, axis, route)


def resample_table(length):
    row_index = lax.broadcasted_iota(jnp.int32, (2 * length, length + 2), 0)
    col_index = lax.broadcasted_iota(jnp.int32, (2 * length, length + 2), 1)
    centre = row_index // 2
    parity = row_index % 2
    weights_table = jnp.where(col_index == centre + 1, 0.75, 0.0)
    weights_table = weights_table + jnp.where((col_index == centre) & (parity == 0), 0.25, 0.0)
    weights_table = weights_table + jnp.where((col_index == centre + 2) & (parity == 1), 0.25, 0.0)
    return weights_table.astype(jnp.bfloat16)


def blend_over(in_front, behind):
    return in_front + (1.0 - in_front[3])[None] * behind


def classify(density, bin_index, tf_colour, tf_extinction, total_depth):
    depth_cells, height_cells, width_cells = density.shape
    lookup = jnp.concatenate([tf_colour, tf_extinction[None, :]], axis=0)
    table_size = lookup.shape[1]
    bin_rows = lax.broadcasted_iota(jnp.int32, (table_size, 1), 0)
    flat_bins = bin_index.reshape(depth_cells, height_cells * width_cells)
    flat_density = density.reshape(depth_cells, height_cells * width_cells)

    def one_layer(layer, result):
        layer_bins = lax.dynamic_index_in_dim(flat_bins, layer, 0, keepdims=True)
        layer_density = lax.dynamic_index_in_dim(flat_density, layer, 0, keepdims=False)
        one_hot = (layer_bins == bin_rows).astype(jnp.bfloat16)
        values = jnp.dot(lookup, one_hot, preferred_element_type=jnp.float32)
        opacity = 1.0 - jnp.exp(-values[3] * layer_density / total_depth)
        cells = jnp.concatenate([values[:3] * opacity[None], opacity[None]], axis=0).astype(
            jnp.bfloat16
        )
        return lax.dynamic_update_slice_in_dim(result, cells[:, None], layer, 1)

    start_cells = jnp.zeros((4, depth_cells, height_cells * width_cells), jnp.bfloat16)
    classified = lax.fori_loop(0, depth_cells, one_layer, start_cells)
    return classified.reshape(4, depth_cells, height_cells, width_cells)


def general_device(density, bin_index, tf_colour, tf_extinction, slab_rank):
    slab_count = lax.axis_size("bz")
    depth_cells, height_cells, width_cells = density.shape
    total_depth = float(depth_cells * slab_count)
    colour_cells = classify(density, bin_index, tf_colour, tf_extinction, total_depth)
    padded = with_halo(colour_cells, (("bz", 1), ("by", 2), ("bx", 3)), 1)
    along_x = jnp.einsum(
        "czyq,pq->czyp", padded, resample_table(width_cells), preferred_element_type=jnp.float32
    ).astype(jnp.bfloat16)
    y_table = resample_table(height_cells)

    def add_sample(sample_index, image_now):
        centre = sample_index // 2
        parity = sample_index % 2
        layers = lax.dynamic_slice_in_dim(along_x, centre, 3, 1).astype(jnp.float32)
        lower_weight = jnp.where(parity == 0, 0.25, 0.0)
        upper_weight = jnp.where(parity == 1, 0.25, 0.0)
        mixed_layer = (
            lower_weight * layers[:, 0] + 0.75 * layers[:, 1] + upper_weight * layers[:, 2]
        ).astype(jnp.bfloat16)
        sample = jnp.einsum("qy,cyp->cqp", y_table, mixed_layer, preferred_element_type=jnp.float32)
        return blend_over(image_now, sample)

    start_image = jnp.zeros((4, 2 * height_cells, 2 * width_cells), jnp.float32)
    slab_image = lax.fori_loop(0, 2 * depth_cells, add_sample, start_image)
    rows_piece = 2 * height_cells // slab_count
    my_index = lax.axis_index("bz")
    bit_levels = slab_count.bit_length() - 1
    composite = slab_image.reshape((4,) + (2,) * bit_levels + (rows_piece, 2 * width_cells))
    my_rank = lax.dynamic_index_in_dim(slab_rank, my_index, 0, keepdims=False)
    for level in range(bit_levels):
        position = bit_levels - level
        my_bit = my_index // 2**level % 2
        kept_half = lax.dynamic_index_in_dim(composite, my_bit, position, keepdims=False)
        outgoing = lax.dynamic_index_in_dim(composite, 1 - my_bit, position, keepdims=False)
        incoming = partner_2(outgoing, "bz", level)
        partner = my_index + (1 - 2 * my_bit) * 2**level
        partner_rank = lax.dynamic_index_in_dim(slab_rank, partner, 0, keepdims=False)
        mine_first = my_rank < partner_rank
        composite = blend_over(
            jnp.where(mine_first, kept_half, incoming), jnp.where(mine_first, incoming, kept_half)
        )
    return composite


LANES = 128
LEVELS = 65535.0
VMEM = pl.BlockSpec(memory_space=pltpu.VMEM)


def pack_words(density, bins):
    level = (density * LEVELS + 0.5).astype(jnp.int32)
    return lax.shift_left(level, 16) | bins


def unpack_words(words):
    density = lax.shift_right_logical(words, 16).astype(jnp.float32) * (1.0 / LEVELS)
    return density, words & 0xFFFF


def cell_values(density, bins, tables, depth):
    low_bits = bins & (LANES - 1)
    upper = bins >= LANES

    def pick(channel):
        first, second = tables[channel]
        return jnp.where(
            upper,
            jnp.take_along_axis(second, low_bits, axis=1, mode="promise_in_bounds"),
            jnp.take_along_axis(first, low_bits, axis=1, mode="promise_in_bounds"),
        )

    opacity = (1.0 - jnp.exp(-pick(3) * density / depth)) * (1.0 / 64.0)
    return [pick(0) * opacity, pick(1) * opacity, pick(2) * opacity, opacity]


def read_tables(tables_ref):
    return [[tables_ref[2 * channel + half] for half in range(2)] for channel in range(4)]


def cost(microseconds):
    return pl.CostEstimate(
        flops=int(1e9 * microseconds), bytes_accessed=int(3.6e6 * microseconds), transcendentals=0
    )


def stage_kernel(
    rank_ref, density_ref, bins_ref, colour_ref, extinction_ref,
    flip_ref, first_ref, second_ref, bulk_ref, inside_ref, dense_ref, index_ref, tables_ref,
):
    flip_ref[0] = rank_ref[0]
    layers, rows, cols = density_ref.shape
    front = lax.axis_index("bz") == 0
    inner = lax.axis_index("by") > 0
    for z in range(layers):
        top, bottom = [
            pack_words(density_ref[z, r : r + 1, :], bins_ref[z, r : r + 1, :]) for r in (0, rows - 1)
        ]
        first_ref[z : z + 1, :] = jnp.where(jnp.logical_not(front) & inner, top, bottom)
        second_ref[z : z + 1, :] = jnp.where(front & inner, top, bottom)
        for tile in range(cols // LANES):
            lanes = slice(tile * LANES, (tile + 1) * LANES)
            dense_ref[z, tile, 0:rows] = density_ref[z, :, lanes]
            index_ref[z, tile, 0:rows] = bins_ref[z, :, lanes]
    pack_block(dense_ref, index_ref, bulk_ref, inside_ref)
    colour = colour_ref[...].astype(jnp.float32)
    extinction = extinction_ref[...].astype(jnp.float32).reshape(1, 2 * LANES)
    for channel in range(4):
        line = extinction if channel == 3 else colour[channel : channel + 1]
        for half in range(2):
            tables_ref[2 * channel + half] = jnp.broadcast_to(
                line[:, half * LANES : (half + 1) * LANES], (8, LANES)
            )


def pack_block(dense_ref, index_ref, bulk_ref, inside_ref):
    layers, tiles, rows = dense_ref.shape[0], dense_ref.shape[1], dense_ref.shape[2] - 8
    half = rows // 2
    front = lax.axis_index("bz") == 0
    start = jnp.where(front, half, 0)
    for tile in range(tiles):
        lanes = slice(tile * LANES, (tile + 1) * LANES)
        for z in range(layers):
            for part in range(2):
                at = pl.ds(start + part, half // 2, stride=2)
                bulk_ref[2 * z + part, :, lanes] = pack_words(
                    dense_ref[z, tile, at, :], index_ref[z, tile, at, :]
                )
            line = [
                pack_words(dense_ref[z, tile, r : r + 1, :], index_ref[z, tile, r : r + 1, :])
                for r in (half - 1, half)
            ]
            bulk_ref[2 * layers, z : z + 1, lanes] = jnp.where(front, line[0], line[1])
            inside_ref[z : z + 1, lanes] = jnp.where(front, line[1], line[0])


def near_words(slab, first_ref, second_ref):
    me = lax.axis_index("bz")
    turned = (me == 0) & (lax.axis_index("by") == 1)
    words = jnp.where((me == slab) != turned, first_ref[...], second_ref[...])
    return jnp.where(has_near(me == 0), words, 0)


def column_lines(read_words, inside, lines_ref, rows):
    layers, cols = inside.shape
    front = lax.axis_index("bz") == 0
    start = lax.axis_index("bz") * (rows // 2)
    middle = LANES // 2
    lane_at = lax.broadcasted_iota(jnp.int32, (8, LANES), 1)
    row_at = start + 2 * lax.broadcasted_iota(jnp.int32, (8, LANES), 0)
    for z in range(layers):
        line = jnp.zeros((8, LANES), jnp.int32)
        for part in range(2):
            first = read_words(z, part, 0)[:, 0:1]
            last = read_words(z, part, cols // LANES - 1)[:, LANES - 1 : LANES]
            line += jnp.where(lane_at == row_at + part, first, 0)
            line += jnp.where(lane_at == row_at + part + middle, last, 0)
        lines_ref[z : z + 1, :] = jnp.sum(line, axis=0, keepdims=True)
    beside = jnp.where(front, rows // 2, rows // 2 - 1)
    lines = jnp.where(lane_at == beside, inside[:, 0:1], lines_ref[...])
    lines_ref[...] = jnp.where(lane_at == beside + middle, inside[:, cols - 1 : cols], lines)


def side_kernel(
    rows, columns_ref, bulk_ref, second_ref, first_ref, part_ref, ends_ref, other_ref
):
    layers, _ = columns_ref.shape
    front = lax.axis_index("bz") == 0
    lane_at = lax.broadcasted_iota(jnp.int32, (layers, LANES), 1)

    def read_words(z, part, tile):
        return bulk_ref[2 * z + part, :, tile * LANES : (tile + 1) * LANES]

    column_lines(read_words, bulk_ref[2 * layers], other_ref, rows)
    for slab in range(2):
        mine = front if slab == 0 else jnp.logical_not(front)
        columns = jnp.where(mine, columns_ref[...], other_ref[...])
        near = near_words(slab, first_ref, second_ref)
        cols = near.shape[1]
        columns = jnp.where(lane_at == rows, near[:, 0:1], columns)
        ends_ref[slab] = jnp.where(
            lane_at == LANES // 2 + rows, near[:, cols - 1 : cols], columns
        )


def has_near(front):
    me_y = lax.axis_index("by")
    return jnp.where(front, me_y > 0, me_y + 1 < lax.axis_size("by"))


def fill_weights(weights_ref):
    cols = weights_ref.shape[0]
    row = lax.broadcasted_iota(jnp.int32, (cols, 2 * cols), 0)
    at = lax.broadcasted_iota(jnp.int32, (cols, 2 * cols), 1)
    centre = lax.shift_right_logical(at, 1)
    beside = centre - 1 + 2 * (at & 1)
    weights_ref[...] = jnp.where(row == centre, 3.0, jnp.where(row == beside, 1.0, 0.0)).astype(
        jnp.bfloat16
    )


def classify_rows(read_cells, tables, cells_ref, layers, tiles):
    total = float(2 * layers)
    for z in range(layers):
        for tile in range(tiles):
            even = cell_values(*read_cells(z, 0, tile), tables, total)
            odd = cell_values(*read_cells(z, 1, tile), tables, total)
            for channel in range(4):
                base = (z * 4 + channel) * 16
                block = jnp.concatenate([even[channel], odd[channel]], axis=0)
                cells_ref[base : base + 16, tile * LANES : (tile + 1) * LANES] = block.astype(jnp.bfloat16)


def rounded(value):
    return value.astype(jnp.bfloat16).astype(jnp.float32)


def cells_kernel(dense_ref, index_ref, inside_ref, tables_ref, cells_ref, weights_ref, mix_ref, lines_ref):
    layers, tiles, rows = dense_ref.shape[0], dense_ref.shape[1], dense_ref.shape[2] - 8
    half = rows // 2
    start = lax.axis_index("bz") * half
    fill_weights(weights_ref)
    fill_rows(mix_ref)

    def read_cells(z, part, tile):
        at = pl.ds(start + part, half // 2, stride=2)
        return dense_ref[z, tile, at, :], index_ref[z, tile, at, :]

    classify_rows(read_cells, read_tables(tables_ref), cells_ref, layers, tiles)
    column_lines(lambda *at: pack_words(*read_cells(*at)), inside_ref[...], lines_ref, rows)


def along_columns(cells, weights_ref, store):
    result = rounded(jnp.dot(cells, weights_ref[...], preferred_element_type=jnp.float32))
    for tile in range(result.shape[1] // LANES):
        store(tile, result[:, tile * LANES : (tile + 1) * LANES])


def own_kernel(cells_ref, weights_ref, along_ref):
    size = cells_ref.shape[0]
    pad = 64
    mine = pl.multiple_of(pad + lax.axis_index("bz") * size, pad)

    def store(tile, block):
        along_ref[tile, 0:pad, :] = jnp.zeros((pad, LANES), jnp.float32)
        along_ref[tile, pad + 2 * size : 2 * pad + 2 * size, :] = jnp.zeros((pad, LANES), jnp.float32)
        along_ref[tile, pl.ds(mine, size), :] = block

    along_columns(cells_ref[...], weights_ref, store)


def other_kernel(bulk_ref, tables_ref, weights_ref, ends_ref, own_ref, along_ref, cells_ref):
    layers = (bulk_ref.shape[0] - 1) // 2
    cols = bulk_ref.shape[2]
    size = cells_ref.shape[0]
    pad = 64
    theirs = pl.multiple_of(pad + (1 - lax.axis_index("bz")) * size, pad)

    def read_cells(z, part, tile):
        return unpack_words(bulk_ref[2 * z + part, :, tile * LANES : (tile + 1) * LANES])

    def store(tile, block):
        along_ref[tile, pl.ds(theirs, size), :] = block

    classify_rows(read_cells, read_tables(tables_ref), cells_ref, layers, cols // LANES)
    along_columns(cells_ref[...], weights_ref, store)


def edge_cells(near, inside, tables, cells_ref, front, base):
    layers, cols = near.shape
    for side in range(2):
        use_near = front if side == 0 else jnp.logical_not(front)
        words = jnp.where(use_near, near, inside)
        for t in range(cols // LANES):
            values = cell_values(
                *unpack_words(words[:, t * LANES : (t + 1) * LANES]), tables, float(2 * layers)
            )
            for channel in range(4):
                at = pl.ds(base + side * 4 + channel, layers, stride=8)
                cells_ref[t, at, :] = values[channel]


def edge_along(cells_ref, count, weights_ref):
    return rounded(
        sum(
            jnp.dot(
                cells_ref[t, 0:count].astype(jnp.bfloat16),
                weights_ref[t * LANES : (t + 1) * LANES, :],
                preferred_element_type=jnp.float32,
            )
            for t in range(cells_ref.shape[0])
        )
    )


def edge_lines(now, packed_ref, lines_ref, depth):
    triple = 3.0 * now
    empty = jnp.zeros((8, LANES), jnp.float32)
    for layer in range(depth):
        at = layer * 8
        here = triple[at : at + 8]
        before = now[at - 8 : at] if layer > 0 else empty
        after = now[at + 8 : at + 16] if layer + 1 < depth else empty
        line = jnp.concatenate([before + here, empty], axis=0)
        packed_ref[2 * at : 2 * at + 16, :] = line.astype(jnp.bfloat16)
        lines_ref[at : at + 8, :] = rounded(after + here)


def row_samples(value, above, below):
    sub_at = lax.broadcasted_iota(jnp.int32, (8, LANES), 0)
    low, high = value[0:8], value[8:16]
    before = jnp.where(sub_at == 0, above, pltpu.roll(high, 1, 0))
    after = jnp.where(sub_at == 7, below, pltpu.roll(low, 7, 0))
    low_centre = 3.0 * low
    high_centre = 3.0 * high
    return [before + low_centre, low_centre + high, low + high_centre, high_centre + after]


def slab_pair(
    along_refs, packed_refs, lines_refs, rows_ref, slab, lines_slab, layers, keep_first=None, keep_last=None
):
    along_at = pl.ds(pl.multiple_of(slab * (layers * 64), 64), (layers + 2) * 64)
    packed_at = pl.ds(pl.multiple_of(lines_slab * (layers * 16), 16), layers * 16)
    lines_at = pl.ds(pl.multiple_of(lines_slab * (layers * 8), 8), layers * 8 + 8)
    views = [ref.at[along_at, :] for ref in along_refs]
    packed = [ref.at[packed_at, :] for ref in packed_refs]
    lines = [ref.at[lines_at, :] for ref in lines_refs]

    def layer_rows(view, layer, channel):
        base = (layer * 4 + channel) * 16
        return view[base : base + 16, :]

    def both(pieces):
        return jnp.concatenate(pieces, axis=1)

    def blend(image, samples, keep):
        updated = []
        for tile in range(2):
            clear = [1.0 - value for value in image[tile][3]]
            updated.append([])
            for c in range(4):
                values = samples[tile][c]
                if keep is not None:
                    values = [jnp.where(keep, value, 0.0) for value in values]
                updated[tile].append([image[tile][c][i] + clear[i] * values[i] for i in range(4)])
        return updated

    zero = jnp.zeros((8, LANES), jnp.float32)
    image = [[[zero] * 4 for _ in range(4)] for _ in range(2)]
    for z in range(layers):
        triple = [[3.0 * layer_rows(v, z + 1, c) for c in range(4)] for v in views]
        mixed = [
            both([(layer_rows(v, z, c) + t[c]).astype(jnp.bfloat16) for v, t in zip(views, triple)])
            for c in range(4)
        ]
        mixed.append(both([line[z * 16 : z * 16 + 16, :] for line in packed]))
        product = jnp.dot(
            rows_ref[...], jnp.concatenate(mixed, axis=0), preferred_element_type=jnp.float32
        )
        even, odd = [], []
        for tile in range(2):
            lanes = slice(tile * LANES, (tile + 1) * LANES)
            even.append(
                [
                    [product[c * 32 + i * 8 : c * 32 + i * 8 + 8, lanes] for i in range(4)]
                    for c in range(4)
                ]
            )
            odd.append([])
            for c in range(4):
                value = rounded(layer_rows(views[tile], z + 2, c) + triple[tile][c])
                above = lines[tile][pl.ds(z * 8 + c, 8, stride=0), :]
                below = lines[tile][pl.ds(z * 8 + 4 + c, 8, stride=0), :]
                odd[tile].append(row_samples(value, above, below))
        image = blend(image, even, keep_first if z == 0 else None)
        image = blend(image, odd, keep_last if z == layers - 1 else None)
    return image


def joined(first, in_front, behind):
    top = [[jnp.where(first, x, y) for x, y in zip(a, b)] for a, b in zip(in_front, behind)]
    low = [[jnp.where(first, y, x) for x, y in zip(a, b)] for a, b in zip(in_front, behind)]
    clear = [1.0 - value for value in top[3]]
    return [[top[c][i] + clear[i] * low[c][i] for i in range(4)] for c in range(4)]


def own_tiles_kernel(
    tables_ref, weights_ref, inside_ref, mix_ref, along_ref, part_ref, cells_ref, packed_ref, lines_ref
):
    layers, cols = inside_ref.shape
    me = lax.axis_index("bz")
    front = me == 0
    inside = inside_ref[...]
    edge_cells(jnp.zeros_like(inside), inside, read_tables(tables_ref), cells_ref, front, 0)
    edge = edge_along(cells_ref, 8 * layers, weights_ref)
    tiles = 2 * cols // LANES
    for tile in range(tiles):
        now = edge[:, tile * LANES : (tile + 1) * LANES]
        edge_lines(now, packed_ref.at[tile], lines_ref.at[tile], layers)
    for pair in range(tiles // 2):
        at = [2 * pair, 2 * pair + 1]
        image = slab_pair(
            [along_ref.at[tile] for tile in at],
            [packed_ref.at[tile] for tile in at],
            [lines_ref.at[tile] for tile in at],
            mix_ref,
            me,
            0,
            layers,
            front,
            jnp.logical_not(front),
        )
        for index, tile in enumerate(at):
            for channel in range(4):
                for i in range(4):
                    part_ref[tile, channel * 4 + i] = image[index][channel][i]


def fill_rows(rows_ref):
    m = lax.broadcasted_iota(jnp.int32, rows_ref.shape, 0)
    k = lax.broadcasted_iota(jnp.int32, rows_ref.shape, 1)
    row = 4 * (m & 7) + (lax.shift_right_logical(m, 3) & 3)
    centre = lax.shift_right_logical(row, 1)
    beside = centre - 1 + 2 * (row & 1)
    own = k < 64
    k_channel = jnp.where(own, lax.shift_right_logical(k, 4), k & 3)
    k_row = 2 * (k & 7) + (lax.shift_right_logical(k, 3) & 1)
    k_row = jnp.where(own, k_row, jnp.where(k < 68, -1, jnp.where(k < 72, 16, 99)))
    same = k_channel == lax.shift_right_logical(m, 5)
    value = jnp.where(k_row == centre, 3.0, jnp.where(k_row == beside, 1.0, 0.0))
    rows_ref[...] = jnp.where(same, value, 0.0).astype(jnp.bfloat16)


def tiles_kernel(
    flip_ref, tables_ref, weights_ref, bulk_ref, inside_ref, second_ref, first_ref, ends_ref, mix_ref,
    part_ref, along_ref, image_ref, mine_ref, cells_ref, packed_ref, lines_ref, edge_ref, between_ref,
):
    layers, cols = inside_ref.shape
    depth = 2 * layers
    tiles = 2 * cols // LANES
    me = lax.axis_index("bz")
    front = me == 0
    tables = read_tables(tables_ref)
    for slab in range(2):
        inside = jnp.where(me == slab, inside_ref[...], bulk_ref[2 * layers])
        near = near_words(slab, first_ref, second_ref)
        edge_cells(near, inside, tables, cells_ref, front, slab * layers * 8)
        values = cell_values(*unpack_words(ends_ref[slab]), tables, float(depth))
        for channel in range(4):
            mine_ref[slab * 4 + channel] = 3.0 * rounded(values[channel])
    edge = edge_along(cells_ref, 8 * depth, weights_ref)
    here_at, beside_at = layers * 8 - 8, layers * 8
    empty = jnp.zeros((8, LANES), jnp.float32)
    for tile in range(tiles):
        now = edge[:, tile * LANES : (tile + 1) * LANES]
        edge_lines(now, packed_ref.at[tile], lines_ref.at[tile], depth)
        upper, lower = now[here_at : here_at + 8], now[beside_at : beside_at + 8]
        between_ref[tile, 0:8] = rounded(
            jnp.where(front, lower, upper) + 3.0 * jnp.where(front, upper, lower)
        )
        edge_ref[tile, 0:8] = empty
        edge_ref[tile, 8 : 8 * depth + 8] = now
        edge_ref[tile, 8 * depth + 8 :] = empty

    row = jnp.where(front, 0, 15)
    first_layer = me * layers
    replaced = []
    for tile in range(tiles):
        inner, outer = [], []
        for z in range(layers + 2):
            at = (first_layer + z) * 64 + row
            inner.append(along_ref[tile, pl.ds(at, 4, stride=16), :])
            both = edge_ref[tile, pl.ds(pl.multiple_of((first_layer + z) * 8, 8), 8), :]
            outer.append(jnp.where(front, both[0:4], both[4:8]))
        image = jnp.zeros((4, LANES), jnp.float32)
        for z in range(layers):
            for parity in range(2):
                beside = z + 2 * parity
                sample = rounded(outer[beside] + 3.0 * outer[z + 1]) + 3.0 * rounded(
                    inner[beside] + 3.0 * inner[z + 1]
                )
                if (z, parity) == (0, 0):
                    sample = jnp.where(front, sample, 0.0)
                if (z, parity) == (layers - 1, 1):
                    sample = jnp.where(front, 0.0, sample)
                image = image + (1.0 - image[3:4]) * sample
        replaced.append(image)

    sub_at = lax.broadcasted_iota(jnp.int32, (8, LANES), 0)
    for pair in range(tiles // 2):
        at = [2 * pair, 2 * pair + 1]
        other = slab_pair(
            [along_ref.at[tile] for tile in at],
            [packed_ref.at[tile] for tile in at],
            [lines_ref.at[tile] for tile in at],
            mix_ref,
            1 - me,
            1 - me,
            layers,
        )
        for index, tile in enumerate(at):
            here = pl.multiple_of(jnp.where(front, layers, layers + 1) * 64, 64)
            beside = pl.multiple_of(jnp.where(front, layers + 1, layers) * 64, 64)
            between, part = [], []
            for c in range(4):
                value = rounded(
                    along_ref[tile, pl.ds(beside + c * 16, 16), :]
                    + 3.0 * along_ref[tile, pl.ds(here + c * 16, 16), :]
                )
                above = between_ref[tile, pl.ds(c, 8, stride=0), :]
                below = between_ref[tile, pl.ds(c + 4, 8, stride=0), :]
                between.append(row_samples(value, above, below))
                values = [part_ref[tile, c * 4 + i] for i in range(4)]
                line = replaced[tile][c : c + 1]
                values[0] = jnp.where(sub_at == 0, jnp.where(front, line, values[0]), values[0])
                values[3] = jnp.where(sub_at == 7, jnp.where(front, values[3], line), values[3])
                part.append(values)
            mine = joined(front, part, between)
            image = joined((me ^ flip_ref[0]) == 0, mine, other[index])
            for c in range(4):
                for i in range(4):
                    image_ref[tile, c, pl.ds(i, 8, stride=4), :] = image[c][i]


def edge_kernel(
    flip_ref, tables_ref, beside_ref, across_ref, mine_ref, image_ref,
    out_ref, samples_ref, final_ref, turned_ref, fixed_ref, sems,
):
    rows = out_ref.shape[1]
    cols = out_ref.shape[2] // 2
    half = rows // 2
    layers = beside_ref.shape[1]
    tiles = 2 * cols // LANES
    middle = LANES // 2
    front = lax.axis_index("bz") == 0
    start = pl.multiple_of(lax.axis_index("bz") * half, half)
    me_x = lax.axis_index("bx")
    even_x = lax.rem(me_x, 2) == 0
    tables = read_tables(tables_ref)

    def to_out(tile, source):
        lanes = pl.ds(tile * LANES, LANES)
        return pltpu.make_async_copy(
            source.at[:, pl.ds(0, rows), :], out_ref.at[:, :, lanes], sems.at[tile]
        )

    copies = [to_out(tile, image_ref.at[tile]) for tile in range(1, tiles - 1)]
    for copy in copies:
        copy.start()
    lane_at = lax.broadcasted_iota(jnp.int32, (layers, LANES), 1)
    layer_at = lax.broadcasted_iota(jnp.int32, (layers, LANES), 0)
    first_lane = (lane_at & (middle - 1)) == 0
    along = [[], []]
    for slab in range(2):
        right = jnp.where(even_x, beside_ref[slab], across_ref[slab])
        left = jnp.where(even_x, across_ref[slab], beside_ref[slab])
        right = jnp.where(me_x + 1 < lax.axis_size("bx"), right, 0)
        left = jnp.where(me_x > 0, left, 0)
        words = pltpu.roll(jnp.where(lane_at < middle, right, left), middle, 1)
        halo = cell_values(*unpack_words(words), tables, float(2 * layers))
        for channel in range(4):
            along[slab].append(rounded(mine_ref[slab * 4 + channel] + rounded(halo[channel])))
    for channel in range(4):
        front_part, back_part = along[0][channel], along[1][channel]
        down = [pltpu.roll(front_part, 1, 0), pltpu.roll(back_part, 1, 0)]
        up = [pltpu.roll(front_part, layers - 1, 0), pltpu.roll(back_part, layers - 1, 0)]
        is_first, is_last = layer_at == 0, layer_at == layers - 1
        before = [jnp.where(is_first, 0.0, down[0]), jnp.where(is_first, down[0], down[1])]
        after = [jnp.where(is_last, up[1], up[0]), jnp.where(is_last, 0.0, up[1])]
        for slab in range(2):
            triple = 3.0 * along[slab][channel]
            for parity, other in enumerate((before[slab], after[slab])):
                mixed = rounded(other + triple)
                centre = 3.0 * mixed
                above = pltpu.roll(mixed, 1, 1)
                near = pltpu.roll(mixed, LANES - rows, 1)
                above = jnp.where(first_lane, jnp.where(front, near, above), above)
                below = pltpu.roll(mixed, LANES - 1, 1)
                for odd, value in enumerate((above + centre, centre + below)):
                    at = (parity * 2 + odd) * 4 + channel
                    samples_ref[slab, at, 0:layers, :] = value

    def over_some(slab, layers_at):
        zero = jnp.zeros((8, LANES), jnp.float32)
        image = [[zero] * 4 for _ in range(2)]
        for z in layers_at:
            for parity in range(2):
                clear = [1.0 - image[odd][3] for odd in range(2)]
                image = [
                    [
                        image[odd][channel]
                        + clear[odd]
                        * samples_ref[slab, (parity * 2 + odd) * 4 + channel, pl.ds(z, 8, stride=0), :]
                        for channel in range(4)
                    ]
                    for odd in range(2)
                ]
        return image

    def over(in_front, behind):
        return [
            [top + (1.0 - tops[3]) * low for top, low in zip(tops, lows)]
            for tops, lows in zip(in_front, behind)
        ]

    slabs = [
        over(
            over_some(slab, range(layers // 2)), over_some(slab, range(layers // 2, layers))
        )
        for slab in range(2)
    ]
    in_order = flip_ref[0] == 0
    image = over(
        *[
            [
                [jnp.where(in_order, x, y) for x, y in zip(xs, ys)]
                for xs, ys in zip(slabs[at], slabs[1 - at])
            ]
            for at in range(2)
        ]
    )
    for odd in range(2):
        for channel in range(4):
            at = odd * 4 + channel
            final_ref[at : at + 1, :] = image[odd][channel][0:1]
    turned_ref[:, 0:8] = final_ref[...].T
    wide = lax.broadcasted_iota(jnp.int32, (half, LANES), 1)
    for index, tile in enumerate((0, tiles - 1)):
        place = wide == index * (LANES - 1)
        turned = turned_ref[pl.ds(start + index * middle, half), :]
        for channel in range(4):
            for odd in range(2):
                at = pl.ds(odd, half, stride=2)
                column = odd * 4 + channel
                fixed_ref[index, channel, at, :] = jnp.where(
                    place, turned[:, column : column + 1], image_ref[tile, channel, at, :]
                )
        copies.append(to_out(tile, fixed_ref.at[index]))
        copies[-1].start()
    for copy in copies:
        copy.wait()


def two_slab_device(density, bin_index, tf_colour, tf_extinction, slab_rank):
    layers, rows, cols = density.shape
    half = rows // 2
    tiles = 2 * cols // LANES
    size = layers * 4 * half
    count_y, count_x = lax.axis_size("by"), lax.axis_size("bx")
    f32, bf16, i32 = jnp.float32, jnp.bfloat16, jnp.int32

    def call(kernel, name, out_shape, time, scratch_shapes=(), in_specs=None, out_specs=None, aliases={}):
        def run(*operands):
            return pl.pallas_call(
                kernel,
                out_shape=out_shape,
                in_specs=in_specs or [VMEM] * len(operands),
                out_specs=out_specs
                or ((VMEM,) * len(out_shape) if isinstance(out_shape, tuple) else VMEM),
                scratch_shapes=scratch_shapes,
                input_output_aliases=aliases,
                compiler_params=pltpu.CompilerParams(vmem_limit_bytes=16 * 1024 * 1024),
                cost_estimate=cost(time),
                name=name,
            )(*operands)

        return run

    def both(route):
        return route + [(target, source) for source, target in route]

    blocks = (layers, cols // LANES, rows + 8, LANES)
    row = pltpu.VMEM((layers, cols), i32)
    smem = pl.BlockSpec(memory_space=pltpu.SMEM)
    inputs = [
        pltpu.with_memory_space_constraint(x, pltpu.HBM)
        for x in (slab_rank, density, bin_index, tf_colour, tf_extinction)
    ]
    flip, first, second, bulk, inside, dense, index, tables = call(
        stage_kernel,
        "stage_block",
        (
            pltpu.SMEM((1,), i32),
            row,
            row,
            pltpu.VMEM((2 * layers + 1, 8, cols), i32),
            row,
            pltpu.VMEM(blocks, f32),
            pltpu.VMEM(blocks, i32),
            pltpu.VMEM((8, 8, LANES), f32),
        ),
        1.2,
        in_specs=[smem] + [VMEM] * 4,
        out_specs=(smem,) + (VMEM,) * 7,
    )(*inputs)
    def place(z, y, x):
        return (z * count_y + y) * count_x + x

    def lanes(route):
        return [(place(*source, x), place(*target, x)) for source, target in route for x in range(count_x)]

    def twins(z, y):
        return both([(place(z, y, x), place(z, y, x + 1)) for x in range(0, count_x, 2)])

    last = count_y - 1
    ring = [((1, 0), (0, 1)), ((0, last), (1, last))]
    ring += [((0, y), (0, y + 1)) for y in range(1, last)] + [((1, y + 1), (1, y)) for y in range(last)]
    ring = lanes(ring) + twins(0, 0)
    diagonal = [((1, 0), (0, 0)), ((0, 0), (0, 1)), ((0, 1), (1, 0))]
    for y in range(1, last):
        diagonal += both([((1, y), (0, y + 1))])
    diagonal = lanes(diagonal) + twins(1, last)
    axes = ("bz", "by", "bx")
    bulk = lax.ppermute(bulk, "bz", [(0, 1), (1, 0)])
    first = lax.ppermute(first, axes, ring)
    second = lax.ppermute(second, axes, diagonal)

    cells, weights, mix, columns = call(
        cells_kernel,
        "own_cells",
        (
            pltpu.VMEM((size, cols), bf16),
            pltpu.VMEM((cols, 2 * cols), bf16),
            pltpu.VMEM((128, 80), bf16),
            pltpu.VMEM((layers, LANES), i32),
        ),
        0.5,
    )(dense, index, inside, tables)
    whole = pltpu.VMEM((tiles, 2 * size + 3 * 4 * half, LANES), f32)
    along = call(own_kernel, "own_slab", whole, 0.4)(cells, weights)
    edges = pltpu.VMEM((cols // LANES, 16 * layers + 8, LANES), f32)
    packed = pltpu.VMEM((tiles, 32 * layers, LANES), bf16)
    lines = pltpu.VMEM((tiles, 16 * layers + 8, LANES), f32)
    part = call(
        own_tiles_kernel,
        "own_tiles",
        pltpu.VMEM((tiles, 16, 8, LANES), f32),
        0.1,
        [edges, packed, lines],
    )(tables, weights, inside, mix, along)
    ends = call(
        functools.partial(side_kernel, rows),
        "side_columns",
        pltpu.VMEM((2, layers, LANES), i32),
        0.1,
        [pltpu.VMEM((layers, LANES), i32)],
    )(columns, bulk, second, first, part)
    pairs = [(x, x + 1) for x in range(0, count_x, 2)]
    cross = [(x, (x + 1) % count_x) for x in range(1, count_x, 2)]
    beside = lax.ppermute(ends, "bx", both(pairs))
    across = lax.ppermute(ends, "bx", both(cross))
    along = call(other_kernel, "other_slab", whole, 0.8, [pltpu.VMEM((size, cols), bf16)], aliases={4: 0})(
        bulk, tables, weights, ends, along
    )
    image, mine = call(
        tiles_kernel,
        "render_tiles",
        (pltpu.VMEM((tiles, 4, rows + 8, LANES), f32), pltpu.VMEM((8, layers, LANES), f32)),
        2.0,
        [
            edges,
            packed,
            lines,
            pltpu.VMEM((tiles, 16 * layers + 16, LANES), f32),
            pltpu.VMEM((tiles, 16, LANES), f32),
        ],
        [smem] + [VMEM] * 10,
    )(flip, tables, weights, bulk, inside, second, first, ends, mix, part, along)
    return call(
        edge_kernel,
        "edge_columns",
        jax.ShapeDtypeStruct((4, rows, 2 * cols), f32),
        1.0,
        [
            pltpu.VMEM((2, 16, 2 * layers, LANES), f32),
            pltpu.VMEM((8, LANES), f32),
            pltpu.VMEM((LANES, LANES), f32),
            pltpu.VMEM((2, 4, rows + 8, LANES), f32),
            pltpu.SemaphoreType.DMA((tiles,)),
        ],
        [smem] + [VMEM] * 5,
        pl.BlockSpec(memory_space=pltpu.HBM),
    )(flip, tables, beside, across, mine, image)


def on_device(density, bin_index, tf_colour, tf_extinction, slab_rank):
    if lax.axis_size("bz") == 2:
        return two_slab_device(density, bin_index, tf_colour, tf_extinction, slab_rank)
    return general_device(density, bin_index, tf_colour, tf_extinction, slab_rank)


def solution(mesh):
    return jax.shard_map(
        on_device,
        mesh=mesh,
        in_specs=(P("bz", "by", "bx"), P("bz", "by", "bx"), P(), P(), P()),
        out_specs=P(None, ("by", "bz"), "bx"),
        check_vma=False,
    )
```

```python
import functools

import jax
import jax.numpy as jnp
from jax import lax
from jax.experimental import pallas as pl
from jax.experimental.pallas import tpu as pltpu
from jax.sharding import PartitionSpec as P


def with_halo(block, sides, width):
    for axis, dim in sides:
        count = lax.axis_size(axis)
        forward = [(i, i + 1) for i in range(count - 1)]
        backward = [(target, source) for source, target in forward]
        low = lax.ppermute(
            lax.slice_in_dim(block, block.shape[dim] - width, None, axis=dim), axis, forward
        )
        high = lax.ppermute(lax.slice_in_dim(block, 0, width, axis=dim), axis, backward)
        block = jnp.concatenate([low, block, high], axis=dim)
    return block


def partner_2(block, axis, stride):
    count = lax.axis_size(axis)
    route = []
    for low in range(count):
        high = low | 1 << stride
        if high != low and high < count:
            route += [(low, high), (high, low)]
    return lax.ppermute(block, axis, route)


def resample_table(length):
    row_index = lax.broadcasted_iota(jnp.int32, (2 * length, length + 2), 0)
    col_index = lax.broadcasted_iota(jnp.int32, (2 * length, length + 2), 1)
    centre = row_index // 2
    parity = row_index % 2
    weights_table = jnp.where(col_index == centre + 1, 0.75, 0.0)
    weights_table = weights_table + jnp.where((col_index == centre) & (parity == 0), 0.25, 0.0)
    weights_table = weights_table + jnp.where((col_index == centre + 2) & (parity == 1), 0.25, 0.0)
    return weights_table.astype(jnp.bfloat16)


def blend_over(in_front, behind):
    return in_front + (1.0 - in_front[3])[None] * behind


def classify(density, bin_index, tf_colour, tf_extinction, total_depth):
    depth_cells, height_cells, width_cells = density.shape
    lookup = jnp.concatenate([tf_colour, tf_extinction[None, :]], axis=0)
    table_size = lookup.shape[1]
    bin_rows = lax.broadcasted_iota(jnp.int32, (table_size, 1), 0)
    flat_bins = bin_index.reshape(depth_cells, height_cells * width_cells)
    flat_density = density.reshape(depth_cells, height_cells * width_cells)

    def one_layer(layer, result):
        layer_bins = lax.dynamic_index_in_dim(flat_bins, layer, 0, keepdims=True)
        layer_density = lax.dynamic_index_in_dim(flat_density, layer, 0, keepdims=False)
        one_hot = (layer_bins == bin_rows).astype(jnp.bfloat16)
        values = jnp.dot(lookup, one_hot, preferred_element_type=jnp.float32)
        opacity = 1.0 - jnp.exp(-values[3] * layer_density / total_depth)
        cells = jnp.concatenate([values[:3] * opacity[None], opacity[None]], axis=0).astype(
            jnp.bfloat16
        )
        return lax.dynamic_update_slice_in_dim(result, cells[:, None], layer, 1)

    start_cells = jnp.zeros((4, depth_cells, height_cells * width_cells), jnp.bfloat16)
    classified = lax.fori_loop(0, depth_cells, one_layer, start_cells)
    return classified.reshape(4, depth_cells, height_cells, width_cells)


def general_device(density, bin_index, tf_colour, tf_extinction, slab_rank):
    slab_count = lax.axis_size("bz")
    depth_cells, height_cells, width_cells = density.shape
    total_depth = float(depth_cells * slab_count)
    colour_cells = classify(density, bin_index, tf_colour, tf_extinction, total_depth)
    padded = with_halo(colour_cells, (("bz", 1), ("by", 2), ("bx", 3)), 1)
    along_x = jnp.einsum(
        "czyq,pq->czyp", padded, resample_table(width_cells), preferred_element_type=jnp.float32
    ).astype(jnp.bfloat16)
    y_table = resample_table(height_cells)

    def add_sample(sample_index, image_now):
        centre = sample_index // 2
        parity = sample_index % 2
        layers = lax.dynamic_slice_in_dim(along_x, centre, 3, 1).astype(jnp.float32)
        lower_weight = jnp.where(parity == 0, 0.25, 0.0)
        upper_weight = jnp.where(parity == 1, 0.25, 0.0)
        mixed_layer = (
            lower_weight * layers[:, 0] + 0.75 * layers[:, 1] + upper_weight * layers[:, 2]
        ).astype(jnp.bfloat16)
        sample = jnp.einsum("qy,cyp->cqp", y_table, mixed_layer, preferred_element_type=jnp.float32)
        return blend_over(image_now, sample)

    start_image = jnp.zeros((4, 2 * height_cells, 2 * width_cells), jnp.float32)
    slab_image = lax.fori_loop(0, 2 * depth_cells, add_sample, start_image)
    rows_piece = 2 * height_cells // slab_count
    my_index = lax.axis_index("bz")
    bit_levels = slab_count.bit_length() - 1
    composite = slab_image.reshape((4,) + (2,) * bit_levels + (rows_piece, 2 * width_cells))
    my_rank = lax.dynamic_index_in_dim(slab_rank, my_index, 0, keepdims=False)
    for level in range(bit_levels):
        position = bit_levels - level
        my_bit = my_index // 2**level % 2
        kept_half = lax.dynamic_index_in_dim(composite, my_bit, position, keepdims=False)
        outgoing = lax.dynamic_index_in_dim(composite, 1 - my_bit, position, keepdims=False)
        incoming = partner_2(outgoing, "bz", level)
        partner = my_index + (1 - 2 * my_bit) * 2**level
        partner_rank = lax.dynamic_index_in_dim(slab_rank, partner, 0, keepdims=False)
        mine_first = my_rank < partner_rank
        composite = blend_over(
            jnp.where(mine_first, kept_half, incoming), jnp.where(mine_first, incoming, kept_half)
        )
    return composite


LANES = 128
LEVELS = 65535.0
VMEM = pl.BlockSpec(memory_space=pltpu.VMEM)
SMEM = pl.BlockSpec(memory_space=pltpu.SMEM)
FLIP, ME, HAS_NEAR, TURNED, ODD_X, HAS_RIGHT, HAS_LEFT = range(7)


def pack_words(density, bins):
    level = (density * LEVELS + 0.5).astype(jnp.int32)
    return lax.shift_left(level, 16) | bins


def unpack_words(words):
    density = lax.shift_right_logical(words, 16).astype(jnp.float32) * (1.0 / LEVELS)
    return density, words & 0xFFFF


def cell_values(density, bins, tables, depth):
    low_bits = bins & (LANES - 1)
    upper = bins >= LANES

    def pick(channel):
        first, second = tables[channel]
        return jnp.where(
            upper,
            jnp.take_along_axis(second, low_bits, axis=1, mode="promise_in_bounds"),
            jnp.take_along_axis(first, low_bits, axis=1, mode="promise_in_bounds"),
        )

    opacity = (1.0 - jnp.exp(-pick(3) * density / depth)) * (1.0 / 64.0)
    return [pick(0) * opacity, pick(1) * opacity, pick(2) * opacity, opacity]


def read_tables(tables_ref):
    return [[tables_ref[2 * channel + half] for half in range(2)] for channel in range(4)]


def cost(microseconds):
    return pl.CostEstimate(
        flops=int(1e9 * microseconds), bytes_accessed=int(3.6e6 * microseconds), transcendentals=0
    )


def stage_kernel(
    rank_ref, density_ref, bins_ref, colour_ref, extinction_ref,
    place_ref, first_ref, second_ref, bulk_ref, inside_ref, dense_ref, index_ref, tables_ref,
):
    me, me_y, me_x = lax.axis_index("bz"), lax.axis_index("by"), lax.axis_index("bx")
    past = jnp.where(me == 0, me_y, lax.axis_size("by") - 1 - me_y)
    for at, value in enumerate(
        (
            rank_ref[0],
            me,
            jnp.minimum(past, 1),
            jnp.where((me == 0) & (me_y == 1), 1, 0),
            lax.rem(me_x, 2),
            jnp.where(me_x + 1 < lax.axis_size("bx"), 1, 0),
            jnp.minimum(me_x, 1),
        )
    ):
        place_ref[at] = value
    layers, rows, cols = density_ref.shape
    front = me == 0
    inner = me_y > 0
    for z in range(layers):
        top, bottom = [
            pack_words(density_ref[z, r : r + 1, :], bins_ref[z, r : r + 1, :]) for r in (0, rows - 1)
        ]
        first_ref[z : z + 1, :] = jnp.where(jnp.logical_not(front) & inner, top, bottom)
        second_ref[z : z + 1, :] = jnp.where(front & inner, top, bottom)
        for tile in range(cols // LANES):
            lanes = slice(tile * LANES, (tile + 1) * LANES)
            dense_ref[z, tile, 0:rows] = density_ref[z, :, lanes]
            index_ref[z, tile, 0:rows] = bins_ref[z, :, lanes]
    pack_block(front, dense_ref, index_ref, bulk_ref, inside_ref)
    colour = colour_ref[...].astype(jnp.float32)
    extinction = extinction_ref[...].astype(jnp.float32).reshape(1, 2 * LANES)
    for channel in range(4):
        line = extinction if channel == 3 else colour[channel : channel + 1]
        for half in range(2):
            tables_ref[2 * channel + half] = jnp.broadcast_to(
                line[:, half * LANES : (half + 1) * LANES], (8, LANES)
            )


def pack_block(front, dense_ref, index_ref, bulk_ref, inside_ref):
    layers, tiles, rows = dense_ref.shape[0], dense_ref.shape[1], dense_ref.shape[2] - 8
    half = rows // 2
    start = jnp.where(front, half, 0)
    for tile in range(tiles):
        lanes = slice(tile * LANES, (tile + 1) * LANES)
        for z in range(layers):
            for part in range(2):
                at = pl.ds(start + part, half // 2, stride=2)
                bulk_ref[2 * z + part, :, lanes] = pack_words(
                    dense_ref[z, tile, at, :], index_ref[z, tile, at, :]
                )
            line = [
                pack_words(dense_ref[z, tile, r : r + 1, :], index_ref[z, tile, r : r + 1, :])
                for r in (half - 1, half)
            ]
            bulk_ref[2 * layers, z : z + 1, lanes] = jnp.where(front, line[0], line[1])
            inside_ref[z : z + 1, lanes] = jnp.where(front, line[1], line[0])


def near_words(slab, place_ref, first_ref, second_ref):
    own = (place_ref[ME] == slab) != (place_ref[TURNED] == 1)
    words = jnp.where(own, first_ref[...], second_ref[...])
    return jnp.where(place_ref[HAS_NEAR] == 1, words, 0)


def column_lines(me, read_words, inside, lines_ref, rows):
    layers, cols = inside.shape
    front = me == 0
    start = me * (rows // 2)
    middle = LANES // 2
    lane_at = lax.broadcasted_iota(jnp.int32, (8, LANES), 1)
    row_at = start + 2 * lax.broadcasted_iota(jnp.int32, (8, LANES), 0)
    for z in range(layers):
        line = jnp.zeros((8, LANES), jnp.int32)
        for part in range(2):
            first = read_words(z, part, 0)[:, 0:1]
            last = read_words(z, part, cols // LANES - 1)[:, LANES - 1 : LANES]
            line += jnp.where(lane_at == row_at + part, first, 0)
            line += jnp.where(lane_at == row_at + part + middle, last, 0)
        lines_ref[z : z + 1, :] = jnp.sum(line, axis=0, keepdims=True)
    beside = jnp.where(front, rows // 2, rows // 2 - 1)
    lines = jnp.where(lane_at == beside, inside[:, 0:1], lines_ref[...])
    lines_ref[...] = jnp.where(lane_at == beside + middle, inside[:, cols - 1 : cols], lines)


def side_kernel(
    rows, place_ref, columns_ref, bulk_ref, second_ref, first_ref, part_ref, ends_ref, other_ref
):
    layers, _ = columns_ref.shape
    me = place_ref[ME]
    front = me == 0
    lane_at = lax.broadcasted_iota(jnp.int32, (layers, LANES), 1)

    def read_words(z, part, tile):
        return bulk_ref[2 * z + part, :, tile * LANES : (tile + 1) * LANES]

    column_lines(me, read_words, bulk_ref[2 * layers], other_ref, rows)
    for slab in range(2):
        mine = front if slab == 0 else jnp.logical_not(front)
        columns = jnp.where(mine, columns_ref[...], other_ref[...])
        near = near_words(slab, place_ref, first_ref, second_ref)
        cols = near.shape[1]
        columns = jnp.where(lane_at == rows, near[:, 0:1], columns)
        ends_ref[slab] = jnp.where(
            lane_at == LANES // 2 + rows, near[:, cols - 1 : cols], columns
        )


def fill_weights(weights_ref):
    cols = weights_ref.shape[0]
    row = lax.broadcasted_iota(jnp.int32, (LANES, 2 * LANES), 0)
    at = lax.broadcasted_iota(jnp.int32, (LANES, 2 * LANES), 1)
    place = at - 2 * row
    block = jnp.where(
        (place == 0) | (place == 1), 3.0, jnp.where((place == -1) | (place == 2), 1.0, 0.0)
    ).astype(jnp.bfloat16)
    after = jnp.where((row == LANES - 1) & (at == 0), 1.0, 0.0).astype(jnp.bfloat16)
    before = jnp.where((row == 0) & (at == 2 * LANES - 1), 1.0, 0.0).astype(jnp.bfloat16)
    count = cols // LANES
    for i in range(count):
        for j in range(count):
            piece = block if i == j else after if j == i + 1 else before if j == i - 1 else None
            if piece is None:
                piece = jnp.zeros((LANES, 2 * LANES), jnp.bfloat16)
            weights_ref[i * LANES : (i + 1) * LANES, 2 * j * LANES : 2 * (j + 1) * LANES] = piece


def classify_rows(read_cells, tables, cells_ref, layers, tiles):
    total = float(2 * layers)
    for z in range(layers):
        for tile in range(tiles):
            even = cell_values(*read_cells(z, 0, tile), tables, total)
            odd = cell_values(*read_cells(z, 1, tile), tables, total)
            for channel in range(4):
                base = (z * 4 + channel) * 16
                block = jnp.concatenate([even[channel], odd[channel]], axis=0)
                cells_ref[base : base + 16, tile * LANES : (tile + 1) * LANES] = block.astype(jnp.bfloat16)


def rounded(value):
    return value.astype(jnp.bfloat16).astype(jnp.float32)


def cells_kernel(
    place_ref, dense_ref, index_ref, inside_ref, tables_ref, cells_ref, weights_ref, mix_ref, lines_ref
):
    layers, tiles, rows = dense_ref.shape[0], dense_ref.shape[1], dense_ref.shape[2] - 8
    half = rows // 2
    start = place_ref[ME] * half
    fill_weights(weights_ref)
    fill_rows(mix_ref)

    def read_cells(z, part, tile):
        at = pl.ds(start + part, half // 2, stride=2)
        return dense_ref[z, tile, at, :], index_ref[z, tile, at, :]

    classify_rows(read_cells, read_tables(tables_ref), cells_ref, layers, tiles)
    column_lines(place_ref[ME], lambda *at: pack_words(*read_cells(*at)), inside_ref[...], lines_ref, rows)


def along_columns(cells, weights_ref, store):
    result = rounded(jnp.dot(cells, weights_ref[...], preferred_element_type=jnp.float32))
    for tile in range(result.shape[1] // LANES):
        store(tile, result[:, tile * LANES : (tile + 1) * LANES])


def own_kernel(place_ref, cells_ref, weights_ref, along_ref):
    size = cells_ref.shape[0]
    pad = 64
    mine = pl.multiple_of(pad + place_ref[ME] * size, pad)

    def store(tile, block):
        along_ref[tile, 0:pad, :] = jnp.zeros((pad, LANES), jnp.float32)
        along_ref[tile, pad + 2 * size : 2 * pad + 2 * size, :] = jnp.zeros((pad, LANES), jnp.float32)
        along_ref[tile, pl.ds(mine, size), :] = block

    along_columns(cells_ref[...], weights_ref, store)


def other_kernel(
    place_ref, bulk_ref, tables_ref, weights_ref, ends_ref, own_ref, along_ref, cells_ref
):
    layers = (bulk_ref.shape[0] - 1) // 2
    cols = bulk_ref.shape[2]
    size = cells_ref.shape[0]
    pad = 64
    theirs = pl.multiple_of(pad + (1 - place_ref[ME]) * size, pad)

    def read_cells(z, part, tile):
        return unpack_words(bulk_ref[2 * z + part, :, tile * LANES : (tile + 1) * LANES])

    def store(tile, block):
        along_ref[tile, pl.ds(theirs, size), :] = block

    classify_rows(read_cells, read_tables(tables_ref), cells_ref, layers, cols // LANES)
    along_columns(cells_ref[...], weights_ref, store)


def edge_cells(near, inside, tables, cells_ref, front, base):
    layers, cols = near.shape
    for side in range(2):
        use_near = front if side == 0 else jnp.logical_not(front)
        words = jnp.where(use_near, near, inside)
        for t in range(cols // LANES):
            values = cell_values(
                *unpack_words(words[:, t * LANES : (t + 1) * LANES]), tables, float(2 * layers)
            )
            for channel in range(4):
                at = pl.ds(base + side * 4 + channel, layers, stride=8)
                cells_ref[t, at, :] = values[channel]


def edge_along(cells_ref, count, weights_ref):
    return rounded(
        sum(
            jnp.dot(
                cells_ref[t, 0:count].astype(jnp.bfloat16),
                weights_ref[t * LANES : (t + 1) * LANES, :],
                preferred_element_type=jnp.float32,
            )
            for t in range(cells_ref.shape[0])
        )
    )


def edge_lines(now, packed_ref, lines_ref, depth):
    triple = 3.0 * now
    empty = jnp.zeros((8, LANES), jnp.float32)
    for layer in range(depth):
        at = layer * 8
        here = triple[at : at + 8]
        before = now[at - 8 : at] if layer > 0 else empty
        after = now[at + 8 : at + 16] if layer + 1 < depth else empty
        line = jnp.concatenate([before + here, empty], axis=0)
        packed_ref[2 * at : 2 * at + 16, :] = line.astype(jnp.bfloat16)
        lines_ref[at : at + 8, :] = rounded(after + here)


def row_samples(value, above, below):
    sub_at = lax.broadcasted_iota(jnp.int32, (8, LANES), 0)
    low, high = value[0:8], value[8:16]
    before = jnp.where(sub_at == 0, above, pltpu.roll(high, 1, 0))
    after = jnp.where(sub_at == 7, below, pltpu.roll(low, 7, 0))
    low_centre = 3.0 * low
    high_centre = 3.0 * high
    return [before + low_centre, low_centre + high, low + high_centre, high_centre + after]


def slab_pair(
    along_refs, packed_refs, lines_refs, rows_ref, slab, lines_slab, layers, keep_first=None, keep_last=None
):
    along_at = pl.ds(pl.multiple_of(slab * (layers * 64), 64), (layers + 2) * 64)
    packed_at = pl.ds(pl.multiple_of(lines_slab * (layers * 16), 16), layers * 16)
    lines_at = pl.ds(pl.multiple_of(lines_slab * (layers * 8), 8), layers * 8 + 8)
    views = [ref.at[along_at, :] for ref in along_refs]
    packed = [ref.at[packed_at, :] for ref in packed_refs]
    lines = [ref.at[lines_at, :] for ref in lines_refs]

    def layer_rows(view, layer, channel):
        base = (layer * 4 + channel) * 16
        return view[base : base + 16, :]

    def both(pieces):
        return jnp.concatenate(pieces, axis=1)

    def blend(image, samples, keep):
        updated = []
        for tile in range(2):
            clear = [1.0 - value for value in image[tile][3]]
            updated.append([])
            for c in range(4):
                values = samples[tile][c]
                if keep is not None:
                    values = [jnp.where(keep, value, 0.0) for value in values]
                updated[tile].append([image[tile][c][i] + clear[i] * values[i] for i in range(4)])
        return updated

    zero = jnp.zeros((8, LANES), jnp.float32)
    image = [[[zero] * 4 for _ in range(4)] for _ in range(2)]
    for z in range(layers):
        triple = [[3.0 * layer_rows(v, z + 1, c) for c in range(4)] for v in views]
        mixed = [
            both([(layer_rows(v, z, c) + t[c]).astype(jnp.bfloat16) for v, t in zip(views, triple)])
            for c in range(4)
        ]
        mixed.append(both([line[z * 16 : z * 16 + 16, :] for line in packed]))
        product = jnp.dot(
            rows_ref[...], jnp.concatenate(mixed, axis=0), preferred_element_type=jnp.float32
        )
        even, odd = [], []
        for tile in range(2):
            lanes = slice(tile * LANES, (tile + 1) * LANES)
            even.append(
                [
                    [product[c * 32 + i * 8 : c * 32 + i * 8 + 8, lanes] for i in range(4)]
                    for c in range(4)
                ]
            )
            odd.append([])
            for c in range(4):
                value = rounded(layer_rows(views[tile], z + 2, c) + triple[tile][c])
                above = lines[tile][pl.ds(z * 8 + c, 8, stride=0), :]
                below = lines[tile][pl.ds(z * 8 + 4 + c, 8, stride=0), :]
                odd[tile].append(row_samples(value, above, below))
        image = blend(image, even, keep_first if z == 0 else None)
        image = blend(image, odd, keep_last if z == layers - 1 else None)
    return image


def joined(first, in_front, behind):
    top = [[jnp.where(first, x, y) for x, y in zip(a, b)] for a, b in zip(in_front, behind)]
    low = [[jnp.where(first, y, x) for x, y in zip(a, b)] for a, b in zip(in_front, behind)]
    clear = [1.0 - value for value in top[3]]
    return [[top[c][i] + clear[i] * low[c][i] for i in range(4)] for c in range(4)]


def own_tiles_kernel(
    place_ref, tables_ref, weights_ref, inside_ref, mix_ref, along_ref, part_ref, cells_ref, packed_ref, lines_ref
):
    layers, cols = inside_ref.shape
    me = place_ref[ME]
    front = me == 0
    inside = inside_ref[...]
    edge_cells(jnp.zeros_like(inside), inside, read_tables(tables_ref), cells_ref, front, 0)
    edge = edge_along(cells_ref, 8 * layers, weights_ref)
    tiles = 2 * cols // LANES
    for tile in range(tiles):
        now = edge[:, tile * LANES : (tile + 1) * LANES]
        edge_lines(now, packed_ref.at[tile], lines_ref.at[tile], layers)
    for pair in range(tiles // 2):
        at = [2 * pair, 2 * pair + 1]
        image = slab_pair(
            [along_ref.at[tile] for tile in at],
            [packed_ref.at[tile] for tile in at],
            [lines_ref.at[tile] for tile in at],
            mix_ref,
            me,
            0,
            layers,
            front,
            jnp.logical_not(front),
        )
        for index, tile in enumerate(at):
            for channel in range(4):
                for i in range(4):
                    part_ref[tile, channel * 4 + i] = image[index][channel][i]


def fill_rows(rows_ref):
    m = lax.broadcasted_iota(jnp.int32, rows_ref.shape, 0)
    k = lax.broadcasted_iota(jnp.int32, rows_ref.shape, 1)
    row = 4 * (m & 7) + (lax.shift_right_logical(m, 3) & 3)
    centre = lax.shift_right_logical(row, 1)
    beside = centre - 1 + 2 * (row & 1)
    own = k < 64
    k_channel = jnp.where(own, lax.shift_right_logical(k, 4), k & 3)
    k_row = 2 * (k & 7) + (lax.shift_right_logical(k, 3) & 1)
    k_row = jnp.where(own, k_row, jnp.where(k < 68, -1, jnp.where(k < 72, 16, 99)))
    same = k_channel == lax.shift_right_logical(m, 5)
    value = jnp.where(k_row == centre, 3.0, jnp.where(k_row == beside, 1.0, 0.0))
    rows_ref[...] = jnp.where(same, value, 0.0).astype(jnp.bfloat16)


def tiles_kernel(
    place_ref, tables_ref, weights_ref, bulk_ref, inside_ref, second_ref, first_ref, ends_ref, mix_ref,
    part_ref, along_ref, image_ref, mine_ref, cells_ref, packed_ref, lines_ref, edge_ref, between_ref,
):
    layers, cols = inside_ref.shape
    depth = 2 * layers
    tiles = 2 * cols // LANES
    me = place_ref[ME]
    front = me == 0
    tables = read_tables(tables_ref)
    for slab in range(2):
        inside = jnp.where(me == slab, inside_ref[...], bulk_ref[2 * layers])
        near = near_words(slab, place_ref, first_ref, second_ref)
        edge_cells(near, inside, tables, cells_ref, front, slab * layers * 8)
        values = cell_values(*unpack_words(ends_ref[slab]), tables, float(depth))
        for channel in range(4):
            mine_ref[slab * 4 + channel] = 3.0 * rounded(values[channel])
    edge = edge_along(cells_ref, 8 * depth, weights_ref)
    here_at, beside_at = layers * 8 - 8, layers * 8
    empty = jnp.zeros((8, LANES), jnp.float32)
    for tile in range(tiles):
        now = edge[:, tile * LANES : (tile + 1) * LANES]
        edge_lines(now, packed_ref.at[tile], lines_ref.at[tile], depth)
        upper, lower = now[here_at : here_at + 8], now[beside_at : beside_at + 8]
        between_ref[tile, 0:8] = rounded(
            jnp.where(front, lower, upper) + 3.0 * jnp.where(front, upper, lower)
        )
        edge_ref[tile, 0:8] = empty
        edge_ref[tile, 8 : 8 * depth + 8] = now
        edge_ref[tile, 8 * depth + 8 :] = empty

    row = jnp.where(front, 0, 15)
    first_layer = me * layers
    replaced = []
    for tile in range(tiles):
        inner, outer = [], []
        for z in range(layers + 2):
            at = (first_layer + z) * 64 + row
            inner.append(along_ref[tile, pl.ds(at, 4, stride=16), :])
            both = edge_ref[tile, pl.ds(pl.multiple_of((first_layer + z) * 8, 8), 8), :]
            outer.append(jnp.where(front, both[0:4], both[4:8]))
        image = jnp.zeros((4, LANES), jnp.float32)
        for z in range(layers):
            for parity in range(2):
                beside = z + 2 * parity
                sample = rounded(outer[beside] + 3.0 * outer[z + 1]) + 3.0 * rounded(
                    inner[beside] + 3.0 * inner[z + 1]
                )
                if (z, parity) == (0, 0):
                    sample = jnp.where(front, sample, 0.0)
                if (z, parity) == (layers - 1, 1):
                    sample = jnp.where(front, 0.0, sample)
                image = image + (1.0 - image[3:4]) * sample
        replaced.append(image)

    sub_at = lax.broadcasted_iota(jnp.int32, (8, LANES), 0)
    for pair in range(tiles // 2):
        at = [2 * pair, 2 * pair + 1]
        other = slab_pair(
            [along_ref.at[tile] for tile in at],
            [packed_ref.at[tile] for tile in at],
            [lines_ref.at[tile] for tile in at],
            mix_ref,
            1 - me,
            1 - me,
            layers,
        )
        for index, tile in enumerate(at):
            here = pl.multiple_of(jnp.where(front, layers, layers + 1) * 64, 64)
            beside = pl.multiple_of(jnp.where(front, layers + 1, layers) * 64, 64)
            between, part = [], []
            for c in range(4):
                value = rounded(
                    along_ref[tile, pl.ds(beside + c * 16, 16), :]
                    + 3.0 * along_ref[tile, pl.ds(here + c * 16, 16), :]
                )
                above = between_ref[tile, pl.ds(c, 8, stride=0), :]
                below = between_ref[tile, pl.ds(c + 4, 8, stride=0), :]
                between.append(row_samples(value, above, below))
                values = [part_ref[tile, c * 4 + i] for i in range(4)]
                line = replaced[tile][c : c + 1]
                values[0] = jnp.where(sub_at == 0, jnp.where(front, line, values[0]), values[0])
                values[3] = jnp.where(sub_at == 7, jnp.where(front, values[3], line), values[3])
                part.append(values)
            mine = joined(front, part, between)
            image = joined((me ^ place_ref[FLIP]) == 0, mine, other[index])
            for c in range(4):
                for i in range(4):
                    image_ref[tile, c, pl.ds(i, 8, stride=4), :] = image[c][i]


def edge_kernel(
    place_ref, tables_ref, beside_ref, across_ref, mine_ref, image_ref,
    out_ref, samples_ref, final_ref, turned_ref, fixed_ref, sems,
):
    rows = out_ref.shape[1]
    cols = out_ref.shape[2] // 2
    half = rows // 2
    layers = beside_ref.shape[1]
    tiles = 2 * cols // LANES
    middle = LANES // 2
    front = place_ref[ME] == 0
    start = pl.multiple_of(place_ref[ME] * half, half)
    even_x = place_ref[ODD_X] == 0
    tables = read_tables(tables_ref)

    def to_out(tile, source):
        lanes = pl.ds(tile * LANES, LANES)
        return pltpu.make_async_copy(
            source.at[:, pl.ds(0, rows), :], out_ref.at[:, :, lanes], sems.at[tile]
        )

    copies = [to_out(tile, image_ref.at[tile]) for tile in range(1, tiles - 1)]
    for copy in copies:
        copy.start()
    lane_at = lax.broadcasted_iota(jnp.int32, (layers, LANES), 1)
    layer_at = lax.broadcasted_iota(jnp.int32, (layers, LANES), 0)
    first_lane = (lane_at & (middle - 1)) == 0
    along = [[], []]
    for slab in range(2):
        right = jnp.where(even_x, beside_ref[slab], across_ref[slab])
        left = jnp.where(even_x, across_ref[slab], beside_ref[slab])
        right = jnp.where(place_ref[HAS_RIGHT] == 1, right, 0)
        left = jnp.where(place_ref[HAS_LEFT] == 1, left, 0)
        words = pltpu.roll(jnp.where(lane_at < middle, right, left), middle, 1)
        halo = cell_values(*unpack_words(words), tables, float(2 * layers))
        for channel in range(4):
            along[slab].append(rounded(mine_ref[slab * 4 + channel] + rounded(halo[channel])))
    for channel in range(4):
        front_part, back_part = along[0][channel], along[1][channel]
        down = [pltpu.roll(front_part, 1, 0), pltpu.roll(back_part, 1, 0)]
        up = [pltpu.roll(front_part, layers - 1, 0), pltpu.roll(back_part, layers - 1, 0)]
        is_first, is_last = layer_at == 0, layer_at == layers - 1
        before = [jnp.where(is_first, 0.0, down[0]), jnp.where(is_first, down[0], down[1])]
        after = [jnp.where(is_last, up[1], up[0]), jnp.where(is_last, 0.0, up[1])]
        for slab in range(2):
            triple = 3.0 * along[slab][channel]
            for parity, other in enumerate((before[slab], after[slab])):
                mixed = rounded(other + triple)
                centre = 3.0 * mixed
                above = pltpu.roll(mixed, 1, 1)
                near = pltpu.roll(mixed, LANES - rows, 1)
                above = jnp.where(first_lane, jnp.where(front, near, above), above)
                below = pltpu.roll(mixed, LANES - 1, 1)
                for odd, value in enumerate((above + centre, centre + below)):
                    at = (parity * 2 + odd) * 4 + channel
                    samples_ref[slab, at, 0:layers, :] = value

    def over_some(slab, layers_at):
        zero = jnp.zeros((8, LANES), jnp.float32)
        image = [[zero] * 4 for _ in range(2)]
        for z in layers_at:
            for parity in range(2):
                clear = [1.0 - image[odd][3] for odd in range(2)]
                image = [
                    [
                        image[odd][channel]
                        + clear[odd]
                        * samples_ref[slab, (parity * 2 + odd) * 4 + channel, pl.ds(z, 8, stride=0), :]
                        for channel in range(4)
                    ]
                    for odd in range(2)
                ]
        return image

    def over(in_front, behind):
        return [
            [top + (1.0 - tops[3]) * low for top, low in zip(tops, lows)]
            for tops, lows in zip(in_front, behind)
        ]

    slabs = [
        over(
            over_some(slab, range(layers // 2)), over_some(slab, range(layers // 2, layers))
        )
        for slab in range(2)
    ]
    in_order = place_ref[FLIP] == 0
    image = over(
        *[
            [
                [jnp.where(in_order, x, y) for x, y in zip(xs, ys)]
                for xs, ys in zip(slabs[at], slabs[1 - at])
            ]
            for at in range(2)
        ]
    )
    for odd in range(2):
        for channel in range(4):
            at = odd * 4 + channel
            final_ref[at : at + 1, :] = image[odd][channel][0:1]
    turned_ref[:, 0:8] = final_ref[...].T
    wide = lax.broadcasted_iota(jnp.int32, (half, LANES), 1)
    for index, tile in enumerate((0, tiles - 1)):
        place = wide == index * (LANES - 1)
        turned = turned_ref[pl.ds(start + index * middle, half), :]
        for channel in range(4):
            for odd in range(2):
                at = pl.ds(odd, half, stride=2)
                column = odd * 4 + channel
                fixed_ref[index, channel, at, :] = jnp.where(
                    place, turned[:, column : column + 1], image_ref[tile, channel, at, :]
                )
        copies.append(to_out(tile, fixed_ref.at[index]))
        copies[-1].start()
    for copy in copies:
        copy.wait()


def two_slab_device(density, bin_index, tf_colour, tf_extinction, slab_rank):
    layers, rows, cols = density.shape
    half = rows // 2
    tiles = 2 * cols // LANES
    size = layers * 4 * half
    count_y, count_x = lax.axis_size("by"), lax.axis_size("bx")
    f32, bf16, i32 = jnp.float32, jnp.bfloat16, jnp.int32

    def call(kernel, name, out_shape, time, scratch_shapes=(), in_specs=None, out_specs=None, aliases={}):
        def run(*operands):
            return pl.pallas_call(
                kernel,
                out_shape=out_shape,
                in_specs=in_specs or [SMEM] + [VMEM] * (len(operands) - 1),
                out_specs=out_specs
                or ((VMEM,) * len(out_shape) if isinstance(out_shape, tuple) else VMEM),
                scratch_shapes=scratch_shapes,
                input_output_aliases=aliases,
                compiler_params=pltpu.CompilerParams(vmem_limit_bytes=16 * 1024 * 1024),
                cost_estimate=cost(time),
                name=name,
            )(*operands)

        return run

    def both(route):
        return route + [(target, source) for source, target in route]

    blocks = (layers, cols // LANES, rows + 8, LANES)
    row = pltpu.VMEM((layers, cols), i32)
    inputs = [
        pltpu.with_memory_space_constraint(x, pltpu.HBM)
        for x in (slab_rank, density, bin_index, tf_colour, tf_extinction)
    ]
    place, first, second, bulk, inside, dense, index, tables = call(
        stage_kernel,
        "stage_block",
        (
            pltpu.SMEM((7,), i32),
            row,
            row,
            pltpu.VMEM((2 * layers + 1, 8, cols), i32),
            row,
            pltpu.VMEM(blocks, f32),
            pltpu.VMEM(blocks, i32),
            pltpu.VMEM((8, 8, LANES), f32),
        ),
        1.2,
        in_specs=[SMEM] + [VMEM] * 4,
        out_specs=(SMEM,) + (VMEM,) * 7,
    )(*inputs)
    def device(z, y, x):
        return (z * count_y + y) * count_x + x

    def lanes(route):
        return [(device(*source, x), device(*target, x)) for source, target in route for x in range(count_x)]

    def twins(z, y):
        return both([(device(z, y, x), device(z, y, x + 1)) for x in range(0, count_x, 2)])

    last = count_y - 1
    ring = [((1, 0), (0, 1)), ((0, last), (1, last))]
    ring += [((0, y), (0, y + 1)) for y in range(1, last)] + [((1, y + 1), (1, y)) for y in range(last)]
    ring = lanes(ring) + twins(0, 0)
    diagonal = [((1, 0), (0, 0)), ((0, 0), (0, 1)), ((0, 1), (1, 0))]
    for y in range(1, last):
        diagonal += both([((1, y), (0, y + 1))])
    diagonal = lanes(diagonal) + twins(1, last)
    axes = ("bz", "by", "bx")
    bulk = lax.ppermute(bulk, "bz", [(0, 1), (1, 0)])
    first = lax.ppermute(first, axes, ring)
    second = lax.ppermute(second, axes, diagonal)

    cells, weights, mix, columns = call(
        cells_kernel,
        "own_cells",
        (
            pltpu.VMEM((size, cols), bf16),
            pltpu.VMEM((cols, 2 * cols), bf16),
            pltpu.VMEM((128, 80), bf16),
            pltpu.VMEM((layers, LANES), i32),
        ),
        0.5,
    )(place, dense, index, inside, tables)
    whole = pltpu.VMEM((tiles, 2 * size + 3 * 4 * half, LANES), f32)
    along = call(own_kernel, "own_slab", whole, 0.4)(place, cells, weights)
    edges = pltpu.VMEM((cols // LANES, 16 * layers + 8, LANES), f32)
    packed = pltpu.VMEM((tiles, 32 * layers, LANES), bf16)
    lines = pltpu.VMEM((tiles, 16 * layers + 8, LANES), f32)
    part = call(
        own_tiles_kernel,
        "own_tiles",
        pltpu.VMEM((tiles, 16, 8, LANES), f32),
        0.1,
        [edges, packed, lines],
    )(place, tables, weights, inside, mix, along)
    ends = call(
        functools.partial(side_kernel, rows),
        "side_columns",
        pltpu.VMEM((2, layers, LANES), i32),
        0.1,
        [pltpu.VMEM((layers, LANES), i32)],
    )(place, columns, bulk, second, first, part)
    pairs = [(x, x + 1) for x in range(0, count_x, 2)]
    cross = [(x, (x + 1) % count_x) for x in range(1, count_x, 2)]
    beside = lax.ppermute(ends, "bx", both(pairs))
    across = lax.ppermute(ends, "bx", both(cross))
    along = call(other_kernel, "other_slab", whole, 0.8, [pltpu.VMEM((size, cols), bf16)], aliases={5: 0})(
        place, bulk, tables, weights, ends, along
    )
    image, mine = call(
        tiles_kernel,
        "render_tiles",
        (pltpu.VMEM((tiles, 4, rows + 8, LANES), f32), pltpu.VMEM((8, layers, LANES), f32)),
        2.0,
        [
            edges,
            packed,
            lines,
            pltpu.VMEM((tiles, 16 * layers + 16, LANES), f32),
            pltpu.VMEM((tiles, 16, LANES), f32),
        ],
    )(place, tables, weights, bulk, inside, second, first, ends, mix, part, along)
    return call(
        edge_kernel,
        "edge_columns",
        jax.ShapeDtypeStruct((4, rows, 2 * cols), f32),
        1.0,
        [
            pltpu.VMEM((2, 16, 2 * layers, LANES), f32),
            pltpu.VMEM((8, LANES), f32),
            pltpu.VMEM((LANES, LANES), f32),
            pltpu.VMEM((2, 4, rows + 8, LANES), f32),
            pltpu.SemaphoreType.DMA((tiles,)),
        ],
        out_specs=pl.BlockSpec(memory_space=pltpu.HBM),
    )(place, tables, beside, across, mine, image)


def on_device(density, bin_index, tf_colour, tf_extinction, slab_rank):
    if lax.axis_size("bz") == 2:
        return two_slab_device(density, bin_index, tf_colour, tf_extinction, slab_rank)
    return general_device(density, bin_index, tf_colour, tf_extinction, slab_rank)


def solution(mesh):
    return jax.shard_map(
        on_device,
        mesh=mesh,
        in_specs=(P("bz", "by", "bx"), P("bz", "by", "bx"), P(), P(), P()),
        out_specs=P(None, ("by", "bz"), "bx"),
        check_vma=False,
    )
```

```python
import functools

import jax
import jax.numpy as jnp
from jax import lax
from jax.experimental import pallas as pl
from jax.experimental.pallas import tpu as pltpu
from jax.sharding import PartitionSpec as P


def with_halo(block, sides, width):
    for axis, dim in sides:
        count = lax.axis_size(axis)
        forward = [(i, i + 1) for i in range(count - 1)]
        backward = [(target, source) for source, target in forward]
        low = lax.ppermute(
            lax.slice_in_dim(block, block.shape[dim] - width, None, axis=dim), axis, forward
        )
        high = lax.ppermute(lax.slice_in_dim(block, 0, width, axis=dim), axis, backward)
        block = jnp.concatenate([low, block, high], axis=dim)
    return block


def partner_2(block, axis, stride):
    count = lax.axis_size(axis)
    route = []
    for low in range(count):
        high = low | 1 << stride
        if high != low and high < count:
            route += [(low, high), (high, low)]
    return lax.ppermute(block, axis, route)


def resample_table(length):
    row_index = lax.broadcasted_iota(jnp.int32, (2 * length, length + 2), 0)
    col_index = lax.broadcasted_iota(jnp.int32, (2 * length, length + 2), 1)
    centre = row_index // 2
    parity = row_index % 2
    weights_table = jnp.where(col_index == centre + 1, 0.75, 0.0)
    weights_table = weights_table + jnp.where((col_index == centre) & (parity == 0), 0.25, 0.0)
    weights_table = weights_table + jnp.where((col_index == centre + 2) & (parity == 1), 0.25, 0.0)
    return weights_table.astype(jnp.bfloat16)


def blend_over(in_front, behind):
    return in_front + (1.0 - in_front[3])[None] * behind


def classify(density, bin_index, tf_colour, tf_extinction, total_depth):
    depth_cells, height_cells, width_cells = density.shape
    lookup = jnp.concatenate([tf_colour, tf_extinction[None, :]], axis=0)
    table_size = lookup.shape[1]
    bin_rows = lax.broadcasted_iota(jnp.int32, (table_size, 1), 0)
    flat_bins = bin_index.reshape(depth_cells, height_cells * width_cells)
    flat_density = density.reshape(depth_cells, height_cells * width_cells)

    def one_layer(layer, result):
        layer_bins = lax.dynamic_index_in_dim(flat_bins, layer, 0, keepdims=True)
        layer_density = lax.dynamic_index_in_dim(flat_density, layer, 0, keepdims=False)
        one_hot = (layer_bins == bin_rows).astype(jnp.bfloat16)
        values = jnp.dot(lookup, one_hot, preferred_element_type=jnp.float32)
        opacity = 1.0 - jnp.exp(-values[3] * layer_density / total_depth)
        cells = jnp.concatenate([values[:3] * opacity[None], opacity[None]], axis=0).astype(
            jnp.bfloat16
        )
        return lax.dynamic_update_slice_in_dim(result, cells[:, None], layer, 1)

    start_cells = jnp.zeros((4, depth_cells, height_cells * width_cells), jnp.bfloat16)
    classified = lax.fori_loop(0, depth_cells, one_layer, start_cells)
    return classified.reshape(4, depth_cells, height_cells, width_cells)


def general_device(density, bin_index, tf_colour, tf_extinction, slab_rank):
    slab_count = lax.axis_size("bz")
    depth_cells, height_cells, width_cells = density.shape
    total_depth = float(depth_cells * slab_count)
    colour_cells = classify(density, bin_index, tf_colour, tf_extinction, total_depth)
    padded = with_halo(colour_cells, (("bz", 1), ("by", 2), ("bx", 3)), 1)
    along_x = jnp.einsum(
        "czyq,pq->czyp", padded, resample_table(width_cells), preferred_element_type=jnp.float32
    ).astype(jnp.bfloat16)
    y_table = resample_table(height_cells)

    def add_sample(sample_index, image_now):
        centre = sample_index // 2
        parity = sample_index % 2
        layers = lax.dynamic_slice_in_dim(along_x, centre, 3, 1).astype(jnp.float32)
        lower_weight = jnp.where(parity == 0, 0.25, 0.0)
        upper_weight = jnp.where(parity == 1, 0.25, 0.0)
        mixed_layer = (
            lower_weight * layers[:, 0] + 0.75 * layers[:, 1] + upper_weight * layers[:, 2]
        ).astype(jnp.bfloat16)
        sample = jnp.einsum("qy,cyp->cqp", y_table, mixed_layer, preferred_element_type=jnp.float32)
        return blend_over(image_now, sample)

    start_image = jnp.zeros((4, 2 * height_cells, 2 * width_cells), jnp.float32)
    slab_image = lax.fori_loop(0, 2 * depth_cells, add_sample, start_image)
    rows_piece = 2 * height_cells // slab_count
    my_index = lax.axis_index("bz")
    bit_levels = slab_count.bit_length() - 1
    composite = slab_image.reshape((4,) + (2,) * bit_levels + (rows_piece, 2 * width_cells))
    my_rank = lax.dynamic_index_in_dim(slab_rank, my_index, 0, keepdims=False)
    for level in range(bit_levels):
        position = bit_levels - level
        my_bit = my_index // 2**level % 2
        kept_half = lax.dynamic_index_in_dim(composite, my_bit, position, keepdims=False)
        outgoing = lax.dynamic_index_in_dim(composite, 1 - my_bit, position, keepdims=False)
        incoming = partner_2(outgoing, "bz", level)
        partner = my_index + (1 - 2 * my_bit) * 2**level
        partner_rank = lax.dynamic_index_in_dim(slab_rank, partner, 0, keepdims=False)
        mine_first = my_rank < partner_rank
        composite = blend_over(
            jnp.where(mine_first, kept_half, incoming), jnp.where(mine_first, incoming, kept_half)
        )
    return composite


LANES = 128
LEVELS = 65535.0
VMEM = pl.BlockSpec(memory_space=pltpu.VMEM)
SMEM = pl.BlockSpec(memory_space=pltpu.SMEM)
FLIP, ME, HAS_NEAR, TURNED, ODD_X, HAS_RIGHT, HAS_LEFT = range(7)


def pack_words(density, bins):
    level = (density * LEVELS + 0.5).astype(jnp.int32)
    return lax.shift_left(level, 16) | bins


def unpack_words(words):
    density = lax.shift_right_logical(words, 16).astype(jnp.float32) * (1.0 / LEVELS)
    return density, words & 0xFFFF


def cell_values(density, bins, tables, depth):
    low_bits = bins & (LANES - 1)
    upper = bins >= LANES

    def pick(channel):
        first, second = tables[channel]
        return jnp.where(
            upper,
            jnp.take_along_axis(second, low_bits, axis=1, mode="promise_in_bounds"),
            jnp.take_along_axis(first, low_bits, axis=1, mode="promise_in_bounds"),
        )

    opacity = (1.0 - jnp.exp(-pick(3) * density / depth)) * (1.0 / 64.0)
    return [pick(0) * opacity, pick(1) * opacity, pick(2) * opacity, opacity]


def read_tables(tables_ref):
    return [[tables_ref[2 * channel + half] for half in range(2)] for channel in range(4)]


def cost(microseconds):
    return pl.CostEstimate(
        flops=int(1e9 * microseconds), bytes_accessed=int(3.6e6 * microseconds), transcendentals=0
    )


def stage_kernel(
    rank_ref, density_ref, bins_ref, colour_ref, extinction_ref,
    place_ref, first_ref, second_ref, bulk_ref, inside_ref, dense_ref, index_ref, tables_ref,
):
    me, me_y, me_x = lax.axis_index("bz"), lax.axis_index("by"), lax.axis_index("bx")
    past = jnp.where(me == 0, me_y, lax.axis_size("by") - 1 - me_y)
    for at, value in enumerate(
        (
            rank_ref[0],
            me,
            jnp.minimum(past, 1),
            jnp.where((me == 0) & (me_y == 1), 1, 0),
            lax.rem(me_x, 2),
            jnp.where(me_x + 1 < lax.axis_size("bx"), 1, 0),
            jnp.minimum(me_x, 1),
        )
    ):
        place_ref[at] = value
    layers, rows, cols = density_ref.shape
    front = me == 0
    inner = me_y > 0
    for z in range(layers):
        top, bottom = [
            pack_words(density_ref[z, r : r + 1, :], bins_ref[z, r : r + 1, :]) for r in (0, rows - 1)
        ]
        first_ref[z : z + 1, :] = jnp.where(jnp.logical_not(front) & inner, top, bottom)
        second_ref[z : z + 1, :] = jnp.where(front & inner, top, bottom)
        for tile in range(cols // LANES):
            lanes = slice(tile * LANES, (tile + 1) * LANES)
            dense_ref[z, tile, 0:rows] = density_ref[z, :, lanes]
            index_ref[z, tile, 0:rows] = bins_ref[z, :, lanes]
    pack_block(front, dense_ref, index_ref, bulk_ref, inside_ref)
    colour = colour_ref[...].astype(jnp.float32)
    extinction = extinction_ref[...].astype(jnp.float32).reshape(1, 2 * LANES)
    for channel in range(4):
        line = extinction if channel == 3 else colour[channel : channel + 1]
        for half in range(2):
            tables_ref[2 * channel + half] = jnp.broadcast_to(
                line[:, half * LANES : (half + 1) * LANES], (8, LANES)
            )


def pack_block(front, dense_ref, index_ref, bulk_ref, inside_ref):
    layers, tiles, rows = dense_ref.shape[0], dense_ref.shape[1], dense_ref.shape[2] - 8
    half = rows // 2
    start = jnp.where(front, half, 0)
    for tile in range(tiles):
        lanes = slice(tile * LANES, (tile + 1) * LANES)
        for z in range(layers):
            for part in range(2):
                at = pl.ds(start + part, half // 2, stride=2)
                bulk_ref[2 * z + part, :, lanes] = pack_words(
                    dense_ref[z, tile, at, :], index_ref[z, tile, at, :]
                )
            line = [
                pack_words(dense_ref[z, tile, r : r + 1, :], index_ref[z, tile, r : r + 1, :])
                for r in (half - 1, half)
            ]
            bulk_ref[2 * layers, z : z + 1, lanes] = jnp.where(front, line[0], line[1])
            inside_ref[z : z + 1, lanes] = jnp.where(front, line[1], line[0])


def near_words(slab, place_ref, first_ref, second_ref):
    own = (place_ref[ME] == slab) != (place_ref[TURNED] == 1)
    words = jnp.where(own, first_ref[...], second_ref[...])
    return jnp.where(place_ref[HAS_NEAR] == 1, words, 0)


def column_lines(me, read_words, inside, lines_ref, rows):
    layers, cols = inside.shape
    front = me == 0
    start = me * (rows // 2)
    middle = LANES // 2
    lane_at = lax.broadcasted_iota(jnp.int32, (8, LANES), 1)
    row_at = start + 2 * lax.broadcasted_iota(jnp.int32, (8, LANES), 0)
    for z in range(layers):
        line = jnp.zeros((8, LANES), jnp.int32)
        for part in range(2):
            first = read_words(z, part, 0)[:, 0:1]
            last = read_words(z, part, cols // LANES - 1)[:, LANES - 1 : LANES]
            line += jnp.where(lane_at == row_at + part, first, 0)
            line += jnp.where(lane_at == row_at + part + middle, last, 0)
        lines_ref[z : z + 1, :] = jnp.sum(line, axis=0, keepdims=True)
    beside = jnp.where(front, rows // 2, rows // 2 - 1)
    lines = jnp.where(lane_at == beside, inside[:, 0:1], lines_ref[...])
    lines_ref[...] = jnp.where(lane_at == beside + middle, inside[:, cols - 1 : cols], lines)


def side_kernel(
    rows, place_ref, columns_ref, bulk_ref, second_ref, first_ref, part_ref, ends_ref, other_ref
):
    layers, _ = columns_ref.shape
    me = place_ref[ME]
    front = me == 0
    lane_at = lax.broadcasted_iota(jnp.int32, (layers, LANES), 1)

    def read_words(z, part, tile):
        return bulk_ref[2 * z + part, :, tile * LANES : (tile + 1) * LANES]

    column_lines(me, read_words, bulk_ref[2 * layers], other_ref, rows)
    for slab in range(2):
        mine = front if slab == 0 else jnp.logical_not(front)
        columns = jnp.where(mine, columns_ref[...], other_ref[...])
        near = near_words(slab, place_ref, first_ref, second_ref)
        cols = near.shape[1]
        columns = jnp.where(lane_at == rows, near[:, 0:1], columns)
        ends_ref[slab] = jnp.where(
            lane_at == LANES // 2 + rows, near[:, cols - 1 : cols], columns
        )


def fill_weights(weights_ref):
    cols = weights_ref.shape[0]
    row = lax.broadcasted_iota(jnp.int32, (LANES, 2 * LANES), 0)
    at = lax.broadcasted_iota(jnp.int32, (LANES, 2 * LANES), 1)
    place = at - 2 * row
    block = jnp.where(
        (place == 0) | (place == 1), 3.0, jnp.where((place == -1) | (place == 2), 1.0, 0.0)
    ).astype(jnp.bfloat16)
    after = jnp.where((row == LANES - 1) & (at == 0), 1.0, 0.0).astype(jnp.bfloat16)
    before = jnp.where((row == 0) & (at == 2 * LANES - 1), 1.0, 0.0).astype(jnp.bfloat16)
    count = cols // LANES
    for i in range(count):
        for j in range(count):
            piece = block if i == j else after if j == i + 1 else before if j == i - 1 else None
            if piece is None:
                piece = jnp.zeros((LANES, 2 * LANES), jnp.bfloat16)
            weights_ref[i * LANES : (i + 1) * LANES, 2 * j * LANES : 2 * (j + 1) * LANES] = piece


def classify_rows(read_cells, tables, cells_ref, layers, tiles):
    total = float(2 * layers)
    for z in range(layers):
        for tile in range(tiles):
            even = cell_values(*read_cells(z, 0, tile), tables, total)
            odd = cell_values(*read_cells(z, 1, tile), tables, total)
            for channel in range(4):
                base = (z * 4 + channel) * 16
                block = jnp.concatenate([even[channel], odd[channel]], axis=0)
                cells_ref[base : base + 16, tile * LANES : (tile + 1) * LANES] = block.astype(jnp.bfloat16)


def rounded(value):
    return value.astype(jnp.bfloat16).astype(jnp.float32)


def cells_kernel(
    place_ref, dense_ref, index_ref, inside_ref, tables_ref, cells_ref, weights_ref, mix_ref, lines_ref
):
    layers, tiles, rows = dense_ref.shape[0], dense_ref.shape[1], dense_ref.shape[2] - 8
    half = rows // 2
    start = place_ref[ME] * half
    fill_weights(weights_ref)
    fill_rows(mix_ref)

    def read_cells(z, part, tile):
        at = pl.ds(start + part, half // 2, stride=2)
        return dense_ref[z, tile, at, :], index_ref[z, tile, at, :]

    classify_rows(read_cells, read_tables(tables_ref), cells_ref, layers, tiles)
    column_lines(place_ref[ME], lambda *at: pack_words(*read_cells(*at)), inside_ref[...], lines_ref, rows)


def along_columns(cells, weights_ref, store):
    result = rounded(jnp.dot(cells, weights_ref[...], preferred_element_type=jnp.float32))
    for tile in range(result.shape[1] // LANES):
        store(tile, result[:, tile * LANES : (tile + 1) * LANES])


def own_kernel(place_ref, cells_ref, weights_ref, along_ref):
    size = cells_ref.shape[0]
    pad = 64
    mine = pl.multiple_of(pad + place_ref[ME] * size, pad)

    def store(tile, block):
        along_ref[tile, 0:pad, :] = jnp.zeros((pad, LANES), jnp.float32)
        along_ref[tile, pad + 2 * size : 2 * pad + 2 * size, :] = jnp.zeros((pad, LANES), jnp.float32)
        along_ref[tile, pl.ds(mine, size), :] = block

    along_columns(cells_ref[...], weights_ref, store)


def other_kernel(
    place_ref, bulk_ref, tables_ref, weights_ref, ends_ref, own_ref, along_ref, cells_ref
):
    layers = (bulk_ref.shape[0] - 1) // 2
    cols = bulk_ref.shape[2]
    size = cells_ref.shape[0]
    pad = 64
    theirs = pl.multiple_of(pad + (1 - place_ref[ME]) * size, pad)

    def read_cells(z, part, tile):
        return unpack_words(bulk_ref[2 * z + part, :, tile * LANES : (tile + 1) * LANES])

    def store(tile, block):
        along_ref[tile, pl.ds(theirs, size), :] = block

    classify_rows(read_cells, read_tables(tables_ref), cells_ref, layers, cols // LANES)
    along_columns(cells_ref[...], weights_ref, store)


def edge_cells(near, inside, tables, cells_ref, front, base):
    layers, cols = near.shape
    for side in range(2):
        use_near = front if side == 0 else jnp.logical_not(front)
        words = jnp.where(use_near, near, inside)
        for t in range(cols // LANES):
            values = cell_values(
                *unpack_words(words[:, t * LANES : (t + 1) * LANES]), tables, float(2 * layers)
            )
            for channel in range(4):
                at = pl.ds(base + side * 4 + channel, layers, stride=8)
                cells_ref[t, at, :] = values[channel]


def edge_along(cells_ref, count, weights_ref):
    return rounded(
        sum(
            jnp.dot(
                cells_ref[t, 0:count].astype(jnp.bfloat16),
                weights_ref[t * LANES : (t + 1) * LANES, :],
                preferred_element_type=jnp.float32,
            )
            for t in range(cells_ref.shape[0])
        )
    )


def edge_lines(now, packed_ref, lines_ref, depth):
    triple = 3.0 * now
    empty = jnp.zeros((8, LANES), jnp.float32)
    for layer in range(depth):
        at = layer * 8
        here = triple[at : at + 8]
        before = now[at - 8 : at] if layer > 0 else empty
        after = now[at + 8 : at + 16] if layer + 1 < depth else empty
        line = jnp.concatenate([before + here, empty], axis=0)
        packed_ref[2 * at : 2 * at + 16, :] = line.astype(jnp.bfloat16)
        lines_ref[at : at + 8, :] = rounded(after + here)


def row_samples(value, above, below):
    sub_at = lax.broadcasted_iota(jnp.int32, (8, LANES), 0)
    low, high = value[0:8], value[8:16]
    before = jnp.where(sub_at == 0, above, pltpu.roll(high, 1, 0))
    after = jnp.where(sub_at == 7, below, pltpu.roll(low, 7, 0))
    low_centre = 3.0 * low
    high_centre = 3.0 * high
    return [before + low_centre, low_centre + high, low + high_centre, high_centre + after]


def slab_pair(
    along_refs, packed_refs, lines_refs, rows_ref, slab, lines_slab, layers, keep_first=None, keep_last=None
):
    along_at = pl.ds(pl.multiple_of(slab * (layers * 64), 64), (layers + 2) * 64)
    packed_at = pl.ds(pl.multiple_of(lines_slab * (layers * 16), 16), layers * 16)
    lines_at = pl.ds(pl.multiple_of(lines_slab * (layers * 8), 8), layers * 8 + 8)
    views = [ref.at[along_at, :] for ref in along_refs]
    packed = [ref.at[packed_at, :] for ref in packed_refs]
    lines = [ref.at[lines_at, :] for ref in lines_refs]

    def layer_rows(view, layer, channel):
        base = (layer * 4 + channel) * 16
        return view[base : base + 16, :]

    def both(pieces):
        return jnp.concatenate(pieces, axis=1)

    def blend(image, samples, keep):
        updated = []
        for tile in range(2):
            clear = [1.0 - value for value in image[tile][3]]
            updated.append([])
            for c in range(4):
                values = samples[tile][c]
                if keep is not None:
                    values = [jnp.where(keep, value, 0.0) for value in values]
                updated[tile].append([image[tile][c][i] + clear[i] * values[i] for i in range(4)])
        return updated

    zero = jnp.zeros((8, LANES), jnp.float32)
    image = [[[zero] * 4 for _ in range(4)] for _ in range(2)]
    for z in range(layers):
        triple = [[3.0 * layer_rows(v, z + 1, c) for c in range(4)] for v in views]
        mixed = [
            both([(layer_rows(v, z, c) + t[c]).astype(jnp.bfloat16) for v, t in zip(views, triple)])
            for c in range(4)
        ]
        mixed.append(both([line[z * 16 : z * 16 + 16, :] for line in packed]))
        product = jnp.dot(
            rows_ref[...], jnp.concatenate(mixed, axis=0), preferred_element_type=jnp.float32
        )
        even, odd = [], []
        for tile in range(2):
            lanes = slice(tile * LANES, (tile + 1) * LANES)
            even.append(
                [
                    [product[c * 32 + i * 8 : c * 32 + i * 8 + 8, lanes] for i in range(4)]
                    for c in range(4)
                ]
            )
            odd.append([])
            for c in range(4):
                value = rounded(layer_rows(views[tile], z + 2, c) + triple[tile][c])
                above = lines[tile][pl.ds(z * 8 + c, 8, stride=0), :]
                below = lines[tile][pl.ds(z * 8 + 4 + c, 8, stride=0), :]
                odd[tile].append(row_samples(value, above, below))
        image = blend(image, even, keep_first if z == 0 else None)
        image = blend(image, odd, keep_last if z == layers - 1 else None)
    return image


def joined(first, in_front, behind):
    top = [[jnp.where(first, x, y) for x, y in zip(a, b)] for a, b in zip(in_front, behind)]
    low = [[jnp.where(first, y, x) for x, y in zip(a, b)] for a, b in zip(in_front, behind)]
    clear = [1.0 - value for value in top[3]]
    return [[top[c][i] + clear[i] * low[c][i] for i in range(4)] for c in range(4)]


def own_tiles_kernel(
    place_ref, tables_ref, weights_ref, inside_ref, mix_ref, along_ref, part_ref, cells_ref, packed_ref, lines_ref
):
    layers, cols = inside_ref.shape
    me = place_ref[ME]
    front = me == 0
    inside = inside_ref[...]
    edge_cells(jnp.zeros_like(inside), inside, read_tables(tables_ref), cells_ref, front, 0)
    edge = edge_along(cells_ref, 8 * layers, weights_ref)
    tiles = 2 * cols // LANES
    for tile in range(tiles):
        now = edge[:, tile * LANES : (tile + 1) * LANES]
        edge_lines(now, packed_ref.at[tile], lines_ref.at[tile], layers)
    for pair in range(tiles // 2):
        at = [2 * pair, 2 * pair + 1]
        image = slab_pair(
            [along_ref.at[tile] for tile in at],
            [packed_ref.at[tile] for tile in at],
            [lines_ref.at[tile] for tile in at],
            mix_ref,
            me,
            0,
            layers,
            front,
            jnp.logical_not(front),
        )
        for index, tile in enumerate(at):
            for channel in range(4):
                for i in range(4):
                    part_ref[tile, channel * 4 + i] = image[index][channel][i]


def fill_rows(rows_ref):
    m = lax.broadcasted_iota(jnp.int32, rows_ref.shape, 0)
    k = lax.broadcasted_iota(jnp.int32, rows_ref.shape, 1)
    row = 4 * (m & 7) + (lax.shift_right_logical(m, 3) & 3)
    centre = lax.shift_right_logical(row, 1)
    beside = centre - 1 + 2 * (row & 1)
    own = k < 64
    k_channel = jnp.where(own, lax.shift_right_logical(k, 4), k & 3)
    k_row = 2 * (k & 7) + (lax.shift_right_logical(k, 3) & 1)
    k_row = jnp.where(own, k_row, jnp.where(k < 68, -1, jnp.where(k < 72, 16, 99)))
    same = k_channel == lax.shift_right_logical(m, 5)
    value = jnp.where(k_row == centre, 3.0, jnp.where(k_row == beside, 1.0, 0.0))
    rows_ref[...] = jnp.where(same, value, 0.0).astype(jnp.bfloat16)


def tiles_kernel(
    place_ref, tables_ref, weights_ref, bulk_ref, inside_ref, second_ref, first_ref, ends_ref, mix_ref,
    part_ref, along_ref, image_ref, mine_ref, cells_ref, packed_ref, lines_ref, edge_ref, between_ref,
):
    layers, cols = inside_ref.shape
    depth = 2 * layers
    tiles = 2 * cols // LANES
    me = place_ref[ME]
    front = me == 0
    tables = read_tables(tables_ref)
    for slab in range(2):
        inside = jnp.where(me == slab, inside_ref[...], bulk_ref[2 * layers])
        near = near_words(slab, place_ref, first_ref, second_ref)
        edge_cells(near, inside, tables, cells_ref, front, slab * layers * 8)
        values = cell_values(*unpack_words(ends_ref[slab]), tables, float(depth))
        for channel in range(4):
            mine_ref[slab * 4 + channel] = 3.0 * rounded(values[channel])
    edge = edge_along(cells_ref, 8 * depth, weights_ref)
    here_at, beside_at = layers * 8 - 8, layers * 8
    empty = jnp.zeros((8, LANES), jnp.float32)
    for tile in range(tiles):
        now = edge[:, tile * LANES : (tile + 1) * LANES]
        edge_lines(now, packed_ref.at[tile], lines_ref.at[tile], depth)
        upper, lower = now[here_at : here_at + 8], now[beside_at : beside_at + 8]
        between_ref[tile, 0:8] = rounded(
            jnp.where(front, lower, upper) + 3.0 * jnp.where(front, upper, lower)
        )
        edge_ref[tile, 0:8] = empty
        edge_ref[tile, 8 : 8 * depth + 8] = now
        edge_ref[tile, 8 * depth + 8 :] = empty

    row = jnp.where(front, 0, 15)
    first_layer = me * layers
    replaced = []
    for tile in range(tiles):
        inner, outer = [], []
        for z in range(layers + 2):
            at = (first_layer + z) * 64 + row
            inner.append(along_ref[tile, pl.ds(at, 4, stride=16), :])
            both = edge_ref[tile, pl.ds(pl.multiple_of((first_layer + z) * 8, 8), 8), :]
            outer.append(jnp.where(front, both[0:4], both[4:8]))
        image = jnp.zeros((4, LANES), jnp.float32)
        for z in range(layers):
            for parity in range(2):
                beside = z + 2 * parity
                sample = rounded(outer[beside] + 3.0 * outer[z + 1]) + 3.0 * rounded(
                    inner[beside] + 3.0 * inner[z + 1]
                )
                if (z, parity) == (0, 0):
                    sample = jnp.where(front, sample, 0.0)
                if (z, parity) == (layers - 1, 1):
                    sample = jnp.where(front, 0.0, sample)
                image = image + (1.0 - image[3:4]) * sample
        replaced.append(image)

    sub_at = lax.broadcasted_iota(jnp.int32, (8, LANES), 0)
    for pair in range(tiles // 2):
        at = [2 * pair, 2 * pair + 1]
        other = slab_pair(
            [along_ref.at[tile] for tile in at],
            [packed_ref.at[tile] for tile in at],
            [lines_ref.at[tile] for tile in at],
            mix_ref,
            1 - me,
            1 - me,
            layers,
        )
        for index, tile in enumerate(at):
            here = pl.multiple_of(jnp.where(front, layers, layers + 1) * 64, 64)
            beside = pl.multiple_of(jnp.where(front, layers + 1, layers) * 64, 64)
            between, part = [], []
            for c in range(4):
                value = rounded(
                    along_ref[tile, pl.ds(beside + c * 16, 16), :]
                    + 3.0 * along_ref[tile, pl.ds(here + c * 16, 16), :]
                )
                above = between_ref[tile, pl.ds(c, 8, stride=0), :]
                below = between_ref[tile, pl.ds(c + 4, 8, stride=0), :]
                between.append(row_samples(value, above, below))
                values = [part_ref[tile, c * 4 + i] for i in range(4)]
                line = replaced[tile][c : c + 1]
                values[0] = jnp.where(sub_at == 0, jnp.where(front, line, values[0]), values[0])
                values[3] = jnp.where(sub_at == 7, jnp.where(front, values[3], line), values[3])
                part.append(values)
            mine = joined(front, part, between)
            image = joined((me ^ place_ref[FLIP]) == 0, mine, other[index])
            for c in range(4):
                for i in range(4):
                    image_ref[tile, c, pl.ds(i, 8, stride=4), :] = image[c][i]


def edge_kernel(
    place_ref, tables_ref, beside_ref, across_ref, mine_ref, image_ref,
    out_ref, final_ref, turned_ref, fixed_ref, sems,
):
    rows = out_ref.shape[1]
    cols = out_ref.shape[2] // 2
    half = rows // 2
    layers = beside_ref.shape[1]
    tiles = 2 * cols // LANES
    middle = LANES // 2
    front = place_ref[ME] == 0
    start = pl.multiple_of(place_ref[ME] * half, half)
    even_x = place_ref[ODD_X] == 0
    tables = read_tables(tables_ref)

    def to_out(tile, source):
        lanes = pl.ds(tile * LANES, LANES)
        return pltpu.make_async_copy(
            source.at[:, pl.ds(0, rows), :], out_ref.at[:, :, lanes], sems.at[tile]
        )

    copies = [to_out(tile, image_ref.at[tile]) for tile in range(1, tiles - 1)]
    for copy in copies:
        copy.start()
    lane_at = lax.broadcasted_iota(jnp.int32, (layers, LANES), 1)
    layer_at = lax.broadcasted_iota(jnp.int32, (layers, LANES), 0)
    first_lane = (lane_at & (middle - 1)) == 0
    along = [[], []]
    samples = {}
    for slab in range(2):
        right = jnp.where(even_x, beside_ref[slab], across_ref[slab])
        left = jnp.where(even_x, across_ref[slab], beside_ref[slab])
        right = jnp.where(place_ref[HAS_RIGHT] == 1, right, 0)
        left = jnp.where(place_ref[HAS_LEFT] == 1, left, 0)
        words = pltpu.roll(jnp.where(lane_at < middle, right, left), middle, 1)
        halo = cell_values(*unpack_words(words), tables, float(2 * layers))
        for channel in range(4):
            along[slab].append(rounded(mine_ref[slab * 4 + channel] + rounded(halo[channel])))
    for channel in range(4):
        front_part, back_part = along[0][channel], along[1][channel]
        down = [pltpu.roll(front_part, 1, 0), pltpu.roll(back_part, 1, 0)]
        up = [pltpu.roll(front_part, layers - 1, 0), pltpu.roll(back_part, layers - 1, 0)]
        is_first, is_last = layer_at == 0, layer_at == layers - 1
        before = [jnp.where(is_first, 0.0, down[0]), jnp.where(is_first, down[0], down[1])]
        after = [jnp.where(is_last, up[1], up[0]), jnp.where(is_last, 0.0, up[1])]
        for slab in range(2):
            triple = 3.0 * along[slab][channel]
            for parity, other in enumerate((before[slab], after[slab])):
                mixed = rounded(other + triple)
                centre = 3.0 * mixed
                above = pltpu.roll(mixed, 1, 1)
                near = pltpu.roll(mixed, LANES - rows, 1)
                above = jnp.where(first_lane, jnp.where(front, near, above), above)
                below = pltpu.roll(mixed, LANES - 1, 1)
                samples[slab, parity, 0, channel] = above + centre
                samples[slab, parity, 1, channel] = centre + below

    def over(in_front, behind):
        clear = 1.0 - in_front[3]
        return [top + clear * low for top, low in zip(in_front, behind)]

    slabs = []
    for slab in range(2):
        slabs.append([])
        for odd in range(2):
            image = over(
                *[[samples[slab, parity, odd, channel] for channel in range(4)] for parity in range(2)]
            )
            step = 1
            while step < layers:
                image = over(image, [pltpu.roll(value, layers - step, 0) for value in image])
                step *= 2
            slabs[slab].append(image)
    in_order = place_ref[FLIP] == 0
    image = [
        over(
            *[
                [jnp.where(in_order, x, y) for x, y in zip(slabs[at][odd], slabs[1 - at][odd])]
                for at in range(2)
            ]
        )
        for odd in range(2)
    ]
    for odd in range(2):
        for channel in range(4):
            at = odd * 4 + channel
            final_ref[at : at + 1, :] = image[odd][channel][0:1]
    turned_ref[:, 0:8] = final_ref[...].T
    wide = lax.broadcasted_iota(jnp.int32, (half, LANES), 1)
    for index, tile in enumerate((0, tiles - 1)):
        place = wide == index * (LANES - 1)
        turned = turned_ref[pl.ds(start + index * middle, half), :]
        for channel in range(4):
            for odd in range(2):
                at = pl.ds(odd, half, stride=2)
                column = odd * 4 + channel
                fixed_ref[index, channel, at, :] = jnp.where(
                    place, turned[:, column : column + 1], image_ref[tile, channel, at, :]
                )
        copies.append(to_out(tile, fixed_ref.at[index]))
        copies[-1].start()
    for copy in copies:
        copy.wait()


def two_slab_device(density, bin_index, tf_colour, tf_extinction, slab_rank):
    layers, rows, cols = density.shape
    half = rows // 2
    tiles = 2 * cols // LANES
    size = layers * 4 * half
    count_y, count_x = lax.axis_size("by"), lax.axis_size("bx")
    f32, bf16, i32 = jnp.float32, jnp.bfloat16, jnp.int32

    def call(kernel, name, out_shape, time, scratch_shapes=(), in_specs=None, out_specs=None, aliases={}):
        def run(*operands):
            return pl.pallas_call(
                kernel,
                out_shape=out_shape,
                in_specs=in_specs or [SMEM] + [VMEM] * (len(operands) - 1),
                out_specs=out_specs
                or ((VMEM,) * len(out_shape) if isinstance(out_shape, tuple) else VMEM),
                scratch_shapes=scratch_shapes,
                input_output_aliases=aliases,
                compiler_params=pltpu.CompilerParams(vmem_limit_bytes=16 * 1024 * 1024),
                cost_estimate=cost(time),
                name=name,
            )(*operands)

        return run

    def both(route):
        return route + [(target, source) for source, target in route]

    blocks = (layers, cols // LANES, rows + 8, LANES)
    row = pltpu.VMEM((layers, cols), i32)
    inputs = [
        pltpu.with_memory_space_constraint(x, pltpu.HBM)
        for x in (slab_rank, density, bin_index, tf_colour, tf_extinction)
    ]
    place, first, second, bulk, inside, dense, index, tables = call(
        stage_kernel,
        "stage_block",
        (
            pltpu.SMEM((7,), i32),
            row,
            row,
            pltpu.VMEM((2 * layers + 1, 8, cols), i32),
            row,
            pltpu.VMEM(blocks, f32),
            pltpu.VMEM(blocks, i32),
            pltpu.VMEM((8, 8, LANES), f32),
        ),
        1.2,
        in_specs=[SMEM] + [VMEM] * 4,
        out_specs=(SMEM,) + (VMEM,) * 7,
    )(*inputs)
    def device(z, y, x):
        return (z * count_y + y) * count_x + x

    def lanes(route):
        return [(device(*source, x), device(*target, x)) for source, target in route for x in range(count_x)]

    def twins(z, y):
        return both([(device(z, y, x), device(z, y, x + 1)) for x in range(0, count_x, 2)])

    last = count_y - 1
    ring = [((1, 0), (0, 1)), ((0, last), (1, last))]
    ring += [((0, y), (0, y + 1)) for y in range(1, last)] + [((1, y + 1), (1, y)) for y in range(last)]
    ring = lanes(ring) + twins(0, 0)
    diagonal = [((1, 0), (0, 0)), ((0, 0), (0, 1)), ((0, 1), (1, 0))]
    for y in range(1, last):
        diagonal += both([((1, y), (0, y + 1))])
    diagonal = lanes(diagonal) + twins(1, last)
    axes = ("bz", "by", "bx")
    bulk = lax.ppermute(bulk, "bz", [(0, 1), (1, 0)])
    first = lax.ppermute(first, axes, ring)
    second = lax.ppermute(second, axes, diagonal)

    cells, weights, mix, columns = call(
        cells_kernel,
        "own_cells",
        (
            pltpu.VMEM((size, cols), bf16),
            pltpu.VMEM((cols, 2 * cols), bf16),
            pltpu.VMEM((128, 80), bf16),
            pltpu.VMEM((layers, LANES), i32),
        ),
        0.5,
    )(place, dense, index, inside, tables)
    whole = pltpu.VMEM((tiles, 2 * size + 3 * 4 * half, LANES), f32)
    along = call(own_kernel, "own_slab", whole, 0.4)(place, cells, weights)
    edges = pltpu.VMEM((cols // LANES, 16 * layers + 8, LANES), f32)
    packed = pltpu.VMEM((tiles, 32 * layers, LANES), bf16)
    lines = pltpu.VMEM((tiles, 16 * layers + 8, LANES), f32)
    part = call(
        own_tiles_kernel,
        "own_tiles",
        pltpu.VMEM((tiles, 16, 8, LANES), f32),
        0.1,
        [edges, packed, lines],
    )(place, tables, weights, inside, mix, along)
    ends = call(
        functools.partial(side_kernel, rows),
        "side_columns",
        pltpu.VMEM((2, layers, LANES), i32),
        0.1,
        [pltpu.VMEM((layers, LANES), i32)],
    )(place, columns, bulk, second, first, part)
    pairs = [(x, x + 1) for x in range(0, count_x, 2)]
    cross = [(x, (x + 1) % count_x) for x in range(1, count_x, 2)]
    beside = lax.ppermute(ends, "bx", both(pairs))
    across = lax.ppermute(ends, "bx", both(cross))
    along = call(other_kernel, "other_slab", whole, 0.8, [pltpu.VMEM((size, cols), bf16)], aliases={5: 0})(
        place, bulk, tables, weights, ends, along
    )
    image, mine = call(
        tiles_kernel,
        "render_tiles",
        (pltpu.VMEM((tiles, 4, rows + 8, LANES), f32), pltpu.VMEM((8, layers, LANES), f32)),
        2.0,
        [
            edges,
            packed,
            lines,
            pltpu.VMEM((tiles, 16 * layers + 16, LANES), f32),
            pltpu.VMEM((tiles, 16, LANES), f32),
        ],
    )(place, tables, weights, bulk, inside, second, first, ends, mix, part, along)
    return call(
        edge_kernel,
        "edge_columns",
        jax.ShapeDtypeStruct((4, rows, 2 * cols), f32),
        1.0,
        [
            pltpu.VMEM((8, LANES), f32),
            pltpu.VMEM((LANES, LANES), f32),
            pltpu.VMEM((2, 4, rows + 8, LANES), f32),
            pltpu.SemaphoreType.DMA((tiles,)),
        ],
        out_specs=pl.BlockSpec(memory_space=pltpu.HBM),
    )(place, tables, beside, across, mine, image)


def on_device(density, bin_index, tf_colour, tf_extinction, slab_rank):
    if lax.axis_size("bz") == 2:
        return two_slab_device(density, bin_index, tf_colour, tf_extinction, slab_rank)
    return general_device(density, bin_index, tf_colour, tf_extinction, slab_rank)


def solution(mesh):
    return jax.shard_map(
        on_device,
        mesh=mesh,
        in_specs=(P("bz", "by", "bx"), P("bz", "by", "bx"), P(), P(), P()),
        out_specs=P(None, ("by", "bz"), "bx"),
        check_vma=False,
    )
```

```python
import functools

import jax
import jax.numpy as jnp
from jax import lax
from jax.experimental import pallas as pl
from jax.experimental.pallas import tpu as pltpu
from jax.sharding import PartitionSpec as P


def with_halo(block, sides, width):
    for axis, dim in sides:
        count = lax.axis_size(axis)
        forward = [(i, i + 1) for i in range(count - 1)]
        backward = [(target, source) for source, target in forward]
        low = lax.ppermute(
            lax.slice_in_dim(block, block.shape[dim] - width, None, axis=dim), axis, forward
        )
        high = lax.ppermute(lax.slice_in_dim(block, 0, width, axis=dim), axis, backward)
        block = jnp.concatenate([low, block, high], axis=dim)
    return block


def partner_2(block, axis, stride):
    count = lax.axis_size(axis)
    route = []
    for low in range(count):
        high = low | 1 << stride
        if high != low and high < count:
            route += [(low, high), (high, low)]
    return lax.ppermute(block, axis, route)


def resample_table(length):
    row_index = lax.broadcasted_iota(jnp.int32, (2 * length, length + 2), 0)
    col_index = lax.broadcasted_iota(jnp.int32, (2 * length, length + 2), 1)
    centre = row_index // 2
    parity = row_index % 2
    weights_table = jnp.where(col_index == centre + 1, 0.75, 0.0)
    weights_table = weights_table + jnp.where((col_index == centre) & (parity == 0), 0.25, 0.0)
    weights_table = weights_table + jnp.where((col_index == centre + 2) & (parity == 1), 0.25, 0.0)
    return weights_table.astype(jnp.bfloat16)


def blend_over(in_front, behind):
    return in_front + (1.0 - in_front[3])[None] * behind


def classify(density, bin_index, tf_colour, tf_extinction, total_depth):
    depth_cells, height_cells, width_cells = density.shape
    lookup = jnp.concatenate([tf_colour, tf_extinction[None, :]], axis=0)
    table_size = lookup.shape[1]
    bin_rows = lax.broadcasted_iota(jnp.int32, (table_size, 1), 0)
    flat_bins = bin_index.reshape(depth_cells, height_cells * width_cells)
    flat_density = density.reshape(depth_cells, height_cells * width_cells)

    def one_layer(layer, result):
        layer_bins = lax.dynamic_index_in_dim(flat_bins, layer, 0, keepdims=True)
        layer_density = lax.dynamic_index_in_dim(flat_density, layer, 0, keepdims=False)
        one_hot = (layer_bins == bin_rows).astype(jnp.bfloat16)
        values = jnp.dot(lookup, one_hot, preferred_element_type=jnp.float32)
        opacity = 1.0 - jnp.exp(-values[3] * layer_density / total_depth)
        cells = jnp.concatenate([values[:3] * opacity[None], opacity[None]], axis=0).astype(
            jnp.bfloat16
        )
        return lax.dynamic_update_slice_in_dim(result, cells[:, None], layer, 1)

    start_cells = jnp.zeros((4, depth_cells, height_cells * width_cells), jnp.bfloat16)
    classified = lax.fori_loop(0, depth_cells, one_layer, start_cells)
    return classified.reshape(4, depth_cells, height_cells, width_cells)


def general_device(density, bin_index, tf_colour, tf_extinction, slab_rank):
    slab_count = lax.axis_size("bz")
    depth_cells, height_cells, width_cells = density.shape
    total_depth = float(depth_cells * slab_count)
    colour_cells = classify(density, bin_index, tf_colour, tf_extinction, total_depth)
    padded = with_halo(colour_cells, (("bz", 1), ("by", 2), ("bx", 3)), 1)
    along_x = jnp.einsum(
        "czyq,pq->czyp", padded, resample_table(width_cells), preferred_element_type=jnp.float32
    ).astype(jnp.bfloat16)
    y_table = resample_table(height_cells)

    def add_sample(sample_index, image_now):
        centre = sample_index // 2
        parity = sample_index % 2
        layers = lax.dynamic_slice_in_dim(along_x, centre, 3, 1).astype(jnp.float32)
        lower_weight = jnp.where(parity == 0, 0.25, 0.0)
        upper_weight = jnp.where(parity == 1, 0.25, 0.0)
        mixed_layer = (
            lower_weight * layers[:, 0] + 0.75 * layers[:, 1] + upper_weight * layers[:, 2]
        ).astype(jnp.bfloat16)
        sample = jnp.einsum("qy,cyp->cqp", y_table, mixed_layer, preferred_element_type=jnp.float32)
        return blend_over(image_now, sample)

    start_image = jnp.zeros((4, 2 * height_cells, 2 * width_cells), jnp.float32)
    slab_image = lax.fori_loop(0, 2 * depth_cells, add_sample, start_image)
    rows_piece = 2 * height_cells // slab_count
    my_index = lax.axis_index("bz")
    bit_levels = slab_count.bit_length() - 1
    composite = slab_image.reshape((4,) + (2,) * bit_levels + (rows_piece, 2 * width_cells))
    my_rank = lax.dynamic_index_in_dim(slab_rank, my_index, 0, keepdims=False)
    for level in range(bit_levels):
        position = bit_levels - level
        my_bit = my_index // 2**level % 2
        kept_half = lax.dynamic_index_in_dim(composite, my_bit, position, keepdims=False)
        outgoing = lax.dynamic_index_in_dim(composite, 1 - my_bit, position, keepdims=False)
        incoming = partner_2(outgoing, "bz", level)
        partner = my_index + (1 - 2 * my_bit) * 2**level
        partner_rank = lax.dynamic_index_in_dim(slab_rank, partner, 0, keepdims=False)
        mine_first = my_rank < partner_rank
        composite = blend_over(
            jnp.where(mine_first, kept_half, incoming), jnp.where(mine_first, incoming, kept_half)
        )
    return composite


LANES = 128
LEVELS = 65535.0
VMEM = pl.BlockSpec(memory_space=pltpu.VMEM)
SMEM = pl.BlockSpec(memory_space=pltpu.SMEM)
FLIP, ME, HAS_NEAR, TURNED, ODD_X, HAS_RIGHT, HAS_LEFT = range(7)


def pack_words(density, bins):
    level = (density * LEVELS + 0.5).astype(jnp.int32)
    return lax.shift_left(level, 16) | bins


def unpack_words(words):
    density = lax.shift_right_logical(words, 16).astype(jnp.float32) * (1.0 / LEVELS)
    return density, words & 0xFFFF


def cell_values(density, bins, tables, depth):
    low_bits = bins & (LANES - 1)
    upper = bins >= LANES

    def pick(channel):
        first, second = tables[channel]
        return jnp.where(
            upper,
            jnp.take_along_axis(second, low_bits, axis=1, mode="promise_in_bounds"),
            jnp.take_along_axis(first, low_bits, axis=1, mode="promise_in_bounds"),
        )

    opacity = (1.0 - jnp.exp(-pick(3) * density / depth)) * (1.0 / 64.0)
    return [pick(0) * opacity, pick(1) * opacity, pick(2) * opacity, opacity]


def read_tables(tables_ref):
    return [[tables_ref[2 * channel + half] for half in range(2)] for channel in range(4)]


def cost(microseconds):
    return pl.CostEstimate(
        flops=int(1e9 * microseconds), bytes_accessed=int(3.6e6 * microseconds), transcendentals=0
    )


def stage_kernel(
    rank_ref, density_ref, bins_ref, colour_ref, extinction_ref,
    place_ref, first_ref, second_ref, bulk_ref, inside_ref, dense_ref, index_ref, tables_ref,
):
    me, me_y, me_x = lax.axis_index("bz"), lax.axis_index("by"), lax.axis_index("bx")
    past = jnp.where(me == 0, me_y, lax.axis_size("by") - 1 - me_y)
    for at, value in enumerate(
        (
            rank_ref[0],
            me,
            jnp.minimum(past, 1),
            jnp.where((me == 0) & (me_y == 1), 1, 0),
            lax.rem(me_x, 2),
            jnp.where(me_x + 1 < lax.axis_size("bx"), 1, 0),
            jnp.minimum(me_x, 1),
        )
    ):
        place_ref[at] = value
    layers, rows, cols = density_ref.shape
    front = me == 0
    inner = me_y > 0
    for z in range(layers):
        top, bottom = [
            pack_words(density_ref[z, r : r + 1, :], bins_ref[z, r : r + 1, :]) for r in (0, rows - 1)
        ]
        first_ref[z : z + 1, :] = jnp.where(jnp.logical_not(front) & inner, top, bottom)
        second_ref[z : z + 1, :] = jnp.where(front & inner, top, bottom)
        for tile in range(cols // LANES):
            lanes = slice(tile * LANES, (tile + 1) * LANES)
            dense_ref[z, tile, 0:rows] = density_ref[z, :, lanes]
            index_ref[z, tile, 0:rows] = bins_ref[z, :, lanes]
    pack_block(front, dense_ref, index_ref, bulk_ref, inside_ref)
    colour = colour_ref[...].astype(jnp.float32)
    extinction = extinction_ref[...].astype(jnp.float32).reshape(1, 2 * LANES)
    for channel in range(4):
        line = extinction if channel == 3 else colour[channel : channel + 1]
        for half in range(2):
            tables_ref[2 * channel + half] = jnp.broadcast_to(
                line[:, half * LANES : (half + 1) * LANES], (8, LANES)
            )


def pack_block(front, dense_ref, index_ref, bulk_ref, inside_ref):
    layers, tiles, rows = dense_ref.shape[0], dense_ref.shape[1], dense_ref.shape[2] - 8
    half = rows // 2
    start = jnp.where(front, half, 0)
    for tile in range(tiles):
        lanes = slice(tile * LANES, (tile + 1) * LANES)
        for z in range(layers):
            for part in range(2):
                at = pl.ds(start + part, half // 2, stride=2)
                bulk_ref[2 * z + part, :, lanes] = pack_words(
                    dense_ref[z, tile, at, :], index_ref[z, tile, at, :]
                )
            line = [
                pack_words(dense_ref[z, tile, r : r + 1, :], index_ref[z, tile, r : r + 1, :])
                for r in (half - 1, half)
            ]
            bulk_ref[2 * layers, z : z + 1, lanes] = jnp.where(front, line[0], line[1])
            inside_ref[z : z + 1, lanes] = jnp.where(front, line[1], line[0])


def near_words(slab, place_ref, first_ref, second_ref):
    own = (place_ref[ME] == slab) != (place_ref[TURNED] == 1)
    words = jnp.where(own, first_ref[...], second_ref[...])
    return jnp.where(place_ref[HAS_NEAR] == 1, words, 0)


def column_lines(me, read_words, inside, lines_ref, rows):
    layers, cols = inside.shape
    front = me == 0
    start = me * (rows // 2)
    middle = LANES // 2
    lane_at = lax.broadcasted_iota(jnp.int32, (8, LANES), 1)
    row_at = start + 2 * lax.broadcasted_iota(jnp.int32, (8, LANES), 0)
    for z in range(layers):
        line = jnp.zeros((8, LANES), jnp.int32)
        for part in range(2):
            first = read_words(z, part, 0)[:, 0:1]
            last = read_words(z, part, cols // LANES - 1)[:, LANES - 1 : LANES]
            line += jnp.where(lane_at == row_at + part, first, 0)
            line += jnp.where(lane_at == row_at + part + middle, last, 0)
        lines_ref[z : z + 1, :] = jnp.sum(line, axis=0, keepdims=True)
    beside = jnp.where(front, rows // 2, rows // 2 - 1)
    lines = jnp.where(lane_at == beside, inside[:, 0:1], lines_ref[...])
    lines_ref[...] = jnp.where(lane_at == beside + middle, inside[:, cols - 1 : cols], lines)


def side_kernel(
    rows, place_ref, columns_ref, bulk_ref, second_ref, first_ref, part_ref, cells_ref, ends_ref, other_ref
):
    layers, _ = columns_ref.shape
    me = place_ref[ME]
    front = me == 0
    lane_at = lax.broadcasted_iota(jnp.int32, (layers, LANES), 1)

    def read_words(z, part, tile):
        return bulk_ref[2 * z + part, :, tile * LANES : (tile + 1) * LANES]

    column_lines(me, read_words, bulk_ref[2 * layers], other_ref, rows)
    for slab in range(2):
        mine = front if slab == 0 else jnp.logical_not(front)
        columns = jnp.where(mine, columns_ref[...], other_ref[...])
        near = near_words(slab, place_ref, first_ref, second_ref)
        cols = near.shape[1]
        columns = jnp.where(lane_at == rows, near[:, 0:1], columns)
        ends_ref[slab] = jnp.where(
            lane_at == LANES // 2 + rows, near[:, cols - 1 : cols], columns
        )


def fill_weights(weights_ref):
    cols = weights_ref.shape[0]
    row = lax.broadcasted_iota(jnp.int32, (LANES, 2 * LANES), 0)
    at = lax.broadcasted_iota(jnp.int32, (LANES, 2 * LANES), 1)
    place = at - 2 * row
    block = jnp.where(
        (place == 0) | (place == 1), 3.0, jnp.where((place == -1) | (place == 2), 1.0, 0.0)
    ).astype(jnp.bfloat16)
    after = jnp.where((row == LANES - 1) & (at == 0), 1.0, 0.0).astype(jnp.bfloat16)
    before = jnp.where((row == 0) & (at == 2 * LANES - 1), 1.0, 0.0).astype(jnp.bfloat16)
    count = cols // LANES
    for i in range(count):
        for j in range(count):
            piece = block if i == j else after if j == i + 1 else before if j == i - 1 else None
            if piece is None:
                piece = jnp.zeros((LANES, 2 * LANES), jnp.bfloat16)
            weights_ref[i * LANES : (i + 1) * LANES, 2 * j * LANES : 2 * (j + 1) * LANES] = piece


def classify_rows(read_cells, tables, cells_ref, layers, tiles):
    total = float(2 * layers)
    for z in range(layers):
        for tile in range(tiles):
            even = cell_values(*read_cells(z, 0, tile), tables, total)
            odd = cell_values(*read_cells(z, 1, tile), tables, total)
            for channel in range(4):
                base = (z * 4 + channel) * 16
                block = jnp.concatenate([even[channel], odd[channel]], axis=0)
                cells_ref[base : base + 16, tile * LANES : (tile + 1) * LANES] = block.astype(jnp.bfloat16)


def rounded(value):
    return value.astype(jnp.bfloat16).astype(jnp.float32)


def cells_kernel(
    place_ref, dense_ref, index_ref, inside_ref, tables_ref, cells_ref, weights_ref, mix_ref, lines_ref
):
    layers, tiles, rows = dense_ref.shape[0], dense_ref.shape[1], dense_ref.shape[2] - 8
    half = rows // 2
    start = place_ref[ME] * half
    fill_weights(weights_ref)
    fill_rows(mix_ref)

    def read_cells(z, part, tile):
        at = pl.ds(start + part, half // 2, stride=2)
        return dense_ref[z, tile, at, :], index_ref[z, tile, at, :]

    classify_rows(read_cells, read_tables(tables_ref), cells_ref, layers, tiles)
    column_lines(place_ref[ME], lambda *at: pack_words(*read_cells(*at)), inside_ref[...], lines_ref, rows)


def along_columns(cells, weights_ref, store):
    result = rounded(jnp.dot(cells, weights_ref[...], preferred_element_type=jnp.float32))
    for tile in range(result.shape[1] // LANES):
        store(tile, result[:, tile * LANES : (tile + 1) * LANES])


def own_kernel(place_ref, cells_ref, weights_ref, along_ref):
    size = cells_ref.shape[0]
    pad = 64
    mine = pl.multiple_of(pad + place_ref[ME] * size, pad)

    def store(tile, block):
        along_ref[tile, 0:pad, :] = jnp.zeros((pad, LANES), jnp.float32)
        along_ref[tile, pad + 2 * size : 2 * pad + 2 * size, :] = jnp.zeros((pad, LANES), jnp.float32)
        along_ref[tile, pl.ds(mine, size), :] = block

    along_columns(cells_ref[...], weights_ref, store)


def other_cells_kernel(bulk_ref, tables_ref, cells_ref):
    layers = (bulk_ref.shape[0] - 1) // 2
    cols = bulk_ref.shape[2]

    def read_cells(z, part, tile):
        return unpack_words(bulk_ref[2 * z + part, :, tile * LANES : (tile + 1) * LANES])

    classify_rows(read_cells, read_tables(tables_ref), cells_ref, layers, cols // LANES)


def edge_cells(near, inside, tables, cells_ref, front, base):
    layers, cols = near.shape
    for side in range(2):
        use_near = front if side == 0 else jnp.logical_not(front)
        words = jnp.where(use_near, near, inside)
        for t in range(cols // LANES):
            values = cell_values(
                *unpack_words(words[:, t * LANES : (t + 1) * LANES]), tables, float(2 * layers)
            )
            for channel in range(4):
                at = pl.ds(base + side * 4 + channel, layers, stride=8)
                cells_ref[t, at, :] = values[channel]


def edge_along(cells_ref, count, weights_ref):
    return rounded(
        sum(
            jnp.dot(
                cells_ref[t, 0:count].astype(jnp.bfloat16),
                weights_ref[t * LANES : (t + 1) * LANES, :],
                preferred_element_type=jnp.float32,
            )
            for t in range(cells_ref.shape[0])
        )
    )


def edge_lines(now, packed_ref, lines_ref, depth):
    triple = 3.0 * now
    empty = jnp.zeros((8, LANES), jnp.float32)
    for layer in range(depth):
        at = layer * 8
        here = triple[at : at + 8]
        before = now[at - 8 : at] if layer > 0 else empty
        after = now[at + 8 : at + 16] if layer + 1 < depth else empty
        line = jnp.concatenate([before + here, empty], axis=0)
        packed_ref[2 * at : 2 * at + 16, :] = line.astype(jnp.bfloat16)
        lines_ref[at : at + 8, :] = rounded(after + here)


def row_samples(value, above, below):
    sub_at = lax.broadcasted_iota(jnp.int32, (8, LANES), 0)
    low, high = value[0:8], value[8:16]
    before = jnp.where(sub_at == 0, above, pltpu.roll(high, 1, 0))
    after = jnp.where(sub_at == 7, below, pltpu.roll(low, 7, 0))
    low_centre = 3.0 * low
    high_centre = 3.0 * high
    return [before + low_centre, low_centre + high, low + high_centre, high_centre + after]


def slab_pair(
    along_refs, packed_refs, lines_refs, rows_ref, slab, lines_slab, layers, keep_first=None, keep_last=None
):
    along_at = pl.ds(pl.multiple_of(slab * (layers * 64), 64), (layers + 2) * 64)
    packed_at = pl.ds(pl.multiple_of(lines_slab * (layers * 16), 16), layers * 16)
    lines_at = pl.ds(pl.multiple_of(lines_slab * (layers * 8), 8), layers * 8 + 8)
    views = [ref.at[along_at, :] for ref in along_refs]
    packed = [ref.at[packed_at, :] for ref in packed_refs]
    lines = [ref.at[lines_at, :] for ref in lines_refs]

    def layer_rows(view, layer, channel):
        base = (layer * 4 + channel) * 16
        return view[base : base + 16, :]

    def both(pieces):
        return jnp.concatenate(pieces, axis=1)

    def blend(image, samples, keep):
        updated = []
        for tile in range(2):
            clear = [1.0 - value for value in image[tile][3]]
            updated.append([])
            for c in range(4):
                values = samples[tile][c]
                if keep is not None:
                    values = [jnp.where(keep, value, 0.0) for value in values]
                updated[tile].append([image[tile][c][i] + clear[i] * values[i] for i in range(4)])
        return updated

    zero = jnp.zeros((8, LANES), jnp.float32)
    image = [[[zero] * 4 for _ in range(4)] for _ in range(2)]
    for z in range(layers):
        triple = [[3.0 * layer_rows(v, z + 1, c) for c in range(4)] for v in views]
        mixed = [
            both([(layer_rows(v, z, c) + t[c]).astype(jnp.bfloat16) for v, t in zip(views, triple)])
            for c in range(4)
        ]
        mixed.append(both([line[z * 16 : z * 16 + 16, :] for line in packed]))
        product = jnp.dot(
            rows_ref[...], jnp.concatenate(mixed, axis=0), preferred_element_type=jnp.float32
        )
        even, odd = [], []
        for tile in range(2):
            lanes = slice(tile * LANES, (tile + 1) * LANES)
            even.append(
                [
                    [product[c * 32 + i * 8 : c * 32 + i * 8 + 8, lanes] for i in range(4)]
                    for c in range(4)
                ]
            )
            odd.append([])
            for c in range(4):
                value = rounded(layer_rows(views[tile], z + 2, c) + triple[tile][c])
                above = lines[tile][pl.ds(z * 8 + c, 8, stride=0), :]
                below = lines[tile][pl.ds(z * 8 + 4 + c, 8, stride=0), :]
                odd[tile].append(row_samples(value, above, below))
        image = blend(image, even, keep_first if z == 0 else None)
        image = blend(image, odd, keep_last if z == layers - 1 else None)
    return image


def joined(first, in_front, behind):
    top = [[jnp.where(first, x, y) for x, y in zip(a, b)] for a, b in zip(in_front, behind)]
    low = [[jnp.where(first, y, x) for x, y in zip(a, b)] for a, b in zip(in_front, behind)]
    clear = [1.0 - value for value in top[3]]
    return [[top[c][i] + clear[i] * low[c][i] for i in range(4)] for c in range(4)]


def own_tiles_kernel(
    place_ref, tables_ref, weights_ref, inside_ref, mix_ref, along_ref, part_ref, cells_ref, packed_ref, lines_ref
):
    layers, cols = inside_ref.shape
    me = place_ref[ME]
    front = me == 0
    inside = inside_ref[...]
    edge_cells(jnp.zeros_like(inside), inside, read_tables(tables_ref), cells_ref, front, 0)
    edge = edge_along(cells_ref, 8 * layers, weights_ref)
    tiles = 2 * cols // LANES
    for tile in range(tiles):
        now = edge[:, tile * LANES : (tile + 1) * LANES]
        edge_lines(now, packed_ref.at[tile], lines_ref.at[tile], layers)
    for pair in range(tiles // 2):
        at = [2 * pair, 2 * pair + 1]
        image = slab_pair(
            [along_ref.at[tile] for tile in at],
            [packed_ref.at[tile] for tile in at],
            [lines_ref.at[tile] for tile in at],
            mix_ref,
            me,
            0,
            layers,
            front,
            jnp.logical_not(front),
        )
        for index, tile in enumerate(at):
            for channel in range(4):
                for i in range(4):
                    part_ref[tile, channel * 4 + i] = image[index][channel][i]


def fill_rows(rows_ref):
    m = lax.broadcasted_iota(jnp.int32, rows_ref.shape, 0)
    k = lax.broadcasted_iota(jnp.int32, rows_ref.shape, 1)
    row = 4 * (m & 7) + (lax.shift_right_logical(m, 3) & 3)
    centre = lax.shift_right_logical(row, 1)
    beside = centre - 1 + 2 * (row & 1)
    own = k < 64
    k_channel = jnp.where(own, lax.shift_right_logical(k, 4), k & 3)
    k_row = 2 * (k & 7) + (lax.shift_right_logical(k, 3) & 1)
    k_row = jnp.where(own, k_row, jnp.where(k < 68, -1, jnp.where(k < 72, 16, 99)))
    same = k_channel == lax.shift_right_logical(m, 5)
    value = jnp.where(k_row == centre, 3.0, jnp.where(k_row == beside, 1.0, 0.0))
    rows_ref[...] = jnp.where(same, value, 0.0).astype(jnp.bfloat16)


def tiles_kernel(
    place_ref, tables_ref, weights_ref, bulk_ref, inside_ref, second_ref, first_ref, ends_ref, mix_ref,
    part_ref, other_ref, own_ref, image_ref, mine_ref, along_ref, cells_ref, packed_ref, lines_ref, edge_ref, between_ref,
):
    layers, cols = inside_ref.shape
    depth = 2 * layers
    tiles = 2 * cols // LANES
    me = place_ref[ME]
    front = me == 0
    tables = read_tables(tables_ref)
    size = other_ref.shape[0]
    theirs = pl.multiple_of(64 + (1 - me) * size, 64)

    def store(tile, block):
        along_ref[tile, pl.ds(theirs, size), :] = block

    along_columns(other_ref[...], weights_ref, store)
    for slab in range(2):
        inside = jnp.where(me == slab, inside_ref[...], bulk_ref[2 * layers])
        near = near_words(slab, place_ref, first_ref, second_ref)
        edge_cells(near, inside, tables, cells_ref, front, slab * layers * 8)
        values = cell_values(*unpack_words(ends_ref[slab]), tables, float(depth))
        for channel in range(4):
            mine_ref[slab * 4 + channel] = 3.0 * rounded(values[channel])
    edge = edge_along(cells_ref, 8 * depth, weights_ref)
    here_at, beside_at = layers * 8 - 8, layers * 8
    empty = jnp.zeros((8, LANES), jnp.float32)
    for tile in range(tiles):
        now = edge[:, tile * LANES : (tile + 1) * LANES]
        edge_lines(now, packed_ref.at[tile], lines_ref.at[tile], depth)
        upper, lower = now[here_at : here_at + 8], now[beside_at : beside_at + 8]
        between_ref[tile, 0:8] = rounded(
            jnp.where(front, lower, upper) + 3.0 * jnp.where(front, upper, lower)
        )
        edge_ref[tile, 0:8] = empty
        edge_ref[tile, 8 : 8 * depth + 8] = now
        edge_ref[tile, 8 * depth + 8 :] = empty

    row = jnp.where(front, 0, 15)
    first_layer = me * layers
    replaced = []
    for tile in range(tiles):
        inner, outer = [], []
        for z in range(layers + 2):
            at = (first_layer + z) * 64 + row
            inner.append(along_ref[tile, pl.ds(at, 4, stride=16), :])
            both = edge_ref[tile, pl.ds(pl.multiple_of((first_layer + z) * 8, 8), 8), :]
            outer.append(jnp.where(front, both[0:4], both[4:8]))
        image = jnp.zeros((4, LANES), jnp.float32)
        for z in range(layers):
            for parity in range(2):
                beside = z + 2 * parity
                sample = rounded(outer[beside] + 3.0 * outer[z + 1]) + 3.0 * rounded(
                    inner[beside] + 3.0 * inner[z + 1]
                )
                if (z, parity) == (0, 0):
                    sample = jnp.where(front, sample, 0.0)
                if (z, parity) == (layers - 1, 1):
                    sample = jnp.where(front, 0.0, sample)
                image = image + (1.0 - image[3:4]) * sample
        replaced.append(image)

    sub_at = lax.broadcasted_iota(jnp.int32, (8, LANES), 0)
    for pair in range(tiles // 2):
        at = [2 * pair, 2 * pair + 1]
        other = slab_pair(
            [along_ref.at[tile] for tile in at],
            [packed_ref.at[tile] for tile in at],
            [lines_ref.at[tile] for tile in at],
            mix_ref,
            1 - me,
            1 - me,
            layers,
        )
        for index, tile in enumerate(at):
            here = pl.multiple_of(jnp.where(front, layers, layers + 1) * 64, 64)
            beside = pl.multiple_of(jnp.where(front, layers + 1, layers) * 64, 64)
            between, part = [], []
            for c in range(4):
                value = rounded(
                    along_ref[tile, pl.ds(beside + c * 16, 16), :]
                    + 3.0 * along_ref[tile, pl.ds(here + c * 16, 16), :]
                )
                above = between_ref[tile, pl.ds(c, 8, stride=0), :]
                below = between_ref[tile, pl.ds(c + 4, 8, stride=0), :]
                between.append(row_samples(value, above, below))
                values = [part_ref[tile, c * 4 + i] for i in range(4)]
                line = replaced[tile][c : c + 1]
                values[0] = jnp.where(sub_at == 0, jnp.where(front, line, values[0]), values[0])
                values[3] = jnp.where(sub_at == 7, jnp.where(front, values[3], line), values[3])
                part.append(values)
            mine = joined(front, part, between)
            image = joined((me ^ place_ref[FLIP]) == 0, mine, other[index])
            for c in range(4):
                for i in range(4):
                    image_ref[tile, c, pl.ds(i, 8, stride=4), :] = image[c][i]


def edge_kernel(
    place_ref, tables_ref, beside_ref, across_ref, mine_ref, image_ref,
    out_ref, final_ref, turned_ref, fixed_ref, sems,
):
    rows = out_ref.shape[1]
    cols = out_ref.shape[2] // 2
    half = rows // 2
    layers = beside_ref.shape[1]
    tiles = 2 * cols // LANES
    middle = LANES // 2
    front = place_ref[ME] == 0
    start = pl.multiple_of(place_ref[ME] * half, half)
    even_x = place_ref[ODD_X] == 0
    tables = read_tables(tables_ref)

    def to_out(tile, source):
        lanes = pl.ds(tile * LANES, LANES)
        return pltpu.make_async_copy(
            source.at[:, pl.ds(0, rows), :], out_ref.at[:, :, lanes], sems.at[tile]
        )

    copies = [to_out(tile, image_ref.at[tile]) for tile in range(1, tiles - 1)]
    for copy in copies:
        copy.start()
    lane_at = lax.broadcasted_iota(jnp.int32, (layers, LANES), 1)
    layer_at = lax.broadcasted_iota(jnp.int32, (layers, LANES), 0)
    first_lane = (lane_at & (middle - 1)) == 0
    along = [[], []]
    samples = {}
    for slab in range(2):
        right = jnp.where(even_x, beside_ref[slab], across_ref[slab])
        left = jnp.where(even_x, across_ref[slab], beside_ref[slab])
        right = jnp.where(place_ref[HAS_RIGHT] == 1, right, 0)
        left = jnp.where(place_ref[HAS_LEFT] == 1, left, 0)
        words = pltpu.roll(jnp.where(lane_at < middle, right, left), middle, 1)
        halo = cell_values(*unpack_words(words), tables, float(2 * layers))
        for channel in range(4):
            along[slab].append(rounded(mine_ref[slab * 4 + channel] + rounded(halo[channel])))
    for channel in range(4):
        front_part, back_part = along[0][channel], along[1][channel]
        down = [pltpu.roll(front_part, 1, 0), pltpu.roll(back_part, 1, 0)]
        up = [pltpu.roll(front_part, layers - 1, 0), pltpu.roll(back_part, layers - 1, 0)]
        is_first, is_last = layer_at == 0, layer_at == layers - 1
        before = [jnp.where(is_first, 0.0, down[0]), jnp.where(is_first, down[0], down[1])]
        after = [jnp.where(is_last, up[1], up[0]), jnp.where(is_last, 0.0, up[1])]
        for slab in range(2):
            triple = 3.0 * along[slab][channel]
            for parity, other in enumerate((before[slab], after[slab])):
                mixed = rounded(other + triple)
                centre = 3.0 * mixed
                above = pltpu.roll(mixed, 1, 1)
                near = pltpu.roll(mixed, LANES - rows, 1)
                above = jnp.where(first_lane, jnp.where(front, near, above), above)
                below = pltpu.roll(mixed, LANES - 1, 1)
                samples[slab, parity, 0, channel] = above + centre
                samples[slab, parity, 1, channel] = centre + below

    def over(in_front, behind):
        clear = 1.0 - in_front[3]
        return [top + clear * low for top, low in zip(in_front, behind)]

    slabs = []
    for slab in range(2):
        slabs.append([])
        for odd in range(2):
            image = over(
                *[[samples[slab, parity, odd, channel] for channel in range(4)] for parity in range(2)]
            )
            step = 1
            while step < layers:
                image = over(image, [pltpu.roll(value, layers - step, 0) for value in image])
                step *= 2
            slabs[slab].append(image)
    in_order = place_ref[FLIP] == 0
    image = [
        over(
            *[
                [jnp.where(in_order, x, y) for x, y in zip(slabs[at][odd], slabs[1 - at][odd])]
                for at in range(2)
            ]
        )
        for odd in range(2)
    ]
    for odd in range(2):
        for channel in range(4):
            at = odd * 4 + channel
            final_ref[at : at + 1, :] = image[odd][channel][0:1]
    turned_ref[:, 0:8] = final_ref[...].T
    wide = lax.broadcasted_iota(jnp.int32, (half, LANES), 1)
    for index, tile in enumerate((0, tiles - 1)):
        place = wide == index * (LANES - 1)
        turned = turned_ref[pl.ds(start + index * middle, half), :]
        for channel in range(4):
            for odd in range(2):
                at = pl.ds(odd, half, stride=2)
                column = odd * 4 + channel
                fixed_ref[index, channel, at, :] = jnp.where(
                    place, turned[:, column : column + 1], image_ref[tile, channel, at, :]
                )
        copies.append(to_out(tile, fixed_ref.at[index]))
        copies[-1].start()
    for copy in copies:
        copy.wait()


def two_slab_device(density, bin_index, tf_colour, tf_extinction, slab_rank):
    layers, rows, cols = density.shape
    half = rows // 2
    tiles = 2 * cols // LANES
    size = layers * 4 * half
    count_y, count_x = lax.axis_size("by"), lax.axis_size("bx")
    f32, bf16, i32 = jnp.float32, jnp.bfloat16, jnp.int32

    def call(kernel, name, out_shape, time, scratch_shapes=(), in_specs=None, out_specs=None, aliases={}):
        def run(*operands):
            return pl.pallas_call(
                kernel,
                out_shape=out_shape,
                in_specs=in_specs or [SMEM] + [VMEM] * (len(operands) - 1),
                out_specs=out_specs
                or ((VMEM,) * len(out_shape) if isinstance(out_shape, tuple) else VMEM),
                scratch_shapes=scratch_shapes,
                input_output_aliases=aliases,
                compiler_params=pltpu.CompilerParams(vmem_limit_bytes=16 * 1024 * 1024),
                cost_estimate=cost(time),
                name=name,
            )(*operands)

        return run

    def both(route):
        return route + [(target, source) for source, target in route]

    blocks = (layers, cols // LANES, rows + 8, LANES)
    row = pltpu.VMEM((layers, cols), i32)
    inputs = [
        pltpu.with_memory_space_constraint(x, pltpu.HBM)
        for x in (slab_rank, density, bin_index, tf_colour, tf_extinction)
    ]
    place, first, second, bulk, inside, dense, index, tables = call(
        stage_kernel,
        "stage_block",
        (
            pltpu.SMEM((7,), i32),
            row,
            row,
            pltpu.VMEM((2 * layers + 1, 8, cols), i32),
            row,
            pltpu.VMEM(blocks, f32),
            pltpu.VMEM(blocks, i32),
            pltpu.VMEM((8, 8, LANES), f32),
        ),
        1.2,
        in_specs=[SMEM] + [VMEM] * 4,
        out_specs=(SMEM,) + (VMEM,) * 7,
    )(*inputs)
    def device(z, y, x):
        return (z * count_y + y) * count_x + x

    def lanes(route):
        return [(device(*source, x), device(*target, x)) for source, target in route for x in range(count_x)]

    def twins(z, y):
        return both([(device(z, y, x), device(z, y, x + 1)) for x in range(0, count_x, 2)])

    last = count_y - 1
    ring = [((1, 0), (0, 1)), ((0, last), (1, last))]
    ring += [((0, y), (0, y + 1)) for y in range(1, last)] + [((1, y + 1), (1, y)) for y in range(last)]
    ring = lanes(ring) + twins(0, 0)
    diagonal = [((1, 0), (0, 0)), ((0, 0), (0, 1)), ((0, 1), (1, 0))]
    for y in range(1, last):
        diagonal += both([((1, y), (0, y + 1))])
    diagonal = lanes(diagonal) + twins(1, last)
    axes = ("bz", "by", "bx")
    bulk = lax.ppermute(bulk, "bz", [(0, 1), (1, 0)])
    first = lax.ppermute(first, axes, ring)
    second = lax.ppermute(second, axes, diagonal)

    cells, weights, mix, columns = call(
        cells_kernel,
        "own_cells",
        (
            pltpu.VMEM((size, cols), bf16),
            pltpu.VMEM((cols, 2 * cols), bf16),
            pltpu.VMEM((128, 80), bf16),
            pltpu.VMEM((layers, LANES), i32),
        ),
        0.5,
    )(place, dense, index, inside, tables)
    whole = pltpu.VMEM((tiles, 2 * size + 3 * 4 * half, LANES), f32)
    along = call(own_kernel, "own_slab", whole, 0.4)(place, cells, weights)
    edges = pltpu.VMEM((cols // LANES, 16 * layers + 8, LANES), f32)
    packed = pltpu.VMEM((tiles, 32 * layers, LANES), bf16)
    lines = pltpu.VMEM((tiles, 16 * layers + 8, LANES), f32)
    part = call(
        own_tiles_kernel,
        "own_tiles",
        pltpu.VMEM((tiles, 16, 8, LANES), f32),
        0.1,
        [edges, packed, lines],
    )(place, tables, weights, inside, mix, along)
    other_cells = call(
        other_cells_kernel, "other_cells", pltpu.VMEM((size, cols), bf16), 0.1, in_specs=[VMEM] * 2
    )(bulk, tables)
    ends = call(
        functools.partial(side_kernel, rows),
        "side_columns",
        pltpu.VMEM((2, layers, LANES), i32),
        0.1,
        [pltpu.VMEM((layers, LANES), i32)],
    )(place, columns, bulk, second, first, part, other_cells)
    pairs = [(x, x + 1) for x in range(0, count_x, 2)]
    cross = [(x, (x + 1) % count_x) for x in range(1, count_x, 2)]
    beside = lax.ppermute(ends, "bx", both(pairs))
    across = lax.ppermute(ends, "bx", both(cross))
    image, mine, _ = call(
        tiles_kernel,
        "render_tiles",
        (pltpu.VMEM((tiles, 4, rows + 8, LANES), f32), pltpu.VMEM((8, layers, LANES), f32), whole),
        2.0,
        [
            edges,
            packed,
            lines,
            pltpu.VMEM((tiles, 16 * layers + 16, LANES), f32),
            pltpu.VMEM((tiles, 16, LANES), f32),
        ],
        aliases={11: 2},
    )(place, tables, weights, bulk, inside, second, first, ends, mix, part, other_cells, along)
    return call(
        edge_kernel,
        "edge_columns",
        jax.ShapeDtypeStruct((4, rows, 2 * cols), f32),
        1.0,
        [
            pltpu.VMEM((8, LANES), f32),
            pltpu.VMEM((LANES, LANES), f32),
            pltpu.VMEM((2, 4, rows + 8, LANES), f32),
            pltpu.SemaphoreType.DMA((tiles,)),
        ],
        out_specs=pl.BlockSpec(memory_space=pltpu.HBM),
    )(place, tables, beside, across, mine, image)


def on_device(density, bin_index, tf_colour, tf_extinction, slab_rank):
    if lax.axis_size("bz") == 2:
        return two_slab_device(density, bin_index, tf_colour, tf_extinction, slab_rank)
    return general_device(density, bin_index, tf_colour, tf_extinction, slab_rank)


def solution(mesh):
    return jax.shard_map(
        on_device,
        mesh=mesh,
        in_specs=(P("bz", "by", "bx"), P("bz", "by", "bx"), P(), P(), P()),
        out_specs=P(None, ("by", "bz"), "bx"),
        check_vma=False,
    )
```

```python
import functools

import jax
import jax.numpy as jnp
from jax import lax
from jax.experimental import pallas as pl
from jax.experimental.pallas import tpu as pltpu
from jax.sharding import PartitionSpec as P


def with_halo(block, sides, width):
    for axis, dim in sides:
        count = lax.axis_size(axis)
        forward = [(i, i + 1) for i in range(count - 1)]
        backward = [(target, source) for source, target in forward]
        low = lax.ppermute(
            lax.slice_in_dim(block, block.shape[dim] - width, None, axis=dim), axis, forward
        )
        high = lax.ppermute(lax.slice_in_dim(block, 0, width, axis=dim), axis, backward)
        block = jnp.concatenate([low, block, high], axis=dim)
    return block


def partner_2(block, axis, stride):
    count = lax.axis_size(axis)
    route = []
    for low in range(count):
        high = low | 1 << stride
        if high != low and high < count:
            route += [(low, high), (high, low)]
    return lax.ppermute(block, axis, route)


def resample_table(length):
    row_index = lax.broadcasted_iota(jnp.int32, (2 * length, length + 2), 0)
    col_index = lax.broadcasted_iota(jnp.int32, (2 * length, length + 2), 1)
    centre = row_index // 2
    parity = row_index % 2
    weights_table = jnp.where(col_index == centre + 1, 0.75, 0.0)
    weights_table = weights_table + jnp.where((col_index == centre) & (parity == 0), 0.25, 0.0)
    weights_table = weights_table + jnp.where((col_index == centre + 2) & (parity == 1), 0.25, 0.0)
    return weights_table.astype(jnp.bfloat16)


def blend_over(in_front, behind):
    return in_front + (1.0 - in_front[3])[None] * behind


def classify(density, bin_index, tf_colour, tf_extinction, total_depth):
    depth_cells, height_cells, width_cells = density.shape
    lookup = jnp.concatenate([tf_colour, tf_extinction[None, :]], axis=0)
    table_size = lookup.shape[1]
    bin_rows = lax.broadcasted_iota(jnp.int32, (table_size, 1), 0)
    flat_bins = bin_index.reshape(depth_cells, height_cells * width_cells)
    flat_density = density.reshape(depth_cells, height_cells * width_cells)

    def one_layer(layer, result):
        layer_bins = lax.dynamic_index_in_dim(flat_bins, layer, 0, keepdims=True)
        layer_density = lax.dynamic_index_in_dim(flat_density, layer, 0, keepdims=False)
        one_hot = (layer_bins == bin_rows).astype(jnp.bfloat16)
        values = jnp.dot(lookup, one_hot, preferred_element_type=jnp.float32)
        opacity = 1.0 - jnp.exp(-values[3] * layer_density / total_depth)
        cells = jnp.concatenate([values[:3] * opacity[None], opacity[None]], axis=0).astype(
            jnp.bfloat16
        )
        return lax.dynamic_update_slice_in_dim(result, cells[:, None], layer, 1)

    start_cells = jnp.zeros((4, depth_cells, height_cells * width_cells), jnp.bfloat16)
    classified = lax.fori_loop(0, depth_cells, one_layer, start_cells)
    return classified.reshape(4, depth_cells, height_cells, width_cells)


def general_device(density, bin_index, tf_colour, tf_extinction, slab_rank):
    slab_count = lax.axis_size("bz")
    depth_cells, height_cells, width_cells = density.shape
    total_depth = float(depth_cells * slab_count)
    colour_cells = classify(density, bin_index, tf_colour, tf_extinction, total_depth)
    padded = with_halo(colour_cells, (("bz", 1), ("by", 2), ("bx", 3)), 1)
    along_x = jnp.einsum(
        "czyq,pq->czyp", padded, resample_table(width_cells), preferred_element_type=jnp.float32
    ).astype(jnp.bfloat16)
    y_table = resample_table(height_cells)

    def add_sample(sample_index, image_now):
        centre = sample_index // 2
        parity = sample_index % 2
        layers = lax.dynamic_slice_in_dim(along_x, centre, 3, 1).astype(jnp.float32)
        lower_weight = jnp.where(parity == 0, 0.25, 0.0)
        upper_weight = jnp.where(parity == 1, 0.25, 0.0)
        mixed_layer = (
            lower_weight * layers[:, 0] + 0.75 * layers[:, 1] + upper_weight * layers[:, 2]
        ).astype(jnp.bfloat16)
        sample = jnp.einsum("qy,cyp->cqp", y_table, mixed_layer, preferred_element_type=jnp.float32)
        return blend_over(image_now, sample)

    start_image = jnp.zeros((4, 2 * height_cells, 2 * width_cells), jnp.float32)
    slab_image = lax.fori_loop(0, 2 * depth_cells, add_sample, start_image)
    rows_piece = 2 * height_cells // slab_count
    my_index = lax.axis_index("bz")
    bit_levels = slab_count.bit_length() - 1
    composite = slab_image.reshape((4,) + (2,) * bit_levels + (rows_piece, 2 * width_cells))
    my_rank = lax.dynamic_index_in_dim(slab_rank, my_index, 0, keepdims=False)
    for level in range(bit_levels):
        position = bit_levels - level
        my_bit = my_index // 2**level % 2
        kept_half = lax.dynamic_index_in_dim(composite, my_bit, position, keepdims=False)
        outgoing = lax.dynamic_index_in_dim(composite, 1 - my_bit, position, keepdims=False)
        incoming = partner_2(outgoing, "bz", level)
        partner = my_index + (1 - 2 * my_bit) * 2**level
        partner_rank = lax.dynamic_index_in_dim(slab_rank, partner, 0, keepdims=False)
        mine_first = my_rank < partner_rank
        composite = blend_over(
            jnp.where(mine_first, kept_half, incoming), jnp.where(mine_first, incoming, kept_half)
        )
    return composite


LANES = 128
LEVELS = 65535.0
VMEM = pl.BlockSpec(memory_space=pltpu.VMEM)
SMEM = pl.BlockSpec(memory_space=pltpu.SMEM)
FLIP, ME, HAS_NEAR, TURNED, ODD_X, HAS_RIGHT, HAS_LEFT = range(7)


def pack_words(density, bins):
    level = (density * LEVELS + 0.5).astype(jnp.int32)
    return lax.shift_left(level, 16) | bins


def unpack_words(words):
    density = lax.shift_right_logical(words, 16).astype(jnp.float32) * (1.0 / LEVELS)
    return density, words & 0xFFFF


def cell_values(density, bins, tables, depth):
    low_bits = bins & (LANES - 1)
    upper = bins >= LANES

    def pick(channel):
        first, second = tables[channel]
        return jnp.where(
            upper,
            jnp.take_along_axis(second, low_bits, axis=1, mode="promise_in_bounds"),
            jnp.take_along_axis(first, low_bits, axis=1, mode="promise_in_bounds"),
        )

    opacity = (1.0 - jnp.exp(-pick(3) * density / depth)) * (1.0 / 64.0)
    return [pick(0) * opacity, pick(1) * opacity, pick(2) * opacity, opacity]


def read_tables(tables_ref):
    return [[tables_ref[2 * channel + half] for half in range(2)] for channel in range(4)]


def cost(microseconds):
    return pl.CostEstimate(
        flops=int(1e9 * microseconds), bytes_accessed=int(3.6e6 * microseconds), transcendentals=0
    )


def stage_kernel(
    rank_ref, density_ref, bins_ref, colour_ref, extinction_ref,
    place_ref, first_ref, second_ref, bulk_ref, inside_ref, dense_ref, index_ref, tables_ref,
):
    me, me_y, me_x = lax.axis_index("bz"), lax.axis_index("by"), lax.axis_index("bx")
    past = jnp.where(me == 0, me_y, lax.axis_size("by") - 1 - me_y)
    for at, value in enumerate(
        (
            rank_ref[0],
            me,
            jnp.minimum(past, 1),
            jnp.where((me == 0) & (me_y == 1), 1, 0),
            lax.rem(me_x, 2),
            jnp.where(me_x + 1 < lax.axis_size("bx"), 1, 0),
            jnp.minimum(me_x, 1),
        )
    ):
        place_ref[at] = value
    layers, rows, cols = density_ref.shape
    front = me == 0
    inner = me_y > 0
    for z in range(layers):
        top, bottom = [
            pack_words(density_ref[z, r : r + 1, :], bins_ref[z, r : r + 1, :]) for r in (0, rows - 1)
        ]
        first_ref[z : z + 1, :] = jnp.where(jnp.logical_not(front) & inner, top, bottom)
        second_ref[z : z + 1, :] = jnp.where(front & inner, top, bottom)
        for tile in range(cols // LANES):
            lanes = slice(tile * LANES, (tile + 1) * LANES)
            dense_ref[z, tile, 0:rows] = density_ref[z, :, lanes]
            index_ref[z, tile, 0:rows] = bins_ref[z, :, lanes]
    pack_block(front, dense_ref, index_ref, bulk_ref, inside_ref)
    colour = colour_ref[...].astype(jnp.float32)
    extinction = extinction_ref[...].astype(jnp.float32).reshape(1, 2 * LANES)
    for channel in range(4):
        line = extinction if channel == 3 else colour[channel : channel + 1]
        for half in range(2):
            tables_ref[2 * channel + half] = jnp.broadcast_to(
                line[:, half * LANES : (half + 1) * LANES], (8, LANES)
            )


def pack_block(front, dense_ref, index_ref, bulk_ref, inside_ref):
    layers, tiles, rows = dense_ref.shape[0], dense_ref.shape[1], dense_ref.shape[2] - 8
    half = rows // 2
    start = jnp.where(front, half, 0)
    for tile in range(tiles):
        lanes = slice(tile * LANES, (tile + 1) * LANES)
        for z in range(layers):
            for part in range(2):
                at = pl.ds(start + part, half // 2, stride=2)
                bulk_ref[2 * z + part, :, lanes] = pack_words(
                    dense_ref[z, tile, at, :], index_ref[z, tile, at, :]
                )
            line = [
                pack_words(dense_ref[z, tile, r : r + 1, :], index_ref[z, tile, r : r + 1, :])
                for r in (half - 1, half)
            ]
            bulk_ref[2 * layers, z : z + 1, lanes] = jnp.where(front, line[0], line[1])
            inside_ref[z : z + 1, lanes] = jnp.where(front, line[1], line[0])


def near_words(slab, place_ref, first_ref, second_ref):
    own = (place_ref[ME] == slab) != (place_ref[TURNED] == 1)
    words = jnp.where(own, first_ref[...], second_ref[...])
    return jnp.where(place_ref[HAS_NEAR] == 1, words, 0)


def column_lines(me, read_words, inside, lines_ref, rows):
    layers, cols = inside.shape
    front = me == 0
    start = me * (rows // 2)
    middle = LANES // 2
    lane_at = lax.broadcasted_iota(jnp.int32, (8, LANES), 1)
    row_at = start + 2 * lax.broadcasted_iota(jnp.int32, (8, LANES), 0)
    for z in range(layers):
        line = jnp.zeros((8, LANES), jnp.int32)
        for part in range(2):
            first = read_words(z, part, 0)[:, 0:1]
            last = read_words(z, part, cols // LANES - 1)[:, LANES - 1 : LANES]
            line += jnp.where(lane_at == row_at + part, first, 0)
            line += jnp.where(lane_at == row_at + part + middle, last, 0)
        lines_ref[z : z + 1, :] = jnp.sum(line, axis=0, keepdims=True)
    beside = jnp.where(front, rows // 2, rows // 2 - 1)
    lines = jnp.where(lane_at == beside, inside[:, 0:1], lines_ref[...])
    lines_ref[...] = jnp.where(lane_at == beside + middle, inside[:, cols - 1 : cols], lines)


def side_kernel(
    rows, place_ref, columns_ref, bulk_ref, second_ref, first_ref, part_ref, ends_ref, other_ref
):
    layers, _ = columns_ref.shape
    me = place_ref[ME]
    front = me == 0
    lane_at = lax.broadcasted_iota(jnp.int32, (layers, LANES), 1)

    def read_words(z, part, tile):
        return bulk_ref[2 * z + part, :, tile * LANES : (tile + 1) * LANES]

    column_lines(me, read_words, bulk_ref[2 * layers], other_ref, rows)
    for slab in range(2):
        mine = front if slab == 0 else jnp.logical_not(front)
        columns = jnp.where(mine, columns_ref[...], other_ref[...])
        near = near_words(slab, place_ref, first_ref, second_ref)
        cols = near.shape[1]
        columns = jnp.where(lane_at == rows, near[:, 0:1], columns)
        ends_ref[slab] = jnp.where(
            lane_at == LANES // 2 + rows, near[:, cols - 1 : cols], columns
        )


def fill_weights(weights_ref):
    cols = weights_ref.shape[0]
    row = lax.broadcasted_iota(jnp.int32, (LANES, 2 * LANES), 0)
    at = lax.broadcasted_iota(jnp.int32, (LANES, 2 * LANES), 1)
    place = at - 2 * row
    block = jnp.where(
        (place == 0) | (place == 1), 3.0, jnp.where((place == -1) | (place == 2), 1.0, 0.0)
    ).astype(jnp.bfloat16)
    after = jnp.where((row == LANES - 1) & (at == 0), 1.0, 0.0).astype(jnp.bfloat16)
    before = jnp.where((row == 0) & (at == 2 * LANES - 1), 1.0, 0.0).astype(jnp.bfloat16)
    count = cols // LANES
    for i in range(count):
        for j in range(count):
            piece = block if i == j else after if j == i + 1 else before if j == i - 1 else None
            if piece is None:
                piece = jnp.zeros((LANES, 2 * LANES), jnp.bfloat16)
            weights_ref[i * LANES : (i + 1) * LANES, 2 * j * LANES : 2 * (j + 1) * LANES] = piece


def classify_rows(read_cells, tables, cells_ref, layers, tiles):
    total = float(2 * layers)
    for z in range(layers):
        for tile in range(tiles):
            even = cell_values(*read_cells(z, 0, tile), tables, total)
            odd = cell_values(*read_cells(z, 1, tile), tables, total)
            for channel in range(4):
                base = (z * 4 + channel) * 16
                block = jnp.concatenate([even[channel], odd[channel]], axis=0)
                cells_ref[base : base + 16, tile * LANES : (tile + 1) * LANES] = block.astype(jnp.bfloat16)


def rounded(value):
    return value.astype(jnp.bfloat16).astype(jnp.float32)


def along_columns(cells, weights_ref, store):
    result = rounded(jnp.dot(cells, weights_ref[...], preferred_element_type=jnp.float32))
    for tile in range(result.shape[1] // LANES):
        store(tile, result[:, tile * LANES : (tile + 1) * LANES])


def edge_cells(near, inside, tables, cells_ref, front, base):
    layers, cols = near.shape
    for side in range(2):
        use_near = front if side == 0 else jnp.logical_not(front)
        words = jnp.where(use_near, near, inside)
        for t in range(cols // LANES):
            values = cell_values(
                *unpack_words(words[:, t * LANES : (t + 1) * LANES]), tables, float(2 * layers)
            )
            for channel in range(4):
                at = pl.ds(base + side * 4 + channel, layers, stride=8)
                cells_ref[t, at, :] = values[channel]


def edge_along(cells_ref, count, weights_ref):
    return rounded(
        sum(
            jnp.dot(
                cells_ref[t, 0:count].astype(jnp.bfloat16),
                weights_ref[t * LANES : (t + 1) * LANES, :],
                preferred_element_type=jnp.float32,
            )
            for t in range(cells_ref.shape[0])
        )
    )


def edge_lines(now, packed_ref, lines_ref, depth):
    triple = 3.0 * now
    empty = jnp.zeros((8, LANES), jnp.float32)
    for layer in range(depth):
        at = layer * 8
        here = triple[at : at + 8]
        before = now[at - 8 : at] if layer > 0 else empty
        after = now[at + 8 : at + 16] if layer + 1 < depth else empty
        line = jnp.concatenate([before + here, empty], axis=0)
        packed_ref[2 * at : 2 * at + 16, :] = line.astype(jnp.bfloat16)
        lines_ref[at : at + 8, :] = rounded(after + here)


def row_samples(value, above, below):
    sub_at = lax.broadcasted_iota(jnp.int32, (8, LANES), 0)
    low, high = value[0:8], value[8:16]
    before = jnp.where(sub_at == 0, above, pltpu.roll(high, 1, 0))
    after = jnp.where(sub_at == 7, below, pltpu.roll(low, 7, 0))
    low_centre = 3.0 * low
    high_centre = 3.0 * high
    return [before + low_centre, low_centre + high, low + high_centre, high_centre + after]


def slab_pair(
    along_refs, packed_refs, lines_refs, rows_ref, slab, lines_slab, layers, keep_first=None, keep_last=None
):
    along_at = pl.ds(pl.multiple_of(slab * (layers * 64), 64), (layers + 2) * 64)
    packed_at = pl.ds(pl.multiple_of(lines_slab * (layers * 16), 16), layers * 16)
    lines_at = pl.ds(pl.multiple_of(lines_slab * (layers * 8), 8), layers * 8 + 8)
    views = [ref.at[along_at, :] for ref in along_refs]
    packed = [ref.at[packed_at, :] for ref in packed_refs]
    lines = [ref.at[lines_at, :] for ref in lines_refs]

    def layer_rows(view, layer, channel):
        base = (layer * 4 + channel) * 16
        return view[base : base + 16, :]

    def both(pieces):
        return jnp.concatenate(pieces, axis=1)

    def blend(image, samples, keep):
        updated = []
        for tile in range(2):
            clear = [1.0 - value for value in image[tile][3]]
            updated.append([])
            for c in range(4):
                values = samples[tile][c]
                if keep is not None:
                    values = [jnp.where(keep, value, 0.0) for value in values]
                updated[tile].append([image[tile][c][i] + clear[i] * values[i] for i in range(4)])
        return updated

    zero = jnp.zeros((8, LANES), jnp.float32)
    image = [[[zero] * 4 for _ in range(4)] for _ in range(2)]
    for z in range(layers):
        triple = [[3.0 * layer_rows(v, z + 1, c) for c in range(4)] for v in views]
        mixed = [
            both([(layer_rows(v, z, c) + t[c]).astype(jnp.bfloat16) for v, t in zip(views, triple)])
            for c in range(4)
        ]
        mixed.append(both([line[z * 16 : z * 16 + 16, :] for line in packed]))
        product = jnp.dot(
            rows_ref[...], jnp.concatenate(mixed, axis=0), preferred_element_type=jnp.float32
        )
        even, odd = [], []
        for tile in range(2):
            lanes = slice(tile * LANES, (tile + 1) * LANES)
            even.append(
                [
                    [product[c * 32 + i * 8 : c * 32 + i * 8 + 8, lanes] for i in range(4)]
                    for c in range(4)
                ]
            )
            odd.append([])
            for c in range(4):
                value = rounded(layer_rows(views[tile], z + 2, c) + triple[tile][c])
                above = lines[tile][pl.ds(z * 8 + c, 8, stride=0), :]
                below = lines[tile][pl.ds(z * 8 + 4 + c, 8, stride=0), :]
                odd[tile].append(row_samples(value, above, below))
        image = blend(image, even, keep_first if z == 0 else None)
        image = blend(image, odd, keep_last if z == layers - 1 else None)
    return image


def joined(first, in_front, behind):
    top = [[jnp.where(first, x, y) for x, y in zip(a, b)] for a, b in zip(in_front, behind)]
    low = [[jnp.where(first, y, x) for x, y in zip(a, b)] for a, b in zip(in_front, behind)]
    clear = [1.0 - value for value in top[3]]
    return [[top[c][i] + clear[i] * low[c][i] for i in range(4)] for c in range(4)]


def own_kernel(
    place_ref, dense_ref, index_ref, inside_ref, tables_ref,
    weights_ref, mix_ref, columns_ref, along_ref, part_ref,
    own_ref, cells_ref, packed_ref, lines_ref,
):
    layers, cols = inside_ref.shape
    me = place_ref[ME]
    rows = dense_ref.shape[2] - 8
    half = rows // 2
    size = own_ref.shape[0]
    pad = 64
    start = me * half
    mine = pl.multiple_of(pad + me * size, pad)
    fill_weights(weights_ref)
    fill_rows(mix_ref)

    def read_cells(z, part, tile):
        at = pl.ds(start + part, half // 2, stride=2)
        return dense_ref[z, tile, at, :], index_ref[z, tile, at, :]

    def store(tile, block):
        along_ref[tile, 0:pad, :] = jnp.zeros((pad, LANES), jnp.float32)
        along_ref[tile, pad + 2 * size : 2 * pad + 2 * size, :] = jnp.zeros((pad, LANES), jnp.float32)
        along_ref[tile, pl.ds(mine, size), :] = block

    classify_rows(read_cells, read_tables(tables_ref), own_ref, layers, cols // LANES)
    along_columns(own_ref[...], weights_ref, store)
    column_lines(me, lambda *at: pack_words(*read_cells(*at)), inside_ref[...], columns_ref, rows)
    front = me == 0
    inside = inside_ref[...]
    edge_cells(jnp.zeros_like(inside), inside, read_tables(tables_ref), cells_ref, front, 0)
    edge = edge_along(cells_ref, 8 * layers, weights_ref)
    tiles = 2 * cols // LANES
    for tile in range(tiles):
        now = edge[:, tile * LANES : (tile + 1) * LANES]
        edge_lines(now, packed_ref.at[tile], lines_ref.at[tile], layers)
    for pair in range(tiles // 2):
        at = [2 * pair, 2 * pair + 1]
        image = slab_pair(
            [along_ref.at[tile] for tile in at],
            [packed_ref.at[tile] for tile in at],
            [lines_ref.at[tile] for tile in at],
            mix_ref,
            me,
            0,
            layers,
            front,
            jnp.logical_not(front),
        )
        for index, tile in enumerate(at):
            for channel in range(4):
                for i in range(4):
                    part_ref[tile, channel * 4 + i] = image[index][channel][i]


def fill_rows(rows_ref):
    m = lax.broadcasted_iota(jnp.int32, rows_ref.shape, 0)
    k = lax.broadcasted_iota(jnp.int32, rows_ref.shape, 1)
    row = 4 * (m & 7) + (lax.shift_right_logical(m, 3) & 3)
    centre = lax.shift_right_logical(row, 1)
    beside = centre - 1 + 2 * (row & 1)
    own = k < 64
    k_channel = jnp.where(own, lax.shift_right_logical(k, 4), k & 3)
    k_row = 2 * (k & 7) + (lax.shift_right_logical(k, 3) & 1)
    k_row = jnp.where(own, k_row, jnp.where(k < 68, -1, jnp.where(k < 72, 16, 99)))
    same = k_channel == lax.shift_right_logical(m, 5)
    value = jnp.where(k_row == centre, 3.0, jnp.where(k_row == beside, 1.0, 0.0))
    rows_ref[...] = jnp.where(same, value, 0.0).astype(jnp.bfloat16)


def tiles_kernel(
    place_ref, tables_ref, weights_ref, bulk_ref, inside_ref, second_ref, first_ref, ends_ref, mix_ref,
    part_ref, own_ref, image_ref, mine_ref, along_ref, other_ref, cells_ref, packed_ref, lines_ref, edge_ref, between_ref,
):
    layers, cols = inside_ref.shape
    depth = 2 * layers
    tiles = 2 * cols // LANES
    me = place_ref[ME]
    front = me == 0
    tables = read_tables(tables_ref)
    size = other_ref.shape[0]
    theirs = pl.multiple_of(64 + (1 - me) * size, 64)

    def store(tile, block):
        along_ref[tile, pl.ds(theirs, size), :] = block

    def read_cells(z, part, tile):
        return unpack_words(bulk_ref[2 * z + part, :, tile * LANES : (tile + 1) * LANES])

    classify_rows(read_cells, tables, other_ref, layers, cols // LANES)
    along_columns(other_ref[...], weights_ref, store)
    for slab in range(2):
        inside = jnp.where(me == slab, inside_ref[...], bulk_ref[2 * layers])
        near = near_words(slab, place_ref, first_ref, second_ref)
        edge_cells(near, inside, tables, cells_ref, front, slab * layers * 8)
        values = cell_values(*unpack_words(ends_ref[slab]), tables, float(depth))
        for channel in range(4):
            mine_ref[slab * 4 + channel] = 3.0 * rounded(values[channel])
    edge = edge_along(cells_ref, 8 * depth, weights_ref)
    here_at, beside_at = layers * 8 - 8, layers * 8
    empty = jnp.zeros((8, LANES), jnp.float32)
    for tile in range(tiles):
        now = edge[:, tile * LANES : (tile + 1) * LANES]
        edge_lines(now, packed_ref.at[tile], lines_ref.at[tile], depth)
        upper, lower = now[here_at : here_at + 8], now[beside_at : beside_at + 8]
        between_ref[tile, 0:8] = rounded(
            jnp.where(front, lower, upper) + 3.0 * jnp.where(front, upper, lower)
        )
        edge_ref[tile, 0:8] = empty
        edge_ref[tile, 8 : 8 * depth + 8] = now
        edge_ref[tile, 8 * depth + 8 :] = empty

    row = jnp.where(front, 0, 15)
    first_layer = me * layers
    replaced = []
    for tile in range(tiles):
        inner, outer = [], []
        for z in range(layers + 2):
            at = (first_layer + z) * 64 + row
            inner.append(along_ref[tile, pl.ds(at, 4, stride=16), :])
            both = edge_ref[tile, pl.ds(pl.multiple_of((first_layer + z) * 8, 8), 8), :]
            outer.append(jnp.where(front, both[0:4], both[4:8]))
        image = jnp.zeros((4, LANES), jnp.float32)
        for z in range(layers):
            for parity in range(2):
                beside = z + 2 * parity
                sample = rounded(outer[beside] + 3.0 * outer[z + 1]) + 3.0 * rounded(
                    inner[beside] + 3.0 * inner[z + 1]
                )
                if (z, parity) == (0, 0):
                    sample = jnp.where(front, sample, 0.0)
                if (z, parity) == (layers - 1, 1):
                    sample = jnp.where(front, 0.0, sample)
                image = image + (1.0 - image[3:4]) * sample
        replaced.append(image)

    sub_at = lax.broadcasted_iota(jnp.int32, (8, LANES), 0)
    for pair in range(tiles // 2):
        at = [2 * pair, 2 * pair + 1]
        other = slab_pair(
            [along_ref.at[tile] for tile in at],
            [packed_ref.at[tile] for tile in at],
            [lines_ref.at[tile] for tile in at],
            mix_ref,
            1 - me,
            1 - me,
            layers,
        )
        for index, tile in enumerate(at):
            here = pl.multiple_of(jnp.where(front, layers, layers + 1) * 64, 64)
            beside = pl.multiple_of(jnp.where(front, layers + 1, layers) * 64, 64)
            between, part = [], []
            for c in range(4):
                value = rounded(
                    along_ref[tile, pl.ds(beside + c * 16, 16), :]
                    + 3.0 * along_ref[tile, pl.ds(here + c * 16, 16), :]
                )
                above = between_ref[tile, pl.ds(c, 8, stride=0), :]
                below = between_ref[tile, pl.ds(c + 4, 8, stride=0), :]
                between.append(row_samples(value, above, below))
                values = [part_ref[tile, c * 4 + i] for i in range(4)]
                line = replaced[tile][c : c + 1]
                values[0] = jnp.where(sub_at == 0, jnp.where(front, line, values[0]), values[0])
                values[3] = jnp.where(sub_at == 7, jnp.where(front, values[3], line), values[3])
                part.append(values)
            mine = joined(front, part, between)
            image = joined((me ^ place_ref[FLIP]) == 0, mine, other[index])
            for c in range(4):
                for i in range(4):
                    image_ref[tile, c, pl.ds(i, 8, stride=4), :] = image[c][i]


def edge_kernel(
    place_ref, tables_ref, beside_ref, across_ref, mine_ref, image_ref,
    out_ref, final_ref, turned_ref, fixed_ref, sems,
):
    rows = out_ref.shape[1]
    cols = out_ref.shape[2] // 2
    half = rows // 2
    layers = beside_ref.shape[1]
    tiles = 2 * cols // LANES
    middle = LANES // 2
    front = place_ref[ME] == 0
    start = pl.multiple_of(place_ref[ME] * half, half)
    even_x = place_ref[ODD_X] == 0
    tables = read_tables(tables_ref)

    def to_out(tile, source):
        lanes = pl.ds(tile * LANES, LANES)
        return pltpu.make_async_copy(
            source.at[:, pl.ds(0, rows), :], out_ref.at[:, :, lanes], sems.at[tile]
        )

    copies = [to_out(tile, image_ref.at[tile]) for tile in range(1, tiles - 1)]
    for copy in copies:
        copy.start()
    lane_at = lax.broadcasted_iota(jnp.int32, (layers, LANES), 1)
    layer_at = lax.broadcasted_iota(jnp.int32, (layers, LANES), 0)
    first_lane = (lane_at & (middle - 1)) == 0
    along = [[], []]
    samples = {}
    for slab in range(2):
        right = jnp.where(even_x, beside_ref[slab], across_ref[slab])
        left = jnp.where(even_x, across_ref[slab], beside_ref[slab])
        right = jnp.where(place_ref[HAS_RIGHT] == 1, right, 0)
        left = jnp.where(place_ref[HAS_LEFT] == 1, left, 0)
        words = pltpu.roll(jnp.where(lane_at < middle, right, left), middle, 1)
        halo = cell_values(*unpack_words(words), tables, float(2 * layers))
        for channel in range(4):
            along[slab].append(rounded(mine_ref[slab * 4 + channel] + rounded(halo[channel])))
    for channel in range(4):
        front_part, back_part = along[0][channel], along[1][channel]
        down = [pltpu.roll(front_part, 1, 0), pltpu.roll(back_part, 1, 0)]
        up = [pltpu.roll(front_part, layers - 1, 0), pltpu.roll(back_part, layers - 1, 0)]
        is_first, is_last = layer_at == 0, layer_at == layers - 1
        before = [jnp.where(is_first, 0.0, down[0]), jnp.where(is_first, down[0], down[1])]
        after = [jnp.where(is_last, up[1], up[0]), jnp.where(is_last, 0.0, up[1])]
        for slab in range(2):
            triple = 3.0 * along[slab][channel]
            for parity, other in enumerate((before[slab], after[slab])):
                mixed = rounded(other + triple)
                centre = 3.0 * mixed
                above = pltpu.roll(mixed, 1, 1)
                near = pltpu.roll(mixed, LANES - rows, 1)
                above = jnp.where(first_lane, jnp.where(front, near, above), above)
                below = pltpu.roll(mixed, LANES - 1, 1)
                samples[slab, parity, 0, channel] = above + centre
                samples[slab, parity, 1, channel] = centre + below

    def over(in_front, behind):
        clear = 1.0 - in_front[3]
        return [top + clear * low for top, low in zip(in_front, behind)]

    slabs = []
    for slab in range(2):
        slabs.append([])
        for odd in range(2):
            image = over(
                *[[samples[slab, parity, odd, channel] for channel in range(4)] for parity in range(2)]
            )
            step = 1
            while step < layers:
                image = over(image, [pltpu.roll(value, layers - step, 0) for value in image])
                step *= 2
            slabs[slab].append(image)
    in_order = place_ref[FLIP] == 0
    image = [
        over(
            *[
                [jnp.where(in_order, x, y) for x, y in zip(slabs[at][odd], slabs[1 - at][odd])]
                for at in range(2)
            ]
        )
        for odd in range(2)
    ]
    for odd in range(2):
        for channel in range(4):
            at = odd * 4 + channel
            final_ref[at : at + 1, :] = image[odd][channel][0:1]
    turned_ref[:, 0:8] = final_ref[...].T
    wide = lax.broadcasted_iota(jnp.int32, (half, LANES), 1)
    for index, tile in enumerate((0, tiles - 1)):
        place = wide == index * (LANES - 1)
        turned = turned_ref[pl.ds(start + index * middle, half), :]
        for channel in range(4):
            for odd in range(2):
                at = pl.ds(odd, half, stride=2)
                column = odd * 4 + channel
                fixed_ref[index, channel, at, :] = jnp.where(
                    place, turned[:, column : column + 1], image_ref[tile, channel, at, :]
                )
        copies.append(to_out(tile, fixed_ref.at[index]))
        copies[-1].start()
    for copy in copies:
        copy.wait()


def two_slab_device(density, bin_index, tf_colour, tf_extinction, slab_rank):
    layers, rows, cols = density.shape
    half = rows // 2
    tiles = 2 * cols // LANES
    size = layers * 4 * half
    count_y, count_x = lax.axis_size("by"), lax.axis_size("bx")
    f32, bf16, i32 = jnp.float32, jnp.bfloat16, jnp.int32

    def call(kernel, name, out_shape, time, scratch_shapes=(), in_specs=None, out_specs=None, aliases={}):
        def run(*operands):
            return pl.pallas_call(
                kernel,
                out_shape=out_shape,
                in_specs=in_specs or [SMEM] + [VMEM] * (len(operands) - 1),
                out_specs=out_specs
                or ((VMEM,) * len(out_shape) if isinstance(out_shape, tuple) else VMEM),
                scratch_shapes=scratch_shapes,
                input_output_aliases=aliases,
                compiler_params=pltpu.CompilerParams(vmem_limit_bytes=16 * 1024 * 1024),
                cost_estimate=cost(time),
                name=name,
            )(*operands)

        return run

    def both(route):
        return route + [(target, source) for source, target in route]

    blocks = (layers, cols // LANES, rows + 8, LANES)
    row = pltpu.VMEM((layers, cols), i32)
    inputs = [
        pltpu.with_memory_space_constraint(x, pltpu.HBM)
        for x in (slab_rank, density, bin_index, tf_colour, tf_extinction)
    ]
    place, first, second, bulk, inside, dense, index, tables = call(
        stage_kernel,
        "stage_block",
        (
            pltpu.SMEM((7,), i32),
            row,
            row,
            pltpu.VMEM((2 * layers + 1, 8, cols), i32),
            row,
            pltpu.VMEM(blocks, f32),
            pltpu.VMEM(blocks, i32),
            pltpu.VMEM((8, 8, LANES), f32),
        ),
        1.2,
        in_specs=[SMEM] + [VMEM] * 4,
        out_specs=(SMEM,) + (VMEM,) * 7,
    )(*inputs)
    def device(z, y, x):
        return (z * count_y + y) * count_x + x

    def lanes(route):
        return [(device(*source, x), device(*target, x)) for source, target in route for x in range(count_x)]

    def twins(z, y):
        return both([(device(z, y, x), device(z, y, x + 1)) for x in range(0, count_x, 2)])

    last = count_y - 1
    ring = [((1, 0), (0, 1)), ((0, last), (1, last))]
    ring += [((0, y), (0, y + 1)) for y in range(1, last)] + [((1, y + 1), (1, y)) for y in range(last)]
    ring = lanes(ring) + twins(0, 0)
    diagonal = [((1, 0), (0, 0)), ((0, 0), (0, 1)), ((0, 1), (1, 0))]
    for y in range(1, last):
        diagonal += both([((1, y), (0, y + 1))])
    diagonal = lanes(diagonal) + twins(1, last)
    axes = ("bz", "by", "bx")
    bulk = lax.ppermute(bulk, "bz", [(0, 1), (1, 0)])
    first = lax.ppermute(first, axes, ring)
    second = lax.ppermute(second, axes, diagonal)

    whole = pltpu.VMEM((tiles, 2 * size + 3 * 4 * half, LANES), f32)
    edges = pltpu.VMEM((cols // LANES, 16 * layers + 8, LANES), f32)
    packed = pltpu.VMEM((tiles, 32 * layers, LANES), bf16)
    lines = pltpu.VMEM((tiles, 16 * layers + 8, LANES), f32)
    weights, mix, columns, along, part = call(
        own_kernel,
        "own_slab",
        (
            pltpu.VMEM((cols, 2 * cols), bf16),
            pltpu.VMEM((128, 80), bf16),
            pltpu.VMEM((layers, LANES), i32),
            whole,
            pltpu.VMEM((tiles, 16, 8, LANES), f32),
        ),
        0.4,
        [pltpu.VMEM((size, cols), bf16), edges, packed, lines],
    )(place, dense, index, inside, tables)
    ends = call(
        functools.partial(side_kernel, rows),
        "side_columns",
        pltpu.VMEM((2, layers, LANES), i32),
        0.1,
        [pltpu.VMEM((layers, LANES), i32)],
    )(place, columns, bulk, second, first, part)
    pairs = [(x, x + 1) for x in range(0, count_x, 2)]
    cross = [(x, (x + 1) % count_x) for x in range(1, count_x, 2)]
    beside = lax.ppermute(ends, "bx", both(pairs))
    across = lax.ppermute(ends, "bx", both(cross))
    image, mine, _ = call(
        tiles_kernel,
        "render_tiles",
        (pltpu.VMEM((tiles, 4, rows + 8, LANES), f32), pltpu.VMEM((8, layers, LANES), f32), whole),
        2.0,
        [
            pltpu.VMEM((size, cols), bf16),
            edges,
            packed,
            lines,
            pltpu.VMEM((tiles, 16 * layers + 16, LANES), f32),
            pltpu.VMEM((tiles, 16, LANES), f32),
        ],
        aliases={10: 2},
    )(place, tables, weights, bulk, inside, second, first, ends, mix, part, along)
    return call(
        edge_kernel,
        "edge_columns",
        jax.ShapeDtypeStruct((4, rows, 2 * cols), f32),
        1.0,
        [
            pltpu.VMEM((8, LANES), f32),
            pltpu.VMEM((LANES, LANES), f32),
            pltpu.VMEM((2, 4, rows + 8, LANES), f32),
            pltpu.SemaphoreType.DMA((tiles,)),
        ],
        out_specs=pl.BlockSpec(memory_space=pltpu.HBM),
    )(place, tables, beside, across, mine, image)


def on_device(density, bin_index, tf_colour, tf_extinction, slab_rank):
    if lax.axis_size("bz") == 2:
        return two_slab_device(density, bin_index, tf_colour, tf_extinction, slab_rank)
    return general_device(density, bin_index, tf_colour, tf_extinction, slab_rank)


def solution(mesh):
    return jax.shard_map(
        on_device,
        mesh=mesh,
        in_specs=(P("bz", "by", "bx"), P("bz", "by", "bx"), P(), P(), P()),
        out_specs=P(None, ("by", "bz"), "bx"),
        check_vma=False,
    )
```

```python
import functools

import jax
import jax.numpy as jnp
from jax import lax
from jax.experimental import pallas as pl
from jax.experimental.pallas import tpu as pltpu
from jax.sharding import PartitionSpec as P


def with_halo(block, sides, width):
    for axis, dim in sides:
        count = lax.axis_size(axis)
        forward = [(i, i + 1) for i in range(count - 1)]
        backward = [(target, source) for source, target in forward]
        low = lax.ppermute(
            lax.slice_in_dim(block, block.shape[dim] - width, None, axis=dim), axis, forward
        )
        high = lax.ppermute(lax.slice_in_dim(block, 0, width, axis=dim), axis, backward)
        block = jnp.concatenate([low, block, high], axis=dim)
    return block


def partner_2(block, axis, stride):
    count = lax.axis_size(axis)
    route = []
    for low in range(count):
        high = low | 1 << stride
        if high != low and high < count:
            route += [(low, high), (high, low)]
    return lax.ppermute(block, axis, route)


def resample_table(length):
    row_index = lax.broadcasted_iota(jnp.int32, (2 * length, length + 2), 0)
    col_index = lax.broadcasted_iota(jnp.int32, (2 * length, length + 2), 1)
    centre = row_index // 2
    parity = row_index % 2
    weights_table = jnp.where(col_index == centre + 1, 0.75, 0.0)
    weights_table = weights_table + jnp.where((col_index == centre) & (parity == 0), 0.25, 0.0)
    weights_table = weights_table + jnp.where((col_index == centre + 2) & (parity == 1), 0.25, 0.0)
    return weights_table.astype(jnp.bfloat16)


def blend_over(in_front, behind):
    return in_front + (1.0 - in_front[3])[None] * behind


def classify(density, bin_index, tf_colour, tf_extinction, total_depth):
    depth_cells, height_cells, width_cells = density.shape
    lookup = jnp.concatenate([tf_colour, tf_extinction[None, :]], axis=0)
    table_size = lookup.shape[1]
    bin_rows = lax.broadcasted_iota(jnp.int32, (table_size, 1), 0)
    flat_bins = bin_index.reshape(depth_cells, height_cells * width_cells)
    flat_density = density.reshape(depth_cells, height_cells * width_cells)

    def one_layer(layer, result):
        layer_bins = lax.dynamic_index_in_dim(flat_bins, layer, 0, keepdims=True)
        layer_density = lax.dynamic_index_in_dim(flat_density, layer, 0, keepdims=False)
        one_hot = (layer_bins == bin_rows).astype(jnp.bfloat16)
        values = jnp.dot(lookup, one_hot, preferred_element_type=jnp.float32)
        opacity = 1.0 - jnp.exp(-values[3] * layer_density / total_depth)
        cells = jnp.concatenate([values[:3] * opacity[None], opacity[None]], axis=0).astype(
            jnp.bfloat16
        )
        return lax.dynamic_update_slice_in_dim(result, cells[:, None], layer, 1)

    start_cells = jnp.zeros((4, depth_cells, height_cells * width_cells), jnp.bfloat16)
    classified = lax.fori_loop(0, depth_cells, one_layer, start_cells)
    return classified.reshape(4, depth_cells, height_cells, width_cells)


def general_device(density, bin_index, tf_colour, tf_extinction, slab_rank):
    slab_count = lax.axis_size("bz")
    depth_cells, height_cells, width_cells = density.shape
    total_depth = float(depth_cells * slab_count)
    colour_cells = classify(density, bin_index, tf_colour, tf_extinction, total_depth)
    padded = with_halo(colour_cells, (("bz", 1), ("by", 2), ("bx", 3)), 1)
    along_x = jnp.einsum(
        "czyq,pq->czyp", padded, resample_table(width_cells), preferred_element_type=jnp.float32
    ).astype(jnp.bfloat16)
    y_table = resample_table(height_cells)

    def add_sample(sample_index, image_now):
        centre = sample_index // 2
        parity = sample_index % 2
        layers = lax.dynamic_slice_in_dim(along_x, centre, 3, 1).astype(jnp.float32)
        lower_weight = jnp.where(parity == 0, 0.25, 0.0)
        upper_weight = jnp.where(parity == 1, 0.25, 0.0)
        mixed_layer = (
            lower_weight * layers[:, 0] + 0.75 * layers[:, 1] + upper_weight * layers[:, 2]
        ).astype(jnp.bfloat16)
        sample = jnp.einsum("qy,cyp->cqp", y_table, mixed_layer, preferred_element_type=jnp.float32)
        return blend_over(image_now, sample)

    start_image = jnp.zeros((4, 2 * height_cells, 2 * width_cells), jnp.float32)
    slab_image = lax.fori_loop(0, 2 * depth_cells, add_sample, start_image)
    rows_piece = 2 * height_cells // slab_count
    my_index = lax.axis_index("bz")
    bit_levels = slab_count.bit_length() - 1
    composite = slab_image.reshape((4,) + (2,) * bit_levels + (rows_piece, 2 * width_cells))
    my_rank = lax.dynamic_index_in_dim(slab_rank, my_index, 0, keepdims=False)
    for level in range(bit_levels):
        position = bit_levels - level
        my_bit = my_index // 2**level % 2
        kept_half = lax.dynamic_index_in_dim(composite, my_bit, position, keepdims=False)
        outgoing = lax.dynamic_index_in_dim(composite, 1 - my_bit, position, keepdims=False)
        incoming = partner_2(outgoing, "bz", level)
        partner = my_index + (1 - 2 * my_bit) * 2**level
        partner_rank = lax.dynamic_index_in_dim(slab_rank, partner, 0, keepdims=False)
        mine_first = my_rank < partner_rank
        composite = blend_over(
            jnp.where(mine_first, kept_half, incoming), jnp.where(mine_first, incoming, kept_half)
        )
    return composite


LANES = 128
LEVELS = 65535.0
VMEM = pl.BlockSpec(memory_space=pltpu.VMEM)
SMEM = pl.BlockSpec(memory_space=pltpu.SMEM)
FLIP, ME, HAS_NEAR, TURNED, ODD_X, HAS_RIGHT, HAS_LEFT = range(7)


def pack_words(density, bins):
    level = (density * LEVELS + 0.5).astype(jnp.int32)
    return lax.shift_left(level, 16) | bins


def unpack_words(words):
    density = lax.shift_right_logical(words, 16).astype(jnp.float32) * (1.0 / LEVELS)
    return density, words & 0xFFFF


def cell_values(density, bins, tables, depth):
    low_bits = bins & (LANES - 1)
    upper = bins >= LANES

    def pick(channel):
        first, second = tables[channel]
        return jnp.where(
            upper,
            jnp.take_along_axis(second, low_bits, axis=1, mode="promise_in_bounds"),
            jnp.take_along_axis(first, low_bits, axis=1, mode="promise_in_bounds"),
        )

    opacity = (1.0 - jnp.exp(-pick(3) * density / depth)) * (1.0 / 64.0)
    return [pick(0) * opacity, pick(1) * opacity, pick(2) * opacity, opacity]


def read_tables(tables_ref):
    return [[tables_ref[2 * channel + half] for half in range(2)] for channel in range(4)]


def cost(microseconds):
    return pl.CostEstimate(
        flops=int(1e9 * microseconds), bytes_accessed=int(3.6e6 * microseconds), transcendentals=0
    )


def stage_kernel(
    rank_ref, density_ref, bins_ref, colour_ref, extinction_ref,
    place_ref, first_ref, second_ref, bulk_ref, inside_ref, dense_ref, index_ref, tables_ref,
):
    me, me_y, me_x = lax.axis_index("bz"), lax.axis_index("by"), lax.axis_index("bx")
    past = jnp.where(me == 0, me_y, lax.axis_size("by") - 1 - me_y)
    for at, value in enumerate(
        (
            rank_ref[0],
            me,
            jnp.minimum(past, 1),
            jnp.where((me == 0) & (me_y == 1), 1, 0),
            lax.rem(me_x, 2),
            jnp.where(me_x + 1 < lax.axis_size("bx"), 1, 0),
            jnp.minimum(me_x, 1),
        )
    ):
        place_ref[at] = value
    layers, rows, cols = density_ref.shape
    front = me == 0
    inner = me_y > 0
    for z in range(layers):
        top, bottom = [
            pack_words(density_ref[z, r : r + 1, :], bins_ref[z, r : r + 1, :]) for r in (0, rows - 1)
        ]
        first_ref[z : z + 1, :] = jnp.where(jnp.logical_not(front) & inner, top, bottom)
        second_ref[z : z + 1, :] = jnp.where(front & inner, top, bottom)
        for tile in range(cols // LANES):
            lanes = slice(tile * LANES, (tile + 1) * LANES)
            dense_ref[z, tile, 0:rows] = density_ref[z, :, lanes]
            index_ref[z, tile, 0:rows] = bins_ref[z, :, lanes]
    pack_block(front, dense_ref, index_ref, bulk_ref, inside_ref)
    colour = colour_ref[...].astype(jnp.float32)
    extinction = extinction_ref[...].astype(jnp.float32).reshape(1, 2 * LANES)
    for channel in range(4):
        line = extinction if channel == 3 else colour[channel : channel + 1]
        for half in range(2):
            tables_ref[2 * channel + half] = jnp.broadcast_to(
                line[:, half * LANES : (half + 1) * LANES], (8, LANES)
            )


def pack_block(front, dense_ref, index_ref, bulk_ref, inside_ref):
    layers, tiles, rows = dense_ref.shape[0], dense_ref.shape[1], dense_ref.shape[2] - 8
    half = rows // 2
    start = jnp.where(front, half, 0)
    for tile in range(tiles):
        lanes = slice(tile * LANES, (tile + 1) * LANES)
        for z in range(layers):
            for part in range(2):
                at = pl.ds(start + part, half // 2, stride=2)
                bulk_ref[2 * z + part, :, lanes] = pack_words(
                    dense_ref[z, tile, at, :], index_ref[z, tile, at, :]
                )
            line = [
                pack_words(dense_ref[z, tile, r : r + 1, :], index_ref[z, tile, r : r + 1, :])
                for r in (half - 1, half)
            ]
            bulk_ref[2 * layers, z : z + 1, lanes] = jnp.where(front, line[0], line[1])
            inside_ref[z : z + 1, lanes] = jnp.where(front, line[1], line[0])


def near_words(slab, place_ref, first_ref, second_ref):
    own = (place_ref[ME] == slab) != (place_ref[TURNED] == 1)
    words = jnp.where(own, first_ref[...], second_ref[...])
    return jnp.where(place_ref[HAS_NEAR] == 1, words, 0)


def column_lines(me, read_words, inside, lines_ref, rows):
    layers, cols = inside.shape
    front = me == 0
    start = me * (rows // 2)
    middle = LANES // 2
    lane_at = lax.broadcasted_iota(jnp.int32, (8, LANES), 1)
    row_at = start + 2 * lax.broadcasted_iota(jnp.int32, (8, LANES), 0)
    for z in range(layers):
        line = jnp.zeros((8, LANES), jnp.int32)
        for part in range(2):
            first = read_words(z, part, 0)[:, 0:1]
            last = read_words(z, part, cols // LANES - 1)[:, LANES - 1 : LANES]
            line += jnp.where(lane_at == row_at + part, first, 0)
            line += jnp.where(lane_at == row_at + part + middle, last, 0)
        lines_ref[z : z + 1, :] = jnp.sum(line, axis=0, keepdims=True)
    beside = jnp.where(front, rows // 2, rows // 2 - 1)
    lines = jnp.where(lane_at == beside, inside[:, 0:1], lines_ref[...])
    lines_ref[...] = jnp.where(lane_at == beside + middle, inside[:, cols - 1 : cols], lines)


def side_kernel(
    rows, place_ref, columns_ref, bulk_ref, second_ref, first_ref, part_ref, cells_ref, ends_ref, other_ref
):
    layers, _ = columns_ref.shape
    me = place_ref[ME]
    front = me == 0
    lane_at = lax.broadcasted_iota(jnp.int32, (layers, LANES), 1)

    def read_words(z, part, tile):
        return bulk_ref[2 * z + part, :, tile * LANES : (tile + 1) * LANES]

    column_lines(me, read_words, bulk_ref[2 * layers], other_ref, rows)
    for slab in range(2):
        mine = front if slab == 0 else jnp.logical_not(front)
        columns = jnp.where(mine, columns_ref[...], other_ref[...])
        near = near_words(slab, place_ref, first_ref, second_ref)
        cols = near.shape[1]
        columns = jnp.where(lane_at == rows, near[:, 0:1], columns)
        ends_ref[slab] = jnp.where(
            lane_at == LANES // 2 + rows, near[:, cols - 1 : cols], columns
        )


def fill_weights(weights_ref):
    cols = weights_ref.shape[0]
    row = lax.broadcasted_iota(jnp.int32, (LANES, 2 * LANES), 0)
    at = lax.broadcasted_iota(jnp.int32, (LANES, 2 * LANES), 1)
    place = at - 2 * row
    block = jnp.where(
        (place == 0) | (place == 1), 3.0, jnp.where((place == -1) | (place == 2), 1.0, 0.0)
    ).astype(jnp.bfloat16)
    after = jnp.where((row == LANES - 1) & (at == 0), 1.0, 0.0).astype(jnp.bfloat16)
    before = jnp.where((row == 0) & (at == 2 * LANES - 1), 1.0, 0.0).astype(jnp.bfloat16)
    count = cols // LANES
    for i in range(count):
        for j in range(count):
            piece = block if i == j else after if j == i + 1 else before if j == i - 1 else None
            if piece is None:
                piece = jnp.zeros((LANES, 2 * LANES), jnp.bfloat16)
            weights_ref[i * LANES : (i + 1) * LANES, 2 * j * LANES : 2 * (j + 1) * LANES] = piece


def classify_rows(read_cells, tables, cells_ref, layers, tiles):
    total = float(2 * layers)
    for z in range(layers):
        for tile in range(tiles):
            even = cell_values(*read_cells(z, 0, tile), tables, total)
            odd = cell_values(*read_cells(z, 1, tile), tables, total)
            for channel in range(4):
                base = (z * 4 + channel) * 16
                block = jnp.concatenate([even[channel], odd[channel]], axis=0)
                cells_ref[base : base + 16, tile * LANES : (tile + 1) * LANES] = block.astype(jnp.bfloat16)


def rounded(value):
    return value.astype(jnp.bfloat16).astype(jnp.float32)


def cells_kernel(
    place_ref, dense_ref, index_ref, inside_ref, tables_ref, cells_ref, weights_ref, mix_ref, lines_ref
):
    layers, tiles, rows = dense_ref.shape[0], dense_ref.shape[1], dense_ref.shape[2] - 8
    half = rows // 2
    start = place_ref[ME] * half
    fill_weights(weights_ref)
    fill_rows(mix_ref)

    def read_cells(z, part, tile):
        at = pl.ds(start + part, half // 2, stride=2)
        return dense_ref[z, tile, at, :], index_ref[z, tile, at, :]

    classify_rows(read_cells, read_tables(tables_ref), cells_ref, layers, tiles)
    column_lines(place_ref[ME], lambda *at: pack_words(*read_cells(*at)), inside_ref[...], lines_ref, rows)


def along_columns(cells, weights_ref, store):
    result = rounded(jnp.dot(cells, weights_ref[...], preferred_element_type=jnp.float32))
    for tile in range(result.shape[1] // LANES):
        store(tile, result[:, tile * LANES : (tile + 1) * LANES])


def own_kernel(place_ref, cells_ref, weights_ref, along_ref):
    size = cells_ref.shape[0]
    pad = 64
    mine = pl.multiple_of(pad + place_ref[ME] * size, pad)

    def store(tile, block):
        along_ref[tile, 0:pad, :] = jnp.zeros((pad, LANES), jnp.float32)
        along_ref[tile, pad + 2 * size : 2 * pad + 2 * size, :] = jnp.zeros((pad, LANES), jnp.float32)
        along_ref[tile, pl.ds(mine, size), :] = block

    along_columns(cells_ref[...], weights_ref, store)


def other_cells_kernel(bulk_ref, tables_ref, cells_ref):
    layers = (bulk_ref.shape[0] - 1) // 2
    cols = bulk_ref.shape[2]

    def read_cells(z, part, tile):
        return unpack_words(bulk_ref[2 * z + part, :, tile * LANES : (tile + 1) * LANES])

    classify_rows(read_cells, read_tables(tables_ref), cells_ref, layers, cols // LANES)


def edge_cells(near, inside, tables, cells_ref, front, base):
    layers, cols = near.shape
    for side in range(2):
        use_near = front if side == 0 else jnp.logical_not(front)
        words = jnp.where(use_near, near, inside)
        for t in range(cols // LANES):
            values = cell_values(
                *unpack_words(words[:, t * LANES : (t + 1) * LANES]), tables, float(2 * layers)
            )
            for channel in range(4):
                at = pl.ds(base + side * 4 + channel, layers, stride=8)
                cells_ref[t, at, :] = values[channel]


def edge_along(cells_ref, count, weights_ref):
    return rounded(
        sum(
            jnp.dot(
                cells_ref[t, 0:count].astype(jnp.bfloat16),
                weights_ref[t * LANES : (t + 1) * LANES, :],
                preferred_element_type=jnp.float32,
            )
            for t in range(cells_ref.shape[0])
        )
    )


def edge_lines(now, packed_ref, lines_ref, depth):
    triple = 3.0 * now
    empty = jnp.zeros((8, LANES), jnp.float32)
    for layer in range(depth):
        at = layer * 8
        here = triple[at : at + 8]
        before = now[at - 8 : at] if layer > 0 else empty
        after = now[at + 8 : at + 16] if layer + 1 < depth else empty
        line = jnp.concatenate([before + here, empty], axis=0)
        packed_ref[2 * at : 2 * at + 16, :] = line.astype(jnp.bfloat16)
        lines_ref[at : at + 8, :] = rounded(after + here)


def row_samples(value, above, below):
    sub_at = lax.broadcasted_iota(jnp.int32, (8, LANES), 0)
    low, high = value[0:8], value[8:16]
    before = jnp.where(sub_at == 0, above, pltpu.roll(high, 1, 0))
    after = jnp.where(sub_at == 7, below, pltpu.roll(low, 7, 0))
    low_centre = 3.0 * low
    high_centre = 3.0 * high
    return [before + low_centre, low_centre + high, low + high_centre, high_centre + after]


def slab_pair(
    along_refs, packed_refs, lines_refs, rows_ref, slab, lines_slab, layers, keep_first=None, keep_last=None
):
    along_at = pl.ds(pl.multiple_of(slab * (layers * 64), 64), (layers + 2) * 64)
    packed_at = pl.ds(pl.multiple_of(lines_slab * (layers * 16), 16), layers * 16)
    lines_at = pl.ds(pl.multiple_of(lines_slab * (layers * 8), 8), layers * 8 + 8)
    views = [ref.at[along_at, :] for ref in along_refs]
    packed = [ref.at[packed_at, :] for ref in packed_refs]
    lines = [ref.at[lines_at, :] for ref in lines_refs]

    def layer_rows(view, layer, channel):
        base = (layer * 4 + channel) * 16
        return view[base : base + 16, :]

    def both(pieces):
        return jnp.concatenate(pieces, axis=1)

    def blend(image, samples, keep):
        updated = []
        for tile in range(2):
            clear = [1.0 - value for value in image[tile][3]]
            updated.append([])
            for c in range(4):
                values = samples[tile][c]
                if keep is not None:
                    values = [jnp.where(keep, value, 0.0) for value in values]
                updated[tile].append([image[tile][c][i] + clear[i] * values[i] for i in range(4)])
        return updated

    zero = jnp.zeros((8, LANES), jnp.float32)
    image = [[[zero] * 4 for _ in range(4)] for _ in range(2)]
    for z in range(layers):
        triple = [[3.0 * layer_rows(v, z + 1, c) for c in range(4)] for v in views]
        mixed = [
            both([(layer_rows(v, z, c) + t[c]).astype(jnp.bfloat16) for v, t in zip(views, triple)])
            for c in range(4)
        ]
        mixed.append(both([line[z * 16 : z * 16 + 16, :] for line in packed]))
        product = jnp.dot(
            rows_ref[...], jnp.concatenate(mixed, axis=0), preferred_element_type=jnp.float32
        )
        even, odd = [], []
        for tile in range(2):
            lanes = slice(tile * LANES, (tile + 1) * LANES)
            even.append(
                [
                    [product[c * 32 + i * 8 : c * 32 + i * 8 + 8, lanes] for i in range(4)]
                    for c in range(4)
                ]
            )
            odd.append([])
            for c in range(4):
                value = rounded(layer_rows(views[tile], z + 2, c) + triple[tile][c])
                above = lines[tile][pl.ds(z * 8 + c, 8, stride=0), :]
                below = lines[tile][pl.ds(z * 8 + 4 + c, 8, stride=0), :]
                odd[tile].append(row_samples(value, above, below))
        image = blend(image, even, keep_first if z == 0 else None)
        image = blend(image, odd, keep_last if z == layers - 1 else None)
    return image


def joined(first, in_front, behind):
    top = [[jnp.where(first, x, y) for x, y in zip(a, b)] for a, b in zip(in_front, behind)]
    low = [[jnp.where(first, y, x) for x, y in zip(a, b)] for a, b in zip(in_front, behind)]
    clear = [1.0 - value for value in top[3]]
    return [[top[c][i] + clear[i] * low[c][i] for i in range(4)] for c in range(4)]


def own_tiles_kernel(
    place_ref, tables_ref, weights_ref, inside_ref, mix_ref, along_ref, part_ref, cells_ref, packed_ref, lines_ref
):
    layers, cols = inside_ref.shape
    me = place_ref[ME]
    front = me == 0
    inside = inside_ref[...]
    edge_cells(jnp.zeros_like(inside), inside, read_tables(tables_ref), cells_ref, front, 0)
    edge = edge_along(cells_ref, 8 * layers, weights_ref)
    tiles = 2 * cols // LANES
    for tile in range(tiles):
        now = edge[:, tile * LANES : (tile + 1) * LANES]
        edge_lines(now, packed_ref.at[tile], lines_ref.at[tile], layers)
    for pair in range(tiles // 2):
        at = [2 * pair, 2 * pair + 1]
        image = slab_pair(
            [along_ref.at[tile] for tile in at],
            [packed_ref.at[tile] for tile in at],
            [lines_ref.at[tile] for tile in at],
            mix_ref,
            me,
            0,
            layers,
            front,
            jnp.logical_not(front),
        )
        for index, tile in enumerate(at):
            for channel in range(4):
                for i in range(4):
                    part_ref[tile, channel * 4 + i] = image[index][channel][i]


def fill_rows(rows_ref):
    m = lax.broadcasted_iota(jnp.int32, rows_ref.shape, 0)
    k = lax.broadcasted_iota(jnp.int32, rows_ref.shape, 1)
    row = 4 * (m & 7) + (lax.shift_right_logical(m, 3) & 3)
    centre = lax.shift_right_logical(row, 1)
    beside = centre - 1 + 2 * (row & 1)
    own = k < 64
    k_channel = jnp.where(own, lax.shift_right_logical(k, 4), k & 3)
    k_row = 2 * (k & 7) + (lax.shift_right_logical(k, 3) & 1)
    k_row = jnp.where(own, k_row, jnp.where(k < 68, -1, jnp.where(k < 72, 16, 99)))
    same = k_channel == lax.shift_right_logical(m, 5)
    value = jnp.where(k_row == centre, 3.0, jnp.where(k_row == beside, 1.0, 0.0))
    rows_ref[...] = jnp.where(same, value, 0.0).astype(jnp.bfloat16)


def over(in_front, behind):
    clear = 1.0 - in_front[3]
    return [top + clear * low for top, low in zip(in_front, behind)]


def through_layers(samples, layers):
    image = over(*samples)
    step = 1
    while step < layers:
        image = over(image, [pltpu.roll(value, layers - step, 0) for value in image])
        step *= 2
    return image


def tiles_kernel(
    place_ref, tables_ref, weights_ref, bulk_ref, inside_ref, second_ref, first_ref, ends_ref, mix_ref,
    part_ref, other_ref, own_ref, image_ref, mine_ref, along_ref, cells_ref, packed_ref, lines_ref, edge_ref, between_ref,
):
    layers, cols = inside_ref.shape
    depth = 2 * layers
    tiles = 2 * cols // LANES
    me = place_ref[ME]
    front = me == 0
    tables = read_tables(tables_ref)
    size = other_ref.shape[0]
    theirs = pl.multiple_of(64 + (1 - me) * size, 64)

    def store(tile, block):
        along_ref[tile, pl.ds(theirs, size), :] = block

    along_columns(other_ref[...], weights_ref, store)
    for slab in range(2):
        inside = jnp.where(me == slab, inside_ref[...], bulk_ref[2 * layers])
        near = near_words(slab, place_ref, first_ref, second_ref)
        edge_cells(near, inside, tables, cells_ref, front, slab * layers * 8)
        values = cell_values(*unpack_words(ends_ref[slab]), tables, float(depth))
        for channel in range(4):
            mine_ref[slab * 4 + channel] = 3.0 * rounded(values[channel])
    edge = edge_along(cells_ref, 8 * depth, weights_ref)
    here_at, beside_at = layers * 8 - 8, layers * 8
    empty = jnp.zeros((8, LANES), jnp.float32)
    for tile in range(tiles):
        now = edge[:, tile * LANES : (tile + 1) * LANES]
        edge_lines(now, packed_ref.at[tile], lines_ref.at[tile], depth)
        upper, lower = now[here_at : here_at + 8], now[beside_at : beside_at + 8]
        between_ref[tile, 0:8] = rounded(
            jnp.where(front, lower, upper) + 3.0 * jnp.where(front, upper, lower)
        )
        edge_ref[tile, 0:8] = empty
        edge_ref[tile, 8 : 8 * depth + 8] = now
        edge_ref[tile, 8 * depth + 8 : 8 * depth + 16] = empty

    row = jnp.where(front, 0, 15)
    line = jnp.where(front, 0, 4)
    first_layer = me * layers
    layer_at = lax.broadcasted_iota(jnp.int32, (layers, LANES), 0)
    replaced = []
    for tile in range(tiles):
        samples = [[], []]
        for channel in range(4):
            inner, outer = [], []
            for z in range(3):
                at = (first_layer + z) * 64 + channel * 16 + row
                inner.append(along_ref[tile, pl.ds(at, layers, stride=64), :])
                at = (first_layer + z) * 8 + channel + line
                outer.append(edge_ref[tile, pl.ds(at, layers, stride=8), :])
            for parity in range(2):
                sample = rounded(outer[2 * parity] + 3.0 * outer[1]) + 3.0 * rounded(
                    inner[2 * parity] + 3.0 * inner[1]
                )
                if parity == 0:
                    kept = jnp.where(front, sample, 0.0)
                    sample = jnp.where(layer_at == 0, kept, sample)
                else:
                    kept = jnp.where(front, 0.0, sample)
                    sample = jnp.where(layer_at == layers - 1, kept, sample)
                samples[parity].append(sample)
        replaced.append(through_layers(samples, layers))

    sub_at = lax.broadcasted_iota(jnp.int32, (8, LANES), 0)
    for pair in range(tiles // 2):
        at = [2 * pair, 2 * pair + 1]
        other = slab_pair(
            [along_ref.at[tile] for tile in at],
            [packed_ref.at[tile] for tile in at],
            [lines_ref.at[tile] for tile in at],
            mix_ref,
            1 - me,
            1 - me,
            layers,
        )
        for index, tile in enumerate(at):
            here = pl.multiple_of(jnp.where(front, layers, layers + 1) * 64, 64)
            beside = pl.multiple_of(jnp.where(front, layers + 1, layers) * 64, 64)
            between, part = [], []
            for c in range(4):
                value = rounded(
                    along_ref[tile, pl.ds(beside + c * 16, 16), :]
                    + 3.0 * along_ref[tile, pl.ds(here + c * 16, 16), :]
                )
                above = between_ref[tile, pl.ds(c, 8, stride=0), :]
                below = between_ref[tile, pl.ds(c + 4, 8, stride=0), :]
                between.append(row_samples(value, above, below))
                values = [part_ref[tile, c * 4 + i] for i in range(4)]
                line = replaced[tile][c][0:1]
                values[0] = jnp.where(sub_at == 0, jnp.where(front, line, values[0]), values[0])
                values[3] = jnp.where(sub_at == 7, jnp.where(front, values[3], line), values[3])
                part.append(values)
            mine = joined(front, part, between)
            image = joined((me ^ place_ref[FLIP]) == 0, mine, other[index])
            for c in range(4):
                for i in range(4):
                    image_ref[tile, c, pl.ds(i, 8, stride=4), :] = image[c][i]


def edge_kernel(
    place_ref, tables_ref, beside_ref, across_ref, mine_ref, image_ref,
    out_ref, final_ref, turned_ref, fixed_ref, sems,
):
    rows = out_ref.shape[1]
    cols = out_ref.shape[2] // 2
    half = rows // 2
    layers = beside_ref.shape[1]
    tiles = 2 * cols // LANES
    middle = LANES // 2
    front = place_ref[ME] == 0
    start = pl.multiple_of(place_ref[ME] * half, half)
    even_x = place_ref[ODD_X] == 0
    tables = read_tables(tables_ref)

    def to_out(tile, source):
        lanes = pl.ds(tile * LANES, LANES)
        return pltpu.make_async_copy(
            source.at[:, pl.ds(0, rows), :], out_ref.at[:, :, lanes], sems.at[tile]
        )

    copies = [to_out(tile, image_ref.at[tile]) for tile in range(1, tiles - 1)]
    for copy in copies:
        copy.start()
    lane_at = lax.broadcasted_iota(jnp.int32, (layers, LANES), 1)
    layer_at = lax.broadcasted_iota(jnp.int32, (layers, LANES), 0)
    first_lane = (lane_at & (middle - 1)) == 0
    along = [[], []]
    samples = {}
    for slab in range(2):
        right = jnp.where(even_x, beside_ref[slab], across_ref[slab])
        left = jnp.where(even_x, across_ref[slab], beside_ref[slab])
        right = jnp.where(place_ref[HAS_RIGHT] == 1, right, 0)
        left = jnp.where(place_ref[HAS_LEFT] == 1, left, 0)
        words = pltpu.roll(jnp.where(lane_at < middle, right, left), middle, 1)
        halo = cell_values(*unpack_words(words), tables, float(2 * layers))
        for channel in range(4):
            along[slab].append(rounded(mine_ref[slab * 4 + channel] + rounded(halo[channel])))
    for channel in range(4):
        front_part, back_part = along[0][channel], along[1][channel]
        down = [pltpu.roll(front_part, 1, 0), pltpu.roll(back_part, 1, 0)]
        up = [pltpu.roll(front_part, layers - 1, 0), pltpu.roll(back_part, layers - 1, 0)]
        is_first, is_last = layer_at == 0, layer_at == layers - 1
        before = [jnp.where(is_first, 0.0, down[0]), jnp.where(is_first, down[0], down[1])]
        after = [jnp.where(is_last, up[1], up[0]), jnp.where(is_last, 0.0, up[1])]
        for slab in range(2):
            triple = 3.0 * along[slab][channel]
            for parity, other in enumerate((before[slab], after[slab])):
                mixed = rounded(other + triple)
                centre = 3.0 * mixed
                above = pltpu.roll(mixed, 1, 1)
                near = pltpu.roll(mixed, LANES - rows, 1)
                above = jnp.where(first_lane, jnp.where(front, near, above), above)
                below = pltpu.roll(mixed, LANES - 1, 1)
                samples[slab, parity, 0, channel] = above + centre
                samples[slab, parity, 1, channel] = centre + below

    slabs = []
    for slab in range(2):
        slabs.append([])
        for odd in range(2):
            image = through_layers(
                [[samples[slab, parity, odd, channel] for channel in range(4)] for parity in range(2)],
                layers,
            )
            slabs[slab].append(image)
    in_order = place_ref[FLIP] == 0
    image = [
        over(
            *[
                [jnp.where(in_order, x, y) for x, y in zip(slabs[at][odd], slabs[1 - at][odd])]
                for at in range(2)
            ]
        )
        for odd in range(2)
    ]
    for odd in range(2):
        for channel in range(4):
            at = odd * 4 + channel
            final_ref[at : at + 1, :] = image[odd][channel][0:1]
    turned_ref[:, 0:8] = final_ref[...].T
    wide = lax.broadcasted_iota(jnp.int32, (half, LANES), 1)
    for index, tile in enumerate((0, tiles - 1)):
        place = wide == index * (LANES - 1)
        turned = turned_ref[pl.ds(start + index * middle, half), :]
        for channel in range(4):
            for odd in range(2):
                at = pl.ds(odd, half, stride=2)
                column = odd * 4 + channel
                fixed_ref[index, channel, at, :] = jnp.where(
                    place, turned[:, column : column + 1], image_ref[tile, channel, at, :]
                )
        copies.append(to_out(tile, fixed_ref.at[index]))
        copies[-1].start()
    for copy in copies:
        copy.wait()


def two_slab_device(density, bin_index, tf_colour, tf_extinction, slab_rank):
    layers, rows, cols = density.shape
    half = rows // 2
    tiles = 2 * cols // LANES
    size = layers * 4 * half
    count_y, count_x = lax.axis_size("by"), lax.axis_size("bx")
    f32, bf16, i32 = jnp.float32, jnp.bfloat16, jnp.int32

    def call(kernel, name, out_shape, time, scratch_shapes=(), in_specs=None, out_specs=None, aliases={}):
        def run(*operands):
            return pl.pallas_call(
                kernel,
                out_shape=out_shape,
                in_specs=in_specs or [SMEM] + [VMEM] * (len(operands) - 1),
                out_specs=out_specs
                or ((VMEM,) * len(out_shape) if isinstance(out_shape, tuple) else VMEM),
                scratch_shapes=scratch_shapes,
                input_output_aliases=aliases,
                compiler_params=pltpu.CompilerParams(vmem_limit_bytes=16 * 1024 * 1024),
                cost_estimate=cost(time),
                name=name,
            )(*operands)

        return run

    def both(route):
        return route + [(target, source) for source, target in route]

    blocks = (layers, cols // LANES, rows + 8, LANES)
    row = pltpu.VMEM((layers, cols), i32)
    inputs = [
        pltpu.with_memory_space_constraint(x, pltpu.HBM)
        for x in (slab_rank, density, bin_index, tf_colour, tf_extinction)
    ]
    place, first, second, bulk, inside, dense, index, tables = call(
        stage_kernel,
        "stage_block",
        (
            pltpu.SMEM((7,), i32),
            row,
            row,
            pltpu.VMEM((2 * layers + 1, 8, cols), i32),
            row,
            pltpu.VMEM(blocks, f32),
            pltpu.VMEM(blocks, i32),
            pltpu.VMEM((8, 8, LANES), f32),
        ),
        1.2,
        in_specs=[SMEM] + [VMEM] * 4,
        out_specs=(SMEM,) + (VMEM,) * 7,
    )(*inputs)
    def device(z, y, x):
        return (z * count_y + y) * count_x + x

    def lanes(route):
        return [(device(*source, x), device(*target, x)) for source, target in route for x in range(count_x)]

    def twins(z, y):
        return both([(device(z, y, x), device(z, y, x + 1)) for x in range(0, count_x, 2)])

    last = count_y - 1
    ring = [((1, 0), (0, 1)), ((0, last), (1, last))]
    ring += [((0, y), (0, y + 1)) for y in range(1, last)] + [((1, y + 1), (1, y)) for y in range(last)]
    ring = lanes(ring) + twins(0, 0)
    diagonal = [((1, 0), (0, 0)), ((0, 0), (0, 1)), ((0, 1), (1, 0))]
    for y in range(1, last):
        diagonal += both([((1, y), (0, y + 1))])
    diagonal = lanes(diagonal) + twins(1, last)
    axes = ("bz", "by", "bx")
    bulk = lax.ppermute(bulk, "bz", [(0, 1), (1, 0)])
    first = lax.ppermute(first, axes, ring)
    second = lax.ppermute(second, axes, diagonal)

    cells, weights, mix, columns = call(
        cells_kernel,
        "own_cells",
        (
            pltpu.VMEM((size, cols), bf16),
            pltpu.VMEM((cols, 2 * cols), bf16),
            pltpu.VMEM((128, 80), bf16),
            pltpu.VMEM((layers, LANES), i32),
        ),
        0.5,
    )(place, dense, index, inside, tables)
    whole = pltpu.VMEM((tiles, 2 * size + 4 * 4 * half, LANES), f32)
    along = call(own_kernel, "own_slab", whole, 0.4)(place, cells, weights)
    edges = pltpu.VMEM((cols // LANES, 16 * layers + 8, LANES), f32)
    packed = pltpu.VMEM((tiles, 32 * layers, LANES), bf16)
    lines = pltpu.VMEM((tiles, 16 * layers + 8, LANES), f32)
    part = call(
        own_tiles_kernel,
        "own_tiles",
        pltpu.VMEM((tiles, 16, 8, LANES), f32),
        0.1,
        [edges, packed, lines],
    )(place, tables, weights, inside, mix, along)
    other_cells = call(
        other_cells_kernel, "other_cells", pltpu.VMEM((size, cols), bf16), 0.1, in_specs=[VMEM] * 2
    )(bulk, tables)
    ends = call(
        functools.partial(side_kernel, rows),
        "side_columns",
        pltpu.VMEM((2, layers, LANES), i32),
        0.1,
        [pltpu.VMEM((layers, LANES), i32)],
    )(place, columns, bulk, second, first, part, other_cells)
    pairs = [(x, x + 1) for x in range(0, count_x, 2)]
    cross = [(x, (x + 1) % count_x) for x in range(1, count_x, 2)]
    beside = lax.ppermute(ends, "bx", both(pairs))
    across = lax.ppermute(ends, "bx", both(cross))
    image, mine, _ = call(
        tiles_kernel,
        "render_tiles",
        (pltpu.VMEM((tiles, 4, rows + 8, LANES), f32), pltpu.VMEM((8, layers, LANES), f32), whole),
        2.0,
        [
            edges,
            packed,
            lines,
            pltpu.VMEM((tiles, 16 * layers + 32, LANES), f32),
            pltpu.VMEM((tiles, 16, LANES), f32),
        ],
        aliases={11: 2},
    )(place, tables, weights, bulk, inside, second, first, ends, mix, part, other_cells, along)
    return call(
        edge_kernel,
        "edge_columns",
        jax.ShapeDtypeStruct((4, rows, 2 * cols), f32),
        1.0,
        [
            pltpu.VMEM((8, LANES), f32),
            pltpu.VMEM((LANES, LANES), f32),
            pltpu.VMEM((2, 4, rows + 8, LANES), f32),
            pltpu.SemaphoreType.DMA((tiles,)),
        ],
        out_specs=pl.BlockSpec(memory_space=pltpu.HBM),
    )(place, tables, beside, across, mine, image)


def on_device(density, bin_index, tf_colour, tf_extinction, slab_rank):
    if lax.axis_size("bz") == 2:
        return two_slab_device(density, bin_index, tf_colour, tf_extinction, slab_rank)
    return general_device(density, bin_index, tf_colour, tf_extinction, slab_rank)


def solution(mesh):
    return jax.shard_map(
        on_device,
        mesh=mesh,
        in_specs=(P("bz", "by", "bx"), P("bz", "by", "bx"), P(), P(), P()),
        out_specs=P(None, ("by", "bz"), "bx"),
        check_vma=False,
    )
```

```python
import functools

import jax
import jax.numpy as jnp
from jax import lax
from jax.experimental import pallas as pl
from jax.experimental.pallas import tpu as pltpu
from jax.sharding import PartitionSpec as P


def with_halo(block, sides, width):
    for axis, dim in sides:
        count = lax.axis_size(axis)
        forward = [(i, i + 1) for i in range(count - 1)]
        backward = [(target, source) for source, target in forward]
        low = lax.ppermute(
            lax.slice_in_dim(block, block.shape[dim] - width, None, axis=dim), axis, forward
        )
        high = lax.ppermute(lax.slice_in_dim(block, 0, width, axis=dim), axis, backward)
        block = jnp.concatenate([low, block, high], axis=dim)
    return block


def partner_2(block, axis, stride):
    count = lax.axis_size(axis)
    route = []
    for low in range(count):
        high = low | 1 << stride
        if high != low and high < count:
            route += [(low, high), (high, low)]
    return lax.ppermute(block, axis, route)


def resample_table(length):
    row_index = lax.broadcasted_iota(jnp.int32, (2 * length, length + 2), 0)
    col_index = lax.broadcasted_iota(jnp.int32, (2 * length, length + 2), 1)
    centre = row_index // 2
    parity = row_index % 2
    weights_table = jnp.where(col_index == centre + 1, 0.75, 0.0)
    weights_table = weights_table + jnp.where((col_index == centre) & (parity == 0), 0.25, 0.0)
    weights_table = weights_table + jnp.where((col_index == centre + 2) & (parity == 1), 0.25, 0.0)
    return weights_table.astype(jnp.bfloat16)


def blend_over(in_front, behind):
    return in_front + (1.0 - in_front[3])[None] * behind


def classify(density, bin_index, tf_colour, tf_extinction, total_depth):
    depth_cells, height_cells, width_cells = density.shape
    lookup = jnp.concatenate([tf_colour, tf_extinction[None, :]], axis=0)
    table_size = lookup.shape[1]
    bin_rows = lax.broadcasted_iota(jnp.int32, (table_size, 1), 0)
    flat_bins = bin_index.reshape(depth_cells, height_cells * width_cells)
    flat_density = density.reshape(depth_cells, height_cells * width_cells)

    def one_layer(layer, result):
        layer_bins = lax.dynamic_index_in_dim(flat_bins, layer, 0, keepdims=True)
        layer_density = lax.dynamic_index_in_dim(flat_density, layer, 0, keepdims=False)
        one_hot = (layer_bins == bin_rows).astype(jnp.bfloat16)
        values = jnp.dot(lookup, one_hot, preferred_element_type=jnp.float32)
        opacity = 1.0 - jnp.exp(-values[3] * layer_density / total_depth)
        cells = jnp.concatenate([values[:3] * opacity[None], opacity[None]], axis=0).astype(
            jnp.bfloat16
        )
        return lax.dynamic_update_slice_in_dim(result, cells[:, None], layer, 1)

    start_cells = jnp.zeros((4, depth_cells, height_cells * width_cells), jnp.bfloat16)
    classified = lax.fori_loop(0, depth_cells, one_layer, start_cells)
    return classified.reshape(4, depth_cells, height_cells, width_cells)


def general_device(density, bin_index, tf_colour, tf_extinction, slab_rank):
    slab_count = lax.axis_size("bz")
    depth_cells, height_cells, width_cells = density.shape
    total_depth = float(depth_cells * slab_count)
    colour_cells = classify(density, bin_index, tf_colour, tf_extinction, total_depth)
    padded = with_halo(colour_cells, (("bz", 1), ("by", 2), ("bx", 3)), 1)
    along_x = jnp.einsum(
        "czyq,pq->czyp", padded, resample_table(width_cells), preferred_element_type=jnp.float32
    ).astype(jnp.bfloat16)
    y_table = resample_table(height_cells)

    def add_sample(sample_index, image_now):
        centre = sample_index // 2
        parity = sample_index % 2
        layers = lax.dynamic_slice_in_dim(along_x, centre, 3, 1).astype(jnp.float32)
        lower_weight = jnp.where(parity == 0, 0.25, 0.0)
        upper_weight = jnp.where(parity == 1, 0.25, 0.0)
        mixed_layer = (
            lower_weight * layers[:, 0] + 0.75 * layers[:, 1] + upper_weight * layers[:, 2]
        ).astype(jnp.bfloat16)
        sample = jnp.einsum("qy,cyp->cqp", y_table, mixed_layer, preferred_element_type=jnp.float32)
        return blend_over(image_now, sample)

    start_image = jnp.zeros((4, 2 * height_cells, 2 * width_cells), jnp.float32)
    slab_image = lax.fori_loop(0, 2 * depth_cells, add_sample, start_image)
    rows_piece = 2 * height_cells // slab_count
    my_index = lax.axis_index("bz")
    bit_levels = slab_count.bit_length() - 1
    composite = slab_image.reshape((4,) + (2,) * bit_levels + (rows_piece, 2 * width_cells))
    my_rank = lax.dynamic_index_in_dim(slab_rank, my_index, 0, keepdims=False)
    for level in range(bit_levels):
        position = bit_levels - level
        my_bit = my_index // 2**level % 2
        kept_half = lax.dynamic_index_in_dim(composite, my_bit, position, keepdims=False)
        outgoing = lax.dynamic_index_in_dim(composite, 1 - my_bit, position, keepdims=False)
        incoming = partner_2(outgoing, "bz", level)
        partner = my_index + (1 - 2 * my_bit) * 2**level
        partner_rank = lax.dynamic_index_in_dim(slab_rank, partner, 0, keepdims=False)
        mine_first = my_rank < partner_rank
        composite = blend_over(
            jnp.where(mine_first, kept_half, incoming), jnp.where(mine_first, incoming, kept_half)
        )
    return composite


LANES = 128
LEVELS = 65535.0
VMEM = pl.BlockSpec(memory_space=pltpu.VMEM)
SMEM = pl.BlockSpec(memory_space=pltpu.SMEM)
FLIP, ME, HAS_NEAR, TURNED, ODD_X, HAS_RIGHT, HAS_LEFT = range(7)


def pack_words(density, bins):
    level = (density * LEVELS + 0.5).astype(jnp.int32)
    return lax.shift_left(level, 16) | bins


def unpack_words(words):
    density = lax.shift_right_logical(words, 16).astype(jnp.float32) * (1.0 / LEVELS)
    return density, words & 0xFFFF


def cell_values(density, bins, tables, depth):
    low_bits = bins & (LANES - 1)
    upper = bins >= LANES

    def pick(channel):
        first, second = tables[channel]
        return jnp.where(
            upper,
            jnp.take_along_axis(second, low_bits, axis=1, mode="promise_in_bounds"),
            jnp.take_along_axis(first, low_bits, axis=1, mode="promise_in_bounds"),
        )

    opacity = (1.0 - jnp.exp(-pick(3) * density / depth)) * (1.0 / 64.0)
    return [pick(0) * opacity, pick(1) * opacity, pick(2) * opacity, opacity]


def read_tables(tables_ref):
    return [[tables_ref[2 * channel + half] for half in range(2)] for channel in range(4)]


def cost(microseconds):
    return pl.CostEstimate(
        flops=int(1e9 * microseconds), bytes_accessed=int(3.6e6 * microseconds), transcendentals=0
    )


def stage_kernel(
    rank_ref, density_ref, bins_ref, colour_ref, extinction_ref,
    place_ref, first_ref, second_ref, bulk_ref, inside_ref, dense_ref, index_ref, tables_ref,
):
    me, me_y, me_x = lax.axis_index("bz"), lax.axis_index("by"), lax.axis_index("bx")
    past = jnp.where(me == 0, me_y, lax.axis_size("by") - 1 - me_y)
    for at, value in enumerate(
        (
            rank_ref[0],
            me,
            jnp.minimum(past, 1),
            jnp.where((me == 0) & (me_y == 1), 1, 0),
            lax.rem(me_x, 2),
            jnp.where(me_x + 1 < lax.axis_size("bx"), 1, 0),
            jnp.minimum(me_x, 1),
        )
    ):
        place_ref[at] = value
    layers, rows, cols = density_ref.shape
    front = me == 0
    inner = me_y > 0
    for z in range(layers):
        top, bottom = [
            pack_words(density_ref[z, r : r + 1, :], bins_ref[z, r : r + 1, :]) for r in (0, rows - 1)
        ]
        first_ref[z : z + 1, :] = jnp.where(jnp.logical_not(front) & inner, top, bottom)
        second_ref[z : z + 1, :] = jnp.where(front & inner, top, bottom)
        for tile in range(cols // LANES):
            lanes = slice(tile * LANES, (tile + 1) * LANES)
            dense_ref[z, tile, 0:rows] = density_ref[z, :, lanes]
            index_ref[z, tile, 0:rows] = bins_ref[z, :, lanes]
    pack_block(front, dense_ref, index_ref, bulk_ref, inside_ref)
    colour = colour_ref[...].astype(jnp.float32)
    extinction = extinction_ref[...].astype(jnp.float32).reshape(1, 2 * LANES)
    for channel in range(4):
        line = extinction if channel == 3 else colour[channel : channel + 1]
        for half in range(2):
            tables_ref[2 * channel + half] = jnp.broadcast_to(
                line[:, half * LANES : (half + 1) * LANES], (8, LANES)
            )


def pack_block(front, dense_ref, index_ref, bulk_ref, inside_ref):
    layers, tiles, rows = dense_ref.shape[0], dense_ref.shape[1], dense_ref.shape[2] - 8
    half = rows // 2
    start = jnp.where(front, half, 0)
    for tile in range(tiles):
        lanes = slice(tile * LANES, (tile + 1) * LANES)
        for z in range(layers):
            for part in range(2):
                at = pl.ds(start + part, half // 2, stride=2)
                bulk_ref[2 * z + part, :, lanes] = pack_words(
                    dense_ref[z, tile, at, :], index_ref[z, tile, at, :]
                )
            line = [
                pack_words(dense_ref[z, tile, r : r + 1, :], index_ref[z, tile, r : r + 1, :])
                for r in (half - 1, half)
            ]
            bulk_ref[2 * layers, z : z + 1, lanes] = jnp.where(front, line[0], line[1])
            inside_ref[z : z + 1, lanes] = jnp.where(front, line[1], line[0])


def near_words(slab, place_ref, first_ref, second_ref):
    own = (place_ref[ME] == slab) != (place_ref[TURNED] == 1)
    words = jnp.where(own, first_ref[...], second_ref[...])
    return jnp.where(place_ref[HAS_NEAR] == 1, words, 0)


def column_lines(me, read_words, inside, lines_ref, rows):
    layers, cols = inside.shape
    front = me == 0
    start = me * (rows // 2)
    middle = LANES // 2
    lane_at = lax.broadcasted_iota(jnp.int32, (8, LANES), 1)
    row_at = start + 2 * lax.broadcasted_iota(jnp.int32, (8, LANES), 0)
    for z in range(layers):
        line = jnp.zeros((8, LANES), jnp.int32)
        for part in range(2):
            first = read_words(z, part, 0)[:, 0:1]
            last = read_words(z, part, cols // LANES - 1)[:, LANES - 1 : LANES]
            line += jnp.where(lane_at == row_at + part, first, 0)
            line += jnp.where(lane_at == row_at + part + middle, last, 0)
        lines_ref[z : z + 1, :] = jnp.sum(line, axis=0, keepdims=True)
    beside = jnp.where(front, rows // 2, rows // 2 - 1)
    lines = jnp.where(lane_at == beside, inside[:, 0:1], lines_ref[...])
    lines_ref[...] = jnp.where(lane_at == beside + middle, inside[:, cols - 1 : cols], lines)


def side_kernel(
    rows, place_ref, columns_ref, bulk_ref, second_ref, first_ref, part_ref, cells_ref, ends_ref, other_ref
):
    layers, _ = columns_ref.shape
    me = place_ref[ME]
    front = me == 0
    lane_at = lax.broadcasted_iota(jnp.int32, (layers, LANES), 1)

    def read_words(z, part, tile):
        return bulk_ref[2 * z + part, :, tile * LANES : (tile + 1) * LANES]

    column_lines(me, read_words, bulk_ref[2 * layers], other_ref, rows)
    for slab in range(2):
        mine = front if slab == 0 else jnp.logical_not(front)
        columns = jnp.where(mine, columns_ref[...], other_ref[...])
        near = near_words(slab, place_ref, first_ref, second_ref)
        cols = near.shape[1]
        columns = jnp.where(lane_at == rows, near[:, 0:1], columns)
        ends_ref[slab] = jnp.where(
            lane_at == LANES // 2 + rows, near[:, cols - 1 : cols], columns
        )


def fill_weights(weights_ref):
    cols = weights_ref.shape[0]
    row = lax.broadcasted_iota(jnp.int32, (LANES, 2 * LANES), 0)
    at = lax.broadcasted_iota(jnp.int32, (LANES, 2 * LANES), 1)
    place = at - 2 * row
    block = jnp.where(
        (place == 0) | (place == 1), 3.0, jnp.where((place == -1) | (place == 2), 1.0, 0.0)
    ).astype(jnp.bfloat16)
    after = jnp.where((row == LANES - 1) & (at == 0), 1.0, 0.0).astype(jnp.bfloat16)
    before = jnp.where((row == 0) & (at == 2 * LANES - 1), 1.0, 0.0).astype(jnp.bfloat16)
    count = cols // LANES
    for i in range(count):
        for j in range(count):
            piece = block if i == j else after if j == i + 1 else before if j == i - 1 else None
            if piece is None:
                piece = jnp.zeros((LANES, 2 * LANES), jnp.bfloat16)
            weights_ref[i * LANES : (i + 1) * LANES, 2 * j * LANES : 2 * (j + 1) * LANES] = piece


def classify_rows(read_cells, tables, cells_ref, layers, tiles):
    total = float(2 * layers)
    for z in range(layers):
        for tile in range(tiles):
            even = cell_values(*read_cells(z, 0, tile), tables, total)
            odd = cell_values(*read_cells(z, 1, tile), tables, total)
            for channel in range(4):
                base = (z * 4 + channel) * 16
                block = jnp.concatenate([even[channel], odd[channel]], axis=0)
                cells_ref[base : base + 16, tile * LANES : (tile + 1) * LANES] = block.astype(jnp.bfloat16)


def rounded(value):
    return value.astype(jnp.bfloat16).astype(jnp.float32)


def cells_kernel(
    place_ref, dense_ref, index_ref, inside_ref, tables_ref, cells_ref, weights_ref, mix_ref, lines_ref
):
    layers, tiles, rows = dense_ref.shape[0], dense_ref.shape[1], dense_ref.shape[2] - 8
    half = rows // 2
    start = place_ref[ME] * half
    fill_weights(weights_ref)
    fill_rows(mix_ref)

    def read_cells(z, part, tile):
        at = pl.ds(start + part, half // 2, stride=2)
        return dense_ref[z, tile, at, :], index_ref[z, tile, at, :]

    classify_rows(read_cells, read_tables(tables_ref), cells_ref, layers, tiles)
    column_lines(place_ref[ME], lambda *at: pack_words(*read_cells(*at)), inside_ref[...], lines_ref, rows)


def along_columns(cells, weights_ref, store):
    result = rounded(jnp.dot(cells, weights_ref[...], preferred_element_type=jnp.float32))
    for tile in range(result.shape[1] // LANES):
        store(tile, result[:, tile * LANES : (tile + 1) * LANES])


def own_kernel(place_ref, cells_ref, weights_ref, along_ref):
    size = cells_ref.shape[0]
    pad = 64
    mine = pl.multiple_of(pad + place_ref[ME] * size, pad)

    def store(tile, block):
        along_ref[tile, 0:pad, :] = jnp.zeros((pad, LANES), jnp.float32)
        along_ref[tile, pad + 2 * size : 2 * pad + 2 * size, :] = jnp.zeros((pad, LANES), jnp.float32)
        along_ref[tile, pl.ds(mine, size), :] = block

    along_columns(cells_ref[...], weights_ref, store)


def other_cells_kernel(bulk_ref, tables_ref, cells_ref):
    layers = (bulk_ref.shape[0] - 1) // 2
    cols = bulk_ref.shape[2]

    def read_cells(z, part, tile):
        return unpack_words(bulk_ref[2 * z + part, :, tile * LANES : (tile + 1) * LANES])

    classify_rows(read_cells, read_tables(tables_ref), cells_ref, layers, cols // LANES)


def edge_cells(near, inside, tables, cells_ref, front, base):
    layers, cols = near.shape
    for side in range(2):
        use_near = front if side == 0 else jnp.logical_not(front)
        words = jnp.where(use_near, near, inside)
        for t in range(cols // LANES):
            values = cell_values(
                *unpack_words(words[:, t * LANES : (t + 1) * LANES]), tables, float(2 * layers)
            )
            for channel in range(4):
                at = pl.ds(base + side * 4 + channel, layers, stride=8)
                cells_ref[t, at, :] = values[channel]


def edge_along(cells_ref, count, weights_ref):
    return rounded(
        sum(
            jnp.dot(
                cells_ref[t, 0:count].astype(jnp.bfloat16),
                weights_ref[t * LANES : (t + 1) * LANES, :],
                preferred_element_type=jnp.float32,
            )
            for t in range(cells_ref.shape[0])
        )
    )


def edge_lines(now, packed_ref, lines_ref, depth):
    triple = 3.0 * now
    empty = jnp.zeros((8, LANES), jnp.float32)
    for layer in range(depth):
        at = layer * 8
        here = triple[at : at + 8]
        before = now[at - 8 : at] if layer > 0 else empty
        after = now[at + 8 : at + 16] if layer + 1 < depth else empty
        line = jnp.concatenate([before + here, empty], axis=0)
        packed_ref[2 * at : 2 * at + 16, :] = line.astype(jnp.bfloat16)
        lines_ref[at : at + 8, :] = rounded(after + here)


def row_samples(value, above, below):
    sub_at = lax.broadcasted_iota(jnp.int32, (8, LANES), 0)
    low, high = value[0:8], value[8:16]
    before = jnp.where(sub_at == 0, above, pltpu.roll(high, 1, 0))
    after = jnp.where(sub_at == 7, below, pltpu.roll(low, 7, 0))
    low_centre = 3.0 * low
    high_centre = 3.0 * high
    return [before + low_centre, low_centre + high, low + high_centre, high_centre + after]


def slab_pair(
    along_refs, packed_refs, lines_refs, rows_ref, slab, lines_slab, layers, keep_first=None, keep_last=None
):
    along_at = pl.ds(pl.multiple_of(slab * (layers * 64), 64), (layers + 2) * 64)
    packed_at = pl.ds(pl.multiple_of(lines_slab * (layers * 16), 16), layers * 16)
    lines_at = pl.ds(pl.multiple_of(lines_slab * (layers * 8), 8), layers * 8 + 8)
    views = [ref.at[along_at, :] for ref in along_refs]
    packed = [ref.at[packed_at, :] for ref in packed_refs]
    lines = [ref.at[lines_at, :] for ref in lines_refs]

    def layer_rows(view, layer, channel):
        base = (layer * 4 + channel) * 16
        return view[base : base + 16, :]

    def both(pieces):
        return jnp.concatenate(pieces, axis=1)

    def blend(image, samples, keep):
        updated = []
        for tile in range(2):
            clear = [1.0 - value for value in image[tile][3]]
            updated.append([])
            for c in range(4):
                values = samples[tile][c]
                if keep is not None:
                    values = [jnp.where(keep, value, 0.0) for value in values]
                updated[tile].append([image[tile][c][i] + clear[i] * values[i] for i in range(4)])
        return updated

    zero = jnp.zeros((8, LANES), jnp.float32)
    image = [[[zero] * 4 for _ in range(4)] for _ in range(2)]
    for z in range(layers):
        triple = [[3.0 * layer_rows(v, z + 1, c) for c in range(4)] for v in views]
        mixed = [
            both([(layer_rows(v, z, c) + t[c]).astype(jnp.bfloat16) for v, t in zip(views, triple)])
            for c in range(4)
        ]
        mixed.append(both([line[z * 16 : z * 16 + 16, :] for line in packed]))
        product = jnp.dot(
            rows_ref[...], jnp.concatenate(mixed, axis=0), preferred_element_type=jnp.float32
        )
        even, odd = [], []
        for tile in range(2):
            lanes = slice(tile * LANES, (tile + 1) * LANES)
            even.append(
                [
                    [product[c * 32 + i * 8 : c * 32 + i * 8 + 8, lanes] for i in range(4)]
                    for c in range(4)
                ]
            )
            odd.append([])
            line = lines[tile][z * 8 : z * 8 + 8, :]
            for c in range(4):
                value = rounded(layer_rows(views[tile], z + 2, c) + triple[tile][c])
                odd[tile].append(row_samples(value, line[c : c + 1], line[4 + c : 5 + c]))
        image = blend(image, even, keep_first if z == 0 else None)
        image = blend(image, odd, keep_last if z == layers - 1 else None)
    return image


def joined(first, in_front, behind):
    top = [[jnp.where(first, x, y) for x, y in zip(a, b)] for a, b in zip(in_front, behind)]
    low = [[jnp.where(first, y, x) for x, y in zip(a, b)] for a, b in zip(in_front, behind)]
    clear = [1.0 - value for value in top[3]]
    return [[top[c][i] + clear[i] * low[c][i] for i in range(4)] for c in range(4)]


def own_tiles_kernel(
    place_ref, tables_ref, weights_ref, inside_ref, mix_ref, along_ref, part_ref, cells_ref, packed_ref, lines_ref
):
    layers, cols = inside_ref.shape
    me = place_ref[ME]
    front = me == 0
    inside = inside_ref[...]
    edge_cells(jnp.zeros_like(inside), inside, read_tables(tables_ref), cells_ref, front, 0)
    edge = edge_along(cells_ref, 8 * layers, weights_ref)
    tiles = 2 * cols // LANES
    for tile in range(tiles):
        now = edge[:, tile * LANES : (tile + 1) * LANES]
        edge_lines(now, packed_ref.at[tile], lines_ref.at[tile], layers)
    for pair in range(tiles // 2):
        at = [2 * pair, 2 * pair + 1]
        image = slab_pair(
            [along_ref.at[tile] for tile in at],
            [packed_ref.at[tile] for tile in at],
            [lines_ref.at[tile] for tile in at],
            mix_ref,
            me,
            0,
            layers,
            front,
            jnp.logical_not(front),
        )
        for index, tile in enumerate(at):
            for channel in range(4):
                for i in range(4):
                    part_ref[tile, channel * 4 + i] = image[index][channel][i]


def fill_rows(rows_ref):
    m = lax.broadcasted_iota(jnp.int32, rows_ref.shape, 0)
    k = lax.broadcasted_iota(jnp.int32, rows_ref.shape, 1)
    row = 4 * (m & 7) + (lax.shift_right_logical(m, 3) & 3)
    centre = lax.shift_right_logical(row, 1)
    beside = centre - 1 + 2 * (row & 1)
    own = k < 64
    k_channel = jnp.where(own, lax.shift_right_logical(k, 4), k & 3)
    k_row = 2 * (k & 7) + (lax.shift_right_logical(k, 3) & 1)
    k_row = jnp.where(own, k_row, jnp.where(k < 68, -1, jnp.where(k < 72, 16, 99)))
    same = k_channel == lax.shift_right_logical(m, 5)
    value = jnp.where(k_row == centre, 3.0, jnp.where(k_row == beside, 1.0, 0.0))
    rows_ref[...] = jnp.where(same, value, 0.0).astype(jnp.bfloat16)


def tiles_kernel(
    place_ref, tables_ref, weights_ref, bulk_ref, inside_ref, second_ref, first_ref, ends_ref, mix_ref,
    part_ref, other_ref, own_ref, image_ref, mine_ref, along_ref, cells_ref, packed_ref, lines_ref, edge_ref, between_ref,
):
    layers, cols = inside_ref.shape
    depth = 2 * layers
    tiles = 2 * cols // LANES
    me = place_ref[ME]
    front = me == 0
    tables = read_tables(tables_ref)
    size = other_ref.shape[0]
    theirs = pl.multiple_of(64 + (1 - me) * size, 64)

    def store(tile, block):
        along_ref[tile, pl.ds(theirs, size), :] = block

    along_columns(other_ref[...], weights_ref, store)
    for slab in range(2):
        inside = jnp.where(me == slab, inside_ref[...], bulk_ref[2 * layers])
        near = near_words(slab, place_ref, first_ref, second_ref)
        edge_cells(near, inside, tables, cells_ref, front, slab * layers * 8)
        values = cell_values(*unpack_words(ends_ref[slab]), tables, float(depth))
        for channel in range(4):
            mine_ref[slab * 4 + channel] = 3.0 * rounded(values[channel])
    edge = edge_along(cells_ref, 8 * depth, weights_ref)
    here_at, beside_at = layers * 8 - 8, layers * 8
    empty = jnp.zeros((8, LANES), jnp.float32)
    for tile in range(tiles):
        now = edge[:, tile * LANES : (tile + 1) * LANES]
        edge_lines(now, packed_ref.at[tile], lines_ref.at[tile], depth)
        upper, lower = now[here_at : here_at + 8], now[beside_at : beside_at + 8]
        between_ref[tile, 0:8] = rounded(
            jnp.where(front, lower, upper) + 3.0 * jnp.where(front, upper, lower)
        )
        edge_ref[tile, 0:8] = empty
        edge_ref[tile, 8 : 8 * depth + 8] = now
        edge_ref[tile, 8 * depth + 8 :] = empty

    row = jnp.where(front, 0, 15)
    first_layer = me * layers
    replaced = []
    for tile in range(tiles):
        inner, outer = [], []
        for z in range(layers + 2):
            at = (first_layer + z) * 64 + row
            inner.append(along_ref[tile, pl.ds(at, 4, stride=16), :])
            both = edge_ref[tile, pl.ds(pl.multiple_of((first_layer + z) * 8, 8), 8), :]
            outer.append(jnp.where(front, both[0:4], both[4:8]))
        image = jnp.zeros((4, LANES), jnp.float32)
        for z in range(layers):
            for parity in range(2):
                beside = z + 2 * parity
                sample = rounded(outer[beside] + 3.0 * outer[z + 1]) + 3.0 * rounded(
                    inner[beside] + 3.0 * inner[z + 1]
                )
                if (z, parity) == (0, 0):
                    sample = jnp.where(front, sample, 0.0)
                if (z, parity) == (layers - 1, 1):
                    sample = jnp.where(front, 0.0, sample)
                image = image + (1.0 - image[3:4]) * sample
        replaced.append(image)

    sub_at = lax.broadcasted_iota(jnp.int32, (8, LANES), 0)
    for pair in range(tiles // 2):
        at = [2 * pair, 2 * pair + 1]
        other = slab_pair(
            [along_ref.at[tile] for tile in at],
            [packed_ref.at[tile] for tile in at],
            [lines_ref.at[tile] for tile in at],
            mix_ref,
            1 - me,
            1 - me,
            layers,
        )
        for index, tile in enumerate(at):
            here = pl.multiple_of(jnp.where(front, layers, layers + 1) * 64, 64)
            beside = pl.multiple_of(jnp.where(front, layers + 1, layers) * 64, 64)
            between, part = [], []
            for c in range(4):
                value = rounded(
                    along_ref[tile, pl.ds(beside + c * 16, 16), :]
                    + 3.0 * along_ref[tile, pl.ds(here + c * 16, 16), :]
                )
                above = between_ref[tile, pl.ds(c, 8, stride=0), :]
                below = between_ref[tile, pl.ds(c + 4, 8, stride=0), :]
                between.append(row_samples(value, above, below))
                values = [part_ref[tile, c * 4 + i] for i in range(4)]
                line = replaced[tile][c : c + 1]
                values[0] = jnp.where(sub_at == 0, jnp.where(front, line, values[0]), values[0])
                values[3] = jnp.where(sub_at == 7, jnp.where(front, values[3], line), values[3])
                part.append(values)
            mine = joined(front, part, between)
            image = joined((me ^ place_ref[FLIP]) == 0, mine, other[index])
            for c in range(4):
                for i in range(4):
                    image_ref[tile, c, pl.ds(i, 8, stride=4), :] = image[c][i]


def edge_kernel(
    place_ref, tables_ref, beside_ref, across_ref, mine_ref, image_ref,
    out_ref, final_ref, turned_ref, fixed_ref, sems,
):
    rows = out_ref.shape[1]
    cols = out_ref.shape[2] // 2
    half = rows // 2
    layers = beside_ref.shape[1]
    tiles = 2 * cols // LANES
    middle = LANES // 2
    front = place_ref[ME] == 0
    start = pl.multiple_of(place_ref[ME] * half, half)
    even_x = place_ref[ODD_X] == 0
    tables = read_tables(tables_ref)

    def to_out(tile, source):
        lanes = pl.ds(tile * LANES, LANES)
        return pltpu.make_async_copy(
            source.at[:, pl.ds(0, rows), :], out_ref.at[:, :, lanes], sems.at[tile]
        )

    copies = [to_out(tile, image_ref.at[tile]) for tile in range(1, tiles - 1)]
    for copy in copies:
        copy.start()
    lane_at = lax.broadcasted_iota(jnp.int32, (layers, LANES), 1)
    layer_at = lax.broadcasted_iota(jnp.int32, (layers, LANES), 0)
    first_lane = (lane_at & (middle - 1)) == 0
    along = [[], []]
    samples = {}
    for slab in range(2):
        right = jnp.where(even_x, beside_ref[slab], across_ref[slab])
        left = jnp.where(even_x, across_ref[slab], beside_ref[slab])
        right = jnp.where(place_ref[HAS_RIGHT] == 1, right, 0)
        left = jnp.where(place_ref[HAS_LEFT] == 1, left, 0)
        words = pltpu.roll(jnp.where(lane_at < middle, right, left), middle, 1)
        halo = cell_values(*unpack_words(words), tables, float(2 * layers))
        for channel in range(4):
            along[slab].append(rounded(mine_ref[slab * 4 + channel] + rounded(halo[channel])))
    for channel in range(4):
        front_part, back_part = along[0][channel], along[1][channel]
        down = [pltpu.roll(front_part, 1, 0), pltpu.roll(back_part, 1, 0)]
        up = [pltpu.roll(front_part, layers - 1, 0), pltpu.roll(back_part, layers - 1, 0)]
        is_first, is_last = layer_at == 0, layer_at == layers - 1
        before = [jnp.where(is_first, 0.0, down[0]), jnp.where(is_first, down[0], down[1])]
        after = [jnp.where(is_last, up[1], up[0]), jnp.where(is_last, 0.0, up[1])]
        for slab in range(2):
            triple = 3.0 * along[slab][channel]
            for parity, other in enumerate((before[slab], after[slab])):
                mixed = rounded(other + triple)
                centre = 3.0 * mixed
                above = pltpu.roll(mixed, 1, 1)
                near = pltpu.roll(mixed, LANES - rows, 1)
                above = jnp.where(first_lane, jnp.where(front, near, above), above)
                below = pltpu.roll(mixed, LANES - 1, 1)
                samples[slab, parity, 0, channel] = above + centre
                samples[slab, parity, 1, channel] = centre + below

    def over(in_front, behind):
        clear = 1.0 - in_front[3]
        return [top + clear * low for top, low in zip(in_front, behind)]

    slabs = []
    for slab in range(2):
        slabs.append([])
        for odd in range(2):
            image = over(
                *[[samples[slab, parity, odd, channel] for channel in range(4)] for parity in range(2)]
            )
            step = 1
            while step < layers:
                image = over(image, [pltpu.roll(value, layers - step, 0) for value in image])
                step *= 2
            slabs[slab].append(image)
    in_order = place_ref[FLIP] == 0
    image = [
        over(
            *[
                [jnp.where(in_order, x, y) for x, y in zip(slabs[at][odd], slabs[1 - at][odd])]
                for at in range(2)
            ]
        )
        for odd in range(2)
    ]
    for odd in range(2):
        for channel in range(4):
            at = odd * 4 + channel
            final_ref[at : at + 1, :] = image[odd][channel][0:1]
    turned_ref[:, 0:8] = final_ref[...].T
    wide = lax.broadcasted_iota(jnp.int32, (half, LANES), 1)
    for index, tile in enumerate((0, tiles - 1)):
        place = wide == index * (LANES - 1)
        turned = turned_ref[pl.ds(start + index * middle, half), :]
        for channel in range(4):
            for odd in range(2):
                at = pl.ds(odd, half, stride=2)
                column = odd * 4 + channel
                fixed_ref[index, channel, at, :] = jnp.where(
                    place, turned[:, column : column + 1], image_ref[tile, channel, at, :]
                )
        copies.append(to_out(tile, fixed_ref.at[index]))
        copies[-1].start()
    for copy in copies:
        copy.wait()


def two_slab_device(density, bin_index, tf_colour, tf_extinction, slab_rank):
    layers, rows, cols = density.shape
    half = rows // 2
    tiles = 2 * cols // LANES
    size = layers * 4 * half
    count_y, count_x = lax.axis_size("by"), lax.axis_size("bx")
    f32, bf16, i32 = jnp.float32, jnp.bfloat16, jnp.int32

    def call(kernel, name, out_shape, time, scratch_shapes=(), in_specs=None, out_specs=None, aliases={}):
        def run(*operands):
            return pl.pallas_call(
                kernel,
                out_shape=out_shape,
                in_specs=in_specs or [SMEM] + [VMEM] * (len(operands) - 1),
                out_specs=out_specs
                or ((VMEM,) * len(out_shape) if isinstance(out_shape, tuple) else VMEM),
                scratch_shapes=scratch_shapes,
                input_output_aliases=aliases,
                compiler_params=pltpu.CompilerParams(vmem_limit_bytes=16 * 1024 * 1024),
                cost_estimate=cost(time),
                name=name,
            )(*operands)

        return run

    def both(route):
        return route + [(target, source) for source, target in route]

    blocks = (layers, cols // LANES, rows + 8, LANES)
    row = pltpu.VMEM((layers, cols), i32)
    inputs = [
        pltpu.with_memory_space_constraint(x, pltpu.HBM)
        for x in (slab_rank, density, bin_index, tf_colour, tf_extinction)
    ]
    place, first, second, bulk, inside, dense, index, tables = call(
        stage_kernel,
        "stage_block",
        (
            pltpu.SMEM((7,), i32),
            row,
            row,
            pltpu.VMEM((2 * layers + 1, 8, cols), i32),
            row,
            pltpu.VMEM(blocks, f32),
            pltpu.VMEM(blocks, i32),
            pltpu.VMEM((8, 8, LANES), f32),
        ),
        1.2,
        in_specs=[SMEM] + [VMEM] * 4,
        out_specs=(SMEM,) + (VMEM,) * 7,
    )(*inputs)
    def device(z, y, x):
        return (z * count_y + y) * count_x + x

    def lanes(route):
        return [(device(*source, x), device(*target, x)) for source, target in route for x in range(count_x)]

    def twins(z, y):
        return both([(device(z, y, x), device(z, y, x + 1)) for x in range(0, count_x, 2)])

    last = count_y - 1
    ring = [((1, 0), (0, 1)), ((0, last), (1, last))]
    ring += [((0, y), (0, y + 1)) for y in range(1, last)] + [((1, y + 1), (1, y)) for y in range(last)]
    ring = lanes(ring) + twins(0, 0)
    diagonal = [((1, 0), (0, 0)), ((0, 0), (0, 1)), ((0, 1), (1, 0))]
    for y in range(1, last):
        diagonal += both([((1, y), (0, y + 1))])
    diagonal = lanes(diagonal) + twins(1, last)
    axes = ("bz", "by", "bx")
    bulk = lax.ppermute(bulk, "bz", [(0, 1), (1, 0)])
    first = lax.ppermute(first, axes, ring)
    second = lax.ppermute(second, axes, diagonal)

    cells, weights, mix, columns = call(
        cells_kernel,
        "own_cells",
        (
            pltpu.VMEM((size, cols), bf16),
            pltpu.VMEM((cols, 2 * cols), bf16),
            pltpu.VMEM((128, 80), bf16),
            pltpu.VMEM((layers, LANES), i32),
        ),
        0.5,
    )(place, dense, index, inside, tables)
    whole = pltpu.VMEM((tiles, 2 * size + 3 * 4 * half, LANES), f32)
    along = call(own_kernel, "own_slab", whole, 0.4)(place, cells, weights)
    edges = pltpu.VMEM((cols // LANES, 16 * layers + 8, LANES), f32)
    packed = pltpu.VMEM((tiles, 32 * layers, LANES), bf16)
    lines = pltpu.VMEM((tiles, 16 * layers + 8, LANES), f32)
    part = call(
        own_tiles_kernel,
        "own_tiles",
        pltpu.VMEM((tiles, 16, 8, LANES), f32),
        0.1,
        [edges, packed, lines],
    )(place, tables, weights, inside, mix, along)
    other_cells = call(
        other_cells_kernel, "other_cells", pltpu.VMEM((size, cols), bf16), 0.1, in_specs=[VMEM] * 2
    )(bulk, tables)
    ends = call(
        functools.partial(side_kernel, rows),
        "side_columns",
        pltpu.VMEM((2, layers, LANES), i32),
        0.1,
        [pltpu.VMEM((layers, LANES), i32)],
    )(place, columns, bulk, second, first, part, other_cells)
    pairs = [(x, x + 1) for x in range(0, count_x, 2)]
    cross = [(x, (x + 1) % count_x) for x in range(1, count_x, 2)]
    beside = lax.ppermute(ends, "bx", both(pairs))
    across = lax.ppermute(ends, "bx", both(cross))
    image, mine, _ = call(
        tiles_kernel,
        "render_tiles",
        (pltpu.VMEM((tiles, 4, rows + 8, LANES), f32), pltpu.VMEM((8, layers, LANES), f32), whole),
        2.0,
        [
            edges,
            packed,
            lines,
            pltpu.VMEM((tiles, 16 * layers + 16, LANES), f32),
            pltpu.VMEM((tiles, 16, LANES), f32),
        ],
        aliases={11: 2},
    )(place, tables, weights, bulk, inside, second, first, ends, mix, part, other_cells, along)
    return call(
        edge_kernel,
        "edge_columns",
        jax.ShapeDtypeStruct((4, rows, 2 * cols), f32),
        1.0,
        [
            pltpu.VMEM((8, LANES), f32),
            pltpu.VMEM((LANES, LANES), f32),
            pltpu.VMEM((2, 4, rows + 8, LANES), f32),
            pltpu.SemaphoreType.DMA((tiles,)),
        ],
        out_specs=pl.BlockSpec(memory_space=pltpu.HBM),
    )(place, tables, beside, across, mine, image)


def on_device(density, bin_index, tf_colour, tf_extinction, slab_rank):
    if lax.axis_size("bz") == 2:
        return two_slab_device(density, bin_index, tf_colour, tf_extinction, slab_rank)
    return general_device(density, bin_index, tf_colour, tf_extinction, slab_rank)


def solution(mesh):
    return jax.shard_map(
        on_device,
        mesh=mesh,
        in_specs=(P("bz", "by", "bx"), P("bz", "by", "bx"), P(), P(), P()),
        out_specs=P(None, ("by", "bz"), "bx"),
        check_vma=False,
    )
```
